32 devices in a mesh: section: 2 (over x), dp: 4 (over z), tensor: 4 (over y, core).
Axes of the slice: x: 2, y: 2, z: 4, core: 2. Of those that a mesh axis runs over, the one named last changes fastest.
Arguments:
- tokens: bfloat16 [2, 4, 1024, 1024], P(None, 'dp', 'tensor'), may hold values from -6 to 6
- cotangent: bfloat16 [2, 4, 1024, 1024], P(None, 'dp', 'tensor'), may hold values from -6 to 6
- ln1_gain: bfloat16 [2, 1024], P('section', 'dp'), may hold values from 0.5 to 1.5
- ln1_bias: bfloat16 [2, 1024], P('section', 'dp'), may hold values from -3 to 3
- w_qkv: bfloat16 [2, 1024, 3072], P('section', 'dp', 'tensor'), may hold values from -0.1875 to 0.1875
- qv_bias: bfloat16 [2, 16, 128], P('section', 'tensor', 'dp'), may hold values from -3 to 3
- w_out: bfloat16 [2, 1024, 1024], P('section', 'tensor', 'dp'), may hold values from -3 to 3
- out_bias: bfloat16 [2, 1024], P('section', 'dp'), may hold values from -3 to 3
- scale_attn: bfloat16 [2, 1024], P('section', 'dp'), may hold values from 0.5 to 1.5
- ln2_gain: bfloat16 [2, 1024], P('section', 'dp'), may hold values from 0.5 to 1.5
- ln2_bias: bfloat16 [2, 1024], P('section', 'dp'), may hold values from -3 to 3
- w_fc1: bfloat16 [2, 1024, 4096], P('section', 'dp', 'tensor'), may hold values from -0.1875 to 0.1875
- fc1_bias: bfloat16 [2, 4, 1024], P('section', 'tensor', 'dp'), may hold values from -3 to 3
- w_fc2: bfloat16 [2, 4096, 1024], P('section', 'tensor', 'dp'), may hold values from -0.09375 to 0.09375
- fc2_bias: bfloat16 [2, 1024], P('section', 'dp'), may hold values from -3 to 3
- scale_mlp: bfloat16 [2, 1024], P('section', 'dp'), may hold values from 0.5 to 1.5
Outputs:
- block_out: bfloat16 [2, 2, 4, 1024, 1024], P('section', None, 'dp', 'tensor')
- input_grads: bfloat16 [2, 2, 4, 1024, 1024], P('section', None, 'dp', 'tensor')
- grad_ln1_gain: float32 [2, 1024], P('section', 'dp')
- grad_ln1_bias: float32 [2, 1024], P('section', 'dp')
- grad_w_qkv: float32 [2, 1024, 3072], P('section', 'dp', 'tensor')
- grad_qv_bias: float32 [2, 16, 128], P('section', 'tensor', 'dp')
- grad_w_out: float32 [2, 1024, 1024], P('section', 'tensor', 'dp')
- grad_out_bias: float32 [2, 1024], P('section', 'dp')
- grad_scale_attn: float32 [2, 1024], P('section', 'dp')
- grad_ln2_gain: float32 [2, 1024], P('section', 'dp')
- grad_ln2_bias: float32 [2, 1024], P('section', 'dp')
- grad_w_fc1: float32 [2, 1024, 4096], P('section', 'dp', 'tensor')
- grad_fc1_bias: float32 [2, 4, 1024], P('section', 'tensor', 'dp')
- grad_w_fc2: float32 [2, 4096, 1024], P('section', 'tensor', 'dp')
- grad_fc2_bias: float32 [2, 1024], P('section', 'dp')
- grad_scale_mlp: float32 [2, 1024], P('section', 'dp')
The draws below stay inside these ranges and needn't reach their ends.
All inputs are finite; a program needn't handle non-finite values.
Results may differ from the reference program's by a relative error of at most 0.014.
Values may be sent and summed in bfloat16 or wider, within the bound.
No kernel may reach another device: no remote copies, remote signals or barrier semaphores. Data moves between devices by JAX's collectives and lax.ppermute only.
A program may use at most 192 MiB of HBM per device.

```python
import jax
import jax.numpy as jnp
from jax import lax

D = 1024
HEADS = 16
HD = 64
FF = 4096
SEQ = 1024
MB = 2
SECTIONS = 2
IMGS = 4
N_TENSOR = 4


def levels(rng, extent, cuts, least, largest):
    level, own = 1.0, jax.random.fold_in(rng, 6)
    for dim, blocks in cuts:
        heights = jnp.exp(jax.random.uniform(jax.random.fold_in(own, dim), (blocks,), jnp.float32, least / len(cuts), largest / len(cuts)))
        level = level * jnp.repeat(heights, extent[dim] // blocks).reshape([-1 if axis == dim else 1 for axis in range(len(extent))])
    return level


def gaussian(rng, shape, scale, most, pieces=(), dtype=jnp.bfloat16):
    factor_of = levels(rng, shape, pieces, -0.22, 0.18) if pieces else 1.0
    result = jax.random.normal(rng, shape, jnp.float32) * scale * factor_of
    return jnp.minimum(jnp.maximum(result, -most), most).astype(dtype)


def setup_inputs(seed: int = 0) -> dict:
    key_of = jax.random.split(jax.random.key(seed), 17)
    tokens = gaussian(key_of[0], (MB, IMGS, SEQ, D), 1.0, 6.0, ((1, 4), (2, 4)))
    cotangent = gaussian(key_of[1], (MB, IMGS, SEQ, D), 1.0, 6.0, ((1, 4), (2, 4)))
    ln1_gain = jnp.clip(0.5 + 1.0 * jax.random.uniform(key_of[2], (SECTIONS, D), jnp.float32) ** levels(key_of[2], (SECTIONS, D), ((0, 2), (1, 4)), -0.2, 0.2), 0.5, 1.5).astype(jnp.bfloat16)
    ln1_bias = gaussian(key_of[3], (SECTIONS, D), 0.3, 3.0, ((0, 2), (1, 4)))
    w_qkv = gaussian(key_of[4], (SECTIONS, D, 3 * D), D ** -0.5, 0.1875, ((0, 2), (1, 4), (2, 4)))
    qv_bias = gaussian(key_of[5], (SECTIONS, HEADS, 2 * HD), 0.5, 3.0, ((0, 2), (1, 4), (2, 4)))
    w_out = gaussian(key_of[6], (SECTIONS, D, D), (max(4 * D // SEQ, 1)) ** -0.5, 3.0, ((0, 2), (1, 4), (2, 4)))
    out_bias = gaussian(key_of[7], (SECTIONS, D), 0.3, 3.0, ((0, 2), (1, 4)))
    scale_attn = jnp.clip(0.5 + 1.0 * jax.random.uniform(key_of[8], (SECTIONS, D), jnp.float32) ** levels(key_of[8], (SECTIONS, D), ((0, 2), (1, 4)), -0.2, 0.2), 0.5, 1.5).astype(jnp.bfloat16)
    ln2_gain = jnp.clip(0.5 + 1.0 * jax.random.uniform(key_of[9], (SECTIONS, D), jnp.float32) ** levels(key_of[9], (SECTIONS, D), ((0, 2), (1, 4)), -0.2, 0.2), 0.5, 1.5).astype(jnp.bfloat16)
    ln2_bias = gaussian(key_of[10], (SECTIONS, D), 0.3, 3.0, ((0, 2), (1, 4)))
    w_fc1 = gaussian(key_of[11], (SECTIONS, D, FF), D ** -0.5, 0.1875, ((0, 2), (1, 4), (2, 4)))
    fc1_bias = gaussian(key_of[12], (SECTIONS, N_TENSOR, FF // N_TENSOR), 0.5, 3.0, ((0, 2), (1, 4), (2, 4)))
    w_fc2 = gaussian(key_of[13], (SECTIONS, FF, D), FF ** -0.5, 0.09375, ((0, 2), (1, 4), (2, 4)))
    fc2_bias = gaussian(key_of[14], (SECTIONS, D), 0.3, 3.0, ((0, 2), (1, 4)))
    scale_mlp = jnp.clip(0.5 + 1.0 * jax.random.uniform(key_of[15], (SECTIONS, D), jnp.float32) ** levels(key_of[15], (SECTIONS, D), ((0, 2), (1, 4)), -0.2, 0.2), 0.5, 1.5).astype(jnp.bfloat16)
    return {"tokens": tokens, "cotangent": cotangent, "ln1_gain": ln1_gain, "ln1_bias": ln1_bias, "w_qkv": w_qkv, "qv_bias": qv_bias, "w_out": w_out, "out_bias": out_bias, "scale_attn": scale_attn, "ln2_gain": ln2_gain, "ln2_bias": ln2_bias, "w_fc1": w_fc1, "fc1_bias": fc1_bias, "w_fc2": w_fc2, "fc2_bias": fc2_bias, "scale_mlp": scale_mlp}


@jax.custom_vjp
def low(v):
    return lax.optimization_barrier(v.astype(jnp.bfloat16)).astype(jnp.float32)

@jax.custom_vjp
def low_back(v):
    return v

def low_keep(v):
    return (low(v), None)

def low_pass(kept, grad):
    return (grad,)

def back_keep(v):
    return (v, None)

def back_low(kept, grad):
    return (low(grad),)
low.defvjp(low_keep, low_pass)
low_back.defvjp(back_keep, back_low)
EPSILON = 1e-06
HIGHEST = lax.Precision.HIGHEST

def layer_norm(values, gain, shift):
    centred = values - lax.optimization_barrier(jnp.mean(values, axis=-1, keepdims=True))
    variance = lax.optimization_barrier(jnp.mean(centred * centred, axis=-1, keepdims=True))
    return centred * lax.rsqrt(variance + EPSILON) * gain + shift

def attend_image(packed):
    queries = packed[:, :, 0]
    key_rows = packed[:, :, 1]
    value_rows = packed[:, :, 2]
    scores = jnp.einsum('qhe,khe->hqk', queries, key_rows, precision=HIGHEST) * HD ** (-0.5)
    scores = low_back(scores)
    probabilities = low(jax.nn.softmax(scores, axis=-1))
    return jnp.einsum('hqk,khe->qhe', probabilities, value_rows, precision=HIGHEST)

def apply_block(inputs, params):
    gain_one, shift_one, qkv_weight, bias_qv, out_weight, bias_out, attn_scale, gain_two, shift_two, fc1_weight, bias_fc1, fc2_weight, bias_fc2, mlp_scale = params
    image_count = inputs.shape[0]
    normed = low(layer_norm(inputs, gain_one, shift_one))
    packed = jnp.einsum('isd,dc->isc', normed, qkv_weight, precision=HIGHEST).reshape(image_count, SEQ, HEADS, 3, HD)
    qkv_bias_full = jnp.stack([bias_qv[:, :HD], jnp.zeros((HEADS, HD), jnp.float32), bias_qv[:, HD:]], axis=1)
    packed = low(low_back(packed + qkv_bias_full))
    heads_all = lax.map(jax.checkpoint(attend_image), packed)
    heads_all = low(low_back(heads_all.reshape(image_count, SEQ, HEADS * HD)))
    attended = low_back(jnp.einsum('isc,cd->isd', heads_all, out_weight, precision=HIGHEST) + bias_out)
    residual = inputs + attn_scale * attended
    normed_two = low(layer_norm(residual, gain_two, shift_two))
    pre_act = low_back(jnp.einsum('isd,df->isf', normed_two, fc1_weight, precision=HIGHEST) + bias_fc1)
    activated = low(jax.nn.gelu(pre_act, approximate=False))
    mlp_out = low_back(jnp.einsum('isf,fd->isd', activated, fc2_weight, precision=HIGHEST) + bias_fc2)
    return residual + mlp_scale * mlp_out

def reference(tokens, cotangent, ln1_gain, ln1_bias, w_qkv, qv_bias, w_out, out_bias, scale_attn, ln2_gain, ln2_bias, w_fc1, fc1_bias, w_fc2, fc2_bias, scale_mlp):
    given = (ln1_gain, ln1_bias, w_qkv, qv_bias, w_out, out_bias, scale_attn, ln2_gain, ln2_bias, w_fc1, fc1_bias, w_fc2, fc2_bias, scale_mlp)
    params = [member.astype(jnp.float32) for member in given]
    params[10] = params[10].reshape(SECTIONS, FF)
    first_params = tuple((member[0] for member in params))
    second_params = tuple((member[1] for member in params))
    zero_first = tuple((jnp.zeros_like(member) for member in first_params))
    zero_second = tuple((jnp.zeros_like(member) for member in second_params))

    def micro_step(totals, inputs_pair):
        image_rows, cotan_in = inputs_pair
        middle, back_first = jax.vjp(apply_block, image_rows.astype(jnp.float32), first_params)
        middle_low = middle.astype(jnp.bfloat16)
        final, back_second = jax.vjp(apply_block, middle_low.astype(jnp.float32), second_params)
        grad_middle, grads_second = back_second(cotan_in.astype(jnp.float32))
        grad_middle_low = grad_middle.astype(jnp.bfloat16)
        grad_start, grads_first = back_first(grad_middle_low.astype(jnp.float32))
        new_first = tuple((left + right for left, right in zip(totals[0], grads_first)))
        new_second = tuple((left + right for left, right in zip(totals[1], grads_second)))
        return ((new_first, new_second), (middle_low, final.astype(jnp.bfloat16), grad_start.astype(jnp.bfloat16), grad_middle_low))
    totals, outputs = lax.scan(micro_step, (zero_first, zero_second), (tokens, cotangent))
    middles, finals, grad_starts, grad_middles = outputs
    block_out = jnp.stack([middles, finals])
    input_grads = jnp.stack([grad_starts, grad_middles])
    stacked = [jnp.stack([left, right]) for left, right in zip(totals[0], totals[1])]
    stacked[10] = stacked[10].reshape(fc1_bias.shape)
    return (block_out, input_grads, stacked[0], stacked[1], stacked[2], stacked[3], stacked[4], stacked[5], stacked[6], stacked[7], stacked[8], stacked[9], stacked[10], stacked[11], stacked[12], stacked[13])
```

```python
from functools import partial

import jax
import jax.numpy as jnp
from jax import lax
from jax.experimental import pallas as pl
from jax.experimental.pallas import tpu as pltpu
from jax.sharding import PartitionSpec as P

EPSILON = 1e-06
BF = jnp.bfloat16
F32 = jnp.float32
MIB = 1 << 20

LN1_G, LN1_B, OUT_B, SC_ATTN, LN2_G, LN2_B, FC2_B, SC_MLP = range(8)


def dot(a, b):
    return lax.dot_general(a, b, (((1,), (0,)), ((), ())), preferred_element_type=F32)


def dot_bt(a, b):
    return lax.dot_general(a, b, (((1,), (1,)), ((), ())), preferred_element_type=F32)


def dot_at(a, b):
    return lax.dot_general(a, b, (((0,), (0,)), ((), ())), preferred_element_type=F32)


def turn(v):
    return v.astype(F32).T


def params(limit, grid=0):
    return pltpu.CompilerParams(
        vmem_limit_bytes=limit * MIB,
        dimension_semantics=("arbitrary",) * grid if grid else None,
    )


def cost(flops, nbytes, trans=0):
    return pl.CostEstimate(flops=int(flops), bytes_accessed=int(nbytes), transcendentals=int(trans))


def sds(shape, dtype):
    return jax.ShapeDtypeStruct(shape, dtype)


def core_swap(v):
    count = lax.axis_size("tensor")
    return lax.ppermute(v, "tensor", [(i, i ^ 1) for i in range(count)])


def from_chip(v, step):
    count = lax.axis_size("tensor")
    chips = count // 2
    pairs = [(((i // 2 + step) % chips) * 2 + i % 2, i) for i in range(count)]
    return lax.ppermute(v, "tensor", pairs)


def gather_tokens(own):
    chips = lax.axis_size("tensor") // 2
    chunks = [(own, core_swap(own))]
    for step in range(1, chips):
        same = from_chip(own, step)
        chunks.append((same, core_swap(same)))
    return chunks


def scatter_tokens(parts):
    chips = len(parts)
    terms = []
    for step in range(1, chips):
        same, other = parts[step]
        both = (same.astype(F32) + core_swap(other).astype(F32)).astype(BF)
        terms.append(from_chip(both, chips - step))
    terms.append(core_swap(parts[0][1]))
    return [parts[0][0]] + terms


def swap_section(v):
    return lax.ppermute(v, "section", [(0, 1), (1, 0)])


def split_gather(w, first):
    rows = w.shape[0]
    low, high = w[: rows // 2], w[rows // 2 :]
    kept = jnp.where(first, low, high)
    came = swap_section(jnp.where(first, high, low))
    halves = (jnp.where(first, kept, came), jnp.where(first, came, kept))
    return [lax.all_gather(h, ("dp", "section"), axis=0, tiled=True) for h in halves]


def scatter_sum(g):
    return lax.psum_scatter(g, ("dp", "section"), scatter_dimension=0, tiled=True)


def standardize(v):
    centred = v - jnp.mean(v, axis=-1, keepdims=True)
    var = jnp.mean(centred * centred, axis=-1, keepdims=True)
    scale = lax.rsqrt(var + EPSILON)
    return centred * scale, scale


def norm_of(v, vec, gain, shift):
    return (standardize(v)[0] * vec[gain : gain + 1, :] + vec[shift : shift + 1, :]).astype(BF)


def norm_back(v, grad, gain):
    xh, scale = standardize(v)
    dxh = grad * gain
    inner = jnp.mean(dxh * xh, axis=-1, keepdims=True)
    out = scale * (dxh - jnp.mean(dxh, axis=-1, keepdims=True) - xh * inner)
    return out, grad * xh


def total(refs):
    out = refs[0][...].astype(F32)
    for ref in refs[1:]:
        out = out + ref[...].astype(F32)
    return out


def add_rows(ref, rows):
    block = jnp.concatenate(
        [jnp.sum(r, axis=0, keepdims=True) for r in rows], axis=0
    )

    @pl.when(pl.program_id(0) == 0)
    def _():
        ref[...] = jnp.zeros_like(ref)

    ref[: len(rows), :] += block


def rowwise(body, row_ins, fulls, row_outs, sums, name):
    rows, width = row_ins[0].shape
    step = min(64, rows)
    row = lambda i: (i, 0)
    whole = lambda i: (0, 0)
    in_specs = [pl.BlockSpec((step, width), row) for _ in row_ins]
    in_specs += [pl.BlockSpec(f.shape, whole) for f in fulls]
    out_specs = [pl.BlockSpec((step, width), row) for _ in row_outs]
    out_specs += [pl.BlockSpec((8, width), whole) for _ in range(sums)]
    out_shape = [sds((rows, width), d) for d in row_outs] + [sds((8, width), F32)] * sums
    nbytes = sum(a.size * a.dtype.itemsize for a in row_ins) + sum(
        rows * width * jnp.dtype(d).itemsize for d in row_outs
    )
    return pl.pallas_call(
        body,
        grid=(rows // step,),
        in_specs=in_specs,
        out_specs=out_specs,
        out_shape=out_shape,
        compiler_params=params(16, 1),
        cost_estimate=cost(20 * rows * width, nbytes),
        name=name,
    )(*row_ins, *fulls)


def norm_first(x, vec):
    def body(x_ref, vec_ref, out_ref):
        out_ref[...] = norm_of(x_ref[...].astype(F32), vec_ref[...], LN1_G, LN1_B)

    return rowwise(body, [x], [vec], [BF], 0, "norm_first")[0]


def after_attention(x, terms, vec):
    count = len(terms)

    def body(*refs):
        x_ref, term_refs, vec_ref = refs[0], refs[1 : 1 + count], refs[1 + count]
        att_ref, res_ref, norm_ref = refs[2 + count :]
        v = vec_ref[...]
        attended = total(term_refs) + v[OUT_B : OUT_B + 1, :]
        residual = x_ref[...].astype(F32) + v[SC_ATTN : SC_ATTN + 1, :] * attended
        att_ref[...] = attended.astype(BF)
        res_ref[...] = residual
        norm_ref[...] = norm_of(residual, v, LN2_G, LN2_B)

    return rowwise(body, [x, *terms], [vec], [BF, F32, BF], 0, "after_attention")


def after_mlp(residual, terms, vec, vec_next):
    count = len(terms)

    def body(*refs):
        res_ref, term_refs = refs[0], refs[1 : 1 + count]
        vec_ref, next_ref, mlp_ref, y_ref, norm_ref = refs[1 + count :]
        v = vec_ref[...]
        mlp = total(term_refs) + v[FC2_B : FC2_B + 1, :]
        y = (res_ref[...] + v[SC_MLP : SC_MLP + 1, :] * mlp).astype(BF)
        mlp_ref[...] = mlp.astype(BF)
        y_ref[...] = y
        norm_ref[...] = norm_of(y.astype(F32), next_ref[...], LN1_G, LN1_B)

    return rowwise(body, [residual, *terms], [vec, vec_next], [BF, BF, BF], 0, "after_mlp")


def last_output(residual, terms, grad, vec):
    count = len(terms)

    def body(*refs):
        res_ref, term_refs = refs[0], refs[1 : 1 + count]
        grad_ref, vec_ref, y_ref, sum_ref = refs[1 + count :]
        v = vec_ref[...]
        mlp = total(term_refs) + v[FC2_B : FC2_B + 1, :]
        y_ref[...] = (res_ref[...] + v[SC_MLP : SC_MLP + 1, :] * mlp).astype(BF)
        add_rows(sum_ref, [grad_ref[...].astype(F32) * mlp])

    return rowwise(body, [residual, *terms, grad], [vec], [BF], 1, "last_output")


def start_back(grad, vec):
    def body(grad_ref, vec_ref, out_ref, sum_ref):
        low = (vec_ref[...][SC_MLP : SC_MLP + 1, :] * grad_ref[...].astype(F32)).astype(BF)
        out_ref[...] = low
        add_rows(sum_ref, [low.astype(F32)])

    return rowwise(body, [grad], [vec], [BF], 1, "start_back")


def back_second(grad, residual, attended, terms, vec):
    count = len(terms)

    def body(*refs):
        grad_ref, res_ref, att_ref = refs[:3]
        term_refs = refs[3 : 3 + count]
        vec_ref, dres_ref, low_ref, sum_ref = refs[3 + count :]
        v = vec_ref[...]
        dn = total(term_refs)
        back, dgain = norm_back(res_ref[...], dn, v[LN2_G : LN2_G + 1, :])
        dres = grad_ref[...].astype(F32) + back
        low = (v[SC_ATTN : SC_ATTN + 1, :] * dres).astype(BF)
        dres_ref[...] = dres
        low_ref[...] = low
        add_rows(sum_ref, [dgain, dn, dres * att_ref[...].astype(F32), low.astype(F32)])

    return rowwise(
        body, [grad, residual, attended, *terms], [vec], [F32, BF], 1, "back_second"
    )


def back_first(dres, x, terms, vec, mlp_below=None, vec_below=None):
    count = len(terms)
    below = mlp_below is not None

    def body(*refs):
        dres_ref, x_ref = refs[:2]
        term_refs = refs[2 : 2 + count]
        rest = refs[2 + count :]
        if below:
            mlp_ref, vec_ref, under_ref, dx_ref, low_ref, sum_ref = rest
        else:
            vec_ref, dx_ref, sum_ref = rest
        v = vec_ref[...]
        dn = total(term_refs)
        back, dgain = norm_back(x_ref[...].astype(F32), dn, v[LN1_G : LN1_G + 1, :])
        dx = (dres_ref[...] + back).astype(BF)
        dx_ref[...] = dx
        rows = [dgain, dn]
        if below:
            wide = dx.astype(F32)
            low = (under_ref[...][SC_MLP : SC_MLP + 1, :] * wide).astype(BF)
            low_ref[...] = low
            rows += [wide * mlp_ref[...].astype(F32), low.astype(F32)]
        add_rows(sum_ref, rows)

    row_ins = [dres, x, *terms] + ([mlp_below] if below else [])
    fulls = [vec] + ([vec_below] if below else [])
    return rowwise(body, row_ins, fulls, [BF, BF] if below else [BF], 1, "back_first")


def project_qkv(pair, weight, bias):
    rows, width = pair[0].shape
    cols = weight.shape[1]

    def body(a_ref, b_ref, w_ref, bias_ref, out_ref):
        w = w_ref[...]
        shift = bias_ref[...]
        out_ref[:rows, :] = (dot(a_ref[...], w) + shift).astype(BF)
        out_ref[rows:, :] = (dot(b_ref[...], w) + shift).astype(BF)

    return pl.pallas_call(
        body,
        out_shape=sds((2 * rows, cols), BF),
        compiler_params=params(24),
        cost_estimate=cost(4 * rows * width * cols, 2 * (2 * rows * (width + cols) + width * cols)),
        name="project_qkv",
    )(*pair, weight, bias)


def head_rows(v, head, size):
    rows = lax.broadcasted_iota(jnp.int32, v.shape, 0)
    return jnp.where(rows // size == head, v, jnp.zeros_like(v))


def head_cols(v, head, size):
    cols = lax.broadcasted_iota(jnp.int32, v.shape, 1)
    return jnp.where(cols // size == head, v, jnp.zeros_like(v))


def attention(packed, out_weight, size):
    chips = len(packed)
    span = packed[0].shape[0]
    half = span // 2
    width = packed[0].shape[1] // 3
    seq = chips * span
    heads = width // size
    blocks, _, part = out_weight.shape
    model = blocks * part
    step = min(256, seq)
    score = size**-0.5

    def body(*refs):
        in_refs, w_ref = refs[:chips], refs[chips]
        head_refs = refs[chips + 1 : 2 * chips + 1]
        lse_ref = refs[2 * chips + 1]
        part_refs = refs[2 * chips + 2 : 4 * chips + 2]
        k_ref, qt_ref, vt_ref, ot_ref = refs[4 * chips + 2 :]
        for c in range(chips):
            at = slice(c * span, (c + 1) * span)
            k_ref[at, :] = in_refs[c][:, width : 2 * width]
            qt_ref[:, at] = (turn(in_refs[c][:, :width]) * score).astype(BF)
            vt_ref[:, at] = turn(in_refs[c][:, 2 * width :]).astype(BF)

        def one(i, carry):
            at = pl.ds(pl.multiple_of(i * step, step), step)
            q = qt_ref[:, at]
            for h in range(heads):
                rows = slice(h * size, (h + 1) * size)
                s = dot(k_ref[...], head_rows(q, h, size))
                top = jnp.max(s, axis=0, keepdims=True)
                p = jnp.exp(s - top)
                norm = jnp.sum(p, axis=0, keepdims=True)
                o = dot(vt_ref[rows, :], p.astype(BF))
                ot_ref[rows, at] = o / norm
                lse_ref[h : h + 1, at] = top + jnp.log(norm)
            return carry

        lax.fori_loop(0, seq // step, one, 0)
        for c in range(chips):
            at = slice(c * span, (c + 1) * span)
            o = ot_ref[:, at].T.astype(BF)
            head_refs[c][...] = o
            for z in range(blocks):
                cols = slice(z * part, (z + 1) * part)
                term = dot(o, w_ref[z]).astype(BF)
                part_refs[2 * c][:, cols] = term[:half]
                part_refs[2 * c + 1][:, cols] = term[half:]

    out = pl.pallas_call(
        body,
        out_shape=[sds((span, width), BF)] * chips
        + [sds((heads, seq), F32)]
        + [sds((half, model), BF)] * (2 * chips),
        scratch_shapes=[
            pltpu.VMEM((seq, width), BF),
            pltpu.VMEM((width, seq), BF),
            pltpu.VMEM((width, seq), BF),
            pltpu.VMEM((width, seq), F32),
        ],
        compiler_params=params(32),
        cost_estimate=cost(
            16 * seq * seq * width, 2 * seq * (4 * width + model), heads * seq * seq
        ),
        name="attention",
    )(*packed, out_weight)
    parts = out[chips + 1 :]
    return out[:chips], out[chips], [(parts[2 * c], parts[2 * c + 1]) for c in range(chips)]


def attention_back(packed, heads_kept, lse, datt, out_weight, qkv_weight, size):
    chips = len(packed)
    span = packed[0].shape[0]
    half = span // 2
    width = packed[0].shape[1] // 3
    seq = chips * span
    heads = width // size
    blocks, _, part = out_weight.shape
    model = blocks * part
    step = min(256, seq)
    score = size**-0.5

    def body(*refs):
        at = 0

        def take(count):
            nonlocal at
            at += count
            return refs[at - count : at]

        in_refs, kept_refs = take(chips), take(chips)
        (lse_ref,) = take(1)
        datt_refs = take(2 * chips)
        wo_ref, wq_ref = take(2)
        dqkv_refs = take(chips)
        part_refs = take(2 * chips)
        (sum_ref,) = take(1)
        k_ref, v_ref, kt_ref, qt_ref, q_ref, do_ref, dot_ref = take(7)
        inner_ref, p_ref, ds_ref, dk_ref, dv_ref, dqt_ref = take(6)
        for c in range(chips):
            rows = slice(c * span, (c + 1) * span)
            q = in_refs[c][:, :width].astype(F32) * score
            k = in_refs[c][:, width : 2 * width]
            q_ref[rows, :] = q.astype(BF)
            qt_ref[:, rows] = q.T.astype(BF)
            k_ref[rows, :] = k
            kt_ref[:, rows] = turn(k).astype(BF)
            v_ref[rows, :] = in_refs[c][:, 2 * width :]
            for b in range(2):
                grad = datt_refs[2 * c + b]
                d = dot_bt(grad[:, :part], wo_ref[0])
                for z in range(1, blocks):
                    d = d + dot_bt(grad[:, z * part : (z + 1) * part], wo_ref[z])
                d = d.astype(BF)
                here = slice(c * span + b * half, c * span + (b + 1) * half)
                do_ref[here, :] = d
                dt = turn(d)
                dot_ref[:, here] = dt.astype(BF)
                ot = turn(kept_refs[c][b * half : (b + 1) * half, :])
                prod = dt * ot
                for h in range(heads):
                    inner_ref[h : h + 1, here] = jnp.sum(
                        prod[h * size : (h + 1) * size, :], axis=0, keepdims=True
                    )

        def one(i, carry):
            at = pl.ds(pl.multiple_of(i * step, step), step)
            qt = qt_ref[:, at]
            dot_t = dot_ref[:, at]
            q = q_ref[at, :]
            do = do_ref[at, :]
            for h in range(heads):
                rows = slice(h * size, (h + 1) * size)
                cols = slice(h * step, (h + 1) * step)
                s = dot(k_ref[...], head_rows(qt, h, size))
                p = jnp.exp(s - lse_ref[h : h + 1, at])
                dp = dot(v_ref[...], head_rows(dot_t, h, size))
                ds = (p * (dp - inner_ref[h : h + 1, at])).astype(BF)
                p_ref[:, cols] = p.astype(BF)
                ds_ref[:, cols] = ds
                dqt_ref[rows, at] = dot(kt_ref[rows, :], ds) * score
            dv = dot(p_ref[...], jnp.concatenate([head_cols(do, h, size) for h in range(heads)], 0))
            dk = dot(ds_ref[...], jnp.concatenate([head_cols(q, h, size) for h in range(heads)], 0))

            @pl.when(i == 0)
            def _():
                dv_ref[...] = dv
                dk_ref[...] = dk

            @pl.when(i > 0)
            def _():
                dv_ref[...] += dv
                dk_ref[...] += dk

            return carry

        lax.fori_loop(0, seq // step, one, 0)
        for c in range(chips):
            rows = slice(c * span, (c + 1) * span)
            out = dqkv_refs[c]
            out[:, :width] = dqt_ref[:, rows].T.astype(BF)
            out[:, width : 2 * width] = dk_ref[rows, :].astype(BF)
            out[:, 2 * width :] = dv_ref[rows, :].astype(BF)
            d = out[...]
            sums = jnp.sum(d.astype(F32), axis=0, keepdims=True)
            if c == 0:
                sum_ref[...] = sums
            else:
                sum_ref[...] += sums
            for j in range(0, model, part):
                term = dot_bt(d, wq_ref[j : j + part, :]).astype(BF)
                part_refs[2 * c][:, j : j + part] = term[:half]
                part_refs[2 * c + 1][:, j : j + part] = term[half:]

    flat = [g for pair in datt for g in pair]
    out = pl.pallas_call(
        body,
        out_shape=[sds((span, 3 * width), BF)] * chips
        + [sds((half, model), BF)] * (2 * chips)
        + [sds((1, 3 * width), F32)],
        scratch_shapes=[
            pltpu.VMEM((seq, width), BF),
            pltpu.VMEM((seq, width), BF),
            pltpu.VMEM((width, seq), BF),
            pltpu.VMEM((width, seq), BF),
            pltpu.VMEM((seq, width), BF),
            pltpu.VMEM((seq, width), BF),
            pltpu.VMEM((width, seq), BF),
            pltpu.VMEM((heads, seq), F32),
            pltpu.VMEM((seq, heads * step), BF),
            pltpu.VMEM((seq, heads * step), BF),
            pltpu.VMEM((seq, width), F32),
            pltpu.VMEM((seq, width), F32),
            pltpu.VMEM((width, seq), F32),
        ],
        compiler_params=params(44),
        cost_estimate=cost(
            40 * seq * seq * width, 2 * seq * (8 * width + 2 * model), heads * seq * seq
        ),
        name="attention_back",
    )(*packed, *heads_kept, lse, *flat, out_weight, qkv_weight)
    parts = out[chips : 3 * chips]
    return (
        out[:chips],
        [(parts[2 * c], parts[2 * c + 1]) for c in range(chips)],
        out[3 * chips],
    )


def gelu_both(x):
    away = jnp.abs(x)
    t = 1.0 / (1.0 + (0.3275911 * 0.5**0.5) * away)
    bell = jnp.exp(-0.5 * (x * x))
    poly = t * (
        0.127414796
        + t * (-0.142248368 + t * (0.7107068705 + t * (-0.7265760135 + t * 0.5307027145)))
    )
    tail = poly * bell
    phi = jnp.where(x >= 0, 1.0 - tail, tail)
    return x * phi, phi + x * (bell * 0.3989422804014327)


def mlp_call(body, pairs, extra, w1, w2, bias, outs, parts, name):
    rows, model = pairs[0].shape
    units = w1.shape[1]
    blocks, _, part = w2.shape
    step = min(256, units)
    whole = lambda j: (0, 0)
    cols = lambda j: (0, j)
    in_specs = [pl.BlockSpec((rows, model), whole) for _ in pairs]
    in_specs += [pl.BlockSpec((2 * rows, step), cols) for _ in extra]
    in_specs += [
        pl.BlockSpec((model, step), cols),
        pl.BlockSpec((blocks, step, part), lambda j: (0, j, 0)),
        pl.BlockSpec((1, step), cols),
    ]
    out_specs = [pl.BlockSpec((2 * rows, step), cols) for _ in outs]
    out_specs += [pl.BlockSpec((1, step), cols)]
    out_specs += [pl.BlockSpec((rows, model), whole)] * (2 * parts)
    out_shape = [sds((2 * rows, units), d) for d in outs] + [sds((1, units), F32)]
    out_shape += [sds((rows, model), BF)] * (2 * parts)
    count = len(pairs) // 2
    return pl.pallas_call(
        body,
        grid=(units // step,),
        in_specs=in_specs,
        out_specs=out_specs,
        out_shape=out_shape,
        scratch_shapes=[pltpu.VMEM((2 * rows, model), BF)] * count
        + [pltpu.VMEM((2 * rows, model), F32)] * parts,
        compiler_params=params(40, 1),
        cost_estimate=cost(
            8 * count * rows * model * units,
            4 * model * units + 4 * rows * (model + units) * (count + 1),
        ),
        name=name,
    )(*pairs, *extra, w1, w2, bias)


def join(dst, low, high):
    rows = low.shape[0]

    @pl.when(pl.program_id(0) == 0)
    def _():
        dst[:rows, :] = low[...]
        dst[rows:, :] = high[...]


def add_up(acc, j, cols, term):
    @pl.when(j == 0)
    def _():
        acc[:, cols] = term

    @pl.when(j > 0)
    def _():
        acc[:, cols] += term


def finish(acc, low, high):
    rows = low.shape[0]

    @pl.when(pl.program_id(0) == pl.num_programs(0) - 1)
    def _():
        low[...] = acc[:rows, :].astype(BF)
        high[...] = acc[rows:, :].astype(BF)


def forward_units(x, acc, w1_ref, w2_ref, bias_ref, act_ref):
    j = pl.program_id(0)
    part = w2_ref.shape[2]
    pre = dot(x[...], w1_ref[...]) + bias_ref[...]
    act, slope = gelu_both(pre)
    act = act.astype(BF)
    act_ref[...] = act
    for z in range(w2_ref.shape[0]):
        add_up(acc, j, slice(z * part, (z + 1) * part), dot(act, w2_ref[z]))
    return slope


def back_units(g, acc, w1_ref, w2_ref, slope, dpre_ref, sum_ref):
    j = pl.program_id(0)
    part = w2_ref.shape[2]
    d = dot_bt(g[:, :part], w2_ref[0])
    for z in range(1, w2_ref.shape[0]):
        d = d + dot_bt(g[:, z * part : (z + 1) * part], w2_ref[z])
    d = (d * slope).astype(BF)
    dpre_ref[...] = d
    sum_ref[...] = jnp.sum(d.astype(F32), axis=0, keepdims=True)
    for m in range(0, w1_ref.shape[0], part):
        add_up(acc, j, slice(m, m + part), dot_bt(d, w1_ref[m : m + part, :]))


def mlp_forward(pair, w1, w2, bias):
    def body(a, b, w1_ref, w2_ref, bias_ref, act_ref, slope_ref, sum_ref, lo, hi, x, acc):
        join(x, a, b)
        slope = forward_units(x, acc, w1_ref, w2_ref, bias_ref, act_ref)
        slope_ref[...] = slope.astype(BF)
        sum_ref[...] = jnp.zeros_like(sum_ref)
        finish(acc, lo, hi)

    act, slope, _, lo, hi = mlp_call(body, pair, [], w1, w2, bias, [BF, BF], 1, "mlp_forward")
    return act, slope, (lo, hi)


def mlp_backward(pair, slope, w1, w2, bias):
    def body(a, b, slope_ref, w1_ref, w2_ref, bias_ref, dpre_ref, sum_ref, lo, hi, g, acc):
        join(g, a, b)
        back_units(g, acc, w1_ref, w2_ref, slope_ref[...].astype(F32), dpre_ref, sum_ref)
        finish(acc, lo, hi)

    dpre, sums, lo, hi = mlp_call(body, pair, [slope], w1, w2, bias, [BF], 1, "mlp_backward")
    return dpre, sums, (lo, hi)


def mlp_both(pair, grads, w1, w2, bias):
    def body(
        a, b, c, d, w1_ref, w2_ref, bias_ref, act_ref, dpre_ref, sum_ref,
        lo, hi, blo, bhi, x, g, acc, back,
    ):
        join(x, a, b)
        join(g, c, d)
        slope = forward_units(x, acc, w1_ref, w2_ref, bias_ref, act_ref)
        back_units(g, back, w1_ref, w2_ref, slope, dpre_ref, sum_ref)
        finish(acc, lo, hi)
        finish(back, blo, bhi)

    act, dpre, sums, lo, hi, blo, bhi = mlp_call(
        body, [*pair, *grads], [], w1, w2, bias, [BF, BF], 2, "mlp_both"
    )
    return act, dpre, sums, (lo, hi), (blo, bhi)


def weight_grad(left, right, blocks, name):
    many, few = (left, right) if len(left) > len(right) else (right, left)
    flip = many is right
    tokens = sum(a.shape[0] for a in left)
    rows, cols = left[0].shape[1], right[0].shape[1]
    step = min(256, rows)
    count = len(left)

    def body(*refs):
        lefts, rights, out = refs[:count], refs[count:-1], refs[-1]
        acc = None
        ratio = len(many) // len(few)
        for i in range(len(many)):
            size = many[i].shape[0]
            here = slice((i % ratio) * size, (i % ratio + 1) * size)
            if flip:
                term = dot_at(lefts[i // ratio][here, :], rights[i][...])
            else:
                term = dot_at(lefts[i][...], rights[i // ratio][here, :])
            acc = term if acc is None else acc + term
        acc = acc.astype(BF)
        if blocks:
            part = cols // blocks
            for z in range(blocks):
                out[z] = acc[:, z * part : (z + 1) * part]
        else:
            out[...] = acc

    if blocks:
        out_spec = pl.BlockSpec((blocks, step, cols // blocks), lambda i: (0, i, 0))
        shape = (blocks, rows, cols // blocks)
    else:
        out_spec = pl.BlockSpec((step, cols), lambda i: (i, 0))
        shape = (rows, cols)
    out = pl.pallas_call(
        body,
        grid=(rows // step,),
        in_specs=[pl.BlockSpec((a.shape[0], step), lambda i: (0, i)) for a in left]
        + [pl.BlockSpec(b.shape, lambda i: (0, 0)) for b in right],
        out_specs=out_spec,
        out_shape=sds(shape, BF),
        compiler_params=params(32, 1),
        cost_estimate=cost(
            2 * tokens * rows * cols, 2 * (tokens * (rows + cols) + rows * cols)
        ),
        name=name,
    )(*left, *right)
    return out.reshape(-1, out.shape[-1])


def pieces(chunks):
    return [p for pair in chunks for p in pair]


def shards(
    tokens, cotangent, ln1_gain, ln1_bias, w_qkv, qv_bias, w_out, out_bias, scale_attn,
    ln2_gain, ln2_bias, w_fc1, fc1_bias, w_fc2, fc2_bias, scale_mlp,
):
    side = lax.axis_index("section")
    first = side == 0
    dp = lax.axis_size("dp")
    here = lax.axis_index("dp")
    count = lax.axis_size("tensor")
    place = lax.axis_index("tensor")
    rows, model = tokens.shape[2:]
    heads = qv_bias.shape[1]
    size = qv_bias.shape[2] * dp // 2
    width = heads * size
    units = w_fc1.shape[2]
    part = model // dp

    x0 = lax.dynamic_index_in_dim(tokens, side, 0, keepdims=False).reshape(rows, model)
    grad_top = lax.dynamic_index_in_dim(cotangent, side, 0, keepdims=False).reshape(rows, model)

    vectors = (ln1_gain, ln1_bias, out_bias, scale_attn, ln2_gain, ln2_bias, fc2_bias, scale_mlp)
    packed = jnp.concatenate(
        [v.reshape(-1) for v in vectors] + [fc1_bias.reshape(-1), qv_bias.reshape(-1)]
    )
    small = lax.all_gather(packed, ("section", "dp"), axis=0).reshape(2, dp, -1).astype(F32)
    cut = 8 * part
    vecs = small[:, :, :cut].reshape(2, dp, 8, part).swapaxes(1, 2).reshape(2, 8, model)
    bias_fc1 = small[:, :, cut : cut + units // dp].reshape(2, 1, units)
    qv = small[:, :, cut + units // dp :].reshape(2, dp, heads, -1).swapaxes(1, 2)
    qv = qv.reshape(2, heads, 2, size)
    bias_qkv = jnp.stack([qv[:, :, 0], jnp.zeros_like(qv[:, :, 0]), qv[:, :, 1]], axis=1)
    bias_qkv = bias_qkv.reshape(2, 1, 3 * width)
    vecs = (vecs[0], vecs[1])

    own_qkv = w_qkv.reshape(part, heads, 3, size).swapaxes(1, 2).reshape(part, 3 * width)
    wq = split_gather(own_qkv, first)
    wo = [w.reshape(dp, width, part) for w in split_gather(w_out[0], first)]
    w1 = split_gather(w_fc1[0], first)
    w2 = [w.reshape(dp, units, part) for w in split_gather(w_fc2[0], first)]

    def front(x, norm, s):
        chunks = gather_tokens(norm)
        qkv = [project_qkv(pair, wq[s], bias_qkv[s]) for pair in chunks]
        kept, lse, parts = attention(qkv, wo[s], size)
        terms = scatter_tokens(parts)
        attended, residual, norm2 = after_attention(x, terms, vecs[s])
        return chunks, qkv, kept, lse, attended, residual, gather_tokens(norm2)

    norm_chunks0, qkv0, kept0, lse0, attended0, residual0, second0 = front(
        x0, norm_first(x0, vecs[0]), 0
    )
    mlp0 = [mlp_forward(pair, w1[0], w2[0], bias_fc1[0]) for pair in second0]
    mlp_out0, y0, norm1 = after_mlp(
        residual0, scatter_tokens([m[2] for m in mlp0]), vecs[0], vecs[1]
    )

    norm_chunks1, qkv1, kept1, lse1, attended1, residual1, second1 = front(y0, norm1, 1)
    low1, sums_fc2_1 = start_back(grad_top, vecs[1])
    grads1 = gather_tokens(low1)
    mlp1 = [
        mlp_both(pair, grad, w1[1], w2[1], bias_fc1[1]) for pair, grad in zip(second1, grads1)
    ]
    y1, sums_sc_1 = last_output(
        residual1, scatter_tokens([m[3] for m in mlp1]), grad_top, vecs[1]
    )

    def attention_part(s, grad, residual, attended, terms, qkv, kept, lse, chunks, second, dpre, act, grads):
        dres, low, sums = back_second(grad, residual, attended, terms, vecs[s])
        datt = gather_tokens(low)
        g_fc1 = scatter_sum(weight_grad(pieces(second), dpre, 0, "grad_fc1"))
        g_fc2 = scatter_sum(weight_grad(act, pieces(grads), dp, "grad_fc2"))
        dqkv, parts, qkv_sums = attention_back(qkv, kept, lse, datt, wo[s], wq[s], size)
        back_terms = scatter_tokens(parts)
        g_out = scatter_sum(weight_grad(kept, pieces(datt), dp, "grad_out"))
        g_qkv = scatter_sum(weight_grad(pieces(chunks), dqkv, 0, "grad_qkv"))
        return dres, sums, back_terms, qkv_sums, (g_qkv, g_out, g_fc1, g_fc2)

    dres1, sums1, terms1, qkv_sums1, big1 = attention_part(
        1, grad_top, residual1, attended1, scatter_tokens([m[4] for m in mlp1]), qkv1, kept1,
        lse1, norm_chunks1, second1, [m[1] for m in mlp1], [m[0] for m in mlp1], grads1,
    )
    dx1, low0, edge1 = back_first(dres1, y0, terms1, vecs[1], mlp_out0, vecs[0])

    grads0 = gather_tokens(low0)
    mlp_back0 = [
        mlp_backward(pair, m[1], w1[0], w2[0], bias_fc1[0]) for pair, m in zip(grads0, mlp0)
    ]
    dres0, sums0, terms0, qkv_sums0, big0 = attention_part(
        0, dx1, residual0, attended0, scatter_tokens([m[2] for m in mlp_back0]), qkv0, kept0,
        lse0, norm_chunks0, second0, [m[0] for m in mlp_back0], [m[0] for m in mlp0], grads0,
    )
    dx0, edge0 = back_first(dres0, x0, terms0, vecs[0])

    def both(low, high):
        mine = jnp.where(first, low, high)
        came_low = lax.ppermute(low, "section", [(1, 0)])
        came_high = lax.ppermute(high, "section", [(0, 1)])
        came = jnp.where(first, came_low, came_high)
        return jnp.stack([jnp.where(first, mine, came), jnp.where(first, came, mine)])[None, :, None]

    block_out = both(y0, y1)
    input_grads = both(dx0, dx1)

    def summed(sums, edge, scale_row, bias_row, qkv_sums, unit_sums):
        block = jnp.stack(
            [edge[0], edge[1], sums[3], sums[2], sums[0], sums[1], bias_row, scale_row]
        )
        unit = jnp.concatenate([qkv_sums.reshape(-1), unit_sums.reshape(-1)])
        spread = jnp.where(
            lax.broadcasted_iota(jnp.int32, (count, 1), 0) == place, unit[None, :], 0.0
        )
        flat = jnp.concatenate([block.reshape(-1), spread.reshape(-1)])
        return lax.psum(flat, ("section", "dp", "tensor"))

    vec1 = summed(sums1, edge1, sums_sc_1[0], sums_fc2_1[0], qkv_sums1, sum(m[2] for m in mlp1))
    vec0 = summed(sums0, edge0, edge1[2], edge1[3], qkv_sums0, sum(m[1] for m in mlp_back0))
    vec = jnp.where(first, vec0, vec1)
    block = lax.dynamic_slice_in_dim(vec[: 8 * model].reshape(8, model), here * part, part, 1)
    unit = lax.dynamic_index_in_dim(
        vec[8 * model :].reshape(count, -1), place, 0, keepdims=False
    )
    bias_grad = jnp.stack(
        [unit[:width].reshape(heads, size), unit[2 * width : 3 * width].reshape(heads, size)], 1
    ).reshape(heads, 2 * size)
    bias_grad = lax.dynamic_slice_in_dim(bias_grad, here * (2 * size // dp), 2 * size // dp, 1)
    fc1_grad = lax.dynamic_slice_in_dim(unit[3 * width :], here * (units // dp), units // dp, 0)

    def owned(low, high):
        came_low = lax.ppermute(low, "section", [(1, 0)])
        came_high = lax.ppermute(high, "section", [(0, 1)])
        top = jnp.where(first, low, came_high)
        bottom = jnp.where(first, came_low, high)
        return jnp.concatenate([top, bottom], 0).astype(F32)

    g_qkv, g_out, g_fc1, g_fc2 = [owned(a, b) for a, b in zip(big0, big1)]
    g_qkv = g_qkv.reshape(part, 3, heads, size).swapaxes(1, 2).reshape(1, part, 3 * width)
    row = lambda i: block[i][None]
    return (
        block_out, input_grads, row(LN1_G), row(LN1_B), g_qkv, bias_grad[None], g_out[None],
        row(OUT_B), row(SC_ATTN), row(LN2_G), row(LN2_B), g_fc1[None],
        fc1_grad[None, None], g_fc2[None], row(FC2_B), row(SC_MLP),
    )


def solution(mesh):
    vec = P("section", "dp")
    by_row = P("section", "dp", "tensor")
    by_unit = P("section", "tensor", "dp")
    data = P(None, "dp", "tensor", None)
    split = P("section", None, "dp", "tensor", None)
    given = (
        vec, vec, by_row, by_unit, by_unit, vec, vec, vec, vec, by_row, by_unit, by_unit, vec, vec,
    )
    return jax.shard_map(
        shards,
        mesh=mesh,
        in_specs=(data, data) + given,
        out_specs=(split, split) + given,
        check_vma=False,
    )
```

```python
from functools import partial

import jax
import jax.numpy as jnp
from jax import lax
from jax.experimental import pallas as pl
from jax.experimental.pallas import tpu as pltpu
from jax.sharding import PartitionSpec as P

EPSILON = 1e-06
BF = jnp.bfloat16
F32 = jnp.float32
MIB = 1 << 20

LN1_G, LN1_B, OUT_B, SC_ATTN, LN2_G, LN2_B, FC2_B, SC_MLP = range(8)


def dot(a, b):
    return lax.dot_general(a, b, (((1,), (0,)), ((), ())), preferred_element_type=F32)


def dot_bt(a, b):
    return lax.dot_general(a, b, (((1,), (1,)), ((), ())), preferred_element_type=F32)


def dot_at(a, b):
    return lax.dot_general(a, b, (((0,), (0,)), ((), ())), preferred_element_type=F32)


def turn(v):
    return v.astype(F32).T


def params(limit, grid=0):
    return pltpu.CompilerParams(
        vmem_limit_bytes=limit * MIB,
        dimension_semantics=("arbitrary",) * grid if grid else None,
    )


def cost(flops, nbytes, trans=0):
    return pl.CostEstimate(flops=int(flops), bytes_accessed=int(nbytes), transcendentals=int(trans))


def sds(shape, dtype):
    return jax.ShapeDtypeStruct(shape, dtype)


def core_swap(v):
    count = lax.axis_size("tensor")
    return lax.ppermute(v, "tensor", [(i, i ^ 1) for i in range(count)])


def from_chip(v, step):
    count = lax.axis_size("tensor")
    chips = count // 2
    pairs = [(((i // 2 + step) % chips) * 2 + i % 2, i) for i in range(count)]
    return lax.ppermute(v, "tensor", pairs)


def gather_tokens(own):
    chips = lax.axis_size("tensor") // 2
    chunks = [(own, core_swap(own))]
    for step in range(1, chips):
        same = from_chip(own, step)
        chunks.append((same, core_swap(same)))
    return chunks


def scatter_tokens(parts):
    chips = len(parts)
    terms = []
    for step in range(1, chips):
        same, other = parts[step]
        both = (same.astype(F32) + core_swap(other).astype(F32)).astype(BF)
        terms.append(from_chip(both, chips - step))
    terms.append(core_swap(parts[0][1]))
    return [parts[0][0]] + terms


def swap_section(v):
    return lax.ppermute(v, "section", [(0, 1), (1, 0)])


def tie(v, after):
    return lax.optimization_barrier((v, after))[0]


def assemble(own, same, other, rows):
    part, cols = own.shape
    half = part // 2
    steps = len(same)
    place = jnp.stack([lax.axis_index("dp"), lax.axis_index("section")])

    def body(place_ref, own_ref, *refs):
        same_refs, other_refs = refs[:steps], refs[steps : 2 * steps]
        out_ref, sems = refs[2 * steps :]
        z, x = place_ref[0], place_ref[1]
        copies = [(own_ref, z * part, part)]
        for k in range(steps):
            base = lax.rem(z + (steps - k), steps + 1) * part
            copies.append((same_refs[k], base + x * half, half))
            copies.append((other_refs[k], base + (1 - x) * half, half))
        started = []
        for i, (ref, at, size) in enumerate(copies):
            at = pl.multiple_of(at, half)
            started.append(
                pltpu.make_async_copy(ref, out_ref.at[pl.ds(at, size), :], sems.at[i])
            )
            started[-1].start()
        for copy in started:
            copy.wait()

    hbm = pl.BlockSpec(memory_space=pl.ANY)
    return pl.pallas_call(
        body,
        in_specs=[pl.BlockSpec(memory_space=pltpu.SMEM)] + [hbm] * (1 + 2 * steps),
        out_specs=hbm,
        out_shape=sds((rows, cols), own.dtype),
        scratch_shapes=[pltpu.SemaphoreType.DMA((1 + 2 * steps,))],
        cost_estimate=cost(0, 4 * rows * cols),
        name="assemble",
    )(place, own, *same, *other)


def spread(both, side, after=None):
    count = lax.axis_size("dp")
    half = both.shape[0] // 2
    ring = [(i, (i + 1) % count) for i in range(count)]
    last = lax.dynamic_slice_in_dim(both, side * half, half, 0)
    if after is not None:
        last = tie(last, after)
    same, other = [], []
    for _ in range(count - 1):
        last = lax.ppermute(last, "dp", ring)
        same.append(last)
        other.append(swap_section(last))
    return assemble(both, same, other, both.shape[0] * count), last


def split_gather(shard, side):
    half = shard.shape[0] // 2
    own = lax.dynamic_slice_in_dim(shard, side * half, half, 0)
    return lax.all_gather(own, ("dp", "section"), axis=0, tiled=True)


def scatter_sum(g):
    return lax.psum_scatter(g, ("dp", "section"), scatter_dimension=0, tiled=True)


def standardize(v):
    centred = v - jnp.mean(v, axis=-1, keepdims=True)
    var = jnp.mean(centred * centred, axis=-1, keepdims=True)
    scale = lax.rsqrt(var + EPSILON)
    return centred * scale, scale


def norm_of(v, vec, gain, shift):
    return (standardize(v)[0] * vec[gain : gain + 1, :] + vec[shift : shift + 1, :]).astype(BF)


def norm_back(v, grad, gain):
    xh, scale = standardize(v)
    dxh = grad * gain
    inner = jnp.mean(dxh * xh, axis=-1, keepdims=True)
    out = scale * (dxh - jnp.mean(dxh, axis=-1, keepdims=True) - xh * inner)
    return out, grad * xh


def total(refs):
    out = refs[0][...].astype(F32)
    for ref in refs[1:]:
        out = out + ref[...].astype(F32)
    return out


def add_rows(ref, rows):
    block = jnp.concatenate(
        [jnp.sum(r, axis=0, keepdims=True) for r in rows], axis=0
    )

    @pl.when(pl.program_id(0) == 0)
    def _():
        ref[...] = jnp.zeros_like(ref)

    ref[: len(rows), :] += block


def rowwise(body, row_ins, fulls, row_outs, sums, name):
    rows, width = row_ins[0].shape
    step = min(64, rows)
    row = lambda i: (i, 0)
    whole = lambda i: (0, 0)
    in_specs = [pl.BlockSpec((step, width), row) for _ in row_ins]
    in_specs += [pl.BlockSpec(f.shape, whole) for f in fulls]
    out_specs = [pl.BlockSpec((step, width), row) for _ in row_outs]
    out_specs += [pl.BlockSpec((8, width), whole) for _ in range(sums)]
    out_shape = [sds((rows, width), d) for d in row_outs] + [sds((8, width), F32)] * sums
    nbytes = sum(a.size * a.dtype.itemsize for a in row_ins) + sum(
        rows * width * jnp.dtype(d).itemsize for d in row_outs
    )
    return pl.pallas_call(
        body,
        grid=(rows // step,),
        in_specs=in_specs,
        out_specs=out_specs,
        out_shape=out_shape,
        compiler_params=params(16, 1),
        cost_estimate=cost(20 * rows * width, nbytes),
        name=name,
    )(*row_ins, *fulls)


def norm_first(x, vec):
    def body(x_ref, vec_ref, out_ref):
        out_ref[...] = norm_of(x_ref[...].astype(F32), vec_ref[...], LN1_G, LN1_B)

    return rowwise(body, [x], [vec], [BF], 0, "norm_first")[0]


def after_attention(x, terms, vec):
    count = len(terms)

    def body(*refs):
        x_ref, term_refs, vec_ref = refs[0], refs[1 : 1 + count], refs[1 + count]
        att_ref, res_ref, norm_ref = refs[2 + count :]
        v = vec_ref[...]
        attended = total(term_refs) + v[OUT_B : OUT_B + 1, :]
        residual = x_ref[...].astype(F32) + v[SC_ATTN : SC_ATTN + 1, :] * attended
        att_ref[...] = attended.astype(BF)
        res_ref[...] = residual
        norm_ref[...] = norm_of(residual, v, LN2_G, LN2_B)

    return rowwise(body, [x, *terms], [vec], [BF, F32, BF], 0, "after_attention")


def after_mlp(residual, terms, vec, vec_next):
    count = len(terms)

    def body(*refs):
        res_ref, term_refs = refs[0], refs[1 : 1 + count]
        vec_ref, next_ref, mlp_ref, y_ref, norm_ref = refs[1 + count :]
        v = vec_ref[...]
        mlp = total(term_refs) + v[FC2_B : FC2_B + 1, :]
        y = (res_ref[...] + v[SC_MLP : SC_MLP + 1, :] * mlp).astype(BF)
        mlp_ref[...] = mlp.astype(BF)
        y_ref[...] = y
        norm_ref[...] = norm_of(y.astype(F32), next_ref[...], LN1_G, LN1_B)

    return rowwise(body, [residual, *terms], [vec, vec_next], [BF, BF, BF], 0, "after_mlp")


def last_output(residual, terms, grad, vec):
    count = len(terms)

    def body(*refs):
        res_ref, term_refs = refs[0], refs[1 : 1 + count]
        grad_ref, vec_ref, y_ref, sum_ref = refs[1 + count :]
        v = vec_ref[...]
        mlp = total(term_refs) + v[FC2_B : FC2_B + 1, :]
        y_ref[...] = (res_ref[...] + v[SC_MLP : SC_MLP + 1, :] * mlp).astype(BF)
        add_rows(sum_ref, [grad_ref[...].astype(F32) * mlp])

    return rowwise(body, [residual, *terms, grad], [vec], [BF], 1, "last_output")


def start_back(grad, vec):
    def body(grad_ref, vec_ref, out_ref, sum_ref):
        low = (vec_ref[...][SC_MLP : SC_MLP + 1, :] * grad_ref[...].astype(F32)).astype(BF)
        out_ref[...] = low
        add_rows(sum_ref, [low.astype(F32)])

    return rowwise(body, [grad], [vec], [BF], 1, "start_back")


def back_second(grad, residual, attended, terms, vec):
    count = len(terms)

    def body(*refs):
        grad_ref, res_ref, att_ref = refs[:3]
        term_refs = refs[3 : 3 + count]
        vec_ref, dres_ref, low_ref, sum_ref = refs[3 + count :]
        v = vec_ref[...]
        dn = total(term_refs)
        back, dgain = norm_back(res_ref[...], dn, v[LN2_G : LN2_G + 1, :])
        dres = grad_ref[...].astype(F32) + back
        low = (v[SC_ATTN : SC_ATTN + 1, :] * dres).astype(BF)
        dres_ref[...] = dres
        low_ref[...] = low
        add_rows(sum_ref, [dgain, dn, dres * att_ref[...].astype(F32), low.astype(F32)])

    return rowwise(
        body, [grad, residual, attended, *terms], [vec], [F32, BF], 1, "back_second"
    )


def back_first(dres, x, terms, vec, mlp_below=None, vec_below=None):
    count = len(terms)
    below = mlp_below is not None

    def body(*refs):
        dres_ref, x_ref = refs[:2]
        term_refs = refs[2 : 2 + count]
        rest = refs[2 + count :]
        if below:
            mlp_ref, vec_ref, under_ref, dx_ref, low_ref, sum_ref = rest
        else:
            vec_ref, dx_ref, sum_ref = rest
        v = vec_ref[...]
        dn = total(term_refs)
        back, dgain = norm_back(x_ref[...].astype(F32), dn, v[LN1_G : LN1_G + 1, :])
        dx = (dres_ref[...] + back).astype(BF)
        dx_ref[...] = dx
        rows = [dgain, dn]
        if below:
            wide = dx.astype(F32)
            low = (under_ref[...][SC_MLP : SC_MLP + 1, :] * wide).astype(BF)
            low_ref[...] = low
            rows += [wide * mlp_ref[...].astype(F32), low.astype(F32)]
        add_rows(sum_ref, rows)

    row_ins = [dres, x, *terms] + ([mlp_below] if below else [])
    fulls = [vec] + ([vec_below] if below else [])
    return rowwise(body, row_ins, fulls, [BF, BF] if below else [BF], 1, "back_first")


def project_qkv(pair, weight, bias):
    rows, width = pair[0].shape
    cols = bias.shape[1]

    def body(a_ref, b_ref, w_ref, bias_ref, out_ref):
        w = w_ref[...]
        shift = bias_ref[...]
        out_ref[:rows, :] = (dot(a_ref[...], w) + shift).astype(BF)
        out_ref[rows:, :] = (dot(b_ref[...], w) + shift).astype(BF)

    whole = lambda i: (0, 0)
    return pl.pallas_call(
        body,
        grid=(1,),
        in_specs=[
            pl.BlockSpec((rows, width), whole),
            pl.BlockSpec((rows, width), whole),
            pl.BlockSpec((width, cols), whole),
            pl.BlockSpec((1, cols), whole),
        ],
        out_specs=pl.BlockSpec((2 * rows, cols), whole),
        out_shape=sds((2 * rows, cols), BF),
        compiler_params=params(24, 1),
        cost_estimate=cost(4 * rows * width * cols, 2 * (2 * rows * (width + cols) + width * cols)),
        name="project_qkv",
    )(*pair, weight, bias)


def head_rows(v, head, size):
    rows = lax.broadcasted_iota(jnp.int32, v.shape, 0)
    return jnp.where(rows // size == head, v, jnp.zeros_like(v))


def head_cols(v, head, size):
    cols = lax.broadcasted_iota(jnp.int32, v.shape, 1)
    return jnp.where(cols // size == head, v, jnp.zeros_like(v))


def fold(v, op):
    return op(v.reshape(-1, 8, v.shape[1]), axis=0)


def attention(packed, weight, size):
    chips = len(packed)
    span = packed[0].shape[0]
    half = span // 2
    width = packed[0].shape[1] // 3
    seq = chips * span
    heads = width // size
    model = weight.shape[0]
    step = min(256, seq)
    chunk = min(128, seq)
    score = size**-0.5

    def body(*refs):
        in_refs, w_ref = refs[:chips], refs[chips]
        head_refs = refs[chips + 1 : 2 * chips + 1]
        lse_ref = refs[2 * chips + 1]
        part_refs = refs[2 * chips + 2 : 4 * chips + 2]
        k_ref, qt_ref, vt_ref, ot_ref, s_ref, p_ref = refs[4 * chips + 2 :]
        for c in range(chips):
            at = slice(c * span, (c + 1) * span)
            k_ref[at, :] = in_refs[c][:, width : 2 * width]
            qt_ref[:, at] = (turn(in_refs[c][:, :width]) * score).astype(BF)
            vt_ref[:, at] = turn(in_refs[c][:, 2 * width :]).astype(BF)

        def one(i, carry):
            at = pl.ds(pl.multiple_of(i * step, step), step)
            q = qt_ref[:, at]
            s_ref[0] = dot(k_ref[...], head_rows(q, 0, size))
            for h in range(heads):
                if h + 1 < heads:
                    s_ref[(h + 1) % 2] = dot(k_ref[...], head_rows(q, h + 1, size))
                now = h % 2
                top = fold(s_ref[now, :chunk, :], jnp.max)
                for r in range(chunk, seq, chunk):
                    top = jnp.maximum(top, fold(s_ref[now, r : r + chunk, :], jnp.max))
                top = jnp.max(top, axis=0, keepdims=True)
                norm = jnp.zeros((8, step), F32)
                for r in range(0, seq, chunk):
                    p = jnp.exp(s_ref[now, r : r + chunk, :] - top)
                    norm = norm + fold(p, jnp.sum)
                    p_ref[now, r : r + chunk, :] = p.astype(BF)
                norm = jnp.sum(norm, axis=0, keepdims=True)
                rows = slice(h * size, (h + 1) * size)
                ot_ref[rows, at] = dot(vt_ref[rows, :], p_ref[now]) / norm
                lse_ref[h : h + 1, at] = top + jnp.log(norm)
            return carry

        lax.fori_loop(0, seq // step, one, 0)
        for c in range(chips):
            at = slice(c * span, (c + 1) * span)
            o = ot_ref[:, at].T.astype(BF)
            head_refs[c][...] = o
            part_refs[2 * c][...] = dot_bt(o[:half], w_ref[...]).astype(BF)
            part_refs[2 * c + 1][...] = dot_bt(o[half:], w_ref[...]).astype(BF)

    whole = lambda i: (0, 0)
    full = lambda shape: pl.BlockSpec(shape, whole)
    out = pl.pallas_call(
        body,
        grid=(1,),
        in_specs=[full((span, 3 * width))] * chips + [pl.BlockSpec((model, width), lambda i: (0, 3))],
        out_specs=[full((span, width))] * chips
        + [full((heads, seq))]
        + [full((half, model))] * (2 * chips),
        out_shape=[sds((span, width), BF)] * chips
        + [sds((heads, seq), F32)]
        + [sds((half, model), BF)] * (2 * chips),
        scratch_shapes=[
            pltpu.VMEM((seq, width), BF),
            pltpu.VMEM((width, seq), BF),
            pltpu.VMEM((width, seq), BF),
            pltpu.VMEM((width, seq), F32),
            pltpu.VMEM((2, seq, step), F32),
            pltpu.VMEM((2, seq, step), BF),
        ],
        compiler_params=params(36, 1),
        cost_estimate=cost(
            16 * seq * seq * width, 2 * seq * (4 * width + model), heads * seq * seq
        ),
        name="attention",
    )(*packed, weight)
    parts = out[chips + 1 :]
    return out[:chips], out[chips], [(parts[2 * c], parts[2 * c + 1]) for c in range(chips)]


def attention_back(packed, heads_kept, lse, datt, weight, size):
    chips = len(packed)
    span = packed[0].shape[0]
    half = span // 2
    width = packed[0].shape[1] // 3
    seq = chips * span
    heads = width // size
    model = weight.shape[0]
    step = min(256, seq)
    chunk = min(128, seq)
    score = size**-0.5

    def body(*refs):
        at = 0

        def take(count):
            nonlocal at
            at += count
            return refs[at - count : at]

        in_refs, kept_refs = take(chips), take(chips)
        (lse_ref,) = take(1)
        datt_refs = take(2 * chips)
        (w_ref,) = take(1)
        dqkv_refs = take(chips)
        part_refs = take(2 * chips)
        (sum_ref,) = take(1)
        k_ref, v_ref, kt_ref, qt_ref, q_ref, do_ref, dot_ref = take(7)
        inner_ref, s_ref, g_ref, p_ref, ds_ref, dk_ref, dv_ref, dqt_ref = take(8)
        for c in range(chips):
            rows = slice(c * span, (c + 1) * span)
            q = in_refs[c][:, :width].astype(F32) * score
            k = in_refs[c][:, width : 2 * width]
            q_ref[rows, :] = q.astype(BF)
            qt_ref[:, rows] = q.T.astype(BF)
            k_ref[rows, :] = k
            kt_ref[:, rows] = turn(k).astype(BF)
            v_ref[rows, :] = in_refs[c][:, 2 * width :]
            for b in range(2):
                d = dot(datt_refs[2 * c + b][...], w_ref[:, 3 * width :]).astype(BF)
                here = slice(c * span + b * half, c * span + (b + 1) * half)
                do_ref[here, :] = d
                dt = turn(d)
                dot_ref[:, here] = dt.astype(BF)
                prod = dt * turn(kept_refs[c][b * half : (b + 1) * half, :])
                for h in range(heads):
                    inner_ref[h : h + 1, here] = jnp.sum(
                        prod[h * size : (h + 1) * size, :], axis=0, keepdims=True
                    )

        def one(i, carry):
            at = pl.ds(pl.multiple_of(i * step, step), step)
            qt = qt_ref[:, at]
            dot_t = dot_ref[:, at]
            q = q_ref[at, :]
            do = do_ref[at, :]

            def scores(h):
                s_ref[h % 2] = dot(k_ref[...], head_rows(qt, h, size))
                g_ref[h % 2] = dot(v_ref[...], head_rows(dot_t, h, size))

            scores(0)
            for h in range(heads):
                if h + 1 < heads:
                    scores(h + 1)
                now = h % 2
                cols = slice(h * step, (h + 1) * step)
                lse = lse_ref[h : h + 1, at]
                inner = inner_ref[h : h + 1, at]
                for r in range(0, seq, chunk):
                    p = jnp.exp(s_ref[now, r : r + chunk, :] - lse)
                    ds = p * (g_ref[now, r : r + chunk, :] - inner)
                    p_ref[r : r + chunk, cols] = p.astype(BF)
                    ds_ref[r : r + chunk, cols] = ds.astype(BF)
                rows = slice(h * size, (h + 1) * size)
                dqt_ref[rows, at] = dot(kt_ref[rows, :], ds_ref[:, cols]) * score
            dv = dot(p_ref[...], jnp.concatenate([head_cols(do, h, size) for h in range(heads)], 0))
            dk = dot(ds_ref[...], jnp.concatenate([head_cols(q, h, size) for h in range(heads)], 0))

            @pl.when(i == 0)
            def _():
                dv_ref[...] = dv
                dk_ref[...] = dk

            @pl.when(i > 0)
            def _():
                dv_ref[...] += dv
                dk_ref[...] += dk

            return carry

        lax.fori_loop(0, seq // step, one, 0)
        for c in range(chips):
            rows = slice(c * span, (c + 1) * span)
            out = dqkv_refs[c]
            out[:, :width] = dqt_ref[:, rows].T.astype(BF)
            out[:, width : 2 * width] = dk_ref[rows, :].astype(BF)
            out[:, 2 * width :] = dv_ref[rows, :].astype(BF)
            sums = jnp.sum(out[...].astype(F32), axis=0, keepdims=True)
            if c == 0:
                sum_ref[...] = sums
            else:
                sum_ref[...] += sums
            for b in range(2):
                part_refs[2 * c + b][...] = dot_bt(
                    out[b * half : (b + 1) * half, :], w_ref[:, : 3 * width]
                ).astype(BF)

    flat = [g for pair in datt for g in pair]
    whole = lambda i: (0, 0)
    full = lambda a: pl.BlockSpec(a.shape, whole)
    out_shape = (
        [sds((span, 3 * width), BF)] * chips
        + [sds((half, model), BF)] * (2 * chips)
        + [sds((1, 3 * width), F32)]
    )
    operands = (*packed, *heads_kept, lse, *flat, weight)
    out = pl.pallas_call(
        body,
        grid=(1,),
        in_specs=[full(a) for a in operands],
        out_specs=[full(a) for a in out_shape],
        out_shape=out_shape,
        scratch_shapes=[
            pltpu.VMEM((seq, width), BF),
            pltpu.VMEM((seq, width), BF),
            pltpu.VMEM((width, seq), BF),
            pltpu.VMEM((width, seq), BF),
            pltpu.VMEM((seq, width), BF),
            pltpu.VMEM((seq, width), BF),
            pltpu.VMEM((width, seq), BF),
            pltpu.VMEM((heads, seq), F32),
            pltpu.VMEM((2, seq, step), F32),
            pltpu.VMEM((2, seq, step), F32),
            pltpu.VMEM((seq, heads * step), BF),
            pltpu.VMEM((seq, heads * step), BF),
            pltpu.VMEM((seq, width), F32),
            pltpu.VMEM((seq, width), F32),
            pltpu.VMEM((width, seq), F32),
        ],
        compiler_params=params(52, 1),
        cost_estimate=cost(
            40 * seq * seq * width, 2 * seq * (8 * width + 2 * model), heads * seq * seq
        ),
        name="attention_back",
    )(*operands)
    parts = out[chips : 3 * chips]
    return (
        out[:chips],
        [(parts[2 * c], parts[2 * c + 1]) for c in range(chips)],
        out[3 * chips],
    )


def gelu_both(x):
    away = jnp.abs(x)
    t = 1.0 / (1.0 + (0.3275911 * 0.5**0.5) * away)
    bell = jnp.exp(-0.5 * (x * x))
    poly = t * (
        0.127414796
        + t * (-0.142248368 + t * (0.7107068705 + t * (-0.7265760135 + t * 0.5307027145)))
    )
    tail = poly * bell
    phi = jnp.where(x >= 0, 1.0 - tail, tail)
    return x * phi, phi + x * (bell * 0.3989422804014327)


def mlp_call(body, pairs, extra, weight, bias, outs, parts, scratch, name):
    rows, model = pairs[0].shape
    units = weight.shape[1] // 2
    step = min(256, units)
    blocks = units // step
    whole = lambda j: (0, 0)
    cols = lambda j: (0, j)
    in_specs = [pl.BlockSpec((rows, model), whole) for _ in pairs]
    in_specs += [pl.BlockSpec((2 * rows, step), cols) for _ in extra]
    in_specs += [
        pl.BlockSpec((model, step), cols),
        pl.BlockSpec((model, step), lambda j: (0, blocks + j)),
        pl.BlockSpec((1, step), cols),
    ]
    out_specs = [pl.BlockSpec((2 * rows, step), cols) for _ in outs]
    out_specs += [pl.BlockSpec((1, step), cols)]
    out_specs += [pl.BlockSpec((rows, model), whole)] * (2 * parts)
    out_shape = [sds((2 * rows, units), d) for d in outs] + [sds((1, units), F32)]
    out_shape += [sds((rows, model), BF)] * (2 * parts)
    count = len(pairs) // 2
    return pl.pallas_call(
        body,
        grid=(blocks,),
        in_specs=in_specs,
        out_specs=out_specs,
        out_shape=out_shape,
        scratch_shapes=[pltpu.VMEM((2 * rows, model), F32)] * parts
        + [pltpu.VMEM((2 * rows, step), F32)] * scratch,
        compiler_params=params(40, 1),
        cost_estimate=cost(
            8 * count * rows * model * units,
            4 * model * units + 4 * rows * (model + units) * (count + 1),
        ),
        name=name,
    )(*pairs, *extra, weight, weight, bias)


def clear(*refs):
    @pl.when(pl.program_id(0) == 0)
    def _():
        for ref in refs:
            ref[...] = jnp.zeros_like(ref)


def finish(acc, low, high):
    rows = low.shape[0]

    @pl.when(pl.program_id(0) == pl.num_programs(0) - 1)
    def _():
        low[...] = acc[:rows, :].astype(BF)
        high[...] = acc[rows:, :].astype(BF)


CHUNK = 32


def mlp_forward(pair, weight, bias):
    rows = pair[0].shape[0]

    def body(a, b, w1_ref, w2_ref, bias_ref, act_ref, slope_ref, sum_ref, lo, hi, acc, pre):
        clear(acc, sum_ref)
        shift = bias_ref[...]
        for i, x in enumerate((a, b)):
            pre[i * rows : (i + 1) * rows, :] = dot(x[...], w1_ref[...])
        for i in range(2):
            at = slice(i * rows, (i + 1) * rows)
            for r in range(i * rows, (i + 1) * rows, CHUNK):
                act, slope = gelu_both(pre[r : r + CHUNK, :] + shift)
                act_ref[r : r + CHUNK, :] = act.astype(BF)
                slope_ref[r : r + CHUNK, :] = slope.astype(BF)
            acc[at, :] += dot_bt(act_ref[at, :], w2_ref[...])
        finish(acc, lo, hi)

    act, slope, _, lo, hi = mlp_call(body, pair, [], weight, bias, [BF, BF], 1, 1, "mlp_forward")
    return act, slope, (lo, hi)


def mlp_backward(pair, slope, weight, bias):
    rows = pair[0].shape[0]

    def body(a, b, slope_ref, w1_ref, w2_ref, bias_ref, dpre_ref, sum_ref, lo, hi, acc, pre):
        clear(acc)
        for i, g in enumerate((a, b)):
            pre[i * rows : (i + 1) * rows, :] = dot(g[...], w2_ref[...])
        sums = jnp.zeros((8, bias_ref.shape[1]), F32)
        for i in range(2):
            at = slice(i * rows, (i + 1) * rows)
            for r in range(i * rows, (i + 1) * rows, CHUNK):
                d = pre[r : r + CHUNK, :] * slope_ref[r : r + CHUNK, :].astype(F32)
                d = d.astype(BF)
                dpre_ref[r : r + CHUNK, :] = d
                sums = sums + fold(d.astype(F32), jnp.sum)
            acc[at, :] += dot_bt(dpre_ref[at, :], w1_ref[...])
        sum_ref[...] = jnp.sum(sums, axis=0, keepdims=True)
        finish(acc, lo, hi)

    dpre, sums, lo, hi = mlp_call(
        body, pair, [slope], weight, bias, [BF], 1, 1, "mlp_backward"
    )
    return dpre, sums, (lo, hi)


def mlp_both(pair, grads, weight, bias):
    rows = pair[0].shape[0]

    def body(
        a, b, c, d, w1_ref, w2_ref, bias_ref, act_ref, dpre_ref, sum_ref,
        lo, hi, blo, bhi, acc, back, pre, grad,
    ):
        clear(acc, back)
        shift = bias_ref[...]
        for i, (x, g) in enumerate(((a, c), (b, d))):
            at = slice(i * rows, (i + 1) * rows)
            pre[at, :] = dot(x[...], w1_ref[...])
            grad[at, :] = dot(g[...], w2_ref[...])
        sums = jnp.zeros((8, bias_ref.shape[1]), F32)
        for i in range(2):
            at = slice(i * rows, (i + 1) * rows)
            for r in range(i * rows, (i + 1) * rows, CHUNK):
                act, slope = gelu_both(pre[r : r + CHUNK, :] + shift)
                act_ref[r : r + CHUNK, :] = act.astype(BF)
                dpre = (grad[r : r + CHUNK, :] * slope).astype(BF)
                dpre_ref[r : r + CHUNK, :] = dpre
                sums = sums + fold(dpre.astype(F32), jnp.sum)
            back[at, :] += dot_bt(dpre_ref[at, :], w1_ref[...])
            acc[at, :] += dot_bt(act_ref[at, :], w2_ref[...])
        sum_ref[...] = jnp.sum(sums, axis=0, keepdims=True)
        finish(acc, lo, hi)
        finish(back, blo, bhi)

    act, dpre, sums, lo, hi, blo, bhi = mlp_call(
        body, [*pair, *grads], [], weight, bias, [BF, BF], 2, 2, "mlp_both"
    )
    return act, dpre, sums, (lo, hi), (blo, bhi)


def weight_grads(products, name):
    model = products[0][0][0].shape[1]
    step = min(256, model)
    sizes = [(len(left), len(right), right[0].shape[1]) for left, right in products]
    cols = sum(n for _, _, n in sizes)
    tokens = sum(a.shape[0] for a in products[0][0])

    def body(*refs):
        out = refs[-1]
        at = base = 0
        for many, few, n in sizes:
            lefts, rights = refs[at : at + many], refs[at + many : at + many + few]
            at += many + few
            ratio = many // few
            acc = None
            for i in range(many):
                size = lefts[i].shape[0]
                here = slice((i % ratio) * size, (i % ratio + 1) * size)
                term = dot_at(lefts[i][...], rights[i // ratio][here, :])
                acc = term if acc is None else acc + term
            out[:, base : base + n] = acc.astype(BF)
            base += n

    specs, operands = [], []
    for left, right in products:
        specs += [pl.BlockSpec((a.shape[0], step), lambda i: (0, i)) for a in left]
        specs += [pl.BlockSpec(b.shape, lambda i: (0, 0)) for b in right]
        operands += [*left, *right]
    return pl.pallas_call(
        body,
        grid=(model // step,),
        in_specs=specs,
        out_specs=pl.BlockSpec((step, cols), lambda i: (i, 0)),
        out_shape=sds((model, cols), BF),
        compiler_params=params(40, 1),
        cost_estimate=cost(
            2 * tokens * model * cols, 2 * (tokens * (2 * model + cols) + model * cols)
        ),
        name=name,
    )(*operands)


def pieces(chunks):
    return [p for pair in chunks for p in pair]


def shards(
    tokens, cotangent, ln1_gain, ln1_bias, w_qkv, qv_bias, w_out, out_bias, scale_attn,
    ln2_gain, ln2_bias, w_fc1, fc1_bias, w_fc2, fc2_bias, scale_mlp,
):
    side = lax.axis_index("section")
    first = side == 0
    dp = lax.axis_size("dp")
    here = lax.axis_index("dp")
    chips = lax.axis_size("tensor") // 2
    rows, model = tokens.shape[2:]
    heads = qv_bias.shape[1]
    size = qv_bias.shape[2] * dp // 2
    width = heads * size
    units = w_fc1.shape[2]
    part = model // dp

    x0 = lax.dynamic_index_in_dim(tokens, side, 0, keepdims=False).reshape(rows, model)
    grad_top = lax.dynamic_index_in_dim(cotangent, side, 0, keepdims=False).reshape(rows, model)

    vectors = (ln1_gain, ln1_bias, out_bias, scale_attn, ln2_gain, ln2_bias, fc2_bias, scale_mlp)
    packed = jnp.concatenate(
        [v.reshape(-1) for v in vectors] + [fc1_bias.reshape(-1), qv_bias.reshape(-1)]
    )
    mine = lax.all_gather(packed, "dp", axis=0)
    came = swap_section(mine)
    small = jnp.stack([jnp.where(first, mine, came), jnp.where(first, came, mine)]).astype(F32)
    cut = 8 * part
    vecs = small[:, :, :cut].reshape(2, dp, 8, part).swapaxes(1, 2).reshape(2, 8, model)
    bias_fc1 = small[:, :, cut : cut + units // dp].reshape(2, 1, units)
    qv = small[:, :, cut + units // dp :].reshape(2, dp, heads, -1).swapaxes(1, 2)
    qv = qv.reshape(2, heads, 2, size)
    bias_qkv = jnp.stack([qv[:, :, 0], jnp.zeros_like(qv[:, :, 0]), qv[:, :, 1]], axis=1)
    bias_qkv = bias_qkv.reshape(2, 1, 3 * width)
    vecs = (vecs[0], vecs[1])

    own_qkv = w_qkv.reshape(part, heads, 3, size).swapaxes(1, 2).reshape(part, 3 * width)
    own_att = jnp.concatenate([own_qkv, w_out[0].T], axis=1)
    own_ff = jnp.concatenate([w_fc1[0], w_fc2[0].T], axis=1)
    came_att = swap_section(own_att)
    came_ff = swap_section(tie(own_ff, came_att))
    att0, last = spread(jnp.where(first, own_att, came_att), side)
    ff0, last = spread(jnp.where(first, own_ff, came_ff), side, last)
    att1 = split_gather(tie(jnp.where(first, came_att, own_att), last), side)
    ff1 = split_gather(tie(jnp.where(first, came_ff, own_ff), last), side)

    def front(x, norm, weight, s):
        chunks = gather_tokens(norm)
        qkv = [project_qkv(pair, weight, bias_qkv[s]) for pair in chunks]
        kept, lse, parts = attention(qkv, weight, size)
        terms = scatter_tokens(parts)
        attended, residual, norm2 = after_attention(x, terms, vecs[s])
        return chunks, qkv, kept, lse, attended, residual, gather_tokens(norm2)

    norm_chunks0, qkv0, kept0, lse0, attended0, residual0, second0 = front(
        x0, norm_first(x0, vecs[0]), att0, 0
    )
    mlp0 = [mlp_forward(pair, ff0, bias_fc1[0]) for pair in second0]
    mlp_out0, y0, norm1 = after_mlp(
        residual0, scatter_tokens([m[2] for m in mlp0]), vecs[0], vecs[1]
    )

    norm_chunks1, qkv1, kept1, lse1, attended1, residual1, second1 = front(y0, norm1, att1, 1)
    low1, sums_fc2_1 = start_back(grad_top, vecs[1])
    grads1 = gather_tokens(low1)
    mlp1 = [mlp_both(pair, grad, ff1, bias_fc1[1]) for pair, grad in zip(second1, grads1)]
    y1, sums_sc_1 = last_output(
        residual1, scatter_tokens([m[3] for m in mlp1]), grad_top, vecs[1]
    )

    def attention_part(s, weight, grad, residual, attended, terms, qkv, kept, lse, chunks, second, dpre, act, grads):
        dres, low, sums = back_second(grad, residual, attended, terms, vecs[s])
        datt = gather_tokens(low)
        g_ff = scatter_sum(
            weight_grads([(pieces(second), dpre), (pieces(grads), act)], "grad_ff")
        )
        dqkv, parts, qkv_sums = attention_back(qkv, kept, lse, datt, weight, size)
        back_terms = scatter_tokens(parts)
        g_att = scatter_sum(
            weight_grads([(pieces(chunks), dqkv), (pieces(datt), kept)], "grad_att")
        )
        return dres, sums, back_terms, qkv_sums, (g_att, g_ff)

    dres1, sums1, terms1, qkv_sums1, big1 = attention_part(
        1, att1, grad_top, residual1, attended1, scatter_tokens([m[4] for m in mlp1]), qkv1, kept1,
        lse1, norm_chunks1, second1, [m[1] for m in mlp1], [m[0] for m in mlp1], grads1,
    )
    dx1, low0, edge1 = back_first(dres1, y0, terms1, vecs[1], mlp_out0, vecs[0])

    grads0 = gather_tokens(low0)
    mlp_back0 = [
        mlp_backward(pair, m[1], ff0, bias_fc1[0]) for pair, m in zip(grads0, mlp0)
    ]
    dres0, sums0, terms0, qkv_sums0, big0 = attention_part(
        0, att0, dx1, residual0, attended0, scatter_tokens([m[2] for m in mlp_back0]), qkv0, kept0,
        lse0, norm_chunks0, second0, [m[0] for m in mlp_back0], [m[0] for m in mlp0], grads0,
    )
    dx0, edge0 = back_first(dres0, x0, terms0, vecs[0])

    def both(low, high):
        mine = jnp.where(first, low, high)
        came_low = lax.ppermute(low, "section", [(1, 0)])
        came_high = lax.ppermute(high, "section", [(0, 1)])
        came = jnp.where(first, came_low, came_high)
        return jnp.stack([jnp.where(first, mine, came), jnp.where(first, came, mine)])[None, :, None]

    block_out = both(y0, y1)
    input_grads = both(dx0, dx1)

    def to_owner(low, high, pick):
        own = jnp.where(first, low, high) + swap_section(jnp.where(first, high, low))
        out = pick(own, here)
        for step in range(1, dp):
            pairs = [(i, (i + step) % dp) for i in range(dp)]
            out = out + lax.ppermute(pick(own, lax.rem(here + step, dp)), "dp", pairs)
        return out

    def by_unit(qkv_sums, unit_sums):
        q = qkv_sums[:, :width].reshape(heads, 1, size)
        v = qkv_sums[:, 2 * width :].reshape(heads, 1, size)
        bias = jnp.concatenate([q, v], 1).reshape(heads, dp, -1).swapaxes(0, 1).reshape(dp, -1)
        return jnp.concatenate([bias, unit_sums.reshape(dp, -1)], axis=1)

    unit = to_owner(
        by_unit(qkv_sums0, sum(m[1] for m in mlp_back0)),
        by_unit(qkv_sums1, sum(m[2] for m in mlp1)),
        lambda v, place: lax.dynamic_slice_in_dim(v, place, 1, 0),
    )
    cut = heads * (2 * size // dp)
    bias_grad = unit[:, :cut].reshape(1, heads, -1)
    fc1_grad = unit[:, cut:].reshape(1, 1, -1)

    vec = jnp.concatenate(
        [edge0[:2], sums0[:4], edge1[2:4], edge1[:2], sums1[:4], sums_sc_1[:1], sums_fc2_1[:1]]
    )
    vec = vec + core_swap(vec)
    vec = sum([from_chip(vec, step) for step in range(1, chips)], vec)
    vec = to_owner(
        vec[:8], vec[8:], lambda v, place: lax.dynamic_slice_in_dim(v, place * part, part, 1)
    )
    g_ln1, b_ln1, g_ln2, b_ln2, g_sc_attn, g_out_bias, g_sc_mlp, g_fc2_bias = (
        vec[i : i + 1] for i in range(8)
    )

    def owned(low, high):
        came_low = lax.ppermute(low, "section", [(1, 0)])
        came_high = lax.ppermute(high, "section", [(0, 1)])
        top = jnp.where(first, low, came_high)
        bottom = jnp.where(first, came_low, high)
        return jnp.concatenate([top, bottom], 0)

    g_att, g_ff = [owned(a, b) for a, b in zip(big0, big1)]
    g_qkv = g_att[:, : 3 * width].reshape(part, 3, heads, size).swapaxes(1, 2)
    g_qkv = g_qkv.reshape(1, part, 3 * width).astype(F32)
    g_out = g_att[:, 3 * width :].T[None].astype(F32)
    g_fc1 = g_ff[:, :units][None].astype(F32)
    g_fc2 = g_ff[:, units:].T[None].astype(F32)
    return (
        block_out, input_grads, g_ln1, b_ln1, g_qkv, bias_grad, g_out, g_out_bias, g_sc_attn,
        g_ln2, b_ln2, g_fc1, fc1_grad, g_fc2, g_fc2_bias, g_sc_mlp,
    )


def solution(mesh):
    vec = P("section", "dp")
    by_row = P("section", "dp", "tensor")
    by_unit = P("section", "tensor", "dp")
    data = P(None, "dp", "tensor", None)
    split = P("section", None, "dp", "tensor", None)
    given = (
        vec, vec, by_row, by_unit, by_unit, vec, vec, vec, vec, by_row, by_unit, by_unit, vec, vec,
    )
    return jax.shard_map(
        shards,
        mesh=mesh,
        in_specs=(data, data) + given,
        out_specs=(split, split) + given,
        check_vma=False,
    )
```

```python
from functools import partial

import jax
import jax.numpy as jnp
from jax import lax
from jax.experimental import pallas as pl
from jax.experimental.pallas import tpu as pltpu
from jax.sharding import PartitionSpec as P

EPSILON = 1e-06
BF = jnp.bfloat16
F32 = jnp.float32
MIB = 1 << 20

LN1_G, LN1_B, OUT_B, SC_ATTN, LN2_G, LN2_B, FC2_B, SC_MLP = range(8)


def dot(a, b):
    return lax.dot_general(a, b, (((1,), (0,)), ((), ())), preferred_element_type=F32)


def dot_bt(a, b):
    return lax.dot_general(a, b, (((1,), (1,)), ((), ())), preferred_element_type=F32)


def dot_at(a, b):
    return lax.dot_general(a, b, (((0,), (0,)), ((), ())), preferred_element_type=F32)


def turn(v):
    return v.astype(F32).T


def params(limit, grid=0):
    return pltpu.CompilerParams(
        vmem_limit_bytes=limit * MIB,
        dimension_semantics=("arbitrary",) * grid if grid else None,
    )


def cost(flops, nbytes, trans=0):
    return pl.CostEstimate(flops=int(flops), bytes_accessed=int(nbytes), transcendentals=int(trans))


def sds(shape, dtype):
    return jax.ShapeDtypeStruct(shape, dtype)


def core_swap(v):
    count = lax.axis_size("tensor")
    return lax.ppermute(v, "tensor", [(i, i ^ 1) for i in range(count)])


def from_chip(v, step):
    count = lax.axis_size("tensor")
    chips = count // 2
    pairs = [(((i // 2 + step) % chips) * 2 + i % 2, i) for i in range(count)]
    return lax.ppermute(v, "tensor", pairs)


def tie(v, *after):
    return lax.optimization_barrier((v, *after))[0]


def gather_tokens(own, work):
    chips = lax.axis_size("tensor") // 2
    came = [from_chip(own, step) for step in range(1, chips)]
    chunks = [(own, core_swap(own))]
    results = [work(chunks[0])]
    for same in came:
        same = tie(same, results[-1])
        chunks.append((same, core_swap(same)))
        results.append(work(chunks[-1]))
    return chunks, results


def core_sums(parts):
    return [
        (same.astype(F32) + core_swap(other).astype(F32)).astype(BF) for same, other in parts[1:]
    ]


def send_sums(sums):
    chips = len(sums) + 1
    return [from_chip(both, chips - step) for step, both in enumerate(sums, 1)]


def scatter_tokens(parts, work=None):
    sums = core_sums(parts)
    terms = send_sums(sums)
    local = core_swap(tie(parts[0][1], sums[-1]))
    made = work(sums[-1]) if work else None
    if work:
        terms = [tie(t, made, local) for t in terms]
    return [parts[0][0], *terms, local], made


def swap_section(v):
    return lax.ppermute(v, "section", [(0, 1), (1, 0)])


def assemble(own, same, other, rows):
    part, cols = own.shape
    half = part // 2
    steps = len(same)
    place = jnp.stack([lax.axis_index("dp"), lax.axis_index("section")])

    def body(place_ref, own_ref, *refs):
        same_refs, other_refs = refs[:steps], refs[steps : 2 * steps]
        out_ref, sems = refs[2 * steps :]
        z, x = place_ref[0], place_ref[1]
        copies = [(own_ref, z * part, part)]
        for k in range(steps):
            base = lax.rem(z + (steps - k), steps + 1) * part
            copies.append((same_refs[k], base + x * half, half))
            copies.append((other_refs[k], base + (1 - x) * half, half))
        started = []
        for i, (ref, at, size) in enumerate(copies):
            at = pl.multiple_of(at, half)
            started.append(
                pltpu.make_async_copy(ref, out_ref.at[pl.ds(at, size), :], sems.at[i])
            )
            started[-1].start()
        for copy in started:
            copy.wait()

    hbm = pl.BlockSpec(memory_space=pl.ANY)
    return pl.pallas_call(
        body,
        in_specs=[pl.BlockSpec(memory_space=pltpu.SMEM)] + [hbm] * (1 + 2 * steps),
        out_specs=pl.BlockSpec(memory_space=pltpu.VMEM),
        out_shape=sds((rows, cols), own.dtype),
        scratch_shapes=[pltpu.SemaphoreType.DMA((1 + 2 * steps,))],
        compiler_params=params(16),
        cost_estimate=cost(0, 4 * rows * cols),
        name="assemble",
    )(place, own, *same, *other)


def spread(both, side, after=None):
    count = lax.axis_size("dp")
    half = both.shape[0] // 2
    ring = [(i, (i + 1) % count) for i in range(count)]
    last = lax.dynamic_slice_in_dim(both, side * half, half, 0)
    if after is not None:
        last = tie(last, after)
    same, other = [], []
    for _ in range(count - 1):
        last = lax.ppermute(last, "dp", ring)
        same.append(last)
        other.append(swap_section(last))
    return assemble(both, same, other, both.shape[0] * count), last


def split_gather(shard, side):
    half = shard.shape[0] // 2
    own = lax.dynamic_slice_in_dim(shard, side * half, half, 0)
    return lax.all_gather(own, ("dp", "section"), axis=0, tiled=True)


def scatter_sum(g):
    return lax.psum_scatter(g, ("dp", "section"), scatter_dimension=0, tiled=True)


def send_sum(g, pair):
    dp = lax.axis_size("dp")
    here = lax.axis_index("dp")
    part = g.shape[0] // dp
    rows = lambda place: lax.dynamic_slice_in_dim(g, place * part, part, 0)
    out = rows(here).astype(F32)
    for step in range(1, dp):
        pairs = [(i, (i + step) % dp) for i in range(dp)]
        out = out + lax.ppermute(rows(lax.rem(here + step, dp)), "dp", pairs).astype(F32)
    return out, lax.ppermute(out.astype(BF), "section", [pair])


def standardize(v):
    centred = v - jnp.mean(v, axis=-1, keepdims=True)
    var = jnp.mean(centred * centred, axis=-1, keepdims=True)
    scale = lax.rsqrt(var + EPSILON)
    return centred * scale, scale


def norm_of(v, vec, gain, shift):
    return (standardize(v)[0] * vec[gain : gain + 1, :] + vec[shift : shift + 1, :]).astype(BF)


def norm_back(v, grad, gain):
    xh, scale = standardize(v)
    dxh = grad * gain
    inner = jnp.mean(dxh * xh, axis=-1, keepdims=True)
    out = scale * (dxh - jnp.mean(dxh, axis=-1, keepdims=True) - xh * inner)
    return out, grad * xh


def total(refs):
    out = refs[0][...].astype(F32)
    for ref in refs[1:]:
        out = out + ref[...].astype(F32)
    return out


def add_rows(ref, rows):
    block = jnp.concatenate(
        [jnp.sum(r, axis=0, keepdims=True) for r in rows], axis=0
    )

    @pl.when(pl.program_id(0) == 0)
    def _():
        ref[...] = jnp.zeros_like(ref)

    ref[: len(rows), :] += block


def rowwise(body, row_ins, fulls, row_outs, sums, name):
    rows, width = row_ins[0].shape
    step = min(64, rows)
    row = lambda i: (i, 0)
    whole = lambda i: (0, 0)
    in_specs = [pl.BlockSpec((step, width), row) for _ in row_ins]
    in_specs += [pl.BlockSpec(f.shape, whole) for f in fulls]
    out_specs = [pl.BlockSpec((step, width), row) for _ in row_outs]
    out_specs += [pl.BlockSpec((8, width), whole) for _ in range(sums)]
    out_shape = [sds((rows, width), d) for d in row_outs] + [sds((8, width), F32)] * sums
    nbytes = sum(a.size * a.dtype.itemsize for a in row_ins) + sum(
        rows * width * jnp.dtype(d).itemsize for d in row_outs
    )
    return pl.pallas_call(
        body,
        grid=(rows // step,),
        in_specs=in_specs,
        out_specs=out_specs,
        out_shape=out_shape,
        compiler_params=params(16, 1),
        cost_estimate=cost(20 * rows * width, nbytes),
        name=name,
    )(*row_ins, *fulls)


def norm_first(x, vec):
    def body(x_ref, vec_ref, out_ref):
        out_ref[...] = norm_of(x_ref[...].astype(F32), vec_ref[...], LN1_G, LN1_B)

    return rowwise(body, [x], [vec], [BF], 0, "norm_first")[0]


def after_attention(x, terms, vec):
    count = len(terms)

    def body(*refs):
        x_ref, term_refs, vec_ref = refs[0], refs[1 : 1 + count], refs[1 + count]
        att_ref, res_ref, norm_ref = refs[2 + count :]
        v = vec_ref[...]
        attended = total(term_refs) + v[OUT_B : OUT_B + 1, :]
        residual = x_ref[...].astype(F32) + v[SC_ATTN : SC_ATTN + 1, :] * attended
        att_ref[...] = attended.astype(BF)
        res_ref[...] = residual
        norm_ref[...] = norm_of(residual, v, LN2_G, LN2_B)

    return rowwise(body, [x, *terms], [vec], [BF, F32, BF], 0, "after_attention")


def after_mlp(residual, terms, vec, vec_next):
    count = len(terms)

    def body(*refs):
        res_ref, term_refs = refs[0], refs[1 : 1 + count]
        vec_ref, next_ref, mlp_ref, y_ref, norm_ref = refs[1 + count :]
        v = vec_ref[...]
        mlp = total(term_refs) + v[FC2_B : FC2_B + 1, :]
        y = (res_ref[...] + v[SC_MLP : SC_MLP + 1, :] * mlp).astype(BF)
        mlp_ref[...] = mlp.astype(BF)
        y_ref[...] = y
        norm_ref[...] = norm_of(y.astype(F32), next_ref[...], LN1_G, LN1_B)

    return rowwise(body, [residual, *terms], [vec, vec_next], [BF, BF, BF], 0, "after_mlp")


def last_output(residual, terms, grad, vec):
    count = len(terms)

    def body(*refs):
        res_ref, term_refs = refs[0], refs[1 : 1 + count]
        grad_ref, vec_ref, y_ref, sum_ref = refs[1 + count :]
        v = vec_ref[...]
        mlp = total(term_refs) + v[FC2_B : FC2_B + 1, :]
        y_ref[...] = (res_ref[...] + v[SC_MLP : SC_MLP + 1, :] * mlp).astype(BF)
        add_rows(sum_ref, [grad_ref[...].astype(F32) * mlp])

    return rowwise(body, [residual, *terms, grad], [vec], [BF], 1, "last_output")


def start_back(grad, vec):
    def body(grad_ref, vec_ref, out_ref, sum_ref):
        low = (vec_ref[...][SC_MLP : SC_MLP + 1, :] * grad_ref[...].astype(F32)).astype(BF)
        out_ref[...] = low
        add_rows(sum_ref, [low.astype(F32)])

    return rowwise(body, [grad], [vec], [BF], 1, "start_back")


def back_second(grad, residual, attended, terms, vec):
    count = len(terms)

    def body(*refs):
        grad_ref, res_ref, att_ref = refs[:3]
        term_refs = refs[3 : 3 + count]
        vec_ref, dres_ref, low_ref, sum_ref = refs[3 + count :]
        v = vec_ref[...]
        dn = total(term_refs)
        back, dgain = norm_back(res_ref[...], dn, v[LN2_G : LN2_G + 1, :])
        dres = grad_ref[...].astype(F32) + back
        low = (v[SC_ATTN : SC_ATTN + 1, :] * dres).astype(BF)
        dres_ref[...] = dres
        low_ref[...] = low
        add_rows(sum_ref, [dgain, dn, dres * att_ref[...].astype(F32), low.astype(F32)])

    return rowwise(
        body, [grad, residual, attended, *terms], [vec], [F32, BF], 1, "back_second"
    )


def back_first(dres, x, terms, vec, mlp_below=None, vec_below=None):
    count = len(terms)
    below = mlp_below is not None

    def body(*refs):
        dres_ref, x_ref = refs[:2]
        term_refs = refs[2 : 2 + count]
        rest = refs[2 + count :]
        if below:
            mlp_ref, vec_ref, under_ref, dx_ref, low_ref, sum_ref = rest
        else:
            vec_ref, dx_ref, sum_ref = rest
        v = vec_ref[...]
        dn = total(term_refs)
        back, dgain = norm_back(x_ref[...].astype(F32), dn, v[LN1_G : LN1_G + 1, :])
        dx = (dres_ref[...] + back).astype(BF)
        dx_ref[...] = dx
        rows = [dgain, dn]
        if below:
            wide = dx.astype(F32)
            low = (under_ref[...][SC_MLP : SC_MLP + 1, :] * wide).astype(BF)
            low_ref[...] = low
            rows += [wide * mlp_ref[...].astype(F32), low.astype(F32)]
        add_rows(sum_ref, rows)

    row_ins = [dres, x, *terms] + ([mlp_below] if below else [])
    fulls = [vec] + ([vec_below] if below else [])
    return rowwise(body, row_ins, fulls, [BF, BF] if below else [BF], 1, "back_first")


def project_qkv(pair, weight, bias):
    rows, width = pair[0].shape
    cols = bias.shape[1]

    def body(a_ref, b_ref, w_ref, bias_ref, out_ref):
        w = w_ref[...]
        shift = bias_ref[...]
        out_ref[:rows, :] = (dot(a_ref[...], w) + shift).astype(BF)
        out_ref[rows:, :] = (dot(b_ref[...], w) + shift).astype(BF)

    whole = lambda i: (0, 0)
    return pl.pallas_call(
        body,
        grid=(1,),
        in_specs=[
            pl.BlockSpec((rows, width), whole),
            pl.BlockSpec((rows, width), whole),
            pl.BlockSpec((width, cols), whole),
            pl.BlockSpec((1, cols), whole),
        ],
        out_specs=pl.BlockSpec((2 * rows, cols), whole),
        out_shape=sds((2 * rows, cols), BF),
        compiler_params=params(24, 1),
        cost_estimate=cost(4 * rows * width * cols, 2 * (2 * rows * (width + cols) + width * cols)),
        name="project_qkv",
    )(*pair, weight, bias)


def head_rows(v, head, size):
    rows = lax.broadcasted_iota(jnp.int32, v.shape, 0)
    return jnp.where(rows // size == head, v, jnp.zeros_like(v))


def head_cols(v, head, size):
    cols = lax.broadcasted_iota(jnp.int32, v.shape, 1)
    return jnp.where(cols // size == head, v, jnp.zeros_like(v))


def fold(v, op):
    return op(v.reshape(-1, 8, v.shape[1]), axis=0)


def attention(packed, weight, size):
    chips = len(packed)
    span = packed[0].shape[0]
    half = span // 2
    width = packed[0].shape[1] // 3
    seq = chips * span
    heads = width // size
    model = weight.shape[0]
    step = min(256, seq)
    chunk = min(128, seq)
    score = size**-0.5

    def body(*refs):
        in_refs, w_ref = refs[:chips], refs[chips]
        head_refs = refs[chips + 1 : 2 * chips + 1]
        lse_ref = refs[2 * chips + 1]
        part_refs = refs[2 * chips + 2 : 4 * chips + 2]
        k_ref, qt_ref, vt_ref, ot_ref, s_ref, p_ref = refs[4 * chips + 2 :]
        for c in range(chips):
            at = slice(c * span, (c + 1) * span)
            k_ref[at, :] = in_refs[c][:, width : 2 * width]
            qt_ref[:, at] = (turn(in_refs[c][:, :width]) * score).astype(BF)
            vt_ref[:, at] = turn(in_refs[c][:, 2 * width :]).astype(BF)

        def one(i, carry):
            at = pl.ds(pl.multiple_of(i * step, step), step)
            q = qt_ref[:, at]
            s_ref[0] = dot(k_ref[...], head_rows(q, 0, size))
            for h in range(heads):
                if h + 1 < heads:
                    s_ref[(h + 1) % 2] = dot(k_ref[...], head_rows(q, h + 1, size))
                now = h % 2
                top = fold(s_ref[now, :chunk, :], jnp.max)
                for r in range(chunk, seq, chunk):
                    top = jnp.maximum(top, fold(s_ref[now, r : r + chunk, :], jnp.max))
                top = jnp.max(top, axis=0, keepdims=True)
                norm = jnp.zeros((8, step), F32)
                for r in range(0, seq, chunk):
                    p = jnp.exp(s_ref[now, r : r + chunk, :] - top)
                    norm = norm + fold(p, jnp.sum)
                    p_ref[now, r : r + chunk, :] = p.astype(BF)
                norm = jnp.sum(norm, axis=0, keepdims=True)
                rows = slice(h * size, (h + 1) * size)
                ot_ref[rows, at] = dot(vt_ref[rows, :], p_ref[now]) / norm
                lse_ref[h : h + 1, at] = top + jnp.log(norm)
            return carry

        lax.fori_loop(0, seq // step, one, 0)
        for c in range(chips):
            at = slice(c * span, (c + 1) * span)
            o = ot_ref[:, at].T.astype(BF)
            head_refs[c][...] = o
            part_refs[2 * c][...] = dot_bt(o[:half], w_ref[...]).astype(BF)
            part_refs[2 * c + 1][...] = dot_bt(o[half:], w_ref[...]).astype(BF)

    whole = lambda i: (0, 0)
    full = lambda shape: pl.BlockSpec(shape, whole)
    out = pl.pallas_call(
        body,
        grid=(1,),
        in_specs=[full((span, 3 * width))] * chips + [pl.BlockSpec((model, width), lambda i: (0, 3))],
        out_specs=[full((span, width))] * chips
        + [full((heads, seq))]
        + [full((half, model))] * (2 * chips),
        out_shape=[sds((span, width), BF)] * chips
        + [sds((heads, seq), F32)]
        + [sds((half, model), BF)] * (2 * chips),
        scratch_shapes=[
            pltpu.VMEM((seq, width), BF),
            pltpu.VMEM((width, seq), BF),
            pltpu.VMEM((width, seq), BF),
            pltpu.VMEM((width, seq), F32),
            pltpu.VMEM((2, seq, step), F32),
            pltpu.VMEM((2, seq, step), BF),
        ],
        compiler_params=params(36, 1),
        cost_estimate=cost(
            16 * seq * seq * width, 2 * seq * (4 * width + model), heads * seq * seq
        ),
        name="attention",
    )(*packed, weight)
    parts = out[chips + 1 :]
    return out[:chips], out[chips], [(parts[2 * c], parts[2 * c + 1]) for c in range(chips)]


def attention_back(packed, heads_kept, lse, datt, weight, size):
    chips = len(packed)
    span = packed[0].shape[0]
    half = span // 2
    width = packed[0].shape[1] // 3
    seq = chips * span
    heads = width // size
    model = weight.shape[0]
    step = min(256, seq)
    chunk = min(128, seq)
    score = size**-0.5

    def body(*refs):
        at = 0

        def take(count):
            nonlocal at
            at += count
            return refs[at - count : at]

        in_refs, kept_refs = take(chips), take(chips)
        (lse_ref,) = take(1)
        datt_refs = take(2 * chips)
        (w_ref,) = take(1)
        dqkv_refs = take(chips)
        part_refs = take(2 * chips)
        (sum_ref,) = take(1)
        k_ref, v_ref, kt_ref, qt_ref, q_ref, do_ref, dot_ref = take(7)
        inner_ref, s_ref, g_ref, p_ref, ds_ref, dk_ref, dv_ref, dqt_ref = take(8)
        for c in range(chips):
            rows = slice(c * span, (c + 1) * span)
            q = in_refs[c][:, :width].astype(F32) * score
            k = in_refs[c][:, width : 2 * width]
            q_ref[rows, :] = q.astype(BF)
            qt_ref[:, rows] = q.T.astype(BF)
            k_ref[rows, :] = k
            kt_ref[:, rows] = turn(k).astype(BF)
            v_ref[rows, :] = in_refs[c][:, 2 * width :]
            for b in range(2):
                d = dot(datt_refs[2 * c + b][...], w_ref[:, 3 * width :]).astype(BF)
                here = slice(c * span + b * half, c * span + (b + 1) * half)
                do_ref[here, :] = d
                dt = turn(d)
                dot_ref[:, here] = dt.astype(BF)
                prod = dt * turn(kept_refs[c][b * half : (b + 1) * half, :])
                for h in range(heads):
                    inner_ref[h : h + 1, here] = jnp.sum(
                        prod[h * size : (h + 1) * size, :], axis=0, keepdims=True
                    )

        def one(i, carry):
            at = pl.ds(pl.multiple_of(i * step, step), step)
            qt = qt_ref[:, at]
            dot_t = dot_ref[:, at]
            q = q_ref[at, :]
            do = do_ref[at, :]

            def scores(h):
                s_ref[h % 2] = dot(k_ref[...], head_rows(qt, h, size))
                g_ref[h % 2] = dot(v_ref[...], head_rows(dot_t, h, size))

            scores(0)
            for h in range(heads):
                if h + 1 < heads:
                    scores(h + 1)
                now = h % 2
                cols = slice(h * step, (h + 1) * step)
                lse = lse_ref[h : h + 1, at]
                inner = inner_ref[h : h + 1, at]
                for r in range(0, seq, chunk):
                    p = jnp.exp(s_ref[now, r : r + chunk, :] - lse)
                    ds = p * (g_ref[now, r : r + chunk, :] - inner)
                    p_ref[r : r + chunk, cols] = p.astype(BF)
                    ds_ref[r : r + chunk, cols] = ds.astype(BF)
                rows = slice(h * size, (h + 1) * size)
                dqt_ref[rows, at] = dot(kt_ref[rows, :], ds_ref[:, cols]) * score
            dv = dot(p_ref[...], jnp.concatenate([head_cols(do, h, size) for h in range(heads)], 0))
            dk = dot(ds_ref[...], jnp.concatenate([head_cols(q, h, size) for h in range(heads)], 0))

            @pl.when(i == 0)
            def _():
                dv_ref[...] = dv
                dk_ref[...] = dk

            @pl.when(i > 0)
            def _():
                dv_ref[...] += dv
                dk_ref[...] += dk

            return carry

        lax.fori_loop(0, seq // step, one, 0)
        for c in range(chips):
            rows = slice(c * span, (c + 1) * span)
            out = dqkv_refs[c]
            out[:, :width] = dqt_ref[:, rows].T.astype(BF)
            out[:, width : 2 * width] = dk_ref[rows, :].astype(BF)
            out[:, 2 * width :] = dv_ref[rows, :].astype(BF)
            sums = jnp.sum(out[...].astype(F32), axis=0, keepdims=True)
            if c == 0:
                sum_ref[...] = sums
            else:
                sum_ref[...] += sums
            for b in range(2):
                part_refs[2 * c + b][...] = dot_bt(
                    out[b * half : (b + 1) * half, :], w_ref[:, : 3 * width]
                ).astype(BF)

    flat = [g for pair in datt for g in pair]
    whole = lambda i: (0, 0)
    full = lambda a: pl.BlockSpec(a.shape, whole)
    out_shape = (
        [sds((span, 3 * width), BF)] * chips
        + [sds((half, model), BF)] * (2 * chips)
        + [sds((1, 3 * width), F32)]
    )
    operands = (*packed, *heads_kept, lse, *flat, weight)
    out = pl.pallas_call(
        body,
        grid=(1,),
        in_specs=[full(a) for a in operands],
        out_specs=[full(a) for a in out_shape],
        out_shape=out_shape,
        scratch_shapes=[
            pltpu.VMEM((seq, width), BF),
            pltpu.VMEM((seq, width), BF),
            pltpu.VMEM((width, seq), BF),
            pltpu.VMEM((width, seq), BF),
            pltpu.VMEM((seq, width), BF),
            pltpu.VMEM((seq, width), BF),
            pltpu.VMEM((width, seq), BF),
            pltpu.VMEM((heads, seq), F32),
            pltpu.VMEM((2, seq, step), F32),
            pltpu.VMEM((2, seq, step), F32),
            pltpu.VMEM((seq, heads * step), BF),
            pltpu.VMEM((seq, heads * step), BF),
            pltpu.VMEM((seq, width), F32),
            pltpu.VMEM((seq, width), F32),
            pltpu.VMEM((width, seq), F32),
        ],
        compiler_params=params(52, 1),
        cost_estimate=cost(
            40 * seq * seq * width, 2 * seq * (8 * width + 2 * model), heads * seq * seq
        ),
        name="attention_back",
    )(*operands)
    parts = out[chips : 3 * chips]
    return (
        out[:chips],
        [(parts[2 * c], parts[2 * c + 1]) for c in range(chips)],
        out[3 * chips],
    )


def gelu_both(x):
    away = jnp.abs(x)
    t = 1.0 / (1.0 + (0.3275911 * 0.5**0.5) * away)
    bell = jnp.exp(-0.5 * (x * x))
    poly = t * (
        0.127414796
        + t * (-0.142248368 + t * (0.7107068705 + t * (-0.7265760135 + t * 0.5307027145)))
    )
    tail = poly * bell
    phi = jnp.where(x >= 0, 1.0 - tail, tail)
    return x * phi, phi + x * (bell * 0.3989422804014327)


def mlp_call(body, pairs, extra, weight, bias, outs, parts, scratch, name):
    rows, model = pairs[0].shape
    units = weight.shape[1] // 2
    step = min(256, units)
    blocks = units // step
    whole = lambda j: (0, 0)
    cols = lambda j: (0, j)
    in_specs = [pl.BlockSpec((rows, model), whole) for _ in pairs]
    in_specs += [pl.BlockSpec((2 * rows, step), cols) for _ in extra]
    in_specs += [
        pl.BlockSpec((model, step), cols),
        pl.BlockSpec((model, step), lambda j: (0, blocks + j)),
        pl.BlockSpec((1, step), cols),
    ]
    out_specs = [pl.BlockSpec((2 * rows, step), cols) for _ in outs]
    out_specs += [pl.BlockSpec((1, step), cols)]
    out_specs += [pl.BlockSpec((rows, model), whole)] * (2 * parts)
    out_shape = [sds((2 * rows, units), d) for d in outs] + [sds((1, units), F32)]
    out_shape += [sds((rows, model), BF)] * (2 * parts)
    count = len(pairs) // 2
    return pl.pallas_call(
        body,
        grid=(blocks,),
        in_specs=in_specs,
        out_specs=out_specs,
        out_shape=out_shape,
        scratch_shapes=[pltpu.VMEM((2 * rows, model), F32)] * parts
        + [pltpu.VMEM((2 * rows, step), F32)] * scratch,
        compiler_params=params(40, 1),
        cost_estimate=cost(
            8 * count * rows * model * units,
            4 * model * units + 4 * rows * (model + units) * (count + 1),
        ),
        name=name,
    )(*pairs, *extra, weight, weight, bias)


def clear(*refs):
    @pl.when(pl.program_id(0) == 0)
    def _():
        for ref in refs:
            ref[...] = jnp.zeros_like(ref)


def finish(acc, low, high):
    rows = low.shape[0]

    @pl.when(pl.program_id(0) == pl.num_programs(0) - 1)
    def _():
        low[...] = acc[:rows, :].astype(BF)
        high[...] = acc[rows:, :].astype(BF)


CHUNK = 32


def mlp_forward(pair, weight, bias):
    rows = pair[0].shape[0]

    def body(a, b, w1_ref, w2_ref, bias_ref, act_ref, slope_ref, sum_ref, lo, hi, acc, pre):
        clear(acc, sum_ref)
        shift = bias_ref[...]
        for i, x in enumerate((a, b)):
            pre[i * rows : (i + 1) * rows, :] = dot(x[...], w1_ref[...])
        for i in range(2):
            at = slice(i * rows, (i + 1) * rows)
            for r in range(i * rows, (i + 1) * rows, CHUNK):
                act, slope = gelu_both(pre[r : r + CHUNK, :] + shift)
                act_ref[r : r + CHUNK, :] = act.astype(BF)
                slope_ref[r : r + CHUNK, :] = slope.astype(BF)
            acc[at, :] += dot_bt(act_ref[at, :], w2_ref[...])
        finish(acc, lo, hi)

    act, slope, _, lo, hi = mlp_call(body, pair, [], weight, bias, [BF, BF], 1, 1, "mlp_forward")
    return act, slope, (lo, hi)


def mlp_backward(pair, slope, weight, bias):
    rows = pair[0].shape[0]

    def body(a, b, slope_ref, w1_ref, w2_ref, bias_ref, dpre_ref, sum_ref, lo, hi, acc, pre):
        clear(acc)
        for i, g in enumerate((a, b)):
            pre[i * rows : (i + 1) * rows, :] = dot(g[...], w2_ref[...])
        sums = jnp.zeros((8, bias_ref.shape[1]), F32)
        for i in range(2):
            at = slice(i * rows, (i + 1) * rows)
            for r in range(i * rows, (i + 1) * rows, CHUNK):
                d = pre[r : r + CHUNK, :] * slope_ref[r : r + CHUNK, :].astype(F32)
                d = d.astype(BF)
                dpre_ref[r : r + CHUNK, :] = d
                sums = sums + fold(d.astype(F32), jnp.sum)
            acc[at, :] += dot_bt(dpre_ref[at, :], w1_ref[...])
        sum_ref[...] = jnp.sum(sums, axis=0, keepdims=True)
        finish(acc, lo, hi)

    dpre, sums, lo, hi = mlp_call(
        body, pair, [slope], weight, bias, [BF], 1, 1, "mlp_backward"
    )
    return dpre, sums, (lo, hi)


def mlp_both(pair, grads, weight, bias):
    rows = pair[0].shape[0]

    def body(
        a, b, c, d, w1_ref, w2_ref, bias_ref, act_ref, dpre_ref, sum_ref,
        lo, hi, blo, bhi, acc, back, pre, grad,
    ):
        clear(acc, back)
        shift = bias_ref[...]
        for i, (x, g) in enumerate(((a, c), (b, d))):
            at = slice(i * rows, (i + 1) * rows)
            pre[at, :] = dot(x[...], w1_ref[...])
            grad[at, :] = dot(g[...], w2_ref[...])
        sums = jnp.zeros((8, bias_ref.shape[1]), F32)
        for i in range(2):
            at = slice(i * rows, (i + 1) * rows)
            for r in range(i * rows, (i + 1) * rows, CHUNK):
                act, slope = gelu_both(pre[r : r + CHUNK, :] + shift)
                act_ref[r : r + CHUNK, :] = act.astype(BF)
                dpre = (grad[r : r + CHUNK, :] * slope).astype(BF)
                dpre_ref[r : r + CHUNK, :] = dpre
                sums = sums + fold(dpre.astype(F32), jnp.sum)
            back[at, :] += dot_bt(dpre_ref[at, :], w1_ref[...])
            acc[at, :] += dot_bt(act_ref[at, :], w2_ref[...])
        sum_ref[...] = jnp.sum(sums, axis=0, keepdims=True)
        finish(acc, lo, hi)
        finish(back, blo, bhi)

    act, dpre, sums, lo, hi, blo, bhi = mlp_call(
        body, [*pair, *grads], [], weight, bias, [BF, BF], 2, 2, "mlp_both"
    )
    return act, dpre, sums, (lo, hi), (blo, bhi)


def weight_grads(products, name):
    model = products[0][0][0].shape[1]
    step = min(256, model)
    sizes = [(len(left), len(right), right[0].shape[1]) for left, right in products]
    cols = sum(n for _, _, n in sizes)
    tokens = sum(a.shape[0] for a in products[0][0])

    def body(*refs):
        out = refs[-1]
        at = base = 0
        for many, few, n in sizes:
            lefts, rights = refs[at : at + many], refs[at + many : at + many + few]
            at += many + few
            ratio = many // few
            acc = None
            for i in range(many):
                size = lefts[i].shape[0]
                here = slice((i % ratio) * size, (i % ratio + 1) * size)
                term = dot_at(lefts[i][...], rights[i // ratio][here, :])
                acc = term if acc is None else acc + term
            out[:, base : base + n] = acc.astype(BF)
            base += n

    specs, operands = [], []
    for left, right in products:
        specs += [pl.BlockSpec((a.shape[0], step), lambda i: (0, i)) for a in left]
        specs += [pl.BlockSpec(b.shape, lambda i: (0, 0)) for b in right]
        operands += [*left, *right]
    return pl.pallas_call(
        body,
        grid=(model // step,),
        in_specs=specs,
        out_specs=pl.BlockSpec((step, cols), lambda i: (i, 0)),
        out_shape=sds((model, cols), BF),
        compiler_params=params(40, 1),
        cost_estimate=cost(
            2 * tokens * model * cols, 2 * (tokens * (2 * model + cols) + model * cols)
        ),
        name=name,
    )(*operands)


def pieces(chunks):
    return [p for pair in chunks for p in pair]


def shards(
    tokens, cotangent, ln1_gain, ln1_bias, w_qkv, qv_bias, w_out, out_bias, scale_attn,
    ln2_gain, ln2_bias, w_fc1, fc1_bias, w_fc2, fc2_bias, scale_mlp,
):
    side = lax.axis_index("section")
    first = side == 0
    dp = lax.axis_size("dp")
    here = lax.axis_index("dp")
    chips = lax.axis_size("tensor") // 2
    rows, model = tokens.shape[2:]
    heads = qv_bias.shape[1]
    size = qv_bias.shape[2] * dp // 2
    width = heads * size
    units = w_fc1.shape[2]
    part = model // dp

    x0 = lax.dynamic_index_in_dim(tokens, side, 0, keepdims=False).reshape(rows, model)
    grad_top = lax.dynamic_index_in_dim(cotangent, side, 0, keepdims=False).reshape(rows, model)

    vectors = (ln1_gain, ln1_bias, out_bias, scale_attn, ln2_gain, ln2_bias, fc2_bias, scale_mlp)
    packed = jnp.concatenate(
        [v.reshape(-1) for v in vectors] + [fc1_bias.reshape(-1), qv_bias.reshape(-1)]
    )
    mine = lax.all_gather(packed, "dp", axis=0)
    came = swap_section(mine)
    small = jnp.stack([jnp.where(first, mine, came), jnp.where(first, came, mine)]).astype(F32)
    cut = 8 * part
    vecs = small[:, :, :cut].reshape(2, dp, 8, part).swapaxes(1, 2).reshape(2, 8, model)
    bias_fc1 = small[:, :, cut : cut + units // dp].reshape(2, 1, units)
    qv = small[:, :, cut + units // dp :].reshape(2, dp, heads, -1).swapaxes(1, 2)
    qv = qv.reshape(2, heads, 2, size)
    bias_qkv = jnp.stack([qv[:, :, 0], jnp.zeros_like(qv[:, :, 0]), qv[:, :, 1]], axis=1)
    bias_qkv = bias_qkv.reshape(2, 1, 3 * width)
    vecs = (vecs[0], vecs[1])

    own_qkv = w_qkv.reshape(part, heads, 3, size).swapaxes(1, 2).reshape(part, 3 * width)
    own_att = jnp.concatenate([own_qkv, w_out[0].T], axis=1)
    own_ff = jnp.concatenate([w_fc1[0], w_fc2[0].T], axis=1)
    came_att = swap_section(own_att)
    came_ff = swap_section(tie(own_ff, came_att))
    att0, last = spread(tie(jnp.where(first, own_att, came_att), mine), side)
    ff0, last = spread(jnp.where(first, own_ff, came_ff), side, last)
    att1 = split_gather(tie(jnp.where(first, came_att, own_att), last), side)
    ff1 = split_gather(tie(jnp.where(first, came_ff, own_ff), last), side)

    def front(x, norm, weight, s):
        chunks, qkv = gather_tokens(norm, lambda pair: project_qkv(pair, weight, bias_qkv[s]))
        kept, lse, parts = attention(qkv, weight, size)
        terms, _ = scatter_tokens(parts)
        attended, residual, norm2 = after_attention(x, terms, vecs[s])
        return (chunks, qkv, kept, lse, attended, residual), norm2

    saved0, norm2 = front(x0, norm_first(x0, vecs[0]), att0, 0)
    second0, mlp0 = gather_tokens(norm2, lambda pair: mlp_forward(pair, ff0, bias_fc1[0]))
    terms, _ = scatter_tokens([m[2] for m in mlp0])
    mlp_out0, y0, norm1 = after_mlp(saved0[5], terms, vecs[0], vecs[1])

    low1, sums_fc2_1 = start_back(grad_top, vecs[1])
    grads1, _ = gather_tokens(tie(low1, norm1), lambda pair: pair[0])
    saved1, norm2 = front(y0, norm1, att1, 1)
    spare = list(grads1)
    second1, mlp1 = gather_tokens(
        norm2, lambda pair: mlp_both(pair, spare.pop(0), ff1, bias_fc1[1])
    )

    def attention_back_part(s, weight, grad, saved, parts, ff_work, more_work, last_work):
        chunks, qkv, kept, lse, attended, residual = saved
        terms, g_ff = scatter_tokens(parts, ff_work)
        dres, low, sums = back_second(grad, residual, attended, terms, vecs[s])
        datt, _ = gather_tokens(low, lambda pair: pair[0])
        before, beside = more_work(datt)
        dqkv, parts, qkv_sums = attention_back(
            [tie(qkv[0], before), *qkv[1:]], kept, lse, datt, weight, size
        )
        parts = [parts[0], *[(same, tie(other, beside)) for same, other in parts[1:]]]
        terms, made = scatter_tokens(
            parts, lambda after: last_work(after, datt, dqkv)
        )
        return dres, sums, terms, qkv_sums, g_ff, before, beside, made

    def grad_ff(second, mlp, grads, acts):
        def work(after):
            return weight_grads(
                [(pieces(second), [tie(mlp[0], after), *mlp[1:]]), (pieces(grads), acts)], "grad_ff"
            )

        return work

    acts1 = [m[0] for m in mlp1]
    parts_y1 = [m[3] for m in mlp1]
    sums_y1 = core_sums(parts_y1)
    local_y1 = [parts_y1[0][0], core_swap(parts_y1[0][1])]
    dres1, sums1, terms, qkv_sums1, g_ff1, _, terms_y1, g_att1 = attention_back_part(
        1, att1, grad_top, saved1, [m[4] for m in mlp1],
        grad_ff(second1, [m[1] for m in mlp1], grads1, acts1),
        lambda datt: (datt[0][0], send_sums([tie(v, datt[-1][0]) for v in sums_y1])),
        lambda after, datt, dqkv: weight_grads(
            [(pieces(saved1[0]), [tie(dqkv[0], after), *dqkv[1:]]), (pieces(datt), saved1[2])],
            "grad_att",
        ),
    )
    dx1, low0, edge1 = back_first(dres1, y0, terms, vecs[1], mlp_out0, vecs[0])
    y1, sums_sc_1 = last_output(saved1[5], local_y1 + terms_y1, grad_top, vecs[1])
    rs_ff1 = scatter_sum(g_ff1)
    rs_att1 = send_sum(g_att1, (0, 1))

    slopes = [m[1] for m in mlp0]
    grads0, mlp_back0 = gather_tokens(
        low0, lambda pair: mlp_backward(pair, slopes.pop(0), ff0, bias_fc1[0])
    )
    dres0, sums0, terms, qkv_sums0, g_ff0, g_out0, _, g_qkv0 = attention_back_part(
        0, att0, dx1, saved0, [m[2] for m in mlp_back0],
        grad_ff(second0, [m[0] for m in mlp_back0], grads0, [m[0] for m in mlp0]),
        lambda datt: (weight_grads([(pieces(datt), saved0[2])], "grad_out"), datt[0][0]),
        lambda after, datt, dqkv: weight_grads(
            [(pieces(saved0[0]), [tie(dqkv[0], after), *dqkv[1:]])], "grad_qkv"
        ),
    )
    rs_ff0 = scatter_sum(g_ff0)
    rs_out0 = send_sum(g_out0, (1, 0))
    rs_qkv0 = send_sum(g_qkv0, (1, 0))
    dx0, edge0 = back_first(dres0, x0, terms, vecs[0])

    def both(low, high):
        mine = jnp.where(first, low, high)
        came_low = lax.ppermute(low, "section", [(1, 0)])
        came_high = lax.ppermute(high, "section", [(0, 1)])
        came = jnp.where(first, came_low, came_high)
        return jnp.stack([jnp.where(first, mine, came), jnp.where(first, came, mine)])[None, :, None]

    block_out = both(y0, y1)
    input_grads = both(dx0, dx1)

    def to_owner(low, high, pick):
        own = jnp.where(first, low, high) + swap_section(jnp.where(first, high, low))
        out = pick(own, here)
        for step in range(1, dp):
            pairs = [(i, (i + step) % dp) for i in range(dp)]
            out = out + lax.ppermute(pick(own, lax.rem(here + step, dp)), "dp", pairs)
        return out

    def by_unit(qkv_sums, unit_sums):
        q = qkv_sums[:, :width].reshape(heads, 1, size)
        v = qkv_sums[:, 2 * width :].reshape(heads, 1, size)
        bias = jnp.concatenate([q, v], 1).reshape(heads, dp, -1).swapaxes(0, 1).reshape(dp, -1)
        return jnp.concatenate([bias, unit_sums.reshape(dp, -1)], axis=1)

    unit = to_owner(
        by_unit(qkv_sums0, sum(m[1] for m in mlp_back0)),
        by_unit(qkv_sums1, sum(m[2] for m in mlp1)),
        lambda v, place: lax.dynamic_slice_in_dim(v, place, 1, 0),
    )
    cut = heads * (2 * size // dp)
    bias_grad = unit[:, :cut].reshape(1, heads, -1)
    fc1_grad = unit[:, cut:].reshape(1, 1, -1)

    vec = jnp.concatenate(
        [edge0[:2], sums0[:4], edge1[2:4], edge1[:2], sums1[:4], sums_sc_1[:1], sums_fc2_1[:1]]
    )
    vec = vec + core_swap(vec)
    vec = sum([from_chip(vec, step) for step in range(1, chips)], vec)
    vec = to_owner(
        vec[:8], vec[8:], lambda v, place: lax.dynamic_slice_in_dim(v, place * part, part, 1)
    )
    g_ln1, b_ln1, g_ln2, b_ln2, g_sc_attn, g_out_bias, g_sc_mlp, g_fc2_bias = (
        vec[i : i + 1] for i in range(8)
    )

    def owned(low, high):
        came_low = lax.ppermute(low, "section", [(1, 0)])
        came_high = lax.ppermute(high, "section", [(0, 1)])
        top = jnp.where(first, low, came_high)
        bottom = jnp.where(first, came_low, high)
        return jnp.concatenate([top, bottom], 0)

    g_ff = owned(rs_ff0, rs_ff1)

    def chosen(low, high):
        return jnp.where(first, low[0] + low[1].astype(F32), high[0] + high[1].astype(F32))

    g_qkv = chosen(rs_qkv0, [v[:, : 3 * width] for v in rs_att1])
    g_qkv = g_qkv.reshape(part, 3, heads, size).swapaxes(1, 2).reshape(1, part, 3 * width)
    g_out = chosen(rs_out0, [v[:, 3 * width :] for v in rs_att1]).T[None]
    g_fc1 = g_ff[:, :units][None].astype(F32)
    g_fc2 = g_ff[:, units:].T[None].astype(F32)
    return (
        block_out, input_grads, g_ln1, b_ln1, g_qkv, bias_grad, g_out, g_out_bias, g_sc_attn,
        g_ln2, b_ln2, g_fc1, fc1_grad, g_fc2, g_fc2_bias, g_sc_mlp,
    )


def solution(mesh):
    vec = P("section", "dp")
    by_row = P("section", "dp", "tensor")
    by_unit = P("section", "tensor", "dp")
    data = P(None, "dp", "tensor", None)
    split = P("section", None, "dp", "tensor", None)
    given = (
        vec, vec, by_row, by_unit, by_unit, vec, vec, vec, vec, by_row, by_unit, by_unit, vec, vec,
    )
    return jax.shard_map(
        shards,
        mesh=mesh,
        in_specs=(data, data) + given,
        out_specs=(split, split) + given,
        check_vma=False,
    )
```

```python
from functools import partial

import jax
import jax.numpy as jnp
from jax import lax
from jax.experimental import pallas as pl
from jax.experimental.pallas import tpu as pltpu
from jax.sharding import PartitionSpec as P

EPSILON = 1e-06
BF = jnp.bfloat16
F32 = jnp.float32
MIB = 1 << 20

LN1_G, LN1_B, OUT_B, SC_ATTN, LN2_G, LN2_B, FC2_B, SC_MLP = range(8)


def dot(a, b):
    return lax.dot_general(a, b, (((1,), (0,)), ((), ())), preferred_element_type=F32)


def dot_bt(a, b):
    return lax.dot_general(a, b, (((1,), (1,)), ((), ())), preferred_element_type=F32)


def dot_at(a, b):
    return lax.dot_general(a, b, (((0,), (0,)), ((), ())), preferred_element_type=F32)


def turn(v):
    return v.astype(F32).T


def params(limit, grid=0):
    return pltpu.CompilerParams(
        vmem_limit_bytes=limit * MIB,
        dimension_semantics=("arbitrary",) * grid if grid else None,
    )


def cost(flops, nbytes, trans=0):
    return pl.CostEstimate(flops=int(flops), bytes_accessed=int(nbytes), transcendentals=int(trans))


def sds(shape, dtype):
    return jax.ShapeDtypeStruct(shape, dtype)


def core_swap(v):
    count = lax.axis_size("tensor")
    return lax.ppermute(v, "tensor", [(i, i ^ 1) for i in range(count)])


def from_chip(v, step):
    count = lax.axis_size("tensor")
    chips = count // 2
    pairs = [(((i // 2 + step) % chips) * 2 + i % 2, i) for i in range(count)]
    return lax.ppermute(v, "tensor", pairs)


def tie(v, *after):
    return lax.optimization_barrier((v, *after))[0]


def gather_tokens(own, work):
    chips = lax.axis_size("tensor") // 2
    came = [from_chip(own, step) for step in range(1, chips)]
    chunks = [(own, core_swap(own))]
    results = [work(chunks[0])]
    for same in came:
        same = tie(same, results[-1])
        chunks.append((same, core_swap(same)))
        results.append(work(chunks[-1]))
    return chunks, results


def core_sums(parts):
    return [
        (same.astype(F32) + core_swap(other).astype(F32)).astype(BF) for same, other in parts[1:]
    ]


def send_sums(sums):
    chips = len(sums) + 1
    return [from_chip(both, chips - step) for step, both in enumerate(sums, 1)]


def scatter_tokens(parts, work=None):
    sums = core_sums(parts)
    terms = send_sums(sums)
    local = core_swap(tie(parts[0][1], sums[-1]))
    made = work(sums[-1]) if work else None
    if work:
        terms = [tie(t, made, local) for t in terms]
    return [parts[0][0], *terms, local], made


def swap_section(v):
    return lax.ppermute(v, "section", [(0, 1), (1, 0)])


def assemble(own, same, other, rows):
    part, cols = own.shape
    half = part // 2
    steps = len(same)
    place = jnp.stack([lax.axis_index("dp"), lax.axis_index("section")])

    def body(place_ref, own_ref, *refs):
        same_refs, other_refs = refs[:steps], refs[steps : 2 * steps]
        out_ref, sems = refs[2 * steps :]
        z, x = place_ref[0], place_ref[1]
        copies = [(own_ref, z * part, part)]
        for k in range(steps):
            base = lax.rem(z + (steps - k), steps + 1) * part
            copies.append((same_refs[k], base + x * half, half))
            copies.append((other_refs[k], base + (1 - x) * half, half))
        started = []
        for i, (ref, at, size) in enumerate(copies):
            at = pl.multiple_of(at, half)
            started.append(
                pltpu.make_async_copy(ref, out_ref.at[pl.ds(at, size), :], sems.at[i])
            )
            started[-1].start()
        for copy in started:
            copy.wait()

    hbm = pl.BlockSpec(memory_space=pl.ANY)
    return pl.pallas_call(
        body,
        in_specs=[pl.BlockSpec(memory_space=pltpu.SMEM)] + [hbm] * (1 + 2 * steps),
        out_specs=pl.BlockSpec(memory_space=pltpu.VMEM),
        out_shape=sds((rows, cols), own.dtype),
        scratch_shapes=[pltpu.SemaphoreType.DMA((1 + 2 * steps,))],
        compiler_params=params(16),
        cost_estimate=cost(0, 4 * rows * cols),
        name="assemble",
    )(place, own, *same, *other)


def spread(both, side):
    count = lax.axis_size("dp")
    half = both.shape[0] // 2
    own = lax.dynamic_slice_in_dim(both, side * half, half, 0)
    return [
        lax.ppermute(own, "dp", [(i, (i + step) % count) for i in range(count)])
        for step in range(1, count)
    ]


def put_together(both, came, after):
    other = [swap_section(tie(v, after)) for v in came]
    return assemble(both, came, other, both.shape[0] * (len(came) + 1))


def gather_small(v, first):
    count = lax.axis_size("dp")
    came = swap_section(v)
    own = jnp.stack([jnp.where(first, v, came), jnp.where(first, came, v)])
    ahead = [own]
    for step in range(1, count):
        ahead.append(lax.ppermute(own, "dp", [(i, (i - step) % count) for i in range(count)]))
    twice = jnp.stack(ahead + ahead, axis=1)
    return lax.dynamic_slice_in_dim(twice, count - lax.axis_index("dp"), count, 1)


def split_gather(shard, side):
    half = shard.shape[0] // 2
    own = lax.dynamic_slice_in_dim(shard, side * half, half, 0)
    return lax.all_gather(own, ("dp", "section"), axis=0, tiled=True)


def scatter_sum(g):
    return lax.psum_scatter(g, ("dp", "section"), scatter_dimension=0, tiled=True)


def send_parts(g):
    dp = lax.axis_size("dp")
    here = lax.axis_index("dp")
    part = g.shape[0] // dp
    rows = lambda place: lax.dynamic_slice_in_dim(g, place * part, part, 0)
    out = [rows(here)]
    for step in range(1, dp):
        pairs = [(i, (i + step) % dp) for i in range(dp)]
        out.append(lax.ppermute(rows(lax.rem(here + step, dp)), "dp", pairs))
    return out


def sum_parts(parts, pair, after=None):
    if after is not None:
        parts = [tie(p, after) for p in parts]
    out = sum(p.astype(F32) for p in parts)
    return out, lax.ppermute(out.astype(BF), "section", [pair])


def standardize(v):
    centred = v - jnp.mean(v, axis=-1, keepdims=True)
    var = jnp.mean(centred * centred, axis=-1, keepdims=True)
    scale = lax.rsqrt(var + EPSILON)
    return centred * scale, scale


def norm_of(v, vec, gain, shift):
    return (standardize(v)[0] * vec[gain : gain + 1, :] + vec[shift : shift + 1, :]).astype(BF)


def norm_back(v, grad, gain):
    xh, scale = standardize(v)
    dxh = grad * gain
    inner = jnp.mean(dxh * xh, axis=-1, keepdims=True)
    out = scale * (dxh - jnp.mean(dxh, axis=-1, keepdims=True) - xh * inner)
    return out, grad * xh


def total(refs):
    out = refs[0][...].astype(F32)
    for ref in refs[1:]:
        out = out + ref[...].astype(F32)
    return out


def fold(v, op):
    return op(v.reshape(-1, 8, v.shape[1]), axis=0)


def add_rows(ref, rows):
    for k, row in enumerate(rows):
        ref[8 * k : 8 * k + 8, :] += fold(row, jnp.sum)


def rowwise(body, row_ins, fulls, row_outs, sums, name):
    rows, width = row_ins[0].shape
    step = min(32, rows)
    many, some, outs = len(row_ins), len(fulls), len(row_outs)

    def kernel(*refs):
        in_refs, full_refs = refs[:many], refs[many : many + some]
        out_refs = refs[many + some : many + some + outs]
        extra = refs[many + some + outs :]
        if sums:
            extra[1][...] = jnp.zeros_like(extra[1])

        def one(i, carry):
            at = pl.ds(pl.multiple_of(i * step, step), step)
            body(
                *[r.at[at, :] for r in in_refs],
                *full_refs,
                *[r.at[at, :] for r in out_refs],
                *extra[1:],
            )
            return carry

        lax.fori_loop(0, rows // step, one, 0)
        for k in range(sums):
            extra[0][k : k + 1, :] = jnp.sum(
                extra[1][8 * k : 8 * k + 8, :], axis=0, keepdims=True
            )

    out_shape = [sds((rows, width), d) for d in row_outs]
    out_shape += [sds((sums, width), F32)] if sums else []
    full = lambda a: pl.BlockSpec(a.shape, lambda i: (0, 0))
    nbytes = sum(a.size * a.dtype.itemsize for a in row_ins) + sum(
        rows * width * jnp.dtype(d).itemsize for d in row_outs
    )
    return pl.pallas_call(
        kernel,
        grid=(1,),
        in_specs=[full(a) for a in (*row_ins, *fulls)],
        out_specs=[full(a) for a in out_shape],
        out_shape=out_shape,
        scratch_shapes=[pltpu.VMEM((8 * sums, width), F32)] if sums else [],
        compiler_params=params(20, 1),
        cost_estimate=cost(20 * rows * width, nbytes),
        name=name,
    )(*row_ins, *fulls)


def norm_first(x, vec):
    def body(x_ref, vec_ref, out_ref):
        out_ref[...] = norm_of(x_ref[...].astype(F32), vec_ref[...], LN1_G, LN1_B)

    return rowwise(body, [x], [vec], [BF], 0, "norm_first")[0]


def after_attention(x, terms, vec):
    count = len(terms)

    def body(*refs):
        x_ref, term_refs, vec_ref = refs[0], refs[1 : 1 + count], refs[1 + count]
        att_ref, res_ref, norm_ref = refs[2 + count :]
        v = vec_ref[...]
        attended = total(term_refs) + v[OUT_B : OUT_B + 1, :]
        residual = x_ref[...].astype(F32) + v[SC_ATTN : SC_ATTN + 1, :] * attended
        att_ref[...] = attended.astype(BF)
        res_ref[...] = residual
        norm_ref[...] = norm_of(residual, v, LN2_G, LN2_B)

    return rowwise(body, [x, *terms], [vec], [BF, F32, BF], 0, "after_attention")


def after_mlp(residual, terms, vec, vec_next):
    count = len(terms)

    def body(*refs):
        res_ref, term_refs = refs[0], refs[1 : 1 + count]
        vec_ref, next_ref, mlp_ref, y_ref, norm_ref = refs[1 + count :]
        v = vec_ref[...]
        mlp = total(term_refs) + v[FC2_B : FC2_B + 1, :]
        y = (res_ref[...] + v[SC_MLP : SC_MLP + 1, :] * mlp).astype(BF)
        mlp_ref[...] = mlp.astype(BF)
        y_ref[...] = y
        norm_ref[...] = norm_of(y.astype(F32), next_ref[...], LN1_G, LN1_B)

    return rowwise(body, [residual, *terms], [vec, vec_next], [BF, BF, BF], 0, "after_mlp")


def last_output(residual, terms, grad, vec):
    count = len(terms)

    def body(*refs):
        res_ref, term_refs = refs[0], refs[1 : 1 + count]
        grad_ref, vec_ref, y_ref, sum_ref = refs[1 + count :]
        v = vec_ref[...]
        mlp = total(term_refs) + v[FC2_B : FC2_B + 1, :]
        y_ref[...] = (res_ref[...] + v[SC_MLP : SC_MLP + 1, :] * mlp).astype(BF)
        add_rows(sum_ref, [grad_ref[...].astype(F32) * mlp])

    return rowwise(body, [residual, *terms, grad], [vec], [BF], 1, "last_output")


def start_back(grad, vec):
    def body(grad_ref, vec_ref, out_ref, sum_ref):
        low = (vec_ref[...][SC_MLP : SC_MLP + 1, :] * grad_ref[...].astype(F32)).astype(BF)
        out_ref[...] = low
        add_rows(sum_ref, [low.astype(F32)])

    return rowwise(body, [grad], [vec], [BF], 1, "start_back")


def back_second(grad, residual, attended, terms, vec):
    count = len(terms)

    def body(*refs):
        grad_ref, res_ref, att_ref = refs[:3]
        term_refs = refs[3 : 3 + count]
        vec_ref, dres_ref, low_ref, sum_ref = refs[3 + count :]
        v = vec_ref[...]
        dn = total(term_refs)
        back, dgain = norm_back(res_ref[...], dn, v[LN2_G : LN2_G + 1, :])
        dres = grad_ref[...].astype(F32) + back
        low = (v[SC_ATTN : SC_ATTN + 1, :] * dres).astype(BF)
        dres_ref[...] = dres
        low_ref[...] = low
        add_rows(sum_ref, [dgain, dn, dres * att_ref[...].astype(F32), low.astype(F32)])

    return rowwise(
        body, [grad, residual, attended, *terms], [vec], [F32, BF], 4, "back_second"
    )


def back_first(dres, x, terms, vec, mlp_below=None, vec_below=None):
    count = len(terms)
    below = mlp_below is not None

    def body(*refs):
        dres_ref, x_ref = refs[:2]
        term_refs = refs[2 : 2 + count]
        rest = refs[2 + count :]
        if below:
            mlp_ref, vec_ref, under_ref, dx_ref, low_ref, sum_ref = rest
        else:
            vec_ref, dx_ref, sum_ref = rest
        v = vec_ref[...]
        dn = total(term_refs)
        back, dgain = norm_back(x_ref[...].astype(F32), dn, v[LN1_G : LN1_G + 1, :])
        dx = (dres_ref[...] + back).astype(BF)
        dx_ref[...] = dx
        rows = [dgain, dn]
        if below:
            wide = dx.astype(F32)
            low = (under_ref[...][SC_MLP : SC_MLP + 1, :] * wide).astype(BF)
            low_ref[...] = low
            rows += [wide * mlp_ref[...].astype(F32), low.astype(F32)]
        add_rows(sum_ref, rows)

    row_ins = [dres, x, *terms] + ([mlp_below] if below else [])
    fulls = [vec] + ([vec_below] if below else [])
    return rowwise(body, row_ins, fulls, [BF, BF] if below else [BF], 4 if below else 2, "back_first")


def project_qkv(pair, weight, bias):
    rows, width = pair[0].shape
    cols = bias.shape[1]

    def body(a_ref, b_ref, w_ref, bias_ref, out_ref):
        w = w_ref[...]
        shift = bias_ref[...]
        out_ref[:rows, :] = (dot(a_ref[...], w) + shift).astype(BF)
        out_ref[rows:, :] = (dot(b_ref[...], w) + shift).astype(BF)

    whole = lambda i: (0, 0)
    return pl.pallas_call(
        body,
        grid=(1,),
        in_specs=[
            pl.BlockSpec((rows, width), whole),
            pl.BlockSpec((rows, width), whole),
            pl.BlockSpec((width, cols), whole),
            pl.BlockSpec((1, cols), whole),
        ],
        out_specs=pl.BlockSpec((2 * rows, cols), whole),
        out_shape=sds((2 * rows, cols), BF),
        compiler_params=params(16, 1),
        cost_estimate=cost(4 * rows * width * cols, 2 * (2 * rows * (width + cols) + width * cols)),
        name="project_qkv",
    )(*pair, weight, bias)


def head_rows(v, head, size):
    rows = lax.broadcasted_iota(jnp.int32, v.shape, 0)
    return jnp.where(rows // size == head, v, jnp.zeros_like(v))


def head_cols(v, head, size):
    cols = lax.broadcasted_iota(jnp.int32, v.shape, 1)
    return jnp.where(cols // size == head, v, jnp.zeros_like(v))


def attention(packed, weight, size):
    chips = len(packed)
    span = packed[0].shape[0]
    half = span // 2
    width = packed[0].shape[1] // 3
    seq = chips * span
    heads = width // size
    model = weight.shape[0]
    step = min(256, seq)
    chunk = min(128, seq)
    score = size**-0.5

    def body(*refs):
        in_refs, w_ref = refs[:chips], refs[chips]
        head_refs = refs[chips + 1 : 2 * chips + 1]
        lse_ref = refs[2 * chips + 1]
        part_refs = refs[2 * chips + 2 : 4 * chips + 2]
        k_ref, qt_ref, vt_ref, ot_ref, s_ref, p_ref = refs[4 * chips + 2 :]
        for c in range(chips):
            at = slice(c * span, (c + 1) * span)
            k_ref[at, :] = in_refs[c][:, width : 2 * width]
            qt_ref[:, at] = (turn(in_refs[c][:, :width]) * score).astype(BF)
            vt_ref[:, at] = turn(in_refs[c][:, 2 * width :]).astype(BF)

        def one(i, carry):
            at = pl.ds(pl.multiple_of(i * step, step), step)
            q = qt_ref[:, at]
            s_ref[0] = dot(k_ref[...], head_rows(q, 0, size))
            for h in range(heads):
                if h + 1 < heads:
                    s_ref[(h + 1) % 2] = dot(k_ref[...], head_rows(q, h + 1, size))
                now = h % 2
                top = fold(s_ref[now, :chunk, :], jnp.max)
                for r in range(chunk, seq, chunk):
                    top = jnp.maximum(top, fold(s_ref[now, r : r + chunk, :], jnp.max))
                top = jnp.max(top, axis=0, keepdims=True)
                norm = jnp.zeros((8, step), F32)
                for r in range(0, seq, chunk):
                    p = jnp.exp(s_ref[now, r : r + chunk, :] - top)
                    norm = norm + fold(p, jnp.sum)
                    p_ref[now, r : r + chunk, :] = p.astype(BF)
                norm = jnp.sum(norm, axis=0, keepdims=True)
                rows = slice(h * size, (h + 1) * size)
                ot_ref[rows, at] = dot(vt_ref[rows, :], p_ref[now]) / norm
                lse_ref[h : h + 1, at] = top + jnp.log(norm)
            return carry

        lax.fori_loop(0, seq // step, one, 0)
        for c in range(chips):
            at = slice(c * span, (c + 1) * span)
            o = ot_ref[:, at].T.astype(BF)
            head_refs[c][...] = o
            part_refs[2 * c][...] = dot_bt(o[:half], w_ref[...]).astype(BF)
            part_refs[2 * c + 1][...] = dot_bt(o[half:], w_ref[...]).astype(BF)

    whole = lambda i: (0, 0)
    full = lambda shape: pl.BlockSpec(shape, whole)
    out = pl.pallas_call(
        body,
        grid=(1,),
        in_specs=[full((span, 3 * width))] * chips + [pl.BlockSpec((model, width), lambda i: (0, 3))],
        out_specs=[full((span, width))] * chips
        + [full((heads, seq))]
        + [full((half, model))] * (2 * chips),
        out_shape=[sds((span, width), BF)] * chips
        + [sds((heads, seq), F32)]
        + [sds((half, model), BF)] * (2 * chips),
        scratch_shapes=[
            pltpu.VMEM((seq, width), BF),
            pltpu.VMEM((width, seq), BF),
            pltpu.VMEM((width, seq), BF),
            pltpu.VMEM((width, seq), F32),
            pltpu.VMEM((2, seq, step), F32),
            pltpu.VMEM((2, seq, step), BF),
        ],
        compiler_params=params(20, 1),
        cost_estimate=cost(
            16 * seq * seq * width, 2 * seq * (4 * width + model), heads * seq * seq
        ),
        name="attention",
    )(*packed, weight)
    parts = out[chips + 1 :]
    return out[:chips], out[chips], [(parts[2 * c], parts[2 * c + 1]) for c in range(chips)]


def attention_back(packed, heads_kept, lse, datt, weight, size):
    chips = len(packed)
    span = packed[0].shape[0]
    half = span // 2
    width = packed[0].shape[1] // 3
    seq = chips * span
    heads = width // size
    model = weight.shape[0]
    step = min(256, seq)
    chunk = min(128, seq)
    score = size**-0.5

    def body(*refs):
        at = 0

        def take(count):
            nonlocal at
            at += count
            return refs[at - count : at]

        in_refs, kept_refs = take(chips), take(chips)
        (lse_ref,) = take(1)
        datt_refs = take(2 * chips)
        (w_ref,) = take(1)
        dqkv_refs = take(chips)
        part_refs = take(2 * chips)
        (sum_ref,) = take(1)
        k_ref, v_ref, kt_ref, qt_ref, q_ref, do_ref, dot_ref = take(7)
        inner_ref, s_ref, g_ref, p_ref, ds_ref, dk_ref, dv_ref, dqt_ref = take(8)
        for c in range(chips):
            rows = slice(c * span, (c + 1) * span)
            q = in_refs[c][:, :width].astype(F32) * score
            k = in_refs[c][:, width : 2 * width]
            q_ref[rows, :] = q.astype(BF)
            qt_ref[:, rows] = q.T.astype(BF)
            k_ref[rows, :] = k
            kt_ref[:, rows] = turn(k).astype(BF)
            v_ref[rows, :] = in_refs[c][:, 2 * width :]
            for b in range(2):
                d = dot(datt_refs[2 * c + b][...], w_ref[:, 3 * width :]).astype(BF)
                here = slice(c * span + b * half, c * span + (b + 1) * half)
                do_ref[here, :] = d
                dt = turn(d)
                dot_ref[:, here] = dt.astype(BF)
                prod = dt * turn(kept_refs[c][b * half : (b + 1) * half, :])
                for h in range(heads):
                    inner_ref[h : h + 1, here] = jnp.sum(
                        prod[h * size : (h + 1) * size, :], axis=0, keepdims=True
                    )

        def one(i, carry):
            at = pl.ds(pl.multiple_of(i * step, step), step)
            qt = qt_ref[:, at]
            dot_t = dot_ref[:, at]
            q = q_ref[at, :]
            do = do_ref[at, :]

            def scores(h):
                s_ref[h % 2] = dot(k_ref[...], head_rows(qt, h, size))
                g_ref[h % 2] = dot(v_ref[...], head_rows(dot_t, h, size))

            scores(0)
            for h in range(heads):
                if h + 1 < heads:
                    scores(h + 1)
                now = h % 2
                cols = slice(h * step, (h + 1) * step)
                lse = lse_ref[h : h + 1, at]
                inner = inner_ref[h : h + 1, at]
                for r in range(0, seq, chunk):
                    p = jnp.exp(s_ref[now, r : r + chunk, :] - lse)
                    ds = p * (g_ref[now, r : r + chunk, :] - inner)
                    p_ref[r : r + chunk, cols] = p.astype(BF)
                    ds_ref[r : r + chunk, cols] = ds.astype(BF)
                rows = slice(h * size, (h + 1) * size)
                dqt_ref[rows, at] = dot(kt_ref[rows, :], ds_ref[:, cols]) * score
            dv = dot(p_ref[...], jnp.concatenate([head_cols(do, h, size) for h in range(heads)], 0))
            dk = dot(ds_ref[...], jnp.concatenate([head_cols(q, h, size) for h in range(heads)], 0))

            @pl.when(i == 0)
            def _():
                dv_ref[...] = dv
                dk_ref[...] = dk

            @pl.when(i > 0)
            def _():
                dv_ref[...] += dv
                dk_ref[...] += dk

            return carry

        lax.fori_loop(0, seq // step, one, 0)
        for c in range(chips):
            rows = slice(c * span, (c + 1) * span)
            out = dqkv_refs[c]
            out[:, :width] = dqt_ref[:, rows].T.astype(BF)
            out[:, width : 2 * width] = dk_ref[rows, :].astype(BF)
            out[:, 2 * width :] = dv_ref[rows, :].astype(BF)
            sums = jnp.sum(out[...].astype(F32), axis=0, keepdims=True)
            if c == 0:
                sum_ref[...] = sums
            else:
                sum_ref[...] += sums
            for b in range(2):
                part_refs[2 * c + b][...] = dot_bt(
                    out[b * half : (b + 1) * half, :], w_ref[:, : 3 * width]
                ).astype(BF)

    flat = [g for pair in datt for g in pair]
    whole = lambda i: (0, 0)
    full = lambda a: pl.BlockSpec(a.shape, whole)
    out_shape = (
        [sds((span, 3 * width), BF)] * chips
        + [sds((half, model), BF)] * (2 * chips)
        + [sds((1, 3 * width), F32)]
    )
    operands = (*packed, *heads_kept, lse, *flat, weight)
    out = pl.pallas_call(
        body,
        grid=(1,),
        in_specs=[full(a) for a in operands],
        out_specs=[full(a) for a in out_shape],
        out_shape=out_shape,
        scratch_shapes=[
            pltpu.VMEM((seq, width), BF),
            pltpu.VMEM((seq, width), BF),
            pltpu.VMEM((width, seq), BF),
            pltpu.VMEM((width, seq), BF),
            pltpu.VMEM((seq, width), BF),
            pltpu.VMEM((seq, width), BF),
            pltpu.VMEM((width, seq), BF),
            pltpu.VMEM((heads, seq), F32),
            pltpu.VMEM((2, seq, step), F32),
            pltpu.VMEM((2, seq, step), F32),
            pltpu.VMEM((seq, heads * step), BF),
            pltpu.VMEM((seq, heads * step), BF),
            pltpu.VMEM((seq, width), F32),
            pltpu.VMEM((seq, width), F32),
            pltpu.VMEM((width, seq), F32),
        ],
        compiler_params=params(36, 1),
        cost_estimate=cost(
            40 * seq * seq * width, 2 * seq * (8 * width + 2 * model), heads * seq * seq
        ),
        name="attention_back",
    )(*operands)
    parts = out[chips : 3 * chips]
    return (
        out[:chips],
        [(parts[2 * c], parts[2 * c + 1]) for c in range(chips)],
        out[3 * chips],
    )


def gelu_both(x):
    away = jnp.abs(x)
    t = 1.0 / (1.0 + (0.3275911 * 0.5**0.5) * away)
    bell = jnp.exp(-0.5 * (x * x))
    poly = t * (
        0.127414796
        + t * (-0.142248368 + t * (0.7107068705 + t * (-0.7265760135 + t * 0.5307027145)))
    )
    tail = poly * bell
    phi = jnp.where(x >= 0, 1.0 - tail, tail)
    return x * phi, phi + x * (bell * 0.3989422804014327)


def mlp_call(body, pairs, extra, weight, bias, outs, parts, scratch, name):
    rows, model = pairs[0].shape
    units = weight.shape[1] // 2
    step = min(256, units)
    blocks = units // step
    whole = lambda j: (0, 0)
    cols = lambda j: (0, j)
    in_specs = [pl.BlockSpec((rows, model), whole) for _ in pairs]
    in_specs += [pl.BlockSpec((2 * rows, step), cols) for _ in extra]
    in_specs += [
        pl.BlockSpec((model, step), cols),
        pl.BlockSpec((model, step), lambda j: (0, blocks + j)),
        pl.BlockSpec((1, step), cols),
    ]
    out_specs = [pl.BlockSpec((2 * rows, step), cols) for _ in outs]
    out_specs += [pl.BlockSpec((1, step), cols)]
    out_specs += [pl.BlockSpec((rows, model), whole)] * (2 * parts)
    out_shape = [sds((2 * rows, units), d) for d in outs] + [sds((1, units), F32)]
    out_shape += [sds((rows, model), BF)] * (2 * parts)
    count = len(pairs) // 2
    return pl.pallas_call(
        body,
        grid=(blocks,),
        in_specs=in_specs,
        out_specs=out_specs,
        out_shape=out_shape,
        scratch_shapes=[pltpu.VMEM((2 * rows, model), F32)] * parts
        + [pltpu.VMEM((2 * rows, step), F32)] * scratch,
        compiler_params=params(20 + 8 * (parts - 1), 1),
        cost_estimate=cost(
            8 * count * rows * model * units,
            4 * model * units + 4 * rows * (model + units) * (count + 1),
        ),
        name=name,
    )(*pairs, *extra, weight, weight, bias)


def clear(*refs):
    @pl.when(pl.program_id(0) == 0)
    def _():
        for ref in refs:
            ref[...] = jnp.zeros_like(ref)


def finish(acc, low, high):
    rows = low.shape[0]

    @pl.when(pl.program_id(0) == pl.num_programs(0) - 1)
    def _():
        low[...] = acc[:rows, :].astype(BF)
        high[...] = acc[rows:, :].astype(BF)


CHUNK = 32


def mlp_forward(pair, weight, bias):
    rows = pair[0].shape[0]

    def body(a, b, w1_ref, w2_ref, bias_ref, act_ref, slope_ref, sum_ref, lo, hi, acc, pre):
        clear(acc, sum_ref)
        shift = bias_ref[...]
        for i, x in enumerate((a, b)):
            pre[i * rows : (i + 1) * rows, :] = dot(x[...], w1_ref[...])
        for i in range(2):
            at = slice(i * rows, (i + 1) * rows)
            for r in range(i * rows, (i + 1) * rows, CHUNK):
                act, slope = gelu_both(pre[r : r + CHUNK, :] + shift)
                act_ref[r : r + CHUNK, :] = act.astype(BF)
                slope_ref[r : r + CHUNK, :] = slope.astype(BF)
            acc[at, :] += dot_bt(act_ref[at, :], w2_ref[...])
        finish(acc, lo, hi)

    act, slope, _, lo, hi = mlp_call(body, pair, [], weight, bias, [BF, BF], 1, 1, "mlp_forward")
    return act, slope, (lo, hi)


def mlp_backward(pair, slope, weight, bias):
    rows = pair[0].shape[0]

    def body(a, b, slope_ref, w1_ref, w2_ref, bias_ref, dpre_ref, sum_ref, lo, hi, acc, pre):
        clear(acc)
        for i, g in enumerate((a, b)):
            pre[i * rows : (i + 1) * rows, :] = dot(g[...], w2_ref[...])
        sums = jnp.zeros((8, bias_ref.shape[1]), F32)
        for i in range(2):
            at = slice(i * rows, (i + 1) * rows)
            for r in range(i * rows, (i + 1) * rows, CHUNK):
                d = pre[r : r + CHUNK, :] * slope_ref[r : r + CHUNK, :].astype(F32)
                d = d.astype(BF)
                dpre_ref[r : r + CHUNK, :] = d
                sums = sums + fold(d.astype(F32), jnp.sum)
            acc[at, :] += dot_bt(dpre_ref[at, :], w1_ref[...])
        sum_ref[...] = jnp.sum(sums, axis=0, keepdims=True)
        finish(acc, lo, hi)

    dpre, sums, lo, hi = mlp_call(
        body, pair, [slope], weight, bias, [BF], 1, 1, "mlp_backward"
    )
    return dpre, sums, (lo, hi)


def mlp_both(pair, grads, weight, bias):
    rows = pair[0].shape[0]

    def body(
        a, b, c, d, w1_ref, w2_ref, bias_ref, act_ref, dpre_ref, sum_ref,
        lo, hi, blo, bhi, acc, back, pre, grad,
    ):
        clear(acc, back)
        shift = bias_ref[...]
        for i, (x, g) in enumerate(((a, c), (b, d))):
            at = slice(i * rows, (i + 1) * rows)
            pre[at, :] = dot(x[...], w1_ref[...])
            grad[at, :] = dot(g[...], w2_ref[...])
        sums = jnp.zeros((8, bias_ref.shape[1]), F32)
        for i in range(2):
            at = slice(i * rows, (i + 1) * rows)
            for r in range(i * rows, (i + 1) * rows, CHUNK):
                act, slope = gelu_both(pre[r : r + CHUNK, :] + shift)
                act_ref[r : r + CHUNK, :] = act.astype(BF)
                dpre = (grad[r : r + CHUNK, :] * slope).astype(BF)
                dpre_ref[r : r + CHUNK, :] = dpre
                sums = sums + fold(dpre.astype(F32), jnp.sum)
            back[at, :] += dot_bt(dpre_ref[at, :], w1_ref[...])
            acc[at, :] += dot_bt(act_ref[at, :], w2_ref[...])
        sum_ref[...] = jnp.sum(sums, axis=0, keepdims=True)
        finish(acc, lo, hi)
        finish(back, blo, bhi)

    act, dpre, sums, lo, hi, blo, bhi = mlp_call(
        body, [*pair, *grads], [], weight, bias, [BF, BF], 2, 2, "mlp_both"
    )
    return act, dpre, sums, (lo, hi), (blo, bhi)


def weight_grads(products, name):
    model = products[0][0][0].shape[1]
    step = min(256, model)
    sizes = [(len(left), len(right), right[0].shape[1]) for left, right in products]
    cols = sum(n for _, _, n in sizes)
    tokens = sum(a.shape[0] for a in products[0][0])

    def body(*refs):
        out = refs[-1]
        at = base = 0
        for many, few, n in sizes:
            lefts, rights = refs[at : at + many], refs[at + many : at + many + few]
            at += many + few
            ratio = many // few
            acc = None
            for i in range(many):
                size = lefts[i].shape[0]
                here = slice((i % ratio) * size, (i % ratio + 1) * size)
                term = dot_at(lefts[i][...], rights[i // ratio][here, :])
                acc = term if acc is None else acc + term
            out[:, base : base + n] = acc.astype(BF)
            base += n

    specs, operands = [], []
    for left, right in products:
        specs += [pl.BlockSpec((a.shape[0], step), lambda i: (0, i)) for a in left]
        specs += [pl.BlockSpec(b.shape, lambda i: (0, 0)) for b in right]
        operands += [*left, *right]
    return pl.pallas_call(
        body,
        grid=(model // step,),
        in_specs=specs,
        out_specs=pl.BlockSpec((step, cols), lambda i: (i, 0)),
        out_shape=sds((model, cols), BF),
        compiler_params=params(24, 1),
        cost_estimate=cost(
            2 * tokens * model * cols, 2 * (tokens * (2 * model + cols) + model * cols)
        ),
        name=name,
    )(*operands)


def pieces(chunks):
    return [p for pair in chunks for p in pair]


def shards(
    tokens, cotangent, ln1_gain, ln1_bias, w_qkv, qv_bias, w_out, out_bias, scale_attn,
    ln2_gain, ln2_bias, w_fc1, fc1_bias, w_fc2, fc2_bias, scale_mlp,
):
    side = lax.axis_index("section")
    first = side == 0
    dp = lax.axis_size("dp")
    here = lax.axis_index("dp")
    chips = lax.axis_size("tensor") // 2
    rows, model = tokens.shape[2:]
    heads = qv_bias.shape[1]
    size = qv_bias.shape[2] * dp // 2
    width = heads * size
    units = w_fc1.shape[2]
    part = model // dp

    x0 = lax.dynamic_index_in_dim(tokens, side, 0, keepdims=False).reshape(rows, model)
    grad_top = lax.dynamic_index_in_dim(cotangent, side, 0, keepdims=False).reshape(rows, model)

    vectors = (ln1_gain, ln1_bias, out_bias, scale_attn, ln2_gain, ln2_bias, fc2_bias, scale_mlp)
    packed = jnp.concatenate(
        [v.reshape(-1) for v in vectors] + [fc1_bias.reshape(-1), qv_bias.reshape(-1)]
    )
    own_qkv = w_qkv.reshape(part, heads, 3, size).swapaxes(1, 2).reshape(part, 3 * width)
    own_att = jnp.concatenate([own_qkv, w_out[0].T], axis=1)
    came_att = swap_section(own_att)
    small = gather_small(packed, first).astype(F32)
    cut = 8 * part
    vecs = small[:, :, :cut].reshape(2, dp, 8, part).swapaxes(1, 2).reshape(2, 8, model)
    bias_fc1 = small[:, :, cut : cut + units // dp].reshape(2, 1, units)
    qv = small[:, :, cut + units // dp :].reshape(2, dp, heads, -1).swapaxes(1, 2)
    qv = qv.reshape(2, heads, 2, size)
    bias_qkv = jnp.stack([qv[:, :, 0], jnp.zeros_like(qv[:, :, 0]), qv[:, :, 1]], axis=1)
    bias_qkv = bias_qkv.reshape(2, 1, 3 * width)
    vecs = (vecs[0], vecs[1])

    norm1 = norm_first(x0, vecs[0])
    own_ff = jnp.concatenate([w_fc1[0], w_fc2[0].T], axis=1)
    came_ff = swap_section(tie(own_ff, came_att))
    shard_att0 = tie(jnp.where(first, own_att, came_att), norm1)
    shard_ff0 = jnp.where(first, own_ff, came_ff)
    shard_att1 = jnp.where(first, came_att, own_att)
    shard_ff1 = jnp.where(first, came_ff, own_ff)
    came_att0 = spread(shard_att0, side)
    came_ff0 = spread(tie(shard_ff0, came_att0[-1]), side)
    came_att1 = spread(tie(shard_att1, came_ff0[-1]), side)
    ff1 = split_gather(tie(shard_ff1, came_att1[-1]), side)

    def front(x, norm, weight, s):
        chunks, qkv = gather_tokens(norm, lambda pair: project_qkv(pair, weight, bias_qkv[s]))
        kept, lse, parts = attention(qkv, weight, size)
        terms, sent = scatter_tokens(parts, lambda after: after)
        attended, residual, norm2 = after_attention(x, terms, vecs[s])
        return (chunks, qkv, kept, lse, attended, residual), norm2, sent

    att0 = put_together(shard_att0, came_att0, norm1)
    saved0, norm2, sent = front(x0, norm1, att0, 0)
    ff0 = put_together(shard_ff0, came_ff0, sent)
    second0, mlp0 = gather_tokens(norm2, lambda pair: mlp_forward(pair, ff0, bias_fc1[0]))
    att1 = put_together(shard_att1, came_att1, mlp0[0][0])
    terms, _ = scatter_tokens([m[2] for m in mlp0])
    mlp_out0, y0, norm1 = after_mlp(saved0[5], terms, vecs[0], vecs[1])

    low1, sums_fc2_1 = start_back(grad_top, vecs[1])
    grads1, _ = gather_tokens(tie(low1, norm1), lambda pair: pair[0])
    saved1, norm2, _ = front(y0, norm1, att1, 1)
    spare = list(grads1)
    second1, mlp1 = gather_tokens(
        norm2, lambda pair: mlp_both(pair, spare.pop(0), ff1, bias_fc1[1])
    )

    def attention_back_part(s, weight, grad, saved, parts, ff_work, more_work, last_work):
        chunks, qkv, kept, lse, attended, residual = saved
        terms, g_ff = scatter_tokens(parts, ff_work)
        dres, low, sums = back_second(grad, residual, attended, terms, vecs[s])
        datt, _ = gather_tokens(low, lambda pair: pair[0])
        before, beside = more_work(datt)
        dqkv, parts, qkv_sums = attention_back(
            [tie(qkv[0], before), *qkv[1:]], kept, lse, datt, weight, size
        )
        parts = [parts[0], *[(same, tie(other, beside)) for same, other in parts[1:]]]
        terms, made = scatter_tokens(
            parts, lambda after: last_work(after, datt, dqkv)
        )
        return dres, sums, terms, qkv_sums, g_ff, before, beside, made

    def grad_ff(second, mlp, grads, acts):
        def work(after):
            return weight_grads(
                [(pieces(second), [tie(mlp[0], after), *mlp[1:]]), (pieces(grads), acts)], "grad_ff"
            )

        return work

    acts1 = [m[0] for m in mlp1]
    parts_y1 = [m[3] for m in mlp1]
    sums_y1 = core_sums(parts_y1)
    local_y1 = [parts_y1[0][0], core_swap(parts_y1[0][1])]
    dres1, sums1, terms, qkv_sums1, g_ff1, _, terms_y1, g_att1 = attention_back_part(
        1, att1, grad_top, saved1, [m[4] for m in mlp1],
        grad_ff(second1, [m[1] for m in mlp1], grads1, acts1),
        lambda datt: (datt[0][0], send_sums([tie(v, datt[-1][0]) for v in sums_y1])),
        lambda after, datt, dqkv: weight_grads(
            [(pieces(saved1[0]), [tie(dqkv[0], after), *dqkv[1:]]), (pieces(datt), saved1[2])],
            "grad_att",
        ),
    )
    dx1, low0, edge1 = back_first(dres1, y0, terms, vecs[1], mlp_out0, vecs[0])
    y1, sums_sc_1 = last_output(saved1[5], local_y1 + terms_y1, grad_top, vecs[1])
    rs_ff1 = scatter_sum(g_ff1)
    parts_att1 = send_parts(g_att1)

    slopes = [m[1] for m in mlp0]
    grads0, mlp_back0 = gather_tokens(
        low0, lambda pair: mlp_backward(pair, slopes.pop(0), ff0, bias_fc1[0])
    )
    dres0, sums0, terms, qkv_sums0, g_ff0, g_out0, _, g_qkv0 = attention_back_part(
        0, att0, dx1, saved0, [m[2] for m in mlp_back0],
        grad_ff(second0, [m[0] for m in mlp_back0], grads0, [m[0] for m in mlp0]),
        lambda datt: (weight_grads([(pieces(datt), saved0[2])], "grad_out"), datt[0][0]),
        lambda after, datt, dqkv: weight_grads(
            [(pieces(saved0[0]), [tie(dqkv[0], after), *dqkv[1:]])], "grad_qkv"
        ),
    )
    rs_ff0 = scatter_sum(g_ff0)
    rs_out0 = sum_parts(send_parts(g_out0), (1, 0), g_qkv0)
    rs_att1 = sum_parts(parts_att1, (0, 1), g_qkv0)
    rs_qkv0 = sum_parts(send_parts(g_qkv0), (1, 0))
    dx0, edge0 = back_first(dres0, x0, terms, vecs[0])

    def both(low, high):
        mine = jnp.where(first, low, high)
        came_low = lax.ppermute(low, "section", [(1, 0)])
        came_high = lax.ppermute(high, "section", [(0, 1)])
        came = jnp.where(first, came_low, came_high)
        return jnp.stack([jnp.where(first, mine, came), jnp.where(first, came, mine)])[None, :, None]

    block_out = both(y0, y1)
    input_grads = both(dx0, dx1)

    def to_owner(low, high, pick):
        own = jnp.where(first, low, high) + swap_section(jnp.where(first, high, low))
        out = pick(own, here)
        for step in range(1, dp):
            pairs = [(i, (i + step) % dp) for i in range(dp)]
            out = out + lax.ppermute(pick(own, lax.rem(here + step, dp)), "dp", pairs)
        return out

    def by_unit(qkv_sums, unit_sums):
        q = qkv_sums[:, :width].reshape(heads, 1, size)
        v = qkv_sums[:, 2 * width :].reshape(heads, 1, size)
        bias = jnp.concatenate([q, v], 1).reshape(heads, dp, -1).swapaxes(0, 1).reshape(dp, -1)
        return jnp.concatenate([bias, unit_sums.reshape(dp, -1)], axis=1)

    unit = to_owner(
        by_unit(qkv_sums0, sum(m[1] for m in mlp_back0)),
        by_unit(qkv_sums1, sum(m[2] for m in mlp1)),
        lambda v, place: lax.dynamic_slice_in_dim(v, place, 1, 0),
    )
    cut = heads * (2 * size // dp)
    bias_grad = unit[:, :cut].reshape(1, heads, -1)
    fc1_grad = unit[:, cut:].reshape(1, 1, -1)

    vec = jnp.concatenate(
        [edge0[:2], sums0[:4], edge1[2:4], edge1[:2], sums1[:4], sums_sc_1[:1], sums_fc2_1[:1]]
    )
    vec = vec + core_swap(vec)
    vec = sum([from_chip(vec, step) for step in range(1, chips)], vec)
    vec = to_owner(
        vec[:8], vec[8:], lambda v, place: lax.dynamic_slice_in_dim(v, place * part, part, 1)
    )
    g_ln1, b_ln1, g_ln2, b_ln2, g_sc_attn, g_out_bias, g_sc_mlp, g_fc2_bias = (
        vec[i : i + 1] for i in range(8)
    )

    def owned(low, high):
        came_low = lax.ppermute(low, "section", [(1, 0)])
        came_high = lax.ppermute(high, "section", [(0, 1)])
        top = jnp.where(first, low, came_high)
        bottom = jnp.where(first, came_low, high)
        return jnp.concatenate([top, bottom], 0)

    g_ff = owned(rs_ff0, rs_ff1)

    def chosen(low, high):
        return jnp.where(first, low[0] + low[1].astype(F32), high[0] + high[1].astype(F32))

    g_qkv = chosen(rs_qkv0, [v[:, : 3 * width] for v in rs_att1])
    g_qkv = g_qkv.reshape(part, 3, heads, size).swapaxes(1, 2).reshape(1, part, 3 * width)
    g_out = chosen(rs_out0, [v[:, 3 * width :] for v in rs_att1]).T[None]
    g_fc1 = g_ff[:, :units][None].astype(F32)
    g_fc2 = g_ff[:, units:].T[None].astype(F32)
    return (
        block_out, input_grads, g_ln1, b_ln1, g_qkv, bias_grad, g_out, g_out_bias, g_sc_attn,
        g_ln2, b_ln2, g_fc1, fc1_grad, g_fc2, g_fc2_bias, g_sc_mlp,
    )


def solution(mesh):
    vec = P("section", "dp")
    by_row = P("section", "dp", "tensor")
    by_unit = P("section", "tensor", "dp")
    data = P(None, "dp", "tensor", None)
    split = P("section", None, "dp", "tensor", None)
    given = (
        vec, vec, by_row, by_unit, by_unit, vec, vec, vec, vec, by_row, by_unit, by_unit, vec, vec,
    )
    return jax.shard_map(
        shards,
        mesh=mesh,
        in_specs=(data, data) + given,
        out_specs=(split, split) + given,
        check_vma=False,
    )
```

```python
from functools import partial

import jax
import jax.numpy as jnp
from jax import lax
from jax.experimental import pallas as pl
from jax.experimental.pallas import tpu as pltpu
from jax.sharding import PartitionSpec as P

EPSILON = 1e-06
BF = jnp.bfloat16
F32 = jnp.float32
MIB = 1 << 20

LN1_G, LN1_B, OUT_B, SC_ATTN, LN2_G, LN2_B, FC2_B, SC_MLP = range(8)


def dot(a, b):
    return lax.dot_general(a, b, (((1,), (0,)), ((), ())), preferred_element_type=F32)


def dot_bt(a, b):
    return lax.dot_general(a, b, (((1,), (1,)), ((), ())), preferred_element_type=F32)


def dot_at(a, b):
    return lax.dot_general(a, b, (((0,), (0,)), ((), ())), preferred_element_type=F32)


def turn(v):
    return v.astype(F32).T


def params(limit, grid=0):
    return pltpu.CompilerParams(
        vmem_limit_bytes=limit * MIB,
        dimension_semantics=("arbitrary",) * grid if grid else None,
    )


def cost(flops, nbytes, trans=0):
    return pl.CostEstimate(flops=0, bytes_accessed=0, transcendentals=0)


def sds(shape, dtype):
    return jax.ShapeDtypeStruct(shape, dtype)


def core_swap(v):
    count = lax.axis_size("tensor")
    return lax.ppermute(v, "tensor", [(i, i ^ 1) for i in range(count)])


def from_chip(v, step):
    count = lax.axis_size("tensor")
    chips = count // 2
    pairs = [(((i // 2 + step) % chips) * 2 + i % 2, i) for i in range(count)]
    return lax.ppermute(v, "tensor", pairs)


def tie(v, *after):
    return lax.optimization_barrier((v, *after))[0]


def tie_all(vs, *after):
    return lax.optimization_barrier((*vs, *after))[: len(vs)]


def gather_tokens(own, work, beside=()):
    chips = lax.axis_size("tensor") // 2
    came = [from_chip(own, step) for step in range(1, chips)]
    chunks = [(own, core_swap(own))]
    results = [work(chunks[0])]
    for same in came:
        same = tie(same, results[-1], *beside)
        chunks.append((same, core_swap(same)))
        results.append(work(chunks[-1]))
    return chunks, results


def core_sums(parts):
    return [
        (same.astype(F32) + core_swap(other).astype(F32)).astype(BF) for same, other in parts[1:]
    ]


def send_sums(sums):
    chips = len(sums) + 1
    return [from_chip(both, chips - step) for step, both in enumerate(sums, 1)]


def scatter_tokens(parts, work=None, beside=()):
    sums = core_sums(parts)
    terms = send_sums(sums)
    local = core_swap(tie(parts[0][1], sums[-1]))
    made = work(sums[-1]) if work else local
    terms = [tie(t, made, local, *beside) for t in terms]
    return [parts[0][0], *terms, local], made


def swap_section(v):
    return lax.ppermute(v, "section", [(0, 1), (1, 0)])


def assemble(same, other, rows):
    half, cols = same[0].shape
    count = len(same)
    place = jnp.stack([lax.axis_index("dp"), lax.axis_index("section")])

    def body(place_ref, *refs):
        same_refs, other_refs = refs[:count], refs[count : 2 * count]
        out_ref, sems = refs[2 * count :]
        z, x = place_ref[0], place_ref[1]
        started = []
        for k in range(count):
            base = lax.rem(z + (count - k), count) * (2 * half)
            for ref, at in ((same_refs[k], base + x * half), (other_refs[k], base + (1 - x) * half)):
                at = pl.multiple_of(at, half)
                copy = pltpu.make_async_copy(
                    ref, out_ref.at[pl.ds(at, half), :], sems.at[len(started)]
                )
                copy.start()
                started.append(copy)
        for copy in started:
            copy.wait()

    hbm = pl.BlockSpec(memory_space=pl.ANY)
    return pl.pallas_call(
        body,
        in_specs=[pl.BlockSpec(memory_space=pltpu.SMEM)] + [hbm] * (2 * count),
        out_specs=pl.BlockSpec(memory_space=pltpu.VMEM),
        out_shape=sds((rows, cols), same[0].dtype),
        scratch_shapes=[pltpu.SemaphoreType.DMA((2 * count,))],
        compiler_params=params(16),
        cost_estimate=cost(0, 4 * rows * cols),
        name="assemble",
    )(place, *same, *other)


def half_of(v, which):
    half = v.shape[0] // 2
    return lax.dynamic_slice_in_dim(v, which * half, half, 0)


def ring(own):
    count = lax.axis_size("dp")
    pairs = [(i, (i + 1) % count) for i in range(count)]
    hops = []
    for _ in range(count - 1):
        own = lax.ppermute(own, "dp", pairs)
        hops.append(own)
    return hops


def direct(own):
    count = lax.axis_size("dp")
    return [
        lax.ppermute(own, "dp", [(i, (i + step) % count) for i in range(count)])
        for step in range(1, count)
    ]


def thirds(values):
    count = len(values)
    cuts = [-(-count * i // 3) for i in range(4)]
    return [values[a:b] for a, b in zip(cuts, cuts[1:])]


def gather_small(v, first):
    count = lax.axis_size("dp")
    came = swap_section(v)
    own = jnp.stack([jnp.where(first, v, came), jnp.where(first, came, v)])
    ahead = [own]
    for step in range(1, count):
        ahead.append(lax.ppermute(own, "dp", [(i, (i - step) % count) for i in range(count)]))
    twice = jnp.stack(ahead + ahead, axis=1)
    return lax.dynamic_slice_in_dim(twice, count - lax.axis_index("dp"), count, 1)


def ring_sum(mine, other, pair):
    dp = lax.axis_size("dp")
    here = lax.axis_index("dp")
    part = mine.shape[0] // dp
    pairs = [(i, (i + 1) % dp) for i in range(dp)]
    rows = lambda v, back: lax.dynamic_slice_in_dim(
        v, lax.rem(here + (dp - back), dp) * part, part, 0
    )
    steps, going = [], None
    for back in range(1, dp + 1):
        step = [] if going is None else [lax.ppermute(going, "dp", pairs)]
        came = swap_section(tie(rows(other, back), *(steps[-1][:1] if steps else ())))
        terms = [rows(mine, back), came, *step]
        going = sum(t.astype(F32) for t in terms)
        if back < dp:
            going = going.astype(BF)
        steps.append([*step, came])
    steps.append([lax.ppermute(going.astype(BF), "section", [pair])])
    return steps, going


def standardize(v):
    centred = v - jnp.mean(v, axis=-1, keepdims=True)
    var = jnp.mean(centred * centred, axis=-1, keepdims=True)
    scale = lax.rsqrt(var + EPSILON)
    return centred * scale, scale


def norm_of(v, vec, gain, shift):
    return (standardize(v)[0] * vec[gain : gain + 1, :] + vec[shift : shift + 1, :]).astype(BF)


def norm_back(v, grad, gain):
    xh, scale = standardize(v)
    dxh = grad * gain
    inner = jnp.mean(dxh * xh, axis=-1, keepdims=True)
    out = scale * (dxh - jnp.mean(dxh, axis=-1, keepdims=True) - xh * inner)
    return out, grad * xh


def total(refs):
    out = refs[0][...].astype(F32)
    for ref in refs[1:]:
        out = out + ref[...].astype(F32)
    return out


def fold(v, op):
    return op(v.reshape(-1, 8, v.shape[1]), axis=0)


def add_rows(ref, rows):
    for k, row in enumerate(rows):
        ref[8 * k : 8 * k + 8, :] += fold(row, jnp.sum)


def rowwise(body, row_ins, fulls, row_outs, sums, name):
    rows, width = row_ins[0].shape
    step = min(32, rows)
    many, some, outs = len(row_ins), len(fulls), len(row_outs)

    def kernel(*refs):
        in_refs, full_refs = refs[:many], refs[many : many + some]
        out_refs = refs[many + some : many + some + outs]
        extra = refs[many + some + outs :]
        if sums:
            extra[1][...] = jnp.zeros_like(extra[1])

        def one(i, carry):
            at = pl.ds(pl.multiple_of(i * step, step), step)
            body(
                *[r.at[at, :] for r in in_refs],
                *full_refs,
                *[r.at[at, :] for r in out_refs],
                *extra[1:],
            )
            return carry

        lax.fori_loop(0, rows // step, one, 0)
        for k in range(sums):
            extra[0][k : k + 1, :] = jnp.sum(
                extra[1][8 * k : 8 * k + 8, :], axis=0, keepdims=True
            )

    out_shape = [sds((rows, width), d) for d in row_outs]
    out_shape += [sds((sums, width), F32)] if sums else []
    full = lambda a: pl.BlockSpec(a.shape, lambda i: (0, 0))
    nbytes = sum(a.size * a.dtype.itemsize for a in row_ins) + sum(
        rows * width * jnp.dtype(d).itemsize for d in row_outs
    )
    return pl.pallas_call(
        kernel,
        grid=(1,),
        in_specs=[full(a) for a in (*row_ins, *fulls)],
        out_specs=[full(a) for a in out_shape],
        out_shape=out_shape,
        scratch_shapes=[pltpu.VMEM((8 * sums, width), F32)] if sums else [],
        compiler_params=params(20, 1),
        cost_estimate=cost(20 * rows * width, nbytes),
        name=name,
    )(*row_ins, *fulls)


def norm_first(x, vec):
    def body(x_ref, vec_ref, out_ref):
        out_ref[...] = norm_of(x_ref[...].astype(F32), vec_ref[...], LN1_G, LN1_B)

    return rowwise(body, [x], [vec], [BF], 0, "norm_first")[0]


def after_attention(x, terms, vec):
    count = len(terms)

    def body(*refs):
        x_ref, term_refs, vec_ref = refs[0], refs[1 : 1 + count], refs[1 + count]
        att_ref, res_ref, norm_ref = refs[2 + count :]
        v = vec_ref[...]
        attended = total(term_refs) + v[OUT_B : OUT_B + 1, :]
        residual = x_ref[...].astype(F32) + v[SC_ATTN : SC_ATTN + 1, :] * attended
        att_ref[...] = attended.astype(BF)
        res_ref[...] = residual
        norm_ref[...] = norm_of(residual, v, LN2_G, LN2_B)

    return rowwise(body, [x, *terms], [vec], [BF, F32, BF], 0, "after_attention")


def after_mlp(residual, terms, vec, vec_next):
    count = len(terms)

    def body(*refs):
        res_ref, term_refs = refs[0], refs[1 : 1 + count]
        vec_ref, next_ref, mlp_ref, y_ref, norm_ref = refs[1 + count :]
        v = vec_ref[...]
        mlp = total(term_refs) + v[FC2_B : FC2_B + 1, :]
        y = (res_ref[...] + v[SC_MLP : SC_MLP + 1, :] * mlp).astype(BF)
        mlp_ref[...] = mlp.astype(BF)
        y_ref[...] = y
        norm_ref[...] = norm_of(y.astype(F32), next_ref[...], LN1_G, LN1_B)

    return rowwise(body, [residual, *terms], [vec, vec_next], [BF, BF, BF], 0, "after_mlp")


def last_output(residual, terms, grad, vec):
    count = len(terms)

    def body(*refs):
        res_ref, term_refs = refs[0], refs[1 : 1 + count]
        grad_ref, vec_ref, y_ref, sum_ref = refs[1 + count :]
        v = vec_ref[...]
        mlp = total(term_refs) + v[FC2_B : FC2_B + 1, :]
        y_ref[...] = (res_ref[...] + v[SC_MLP : SC_MLP + 1, :] * mlp).astype(BF)
        add_rows(sum_ref, [grad_ref[...].astype(F32) * mlp])

    return rowwise(body, [residual, *terms, grad], [vec], [BF], 1, "last_output")


def start_back(grad, vec):
    def body(grad_ref, vec_ref, out_ref, sum_ref):
        low = (vec_ref[...][SC_MLP : SC_MLP + 1, :] * grad_ref[...].astype(F32)).astype(BF)
        out_ref[...] = low
        add_rows(sum_ref, [low.astype(F32)])

    return rowwise(body, [grad], [vec], [BF], 1, "start_back")


def back_second(grad, residual, attended, terms, vec):
    count = len(terms)

    def body(*refs):
        grad_ref, res_ref, att_ref = refs[:3]
        term_refs = refs[3 : 3 + count]
        vec_ref, dres_ref, low_ref, sum_ref = refs[3 + count :]
        v = vec_ref[...]
        dn = total(term_refs)
        back, dgain = norm_back(res_ref[...], dn, v[LN2_G : LN2_G + 1, :])
        dres = grad_ref[...].astype(F32) + back
        low = (v[SC_ATTN : SC_ATTN + 1, :] * dres).astype(BF)
        dres_ref[...] = dres
        low_ref[...] = low
        add_rows(sum_ref, [dgain, dn, dres * att_ref[...].astype(F32), low.astype(F32)])

    return rowwise(
        body, [grad, residual, attended, *terms], [vec], [F32, BF], 4, "back_second"
    )


def back_first(dres, x, terms, vec, mlp_below=None, vec_below=None):
    count = len(terms)
    below = mlp_below is not None

    def body(*refs):
        dres_ref, x_ref = refs[:2]
        term_refs = refs[2 : 2 + count]
        rest = refs[2 + count :]
        if below:
            mlp_ref, vec_ref, under_ref, dx_ref, low_ref, sum_ref = rest
        else:
            vec_ref, dx_ref, sum_ref = rest
        v = vec_ref[...]
        dn = total(term_refs)
        back, dgain = norm_back(x_ref[...].astype(F32), dn, v[LN1_G : LN1_G + 1, :])
        dx = (dres_ref[...] + back).astype(BF)
        dx_ref[...] = dx
        rows = [dgain, dn]
        if below:
            wide = dx.astype(F32)
            low = (under_ref[...][SC_MLP : SC_MLP + 1, :] * wide).astype(BF)
            low_ref[...] = low
            rows += [wide * mlp_ref[...].astype(F32), low.astype(F32)]
        add_rows(sum_ref, rows)

    row_ins = [dres, x, *terms] + ([mlp_below] if below else [])
    fulls = [vec] + ([vec_below] if below else [])
    return rowwise(body, row_ins, fulls, [BF, BF] if below else [BF], 4 if below else 2, "back_first")


def project_qkv(pair, weight, bias):
    rows, width = pair[0].shape
    cols = bias.shape[1]

    def body(a_ref, b_ref, w_ref, bias_ref, out_ref):
        w = w_ref[...]
        shift = bias_ref[...]
        out_ref[:rows, :] = (dot(a_ref[...], w) + shift).astype(BF)
        out_ref[rows:, :] = (dot(b_ref[...], w) + shift).astype(BF)

    whole = lambda i: (0, 0)
    return pl.pallas_call(
        body,
        grid=(1,),
        in_specs=[
            pl.BlockSpec((rows, width), whole),
            pl.BlockSpec((rows, width), whole),
            pl.BlockSpec((width, cols), whole),
            pl.BlockSpec((1, cols), whole),
        ],
        out_specs=pl.BlockSpec((2 * rows, cols), whole),
        out_shape=sds((2 * rows, cols), BF),
        compiler_params=params(16, 1),
        cost_estimate=cost(4 * rows * width * cols, 2 * (2 * rows * (width + cols) + width * cols)),
        name="project_qkv",
    )(*pair, weight, bias)


def head_rows(v, head, size):
    rows = lax.broadcasted_iota(jnp.int32, v.shape, 0)
    return jnp.where(rows // size == head, v, jnp.zeros_like(v))


def head_cols(v, head, size):
    cols = lax.broadcasted_iota(jnp.int32, v.shape, 1)
    return jnp.where(cols // size == head, v, jnp.zeros_like(v))


def attention(packed, weight, size):
    chips = len(packed)
    span = packed[0].shape[0]
    half = span // 2
    width = packed[0].shape[1] // 3
    seq = chips * span
    heads = width // size
    model = weight.shape[0]
    step = min(256, seq)
    chunk = min(128, seq)
    score = size**-0.5

    def body(*refs):
        in_refs, w_ref = refs[:chips], refs[chips]
        head_refs = refs[chips + 1 : 2 * chips + 1]
        lse_ref = refs[2 * chips + 1]
        part_refs = refs[2 * chips + 2 : 4 * chips + 2]
        k_ref, qt_ref, vt_ref, ot_ref, s_ref, p_ref = refs[4 * chips + 2 :]
        for c in range(chips):
            at = slice(c * span, (c + 1) * span)
            k_ref[at, :] = in_refs[c][:, width : 2 * width]
            qt_ref[:, at] = (turn(in_refs[c][:, :width]) * score).astype(BF)
            vt_ref[:, at] = turn(in_refs[c][:, 2 * width :]).astype(BF)

        def one(i, carry):
            at = pl.ds(pl.multiple_of(i * step, step), step)
            q = qt_ref[:, at]
            s_ref[0] = dot(k_ref[...], head_rows(q, 0, size))
            for h in range(heads):
                if h + 1 < heads:
                    s_ref[(h + 1) % 2] = dot(k_ref[...], head_rows(q, h + 1, size))
                now = h % 2
                top = fold(s_ref[now, :chunk, :], jnp.max)
                for r in range(chunk, seq, chunk):
                    top = jnp.maximum(top, fold(s_ref[now, r : r + chunk, :], jnp.max))
                top = jnp.max(top, axis=0, keepdims=True)
                norm = jnp.zeros((8, step), F32)
                for r in range(0, seq, chunk):
                    p = jnp.exp(s_ref[now, r : r + chunk, :] - top)
                    norm = norm + fold(p, jnp.sum)
                    p_ref[now, r : r + chunk, :] = p.astype(BF)
                norm = jnp.sum(norm, axis=0, keepdims=True)
                rows = slice(h * size, (h + 1) * size)
                ot_ref[rows, at] = dot(vt_ref[rows, :], p_ref[now]) / norm
                lse_ref[h : h + 1, at] = top + jnp.log(norm)
            return carry

        lax.fori_loop(0, seq // step, one, 0)
        for c in range(chips):
            at = slice(c * span, (c + 1) * span)
            o = ot_ref[:, at].T.astype(BF)
            head_refs[c][...] = o
            part_refs[2 * c][...] = dot_bt(o[:half], w_ref[...]).astype(BF)
            part_refs[2 * c + 1][...] = dot_bt(o[half:], w_ref[...]).astype(BF)

    whole = lambda i: (0, 0)
    full = lambda shape: pl.BlockSpec(shape, whole)
    out = pl.pallas_call(
        body,
        grid=(1,),
        in_specs=[full((span, 3 * width))] * chips + [pl.BlockSpec((model, width), lambda i: (0, 3))],
        out_specs=[full((span, width))] * chips
        + [full((heads, seq))]
        + [full((half, model))] * (2 * chips),
        out_shape=[sds((span, width), BF)] * chips
        + [sds((heads, seq), F32)]
        + [sds((half, model), BF)] * (2 * chips),
        scratch_shapes=[
            pltpu.VMEM((seq, width), BF),
            pltpu.VMEM((width, seq), BF),
            pltpu.VMEM((width, seq), BF),
            pltpu.VMEM((width, seq), F32),
            pltpu.VMEM((2, seq, step), F32),
            pltpu.VMEM((2, seq, step), BF),
        ],
        compiler_params=params(20, 1),
        cost_estimate=cost(
            16 * seq * seq * width, 2 * seq * (4 * width + model), heads * seq * seq
        ),
        name="attention",
    )(*packed, weight)
    parts = out[chips + 1 :]
    return out[:chips], out[chips], [(parts[2 * c], parts[2 * c + 1]) for c in range(chips)]


def attention_back(packed, heads_kept, lse, datt, weight, size):
    chips = len(packed)
    span = packed[0].shape[0]
    half = span // 2
    width = packed[0].shape[1] // 3
    seq = chips * span
    heads = width // size
    model = weight.shape[0]
    step = min(256, seq)
    chunk = min(128, seq)
    score = size**-0.5

    def body(*refs):
        at = 0

        def take(count):
            nonlocal at
            at += count
            return refs[at - count : at]

        in_refs, kept_refs = take(chips), take(chips)
        (lse_ref,) = take(1)
        datt_refs = take(2 * chips)
        (w_ref,) = take(1)
        dqkv_refs = take(chips)
        part_refs = take(2 * chips)
        (sum_ref,) = take(1)
        k_ref, v_ref, kt_ref, qt_ref, q_ref, do_ref, dot_ref = take(7)
        inner_ref, s_ref, g_ref, p_ref, ds_ref, dk_ref, dv_ref, dqt_ref = take(8)
        for c in range(chips):
            rows = slice(c * span, (c + 1) * span)
            q = in_refs[c][:, :width].astype(F32) * score
            k = in_refs[c][:, width : 2 * width]
            q_ref[rows, :] = q.astype(BF)
            qt_ref[:, rows] = q.T.astype(BF)
            k_ref[rows, :] = k
            kt_ref[:, rows] = turn(k).astype(BF)
            v_ref[rows, :] = in_refs[c][:, 2 * width :]
            for b in range(2):
                d = dot(datt_refs[2 * c + b][...], w_ref[:, 3 * width :]).astype(BF)
                here = slice(c * span + b * half, c * span + (b + 1) * half)
                do_ref[here, :] = d
                dt = turn(d)
                dot_ref[:, here] = dt.astype(BF)
                prod = dt * turn(kept_refs[c][b * half : (b + 1) * half, :])
                for h in range(heads):
                    inner_ref[h : h + 1, here] = jnp.sum(
                        prod[h * size : (h + 1) * size, :], axis=0, keepdims=True
                    )

        def one(i, carry):
            at = pl.ds(pl.multiple_of(i * step, step), step)
            qt = qt_ref[:, at]
            dot_t = dot_ref[:, at]
            q = q_ref[at, :]
            do = do_ref[at, :]

            def scores(h):
                s_ref[h % 2] = dot(k_ref[...], head_rows(qt, h, size))
                g_ref[h % 2] = dot(v_ref[...], head_rows(dot_t, h, size))

            scores(0)
            for h in range(heads):
                if h + 1 < heads:
                    scores(h + 1)
                now = h % 2
                cols = slice(h * step, (h + 1) * step)
                lse = lse_ref[h : h + 1, at]
                inner = inner_ref[h : h + 1, at]
                for r in range(0, seq, chunk):
                    p = jnp.exp(s_ref[now, r : r + chunk, :] - lse)
                    ds = p * (g_ref[now, r : r + chunk, :] - inner)
                    p_ref[r : r + chunk, cols] = p.astype(BF)
                    ds_ref[r : r + chunk, cols] = ds.astype(BF)
                rows = slice(h * size, (h + 1) * size)
                dqt_ref[rows, at] = dot(kt_ref[rows, :], ds_ref[:, cols]) * score
            dv = dot(p_ref[...], jnp.concatenate([head_cols(do, h, size) for h in range(heads)], 0))
            dk = dot(ds_ref[...], jnp.concatenate([head_cols(q, h, size) for h in range(heads)], 0))

            @pl.when(i == 0)
            def _():
                dv_ref[...] = dv
                dk_ref[...] = dk

            @pl.when(i > 0)
            def _():
                dv_ref[...] += dv
                dk_ref[...] += dk

            return carry

        lax.fori_loop(0, seq // step, one, 0)
        for c in range(chips):
            rows = slice(c * span, (c + 1) * span)
            out = dqkv_refs[c]
            out[:, :width] = dqt_ref[:, rows].T.astype(BF)
            out[:, width : 2 * width] = dk_ref[rows, :].astype(BF)
            out[:, 2 * width :] = dv_ref[rows, :].astype(BF)
            sums = jnp.sum(out[...].astype(F32), axis=0, keepdims=True)
            if c == 0:
                sum_ref[...] = sums
            else:
                sum_ref[...] += sums
            for b in range(2):
                part_refs[2 * c + b][...] = dot_bt(
                    out[b * half : (b + 1) * half, :], w_ref[:, : 3 * width]
                ).astype(BF)

    flat = [g for pair in datt for g in pair]
    whole = lambda i: (0, 0)
    full = lambda a: pl.BlockSpec(a.shape, whole)
    out_shape = (
        [sds((span, 3 * width), BF)] * chips
        + [sds((half, model), BF)] * (2 * chips)
        + [sds((1, 3 * width), F32)]
    )
    operands = (*packed, *heads_kept, lse, *flat, weight)
    out = pl.pallas_call(
        body,
        grid=(1,),
        in_specs=[full(a) for a in operands],
        out_specs=[full(a) for a in out_shape],
        out_shape=out_shape,
        scratch_shapes=[
            pltpu.VMEM((seq, width), BF),
            pltpu.VMEM((seq, width), BF),
            pltpu.VMEM((width, seq), BF),
            pltpu.VMEM((width, seq), BF),
            pltpu.VMEM((seq, width), BF),
            pltpu.VMEM((seq, width), BF),
            pltpu.VMEM((width, seq), BF),
            pltpu.VMEM((heads, seq), F32),
            pltpu.VMEM((2, seq, step), F32),
            pltpu.VMEM((2, seq, step), F32),
            pltpu.VMEM((seq, heads * step), BF),
            pltpu.VMEM((seq, heads * step), BF),
            pltpu.VMEM((seq, width), F32),
            pltpu.VMEM((seq, width), F32),
            pltpu.VMEM((width, seq), F32),
        ],
        compiler_params=params(36, 1),
        cost_estimate=cost(
            40 * seq * seq * width, 2 * seq * (8 * width + 2 * model), heads * seq * seq
        ),
        name="attention_back",
    )(*operands)
    parts = out[chips : 3 * chips]
    return (
        out[:chips],
        [(parts[2 * c], parts[2 * c + 1]) for c in range(chips)],
        out[3 * chips],
    )


def gelu_both(x):
    away = jnp.abs(x)
    t = 1.0 / (1.0 + (0.3275911 * 0.5**0.5) * away)
    bell = jnp.exp(-0.5 * (x * x))
    poly = t * (
        0.127414796
        + t * (-0.142248368 + t * (0.7107068705 + t * (-0.7265760135 + t * 0.5307027145)))
    )
    tail = poly * bell
    phi = jnp.where(x >= 0, 1.0 - tail, tail)
    return x * phi, phi + x * (bell * 0.3989422804014327)


def mlp_call(body, pairs, extra, weight, bias, outs, parts, scratch, name):
    rows, model = pairs[0].shape
    units = weight.shape[1] // 2
    step = min(256, units)
    blocks = units // step
    whole = lambda j: (0, 0)
    cols = lambda j: (0, j)
    in_specs = [pl.BlockSpec((rows, model), whole) for _ in pairs]
    in_specs += [pl.BlockSpec((2 * rows, step), cols) for _ in extra]
    in_specs += [
        pl.BlockSpec((model, step), cols),
        pl.BlockSpec((model, step), lambda j: (0, blocks + j)),
        pl.BlockSpec((1, step), cols),
    ]
    out_specs = [pl.BlockSpec((2 * rows, step), cols) for _ in outs]
    out_specs += [pl.BlockSpec((1, step), cols)]
    out_specs += [pl.BlockSpec((rows, model), whole)] * (2 * parts)
    out_shape = [sds((2 * rows, units), d) for d in outs] + [sds((1, units), F32)]
    out_shape += [sds((rows, model), BF)] * (2 * parts)
    count = len(pairs) // 2
    return pl.pallas_call(
        body,
        grid=(blocks,),
        in_specs=in_specs,
        out_specs=out_specs,
        out_shape=out_shape,
        scratch_shapes=[pltpu.VMEM((2 * rows, model), F32)] * parts
        + [pltpu.VMEM((2 * rows, step), F32)] * scratch,
        compiler_params=params(20 + 8 * (parts - 1), 1),
        cost_estimate=cost(
            8 * count * rows * model * units,
            4 * model * units + 4 * rows * (model + units) * (count + 1),
        ),
        name=name,
    )(*pairs, *extra, weight, weight, bias)


def clear(*refs):
    @pl.when(pl.program_id(0) == 0)
    def _():
        for ref in refs:
            ref[...] = jnp.zeros_like(ref)


def finish(acc, low, high):
    rows = low.shape[0]

    @pl.when(pl.program_id(0) == pl.num_programs(0) - 1)
    def _():
        low[...] = acc[:rows, :].astype(BF)
        high[...] = acc[rows:, :].astype(BF)


CHUNK = 32


def mlp_forward(pair, weight, bias):
    rows = pair[0].shape[0]

    def body(a, b, w1_ref, w2_ref, bias_ref, act_ref, slope_ref, sum_ref, lo, hi, acc, pre):
        clear(acc, sum_ref)
        shift = bias_ref[...]
        for i, x in enumerate((a, b)):
            pre[i * rows : (i + 1) * rows, :] = dot(x[...], w1_ref[...])
        for i in range(2):
            at = slice(i * rows, (i + 1) * rows)
            for r in range(i * rows, (i + 1) * rows, CHUNK):
                act, slope = gelu_both(pre[r : r + CHUNK, :] + shift)
                act_ref[r : r + CHUNK, :] = act.astype(BF)
                slope_ref[r : r + CHUNK, :] = slope.astype(BF)
            acc[at, :] += dot_bt(act_ref[at, :], w2_ref[...])
        finish(acc, lo, hi)

    act, slope, _, lo, hi = mlp_call(body, pair, [], weight, bias, [BF, BF], 1, 1, "mlp_forward")
    return act, slope, (lo, hi)


def mlp_backward(pair, slope, weight, bias):
    rows = pair[0].shape[0]

    def body(a, b, slope_ref, w1_ref, w2_ref, bias_ref, dpre_ref, sum_ref, lo, hi, acc, pre):
        clear(acc)
        for i, g in enumerate((a, b)):
            pre[i * rows : (i + 1) * rows, :] = dot(g[...], w2_ref[...])
        sums = jnp.zeros((8, bias_ref.shape[1]), F32)
        for i in range(2):
            at = slice(i * rows, (i + 1) * rows)
            for r in range(i * rows, (i + 1) * rows, CHUNK):
                d = pre[r : r + CHUNK, :] * slope_ref[r : r + CHUNK, :].astype(F32)
                d = d.astype(BF)
                dpre_ref[r : r + CHUNK, :] = d
                sums = sums + fold(d.astype(F32), jnp.sum)
            acc[at, :] += dot_bt(dpre_ref[at, :], w1_ref[...])
        sum_ref[...] = jnp.sum(sums, axis=0, keepdims=True)
        finish(acc, lo, hi)

    dpre, sums, lo, hi = mlp_call(
        body, pair, [slope], weight, bias, [BF], 1, 1, "mlp_backward"
    )
    return dpre, sums, (lo, hi)


def mlp_both(pair, grads, weight, bias):
    rows = pair[0].shape[0]

    def body(
        a, b, c, d, w1_ref, w2_ref, bias_ref, act_ref, dpre_ref, sum_ref,
        lo, hi, blo, bhi, acc, back, pre, grad,
    ):
        clear(acc, back)
        shift = bias_ref[...]
        for i, (x, g) in enumerate(((a, c), (b, d))):
            at = slice(i * rows, (i + 1) * rows)
            pre[at, :] = dot(x[...], w1_ref[...])
            grad[at, :] = dot(g[...], w2_ref[...])
        sums = jnp.zeros((8, bias_ref.shape[1]), F32)
        for i in range(2):
            at = slice(i * rows, (i + 1) * rows)
            for r in range(i * rows, (i + 1) * rows, CHUNK):
                act, slope = gelu_both(pre[r : r + CHUNK, :] + shift)
                act_ref[r : r + CHUNK, :] = act.astype(BF)
                dpre = (grad[r : r + CHUNK, :] * slope).astype(BF)
                dpre_ref[r : r + CHUNK, :] = dpre
                sums = sums + fold(dpre.astype(F32), jnp.sum)
            back[at, :] += dot_bt(dpre_ref[at, :], w1_ref[...])
            acc[at, :] += dot_bt(act_ref[at, :], w2_ref[...])
        sum_ref[...] = jnp.sum(sums, axis=0, keepdims=True)
        finish(acc, lo, hi)
        finish(back, blo, bhi)

    act, dpre, sums, lo, hi, blo, bhi = mlp_call(
        body, [*pair, *grads], [], weight, bias, [BF, BF], 2, 2, "mlp_both"
    )
    return act, dpre, sums, (lo, hi), (blo, bhi)


def weight_grads(products, dp, side, name):
    model = products[0][0][0].shape[1]
    step = model // dp
    half = step // 2
    sizes = [(len(left), len(right), right[0].shape[1]) for left, right in products]
    cols = sum(n for _, _, n in sizes)
    tokens = sum(a.shape[0] for a in products[0][0])

    def body(side_ref, *refs):
        mine, other, acc_ref = refs[-3:]
        at = base = 0
        for many, few, n in sizes:
            lefts, rights = refs[at : at + many], refs[at + many : at + many + few]
            at += many + few
            ratio = many // few
            acc = None
            for i in range(many):
                size = lefts[i].shape[0]
                here = slice((i % ratio) * size, (i % ratio + 1) * size)
                term = dot_at(lefts[i][...], rights[i // ratio][here, :])
                acc = term if acc is None else acc + term
            acc_ref[:, base : base + n] = acc
            base += n
        low = pl.multiple_of(side_ref[0] * half, half)
        high = pl.multiple_of((1 - side_ref[0]) * half, half)
        mine[...] = acc_ref[pl.ds(low, half), :].astype(BF)
        other[...] = acc_ref[pl.ds(high, half), :].astype(BF)

    specs, operands = [pl.BlockSpec(memory_space=pltpu.SMEM)], [side.reshape(1)]
    for left, right in products:
        specs += [pl.BlockSpec((a.shape[0], step), lambda i: (0, i)) for a in left]
        specs += [pl.BlockSpec(b.shape, lambda i: (0, 0)) for b in right]
        operands += [*left, *right]
    return pl.pallas_call(
        body,
        grid=(dp,),
        in_specs=specs,
        out_specs=[pl.BlockSpec((half, cols), lambda i: (i, 0))] * 2,
        out_shape=[sds((model // 2, cols), BF)] * 2,
        scratch_shapes=[pltpu.VMEM((step, cols), F32)],
        compiler_params=params(24, 1),
        cost_estimate=cost(
            2 * tokens * model * cols, 2 * (tokens * (2 * model + cols) + model * cols)
        ),
        name=name,
    )(*operands)


def pieces(chunks):
    return [p for pair in chunks for p in pair]


def shards(
    tokens, cotangent, ln1_gain, ln1_bias, w_qkv, qv_bias, w_out, out_bias, scale_attn,
    ln2_gain, ln2_bias, w_fc1, fc1_bias, w_fc2, fc2_bias, scale_mlp,
):
    side = lax.axis_index("section")
    first = side == 0
    dp = lax.axis_size("dp")
    here = lax.axis_index("dp")
    chips = lax.axis_size("tensor") // 2
    rows, model = tokens.shape[2:]
    heads = qv_bias.shape[1]
    size = qv_bias.shape[2] * dp // 2
    width = heads * size
    units = w_fc1.shape[2]
    part = model // dp

    x0 = lax.dynamic_index_in_dim(tokens, side, 0, keepdims=False).reshape(rows, model)
    grad_top = lax.dynamic_index_in_dim(cotangent, side, 0, keepdims=False).reshape(rows, model)

    vectors = (ln1_gain, ln1_bias, out_bias, scale_attn, ln2_gain, ln2_bias, fc2_bias, scale_mlp)
    packed = jnp.concatenate(
        [v.reshape(-1) for v in vectors] + [fc1_bias.reshape(-1), qv_bias.reshape(-1)]
    )
    own_qkv = w_qkv.reshape(part, heads, 3, size).swapaxes(1, 2).reshape(part, 3 * width)
    own_att = jnp.concatenate([own_qkv, w_out[0].T], axis=1)
    own_ff = jnp.concatenate([w_fc1[0], w_fc2[0].T], axis=1)

    def halves(own, came, rest):
        mine, left = half_of(own, side), half_of(own, 1 - side)
        return (
            (jnp.where(first, mine, came), jnp.where(first, left, rest)),
            (jnp.where(first, came, mine), jnp.where(first, rest, left)),
        )

    came_att = swap_section(half_of(own_att, 1 - side))
    small = gather_small(packed, first).astype(F32)
    cut = 8 * part
    vecs = small[:, :, :cut].reshape(2, dp, 8, part).swapaxes(1, 2).reshape(2, 8, model)
    bias_fc1 = small[:, :, cut : cut + units // dp].reshape(2, 1, units)
    qv = small[:, :, cut + units // dp :].reshape(2, dp, heads, -1).swapaxes(1, 2)
    qv = qv.reshape(2, heads, 2, size)
    bias_qkv = jnp.stack([qv[:, :, 0], jnp.zeros_like(qv[:, :, 0]), qv[:, :, 1]], axis=1)
    bias_qkv = bias_qkv.reshape(2, 1, 3 * width)
    vecs = (vecs[0], vecs[1])

    norm1 = norm_first(tie(x0, came_att), vecs[0])
    came_ff = swap_section(tie(half_of(own_ff, 1 - side), came_att))
    rest_att = swap_section(tie(half_of(own_att, side), came_att))
    half_att0, half_att1 = halves(own_att, came_att, rest_att)
    ring_ff0 = jnp.where(first, half_of(own_ff, side), came_ff)

    def put_together(half, hops, backs):
        return assemble([half[0], *hops], [half[1], *backs], part * dp)

    hops_att0 = direct(half_att0[0])
    att0 = put_together(half_att0, hops_att0, [swap_section(tie(v, norm1)) for v in hops_att0])
    hops_ff0 = ring(tie(ring_ff0, hops_att0[-1]))
    rest_ff = swap_section(tie(half_of(own_ff, side), hops_ff0[0]))
    half_ff0, half_ff1 = halves(own_ff, came_ff, rest_ff)
    hops_att1 = ring(tie(half_att1[0], hops_ff0[-1]))
    hops_ff1 = ring(tie(half_ff1[0], hops_att1[-1]))
    backs_ff0, backs_att1, backs_ff1 = (
        [swap_section(v) for v in hops] for hops in (hops_ff0, hops_att1, hops_ff1)
    )

    def front(x, norm, weight, s, gather_beside, before, under, scatter_beside):
        chunks, qkv = gather_tokens(
            norm, lambda pair: project_qkv(pair, weight, bias_qkv[s]), gather_beside
        )
        kept, lse, parts = attention([*qkv[:-1], tie(qkv[-1], *before)], weight, size)
        parts = [parts[0], *[(same, tie(other, *under)) for same, other in parts[1:]]]
        terms, _ = scatter_tokens(parts, beside=scatter_beside)
        attended, residual, norm2 = after_attention(x, terms, vecs[s])
        return (chunks, qkv, kept, lse, attended, residual), norm2

    ff0, att1, ff1 = thirds(hops_ff0), thirds(hops_att1), thirds(hops_ff1)
    back_ff0, back_att1, back_ff1 = thirds(backs_ff0), thirds(backs_att1), thirds(backs_ff1)
    saved0, norm2 = front(
        x0, norm1, att0, 0, (), ff0[0], (*ff0[1], *back_ff0[0]),
        (*ff0[2], *back_ff0[1], *att1[0]),
    )
    w_ff0 = put_together(half_ff0, hops_ff0, backs_ff0)
    second0, mlp0 = gather_tokens(
        norm2, lambda pair: mlp_forward(pair, w_ff0, bias_fc1[0]), att1[1]
    )
    terms, _ = scatter_tokens(
        [m[2] for m in mlp0], beside=(*att1[2], *back_att1[0], *back_att1[1], *ff1[0])
    )
    mlp_out0, y0, norm1 = after_mlp(saved0[5], terms, vecs[0], vecs[1])

    w_att1 = put_together(half_att1, hops_att1, backs_att1)
    low1, sums_fc2_1 = start_back(grad_top, vecs[1])
    grads1, _ = gather_tokens(tie(low1, norm1), lambda pair: pair[0])
    saved1, norm2 = front(
        y0, norm1, w_att1, 1, ff1[1], (), pieces(grads1), (*ff1[2], *back_ff1[0], *back_ff1[1])
    )
    w_ff1 = put_together(half_ff1, hops_ff1, backs_ff1)
    spare = list(grads1)
    second1, mlp1 = gather_tokens(
        norm2, lambda pair: mlp_both(pair, spare.pop(0), w_ff1, bias_fc1[1])
    )

    def grad_ff(second, mlp, grads, acts):
        def work(after):
            return weight_grads(
                [(pieces(second), [tie(mlp[0], after), *mlp[1:]]), (pieces(grads), acts)],
                dp,
                side,
                "grad_ff",
            )

        return work

    def grad_att(saved):
        def work(after, datt, dqkv):
            return weight_grads(
                [(pieces(saved[0]), [tie(dqkv[0], after), *dqkv[1:]]), (pieces(datt), saved[2])],
                dp,
                side,
                "grad_att",
            )

        return work

    acts1 = [m[0] for m in mlp1]
    parts_y1 = [m[3] for m in mlp1]
    sums_y1 = core_sums(parts_y1)
    local_y1 = [parts_y1[0][0], core_swap(parts_y1[0][1])]
    chain = {}

    def ff1_ready(after):
        g = grad_ff(second1, [m[1] for m in mlp1], grads1, acts1)(after)
        chain["ff1"] = ring_sum(*g, (0, 1))
        return g

    parts_back1 = [m[4] for m in mlp1]
    terms, g_ff1 = scatter_tokens(parts_back1, ff1_ready)
    step_ff1, own_ff1 = chain["ff1"]
    step_ff1 = [step_ff1[0], *thirds(step_ff1[1:-1]), step_ff1[-1]]
    flat = lambda steps: [v for step in steps for v in step]
    dres1, low1b, sums1 = back_second(grad_top, saved1[5], saved1[4], terms, vecs[1])
    datt1, _ = gather_tokens(low1b, lambda pair: pair[0], step_ff1[0])
    terms_y1 = send_sums([tie(v, datt1[-1][0]) for v in sums_y1])
    dqkv1, parts, qkv_sums1 = attention_back(
        saved1[1], saved1[2], saved1[3], datt1, w_att1, size
    )
    parts = [
        parts[0],
        *[(same, tie(other, *terms_y1, *flat(step_ff1[1]))) for same, other in parts[1:]],
    ]
    terms, g_att1 = scatter_tokens(
        parts, lambda after: grad_att(saved1)(after, datt1, dqkv1), flat(step_ff1[2])
    )
    dx1, low0, edge1 = back_first(dres1, y0, terms, vecs[1], mlp_out0, vecs[0])
    y1, sums_sc_1 = last_output(saved1[5], local_y1 + terms_y1, grad_top, vecs[1])
    step_att1, own_att1 = ring_sum(*tie_all(g_att1, low0), (0, 1))
    step_att1 = [step_att1[0], *thirds(step_att1[1:-1]), step_att1[-1]]

    slopes = [m[1] for m in mlp0]
    grads0, mlp_back0 = gather_tokens(
        low0,
        lambda pair: mlp_backward(pair, slopes.pop(0), w_ff0, bias_fc1[0]),
        (*flat(step_ff1[3]), *step_att1[0]),
    )
    terms, g_ff0 = scatter_tokens(
        [m[2] for m in mlp_back0],
        grad_ff(second0, [m[0] for m in mlp_back0], grads0, [m[0] for m in mlp0]),
        (*step_ff1[4], *flat(step_att1[1])),
    )
    dres0, low, sums0 = back_second(dx1, saved0[5], saved0[4], terms, vecs[0])
    step_ff0, own_ff0 = ring_sum(*tie_all(g_ff0, low), (1, 0))
    step_ff0 = [step_ff0[0], *thirds(step_ff0[1:-1]), step_ff0[-1]]
    datt0, _ = gather_tokens(
        low, lambda pair: pair[0], (*flat(step_att1[2]), *step_ff0[0])
    )
    dqkv0, parts, qkv_sums0 = attention_back(saved0[1], saved0[2], saved0[3], datt0, att0, size)
    parts = [
        parts[0],
        *[
            (same, tie(other, *flat(step_att1[3]), *flat(step_ff0[1])))
            for same, other in parts[1:]
        ],
    ]
    terms, g_att0 = scatter_tokens(
        parts,
        lambda after: grad_att(saved0)(after, datt0, dqkv0),
        (*step_att1[4], *flat(step_ff0[2])),
    )
    dx0, edge0 = back_first(dres0, x0, terms, vecs[0])
    step_att0, own_att0 = ring_sum(*g_att0, (1, 0))
    rs_ff1, rs_att1 = (own_ff1, step_ff1[-1][0]), (own_att1, step_att1[-1][0])
    rs_ff0, rs_att0 = (own_ff0, step_ff0[-1][0]), (own_att0, step_att0[-1][0])

    def both(low, high):
        mine = jnp.where(first, low, high)
        came_low = lax.ppermute(low, "section", [(1, 0)])
        came_high = lax.ppermute(high, "section", [(0, 1)])
        came = jnp.where(first, came_low, came_high)
        return jnp.stack([jnp.where(first, mine, came), jnp.where(first, came, mine)])[None, :, None]

    block_out = both(y0, y1)
    input_grads = both(dx0, dx1)

    def to_owner(low, high, pick):
        own = jnp.where(first, low, high) + swap_section(jnp.where(first, high, low))
        out = pick(own, here)
        for step in range(1, dp):
            pairs = [(i, (i + step) % dp) for i in range(dp)]
            out = out + lax.ppermute(pick(own, lax.rem(here + step, dp)), "dp", pairs)
        return out

    def by_unit(qkv_sums, unit_sums):
        q = qkv_sums[:, :width].reshape(heads, 1, size)
        v = qkv_sums[:, 2 * width :].reshape(heads, 1, size)
        bias = jnp.concatenate([q, v], 1).reshape(heads, dp, -1).swapaxes(0, 1).reshape(dp, -1)
        return jnp.concatenate([bias, unit_sums.reshape(dp, -1)], axis=1)

    unit = to_owner(
        by_unit(qkv_sums0, sum(m[1] for m in mlp_back0)),
        by_unit(qkv_sums1, sum(m[2] for m in mlp1)),
        lambda v, place: lax.dynamic_slice_in_dim(v, place, 1, 0),
    )
    cut = heads * (2 * size // dp)
    bias_grad = unit[:, :cut].reshape(1, heads, -1)
    fc1_grad = unit[:, cut:].reshape(1, 1, -1)

    vec = jnp.concatenate(
        [edge0[:2], sums0[:4], edge1[2:4], edge1[:2], sums1[:4], sums_sc_1[:1], sums_fc2_1[:1]]
    )
    vec = vec + core_swap(vec)
    vec = sum([from_chip(vec, step) for step in range(1, chips)], vec)
    vec = to_owner(
        vec[:8], vec[8:], lambda v, place: lax.dynamic_slice_in_dim(v, place * part, part, 1)
    )
    g_ln1, b_ln1, g_ln2, b_ln2, g_sc_attn, g_out_bias, g_sc_mlp, g_fc2_bias = (
        vec[i : i + 1] for i in range(8)
    )

    def owned(low, high):
        top = jnp.where(first, low[0], high[1].astype(F32))
        bottom = jnp.where(first, low[1].astype(F32), high[0])
        return jnp.concatenate([top, bottom], 0)

    g_att, g_ff = owned(rs_att0, rs_att1), owned(rs_ff0, rs_ff1)
    g_qkv = g_att[:, : 3 * width].reshape(part, 3, heads, size).swapaxes(1, 2)
    g_qkv = g_qkv.reshape(1, part, 3 * width)
    g_out = g_att[:, 3 * width :].T[None]
    g_fc1 = g_ff[:, :units][None]
    g_fc2 = g_ff[:, units:].T[None]
    return (
        block_out, input_grads, g_ln1, b_ln1, g_qkv, bias_grad, g_out, g_out_bias, g_sc_attn,
        g_ln2, b_ln2, g_fc1, fc1_grad, g_fc2, g_fc2_bias, g_sc_mlp,
    )


def solution(mesh):
    vec = P("section", "dp")
    by_row = P("section", "dp", "tensor")
    by_unit = P("section", "tensor", "dp")
    data = P(None, "dp", "tensor", None)
    split = P("section", None, "dp", "tensor", None)
    given = (
        vec, vec, by_row, by_unit, by_unit, vec, vec, vec, vec, by_row, by_unit, by_unit, vec, vec,
    )
    return jax.shard_map(
        shards,
        mesh=mesh,
        in_specs=(data, data) + given,
        out_specs=(split, split) + given,
        check_vma=False,
    )
```

```python
from functools import partial

import jax
import jax.numpy as jnp
from jax import lax
from jax.experimental import pallas as pl
from jax.experimental.pallas import tpu as pltpu
from jax.sharding import PartitionSpec as P

EPSILON = 1e-06
BF = jnp.bfloat16
F32 = jnp.float32
MIB = 1 << 20

LN1_G, LN1_B, OUT_B, SC_ATTN, LN2_G, LN2_B, FC2_B, SC_MLP = range(8)


def dot(a, b):
    return lax.dot_general(a, b, (((1,), (0,)), ((), ())), preferred_element_type=F32)


def dot_bt(a, b):
    return lax.dot_general(a, b, (((1,), (1,)), ((), ())), preferred_element_type=F32)


def dot_at(a, b):
    return lax.dot_general(a, b, (((0,), (0,)), ((), ())), preferred_element_type=F32)


def turn(v):
    return v.astype(F32).T


def params(limit, grid=0):
    return pltpu.CompilerParams(
        vmem_limit_bytes=limit * MIB,
        dimension_semantics=("arbitrary",) * grid if grid else None,
    )


def whole(shape):
    return pl.BlockSpec(shape, lambda i: (0, 0), pipeline_mode=pl.Buffered(1))


def cost(micros):
    return pl.CostEstimate(flops=int(micros * 1.15e9), bytes_accessed=0, transcendentals=0)


def sds(shape, dtype):
    return jax.ShapeDtypeStruct(shape, dtype)


def core_swap(v):
    count = lax.axis_size("tensor")
    return lax.ppermute(v, "tensor", [(i, i ^ 1) for i in range(count)])


def from_chip(v, step):
    count = lax.axis_size("tensor")
    chips = count // 2
    pairs = [(((i // 2 + step) % chips) * 2 + i % 2, i) for i in range(count)]
    return lax.ppermute(v, "tensor", pairs)


def tie(v, *after):
    return lax.optimization_barrier((v, *after))[0]


def tie_all(vs, *after):
    return lax.optimization_barrier((*vs, *after))[: len(vs)]


def gather_tokens(own, work, beside=()):
    chips = lax.axis_size("tensor") // 2
    came = [from_chip(own, step) for step in range(1, chips)]
    chunks = [(own, core_swap(own))]
    results = [work(chunks[0])]
    for same in came:
        same = tie(same, results[-1], *beside)
        chunks.append((same, core_swap(same)))
        results.append(work(chunks[-1]))
    return chunks, results


def core_sums(parts):
    return [
        (same.astype(F32) + core_swap(other).astype(F32)).astype(BF) for same, other in parts[1:]
    ]


def send_sums(sums):
    chips = len(sums) + 1
    return [from_chip(both, chips - step) for step, both in enumerate(sums, 1)]


def scatter_tokens(parts, work=None, beside=()):
    sums = core_sums(parts)
    terms = send_sums(sums)
    local = core_swap(tie(parts[0][1], sums[-1]))
    made = work(sums[-1]) if work else local
    terms = [tie(t, made, local, *beside) for t in terms]
    return [parts[0][0], *terms, local], made


def swap_section(v):
    return lax.ppermute(v, "section", [(0, 1), (1, 0)])


def assemble(shards, rows):
    count = len(shards)
    cut = len(shards[0])
    size, cols = shards[0][0].shape
    place = jnp.stack([lax.axis_index("dp"), lax.axis_index("section")])

    def body(place_ref, *refs):
        out_ref, sems = refs[count * cut :]
        z, x = place_ref[0], place_ref[1]
        started = []
        for k in range(count):
            base = lax.rem(z + (count - k), count) * (cut * size)
            for i, at in enumerate([base] if cut == 1 else [base + x * size, base + (1 - x) * size]):
                copy = pltpu.make_async_copy(
                    refs[k * cut + i],
                    out_ref.at[pl.ds(pl.multiple_of(at, size), size), :],
                    sems.at[k * cut + i],
                )
                copy.start()
                started.append(copy)
        for copy in started:
            copy.wait()

    hbm = pl.BlockSpec(memory_space=pl.ANY)
    return pl.pallas_call(
        body,
        in_specs=[pl.BlockSpec(memory_space=pltpu.SMEM)] + [hbm] * (count * cut),
        out_specs=pl.BlockSpec(memory_space=pltpu.VMEM),
        out_shape=sds((rows, cols), shards[0][0].dtype),
        scratch_shapes=[pltpu.SemaphoreType.DMA((count * cut,))],
        compiler_params=params(6),
        cost_estimate=cost(2),
        name="assemble",
    )(place, *[v for shard in shards for v in shard])


def half_of(v, which):
    half = v.shape[0] // 2
    return lax.dynamic_slice_in_dim(v, which * half, half, 0)


def ring(own):
    count = lax.axis_size("dp")
    pairs = [(i, (i + 1) % count) for i in range(count)]
    hops = []
    for _ in range(count - 1):
        own = lax.ppermute(own, "dp", pairs)
        hops.append(own)
    return hops


def direct(own):
    count = lax.axis_size("dp")
    return [
        lax.ppermute(own, "dp", [(i, (i + step) % count) for i in range(count)])
        for step in range(1, count)
    ]


def thirds(values):
    count = len(values)
    cuts = [-(-count * i // 3) for i in range(4)]
    return [values[a:b] for a, b in zip(cuts, cuts[1:])]


def gather_small(v, first, after):
    count = lax.axis_size("dp")
    came = swap_section(v)
    own = tie(jnp.stack([jnp.where(first, v, came), jnp.where(first, came, v)]), after)
    ahead = [own]
    for step in range(1, count):
        ahead.append(lax.ppermute(own, "dp", [(i, (i - step) % count) for i in range(count)]))
    twice = jnp.stack(ahead + ahead, axis=1)
    return lax.dynamic_slice_in_dim(twice, count - lax.axis_index("dp"), count, 1)


def dp_rows(v, back):
    dp = lax.axis_size("dp")
    part = v.shape[0] // dp
    place = lax.rem(lax.axis_index("dp") + (dp - back), dp)
    return lax.dynamic_slice_in_dim(v, place * part, part, 0)


def ring_sum(mine, other, pair, late=()):
    dp = lax.axis_size("dp")
    pairs = [(i, (i + 1) % dp) for i in range(dp)]
    steps, going = [], None
    for back in range(1, dp + 1):
        step = [] if going is None else [lax.ppermute(going, "dp", pairs)]
        if other is not None:
            cut = dp_rows(other, back)
            step.append(swap_section(tie(cut, *late) if late and back > 2 else cut))
        going = sum(t.astype(F32) for t in [dp_rows(mine, back), *step])
        if back < dp:
            going = going.astype(BF)
            if late and back == 2:
                going = tie(going, *late)
        if step:
            steps.append(step)
    steps.append([lax.ppermute(going.astype(BF), "section", [pair])])
    return steps, going


def standardize(v):
    centred = v - jnp.mean(v, axis=-1, keepdims=True)
    var = jnp.mean(centred * centred, axis=-1, keepdims=True)
    scale = lax.rsqrt(var + EPSILON)
    return centred * scale, scale


def norm_of(v, vec, gain, shift):
    return (standardize(v)[0] * vec[gain : gain + 1, :] + vec[shift : shift + 1, :]).astype(BF)


def norm_back(v, grad, gain):
    xh, scale = standardize(v)
    dxh = grad * gain
    inner = jnp.mean(dxh * xh, axis=-1, keepdims=True)
    out = scale * (dxh - jnp.mean(dxh, axis=-1, keepdims=True) - xh * inner)
    return out, grad * xh


def total(refs):
    out = refs[0][...].astype(F32)
    for ref in refs[1:]:
        out = out + ref[...].astype(F32)
    return out


def fold(v, op):
    return op(v.reshape(-1, 8, v.shape[1]), axis=0)


def add_rows(ref, rows):
    for k, row in enumerate(rows):
        ref[8 * k : 8 * k + 8, :] += fold(row, jnp.sum)


def rowwise(body, row_ins, fulls, row_outs, sums, name):
    rows, width = row_ins[0].shape
    step = min(32, rows)
    many, some, outs = len(row_ins), len(fulls), len(row_outs)

    def kernel(*refs):
        in_refs, full_refs = refs[:many], refs[many : many + some]
        out_refs = refs[many + some : many + some + outs]
        extra = refs[many + some + outs :]
        if sums:
            extra[1][...] = jnp.zeros_like(extra[1])

        def one(i, carry):
            at = pl.ds(pl.multiple_of(i * step, step), step)
            body(
                *[r.at[at, :] for r in in_refs],
                *full_refs,
                *[r.at[at, :] for r in out_refs],
                *extra[1:],
            )
            return carry

        lax.fori_loop(0, rows // step, one, 0)
        for k in range(sums):
            extra[0][k : k + 1, :] = jnp.sum(
                extra[1][8 * k : 8 * k + 8, :], axis=0, keepdims=True
            )

    out_shape = [sds((rows, width), d) for d in row_outs]
    out_shape += [sds((sums, width), F32)] if sums else []
    return pl.pallas_call(
        kernel,
        grid=(1,),
        in_specs=[whole(a.shape) for a in (*row_ins, *fulls)],
        out_specs=[whole(a.shape) for a in out_shape],
        out_shape=out_shape,
        scratch_shapes=[pltpu.VMEM((8 * sums, width), F32)] if sums else [],
        compiler_params=params(8, 1),
        cost_estimate=cost(2),
        name=name,
    )(*row_ins, *fulls)


def norm_first(x, vec):
    def body(x_ref, vec_ref, out_ref):
        out_ref[...] = norm_of(x_ref[...].astype(F32), vec_ref[...], LN1_G, LN1_B)

    return rowwise(body, [x], [vec], [BF], 0, "norm_first")[0]


def after_attention(x, terms, vec):
    count = len(terms)

    def body(*refs):
        x_ref, term_refs, vec_ref = refs[0], refs[1 : 1 + count], refs[1 + count]
        att_ref, res_ref, norm_ref = refs[2 + count :]
        v = vec_ref[...]
        attended = total(term_refs) + v[OUT_B : OUT_B + 1, :]
        residual = x_ref[...].astype(F32) + v[SC_ATTN : SC_ATTN + 1, :] * attended
        att_ref[...] = attended.astype(BF)
        res_ref[...] = residual
        norm_ref[...] = norm_of(residual, v, LN2_G, LN2_B)

    return rowwise(body, [x, *terms], [vec], [BF, F32, BF], 0, "after_attention")


def after_mlp(residual, terms, vec, vec_next):
    count = len(terms)

    def body(*refs):
        res_ref, term_refs = refs[0], refs[1 : 1 + count]
        vec_ref, next_ref, mlp_ref, y_ref, norm_ref = refs[1 + count :]
        v = vec_ref[...]
        mlp = total(term_refs) + v[FC2_B : FC2_B + 1, :]
        y = (res_ref[...] + v[SC_MLP : SC_MLP + 1, :] * mlp).astype(BF)
        mlp_ref[...] = mlp.astype(BF)
        y_ref[...] = y
        norm_ref[...] = norm_of(y.astype(F32), next_ref[...], LN1_G, LN1_B)

    return rowwise(body, [residual, *terms], [vec, vec_next], [BF, BF, BF], 0, "after_mlp")


def last_output(residual, terms, grad, vec):
    count = len(terms)

    def body(*refs):
        res_ref, term_refs = refs[0], refs[1 : 1 + count]
        grad_ref, vec_ref, y_ref, sum_ref = refs[1 + count :]
        v = vec_ref[...]
        mlp = total(term_refs) + v[FC2_B : FC2_B + 1, :]
        y_ref[...] = (res_ref[...] + v[SC_MLP : SC_MLP + 1, :] * mlp).astype(BF)
        add_rows(sum_ref, [grad_ref[...].astype(F32) * mlp])

    return rowwise(body, [residual, *terms, grad], [vec], [BF], 1, "last_output")


def start_back(grad, vec):
    def body(grad_ref, vec_ref, out_ref, sum_ref):
        low = (vec_ref[...][SC_MLP : SC_MLP + 1, :] * grad_ref[...].astype(F32)).astype(BF)
        out_ref[...] = low
        add_rows(sum_ref, [low.astype(F32)])

    return rowwise(body, [grad], [vec], [BF], 1, "start_back")


def back_second(grad, residual, attended, terms, vec):
    count = len(terms)

    def body(*refs):
        grad_ref, res_ref, att_ref = refs[:3]
        term_refs = refs[3 : 3 + count]
        vec_ref, dres_ref, low_ref, sum_ref = refs[3 + count :]
        v = vec_ref[...]
        dn = total(term_refs)
        back, dgain = norm_back(res_ref[...], dn, v[LN2_G : LN2_G + 1, :])
        dres = grad_ref[...].astype(F32) + back
        low = (v[SC_ATTN : SC_ATTN + 1, :] * dres).astype(BF)
        dres_ref[...] = dres
        low_ref[...] = low
        add_rows(sum_ref, [dgain, dn, dres * att_ref[...].astype(F32), low.astype(F32)])

    return rowwise(
        body, [grad, residual, attended, *terms], [vec], [F32, BF], 4, "back_second"
    )


def back_first(dres, x, terms, vec, mlp_below=None, vec_below=None):
    count = len(terms)
    below = mlp_below is not None

    def body(*refs):
        dres_ref, x_ref = refs[:2]
        term_refs = refs[2 : 2 + count]
        rest = refs[2 + count :]
        if below:
            mlp_ref, vec_ref, under_ref, dx_ref, low_ref, sum_ref = rest
        else:
            vec_ref, dx_ref, sum_ref = rest
        v = vec_ref[...]
        dn = total(term_refs)
        back, dgain = norm_back(x_ref[...].astype(F32), dn, v[LN1_G : LN1_G + 1, :])
        dx = (dres_ref[...] + back).astype(BF)
        dx_ref[...] = dx
        rows = [dgain, dn]
        if below:
            wide = dx.astype(F32)
            low = (under_ref[...][SC_MLP : SC_MLP + 1, :] * wide).astype(BF)
            low_ref[...] = low
            rows += [wide * mlp_ref[...].astype(F32), low.astype(F32)]
        add_rows(sum_ref, rows)

    row_ins = [dres, x, *terms] + ([mlp_below] if below else [])
    fulls = [vec] + ([vec_below] if below else [])
    return rowwise(body, row_ins, fulls, [BF, BF] if below else [BF], 4 if below else 2, "back_first")


def project_qkv(pair, weight, bias):
    rows, width = pair[0].shape
    cols = bias.shape[1]

    def body(a_ref, b_ref, w_ref, bias_ref, out_ref):
        w = w_ref[...]
        shift = bias_ref[...]
        out_ref[:rows, :] = (dot(a_ref[...], w) + shift).astype(BF)
        out_ref[rows:, :] = (dot(b_ref[...], w) + shift).astype(BF)

    return pl.pallas_call(
        body,
        grid=(1,),
        in_specs=[
            whole((rows, width)), whole((rows, width)), whole((width, cols)), whole((1, cols))
        ],
        out_specs=whole((2 * rows, cols)),
        out_shape=sds((2 * rows, cols), BF),
        compiler_params=params(6, 1),
        cost_estimate=cost(2),
        name="project_qkv",
    )(*pair, weight, bias)


def head_rows(v, head, size):
    rows = lax.broadcasted_iota(jnp.int32, v.shape, 0)
    return jnp.where(rows // size == head, v, jnp.zeros_like(v))


def head_cols(v, head, size):
    cols = lax.broadcasted_iota(jnp.int32, v.shape, 1)
    return jnp.where(cols // size == head, v, jnp.zeros_like(v))


def attention(packed, weight, size):
    chips = len(packed)
    span = packed[0].shape[0]
    half = span // 2
    width = packed[0].shape[1] // 3
    seq = chips * span
    heads = width // size
    model = weight.shape[0]
    step = min(256, seq)
    chunk = min(128, seq)
    score = size**-0.5

    def body(*refs):
        in_refs, w_ref = refs[:chips], refs[chips]
        head_refs = refs[chips + 1 : 2 * chips + 1]
        lse_ref = refs[2 * chips + 1]
        part_refs = refs[2 * chips + 2 : 4 * chips + 2]
        k_ref, qt_ref, vt_ref, ot_ref, s_ref, p_ref = refs[4 * chips + 2 :]
        for c in range(chips):
            at = slice(c * span, (c + 1) * span)
            k_ref[at, :] = in_refs[c][:, width : 2 * width]
            qt_ref[:, at] = (turn(in_refs[c][:, :width]) * score).astype(BF)
            vt_ref[:, at] = turn(in_refs[c][:, 2 * width :]).astype(BF)

        def one(i, carry):
            at = pl.ds(pl.multiple_of(i * step, step), step)
            q = qt_ref[:, at]
            s_ref[0] = dot(k_ref[...], head_rows(q, 0, size))
            for h in range(heads):
                if h + 1 < heads:
                    s_ref[(h + 1) % 2] = dot(k_ref[...], head_rows(q, h + 1, size))
                now = h % 2
                top = fold(s_ref[now, :chunk, :], jnp.max)
                for r in range(chunk, seq, chunk):
                    top = jnp.maximum(top, fold(s_ref[now, r : r + chunk, :], jnp.max))
                top = jnp.max(top, axis=0, keepdims=True)
                norm = jnp.zeros((8, step), F32)
                for r in range(0, seq, chunk):
                    p = jnp.exp(s_ref[now, r : r + chunk, :] - top)
                    norm = norm + fold(p, jnp.sum)
                    p_ref[now, r : r + chunk, :] = p.astype(BF)
                norm = jnp.sum(norm, axis=0, keepdims=True)
                rows = slice(h * size, (h + 1) * size)
                ot_ref[rows, at] = dot(vt_ref[rows, :], p_ref[now]) / norm
                lse_ref[h : h + 1, at] = top + jnp.log(norm)
            return carry

        lax.fori_loop(0, seq // step, one, 0)
        for c in range(chips):
            at = slice(c * span, (c + 1) * span)
            o = ot_ref[:, at].T.astype(BF)
            head_refs[c][...] = o
            part_refs[2 * c][...] = dot_bt(o[:half], w_ref[...]).astype(BF)
            part_refs[2 * c + 1][...] = dot_bt(o[half:], w_ref[...]).astype(BF)

    out = pl.pallas_call(
        body,
        grid=(1,),
        in_specs=[whole((span, 3 * width))] * chips
        + [pl.BlockSpec((model, width), lambda i: (0, 3), pipeline_mode=pl.Buffered(1))],
        out_specs=[whole((span, width))] * chips
        + [whole((heads, seq))]
        + [whole((half, model))] * (2 * chips),
        out_shape=[sds((span, width), BF)] * chips
        + [sds((heads, seq), F32)]
        + [sds((half, model), BF)] * (2 * chips),
        scratch_shapes=[
            pltpu.VMEM((seq, width), BF),
            pltpu.VMEM((width, seq), BF),
            pltpu.VMEM((width, seq), BF),
            pltpu.VMEM((width, seq), F32),
            pltpu.VMEM((2, seq, step), F32),
            pltpu.VMEM((2, seq, step), BF),
        ],
        compiler_params=params(14, 1),
        cost_estimate=cost(9),
        name="attention",
    )(*packed, weight)
    parts = out[chips + 1 :]
    return out[:chips], out[chips], [(parts[2 * c], parts[2 * c + 1]) for c in range(chips)]


def attention_back(packed, heads_kept, lse, datt, weight, size):
    chips = len(packed)
    span = packed[0].shape[0]
    half = span // 2
    width = packed[0].shape[1] // 3
    seq = chips * span
    heads = width // size
    model = weight.shape[0]
    step = min(256, seq)
    chunk = min(128, seq)
    score = size**-0.5

    def body(*refs):
        at = 0

        def take(count):
            nonlocal at
            at += count
            return refs[at - count : at]

        in_refs, kept_refs = take(chips), take(chips)
        (lse_ref,) = take(1)
        datt_refs = take(2 * chips)
        (w_ref,) = take(1)
        dqkv_refs = take(chips)
        part_refs = take(2 * chips)
        (sum_ref,) = take(1)
        k_ref, v_ref, kt_ref, qt_ref, q_ref, do_ref, dot_ref = take(7)
        inner_ref, s_ref, g_ref, p_ref, ds_ref, dk_ref, dv_ref, dqt_ref = take(8)
        for c in range(chips):
            rows = slice(c * span, (c + 1) * span)
            q = in_refs[c][:, :width].astype(F32) * score
            k = in_refs[c][:, width : 2 * width]
            q_ref[rows, :] = q.astype(BF)
            qt_ref[:, rows] = q.T.astype(BF)
            k_ref[rows, :] = k
            kt_ref[:, rows] = turn(k).astype(BF)
            v_ref[rows, :] = in_refs[c][:, 2 * width :]
            for b in range(2):
                d = dot(datt_refs[2 * c + b][...], w_ref[:, 3 * width :]).astype(BF)
                here = slice(c * span + b * half, c * span + (b + 1) * half)
                do_ref[here, :] = d
                dt = turn(d)
                dot_ref[:, here] = dt.astype(BF)
                prod = dt * turn(kept_refs[c][b * half : (b + 1) * half, :])
                for h in range(heads):
                    inner_ref[h : h + 1, here] = jnp.sum(
                        prod[h * size : (h + 1) * size, :], axis=0, keepdims=True
                    )

        def one(i, carry):
            at = pl.ds(pl.multiple_of(i * step, step), step)
            qt = qt_ref[:, at]
            dot_t = dot_ref[:, at]
            q = q_ref[at, :]
            do = do_ref[at, :]

            def scores(h):
                s_ref[h % 2] = dot(k_ref[...], head_rows(qt, h, size))
                g_ref[h % 2] = dot(v_ref[...], head_rows(dot_t, h, size))

            scores(0)
            for h in range(heads):
                if h + 1 < heads:
                    scores(h + 1)
                now = h % 2
                cols = slice(h * step, (h + 1) * step)
                lse = lse_ref[h : h + 1, at]
                inner = inner_ref[h : h + 1, at]
                for r in range(0, seq, chunk):
                    p = jnp.exp(s_ref[now, r : r + chunk, :] - lse)
                    ds = p * (g_ref[now, r : r + chunk, :] - inner)
                    p_ref[r : r + chunk, cols] = p.astype(BF)
                    ds_ref[r : r + chunk, cols] = ds.astype(BF)
                rows = slice(h * size, (h + 1) * size)
                dqt_ref[rows, at] = dot(kt_ref[rows, :], ds_ref[:, cols]) * score
            dv = dot(p_ref[...], jnp.concatenate([head_cols(do, h, size) for h in range(heads)], 0))
            dk = dot(ds_ref[...], jnp.concatenate([head_cols(q, h, size) for h in range(heads)], 0))

            @pl.when(i == 0)
            def _():
                dv_ref[...] = dv
                dk_ref[...] = dk

            @pl.when(i > 0)
            def _():
                dv_ref[...] += dv
                dk_ref[...] += dk

            return carry

        lax.fori_loop(0, seq // step, one, 0)
        for c in range(chips):
            rows = slice(c * span, (c + 1) * span)
            out = dqkv_refs[c]
            out[:, :width] = dqt_ref[:, rows].T.astype(BF)
            out[:, width : 2 * width] = dk_ref[rows, :].astype(BF)
            out[:, 2 * width :] = dv_ref[rows, :].astype(BF)
            sums = jnp.sum(out[...].astype(F32), axis=0, keepdims=True)
            if c == 0:
                sum_ref[...] = sums
            else:
                sum_ref[...] += sums
            for b in range(2):
                part_refs[2 * c + b][...] = dot_bt(
                    out[b * half : (b + 1) * half, :], w_ref[:, : 3 * width]
                ).astype(BF)

    flat = [g for pair in datt for g in pair]
    out_shape = (
        [sds((span, 3 * width), BF)] * chips
        + [sds((half, model), BF)] * (2 * chips)
        + [sds((1, 3 * width), F32)]
    )
    operands = (*packed, *heads_kept, lse, *flat, weight)
    out = pl.pallas_call(
        body,
        grid=(1,),
        in_specs=[whole(a.shape) for a in operands],
        out_specs=[whole(a.shape) for a in out_shape],
        out_shape=out_shape,
        scratch_shapes=[
            pltpu.VMEM((seq, width), BF),
            pltpu.VMEM((seq, width), BF),
            pltpu.VMEM((width, seq), BF),
            pltpu.VMEM((width, seq), BF),
            pltpu.VMEM((seq, width), BF),
            pltpu.VMEM((seq, width), BF),
            pltpu.VMEM((width, seq), BF),
            pltpu.VMEM((heads, seq), F32),
            pltpu.VMEM((2, seq, step), F32),
            pltpu.VMEM((2, seq, step), F32),
            pltpu.VMEM((seq, heads * step), BF),
            pltpu.VMEM((seq, heads * step), BF),
            pltpu.VMEM((seq, width), F32),
            pltpu.VMEM((seq, width), F32),
            pltpu.VMEM((width, seq), F32),
        ],
        compiler_params=params(26, 1),
        cost_estimate=cost(15),
        name="attention_back",
    )(*operands)
    parts = out[chips : 3 * chips]
    return (
        out[:chips],
        [(parts[2 * c], parts[2 * c + 1]) for c in range(chips)],
        out[3 * chips],
    )


def gelu_both(x):
    away = jnp.abs(x)
    t = 1.0 / (1.0 + (0.3275911 * 0.5**0.5) * away)
    bell = jnp.exp(-0.5 * (x * x))
    poly = t * (
        0.127414796
        + t * (-0.142248368 + t * (0.7107068705 + t * (-0.7265760135 + t * 0.5307027145)))
    )
    tail = poly * bell
    phi = jnp.where(x >= 0, 1.0 - tail, tail)
    return x * phi, phi + x * (bell * 0.3989422804014327)


def mlp_call(body, pairs, extra, weight, bias, outs, parts, scratch, name):
    rows, model = pairs[0].shape
    units = weight.shape[1] // 2
    step = min(256, units)
    blocks = units // step
    cols = lambda j: (0, j)
    in_specs = [whole((rows, model)) for _ in pairs]
    in_specs += [pl.BlockSpec((2 * rows, step), cols) for _ in extra]
    in_specs += [
        pl.BlockSpec((model, step), cols),
        pl.BlockSpec((model, step), lambda j: (0, blocks + j)),
        pl.BlockSpec((1, step), cols),
    ]
    out_specs = [pl.BlockSpec((2 * rows, step), cols) for _ in outs]
    out_specs += [pl.BlockSpec((1, step), cols)]
    out_specs += [whole((rows, model))] * (2 * parts)
    out_shape = [sds((2 * rows, units), d) for d in outs] + [sds((1, units), F32)]
    out_shape += [sds((rows, model), BF)] * (2 * parts)
    count = len(pairs) // 2
    return pl.pallas_call(
        body,
        grid=(blocks,),
        in_specs=in_specs,
        out_specs=out_specs,
        out_shape=out_shape,
        scratch_shapes=[pltpu.VMEM((2 * rows, model), F32)] * parts
        + [pltpu.VMEM((2 * rows, step), F32)] * scratch,
        compiler_params=params(8 + 5 * parts, 1),
        cost_estimate=cost(3 + 3 * parts),
        name=name,
    )(*pairs, *extra, weight, weight, bias)


def clear(*refs):
    @pl.when(pl.program_id(0) == 0)
    def _():
        for ref in refs:
            ref[...] = jnp.zeros_like(ref)


def finish(acc, low, high):
    rows = low.shape[0]

    @pl.when(pl.program_id(0) == pl.num_programs(0) - 1)
    def _():
        low[...] = acc[:rows, :].astype(BF)
        high[...] = acc[rows:, :].astype(BF)


CHUNK = 32


def mlp_forward(pair, weight, bias):
    rows = pair[0].shape[0]

    def body(a, b, w1_ref, w2_ref, bias_ref, act_ref, slope_ref, sum_ref, lo, hi, acc, pre):
        clear(acc, sum_ref)
        shift = bias_ref[...]
        for i, x in enumerate((a, b)):
            pre[i * rows : (i + 1) * rows, :] = dot(x[...], w1_ref[...])
        for i in range(2):
            at = slice(i * rows, (i + 1) * rows)
            for r in range(i * rows, (i + 1) * rows, CHUNK):
                act, slope = gelu_both(pre[r : r + CHUNK, :] + shift)
                act_ref[r : r + CHUNK, :] = act.astype(BF)
                slope_ref[r : r + CHUNK, :] = slope.astype(BF)
            acc[at, :] += dot_bt(act_ref[at, :], w2_ref[...])
        finish(acc, lo, hi)

    act, slope, _, lo, hi = mlp_call(body, pair, [], weight, bias, [BF, BF], 1, 1, "mlp_forward")
    return act, slope, (lo, hi)


def mlp_backward(pair, slope, weight, bias):
    rows = pair[0].shape[0]

    def body(a, b, slope_ref, w1_ref, w2_ref, bias_ref, dpre_ref, sum_ref, lo, hi, acc, pre):
        clear(acc)
        for i, g in enumerate((a, b)):
            pre[i * rows : (i + 1) * rows, :] = dot(g[...], w2_ref[...])
        sums = jnp.zeros((8, bias_ref.shape[1]), F32)
        for i in range(2):
            at = slice(i * rows, (i + 1) * rows)
            for r in range(i * rows, (i + 1) * rows, CHUNK):
                d = pre[r : r + CHUNK, :] * slope_ref[r : r + CHUNK, :].astype(F32)
                d = d.astype(BF)
                dpre_ref[r : r + CHUNK, :] = d
                sums = sums + fold(d.astype(F32), jnp.sum)
            acc[at, :] += dot_bt(dpre_ref[at, :], w1_ref[...])
        sum_ref[...] = jnp.sum(sums, axis=0, keepdims=True)
        finish(acc, lo, hi)

    dpre, sums, lo, hi = mlp_call(
        body, pair, [slope], weight, bias, [BF], 1, 1, "mlp_backward"
    )
    return dpre, sums, (lo, hi)


def mlp_both(pair, grads, weight, bias):
    rows = pair[0].shape[0]

    def body(
        a, b, c, d, w1_ref, w2_ref, bias_ref, act_ref, dpre_ref, sum_ref,
        lo, hi, blo, bhi, acc, back, pre, grad,
    ):
        clear(acc, back)
        shift = bias_ref[...]
        for i, (x, g) in enumerate(((a, c), (b, d))):
            at = slice(i * rows, (i + 1) * rows)
            pre[at, :] = dot(x[...], w1_ref[...])
            grad[at, :] = dot(g[...], w2_ref[...])
        sums = jnp.zeros((8, bias_ref.shape[1]), F32)
        for i in range(2):
            at = slice(i * rows, (i + 1) * rows)
            for r in range(i * rows, (i + 1) * rows, CHUNK):
                act, slope = gelu_both(pre[r : r + CHUNK, :] + shift)
                act_ref[r : r + CHUNK, :] = act.astype(BF)
                dpre = (grad[r : r + CHUNK, :] * slope).astype(BF)
                dpre_ref[r : r + CHUNK, :] = dpre
                sums = sums + fold(dpre.astype(F32), jnp.sum)
            back[at, :] += dot_bt(dpre_ref[at, :], w1_ref[...])
            acc[at, :] += dot_bt(act_ref[at, :], w2_ref[...])
        sum_ref[...] = jnp.sum(sums, axis=0, keepdims=True)
        finish(acc, lo, hi)
        finish(back, blo, bhi)

    act, dpre, sums, lo, hi, blo, bhi = mlp_call(
        body, [*pair, *grads], [], weight, bias, [BF, BF], 2, 2, "mlp_both"
    )
    return act, dpre, sums, (lo, hi), (blo, bhi)


def weight_grads(products, dp, side, name, halves=True):
    model = products[0][0][0].shape[1]
    step = model // dp
    half = step // 2
    sizes = [(len(left), len(right), right[0].shape[1]) for left, right in products]
    cols = sum(n for _, _, n in sizes)

    def body(side_ref, *refs):
        acc_ref = refs[-1]
        outs = refs[-3:-1] if halves else refs[-2:-1]
        at = base = 0
        for many, few, n in sizes:
            lefts, rights = refs[at : at + many], refs[at + many : at + many + few]
            at += many + few
            ratio = many // few
            acc = None
            for i in range(many):
                size = lefts[i].shape[0]
                here = slice((i % ratio) * size, (i % ratio + 1) * size)
                term = dot_at(lefts[i][...], rights[i // ratio][here, :])
                acc = term if acc is None else acc + term
            if halves:
                acc_ref[:, base : base + n] = acc
            else:
                outs[0][:, base : base + n] = acc.astype(BF)
            base += n
        if not halves:
            return
        low = pl.multiple_of(side_ref[0] * half, half)
        high = pl.multiple_of((1 - side_ref[0]) * half, half)
        outs[0][...] = acc_ref[pl.ds(low, half), :].astype(BF)
        outs[1][...] = acc_ref[pl.ds(high, half), :].astype(BF)

    specs, operands = [pl.BlockSpec(memory_space=pltpu.SMEM)], [side.reshape(1)]
    for left, right in products:
        specs += [pl.BlockSpec((a.shape[0], step), lambda i: (0, i)) for a in left]
        specs += [whole(b.shape) for b in right]
        operands += [*left, *right]
    size = half if halves else step
    out = pl.pallas_call(
        body,
        grid=(dp,),
        in_specs=specs,
        out_specs=[pl.BlockSpec((size, cols), lambda i: (i, 0))] * (step // size),
        out_shape=[sds((dp * size, cols), BF)] * (step // size),
        scratch_shapes=[pltpu.VMEM((step, cols), F32)],
        compiler_params=params(14, 1),
        cost_estimate=cost(5),
        name=name,
    )(*operands)
    return out if halves else (out[0], None)


def pieces(chunks):
    return [p for pair in chunks for p in pair]


def shards(
    tokens, cotangent, ln1_gain, ln1_bias, w_qkv, qv_bias, w_out, out_bias, scale_attn,
    ln2_gain, ln2_bias, w_fc1, fc1_bias, w_fc2, fc2_bias, scale_mlp,
):
    side = lax.axis_index("section")
    first = side == 0
    dp = lax.axis_size("dp")
    here = lax.axis_index("dp")
    chips = lax.axis_size("tensor") // 2
    rows, model = tokens.shape[2:]
    heads = qv_bias.shape[1]
    size = qv_bias.shape[2] * dp // 2
    width = heads * size
    units = w_fc1.shape[2]
    part = model // dp

    x0 = lax.dynamic_index_in_dim(tokens, side, 0, keepdims=False).reshape(rows, model)
    grad_top = lax.dynamic_index_in_dim(cotangent, side, 0, keepdims=False).reshape(rows, model)

    vectors = (ln1_gain, ln1_bias, out_bias, scale_attn, ln2_gain, ln2_bias, fc2_bias, scale_mlp)
    packed = jnp.concatenate(
        [v.reshape(-1) for v in vectors] + [fc1_bias.reshape(-1), qv_bias.reshape(-1)]
    )
    own_qkv = w_qkv.reshape(part, heads, 3, size).swapaxes(1, 2).reshape(part, 3 * width)
    own_att = jnp.concatenate([own_qkv, w_out[0].T], axis=1)
    own_ff = jnp.concatenate([w_fc1[0], w_fc2[0].T], axis=1)

    def halves(own, came, rest):
        mine, left = half_of(own, side), half_of(own, 1 - side)
        return (
            (jnp.where(first, mine, came), jnp.where(first, left, rest)),
            (jnp.where(first, came, mine), jnp.where(first, rest, left)),
        )

    came_att = swap_section(half_of(own_att, 1 - side))
    ring_att0 = jnp.where(first, half_of(own_att, side), came_att)
    small = gather_small(packed, first, ring_att0).astype(F32)
    cut = 8 * part
    vecs = small[:, :, :cut].reshape(2, dp, 8, part).swapaxes(1, 2).reshape(2, 8, model)
    bias_fc1 = small[:, :, cut : cut + units // dp].reshape(2, 1, units)
    qv = small[:, :, cut + units // dp :].reshape(2, dp, heads, -1).swapaxes(1, 2)
    qv = qv.reshape(2, heads, 2, size)
    bias_qkv = jnp.stack([qv[:, :, 0], jnp.zeros_like(qv[:, :, 0]), qv[:, :, 1]], axis=1)
    bias_qkv = bias_qkv.reshape(2, 1, 3 * width)
    vecs = (vecs[0], vecs[1])

    norm1 = norm_first(tie(x0, came_att), vecs[0])
    came_ff = swap_section(tie(half_of(own_ff, 1 - side), came_att))
    rest_att = swap_section(tie(half_of(own_att, side), came_att))
    half_att0, half_att1 = halves(own_att, came_att, rest_att)
    ring_ff0 = jnp.where(first, half_of(own_ff, side), came_ff)

    def put_together(half, hops, backs):
        return assemble([half, *zip(hops, backs)], model)

    hops_att0 = direct(ring_att0)
    att0 = put_together(half_att0, hops_att0, [swap_section(tie(v, norm1)) for v in hops_att0])
    hops_ff0 = ring(tie(ring_ff0, hops_att0[-1]))
    rest_ff = swap_section(tie(half_of(own_ff, side), hops_ff0[0]))
    half_ff0, half_ff1 = halves(own_ff, came_ff, rest_ff)
    whole_att1 = jnp.where(
        first, jnp.concatenate(half_att1), jnp.concatenate(half_att1[::-1])
    )
    hops_att1 = ring(tie(whole_att1, hops_ff0[-1]))
    hops_ff1 = ring(tie(half_ff1[0], hops_att1[-1]))
    backs_ff0, backs_ff1 = ([swap_section(v) for v in hops] for hops in (hops_ff0, hops_ff1))

    def front(x, norm, weight, s, gather_beside, before, under, scatter_beside):
        chunks, qkv = gather_tokens(
            norm, lambda pair: project_qkv(pair, weight, bias_qkv[s]), gather_beside
        )
        kept, lse, parts = attention([*qkv[:-1], tie(qkv[-1], *before)], weight, size)
        parts = [parts[0], *[(same, tie(other, *under)) for same, other in parts[1:]]]
        terms, _ = scatter_tokens(parts, beside=scatter_beside)
        attended, residual, norm2 = after_attention(x, terms, vecs[s])
        return (chunks, qkv, kept, lse, attended, residual), norm2

    ff0, att1, ff1 = thirds(hops_ff0), thirds(hops_att1), thirds(hops_ff1)
    back_ff0, back_ff1 = thirds(backs_ff0), thirds(backs_ff1)
    saved0, norm2 = front(
        x0, norm1, att0, 0, (), ff0[0], (*ff0[1], *back_ff0[0]),
        (*ff0[2], *back_ff0[1], *att1[0]),
    )
    w_ff0 = put_together(half_ff0, hops_ff0, backs_ff0)
    second0, mlp0 = gather_tokens(
        norm2, lambda pair: mlp_forward(pair, w_ff0, bias_fc1[0]), att1[1]
    )
    terms, _ = scatter_tokens([m[2] for m in mlp0], beside=att1[2])
    mlp_out0, y0, norm1 = after_mlp(saved0[5], terms, vecs[0], vecs[1])

    w_att1 = assemble([(v,) for v in (whole_att1, *hops_att1)], model)
    low1, sums_fc2_1 = start_back(grad_top, vecs[1])
    grads1, _ = gather_tokens(tie(low1, norm1), lambda pair: pair[0])
    saved1, norm2 = front(
        y0, norm1, w_att1, 1, ff1[0], (), (*pieces(grads1), *ff1[1], *back_ff1[0]),
        (*ff1[2], *back_ff1[1]),
    )
    w_ff1 = put_together(half_ff1, hops_ff1, backs_ff1)
    spare = list(grads1)
    second1, mlp1 = gather_tokens(
        norm2, lambda pair: mlp_both(pair, spare.pop(0), w_ff1, bias_fc1[1])
    )

    def grad_ff(second, mlp, grads, acts):
        def work(after):
            return weight_grads(
                [(pieces(second), [tie(mlp[0], after), *mlp[1:]]), (pieces(grads), acts)],
                dp,
                side,
                "grad_ff",
            )

        return work

    def grad_att(saved, halves):
        def work(after, datt, dqkv):
            return weight_grads(
                [(pieces(saved[0]), [tie(dqkv[0], after), *dqkv[1:]]), (pieces(datt), saved[2])],
                dp,
                side,
                "grad_att",
                halves,
            )

        return work

    acts1 = [m[0] for m in mlp1]
    parts_y1 = [m[3] for m in mlp1]
    sums_y1 = core_sums(parts_y1)
    local_y1 = [parts_y1[0][0], core_swap(parts_y1[0][1])]
    chain = {}

    def ff1_ready(after):
        g = grad_ff(second1, [m[1] for m in mlp1], grads1, acts1)(after)
        chain["ff1"] = ring_sum(*g, (0, 1))
        return g

    parts_back1 = [m[4] for m in mlp1]
    came_y0 = lax.ppermute(y0, "section", [(1, 0)])
    terms, g_ff1 = scatter_tokens(parts_back1, ff1_ready, [came_y0])
    step_ff1, own_ff1 = chain["ff1"]
    step_ff1 = [step_ff1[0], *thirds(step_ff1[1:-1]), step_ff1[-1]]
    flat = lambda steps: [v for step in steps for v in step]
    dres1, low1b, sums1 = back_second(grad_top, saved1[5], saved1[4], terms, vecs[1])
    datt1, _ = gather_tokens(low1b, lambda pair: pair[0], step_ff1[0])
    terms_y1 = send_sums([tie(v, datt1[-1][0]) for v in sums_y1])
    dqkv1, parts, qkv_sums1 = attention_back(
        saved1[1], saved1[2], saved1[3], datt1, w_att1, size
    )
    parts = [
        parts[0],
        *[(same, tie(other, *terms_y1, *flat(step_ff1[1]))) for same, other in parts[1:]],
    ]
    terms, g_att1 = scatter_tokens(
        parts, lambda after: grad_att(saved1, False)(after, datt1, dqkv1)[0], flat(step_ff1[2])
    )
    dx1, low0, edge1 = back_first(dres1, y0, terms, vecs[1], mlp_out0, vecs[0])
    y1, sums_sc_1 = last_output(saved1[5], local_y1 + terms_y1, grad_top, vecs[1])
    step_att1, own_att1 = ring_sum(tie(g_att1, low0), None, (0, 1))
    step_att1 = [*thirds(step_att1[:-1]), step_att1[-1]]

    came_y1 = lax.ppermute(tie(y1, low0), "section", [(0, 1)])

    slopes = [m[1] for m in mlp0]
    grads0, mlp_back0 = gather_tokens(
        low0,
        lambda pair: mlp_backward(pair, slopes.pop(0), w_ff0, bias_fc1[0]),
        (*flat(step_ff1[3]), *flat(step_att1[0])),
    )
    terms, g_ff0 = scatter_tokens(
        [m[2] for m in mlp_back0],
        grad_ff(second0, [m[0] for m in mlp_back0], grads0, [m[0] for m in mlp0]),
        (*step_ff1[4], *flat(step_att1[1]), came_y1),
    )
    dres0, low, sums0 = back_second(dx1, saved0[5], saved0[4], terms, vecs[0])
    step_ff0, own_ff0 = ring_sum(*tie_all(g_ff0, low), (1, 0))
    step_ff0 = [step_ff0[0], *thirds(step_ff0[1:-1]), step_ff0[-1]]
    datt0, _ = gather_tokens(
        low, lambda pair: pair[0], (*flat(step_att1[2]), *step_ff0[0])
    )
    dqkv0, parts, qkv_sums0 = attention_back(saved0[1], saved0[2], saved0[3], datt0, att0, size)
    parts = [
        parts[0],
        *[
            (same, tie(other, *step_att1[3], *flat(step_ff0[1])))
            for same, other in parts[1:]
        ],
    ]
    terms, g_att0 = scatter_tokens(
        parts,
        lambda after: grad_att(saved0, False)(after, datt0, dqkv0)[0],
        flat(step_ff0[2]),
    )
    came_dx1 = lax.ppermute(tie(dx1, dqkv0[0]), "section", [(0, 1)])
    dx0, edge0 = back_first(dres0, x0, terms, vecs[0])
    step_att0, own_att0 = ring_sum(g_att0, None, (1, 0), (dx0,))
    rs_ff1, rs_att1 = (own_ff1, step_ff1[-1][0]), (own_att1, step_att1[-1][0])
    rs_ff0, rs_att0 = (own_ff0, step_ff0[-1][0]), (own_att0, step_att0[-1][0])

    def both(low, high, came_low, came_high):
        mine = jnp.where(first, low, high)
        came = jnp.where(first, came_low, came_high)
        return jnp.stack([jnp.where(first, mine, came), jnp.where(first, came, mine)])[None, :, None]

    block_out = both(y0, y1, came_y0, came_y1)
    input_grads = both(dx0, dx1, lax.ppermute(dx0, "section", [(1, 0)]), came_dx1)

    def to_owner(low, high, pick):
        own = jnp.where(first, low, high) + swap_section(jnp.where(first, high, low))
        out = pick(own, here)
        for step in range(1, dp):
            pairs = [(i, (i + step) % dp) for i in range(dp)]
            out = out + lax.ppermute(pick(own, lax.rem(here + step, dp)), "dp", pairs)
        return out

    def by_unit(qkv_sums, unit_sums):
        q = qkv_sums[:, :width].reshape(heads, 1, size)
        v = qkv_sums[:, 2 * width :].reshape(heads, 1, size)
        bias = jnp.concatenate([q, v], 1).reshape(heads, dp, -1).swapaxes(0, 1).reshape(dp, -1)
        return jnp.concatenate([bias, unit_sums.reshape(dp, -1)], axis=1)

    unit = to_owner(
        by_unit(tie(qkv_sums0, dx0), sum(m[1] for m in mlp_back0)),
        by_unit(qkv_sums1, sum(m[2] for m in mlp1)),
        lambda v, place: lax.dynamic_slice_in_dim(v, place, 1, 0),
    )
    cut = heads * (2 * size // dp)
    bias_grad = unit[:, :cut].reshape(1, heads, -1)
    fc1_grad = unit[:, cut:].reshape(1, 1, -1)

    vec = jnp.concatenate(
        [edge0[:2], sums0[:4], edge1[2:4], edge1[:2], sums1[:4], sums_sc_1[:1], sums_fc2_1[:1]]
    )
    vec = vec + core_swap(vec)
    vec = tie(sum([from_chip(vec, step) for step in range(1, chips)], vec), *step_att0[0])
    vec = to_owner(
        vec[:8], vec[8:], lambda v, place: lax.dynamic_slice_in_dim(v, place * part, part, 1)
    )
    g_ln1, b_ln1, g_ln2, b_ln2, g_sc_attn, g_out_bias, g_sc_mlp, g_fc2_bias = (
        vec[i : i + 1] for i in range(8)
    )

    def owned(low, high):
        top = jnp.where(first, low[0], high[1].astype(F32))
        bottom = jnp.where(first, low[1].astype(F32), high[0])
        return jnp.concatenate([top, bottom], 0)

    g_ff = owned(rs_ff0, rs_ff1)
    g_att = jnp.where(
        first, rs_att0[0] + rs_att0[1].astype(F32), rs_att1[0] + rs_att1[1].astype(F32)
    )
    g_qkv = g_att[:, : 3 * width].reshape(part, 3, heads, size).swapaxes(1, 2)
    g_qkv = g_qkv.reshape(1, part, 3 * width)
    g_out = g_att[:, 3 * width :].T[None]
    g_fc1 = g_ff[:, :units][None]
    g_fc2 = g_ff[:, units:].T[None]
    return (
        block_out, input_grads, g_ln1, b_ln1, g_qkv, bias_grad, g_out, g_out_bias, g_sc_attn,
        g_ln2, b_ln2, g_fc1, fc1_grad, g_fc2, g_fc2_bias, g_sc_mlp,
    )


def solution(mesh):
    vec = P("section", "dp")
    by_row = P("section", "dp", "tensor")
    by_unit = P("section", "tensor", "dp")
    data = P(None, "dp", "tensor", None)
    split = P("section", None, "dp", "tensor", None)
    given = (
        vec, vec, by_row, by_unit, by_unit, vec, vec, vec, vec, by_row, by_unit, by_unit, vec, vec,
    )
    return jax.shard_map(
        shards,
        mesh=mesh,
        in_specs=(data, data) + given,
        out_specs=(split, split) + given,
        check_vma=False,
    )
```

```python
from functools import partial

import jax
import jax.numpy as jnp
from jax import lax
from jax.experimental import pallas as pl
from jax.experimental.pallas import tpu as pltpu
from jax.sharding import PartitionSpec as P

EPSILON = 1e-06
BF = jnp.bfloat16
F32 = jnp.float32
MIB = 1 << 20

LN1_G, LN1_B, OUT_B, SC_ATTN, LN2_G, LN2_B, FC2_B, SC_MLP = range(8)


def dot(a, b):
    return lax.dot_general(a, b, (((1,), (0,)), ((), ())), preferred_element_type=F32)


def dot_bt(a, b):
    return lax.dot_general(a, b, (((1,), (1,)), ((), ())), preferred_element_type=F32)


def dot_at(a, b):
    return lax.dot_general(a, b, (((0,), (0,)), ((), ())), preferred_element_type=F32)


def turn(v):
    return v.astype(F32).T


def params(limit, grid=0):
    return pltpu.CompilerParams(
        vmem_limit_bytes=limit * MIB,
        dimension_semantics=("arbitrary",) * grid if grid else None,
    )


def late(v):
    return pltpu.with_memory_space_constraint(v, pltpu.HBM)


def whole(shape):
    return pl.BlockSpec(shape, lambda i: (0, 0), pipeline_mode=pl.Buffered(1))


def cost(micros):
    return pl.CostEstimate(flops=int(micros * 1.15e9), bytes_accessed=0, transcendentals=0)


def sds(shape, dtype):
    return jax.ShapeDtypeStruct(shape, dtype)


def core_swap(v):
    count = lax.axis_size("tensor")
    return lax.ppermute(v, "tensor", [(i, i ^ 1) for i in range(count)])


def from_chip(v, step):
    count = lax.axis_size("tensor")
    chips = count // 2
    pairs = [(((i // 2 + step) % chips) * 2 + i % 2, i) for i in range(count)]
    return lax.ppermute(v, "tensor", pairs)


def tie(v, *after):
    if not after:
        return v
    return lax.optimization_barrier((v, *after))[0]


def tie_all(vs, *after):
    return lax.optimization_barrier((*vs, *after))[: len(vs)]


def gather_tokens(own, work, beside=()):
    chips = lax.axis_size("tensor") // 2
    came = [from_chip(own, step) for step in range(1, chips)]
    chunks = [(own, core_swap(own))]
    results = [work(chunks[0])]
    for same in came:
        same = tie(same, results[-1], *beside)
        chunks.append((same, core_swap(same)))
        results.append(work(chunks[-1]))
    return chunks, results


def core_sums(parts):
    return [
        (same.astype(F32) + core_swap(other).astype(F32)).astype(BF) for same, other in parts[1:]
    ]


def send_sums(sums):
    chips = len(sums) + 1
    return [from_chip(both, chips - step) for step, both in enumerate(sums, 1)]


def scatter_tokens(parts, work=None, beside=()):
    sums = core_sums(parts)
    terms = send_sums(sums)
    local = core_swap(tie(parts[0][1], sums[-1]))
    made = work(sums[-1]) if work else local
    terms = [tie(t, made, local, *beside) for t in terms]
    return [parts[0][0], *terms, local], made


def swap_section(v):
    return lax.ppermute(v, "section", [(0, 1), (1, 0)])


def assemble(shards, rows):
    count = len(shards)
    cut = len(shards[0])
    size, cols = shards[0][0].shape
    place = jnp.stack([lax.axis_index("dp"), lax.axis_index("section")])

    def body(place_ref, *refs):
        out_ref, sems = refs[count * cut :]
        z, x = place_ref[0], place_ref[1]
        started = []
        for k in range(count):
            base = lax.rem(z + (count - k), count) * (cut * size)
            for i, at in enumerate([base] if cut == 1 else [base + x * size, base + (1 - x) * size]):
                copy = pltpu.make_async_copy(
                    refs[k * cut + i],
                    out_ref.at[pl.ds(pl.multiple_of(at, size), size), :],
                    sems.at[k * cut + i],
                )
                copy.start()
                started.append(copy)
        for copy in started:
            copy.wait()

    hbm = pl.BlockSpec(memory_space=pl.ANY)
    return pl.pallas_call(
        body,
        in_specs=[pl.BlockSpec(memory_space=pltpu.SMEM)] + [hbm] * (count * cut),
        out_specs=pl.BlockSpec(memory_space=pltpu.VMEM),
        out_shape=sds((rows, cols), shards[0][0].dtype),
        scratch_shapes=[pltpu.SemaphoreType.DMA((count * cut,))],
        compiler_params=params(6),
        cost_estimate=cost(2),
        name="assemble",
    )(place, *[v for shard in shards for v in shard])


def half_of(v, which):
    half = v.shape[0] // 2
    return lax.dynamic_slice_in_dim(v, which * half, half, 0)


def direct(own):
    count = lax.axis_size("dp")
    return [
        lax.ppermute(own, "dp", [(i, (i + step) % count) for i in range(count)])
        for step in range(1, count)
    ]


def third(values, index):
    cuts = [-(-len(values) * i // 3) for i in range(4)]
    return values[cuts[index] : cuts[index + 1]]


class Ring:
    def __init__(self, own):
        self.last, self.hops, self.backs, self.at, self.back_at = own, [], [], 0, 0

    def hop(self, *gate):
        count = lax.axis_size("dp")
        pairs = [(i, (i + 1) % count) for i in range(count)]
        new = []
        for i in range(len(third(range(count - 1), self.at))):
            self.last = lax.ppermute(tie(self.last, *gate) if i == 0 else self.last, "dp", pairs)
            new.append(self.last)
        self.hops += new
        self.at += 1
        return new

    def back(self, *gate):
        count = lax.axis_size("dp")
        which = third(range(count - 1), self.back_at)
        new = [swap_section(tie(self.hops[i], *gate)) for i in which]
        self.backs += new
        self.back_at += 1
        return new


def gather_small(v, first, after):
    count = lax.axis_size("dp")
    came = swap_section(v)
    own = tie(jnp.stack([jnp.where(first, v, came), jnp.where(first, came, v)]), after)
    ahead = [own]
    for step in range(1, count):
        ahead.append(lax.ppermute(own, "dp", [(i, (i - step) % count) for i in range(count)]))
    twice = jnp.stack(ahead + ahead, axis=1)
    return lax.dynamic_slice_in_dim(twice, count - lax.axis_index("dp"), count, 1)


def dp_rows(v, back):
    dp = lax.axis_size("dp")
    part = v.shape[0] // dp
    place = lax.rem(lax.axis_index("dp") + (dp - back), dp)
    return lax.dynamic_slice_in_dim(v, place * part, part, 0)


class RingSum:
    def __init__(self, mine, other, pair):
        self.mine, self.other, self.pair = mine, other, pair
        self.going, self.at, self.done = None, 0, 0

    def one(self, gate):
        dp = lax.axis_size("dp")
        self.done += 1
        new = []
        if self.going is not None:
            pairs = [(i, (i + 1) % dp) for i in range(dp)]
            new.append(lax.ppermute(tie(self.going, *gate), "dp", pairs))
        new.append(swap_section(tie(dp_rows(self.other, self.done), *gate)))
        self.going = sum(t.astype(F32) for t in [dp_rows(self.mine, self.done), *new])
        if self.done < dp:
            self.going = self.going.astype(BF)
        return new

    def step(self, *gate):
        self.at += 1
        if self.at == 5:
            self.came = lax.ppermute(tie(self.going.astype(BF), *gate), "section", [self.pair])
            return [self.came]
        count = 1 if self.at == 1 else len(third(range(lax.axis_size("dp") - 1), self.at - 2))
        return [v for i in range(count) for v in self.one(gate if i == 0 else ())]


def standardize(v):
    centred = v - jnp.mean(v, axis=-1, keepdims=True)
    var = jnp.mean(centred * centred, axis=-1, keepdims=True)
    scale = lax.rsqrt(var + EPSILON)
    return centred * scale, scale


def norm_of(v, vec, gain, shift):
    return (standardize(v)[0] * vec[gain : gain + 1, :] + vec[shift : shift + 1, :]).astype(BF)


def norm_back(v, grad, gain):
    xh, scale = standardize(v)
    dxh = grad * gain
    inner = jnp.mean(dxh * xh, axis=-1, keepdims=True)
    out = scale * (dxh - jnp.mean(dxh, axis=-1, keepdims=True) - xh * inner)
    return out, grad * xh


def total(refs):
    out = refs[0][...].astype(F32)
    for ref in refs[1:]:
        out = out + ref[...].astype(F32)
    return out


def fold(v, op):
    return op(v.reshape(-1, 8, v.shape[1]), axis=0)


def add_rows(ref, rows):
    for k, row in enumerate(rows):
        ref[8 * k : 8 * k + 8, :] += fold(row, jnp.sum)


def rowwise(body, row_ins, fulls, row_outs, sums, name):
    rows, width = row_ins[0].shape
    step = min(32, rows)
    many, some, outs = len(row_ins), len(fulls), len(row_outs)

    def kernel(*refs):
        in_refs, full_refs = refs[:many], refs[many : many + some]
        out_refs = refs[many + some : many + some + outs]
        extra = refs[many + some + outs :]
        if sums:
            extra[1][...] = jnp.zeros_like(extra[1])

        def one(i, carry):
            at = pl.ds(pl.multiple_of(i * step, step), step)
            body(
                *[r.at[at, :] for r in in_refs],
                *full_refs,
                *[r.at[at, :] for r in out_refs],
                *extra[1:],
            )
            return carry

        lax.fori_loop(0, rows // step, one, 0)
        for k in range(sums):
            extra[0][k : k + 1, :] = jnp.sum(
                extra[1][8 * k : 8 * k + 8, :], axis=0, keepdims=True
            )

    out_shape = [sds((rows, width), d) for d in row_outs]
    out_shape += [sds((sums, width), F32)] if sums else []
    return pl.pallas_call(
        kernel,
        grid=(1,),
        in_specs=[whole(a.shape) for a in (*row_ins, *fulls)],
        out_specs=[whole(a.shape) for a in out_shape],
        out_shape=out_shape,
        scratch_shapes=[pltpu.VMEM((8 * sums, width), F32)] if sums else [],
        compiler_params=params(8, 1),
        cost_estimate=cost(2),
        name=name,
    )(*row_ins, *fulls)


def norm_first(x, vec):
    def body(x_ref, vec_ref, out_ref):
        out_ref[...] = norm_of(x_ref[...].astype(F32), vec_ref[...], LN1_G, LN1_B)

    return rowwise(body, [x], [vec], [BF], 0, "norm_first")[0]


def after_attention(x, terms, vec):
    count = len(terms)

    def body(*refs):
        x_ref, term_refs, vec_ref = refs[0], refs[1 : 1 + count], refs[1 + count]
        att_ref, res_ref, norm_ref = refs[2 + count :]
        v = vec_ref[...]
        attended = total(term_refs) + v[OUT_B : OUT_B + 1, :]
        residual = x_ref[...].astype(F32) + v[SC_ATTN : SC_ATTN + 1, :] * attended
        att_ref[...] = attended.astype(BF)
        res_ref[...] = residual
        norm_ref[...] = norm_of(residual, v, LN2_G, LN2_B)

    return rowwise(body, [x, *terms], [vec], [BF, F32, BF], 0, "after_attention")


def after_mlp(residual, terms, vec, vec_next):
    count = len(terms)

    def body(*refs):
        res_ref, term_refs = refs[0], refs[1 : 1 + count]
        vec_ref, next_ref, mlp_ref, y_ref, norm_ref = refs[1 + count :]
        v = vec_ref[...]
        mlp = total(term_refs) + v[FC2_B : FC2_B + 1, :]
        y = (res_ref[...] + v[SC_MLP : SC_MLP + 1, :] * mlp).astype(BF)
        mlp_ref[...] = mlp.astype(BF)
        y_ref[...] = y
        norm_ref[...] = norm_of(y.astype(F32), next_ref[...], LN1_G, LN1_B)

    return rowwise(body, [residual, *terms], [vec, vec_next], [BF, BF, BF], 0, "after_mlp")


def last_output(residual, terms, grad, vec):
    count = len(terms)

    def body(*refs):
        res_ref, term_refs = refs[0], refs[1 : 1 + count]
        grad_ref, vec_ref, y_ref, sum_ref = refs[1 + count :]
        v = vec_ref[...]
        mlp = total(term_refs) + v[FC2_B : FC2_B + 1, :]
        y_ref[...] = (res_ref[...] + v[SC_MLP : SC_MLP + 1, :] * mlp).astype(BF)
        add_rows(sum_ref, [grad_ref[...].astype(F32) * mlp])

    return rowwise(body, [residual, *terms, grad], [vec], [BF], 1, "last_output")


def start_back(grad, vec):
    def body(grad_ref, vec_ref, out_ref, sum_ref):
        low = (vec_ref[...][SC_MLP : SC_MLP + 1, :] * grad_ref[...].astype(F32)).astype(BF)
        out_ref[...] = low
        add_rows(sum_ref, [low.astype(F32)])

    return rowwise(body, [grad], [vec], [BF], 1, "start_back")


def back_second(grad, residual, attended, terms, vec):
    count = len(terms)

    def body(*refs):
        grad_ref, res_ref, att_ref = refs[:3]
        term_refs = refs[3 : 3 + count]
        vec_ref, dres_ref, low_ref, sum_ref = refs[3 + count :]
        v = vec_ref[...]
        dn = total(term_refs)
        back, dgain = norm_back(res_ref[...], dn, v[LN2_G : LN2_G + 1, :])
        dres = grad_ref[...].astype(F32) + back
        low = (v[SC_ATTN : SC_ATTN + 1, :] * dres).astype(BF)
        dres_ref[...] = dres
        low_ref[...] = low
        add_rows(sum_ref, [dgain, dn, dres * att_ref[...].astype(F32), low.astype(F32)])

    return rowwise(
        body, [grad, residual, attended, *terms], [vec], [F32, BF], 4, "back_second"
    )


def back_first(dres, x, terms, vec, mlp_below=None, vec_below=None):
    count = len(terms)
    below = mlp_below is not None

    def body(*refs):
        dres_ref, x_ref = refs[:2]
        term_refs = refs[2 : 2 + count]
        rest = refs[2 + count :]
        if below:
            mlp_ref, vec_ref, under_ref, dx_ref, low_ref, sum_ref = rest
        else:
            vec_ref, dx_ref, sum_ref = rest
        v = vec_ref[...]
        dn = total(term_refs)
        back, dgain = norm_back(x_ref[...].astype(F32), dn, v[LN1_G : LN1_G + 1, :])
        dx = (dres_ref[...] + back).astype(BF)
        dx_ref[...] = dx
        rows = [dgain, dn]
        if below:
            wide = dx.astype(F32)
            low = (under_ref[...][SC_MLP : SC_MLP + 1, :] * wide).astype(BF)
            low_ref[...] = low
            rows += [wide * mlp_ref[...].astype(F32), low.astype(F32)]
        add_rows(sum_ref, rows)

    row_ins = [dres, x, *terms] + ([mlp_below] if below else [])
    fulls = [vec] + ([vec_below] if below else [])
    return rowwise(body, row_ins, fulls, [BF, BF] if below else [BF], 4 if below else 2, "back_first")


def project_qkv(pair, weight, bias):
    rows, width = pair[0].shape
    cols = bias.shape[1]

    def body(a_ref, b_ref, w_ref, bias_ref, out_ref):
        w = w_ref[...]
        shift = bias_ref[...]
        out_ref[:rows, :] = (dot(a_ref[...], w) + shift).astype(BF)
        out_ref[rows:, :] = (dot(b_ref[...], w) + shift).astype(BF)

    return pl.pallas_call(
        body,
        grid=(1,),
        in_specs=[
            whole((rows, width)), whole((rows, width)), whole((width, cols)), whole((1, cols))
        ],
        out_specs=whole((2 * rows, cols)),
        out_shape=sds((2 * rows, cols), BF),
        compiler_params=params(6, 1),
        cost_estimate=cost(2),
        name="project_qkv",
    )(*pair, weight, bias)


def head_rows(v, head, size):
    rows = lax.broadcasted_iota(jnp.int32, v.shape, 0)
    return jnp.where(rows // size == head, v, jnp.zeros_like(v))


def head_cols(v, head, size):
    cols = lax.broadcasted_iota(jnp.int32, v.shape, 1)
    return jnp.where(cols // size == head, v, jnp.zeros_like(v))


def attention(packed, weight, size):
    chips = len(packed)
    span = packed[0].shape[0]
    half = span // 2
    width = packed[0].shape[1] // 3
    seq = chips * span
    heads = width // size
    model = weight.shape[0]
    step = min(256, seq)
    chunk = min(128, seq)
    score = size**-0.5

    def body(*refs):
        in_refs, w_ref = refs[:chips], refs[chips]
        head_refs = refs[chips + 1 : 2 * chips + 1]
        lse_ref = refs[2 * chips + 1]
        part_refs = refs[2 * chips + 2 : 4 * chips + 2]
        k_ref, qt_ref, vt_ref, ot_ref, s_ref, p_ref = refs[4 * chips + 2 :]
        for c in range(chips):
            at = slice(c * span, (c + 1) * span)
            k_ref[at, :] = in_refs[c][:, width : 2 * width]
            qt_ref[:, at] = (turn(in_refs[c][:, :width]) * score).astype(BF)
            vt_ref[:, at] = turn(in_refs[c][:, 2 * width :]).astype(BF)

        def one(i, carry):
            at = pl.ds(pl.multiple_of(i * step, step), step)
            q = qt_ref[:, at]
            s_ref[0] = dot(k_ref[...], head_rows(q, 0, size))
            for h in range(heads):
                if h + 1 < heads:
                    s_ref[(h + 1) % 2] = dot(k_ref[...], head_rows(q, h + 1, size))
                now = h % 2
                top = fold(s_ref[now, :chunk, :], jnp.max)
                for r in range(chunk, seq, chunk):
                    top = jnp.maximum(top, fold(s_ref[now, r : r + chunk, :], jnp.max))
                top = jnp.max(top, axis=0, keepdims=True)
                norm = jnp.zeros((8, step), F32)
                for r in range(0, seq, chunk):
                    p = jnp.exp(s_ref[now, r : r + chunk, :] - top)
                    norm = norm + fold(p, jnp.sum)
                    p_ref[now, r : r + chunk, :] = p.astype(BF)
                norm = jnp.sum(norm, axis=0, keepdims=True)
                rows = slice(h * size, (h + 1) * size)
                ot_ref[rows, at] = dot(vt_ref[rows, :], p_ref[now]) / norm
                lse_ref[h : h + 1, at] = top + jnp.log(norm)
            return carry

        lax.fori_loop(0, seq // step, one, 0)
        for c in range(chips):
            at = slice(c * span, (c + 1) * span)
            o = ot_ref[:, at].T.astype(BF)
            head_refs[c][...] = o
            part_refs[2 * c][...] = dot_bt(o[:half], w_ref[...]).astype(BF)
            part_refs[2 * c + 1][...] = dot_bt(o[half:], w_ref[...]).astype(BF)

    out = pl.pallas_call(
        body,
        grid=(1,),
        in_specs=[whole((span, 3 * width))] * chips
        + [pl.BlockSpec((model, width), lambda i: (0, 3), pipeline_mode=pl.Buffered(1))],
        out_specs=[whole((span, width))] * chips
        + [whole((heads, seq))]
        + [whole((half, model))] * (2 * chips),
        out_shape=[pltpu.HBM((span, width), BF)] * chips
        + [sds((heads, seq), F32)]
        + [sds((half, model), BF)] * (2 * chips),
        scratch_shapes=[
            pltpu.VMEM((seq, width), BF),
            pltpu.VMEM((width, seq), BF),
            pltpu.VMEM((width, seq), BF),
            pltpu.VMEM((width, seq), F32),
            pltpu.VMEM((2, seq, step), F32),
            pltpu.VMEM((2, seq, step), BF),
        ],
        compiler_params=params(14, 1),
        cost_estimate=cost(9),
        name="attention",
    )(*packed, weight)
    parts = out[chips + 1 :]
    return out[:chips], out[chips], [(parts[2 * c], parts[2 * c + 1]) for c in range(chips)]


def attention_back(packed, heads_kept, lse, datt, weight, size):
    chips = len(packed)
    span = packed[0].shape[0]
    half = span // 2
    width = packed[0].shape[1] // 3
    seq = chips * span
    heads = width // size
    model = weight.shape[0]
    step = min(256, seq)
    chunk = min(128, seq)
    score = size**-0.5

    def body(*refs):
        at = 0

        def take(count):
            nonlocal at
            at += count
            return refs[at - count : at]

        in_refs, kept_refs = take(chips), take(chips)
        (lse_ref,) = take(1)
        datt_refs = take(2 * chips)
        (w_ref,) = take(1)
        dqkv_refs = take(chips)
        part_refs = take(2 * chips)
        (sum_ref,) = take(1)
        k_ref, v_ref, kt_ref, qt_ref, q_ref, do_ref, dot_ref = take(7)
        inner_ref, s_ref, g_ref, p_ref, ds_ref, dk_ref, dv_ref, dqt_ref = take(8)
        for c in range(chips):
            rows = slice(c * span, (c + 1) * span)
            q = in_refs[c][:, :width].astype(F32) * score
            k = in_refs[c][:, width : 2 * width]
            q_ref[rows, :] = q.astype(BF)
            qt_ref[:, rows] = q.T.astype(BF)
            k_ref[rows, :] = k
            kt_ref[:, rows] = turn(k).astype(BF)
            v_ref[rows, :] = in_refs[c][:, 2 * width :]
            for b in range(2):
                d = dot(datt_refs[2 * c + b][...], w_ref[:, 3 * width :]).astype(BF)
                here = slice(c * span + b * half, c * span + (b + 1) * half)
                do_ref[here, :] = d
                dt = turn(d)
                dot_ref[:, here] = dt.astype(BF)
                prod = dt * turn(kept_refs[c][b * half : (b + 1) * half, :])
                for h in range(heads):
                    inner_ref[h : h + 1, here] = jnp.sum(
                        prod[h * size : (h + 1) * size, :], axis=0, keepdims=True
                    )

        def one(i, carry):
            at = pl.ds(pl.multiple_of(i * step, step), step)
            qt = qt_ref[:, at]
            dot_t = dot_ref[:, at]
            q = q_ref[at, :]
            do = do_ref[at, :]

            def scores(h):
                s_ref[h % 2] = dot(k_ref[...], head_rows(qt, h, size))
                g_ref[h % 2] = dot(v_ref[...], head_rows(dot_t, h, size))

            scores(0)
            for h in range(heads):
                if h + 1 < heads:
                    scores(h + 1)
                now = h % 2
                cols = slice(h * step, (h + 1) * step)
                lse = lse_ref[h : h + 1, at]
                inner = inner_ref[h : h + 1, at]
                for r in range(0, seq, chunk):
                    p = jnp.exp(s_ref[now, r : r + chunk, :] - lse)
                    ds = p * (g_ref[now, r : r + chunk, :] - inner)
                    p_ref[r : r + chunk, cols] = p.astype(BF)
                    ds_ref[r : r + chunk, cols] = ds.astype(BF)
                rows = slice(h * size, (h + 1) * size)
                dqt_ref[rows, at] = dot(kt_ref[rows, :], ds_ref[:, cols]) * score
            dv = dot(p_ref[...], jnp.concatenate([head_cols(do, h, size) for h in range(heads)], 0))
            dk = dot(ds_ref[...], jnp.concatenate([head_cols(q, h, size) for h in range(heads)], 0))

            @pl.when(i == 0)
            def _():
                dv_ref[...] = dv
                dk_ref[...] = dk

            @pl.when(i > 0)
            def _():
                dv_ref[...] += dv
                dk_ref[...] += dk

            return carry

        lax.fori_loop(0, seq // step, one, 0)
        for c in range(chips):
            rows = slice(c * span, (c + 1) * span)
            out = dqkv_refs[c]
            out[:, :width] = dqt_ref[:, rows].T.astype(BF)
            out[:, width : 2 * width] = dk_ref[rows, :].astype(BF)
            out[:, 2 * width :] = dv_ref[rows, :].astype(BF)
            sums = jnp.sum(out[...].astype(F32), axis=0, keepdims=True)
            if c == 0:
                sum_ref[...] = sums
            else:
                sum_ref[...] += sums
            for b in range(2):
                part_refs[2 * c + b][...] = dot_bt(
                    out[b * half : (b + 1) * half, :], w_ref[:, : 3 * width]
                ).astype(BF)

    flat = [g for pair in datt for g in pair]
    out_shape = (
        [sds((span, 3 * width), BF)] * chips
        + [sds((half, model), BF)] * (2 * chips)
        + [sds((1, 3 * width), F32)]
    )
    operands = (*map(late, (*packed, *heads_kept)), lse, *flat, late(weight))
    out = pl.pallas_call(
        body,
        grid=(1,),
        in_specs=[whole(a.shape) for a in operands],
        out_specs=[whole(a.shape) for a in out_shape],
        out_shape=out_shape,
        scratch_shapes=[
            pltpu.VMEM((seq, width), BF),
            pltpu.VMEM((seq, width), BF),
            pltpu.VMEM((width, seq), BF),
            pltpu.VMEM((width, seq), BF),
            pltpu.VMEM((seq, width), BF),
            pltpu.VMEM((seq, width), BF),
            pltpu.VMEM((width, seq), BF),
            pltpu.VMEM((heads, seq), F32),
            pltpu.VMEM((2, seq, step), F32),
            pltpu.VMEM((2, seq, step), F32),
            pltpu.VMEM((seq, heads * step), BF),
            pltpu.VMEM((seq, heads * step), BF),
            pltpu.VMEM((seq, width), F32),
            pltpu.VMEM((seq, width), F32),
            pltpu.VMEM((width, seq), F32),
        ],
        compiler_params=params(26, 1),
        cost_estimate=cost(15),
        name="attention_back",
    )(*operands)
    parts = out[chips : 3 * chips]
    return (
        out[:chips],
        [(parts[2 * c], parts[2 * c + 1]) for c in range(chips)],
        out[3 * chips],
    )


def gelu_both(x):
    away = jnp.abs(x)
    t = 1.0 / (1.0 + (0.3275911 * 0.5**0.5) * away)
    bell = jnp.exp(-0.5 * (x * x))
    poly = t * (
        0.127414796
        + t * (-0.142248368 + t * (0.7107068705 + t * (-0.7265760135 + t * 0.5307027145)))
    )
    tail = poly * bell
    phi = jnp.where(x >= 0, 1.0 - tail, tail)
    return x * phi, phi + x * (bell * 0.3989422804014327)


def mlp_call(body, pairs, extra, weight, bias, outs, parts, scratch, name):
    rows, model = pairs[0].shape
    units = weight.shape[1] // 2
    step = min(256, units)
    blocks = units // step
    cols = lambda j: (0, j)
    in_specs = [whole((rows, model)) for _ in pairs]
    in_specs += [pl.BlockSpec((2 * rows, step), cols) for _ in extra]
    in_specs += [
        pl.BlockSpec((model, step), cols),
        pl.BlockSpec((model, step), lambda j: (0, blocks + j)),
        pl.BlockSpec((1, step), cols),
    ]
    out_specs = [pl.BlockSpec((2 * rows, step), cols) for _ in outs]
    out_specs += [pl.BlockSpec((1, step), cols)]
    out_specs += [whole((rows, model))] * (2 * parts)
    out_shape = [pltpu.HBM((2 * rows, units), d) for d in outs] + [sds((1, units), F32)]
    out_shape += [sds((rows, model), BF)] * (2 * parts)
    count = len(pairs) // 2
    return pl.pallas_call(
        body,
        grid=(blocks,),
        in_specs=in_specs,
        out_specs=out_specs,
        out_shape=out_shape,
        scratch_shapes=[pltpu.VMEM((2 * rows, model), F32)] * parts
        + [pltpu.VMEM((2 * rows, step), F32)] * scratch,
        compiler_params=params(8 + 5 * parts, 1),
        cost_estimate=cost(3 + 3 * parts),
        name=name,
    )(*pairs, *map(late, extra), weight, weight, bias)


def clear(*refs):
    @pl.when(pl.program_id(0) == 0)
    def _():
        for ref in refs:
            ref[...] = jnp.zeros_like(ref)


def finish(acc, low, high):
    rows = low.shape[0]

    @pl.when(pl.program_id(0) == pl.num_programs(0) - 1)
    def _():
        low[...] = acc[:rows, :].astype(BF)
        high[...] = acc[rows:, :].astype(BF)


CHUNK = 32


def mlp_forward(pair, weight, bias):
    rows = pair[0].shape[0]

    def body(a, b, w1_ref, w2_ref, bias_ref, act_ref, slope_ref, sum_ref, lo, hi, acc, pre):
        clear(acc, sum_ref)
        shift = bias_ref[...]
        for i, x in enumerate((a, b)):
            pre[i * rows : (i + 1) * rows, :] = dot(x[...], w1_ref[...])
        for i in range(2):
            at = slice(i * rows, (i + 1) * rows)
            for r in range(i * rows, (i + 1) * rows, CHUNK):
                act, slope = gelu_both(pre[r : r + CHUNK, :] + shift)
                act_ref[r : r + CHUNK, :] = act.astype(BF)
                slope_ref[r : r + CHUNK, :] = slope.astype(BF)
            acc[at, :] += dot_bt(act_ref[at, :], w2_ref[...])
        finish(acc, lo, hi)

    act, slope, _, lo, hi = mlp_call(body, pair, [], weight, bias, [BF, BF], 1, 1, "mlp_forward")
    return act, slope, (lo, hi)


def mlp_backward(pair, slope, weight, bias):
    rows = pair[0].shape[0]

    def body(a, b, slope_ref, w1_ref, w2_ref, bias_ref, dpre_ref, sum_ref, lo, hi, acc, pre):
        clear(acc)
        for i, g in enumerate((a, b)):
            pre[i * rows : (i + 1) * rows, :] = dot(g[...], w2_ref[...])
        sums = jnp.zeros((8, bias_ref.shape[1]), F32)
        for i in range(2):
            at = slice(i * rows, (i + 1) * rows)
            for r in range(i * rows, (i + 1) * rows, CHUNK):
                d = pre[r : r + CHUNK, :] * slope_ref[r : r + CHUNK, :].astype(F32)
                d = d.astype(BF)
                dpre_ref[r : r + CHUNK, :] = d
                sums = sums + fold(d.astype(F32), jnp.sum)
            acc[at, :] += dot_bt(dpre_ref[at, :], w1_ref[...])
        sum_ref[...] = jnp.sum(sums, axis=0, keepdims=True)
        finish(acc, lo, hi)

    dpre, sums, lo, hi = mlp_call(
        body, pair, [slope], weight, bias, [BF], 1, 1, "mlp_backward"
    )
    return dpre, sums, (lo, hi)


def mlp_both(pair, grads, weight, bias):
    rows = pair[0].shape[0]

    def body(
        a, b, c, d, w1_ref, w2_ref, bias_ref, act_ref, dpre_ref, sum_ref,
        lo, hi, blo, bhi, acc, back, pre, grad,
    ):
        clear(acc, back)
        shift = bias_ref[...]
        for i, (x, g) in enumerate(((a, c), (b, d))):
            at = slice(i * rows, (i + 1) * rows)
            pre[at, :] = dot(x[...], w1_ref[...])
            grad[at, :] = dot(g[...], w2_ref[...])
        sums = jnp.zeros((8, bias_ref.shape[1]), F32)
        for i in range(2):
            at = slice(i * rows, (i + 1) * rows)
            for r in range(i * rows, (i + 1) * rows, CHUNK):
                act, slope = gelu_both(pre[r : r + CHUNK, :] + shift)
                act_ref[r : r + CHUNK, :] = act.astype(BF)
                dpre = (grad[r : r + CHUNK, :] * slope).astype(BF)
                dpre_ref[r : r + CHUNK, :] = dpre
                sums = sums + fold(dpre.astype(F32), jnp.sum)
            back[at, :] += dot_bt(dpre_ref[at, :], w1_ref[...])
            acc[at, :] += dot_bt(act_ref[at, :], w2_ref[...])
        sum_ref[...] = jnp.sum(sums, axis=0, keepdims=True)
        finish(acc, lo, hi)
        finish(back, blo, bhi)

    act, dpre, sums, lo, hi, blo, bhi = mlp_call(
        body, [*pair, *grads], [], weight, bias, [BF, BF], 2, 2, "mlp_both"
    )
    return act, dpre, sums, (lo, hi), (blo, bhi)


def weight_grads(products, dp, side, name):
    model = products[0][0][0].shape[1]
    step = model // dp
    half = step // 2
    sizes = [(len(left), len(right), right[0].shape[1]) for left, right in products]
    cols = sum(n for _, _, n in sizes)

    def body(side_ref, *refs):
        mine, other, acc_ref = refs[-3:]
        at = base = 0
        for many, few, n in sizes:
            lefts, rights = refs[at : at + many], refs[at + many : at + many + few]
            at += many + few
            ratio = many // few
            acc = None
            for i in range(many):
                size = lefts[i].shape[0]
                here = slice((i % ratio) * size, (i % ratio + 1) * size)
                term = dot_at(lefts[i][...], rights[i // ratio][here, :])
                acc = term if acc is None else acc + term
            acc_ref[:, base : base + n] = acc
            base += n
        low = pl.multiple_of(side_ref[0] * half, half)
        high = pl.multiple_of((1 - side_ref[0]) * half, half)
        mine[...] = acc_ref[pl.ds(low, half), :].astype(BF)
        other[...] = acc_ref[pl.ds(high, half), :].astype(BF)

    specs, operands = [pl.BlockSpec(memory_space=pltpu.SMEM)], [side.reshape(1)]
    for left, right in products:
        specs += [pl.BlockSpec((a.shape[0], step), lambda i: (0, i)) for a in left]
        specs += [whole(b.shape) for b in right]
        operands += [*left, *right]
    return pl.pallas_call(
        body,
        grid=(dp,),
        in_specs=specs,
        out_specs=[pl.BlockSpec((half, cols), lambda i: (i, 0))] * 2,
        out_shape=[sds((dp * half, cols), BF)] * 2,
        scratch_shapes=[pltpu.VMEM((step, cols), F32)],
        compiler_params=params(14, 1),
        cost_estimate=cost(5),
        name=name,
    )(*operands)


def pieces(chunks):
    return [p for pair in chunks for p in pair]


def shards(
    tokens, cotangent, ln1_gain, ln1_bias, w_qkv, qv_bias, w_out, out_bias, scale_attn,
    ln2_gain, ln2_bias, w_fc1, fc1_bias, w_fc2, fc2_bias, scale_mlp,
):
    side = lax.axis_index("section")
    first = side == 0
    dp = lax.axis_size("dp")
    here = lax.axis_index("dp")
    chips = lax.axis_size("tensor") // 2
    rows, model = tokens.shape[2:]
    heads = qv_bias.shape[1]
    size = qv_bias.shape[2] * dp // 2
    width = heads * size
    units = w_fc1.shape[2]
    part = model // dp

    x0 = lax.dynamic_index_in_dim(tokens, side, 0, keepdims=False).reshape(rows, model)
    grad_top = lax.dynamic_index_in_dim(cotangent, side, 0, keepdims=False).reshape(rows, model)

    vectors = (ln1_gain, ln1_bias, out_bias, scale_attn, ln2_gain, ln2_bias, fc2_bias, scale_mlp)
    packed = jnp.concatenate(
        [v.reshape(-1) for v in vectors] + [fc1_bias.reshape(-1), qv_bias.reshape(-1)]
    )
    own_qkv = w_qkv.reshape(part, heads, 3, size).swapaxes(1, 2).reshape(part, 3 * width)
    own_att = jnp.concatenate([own_qkv, w_out[0].T], axis=1)
    own_ff = jnp.concatenate([w_fc1[0], w_fc2[0].T], axis=1)

    def halves(own, came, rest):
        mine, left = half_of(own, side), half_of(own, 1 - side)
        return (
            (jnp.where(first, mine, came), jnp.where(first, left, rest)),
            (jnp.where(first, came, mine), jnp.where(first, rest, left)),
        )

    came_att = swap_section(half_of(own_att, 1 - side))
    ring_att0 = jnp.where(first, half_of(own_att, side), came_att)
    small = gather_small(packed, first, ring_att0).astype(F32)
    cut = 8 * part
    vecs = small[:, :, :cut].reshape(2, dp, 8, part).swapaxes(1, 2).reshape(2, 8, model)
    bias_fc1 = small[:, :, cut : cut + units // dp].reshape(2, 1, units)
    qv = small[:, :, cut + units // dp :].reshape(2, dp, heads, -1).swapaxes(1, 2)
    qv = qv.reshape(2, heads, 2, size)
    bias_qkv = jnp.stack([qv[:, :, 0], jnp.zeros_like(qv[:, :, 0]), qv[:, :, 1]], axis=1)
    bias_qkv = bias_qkv.reshape(2, 1, 3 * width)
    vecs = (vecs[0], vecs[1])

    norm1 = norm_first(tie(x0, came_att), vecs[0])
    came_ff = swap_section(tie(half_of(own_ff, 1 - side), came_att))
    rest_att = swap_section(tie(half_of(own_att, side), came_att))
    half_att0, half_att1 = halves(own_att, came_att, rest_att)
    ring_ff0 = jnp.where(first, half_of(own_ff, side), came_ff)

    def put_together(half, hops, backs):
        return assemble([half, *zip(hops, backs)], model)

    hops_att0 = direct(ring_att0)
    att0 = put_together(half_att0, hops_att0, [swap_section(tie(v, norm1)) for v in hops_att0])
    ff0, att1 = Ring(tie(ring_ff0, hops_att0[-1])), Ring(half_att1[0])
    hop_ff0 = ff0.hop()
    rest_ff = swap_section(tie(half_of(own_ff, side), hop_ff0[-1]))
    half_ff0, half_ff1 = halves(own_ff, came_ff, rest_ff)
    ff1 = Ring(half_ff1[0])

    def projection(weight, s):
        return lambda pair: project_qkv(pair, weight, bias_qkv[s])

    def under(parts, beside):
        return [parts[0], *[(same, tie(other, *beside)) for same, other in parts[1:]]]

    chunks0, qkv0 = gather_tokens(norm1, projection(att0, 0))
    beside = [*ff0.hop(qkv0[-1]), *ff0.back(qkv0[-1])]
    kept0, lse0, parts = attention([*qkv0[:-1], tie(qkv0[-1], *hop_ff0)], att0, size)
    gate = parts[-1][0]
    parts = under(parts, beside)
    beside = [*ff0.hop(gate), *ff0.back(gate), *att1.hop(gate)]
    terms, _ = scatter_tokens(parts, beside=beside)
    attended0, residual0, norm2 = after_attention(x0, terms, vecs[0])
    beside = [*att1.hop(norm2)]
    ff0.back(norm2)
    w_ff0 = put_together(half_ff0, ff0.hops, ff0.backs)
    second0, mlp0 = gather_tokens(
        norm2, lambda pair: mlp_forward(pair, w_ff0, bias_fc1[0]), beside
    )
    gate = mlp0[-1][2][0]
    beside = [*att1.hop(gate), *att1.back(gate), *att1.back(gate), *ff1.hop(gate)]
    terms, _ = scatter_tokens([m[2] for m in mlp0], beside=beside)
    mlp_out0, y0, norm1 = after_mlp(residual0, terms, vecs[0], vecs[1])

    att1.back(norm1)
    w_att1 = put_together(half_att1, att1.hops, att1.backs)
    low1, sums_fc2_1 = start_back(grad_top, vecs[1])
    beside = [*ff1.hop(norm1), *ff1.back(norm1)]
    chunks1, qkv1 = gather_tokens(norm1, projection(w_att1, 1), beside)
    gate = qkv1[-1]
    grads1, _ = gather_tokens(tie(low1, gate), lambda pair: pair[0])
    beside = [*pieces(grads1), *ff1.hop(gate), *ff1.back(gate)]
    kept1, lse1, parts = attention(qkv1, w_att1, size)
    gate = parts[-1][0]
    beside_next = ff1.back(gate)
    terms, _ = scatter_tokens(under(parts, beside), beside=beside_next)
    attended1, residual1, norm2 = after_attention(y0, terms, vecs[1])
    w_ff1 = put_together(half_ff1, ff1.hops, ff1.backs)
    spare = list(grads1)
    second1, mlp1 = gather_tokens(
        norm2, lambda pair: mlp_both(pair, spare.pop(0), w_ff1, bias_fc1[1])
    )
    act1, dpre1, sums_fc1_1, parts_y1, parts_back1 = zip(*mlp1)

    def grad_ff(second, dpre, grads, act):
        return lambda after: weight_grads(
            [
                (pieces(second), [late(tie(dpre[0], after)), *map(late, dpre[1:])]),
                (pieces(grads), [late(a) for a in act]),
            ],
            dp,
            side,
            "grad_ff",
        )

    def grad_att(chunks, dqkv, datt, kept):
        return lambda after: weight_grads(
            [
                (pieces(chunks), [tie(dqkv[0], after), *dqkv[1:]]),
                (pieces(datt), [late(a) for a in kept]),
            ],
            dp,
            side,
            "grad_att",
        )

    came_y0 = lax.ppermute(tie(y0, parts_back1[-1][0]), "section", [(1, 0)])
    sums_y1 = core_sums(parts_y1)
    local_y1 = [parts_y1[0][0], core_swap(parts_y1[0][1])]
    old = [tuple(map(late, pair)) for pair in grads1]
    terms, g = scatter_tokens(parts_back1, grad_ff(second1, dpre1, old, act1), [came_y0])
    sum_ff1 = RingSum(*g, (0, 1))
    beside = sum_ff1.step()
    dres1, low, sums1 = back_second(grad_top, residual1, attended1, terms, vecs[1])
    datt, _ = gather_tokens(low, lambda pair: pair[0], beside)
    gate = datt[-1][0]
    terms_y1 = send_sums([tie(v, gate) for v in sums_y1])
    beside = [*terms_y1, *sum_ff1.step(gate)]
    dqkv, parts, qkv_sums1 = attention_back(qkv1, kept1, lse1, datt, w_att1, size)
    gate = parts[-1][0]
    y1, sums_sc_1 = last_output(
        residual1, [tie(local_y1[0], gate), local_y1[1], *terms_y1], grad_top, vecs[1]
    )
    came_y1 = lax.ppermute(y1, "section", [(0, 1)])
    beside_next = sum_ff1.step(gate)
    old = [tuple(map(late, pair)) for pair in chunks1]
    terms, g = scatter_tokens(
        under(parts, beside), grad_att(old, dqkv, datt, kept1), beside_next
    )
    sum_att1 = RingSum(*g, (0, 1))
    dx1, low0, edge1 = back_first(dres1, late(y0), terms, vecs[1], late(mlp_out0), vecs[0])

    beside = [came_y1, *sum_ff1.step(low0), *sum_att1.step(low0)]
    slopes = [m[1] for m in mlp0]
    grads0, mlp_back0 = gather_tokens(
        low0, lambda pair: mlp_backward(pair, slopes.pop(0), w_ff0, bias_fc1[0]), beside
    )
    dpre0, sums_fc1_0, parts = zip(*mlp_back0)
    gate = parts[-1][0]
    beside = [*sum_ff1.step(gate), *sum_att1.step(gate)]
    old = [tuple(map(late, pair)) for pair in second0]
    terms, g = scatter_tokens(
        parts, grad_ff(old, dpre0, grads0, [m[0] for m in mlp0]), beside
    )
    sum_ff0 = RingSum(*g, (1, 0))
    dres0, low, sums0 = back_second(
        dx1, late(residual0), late(attended0), terms, vecs[0]
    )
    beside = [*sum_att1.step(low), *sum_ff0.step(low)]
    datt, _ = gather_tokens(low, lambda pair: pair[0], beside)
    gate = datt[-1][0]
    beside = [*sum_att1.step(gate), *sum_ff0.step(gate)]
    dqkv, parts, qkv_sums0 = attention_back(qkv0, kept0, lse0, datt, att0, size)
    gate = parts[-1][0]
    beside_next = [*sum_att1.step(gate), *sum_ff0.step(gate)]
    old = [tuple(map(late, pair)) for pair in chunks0]
    terms, g = scatter_tokens(
        under(parts, beside), grad_att(old, dqkv, datt, kept0), beside_next
    )
    sum_att0 = RingSum(*g, (1, 0))
    going = sum_att0.step()
    dx0, edge0 = back_first(dres0, x0, terms, vecs[0])
    sum_att0.step(dx0)
    sum_ff0.step(dx0)
    came_dx1 = lax.ppermute(tie(dx1, dx0), "section", [(0, 1)])
    sum_att0.step(), sum_ff0.step(), sum_att0.step(), sum_att0.step()

    def both(low, high, came_low, came_high):
        mine = jnp.where(first, low, high)
        came = jnp.where(first, came_low, came_high)
        return jnp.stack([jnp.where(first, mine, came), jnp.where(first, came, mine)])[None, :, None]

    block_out = both(y0, y1, came_y0, came_y1)
    input_grads = both(dx0, dx1, lax.ppermute(dx0, "section", [(1, 0)]), came_dx1)

    def to_owner(low, high, pick):
        own = jnp.where(first, low, high) + swap_section(jnp.where(first, high, low))
        out = pick(own, here)
        for step in range(1, dp):
            pairs = [(i, (i + step) % dp) for i in range(dp)]
            out = out + lax.ppermute(pick(own, lax.rem(here + step, dp)), "dp", pairs)
        return out

    def by_unit(qkv_sums, unit_sums):
        q = qkv_sums[:, :width].reshape(heads, 1, size)
        v = qkv_sums[:, 2 * width :].reshape(heads, 1, size)
        bias = jnp.concatenate([q, v], 1).reshape(heads, dp, -1).swapaxes(0, 1).reshape(dp, -1)
        return jnp.concatenate([bias, unit_sums.reshape(dp, -1)], axis=1)

    unit = to_owner(
        by_unit(tie(qkv_sums0, dx0), sum(sums_fc1_0)),
        by_unit(qkv_sums1, sum(sums_fc1_1)),
        lambda v, place: lax.dynamic_slice_in_dim(v, place, 1, 0),
    )
    cut = heads * (2 * size // dp)
    bias_grad = unit[:, :cut].reshape(1, heads, -1)
    fc1_grad = unit[:, cut:].reshape(1, 1, -1)

    vec = jnp.concatenate(
        [edge0[:2], sums0[:4], edge1[2:4], edge1[:2], sums1[:4], sums_sc_1[:1], sums_fc2_1[:1]]
    )
    vec = vec + core_swap(vec)
    vec = tie(sum([from_chip(vec, step) for step in range(1, chips)], vec), *going)
    vec = to_owner(
        vec[:8], vec[8:], lambda v, place: lax.dynamic_slice_in_dim(v, place * part, part, 1)
    )
    g_ln1, b_ln1, g_ln2, b_ln2, g_sc_attn, g_out_bias, g_sc_mlp, g_fc2_bias = (
        vec[i : i + 1] for i in range(8)
    )

    def owned(low, high):
        top = jnp.where(first, low.going, high.came.astype(F32))
        bottom = jnp.where(first, low.came.astype(F32), high.going)
        return jnp.concatenate([top, bottom], 0)

    g_ff, g_att = owned(sum_ff0, sum_ff1), owned(sum_att0, sum_att1)
    g_qkv = g_att[:, : 3 * width].reshape(part, 3, heads, size).swapaxes(1, 2)
    g_qkv = g_qkv.reshape(1, part, 3 * width)
    g_out = g_att[:, 3 * width :].T[None]
    g_fc1 = g_ff[:, :units][None]
    g_fc2 = g_ff[:, units:].T[None]
    return (
        block_out, input_grads, g_ln1, b_ln1, g_qkv, bias_grad, g_out, g_out_bias, g_sc_attn,
        g_ln2, b_ln2, g_fc1, fc1_grad, g_fc2, g_fc2_bias, g_sc_mlp,
    )


def solution(mesh):
    vec = P("section", "dp")
    by_row = P("section", "dp", "tensor")
    by_unit = P("section", "tensor", "dp")
    data = P(None, "dp", "tensor", None)
    split = P("section", None, "dp", "tensor", None)
    given = (
        vec, vec, by_row, by_unit, by_unit, vec, vec, vec, vec, by_row, by_unit, by_unit, vec, vec,
    )
    return jax.shard_map(
        shards,
        mesh=mesh,
        in_specs=(data, data) + given,
        out_specs=(split, split) + given,
        check_vma=False,
    )
```

```python
from functools import partial

import jax
import jax.numpy as jnp
from jax import lax
from jax.experimental import pallas as pl
from jax.experimental.pallas import tpu as pltpu
from jax.sharding import PartitionSpec as P

EPSILON = 1e-06
BF = jnp.bfloat16
F32 = jnp.float32
MIB = 1 << 20

LN1_G, LN1_B, OUT_B, SC_ATTN, LN2_G, LN2_B, FC2_B, SC_MLP = range(8)


def dot(a, b):
    return lax.dot_general(a, b, (((1,), (0,)), ((), ())), preferred_element_type=F32)


def dot_bt(a, b):
    return lax.dot_general(a, b, (((1,), (1,)), ((), ())), preferred_element_type=F32)


def dot_at(a, b):
    return lax.dot_general(a, b, (((0,), (0,)), ((), ())), preferred_element_type=F32)


def turn(v):
    return v.astype(F32).T


def params(limit, grid=0):
    return pltpu.CompilerParams(
        vmem_limit_bytes=limit * MIB,
        dimension_semantics=("arbitrary",) * grid if grid else None,
    )


def late(v):
    return pltpu.with_memory_space_constraint(v, pltpu.HBM)


def whole(shape):
    return pl.BlockSpec(shape, lambda i: (0, 0), pipeline_mode=pl.Buffered(1))


def cost(micros):
    return pl.CostEstimate(flops=int(micros * 1.15e9), bytes_accessed=0, transcendentals=0)


def sds(shape, dtype):
    return jax.ShapeDtypeStruct(shape, dtype)


def core_swap(v):
    count = lax.axis_size("tensor")
    return lax.ppermute(v, "tensor", [(i, i ^ 1) for i in range(count)])


def from_chip(v, step):
    count = lax.axis_size("tensor")
    chips = count // 2
    pairs = [(((i // 2 + step) % chips) * 2 + i % 2, i) for i in range(count)]
    return lax.ppermute(v, "tensor", pairs)


def tie(v, *after):
    if not after:
        return v
    return lax.optimization_barrier((v, *after))[0]


def tie_all(vs, *after):
    return lax.optimization_barrier((*vs, *after))[: len(vs)]


def gather_tokens(own, work, beside=()):
    chips = lax.axis_size("tensor") // 2
    came = [from_chip(own, step) for step in range(1, chips)]
    chunks = [(own, core_swap(own))]
    results = [work(chunks[0])]
    for same in came:
        same = tie(same, results[-1], *beside)
        chunks.append((same, core_swap(same)))
        results.append(work(chunks[-1]))
    return chunks, results


def core_sums(sames, others):
    chips, rows = len(sames), sames[0].shape[0]
    if isinstance(others, (list, tuple)):
        came = [core_swap(v) for v in others[1:]]
        local = core_swap(tie(others[0], came[-1]))
    else:
        local = core_swap(others)
        came = [local[c * rows : (c + 1) * rows] for c in range(1, chips)]
    sums = [(a.astype(F32) + b.astype(F32)).astype(BF) for a, b in zip(sames[1:], came)]
    return sums, local


def send_sums(sums):
    chips = len(sums) + 1
    return [from_chip(both, chips - step) for step, both in enumerate(sums, 1)]


def scatter_tokens(sames, others, work=None, beside=None):
    sums, local = core_sums(sames, others)
    terms = send_sums(sums)
    made = work(sums[-1]) if work else local
    more = beside(sums[-1]) if beside else ()
    terms = [tie(t, made, local, *more) for t in terms]
    return [sames[0], *terms, local], made


def swap_section(v):
    return lax.ppermute(v, "section", [(0, 1), (1, 0)])


def assemble(shards, rows):
    count = len(shards)
    cut = len(shards[0])
    size, cols = shards[0][0].shape
    place = jnp.stack([lax.axis_index("dp"), lax.axis_index("section")])

    def body(place_ref, *refs):
        out_ref, sems = refs[count * cut :]
        z, x = place_ref[0], place_ref[1]
        started = []
        for k in range(count):
            base = lax.rem(z + (count - k), count) * (cut * size)
            for i, at in enumerate([base] if cut == 1 else [base + x * size, base + (1 - x) * size]):
                copy = pltpu.make_async_copy(
                    refs[k * cut + i],
                    out_ref.at[pl.ds(pl.multiple_of(at, size), size), :],
                    sems.at[k * cut + i],
                )
                copy.start()
                started.append(copy)
        for copy in started:
            copy.wait()

    hbm = pl.BlockSpec(memory_space=pl.ANY)
    return pl.pallas_call(
        body,
        in_specs=[pl.BlockSpec(memory_space=pltpu.SMEM)] + [hbm] * (count * cut),
        out_specs=pl.BlockSpec(memory_space=pltpu.VMEM),
        out_shape=sds((rows, cols), shards[0][0].dtype),
        scratch_shapes=[pltpu.SemaphoreType.DMA((count * cut,))],
        compiler_params=params(6),
        cost_estimate=cost(2),
        name="assemble",
    )(place, *[v for shard in shards for v in shard])


def half_of(v, which):
    half = v.shape[0] // 2
    return lax.dynamic_slice_in_dim(v, which * half, half, 0)


def direct(own):
    count = lax.axis_size("dp")
    return [
        lax.ppermute(own, "dp", [(i, (i + step) % count) for i in range(count)])
        for step in range(1, count)
    ]


def third(values, index):
    cuts = [-(-len(values) * i // 3) for i in range(4)]
    return values[cuts[index] : cuts[index + 1]]


class Ring:
    def __init__(self, own):
        self.last, self.hops, self.backs, self.at, self.back_at = own, [], [], 0, 0

    def hop(self, *gate):
        count = lax.axis_size("dp")
        pairs = [(i, (i + 1) % count) for i in range(count)]
        new = []
        for i in range(len(third(range(count - 1), self.at))):
            self.last = lax.ppermute(tie(self.last, *gate) if i == 0 else self.last, "dp", pairs)
            new.append(self.last)
        self.hops += new
        self.at += 1
        return new

    def back(self, *gate):
        count = lax.axis_size("dp")
        which = third(range(count - 1), self.back_at)
        new = [swap_section(tie(self.hops[i], *gate)) for i in which]
        self.backs += new
        self.back_at += 1
        return new


def gather_small(v, first, after):
    count = lax.axis_size("dp")
    came = swap_section(v)
    own = tie(jnp.stack([jnp.where(first, v, came), jnp.where(first, came, v)]), after)
    ahead = [own]
    for step in range(1, count):
        ahead.append(lax.ppermute(own, "dp", [(i, (i - step) % count) for i in range(count)]))
    twice = jnp.stack(ahead + ahead, axis=1)
    return lax.dynamic_slice_in_dim(twice, count - lax.axis_index("dp"), count, 1)


def dp_rows(v, back):
    dp = lax.axis_size("dp")
    part = v.shape[0] // dp
    place = lax.rem(lax.axis_index("dp") + (dp - back), dp)
    return lax.dynamic_slice_in_dim(v, place * part, part, 0)


class RingSum:
    def __init__(self, pair, mine, other=None):
        self.mine, self.other, self.pair = mine, other, pair
        self.going, self.at, self.done = None, 0, 0

    def one(self, gate):
        dp = lax.axis_size("dp")
        self.done += 1
        new = []
        if self.going is not None:
            pairs = [(i, (i + 1) % dp) for i in range(dp)]
            new.append(lax.ppermute(tie(self.going, *gate), "dp", pairs))
        if self.other is not None:
            new.append(swap_section(tie(dp_rows(self.other, self.done), *gate)))
        self.going = sum(t.astype(F32) for t in [dp_rows(self.mine, self.done), *new])
        if self.done < dp:
            self.going = self.going.astype(BF)
        return new

    def step(self, *gate):
        self.at += 1
        if self.at == 5:
            self.came = lax.ppermute(tie(self.going.astype(BF), *gate), "section", [self.pair])
            return [self.came]
        count = 1 if self.at == 1 else len(third(range(lax.axis_size("dp") - 1), self.at - 2))
        return [v for i in range(count) for v in self.one(gate if i == 0 else ())]


def standardize(v):
    centred = v - jnp.mean(v, axis=-1, keepdims=True)
    var = jnp.mean(centred * centred, axis=-1, keepdims=True)
    scale = lax.rsqrt(var + EPSILON)
    return centred * scale, scale


def norm_of(v, vec, gain, shift):
    return (standardize(v)[0] * vec[gain : gain + 1, :] + vec[shift : shift + 1, :]).astype(BF)


def norm_back(v, grad, gain):
    xh, scale = standardize(v)
    dxh = grad * gain
    inner = jnp.mean(dxh * xh, axis=-1, keepdims=True)
    out = scale * (dxh - jnp.mean(dxh, axis=-1, keepdims=True) - xh * inner)
    return out, grad * xh


def total(refs):
    out = refs[0][...].astype(F32)
    for ref in refs[1:]:
        out = out + ref[...].astype(F32)
    return out


def fold(v, op):
    return op(v.reshape(-1, 8, v.shape[1]), axis=0)


def add_rows(ref, rows):
    for k, row in enumerate(rows):
        ref[8 * k : 8 * k + 8, :] += fold(row, jnp.sum)


def rowwise(body, row_ins, fulls, row_outs, sums, name):
    rows, width = row_ins[0].shape
    step = min(32, rows)
    many, some, outs = len(row_ins), len(fulls), len(row_outs)

    def kernel(*refs):
        in_refs, full_refs = refs[:many], refs[many : many + some]
        out_refs = refs[many + some : many + some + outs]
        extra = refs[many + some + outs :]
        if sums:
            extra[1][...] = jnp.zeros_like(extra[1])

        def one(i, carry):
            at = pl.ds(pl.multiple_of(i * step, step), step)
            body(
                *[r.at[at, :] for r in in_refs],
                *full_refs,
                *[r.at[at, :] for r in out_refs],
                *extra[1:],
            )
            return carry

        lax.fori_loop(0, rows // step, one, 0)
        for k in range(sums):
            extra[0][k : k + 1, :] = jnp.sum(
                extra[1][8 * k : 8 * k + 8, :], axis=0, keepdims=True
            )

    out_shape = [sds((rows, width), d) for d in row_outs]
    out_shape += [sds((sums, width), F32)] if sums else []
    return pl.pallas_call(
        kernel,
        grid=(1,),
        in_specs=[whole((rows, width)) for _ in row_ins] + [whole(a.shape) for a in fulls],
        out_specs=[whole(a.shape) for a in out_shape],
        out_shape=out_shape,
        scratch_shapes=[pltpu.VMEM((8 * sums, width), F32)] if sums else [],
        compiler_params=params(8, 1),
        cost_estimate=cost(2),
        name=name,
    )(*row_ins, *fulls)


def norm_first(x, vec):
    def body(x_ref, vec_ref, out_ref):
        out_ref[...] = norm_of(x_ref[...].astype(F32), vec_ref[...], LN1_G, LN1_B)

    return rowwise(body, [x], [vec], [BF], 0, "norm_first")[0]


def after_attention(x, terms, vec):
    count = len(terms)

    def body(*refs):
        x_ref, term_refs, vec_ref = refs[0], refs[1 : 1 + count], refs[1 + count]
        att_ref, res_ref, norm_ref = refs[2 + count :]
        v = vec_ref[...]
        attended = total(term_refs) + v[OUT_B : OUT_B + 1, :]
        residual = x_ref[...].astype(F32) + v[SC_ATTN : SC_ATTN + 1, :] * attended
        att_ref[...] = attended.astype(BF)
        res_ref[...] = residual
        norm_ref[...] = norm_of(residual, v, LN2_G, LN2_B)

    return rowwise(body, [x, *terms], [vec], [BF, F32, BF], 0, "after_attention")


def after_mlp(residual, terms, vec, vec_next):
    count = len(terms)

    def body(*refs):
        res_ref, term_refs = refs[0], refs[1 : 1 + count]
        vec_ref, next_ref, mlp_ref, y_ref, norm_ref = refs[1 + count :]
        v = vec_ref[...]
        mlp = total(term_refs) + v[FC2_B : FC2_B + 1, :]
        y = (res_ref[...] + v[SC_MLP : SC_MLP + 1, :] * mlp).astype(BF)
        mlp_ref[...] = mlp.astype(BF)
        y_ref[...] = y
        norm_ref[...] = norm_of(y.astype(F32), next_ref[...], LN1_G, LN1_B)

    return rowwise(body, [residual, *terms], [vec, vec_next], [BF, BF, BF], 0, "after_mlp")


def last_output(residual, terms, grad, vec):
    count = len(terms)

    def body(*refs):
        res_ref, term_refs = refs[0], refs[1 : 1 + count]
        grad_ref, vec_ref, y_ref, sum_ref = refs[1 + count :]
        v = vec_ref[...]
        mlp = total(term_refs) + v[FC2_B : FC2_B + 1, :]
        y_ref[...] = (res_ref[...] + v[SC_MLP : SC_MLP + 1, :] * mlp).astype(BF)
        add_rows(sum_ref, [grad_ref[...].astype(F32) * mlp])

    return rowwise(body, [residual, *terms, grad], [vec], [BF], 1, "last_output")


def start_back(grad, vec):
    def body(grad_ref, vec_ref, out_ref, sum_ref):
        low = (vec_ref[...][SC_MLP : SC_MLP + 1, :] * grad_ref[...].astype(F32)).astype(BF)
        out_ref[...] = low
        add_rows(sum_ref, [low.astype(F32)])

    return rowwise(body, [grad], [vec], [BF], 1, "start_back")


def back_second(grad, residual, attended, terms, vec):
    count = len(terms)

    def body(*refs):
        grad_ref, res_ref, att_ref = refs[:3]
        term_refs = refs[3 : 3 + count]
        vec_ref, dres_ref, low_ref, sum_ref = refs[3 + count :]
        v = vec_ref[...]
        dn = total(term_refs)
        back, dgain = norm_back(res_ref[...], dn, v[LN2_G : LN2_G + 1, :])
        dres = grad_ref[...].astype(F32) + back
        low = (v[SC_ATTN : SC_ATTN + 1, :] * dres).astype(BF)
        dres_ref[...] = dres
        low_ref[...] = low
        add_rows(sum_ref, [dgain, dn, dres * att_ref[...].astype(F32), low.astype(F32)])

    return rowwise(
        body, [grad, residual, attended, *terms], [vec], [F32, BF], 4, "back_second"
    )


def back_first(dres, x, terms, vec, mlp_below=None, vec_below=None):
    count = len(terms)
    below = mlp_below is not None

    def body(*refs):
        dres_ref, x_ref = refs[:2]
        term_refs = refs[2 : 2 + count]
        rest = refs[2 + count :]
        if below:
            mlp_ref, vec_ref, under_ref, dx_ref, low_ref, sum_ref = rest
        else:
            vec_ref, dx_ref, sum_ref = rest
        v = vec_ref[...]
        dn = total(term_refs)
        back, dgain = norm_back(x_ref[...].astype(F32), dn, v[LN1_G : LN1_G + 1, :])
        dx = (dres_ref[...] + back).astype(BF)
        dx_ref[...] = dx
        rows = [dgain, dn]
        if below:
            wide = dx.astype(F32)
            low = (under_ref[...][SC_MLP : SC_MLP + 1, :] * wide).astype(BF)
            low_ref[...] = low
            rows += [wide * mlp_ref[...].astype(F32), low.astype(F32)]
        add_rows(sum_ref, rows)

    row_ins = [dres, x, *terms] + ([mlp_below] if below else [])
    fulls = [vec] + ([vec_below] if below else [])
    return rowwise(body, row_ins, fulls, [BF, BF] if below else [BF], 4 if below else 2, "back_first")


def project_qkv(pair, weight, bias):
    rows, width = pair[0].shape
    cols = bias.shape[1]

    def body(a_ref, b_ref, w_ref, bias_ref, out_ref):
        w = w_ref[...]
        shift = bias_ref[...]
        out_ref[:rows, :] = (dot(a_ref[...], w) + shift).astype(BF)
        out_ref[rows:, :] = (dot(b_ref[...], w) + shift).astype(BF)

    return pl.pallas_call(
        body,
        grid=(1,),
        in_specs=[
            whole((rows, width)), whole((rows, width)), whole((width, cols)), whole((1, cols))
        ],
        out_specs=whole((2 * rows, cols)),
        out_shape=sds((2 * rows, cols), BF),
        compiler_params=params(6, 1),
        cost_estimate=cost(2),
        name="project_qkv",
    )(*pair, weight, bias)


def head_rows(v, head, size):
    rows = lax.broadcasted_iota(jnp.int32, v.shape, 0)
    return jnp.where(rows // size == head, v, jnp.zeros_like(v))


def head_cols(v, head, size):
    cols = lax.broadcasted_iota(jnp.int32, v.shape, 1)
    return jnp.where(cols // size == head, v, jnp.zeros_like(v))


def attention(packed, weight, size):
    chips = len(packed)
    span = packed[0].shape[0]
    half = span // 2
    width = packed[0].shape[1] // 3
    seq = chips * span
    heads = width // size
    model = weight.shape[0]
    step = min(256, seq)
    chunk = min(128, seq)
    score = size**-0.5

    def body(*refs):
        in_refs, w_ref = refs[:chips], refs[chips]
        head_refs = refs[chips + 1 : 2 * chips + 1]
        lse_ref = refs[2 * chips + 1]
        same_refs, other_ref = refs[2 * chips + 2 : 3 * chips + 2], refs[3 * chips + 2]
        k_ref, qt_ref, vt_ref, ot_ref, s_ref, p_ref = refs[3 * chips + 3 :]
        for c in range(chips):
            at = slice(c * span, (c + 1) * span)
            k_ref[at, :] = in_refs[c][:, width : 2 * width]
            qt_ref[:, at] = (turn(in_refs[c][:, :width]) * score).astype(BF)
            vt_ref[:, at] = turn(in_refs[c][:, 2 * width :]).astype(BF)

        def one(i, carry):
            at = pl.ds(pl.multiple_of(i * step, step), step)
            q = qt_ref[:, at]
            s_ref[0] = dot(k_ref[...], head_rows(q, 0, size))
            for h in range(heads):
                if h + 1 < heads:
                    s_ref[(h + 1) % 2] = dot(k_ref[...], head_rows(q, h + 1, size))
                now = h % 2
                top = fold(s_ref[now, :chunk, :], jnp.max)
                for r in range(chunk, seq, chunk):
                    top = jnp.maximum(top, fold(s_ref[now, r : r + chunk, :], jnp.max))
                top = jnp.max(top, axis=0, keepdims=True)
                norm = jnp.zeros((8, step), F32)
                for r in range(0, seq, chunk):
                    p = jnp.exp(s_ref[now, r : r + chunk, :] - top)
                    norm = norm + fold(p, jnp.sum)
                    p_ref[now, r : r + chunk, :] = p.astype(BF)
                norm = jnp.sum(norm, axis=0, keepdims=True)
                rows = slice(h * size, (h + 1) * size)
                ot_ref[rows, at] = dot(vt_ref[rows, :], p_ref[now]) / norm
                lse_ref[h : h + 1, at] = top + jnp.log(norm)
            return carry

        lax.fori_loop(0, seq // step, one, 0)
        for c in range(chips):
            at = slice(c * span, (c + 1) * span)
            o = ot_ref[:, at].T.astype(BF)
            head_refs[c][...] = o
            same_refs[c][...] = dot_bt(o[:half], w_ref[...]).astype(BF)
            other_ref[c * half : (c + 1) * half, :] = dot_bt(o[half:], w_ref[...]).astype(BF)

    out = pl.pallas_call(
        body,
        grid=(1,),
        in_specs=[whole((span, 3 * width))] * chips
        + [pl.BlockSpec((model, width), lambda i: (0, 3), pipeline_mode=pl.Buffered(1))],
        out_specs=[whole((span, width))] * chips
        + [whole((heads, seq))]
        + [whole((half, model))] * chips
        + [whole((seq // 2, model))],
        out_shape=[pltpu.HBM((span, width), BF)] * chips
        + [sds((heads, seq), F32)]
        + [sds((half, model), BF)] * chips
        + [sds((seq // 2, model), BF)],
        scratch_shapes=[
            pltpu.VMEM((seq, width), BF),
            pltpu.VMEM((width, seq), BF),
            pltpu.VMEM((width, seq), BF),
            pltpu.VMEM((width, seq), F32),
            pltpu.VMEM((2, seq, step), F32),
            pltpu.VMEM((2, seq, step), BF),
        ],
        compiler_params=params(14, 1),
        cost_estimate=cost(9),
        name="attention",
    )(*packed, weight)
    return out[:chips], out[chips], out[chips + 1 : -1], out[-1]


def attention_back(packed, heads_kept, lse, datt, weight, size):
    chips = len(packed)
    span = packed[0].shape[0]
    half = span // 2
    width = packed[0].shape[1] // 3
    seq = chips * span
    heads = width // size
    model = weight.shape[0]
    step = min(256, seq)
    chunk = min(128, seq)
    score = size**-0.5

    def body(*refs):
        at = 0

        def take(count):
            nonlocal at
            at += count
            return refs[at - count : at]

        in_refs, kept_refs = take(chips), take(chips)
        (lse_ref,) = take(1)
        datt_refs = take(2 * chips)
        (w_ref,) = take(1)
        dqkv_refs = take(chips)
        same_refs = take(chips)
        other_ref, sum_ref = take(2)
        k_ref, v_ref, kt_ref, qt_ref, q_ref, do_ref, dot_ref = take(7)
        inner_ref, s_ref, g_ref, p_ref, ds_ref, dk_ref, dv_ref, dqt_ref = take(8)
        for c in range(chips):
            rows = slice(c * span, (c + 1) * span)
            q = in_refs[c][:, :width].astype(F32) * score
            k = in_refs[c][:, width : 2 * width]
            q_ref[rows, :] = q.astype(BF)
            qt_ref[:, rows] = q.T.astype(BF)
            k_ref[rows, :] = k
            kt_ref[:, rows] = turn(k).astype(BF)
            v_ref[rows, :] = in_refs[c][:, 2 * width :]
            for b in range(2):
                d = dot(datt_refs[2 * c + b][...], w_ref[:, 3 * width :]).astype(BF)
                here = slice(c * span + b * half, c * span + (b + 1) * half)
                do_ref[here, :] = d
                dt = turn(d)
                dot_ref[:, here] = dt.astype(BF)
                prod = dt * turn(kept_refs[c][b * half : (b + 1) * half, :])
                for h in range(heads):
                    inner_ref[h : h + 1, here] = jnp.sum(
                        prod[h * size : (h + 1) * size, :], axis=0, keepdims=True
                    )

        def one(i, carry):
            at = pl.ds(pl.multiple_of(i * step, step), step)
            qt = qt_ref[:, at]
            dot_t = dot_ref[:, at]
            q = q_ref[at, :]
            do = do_ref[at, :]

            def scores(h):
                s_ref[h % 2] = dot(k_ref[...], head_rows(qt, h, size))
                g_ref[h % 2] = dot(v_ref[...], head_rows(dot_t, h, size))

            scores(0)
            for h in range(heads):
                if h + 1 < heads:
                    scores(h + 1)
                now = h % 2
                cols = slice(h * step, (h + 1) * step)
                lse = lse_ref[h : h + 1, at]
                inner = inner_ref[h : h + 1, at]
                for r in range(0, seq, chunk):
                    p = jnp.exp(s_ref[now, r : r + chunk, :] - lse)
                    ds = p * (g_ref[now, r : r + chunk, :] - inner)
                    p_ref[r : r + chunk, cols] = p.astype(BF)
                    ds_ref[r : r + chunk, cols] = ds.astype(BF)
                rows = slice(h * size, (h + 1) * size)
                dqt_ref[rows, at] = dot(kt_ref[rows, :], ds_ref[:, cols]) * score
            dv = dot(p_ref[...], jnp.concatenate([head_cols(do, h, size) for h in range(heads)], 0))
            dk = dot(ds_ref[...], jnp.concatenate([head_cols(q, h, size) for h in range(heads)], 0))

            @pl.when(i == 0)
            def _():
                dv_ref[...] = dv
                dk_ref[...] = dk

            @pl.when(i > 0)
            def _():
                dv_ref[...] += dv
                dk_ref[...] += dk

            return carry

        lax.fori_loop(0, seq // step, one, 0)
        for c in range(chips):
            rows = slice(c * span, (c + 1) * span)
            out = dqkv_refs[c]
            out[:, :width] = dqt_ref[:, rows].T.astype(BF)
            out[:, width : 2 * width] = dk_ref[rows, :].astype(BF)
            out[:, 2 * width :] = dv_ref[rows, :].astype(BF)
            sums = jnp.sum(out[...].astype(F32), axis=0, keepdims=True)
            if c == 0:
                sum_ref[...] = sums
            else:
                sum_ref[...] += sums
            w = w_ref[:, : 3 * width]
            same_refs[c][...] = dot_bt(out[:half, :], w).astype(BF)
            other_ref[c * half : (c + 1) * half, :] = dot_bt(out[half:, :], w).astype(BF)

    flat = [g for pair in datt for g in pair]
    out_shape = (
        [sds((span, 3 * width), BF)] * chips
        + [sds((half, model), BF)] * chips
        + [sds((seq // 2, model), BF), sds((1, 3 * width), F32)]
    )
    operands = (*map(late, (*packed, *heads_kept)), lse, *flat, late(weight))
    out = pl.pallas_call(
        body,
        grid=(1,),
        in_specs=[whole(a.shape) for a in operands],
        out_specs=[whole(a.shape) for a in out_shape],
        out_shape=out_shape,
        scratch_shapes=[
            pltpu.VMEM((seq, width), BF),
            pltpu.VMEM((seq, width), BF),
            pltpu.VMEM((width, seq), BF),
            pltpu.VMEM((width, seq), BF),
            pltpu.VMEM((seq, width), BF),
            pltpu.VMEM((seq, width), BF),
            pltpu.VMEM((width, seq), BF),
            pltpu.VMEM((heads, seq), F32),
            pltpu.VMEM((2, seq, step), F32),
            pltpu.VMEM((2, seq, step), F32),
            pltpu.VMEM((seq, heads * step), BF),
            pltpu.VMEM((seq, heads * step), BF),
            pltpu.VMEM((seq, width), F32),
            pltpu.VMEM((seq, width), F32),
            pltpu.VMEM((width, seq), F32),
        ],
        compiler_params=params(26, 1),
        cost_estimate=cost(15),
        name="attention_back",
    )(*operands)
    return out[:chips], out[chips : 2 * chips], out[2 * chips], out[2 * chips + 1]


def gelu_both(x):
    away = jnp.abs(x)
    t = 1.0 / (1.0 + (0.3275911 * 0.5**0.5) * away)
    bell = jnp.exp(-0.5 * (x * x))
    poly = t * (
        0.127414796
        + t * (-0.142248368 + t * (0.7107068705 + t * (-0.7265760135 + t * 0.5307027145)))
    )
    tail = poly * bell
    phi = jnp.where(x >= 0, 1.0 - tail, tail)
    return x * phi, phi + x * (bell * 0.3989422804014327)


def mlp_call(body, pairs, extra, weight, bias, outs, parts, scratch, name):
    rows, model = pairs[0].shape
    units = weight.shape[1] // 2
    step = min(256, units)
    blocks = units // step
    cols = lambda j: (0, j)
    in_specs = [whole((rows, model)) for _ in pairs]
    in_specs += [pl.BlockSpec((2 * rows, step), cols) for _ in extra]
    in_specs += [
        pl.BlockSpec((model, step), cols),
        pl.BlockSpec((model, step), lambda j: (0, blocks + j)),
        pl.BlockSpec((1, step), cols),
    ]
    out_specs = [pl.BlockSpec((2 * rows, step), cols) for _ in outs]
    out_specs += [pl.BlockSpec((1, step), cols)]
    out_specs += [whole((rows, model))] * (2 * parts)
    out_shape = [pltpu.HBM((2 * rows, units), d) for d in outs] + [sds((1, units), F32)]
    out_shape += [sds((rows, model), BF)] * (2 * parts)
    count = len(pairs) // 2
    return pl.pallas_call(
        body,
        grid=(blocks,),
        in_specs=in_specs,
        out_specs=out_specs,
        out_shape=out_shape,
        scratch_shapes=[pltpu.VMEM((2 * rows, model), F32)] * parts
        + [pltpu.VMEM((2 * rows, step), F32)] * scratch,
        compiler_params=params(8 + 5 * parts, 1),
        cost_estimate=cost(3 + 3 * parts),
        name=name,
    )(*pairs, *map(late, extra), weight, weight, bias)


def clear(*refs):
    @pl.when(pl.program_id(0) == 0)
    def _():
        for ref in refs:
            ref[...] = jnp.zeros_like(ref)


def finish(acc, low, high):
    rows = low.shape[0]

    @pl.when(pl.program_id(0) == pl.num_programs(0) - 1)
    def _():
        low[...] = acc[:rows, :].astype(BF)
        high[...] = acc[rows:, :].astype(BF)


CHUNK = 32


def mlp_forward(pair, weight, bias):
    rows = pair[0].shape[0]

    def body(a, b, w1_ref, w2_ref, bias_ref, act_ref, slope_ref, sum_ref, lo, hi, acc, pre):
        clear(acc, sum_ref)
        shift = bias_ref[...]
        for i, x in enumerate((a, b)):
            pre[i * rows : (i + 1) * rows, :] = dot(x[...], w1_ref[...])
        for i in range(2):
            at = slice(i * rows, (i + 1) * rows)
            for r in range(i * rows, (i + 1) * rows, CHUNK):
                act, slope = gelu_both(pre[r : r + CHUNK, :] + shift)
                act_ref[r : r + CHUNK, :] = act.astype(BF)
                slope_ref[r : r + CHUNK, :] = slope.astype(BF)
            acc[at, :] += dot_bt(act_ref[at, :], w2_ref[...])
        finish(acc, lo, hi)

    act, slope, _, lo, hi = mlp_call(body, pair, [], weight, bias, [BF, BF], 1, 1, "mlp_forward")
    return act, slope, lo, hi


def mlp_backward(pair, slope, weight, bias):
    rows = pair[0].shape[0]

    def body(a, b, slope_ref, w1_ref, w2_ref, bias_ref, dpre_ref, sum_ref, lo, hi, acc, pre):
        clear(acc)
        for i, g in enumerate((a, b)):
            pre[i * rows : (i + 1) * rows, :] = dot(g[...], w2_ref[...])
        sums = jnp.zeros((8, bias_ref.shape[1]), F32)
        for i in range(2):
            at = slice(i * rows, (i + 1) * rows)
            for r in range(i * rows, (i + 1) * rows, CHUNK):
                d = pre[r : r + CHUNK, :] * slope_ref[r : r + CHUNK, :].astype(F32)
                d = d.astype(BF)
                dpre_ref[r : r + CHUNK, :] = d
                sums = sums + fold(d.astype(F32), jnp.sum)
            acc[at, :] += dot_bt(dpre_ref[at, :], w1_ref[...])
        sum_ref[...] = jnp.sum(sums, axis=0, keepdims=True)
        finish(acc, lo, hi)

    dpre, sums, lo, hi = mlp_call(
        body, pair, [slope], weight, bias, [BF], 1, 1, "mlp_backward"
    )
    return dpre, sums, lo, hi


def mlp_both(pair, grads, weight, bias):
    rows = pair[0].shape[0]

    def body(
        a, b, c, d, w1_ref, w2_ref, bias_ref, act_ref, dpre_ref, sum_ref,
        lo, hi, blo, bhi, acc, back, pre, grad,
    ):
        clear(acc, back)
        shift = bias_ref[...]
        for i, (x, g) in enumerate(((a, c), (b, d))):
            at = slice(i * rows, (i + 1) * rows)
            pre[at, :] = dot(x[...], w1_ref[...])
            grad[at, :] = dot(g[...], w2_ref[...])
        sums = jnp.zeros((8, bias_ref.shape[1]), F32)
        for i in range(2):
            at = slice(i * rows, (i + 1) * rows)
            for r in range(i * rows, (i + 1) * rows, CHUNK):
                act, slope = gelu_both(pre[r : r + CHUNK, :] + shift)
                act_ref[r : r + CHUNK, :] = act.astype(BF)
                dpre = (grad[r : r + CHUNK, :] * slope).astype(BF)
                dpre_ref[r : r + CHUNK, :] = dpre
                sums = sums + fold(dpre.astype(F32), jnp.sum)
            back[at, :] += dot_bt(dpre_ref[at, :], w1_ref[...])
            acc[at, :] += dot_bt(act_ref[at, :], w2_ref[...])
        sum_ref[...] = jnp.sum(sums, axis=0, keepdims=True)
        finish(acc, lo, hi)
        finish(back, blo, bhi)

    act, dpre, sums, lo, hi, blo, bhi = mlp_call(
        body, [*pair, *grads], [], weight, bias, [BF, BF], 2, 2, "mlp_both"
    )
    return act, dpre, sums, lo, hi, blo, bhi


def weight_grads(products, dp, side, name, halves=True):
    model = products[0][0][0].shape[1]
    step = model // dp
    half = step // 2
    cut = 2 if halves else 1
    sizes = [(len(left), len(right), right[0].shape[1]) for left, right in products]
    cols = sum(n for _, _, n in sizes)

    def body(side_ref, *refs):
        acc_ref = refs[-1]
        mine, other = refs[-3:-1] if halves else (refs[-2], None)
        at = base = 0
        for many, few, n in sizes:
            lefts, rights = refs[at : at + many], refs[at + many : at + many + few]
            at += many + few
            ratio = many // few
            acc = None
            for i in range(many):
                size = lefts[i].shape[0]
                here = slice((i % ratio) * size, (i % ratio + 1) * size)
                term = dot_at(lefts[i][...], rights[i // ratio][here, :])
                acc = term if acc is None else acc + term
            if halves:
                acc_ref[:, base : base + n] = acc
            else:
                mine[:, base : base + n] = acc.astype(BF)
            base += n
        if not halves:
            return
        low = pl.multiple_of(side_ref[0] * half, half)
        high = pl.multiple_of((1 - side_ref[0]) * half, half)
        mine[...] = acc_ref[pl.ds(low, half), :].astype(BF)
        other[...] = acc_ref[pl.ds(high, half), :].astype(BF)

    specs, operands = [pl.BlockSpec(memory_space=pltpu.SMEM)], [side.reshape(1)]
    for left, right in products:
        specs += [pl.BlockSpec((a.shape[0], step), lambda i: (0, i)) for a in left]
        specs += [whole(b.shape) for b in right]
        operands += [*left, *right]
    return pl.pallas_call(
        body,
        grid=(dp,),
        in_specs=specs,
        out_specs=[pl.BlockSpec((step // cut, cols), lambda i: (i, 0))] * cut,
        out_shape=[sds((model // cut, cols), BF)] * cut,
        scratch_shapes=[pltpu.VMEM((step, cols), F32)],
        compiler_params=params(14, 1),
        cost_estimate=cost(5),
        name=name,
    )(*operands)


def pieces(chunks):
    return [p for pair in chunks for p in pair]


def shards(
    tokens, cotangent, ln1_gain, ln1_bias, w_qkv, qv_bias, w_out, out_bias, scale_attn,
    ln2_gain, ln2_bias, w_fc1, fc1_bias, w_fc2, fc2_bias, scale_mlp,
):
    side = lax.axis_index("section")
    first = side == 0
    dp = lax.axis_size("dp")
    here = lax.axis_index("dp")
    chips = lax.axis_size("tensor") // 2
    rows, model = tokens.shape[2:]
    heads = qv_bias.shape[1]
    size = qv_bias.shape[2] * dp // 2
    width = heads * size
    units = w_fc1.shape[2]
    part = model // dp

    x0 = lax.dynamic_index_in_dim(tokens, side, 0, keepdims=False).reshape(rows, model)
    grad_top = lax.dynamic_index_in_dim(cotangent, side, 0, keepdims=False).reshape(rows, model)

    vectors = (ln1_gain, ln1_bias, out_bias, scale_attn, ln2_gain, ln2_bias, fc2_bias, scale_mlp)
    packed = jnp.concatenate(
        [v.reshape(-1) for v in vectors] + [fc1_bias.reshape(-1), qv_bias.reshape(-1)]
    )
    own_qkv = w_qkv.reshape(part, heads, 3, size).swapaxes(1, 2).reshape(part, 3 * width)
    own_att = jnp.concatenate([own_qkv, w_out[0].T], axis=1)
    own_ff = jnp.concatenate([w_fc1[0], w_fc2[0].T], axis=1)

    def halves(own, came, rest):
        mine, left = half_of(own, side), half_of(own, 1 - side)
        return (
            (jnp.where(first, mine, came), jnp.where(first, left, rest)),
            (jnp.where(first, came, mine), jnp.where(first, rest, left)),
        )

    came_att = swap_section(half_of(own_att, 1 - side))
    ring_att0 = jnp.where(first, half_of(own_att, side), came_att)
    small = gather_small(packed, first, ring_att0).astype(F32)
    cut = 8 * part
    vecs = small[:, :, :cut].reshape(2, dp, 8, part).swapaxes(1, 2).reshape(2, 8, model)
    bias_fc1 = small[:, :, cut : cut + units // dp].reshape(2, 1, units)
    qv = small[:, :, cut + units // dp :].reshape(2, dp, heads, -1).swapaxes(1, 2)
    qv = qv.reshape(2, heads, 2, size)
    bias_qkv = jnp.stack([qv[:, :, 0], jnp.zeros_like(qv[:, :, 0]), qv[:, :, 1]], axis=1)
    bias_qkv = bias_qkv.reshape(2, 1, 3 * width)
    vecs = (vecs[0], vecs[1])

    norm1 = norm_first(tie(x0, came_att), vecs[0])
    came_ff = swap_section(tie(half_of(own_ff, 1 - side), came_att))
    rest_att = swap_section(tie(half_of(own_att, side), came_att))
    half_att0, half_att1 = halves(own_att, came_att, rest_att)
    ring_ff0 = jnp.where(first, half_of(own_ff, side), came_ff)

    def put_together(half, hops, backs):
        return assemble([half, *zip(hops, backs)], model)

    hops_att0 = direct(ring_att0)
    att0 = put_together(half_att0, hops_att0, [swap_section(tie(v, norm1)) for v in hops_att0])
    ff0, att1 = Ring(tie(ring_ff0, hops_att0[-1])), Ring(tie(half_att1[0], hops_att0[-1]))
    att0 = tie(att0, *att1.hop())
    beside = ff0.hop()
    rest_ff = swap_section(tie(half_of(own_ff, side), ff0.hops[0]))
    half_ff0, half_ff1 = halves(own_ff, came_ff, rest_ff)
    ff1 = Ring(half_ff1[0])

    def projection(weight, s):
        return lambda pair: project_qkv(pair, weight, bias_qkv[s])

    chunks0, qkv0 = gather_tokens(norm1, projection(att0, 0), beside)
    gate = qkv0[-1]
    beside = [*ff0.hop(gate), *ff0.back(gate)]
    kept0, lse0, sames, others = attention([*qkv0[:-1], tie(gate, rest_ff)], att0, size)
    terms, _ = scatter_tokens(
        sames, tie(others, *beside), beside=lambda gate: [*ff0.hop(gate), *ff0.back(gate)]
    )
    attended0, residual0, norm2 = after_attention(x0, terms, vecs[0])
    ff0.back(norm2)
    beside = att1.hop(norm2)
    w_ff0 = put_together(half_ff0, ff0.hops, ff0.backs)
    second0, mlp0 = gather_tokens(
        norm2, lambda pair: mlp_forward(pair, w_ff0, bias_fc1[0]), beside
    )
    act0, slope0, sames, others = zip(*mlp0)
    beside = att1.hop(second0[-1][0])
    terms, _ = scatter_tokens(
        sames,
        [others[0], *[tie(v, *beside) for v in others[1:]]],
        beside=lambda gate: [*ff1.hop(gate), *att1.back(gate), *att1.back(gate)],
    )
    mlp_out0, y0, norm1 = after_mlp(residual0, terms, vecs[0], vecs[1])

    att1.back(norm1)
    w_att1 = put_together(half_att1, att1.hops, att1.backs)
    low1, sums_fc2_1 = start_back(grad_top, vecs[1])
    beside = [*ff1.hop(norm1), *ff1.back(norm1)]
    chunks1, qkv1 = gather_tokens(norm1, projection(w_att1, 1), beside)
    gate = chunks1[-1][0]
    came = [from_chip(tie(low1, gate), step) for step in range(1, chips)]
    beside = [*came, *ff1.hop(gate), *ff1.back(gate)]
    kept1, lse1, sames, others = attention(qkv1, w_att1, size)
    others = tie(others, *beside)
    grads1 = [(low1, core_swap(low1))] + [(v, core_swap(tie(v, lse1))) for v in came]
    terms, _ = scatter_tokens(
        sames, others, beside=lambda gate: [*ff1.back(gate), *pieces(grads1)]
    )
    attended1, residual1, norm2 = after_attention(y0, terms, vecs[1])
    w_ff1 = put_together(half_ff1, ff1.hops, ff1.backs)
    spare = list(grads1)
    second1, mlp1 = gather_tokens(
        norm2, lambda pair: mlp_both(pair, spare.pop(0), w_ff1, bias_fc1[1])
    )
    act1, dpre1, sums_fc1_1, sames_y1, others_y1, sames, others = zip(*mlp1)

    def grad_ff(second, dpre, grads, act):
        return lambda after: weight_grads(
            [
                (pieces(second), [late(tie(dpre[0], after)), *map(late, dpre[1:])]),
                (pieces(grads), [late(a) for a in act]),
            ],
            dp,
            side,
            "grad_ff",
        )

    def grad_att(chunks, dqkv, datt, kept):
        return lambda after: weight_grads(
            [
                (pieces(chunks), [tie(dqkv[0], after), *dqkv[1:]]),
                (pieces(datt), [late(a) for a in kept]),
            ],
            dp,
            side,
            "grad_att",
            False,
        )[0]

    old = [tuple(map(late, pair)) for pair in grads1]
    terms, g = scatter_tokens(sames, others, grad_ff(second1, dpre1, old, act1))
    sum_ff1 = RingSum((0, 1), *g)
    dres1, low, sums1 = back_second(grad_top, residual1, attended1, terms, vecs[1])
    came_y0 = lax.ppermute(tie(y0, low), "section", [(1, 0)])
    datt, _ = gather_tokens(low, lambda pair: pair[0], sum_ff1.step())
    sums_y1, local_y1 = core_sums(sames_y1, [tie(v, low) for v in others_y1])
    terms_y1 = send_sums([tie(v, datt[-1][0]) for v in sums_y1])
    beside = [came_y0, *terms_y1, *sum_ff1.step(low)]
    dqkv, sames, others, qkv_sums1 = attention_back(qkv1, kept1, lse1, datt, w_att1, size)
    old = [tuple(map(late, pair)) for pair in chunks1]
    terms, g = scatter_tokens(
        sames, tie(others, *beside), grad_att(old, dqkv, datt, kept1), sum_ff1.step
    )
    sum_att1 = RingSum((0, 1), g)
    dx1, low0, edge1 = back_first(dres1, late(y0), terms, vecs[1], late(mlp_out0), vecs[0])
    y1, sums_sc_1 = last_output(
        residual1, [tie(sames_y1[0], low0), *terms_y1, local_y1], grad_top, vecs[1]
    )

    slopes = list(slope0)
    grads0, mlp_back0 = gather_tokens(
        low0,
        lambda pair: mlp_backward(pair, slopes.pop(0), w_ff0, bias_fc1[0]),
        [y1, *sum_ff1.step(low0)],
    )
    dpre0, sums_fc1_0, sames, others = zip(*mlp_back0)
    old = [tuple(map(late, pair)) for pair in second0]
    sum_att1.step()
    terms, g = scatter_tokens(
        sames,
        others,
        grad_ff(old, dpre0, grads0, act0),
        lambda gate: [*sum_ff1.step(gate), *sum_att1.step(gate)],
    )
    sum_ff0 = RingSum((1, 0), *g)
    dres0, low, sums0 = back_second(
        dx1, late(residual0), late(attended0), terms, vecs[0]
    )
    beside = [*sum_att1.step(low), *sum_ff0.step(low)]
    datt, _ = gather_tokens(low, lambda pair: pair[0], beside)
    beside = [*sum_att1.step(low), *sum_ff0.step(low)]
    dqkv, sames, others, qkv_sums0 = attention_back(qkv0, kept0, lse0, datt, att0, size)
    old = [tuple(map(late, pair)) for pair in chunks0]
    terms, g = scatter_tokens(
        sames, tie(others, *beside), grad_att(old, dqkv, datt, kept0), sum_ff0.step
    )
    sum_att0 = RingSum((1, 0), g)
    sum_att0.step()
    going = sum_att0.step()
    dx0, edge0 = back_first(dres0, x0, terms, vecs[0])
    came_dx0 = lax.ppermute(dx0, "section", [(1, 0)])
    sum_att1.step(dx0)
    sum_ff0.step(dx0)
    ready = sum_att0.step(dx0)[-1]
    came_y1 = lax.ppermute(tie(y1, ready), "section", [(0, 1)])
    came_dx1 = lax.ppermute(tie(dx1, ready), "section", [(0, 1)])
    sum_ff0.step(), sum_att0.step(), sum_att0.step()

    def both(low, high, came_low, came_high):
        mine = jnp.where(first, low, high)
        came = jnp.where(first, came_low, came_high)
        return jnp.stack([jnp.where(first, mine, came), jnp.where(first, came, mine)])[None, :, None]

    block_out = both(tie(y0, ready), y1, came_y0, came_y1)
    input_grads = both(dx0, dx1, came_dx0, came_dx1)

    def by_unit(qkv_sums, unit_sums):
        q = qkv_sums[:, :width].reshape(heads, 1, size)
        v = qkv_sums[:, 2 * width :].reshape(heads, 1, size)
        bias = jnp.concatenate([q, v], 1).reshape(heads, dp, -1).swapaxes(0, 1).reshape(dp, -1)
        return jnp.concatenate([bias, unit_sums.reshape(dp, -1)], axis=1)

    unit0 = by_unit(tie(qkv_sums0, dx0), sum(sums_fc1_0))
    unit1 = by_unit(tie(qkv_sums1, dx0), sum(sums_fc1_1))
    vec = jnp.concatenate(
        [edge0[:2], sums0[:4], edge1[2:4], edge1[:2], sums1[:4], sums_sc_1[:1], sums_fc2_1[:1]]
    )
    vec = vec + core_swap(vec)
    vec = tie(sum([from_chip(vec, step) for step in range(1, chips)], vec), *going)
    vec = vec.reshape(2, 8, dp, part).swapaxes(1, 2).reshape(2, dp, 8 * part)
    vec0 = jnp.concatenate([vec[0], unit0], axis=1)
    vec1 = jnp.concatenate([vec[1], unit1], axis=1)
    own = jnp.where(first, vec0, vec1) + swap_section(jnp.where(first, vec1, vec0))
    vec = lax.dynamic_slice_in_dim(own, here, 1, 0)
    for step in range(1, dp):
        pairs = [(i, (i + step) % dp) for i in range(dp)]
        other = lax.dynamic_slice_in_dim(own, lax.rem(here + step, dp), 1, 0)
        vec = vec + lax.ppermute(other, "dp", pairs)
    cut = 8 * part + heads * (2 * size // dp)
    bias_grad = vec[:, 8 * part : cut].reshape(1, heads, -1)
    fc1_grad = vec[:, cut:].reshape(1, 1, -1)
    g_ln1, b_ln1, g_ln2, b_ln2, g_sc_attn, g_out_bias, g_sc_mlp, g_fc2_bias = (
        vec[:, i * part : (i + 1) * part] for i in range(8)
    )

    def owned(low, high):
        top = jnp.where(first, low.going, high.came.astype(F32))
        bottom = jnp.where(first, low.came.astype(F32), high.going)
        return jnp.concatenate([top, bottom], 0)

    g_ff = owned(sum_ff0, sum_ff1)
    g_att = jnp.where(
        first,
        sum_att0.going + sum_att0.came.astype(F32),
        sum_att1.going + sum_att1.came.astype(F32),
    )
    g_qkv = g_att[:, : 3 * width].reshape(part, 3, heads, size).swapaxes(1, 2)
    g_qkv = g_qkv.reshape(1, part, 3 * width)
    g_out = g_att[:, 3 * width :].T[None]
    g_fc1 = g_ff[:, :units][None]
    g_fc2 = g_ff[:, units:].T[None]
    return (
        block_out, input_grads, g_ln1, b_ln1, g_qkv, bias_grad, g_out, g_out_bias, g_sc_attn,
        g_ln2, b_ln2, g_fc1, fc1_grad, g_fc2, g_fc2_bias, g_sc_mlp,
    )


def solution(mesh):
    vec = P("section", "dp")
    by_row = P("section", "dp", "tensor")
    by_unit = P("section", "tensor", "dp")
    data = P(None, "dp", "tensor", None)
    split = P("section", None, "dp", "tensor", None)
    given = (
        vec, vec, by_row, by_unit, by_unit, vec, vec, vec, vec, by_row, by_unit, by_unit, vec, vec,
    )
    return jax.shard_map(
        shards,
        mesh=mesh,
        in_specs=(data, data) + given,
        out_specs=(split, split) + given,
        check_vma=False,
    )
```

```python
from functools import partial

import jax
import jax.numpy as jnp
from jax import lax
from jax.experimental import pallas as pl
from jax.experimental.pallas import tpu as pltpu
from jax.sharding import PartitionSpec as P

EPSILON = 1e-06
BF = jnp.bfloat16
F32 = jnp.float32
MIB = 1 << 20

LN1_G, LN1_B, OUT_B, SC_ATTN, LN2_G, LN2_B, FC2_B, SC_MLP = range(8)


def dot(a, b):
    return lax.dot_general(a, b, (((1,), (0,)), ((), ())), preferred_element_type=F32)


def dot_bt(a, b):
    return lax.dot_general(a, b, (((1,), (1,)), ((), ())), preferred_element_type=F32)


def dot_at(a, b):
    return lax.dot_general(a, b, (((0,), (0,)), ((), ())), preferred_element_type=F32)


def turn(v):
    return v.astype(F32).T


def params(limit, grid=0):
    return pltpu.CompilerParams(
        vmem_limit_bytes=limit * MIB,
        dimension_semantics=("arbitrary",) * grid if grid else None,
    )


def late(v):
    return pltpu.with_memory_space_constraint(v, pltpu.HBM)


def whole(shape):
    return pl.BlockSpec(shape, lambda i: (0, 0), pipeline_mode=pl.Buffered(1))


def cost(micros):
    return pl.CostEstimate(flops=int(micros * 1.15e9), bytes_accessed=0, transcendentals=0)


def sds(shape, dtype):
    return jax.ShapeDtypeStruct(shape, dtype)


def core_swap(v):
    count = lax.axis_size("tensor")
    return lax.ppermute(v, "tensor", [(i, i ^ 1) for i in range(count)])


def from_chip(v, step):
    count = lax.axis_size("tensor")
    chips = count // 2
    pairs = [(((i // 2 + step) % chips) * 2 + i % 2, i) for i in range(count)]
    return lax.ppermute(v, "tensor", pairs)


def tie(v, *after):
    if not after:
        return v
    return lax.optimization_barrier((v, *after))[0]


def tie_all(vs, *after):
    return lax.optimization_barrier((*vs, *after))[: len(vs)]


def gather_tokens(own, work, beside=()):
    chips = lax.axis_size("tensor") // 2
    came = [from_chip(own, step) for step in range(1, chips)]
    chunks = [(own, core_swap(own))]
    results = [work(chunks[0])]
    for same in came:
        same = tie(same, results[-1], *beside)
        chunks.append((same, core_swap(same)))
        results.append(work(chunks[-1]))
    return chunks, results


def core_sums(sames, others):
    chips, rows = len(sames), sames[0].shape[0]
    if isinstance(others, (list, tuple)):
        came = [core_swap(v) for v in others[1:]]
        local = core_swap(tie(others[0], came[-1]))
    else:
        local = core_swap(others)
        came = [local[c * rows : (c + 1) * rows] for c in range(1, chips)]
    sums = [(a.astype(F32) + b.astype(F32)).astype(BF) for a, b in zip(sames[1:], came)]
    return sums, local


def send_sums(sums):
    chips = len(sums) + 1
    return [from_chip(both, chips - step) for step, both in enumerate(sums, 1)]


def scatter_tokens(sames, others, work=None, beside=None):
    sums, local = core_sums(sames, others)
    terms = send_sums(sums)
    made = work(sums[-1]) if work else local
    more = beside(sums[-1]) if beside else ()
    terms = [tie(t, made, local, *more) for t in terms]
    return [sames[0], *terms, local], made


def swap_section(v):
    return lax.ppermute(v, "section", [(0, 1), (1, 0)])


def assemble(shards, rows):
    count = len(shards)
    cut = len(shards[0])
    size, cols = rows // (count * cut), shards[0][0].shape[1]
    place = jnp.stack([lax.axis_index("dp"), lax.axis_index("section")])

    def body(place_ref, *refs):
        out_ref, sems = refs[count * cut :]
        z, x = place_ref[0], place_ref[1]
        started = []
        for k in range(count):
            base = lax.rem(z + (count - k), count) * (cut * size)
            for i, at in enumerate([base] if cut == 1 else [base + x * size, base + (1 - x) * size]):
                copy = pltpu.make_async_copy(
                    refs[k * cut + i].at[pl.ds(0, size), :],
                    out_ref.at[pl.ds(pl.multiple_of(at, size), size), :],
                    sems.at[k * cut + i],
                )
                copy.start()
                started.append(copy)
        for copy in started:
            copy.wait()

    hbm = pl.BlockSpec(memory_space=pl.ANY)
    return pl.pallas_call(
        body,
        in_specs=[pl.BlockSpec(memory_space=pltpu.SMEM)] + [hbm] * (count * cut),
        out_specs=pl.BlockSpec(memory_space=pltpu.VMEM),
        out_shape=sds((rows, cols), shards[0][0].dtype),
        scratch_shapes=[pltpu.SemaphoreType.DMA((count * cut,))],
        compiler_params=params(6),
        cost_estimate=cost(2),
        name="assemble",
    )(place, *[v for shard in shards for v in shard])


def half_of(v, which):
    half = v.shape[0] // 2
    return lax.dynamic_slice_in_dim(v, which * half, half, 0)


def direct(own):
    count = lax.axis_size("dp")
    return [
        lax.ppermute(own, "dp", [(i, (i + step) % count) for i in range(count)])
        for step in range(1, count)
    ]


def third(values, index):
    cuts = [-(-len(values) * i // 3) for i in range(4)]
    return values[cuts[index] : cuts[index + 1]]


class Ring:
    def __init__(self, own):
        self.last, self.hops, self.backs, self.at, self.back_at = own, [], [], 0, 0

    def hop(self, *gate):
        count = lax.axis_size("dp")
        pairs = [(i, (i + 1) % count) for i in range(count)]
        new = []
        for i in range(len(third(range(count - 1), self.at))):
            self.last = lax.ppermute(tie(self.last, *gate) if i == 0 else self.last, "dp", pairs)
            new.append(self.last)
        self.hops += new
        self.at += 1
        return new

    def back(self, *gate):
        count = lax.axis_size("dp")
        which = third(range(count - 1), self.back_at)
        new = [swap_section(tie(self.hops[i], *gate)) for i in which]
        self.backs += new
        self.back_at += 1
        return new


def in_order(back):
    count = len(back)
    ahead = [back[0], *back[:0:-1]]
    twice = jnp.stack(ahead + ahead)
    return lax.dynamic_slice_in_dim(twice, count - lax.axis_index("dp"), count, 0)


def dp_rows(v, back):
    dp = lax.axis_size("dp")
    part = v.shape[0] // dp
    place = lax.rem(lax.axis_index("dp") + (dp - back), dp)
    return lax.dynamic_slice_in_dim(v, place * part, part, 0)


class RingSum:
    def __init__(self, pair, mine, other=None):
        self.mine, self.other, self.pair = mine, other, pair
        self.terms, self.at, self.done = [], 0, 0

    def total(self, gate=()):
        first = tie(self.terms[0], *gate)
        return sum(t.astype(F32) for t in [first, *self.terms[1:]])

    def one(self, gate):
        dp = lax.axis_size("dp")
        self.done += 1
        new = []
        if self.terms:
            pairs = [(i, (i + 1) % dp) for i in range(dp)]
            new.append(lax.ppermute(self.total(gate).astype(BF), "dp", pairs))
        if self.other is not None:
            new.append(swap_section(tie(dp_rows(self.other, self.done), *gate)))
        self.terms = [*new, dp_rows(self.mine, self.done)]
        return new

    def step(self, *gate):
        self.at += 1
        if self.at == 5:
            self.own = self.total(gate)
            self.came = lax.ppermute(self.own.astype(BF), "section", [self.pair])
            return [self.came]
        count = 1 if self.at == 1 else len(third(range(lax.axis_size("dp") - 1), self.at - 2))
        return [v for i in range(count) for v in self.one(gate if i == 0 else ())]


def standardize(v):
    centred = v - jnp.mean(v, axis=-1, keepdims=True)
    var = jnp.mean(centred * centred, axis=-1, keepdims=True)
    scale = lax.rsqrt(var + EPSILON)
    return centred * scale, scale


def norm_of(v, vec, gain, shift):
    return (standardize(v)[0] * vec[gain : gain + 1, :] + vec[shift : shift + 1, :]).astype(BF)


def norm_back(v, grad, gain):
    xh, scale = standardize(v)
    dxh = grad * gain
    inner = jnp.mean(dxh * xh, axis=-1, keepdims=True)
    out = scale * (dxh - jnp.mean(dxh, axis=-1, keepdims=True) - xh * inner)
    return out, grad * xh


def total(refs):
    out = refs[0][...].astype(F32)
    for ref in refs[1:]:
        out = out + ref[...].astype(F32)
    return out


def fold(v, op):
    return op(v.reshape(-1, 8, v.shape[1]), axis=0)


def add_rows(ref, rows):
    for k, row in enumerate(rows):
        ref[8 * k : 8 * k + 8, :] += fold(row, jnp.sum)


def rowwise(body, row_ins, fulls, row_outs, sums, name):
    rows, width = row_ins[0].shape
    step = min(64, rows)
    some, outs = len(row_ins) + len(fulls), len(row_outs)

    def kernel(*refs):
        if not sums:
            body(*refs)
            return
        sum_ref, acc_ref = refs[some + outs :]

        @pl.when(pl.program_id(0) == 0)
        def _():
            acc_ref[...] = jnp.zeros_like(acc_ref)

        body(*refs[: some + outs], acc_ref)

        @pl.when(pl.program_id(0) == pl.num_programs(0) - 1)
        def _():
            for k in range(sums):
                sum_ref[k : k + 1, :] = jnp.sum(
                    acc_ref[8 * k : 8 * k + 8, :], axis=0, keepdims=True
                )

    out_shape = [sds((rows, width), d) for d in row_outs]
    out_shape += [sds((sums, width), F32)] if sums else []
    block = pl.BlockSpec((step, width), lambda i: (i, 0))
    return pl.pallas_call(
        kernel,
        grid=(rows // step,),
        in_specs=[block] * len(row_ins) + [whole(a.shape) for a in fulls],
        out_specs=[block] * outs + ([whole((sums, width))] if sums else []),
        out_shape=out_shape,
        scratch_shapes=[pltpu.VMEM((8 * sums, width), F32)] if sums else [],
        compiler_params=params(8, 1),
        cost_estimate=cost(2),
        name=name,
    )(*row_ins, *fulls)


def norm_first(x, vec):
    def body(x_ref, vec_ref, out_ref):
        out_ref[...] = norm_of(x_ref[...].astype(F32), vec_ref[...], LN1_G, LN1_B)

    return rowwise(body, [x], [vec], [BF], 0, "norm_first")[0]


def after_attention(x, terms, vec):
    count = len(terms)

    def body(*refs):
        x_ref, term_refs, vec_ref = refs[0], refs[1 : 1 + count], refs[1 + count]
        att_ref, res_ref, norm_ref = refs[2 + count :]
        v = vec_ref[...]
        attended = total(term_refs) + v[OUT_B : OUT_B + 1, :]
        residual = x_ref[...].astype(F32) + v[SC_ATTN : SC_ATTN + 1, :] * attended
        att_ref[...] = attended.astype(BF)
        res_ref[...] = residual
        norm_ref[...] = norm_of(residual, v, LN2_G, LN2_B)

    return rowwise(body, [x, *terms], [vec], [BF, F32, BF], 0, "after_attention")


def after_mlp(residual, terms, vec, vec_next):
    count = len(terms)

    def body(*refs):
        res_ref, term_refs = refs[0], refs[1 : 1 + count]
        vec_ref, next_ref, mlp_ref, y_ref, norm_ref = refs[1 + count :]
        v = vec_ref[...]
        mlp = total(term_refs) + v[FC2_B : FC2_B + 1, :]
        y = (res_ref[...] + v[SC_MLP : SC_MLP + 1, :] * mlp).astype(BF)
        mlp_ref[...] = mlp.astype(BF)
        y_ref[...] = y
        norm_ref[...] = norm_of(y.astype(F32), next_ref[...], LN1_G, LN1_B)

    return rowwise(body, [residual, *terms], [vec, vec_next], [BF, BF, BF], 0, "after_mlp")


def last_output(residual, terms, grad, vec):
    count = len(terms)

    def body(*refs):
        res_ref, term_refs = refs[0], refs[1 : 1 + count]
        grad_ref, vec_ref, y_ref, sum_ref = refs[1 + count :]
        v = vec_ref[...]
        mlp = total(term_refs) + v[FC2_B : FC2_B + 1, :]
        y_ref[...] = (res_ref[...] + v[SC_MLP : SC_MLP + 1, :] * mlp).astype(BF)
        add_rows(sum_ref, [grad_ref[...].astype(F32) * mlp])

    return rowwise(body, [residual, *terms, grad], [vec], [BF], 1, "last_output")


def start_back(grad, vec):
    def body(grad_ref, vec_ref, out_ref, sum_ref):
        low = (vec_ref[...][SC_MLP : SC_MLP + 1, :] * grad_ref[...].astype(F32)).astype(BF)
        out_ref[...] = low
        add_rows(sum_ref, [low.astype(F32)])

    return rowwise(body, [grad], [vec], [BF], 1, "start_back")


def back_second(grad, residual, attended, terms, vec):
    count = len(terms)

    def body(*refs):
        grad_ref, res_ref, att_ref = refs[:3]
        term_refs = refs[3 : 3 + count]
        vec_ref, dres_ref, low_ref, sum_ref = refs[3 + count :]
        v = vec_ref[...]
        dn = total(term_refs)
        back, dgain = norm_back(res_ref[...], dn, v[LN2_G : LN2_G + 1, :])
        dres = grad_ref[...].astype(F32) + back
        low = (v[SC_ATTN : SC_ATTN + 1, :] * dres).astype(BF)
        dres_ref[...] = dres
        low_ref[...] = low
        add_rows(sum_ref, [dgain, dn, dres * att_ref[...].astype(F32), low.astype(F32)])

    return rowwise(
        body, [grad, residual, attended, *terms], [vec], [F32, BF], 4, "back_second"
    )


def back_first(dres, x, terms, vec, mlp_below=None, vec_below=None):
    count = len(terms)
    below = mlp_below is not None

    def body(*refs):
        dres_ref, x_ref = refs[:2]
        term_refs = refs[2 : 2 + count]
        rest = refs[2 + count :]
        if below:
            mlp_ref, vec_ref, under_ref, dx_ref, low_ref, sum_ref = rest
        else:
            vec_ref, dx_ref, sum_ref = rest
        v = vec_ref[...]
        dn = total(term_refs)
        back, dgain = norm_back(x_ref[...].astype(F32), dn, v[LN1_G : LN1_G + 1, :])
        dx = (dres_ref[...] + back).astype(BF)
        dx_ref[...] = dx
        rows = [dgain, dn]
        if below:
            wide = dx.astype(F32)
            low = (under_ref[...][SC_MLP : SC_MLP + 1, :] * wide).astype(BF)
            low_ref[...] = low
            rows += [wide * mlp_ref[...].astype(F32), low.astype(F32)]
        add_rows(sum_ref, rows)

    row_ins = [dres, x, *terms] + ([mlp_below] if below else [])
    fulls = [vec] + ([vec_below] if below else [])
    return rowwise(body, row_ins, fulls, [BF, BF] if below else [BF], 4 if below else 2, "back_first")


def project_qkv(pair, weight, bias):
    rows, width = pair[0].shape
    cols = bias.shape[1]

    def body(a_ref, b_ref, w_ref, bias_ref, out_ref):
        w = w_ref[...]
        shift = bias_ref[...]
        out_ref[:rows, :] = (dot(a_ref[...], w) + shift).astype(BF)
        out_ref[rows:, :] = (dot(b_ref[...], w) + shift).astype(BF)

    return pl.pallas_call(
        body,
        grid=(1,),
        in_specs=[
            whole((rows, width)), whole((rows, width)), whole((width, cols)), whole((1, cols))
        ],
        out_specs=whole((2 * rows, cols)),
        out_shape=sds((2 * rows, cols), BF),
        compiler_params=params(6, 1),
        cost_estimate=cost(2),
        name="project_qkv",
    )(*pair, weight, bias)


def head_rows(v, head, size):
    rows = lax.broadcasted_iota(jnp.int32, v.shape, 0)
    return jnp.where(rows // size == head, v, jnp.zeros_like(v))


def head_cols(v, head, size):
    cols = lax.broadcasted_iota(jnp.int32, v.shape, 1)
    return jnp.where(cols // size == head, v, jnp.zeros_like(v))


def attention(packed, weight, size):
    chips = len(packed)
    span = packed[0].shape[0]
    half = span // 2
    width = packed[0].shape[1] // 3
    seq = chips * span
    heads = width // size
    model = weight.shape[0]
    step = min(256, seq)
    chunk = min(128, seq)
    score = size**-0.5

    def body(*refs):
        in_refs, w_ref = refs[:chips], refs[chips]
        head_refs = refs[chips + 1 : 2 * chips + 1]
        lse_ref = refs[2 * chips + 1]
        same_refs, other_ref = refs[2 * chips + 2 : 3 * chips + 2], refs[3 * chips + 2]
        k_ref, qt_ref, vt_ref, ot_ref, s_ref, p_ref = refs[3 * chips + 3 :]
        for c in range(chips):
            at = slice(c * span, (c + 1) * span)
            k_ref[at, :] = in_refs[c][:, width : 2 * width]
            qt_ref[:, at] = (turn(in_refs[c][:, :width]) * score).astype(BF)
            vt_ref[:, at] = turn(in_refs[c][:, 2 * width :]).astype(BF)

        def one(i, carry):
            at = pl.ds(pl.multiple_of(i * step, step), step)
            q = qt_ref[:, at]
            s_ref[0] = dot(k_ref[...], head_rows(q, 0, size))
            for h in range(heads):
                if h + 1 < heads:
                    s_ref[(h + 1) % 2] = dot(k_ref[...], head_rows(q, h + 1, size))
                now = h % 2
                top = fold(s_ref[now, :chunk, :], jnp.max)
                for r in range(chunk, seq, chunk):
                    top = jnp.maximum(top, fold(s_ref[now, r : r + chunk, :], jnp.max))
                top = jnp.max(top, axis=0, keepdims=True)
                norm = jnp.zeros((8, step), F32)
                for r in range(0, seq, chunk):
                    p = jnp.exp(s_ref[now, r : r + chunk, :] - top)
                    norm = norm + fold(p, jnp.sum)
                    p_ref[now, r : r + chunk, :] = p.astype(BF)
                norm = jnp.sum(norm, axis=0, keepdims=True)
                rows = slice(h * size, (h + 1) * size)
                ot_ref[rows, at] = dot(vt_ref[rows, :], p_ref[now]) / norm
                lse_ref[h : h + 1, at] = top + jnp.log(norm)
            return carry

        lax.fori_loop(0, seq // step, one, 0)
        for c in range(chips):
            at = slice(c * span, (c + 1) * span)
            o = ot_ref[:, at].T.astype(BF)
            head_refs[c][...] = o
            same_refs[c][...] = dot_bt(o[:half], w_ref[...]).astype(BF)
            other_ref[c * half : (c + 1) * half, :] = dot_bt(o[half:], w_ref[...]).astype(BF)

    out = pl.pallas_call(
        body,
        grid=(1,),
        in_specs=[whole((span, 3 * width))] * chips
        + [pl.BlockSpec((model, width), lambda i: (0, 3), pipeline_mode=pl.Buffered(1))],
        out_specs=[whole((span, width))] * chips
        + [whole((heads, seq))]
        + [whole((half, model))] * chips
        + [whole((seq // 2, model))],
        out_shape=[pltpu.HBM((span, width), BF)] * chips
        + [sds((heads, seq), F32)]
        + [sds((half, model), BF)] * chips
        + [sds((seq // 2, model), BF)],
        scratch_shapes=[
            pltpu.VMEM((seq, width), BF),
            pltpu.VMEM((width, seq), BF),
            pltpu.VMEM((width, seq), BF),
            pltpu.VMEM((width, seq), F32),
            pltpu.VMEM((2, seq, step), F32),
            pltpu.VMEM((2, seq, step), BF),
        ],
        compiler_params=params(14, 1),
        cost_estimate=cost(9),
        name="attention",
    )(*packed, weight)
    return out[:chips], out[chips], out[chips + 1 : -1], out[-1]


def attention_back(packed, heads_kept, lse, datt, weight, size):
    chips = len(packed)
    span = packed[0].shape[0]
    half = span // 2
    width = packed[0].shape[1] // 3
    seq = chips * span
    heads = width // size
    model = weight.shape[0]
    step = min(256, seq)
    chunk = min(128, seq)
    score = size**-0.5

    def body(*refs):
        at = 0

        def take(count):
            nonlocal at
            at += count
            return refs[at - count : at]

        in_refs, kept_refs = take(chips), take(chips)
        (lse_ref,) = take(1)
        datt_refs = take(2 * chips)
        (w_ref,) = take(1)
        dqkv_refs = take(chips)
        same_refs = take(chips)
        other_ref, sum_ref = take(2)
        k_ref, v_ref, kt_ref, qt_ref, q_ref, do_ref, dot_ref = take(7)
        inner_ref, s_ref, g_ref, p_ref, ds_ref, dk_ref, dv_ref, dqt_ref = take(8)
        for c in range(chips):
            rows = slice(c * span, (c + 1) * span)
            q = in_refs[c][:, :width].astype(F32) * score
            k = in_refs[c][:, width : 2 * width]
            q_ref[rows, :] = q.astype(BF)
            qt_ref[:, rows] = q.T.astype(BF)
            k_ref[rows, :] = k
            kt_ref[:, rows] = turn(k).astype(BF)
            v_ref[rows, :] = in_refs[c][:, 2 * width :]
            for b in range(2):
                d = dot(datt_refs[2 * c + b][...], w_ref[:, 3 * width :]).astype(BF)
                here = slice(c * span + b * half, c * span + (b + 1) * half)
                do_ref[here, :] = d
                dt = turn(d)
                dot_ref[:, here] = dt.astype(BF)
                prod = dt * turn(kept_refs[c][b * half : (b + 1) * half, :])
                for h in range(heads):
                    inner_ref[h : h + 1, here] = jnp.sum(
                        prod[h * size : (h + 1) * size, :], axis=0, keepdims=True
                    )

        def one(i, carry):
            at = pl.ds(pl.multiple_of(i * step, step), step)
            qt = qt_ref[:, at]
            dot_t = dot_ref[:, at]
            q = q_ref[at, :]
            do = do_ref[at, :]

            def scores(h):
                s_ref[h % 2] = dot(k_ref[...], head_rows(qt, h, size))
                g_ref[h % 2] = dot(v_ref[...], head_rows(dot_t, h, size))

            scores(0)
            for h in range(heads):
                if h + 1 < heads:
                    scores(h + 1)
                now = h % 2
                cols = slice(h * step, (h + 1) * step)
                lse = lse_ref[h : h + 1, at]
                inner = inner_ref[h : h + 1, at]
                for r in range(0, seq, chunk):
                    p = jnp.exp(s_ref[now, r : r + chunk, :] - lse)
                    ds = p * (g_ref[now, r : r + chunk, :] - inner)
                    p_ref[r : r + chunk, cols] = p.astype(BF)
                    ds_ref[r : r + chunk, cols] = ds.astype(BF)
                rows = slice(h * size, (h + 1) * size)
                dqt_ref[rows, at] = dot(kt_ref[rows, :], ds_ref[:, cols]) * score
            dv = dot(p_ref[...], jnp.concatenate([head_cols(do, h, size) for h in range(heads)], 0))
            dk = dot(ds_ref[...], jnp.concatenate([head_cols(q, h, size) for h in range(heads)], 0))

            @pl.when(i == 0)
            def _():
                dv_ref[...] = dv
                dk_ref[...] = dk

            @pl.when(i > 0)
            def _():
                dv_ref[...] += dv
                dk_ref[...] += dk

            return carry

        lax.fori_loop(0, seq // step, one, 0)
        for c in range(chips):
            rows = slice(c * span, (c + 1) * span)
            out = dqkv_refs[c]
            out[:, :width] = dqt_ref[:, rows].T.astype(BF)
            out[:, width : 2 * width] = dk_ref[rows, :].astype(BF)
            out[:, 2 * width :] = dv_ref[rows, :].astype(BF)
            sums = jnp.sum(out[...].astype(F32), axis=0, keepdims=True)
            if c == 0:
                sum_ref[...] = sums
            else:
                sum_ref[...] += sums
            w = w_ref[:, : 3 * width]
            same_refs[c][...] = dot_bt(out[:half, :], w).astype(BF)
            other_ref[c * half : (c + 1) * half, :] = dot_bt(out[half:, :], w).astype(BF)

    flat = [g for pair in datt for g in pair]
    out_shape = (
        [sds((span, 3 * width), BF)] * chips
        + [sds((half, model), BF)] * chips
        + [sds((seq // 2, model), BF), sds((1, 3 * width), F32)]
    )
    operands = (*map(late, (*packed, *heads_kept)), lse, *flat, late(weight))
    out = pl.pallas_call(
        body,
        grid=(1,),
        in_specs=[whole(a.shape) for a in operands],
        out_specs=[whole(a.shape) for a in out_shape],
        out_shape=out_shape,
        scratch_shapes=[
            pltpu.VMEM((seq, width), BF),
            pltpu.VMEM((seq, width), BF),
            pltpu.VMEM((width, seq), BF),
            pltpu.VMEM((width, seq), BF),
            pltpu.VMEM((seq, width), BF),
            pltpu.VMEM((seq, width), BF),
            pltpu.VMEM((width, seq), BF),
            pltpu.VMEM((heads, seq), F32),
            pltpu.VMEM((2, seq, step), F32),
            pltpu.VMEM((2, seq, step), F32),
            pltpu.VMEM((seq, heads * step), BF),
            pltpu.VMEM((seq, heads * step), BF),
            pltpu.VMEM((seq, width), F32),
            pltpu.VMEM((seq, width), F32),
            pltpu.VMEM((width, seq), F32),
        ],
        compiler_params=params(26, 1),
        cost_estimate=cost(15),
        name="attention_back",
    )(*operands)
    return out[:chips], out[chips : 2 * chips], out[2 * chips], out[2 * chips + 1]


def gelu_both(x):
    away = jnp.abs(x)
    t = 1.0 / (1.0 + (0.3275911 * 0.5**0.5) * away)
    bell = jnp.exp(-0.5 * (x * x))
    poly = t * (
        0.127414796
        + t * (-0.142248368 + t * (0.7107068705 + t * (-0.7265760135 + t * 0.5307027145)))
    )
    tail = poly * bell
    phi = jnp.where(x >= 0, 1.0 - tail, tail)
    return x * phi, phi + x * (bell * 0.3989422804014327)


def mlp_call(body, pairs, extra, weight, bias, outs, parts, scratch, name):
    rows, model = pairs[0].shape
    units = weight.shape[1] // 2
    step = min(256, units)
    blocks = units // step
    cols = lambda j: (0, j)
    in_specs = [whole((rows, model)) for _ in pairs]
    in_specs += [pl.BlockSpec((2 * rows, step), cols) for _ in extra]
    in_specs += [
        pl.BlockSpec((model, step), cols),
        pl.BlockSpec((model, step), lambda j: (0, blocks + j)),
        pl.BlockSpec((1, step), cols),
    ]
    out_specs = [pl.BlockSpec((2 * rows, step), cols) for _ in outs]
    out_specs += [pl.BlockSpec((1, step), cols)]
    out_specs += [whole((rows, model))] * (2 * parts)
    out_shape = [pltpu.HBM((2 * rows, units), d) for d in outs] + [sds((1, units), F32)]
    out_shape += [sds((rows, model), BF)] * (2 * parts)
    count = len(pairs) // 2
    return pl.pallas_call(
        body,
        grid=(blocks,),
        in_specs=in_specs,
        out_specs=out_specs,
        out_shape=out_shape,
        scratch_shapes=[pltpu.VMEM((2 * rows, model), F32)] * parts
        + [pltpu.VMEM((2 * rows, step), F32)] * scratch,
        compiler_params=params(8 + 5 * parts, 1),
        cost_estimate=cost(3 + 3 * parts),
        name=name,
    )(*pairs, *map(late, extra), weight, weight, bias)


def clear(*refs):
    @pl.when(pl.program_id(0) == 0)
    def _():
        for ref in refs:
            ref[...] = jnp.zeros_like(ref)


def finish(acc, low, high):
    rows = low.shape[0]

    @pl.when(pl.program_id(0) == pl.num_programs(0) - 1)
    def _():
        low[...] = acc[:rows, :].astype(BF)
        high[...] = acc[rows:, :].astype(BF)


CHUNK = 32


def mlp_forward(pair, weight, bias):
    rows = pair[0].shape[0]

    def body(a, b, w1_ref, w2_ref, bias_ref, act_ref, slope_ref, sum_ref, lo, hi, acc, pre):
        clear(acc, sum_ref)
        shift = bias_ref[...]
        for i, x in enumerate((a, b)):
            pre[i * rows : (i + 1) * rows, :] = dot(x[...], w1_ref[...])
        for i in range(2):
            at = slice(i * rows, (i + 1) * rows)
            for r in range(i * rows, (i + 1) * rows, CHUNK):
                act, slope = gelu_both(pre[r : r + CHUNK, :] + shift)
                act_ref[r : r + CHUNK, :] = act.astype(BF)
                slope_ref[r : r + CHUNK, :] = slope.astype(BF)
            acc[at, :] += dot_bt(act_ref[at, :], w2_ref[...])
        finish(acc, lo, hi)

    act, slope, _, lo, hi = mlp_call(body, pair, [], weight, bias, [BF, BF], 1, 1, "mlp_forward")
    return act, slope, lo, hi


def mlp_backward(pair, slope, weight, bias):
    rows = pair[0].shape[0]

    def body(a, b, slope_ref, w1_ref, w2_ref, bias_ref, dpre_ref, sum_ref, lo, hi, acc, pre):
        clear(acc)
        for i, g in enumerate((a, b)):
            pre[i * rows : (i + 1) * rows, :] = dot(g[...], w2_ref[...])
        sums = jnp.zeros((8, bias_ref.shape[1]), F32)
        for i in range(2):
            at = slice(i * rows, (i + 1) * rows)
            for r in range(i * rows, (i + 1) * rows, CHUNK):
                d = pre[r : r + CHUNK, :] * slope_ref[r : r + CHUNK, :].astype(F32)
                d = d.astype(BF)
                dpre_ref[r : r + CHUNK, :] = d
                sums = sums + fold(d.astype(F32), jnp.sum)
            acc[at, :] += dot_bt(dpre_ref[at, :], w1_ref[...])
        sum_ref[...] = jnp.sum(sums, axis=0, keepdims=True)
        finish(acc, lo, hi)

    dpre, sums, lo, hi = mlp_call(
        body, pair, [slope], weight, bias, [BF], 1, 1, "mlp_backward"
    )
    return dpre, sums, lo, hi


def mlp_both(pair, grads, weight, bias):
    rows = pair[0].shape[0]

    def body(
        a, b, c, d, w1_ref, w2_ref, bias_ref, act_ref, dpre_ref, sum_ref,
        lo, hi, blo, bhi, acc, back, pre, grad,
    ):
        clear(acc, back)
        shift = bias_ref[...]
        for i, (x, g) in enumerate(((a, c), (b, d))):
            at = slice(i * rows, (i + 1) * rows)
            pre[at, :] = dot(x[...], w1_ref[...])
            grad[at, :] = dot(g[...], w2_ref[...])
        sums = jnp.zeros((8, bias_ref.shape[1]), F32)
        for i in range(2):
            at = slice(i * rows, (i + 1) * rows)
            for r in range(i * rows, (i + 1) * rows, CHUNK):
                act, slope = gelu_both(pre[r : r + CHUNK, :] + shift)
                act_ref[r : r + CHUNK, :] = act.astype(BF)
                dpre = (grad[r : r + CHUNK, :] * slope).astype(BF)
                dpre_ref[r : r + CHUNK, :] = dpre
                sums = sums + fold(dpre.astype(F32), jnp.sum)
            back[at, :] += dot_bt(dpre_ref[at, :], w1_ref[...])
            acc[at, :] += dot_bt(act_ref[at, :], w2_ref[...])
        sum_ref[...] = jnp.sum(sums, axis=0, keepdims=True)
        finish(acc, lo, hi)
        finish(back, blo, bhi)

    act, dpre, sums, lo, hi, blo, bhi = mlp_call(
        body, [*pair, *grads], [], weight, bias, [BF, BF], 2, 2, "mlp_both"
    )
    return act, dpre, sums, lo, hi, blo, bhi


def weight_grads(products, dp, side, name, halves=True):
    model = products[0][0][0].shape[1]
    step = model // dp
    half = step // 2
    cut = 2 if halves else 1
    sizes = [(len(left), len(right), right[0].shape[1]) for left, right in products]
    cols = sum(n for _, _, n in sizes)

    def body(side_ref, *refs):
        acc_ref = refs[-1]
        mine, other = refs[-3:-1] if halves else (refs[-2], None)
        at = base = 0
        for many, few, n in sizes:
            lefts, rights = refs[at : at + many], refs[at + many : at + many + few]
            at += many + few
            ratio = many // few
            acc = None
            for i in range(many):
                size = lefts[i].shape[0]
                here = slice((i % ratio) * size, (i % ratio + 1) * size)
                term = dot_at(lefts[i][...], rights[i // ratio][here, :])
                acc = term if acc is None else acc + term
            if halves:
                acc_ref[:, base : base + n] = acc
            else:
                mine[:, base : base + n] = acc.astype(BF)
            base += n
        if not halves:
            return
        low = pl.multiple_of(side_ref[0] * half, half)
        high = pl.multiple_of((1 - side_ref[0]) * half, half)
        mine[...] = acc_ref[pl.ds(low, half), :].astype(BF)
        other[...] = acc_ref[pl.ds(high, half), :].astype(BF)

    specs, operands = [pl.BlockSpec(memory_space=pltpu.SMEM)], [side.reshape(1)]
    for left, right in products:
        specs += [pl.BlockSpec((a.shape[0], step), lambda i: (0, i)) for a in left]
        specs += [whole(b.shape) for b in right]
        operands += [*left, *right]
    return pl.pallas_call(
        body,
        grid=(dp,),
        in_specs=specs,
        out_specs=[pl.BlockSpec((step // cut, cols), lambda i: (i, 0))] * cut,
        out_shape=[sds((model // cut, cols), BF)] * cut,
        scratch_shapes=[pltpu.VMEM((step, cols), F32)],
        compiler_params=params(14, 1),
        cost_estimate=cost(5),
        name=name,
    )(*operands)


def pieces(chunks):
    return [p for pair in chunks for p in pair]


def shards(
    tokens, cotangent, ln1_gain, ln1_bias, w_qkv, qv_bias, w_out, out_bias, scale_attn,
    ln2_gain, ln2_bias, w_fc1, fc1_bias, w_fc2, fc2_bias, scale_mlp,
):
    side = lax.axis_index("section")
    first = side == 0
    dp = lax.axis_size("dp")
    here = lax.axis_index("dp")
    chips = lax.axis_size("tensor") // 2
    rows, model = tokens.shape[2:]
    heads = qv_bias.shape[1]
    size = qv_bias.shape[2] * dp // 2
    width = heads * size
    units = w_fc1.shape[2]
    part = model // dp

    x0 = lax.dynamic_index_in_dim(tokens, side, 0, keepdims=False).reshape(rows, model)
    grad_top = lax.dynamic_index_in_dim(cotangent, side, 0, keepdims=False).reshape(rows, model)

    vectors = (ln1_gain, ln1_bias, out_bias, scale_attn, ln2_gain, ln2_bias, fc2_bias, scale_mlp)
    packed = jnp.concatenate(
        [v.reshape(-1) for v in vectors] + [fc1_bias.reshape(-1), qv_bias.reshape(-1)]
    )
    own_qkv = w_qkv.reshape(part, heads, 3, size).swapaxes(1, 2).reshape(part, 3 * width)
    own_att = jnp.concatenate([own_qkv, w_out[0].T], axis=1)
    cols = 4 * width
    tail = -(-packed.size // (16 * cols)) * 16
    packed = jnp.pad(packed, (0, tail * cols - packed.size)).reshape(tail, cols)
    mine_att = jnp.concatenate([half_of(own_att, side), packed])
    came_att = swap_section(jnp.concatenate([half_of(own_att, 1 - side), packed]))
    ring_att0 = jnp.where(first, mine_att, came_att)
    ring_att1 = jnp.where(first, came_att, mine_att)
    hops_att0 = direct(ring_att0)
    own_ff = jnp.concatenate([w_fc1[0], w_fc2[0].T], axis=1)
    rest_att = swap_section(tie(half_of(own_att, side), ring_att0))
    came_ff = swap_section(tie(half_of(own_ff, 1 - side), ring_att0))
    ring_ff0 = jnp.where(first, half_of(own_ff, side), came_ff)
    ring_ff1 = jnp.where(first, came_ff, half_of(own_ff, side))

    def other_half(own, rest):
        left = half_of(own, 1 - side)
        return jnp.where(first, left, rest), jnp.where(first, rest, left)

    def vectors_of(back):
        flat = in_order([v[-tail:] for v in back]).reshape(dp, -1).astype(F32)
        cut = 8 * part
        vec = flat[:, :cut].reshape(dp, 8, part).swapaxes(0, 1).reshape(8, model)
        bias_fc1 = flat[:, cut : cut + units // dp].reshape(1, units)
        size_qv = heads * 2 * size // dp
        qv = flat[:, cut + units // dp : cut + units // dp + size_qv]
        qv = qv.reshape(dp, heads, -1).swapaxes(0, 1).reshape(heads, 2, size)
        bias_qkv = jnp.stack([qv[:, 0], jnp.zeros_like(qv[:, 0]), qv[:, 1]]).reshape(1, 3 * width)
        return vec, bias_fc1, bias_qkv

    vec0, bias_fc1_0, bias_qkv_0 = vectors_of([ring_att0, *hops_att0])
    norm1 = norm_first(tie(x0, came_ff), vec0)
    rest_att0, rest_att1 = other_half(own_att, rest_att)
    backs = [swap_section(tie(v, norm1)) for v in hops_att0]
    att0 = assemble([(ring_att0, rest_att0), *zip(hops_att0, backs)], model)
    rest_ff = swap_section(tie(half_of(own_ff, side), att0))
    rest_ff0, rest_ff1 = other_half(own_ff, rest_ff)
    ff0, ff1 = Ring(tie(ring_ff0, norm1)), Ring(ring_ff1)
    att1 = Ring(ring_att1)
    att0 = tie(att0, *ff0.hop())

    chunks0, qkv0 = gather_tokens(norm1, lambda pair: project_qkv(pair, att0, bias_qkv_0))
    beside = ff0.hop()
    kept0, lse0, sames, others = attention([*qkv0[:-1], tie(qkv0[-1], *beside)], att0, size)
    beside = [rest_ff, *ff0.hop(qkv0[-1])]
    terms, _ = scatter_tokens(
        sames,
        tie(others, *beside),
        beside=lambda gate: [*ff0.back(gate), *ff0.back(gate), *att1.hop(gate)],
    )
    attended0, residual0, norm2 = after_attention(x0, terms, vec0)
    ff0.back(norm2)
    w_ff0 = assemble([(ring_ff0, rest_ff0), *zip(ff0.hops, ff0.backs)], model)
    beside = att1.hop(norm2)
    second0, mlp0 = gather_tokens(
        norm2, lambda pair: mlp_forward(pair, w_ff0, bias_fc1_0), beside
    )
    act0, slope0, sames, others = zip(*mlp0)
    beside = [*att1.hop(second0[-1][0]), *att1.back(second0[-1][0])]
    terms, _ = scatter_tokens(
        sames,
        [others[0], *[tie(v, *beside) for v in others[1:]]],
        beside=lambda gate: [*ff1.hop(gate), *att1.back(gate), *att1.back(gate)],
    )
    back = [tie(v, sames[-1]) for v in (ring_att1, *att1.hops)]
    vec1, bias_fc1_1, bias_qkv_1 = vectors_of(back)
    mlp_out0, y0, norm1 = after_mlp(residual0, terms, vec0, vec1)

    w_att1 = assemble([(ring_att1, rest_att1), *zip(att1.hops, att1.backs)], model)
    low1, sums_fc2_1 = start_back(grad_top, vec1)
    beside = [*ff1.hop(norm1), *ff1.back(norm1)]
    chunks1, qkv1 = gather_tokens(
        norm1, lambda pair: project_qkv(pair, w_att1, bias_qkv_1), beside
    )
    gate = chunks1[-1][0]
    came = [from_chip(tie(low1, gate), step) for step in range(1, chips)]
    beside = [*came, *ff1.hop(gate), *ff1.back(gate)]
    kept1, lse1, sames, others = attention(qkv1, w_att1, size)
    others = tie(others, *beside)
    grads1 = [(low1, core_swap(low1))] + [(v, core_swap(tie(v, lse1))) for v in came]
    terms, _ = scatter_tokens(
        sames, others, beside=lambda gate: [*ff1.back(gate), *pieces(grads1)]
    )
    attended1, residual1, norm2 = after_attention(y0, terms, vec1)
    w_ff1 = assemble([(ring_ff1, rest_ff1), *zip(ff1.hops, ff1.backs)], model)
    spare = list(grads1)
    second1, mlp1 = gather_tokens(
        norm2, lambda pair: mlp_both(pair, spare.pop(0), w_ff1, bias_fc1_1)
    )
    act1, dpre1, sums_fc1_1, sames_y1, others_y1, sames, others = zip(*mlp1)

    def grad_ff(second, dpre, grads, act):
        return lambda after: weight_grads(
            [
                (pieces(second), [late(tie(dpre[0], after)), *map(late, dpre[1:])]),
                (pieces(grads), [late(a) for a in act]),
            ],
            dp,
            side,
            "grad_ff",
        )

    def grad_att(chunks, dqkv, datt, kept):
        return lambda after: weight_grads(
            [
                (pieces(chunks), [tie(dqkv[0], after), *dqkv[1:]]),
                (pieces(datt), [late(a) for a in kept]),
            ],
            dp,
            side,
            "grad_att",
            False,
        )[0]

    old = [tuple(map(late, pair)) for pair in grads1]
    terms, g = scatter_tokens(sames, others, grad_ff(second1, dpre1, old, act1))
    sum_ff1 = RingSum((0, 1), *g)
    dres1, low, sums1 = back_second(grad_top, residual1, attended1, terms, vec1)
    came_y0 = lax.ppermute(tie(y0, low), "section", [(1, 0)])
    datt, _ = gather_tokens(low, lambda pair: pair[0], sum_ff1.step())
    sums_y1, local_y1 = core_sums(sames_y1, [tie(v, low) for v in others_y1])
    terms_y1 = send_sums([tie(v, datt[-1][0]) for v in sums_y1])
    beside = [came_y0, *terms_y1, *sum_ff1.step(low)]
    dqkv, sames, others, qkv_sums1 = attention_back(qkv1, kept1, lse1, datt, w_att1, size)
    old = [tuple(map(late, pair)) for pair in chunks1]
    terms, g = scatter_tokens(
        sames, tie(others, *beside), grad_att(old, dqkv, datt, kept1), sum_ff1.step
    )
    sum_att1 = RingSum((0, 1), g)
    dx1, low0, edge1 = back_first(dres1, late(y0), terms, vec1, late(mlp_out0), vec0)
    y1, sums_sc_1 = last_output(
        residual1, [tie(sames_y1[0], low0), *terms_y1, local_y1], grad_top, vec1
    )

    slopes = list(slope0)
    grads0, mlp_back0 = gather_tokens(
        low0,
        lambda pair: mlp_backward(pair, slopes.pop(0), w_ff0, bias_fc1_0),
        [y1, *sum_ff1.step(low0)],
    )
    dpre0, sums_fc1_0, sames, others = zip(*mlp_back0)
    old = [tuple(map(late, pair)) for pair in second0]
    sum_att1.step()
    terms, g = scatter_tokens(
        sames,
        others,
        grad_ff(old, dpre0, grads0, act0),
        lambda gate: [*sum_ff1.step(gate), *sum_att1.step(gate)],
    )
    sum_ff0 = RingSum((1, 0), *g)
    dres0, low, sums0 = back_second(
        dx1, late(residual0), late(attended0), terms, vec0
    )
    beside = [*sum_att1.step(low), *sum_ff0.step(low)]
    datt, _ = gather_tokens(low, lambda pair: pair[0], beside)
    beside = [*sum_att1.step(low), *sum_ff0.step(low)]
    dqkv, sames, others, qkv_sums0 = attention_back(qkv0, kept0, lse0, datt, att0, size)
    old = [tuple(map(late, pair)) for pair in chunks0]
    terms, g = scatter_tokens(
        sames, tie(others, *beside), grad_att(old, dqkv, datt, kept0), sum_ff0.step
    )
    sum_att0 = RingSum((1, 0), g)
    sum_att0.step()
    hop_att0 = sum_att0.step()
    dx0, edge0 = back_first(dres0, x0, terms, vec0)
    came_dx0 = lax.ppermute(dx0, "section", [(1, 0)])
    second_round = [*sum_ff0.step(dx0), *sum_att0.step()]
    sum_att1.step(second_round[-1])
    sum_ff0.step()
    ready = sum_att0.step()[-1]
    came_y1 = lax.ppermute(tie(y1, second_round[-1]), "section", [(0, 1)])
    came_dx1 = lax.ppermute(tie(dx1, ready), "section", [(0, 1)])
    sum_att0.step()

    def both(low, high, came_low, came_high):
        mine = jnp.where(first, low, high)
        came = jnp.where(first, came_low, came_high)
        return jnp.stack([jnp.where(first, mine, came), jnp.where(first, came, mine)])[None, :, None]

    block_out = both(tie(y0, ready), y1, came_y0, came_y1)
    input_grads = both(dx0, dx1, came_dx0, came_dx1)

    def by_unit(qkv_sums, unit_sums):
        q = qkv_sums[:, :width].reshape(heads, 1, size)
        v = qkv_sums[:, 2 * width :].reshape(heads, 1, size)
        bias = jnp.concatenate([q, v], 1).reshape(heads, dp, -1).swapaxes(0, 1).reshape(dp, -1)
        return jnp.concatenate([bias, unit_sums.reshape(dp, -1)], axis=1)

    unit0 = by_unit(tie(qkv_sums0, dx0), sum(sums_fc1_0))
    unit1 = by_unit(tie(qkv_sums1, dx0), sum(sums_fc1_1))
    vec = jnp.concatenate(
        [edge0[:2], sums0[:4], edge1[2:4], edge1[:2], sums1[:4], sums_sc_1[:1], sums_fc2_1[:1]]
    )
    vec = tie(vec, *hop_att0)
    vec = vec + core_swap(vec)
    vec = tie(sum([from_chip(vec, step) for step in range(1, chips)], vec), *second_round)
    vec = vec.reshape(2, 8, dp, part).swapaxes(1, 2).reshape(2, dp, 8 * part)
    low = jnp.concatenate([vec[0], unit0], axis=1)
    high = jnp.concatenate([vec[1], unit1], axis=1)
    own = jnp.where(first, low, high) + swap_section(jnp.where(first, high, low))
    vec = lax.dynamic_slice_in_dim(own, here, 1, 0)
    for step in range(1, dp):
        pairs = [(i, (i + step) % dp) for i in range(dp)]
        other = lax.dynamic_slice_in_dim(own, lax.rem(here + step, dp), 1, 0)
        vec = vec + lax.ppermute(other, "dp", pairs)
    cut = 8 * part + heads * (2 * size // dp)
    bias_grad = vec[:, 8 * part : cut].reshape(1, heads, -1)
    fc1_grad = vec[:, cut:].reshape(1, 1, -1)
    g_ln1, b_ln1, g_ln2, b_ln2, g_sc_attn, g_out_bias, g_sc_mlp, g_fc2_bias = (
        vec[:, i * part : (i + 1) * part] for i in range(8)
    )

    def owned(low, high):
        top = jnp.where(first, low.own, high.came.astype(F32))
        bottom = jnp.where(first, low.came.astype(F32), high.own)
        return jnp.concatenate([top, bottom], 0)

    g_ff = owned(sum_ff0, sum_ff1)
    g_att = jnp.where(
        first,
        sum_att0.own + sum_att0.came.astype(F32),
        sum_att1.own + sum_att1.came.astype(F32),
    )
    g_qkv = g_att[:, : 3 * width].reshape(part, 3, heads, size).swapaxes(1, 2)
    g_qkv = g_qkv.reshape(1, part, 3 * width)
    g_out = g_att[:, 3 * width :].T[None]
    g_fc1 = g_ff[:, :units][None]
    g_fc2 = g_ff[:, units:].T[None]
    return (
        block_out, input_grads, g_ln1, b_ln1, g_qkv, bias_grad, g_out, g_out_bias, g_sc_attn,
        g_ln2, b_ln2, g_fc1, fc1_grad, g_fc2, g_fc2_bias, g_sc_mlp,
    )


def solution(mesh):
    vec = P("section", "dp")
    by_row = P("section", "dp", "tensor")
    by_unit = P("section", "tensor", "dp")
    data = P(None, "dp", "tensor", None)
    split = P("section", None, "dp", "tensor", None)
    given = (
        vec, vec, by_row, by_unit, by_unit, vec, vec, vec, vec, by_row, by_unit, by_unit, vec, vec,
    )
    return jax.shard_map(
        shards,
        mesh=mesh,
        in_specs=(data, data) + given,
        out_specs=(split, split) + given,
        check_vma=False,
    )
```

```python
from functools import partial

import jax
import jax.numpy as jnp
from jax import lax
from jax.experimental import pallas as pl
from jax.experimental.pallas import tpu as pltpu
from jax.sharding import PartitionSpec as P

EPSILON = 1e-06
BF = jnp.bfloat16
F32 = jnp.float32
MIB = 1 << 20

LN1_G, LN1_B, OUT_B, SC_ATTN, LN2_G, LN2_B, FC2_B, SC_MLP = range(8)


def dot(a, b):
    return lax.dot_general(a, b, (((1,), (0,)), ((), ())), preferred_element_type=F32)


def dot_bt(a, b):
    return lax.dot_general(a, b, (((1,), (1,)), ((), ())), preferred_element_type=F32)


def dot_at(a, b):
    return lax.dot_general(a, b, (((0,), (0,)), ((), ())), preferred_element_type=F32)


def turn(v):
    return v.astype(F32).T


def params(limit, grid=0):
    return pltpu.CompilerParams(
        vmem_limit_bytes=limit * MIB,
        dimension_semantics=("arbitrary",) * grid if grid else None,
    )


def late(v):
    return pltpu.with_memory_space_constraint(v, pltpu.HBM)


def whole(shape):
    return pl.BlockSpec(shape, lambda i: (0, 0), pipeline_mode=pl.Buffered(1))


def cost(micros):
    return pl.CostEstimate(flops=int(micros * 1.15e9), bytes_accessed=0, transcendentals=0)


def sds(shape, dtype):
    return jax.ShapeDtypeStruct(shape, dtype)


def core_swap(v):
    count = lax.axis_size("tensor")
    return lax.ppermute(v, "tensor", [(i, i ^ 1) for i in range(count)])


def from_chip(v, step):
    count = lax.axis_size("tensor")
    chips = count // 2
    pairs = [(((i // 2 + step) % chips) * 2 + i % 2, i) for i in range(count)]
    return lax.ppermute(v, "tensor", pairs)


def tie(v, *after):
    if not after:
        return v
    return lax.optimization_barrier((v, *after))[0]


def tie_all(vs, *after):
    return lax.optimization_barrier((*vs, *after))[: len(vs)]


def gather_tokens(own, work, beside=()):
    chips = lax.axis_size("tensor") // 2
    came = [from_chip(own, step) for step in range(1, chips)]
    chunks = [(own, core_swap(own))]
    results = [work(chunks[0])]
    for same in came:
        same = tie(same, results[-1], *beside)
        chunks.append((same, core_swap(same)))
        results.append(work(chunks[-1]))
    return chunks, results


def core_sums(sames, others):
    chips, rows = len(sames), sames[0].shape[0]
    if isinstance(others, (list, tuple)):
        came = [core_swap(v) for v in others[1:]]
        local = core_swap(tie(others[0], came[-1]))
    else:
        local = core_swap(others)
        came = [local[c * rows : (c + 1) * rows] for c in range(1, chips)]
    sums = [(a.astype(F32) + b.astype(F32)).astype(BF) for a, b in zip(sames[1:], came)]
    return sums, local


def send_sums(sums):
    chips = len(sums) + 1
    return [from_chip(both, chips - step) for step, both in enumerate(sums, 1)]


def scatter_tokens(sames, others, work=None, beside=None):
    sums, local = core_sums(sames, others)
    terms = send_sums(sums)
    made = work(sums[-1]) if work else local
    more = beside(sums[-1]) if beside else ()
    terms = [tie(t, made, local, *more) for t in terms]
    return [late(sames[0]), *terms, local], made


def swap_section(v):
    return lax.ppermute(v, "section", [(0, 1), (1, 0)])


def assemble(shards, rows):
    count = len(shards)
    cut = len(shards[0])
    size, cols = shards[0][0].shape
    place = jnp.stack([lax.axis_index("dp"), lax.axis_index("section")])

    def body(place_ref, *refs):
        out_ref, sems = refs[count * cut :]
        z, x = place_ref[0], place_ref[1]
        started = []
        for k in range(count):
            base = lax.rem(z + (count - k), count) * (cut * size)
            for i, at in enumerate([base] if cut == 1 else [base + x * size, base + (1 - x) * size]):
                copy = pltpu.make_async_copy(
                    refs[k * cut + i],
                    out_ref.at[pl.ds(pl.multiple_of(at, size), size), :],
                    sems.at[k * cut + i],
                )
                copy.start()
                started.append(copy)
        for copy in started:
            copy.wait()

    hbm = pl.BlockSpec(memory_space=pl.ANY)
    return pl.pallas_call(
        body,
        in_specs=[pl.BlockSpec(memory_space=pltpu.SMEM)] + [hbm] * (count * cut),
        out_specs=pl.BlockSpec(memory_space=pltpu.VMEM),
        out_shape=sds((rows, cols), shards[0][0].dtype),
        scratch_shapes=[pltpu.SemaphoreType.DMA((count * cut,))],
        compiler_params=params(6),
        cost_estimate=cost(2),
        name="assemble",
    )(place, *[v for shard in shards for v in shard])


def half_of(v, which):
    half = v.shape[0] // 2
    return lax.dynamic_slice_in_dim(v, which * half, half, 0)


def direct(own):
    count = lax.axis_size("dp")
    return [
        lax.ppermute(own, "dp", [(i, (i + step) % count) for i in range(count)])
        for step in range(1, count)
    ]


def third(values, index):
    cuts = [-(-len(values) * i // 3) for i in range(4)]
    return values[cuts[index] : cuts[index + 1]]


class Ring:
    def __init__(self, own):
        self.last, self.hops, self.backs, self.at, self.back_at = own, [], [], 0, 0

    def hop(self, *gate):
        count = lax.axis_size("dp")
        pairs = [(i, (i + 1) % count) for i in range(count)]
        new = []
        for i in range(len(third(range(count - 1), self.at))):
            self.last = lax.ppermute(tie(self.last, *gate) if i == 0 else self.last, "dp", pairs)
            new.append(self.last)
        self.hops += new
        self.at += 1
        return new

    def back(self, *gate):
        count = lax.axis_size("dp")
        which = third(range(count - 1), self.back_at)
        new = [swap_section(tie(self.hops[i], *gate)) for i in which]
        self.backs += new
        self.back_at += 1
        return new


def gather_small(v, first, after):
    count = lax.axis_size("dp")
    came = swap_section(v)
    own = tie(jnp.stack([jnp.where(first, v, came), jnp.where(first, came, v)]), after)
    ahead = [own]
    for step in range(1, count):
        ahead.append(lax.ppermute(own, "dp", [(i, (i - step) % count) for i in range(count)]))
    twice = jnp.stack(ahead + ahead, axis=1)
    return lax.dynamic_slice_in_dim(twice, count - lax.axis_index("dp"), count, 1)


def dp_rows(v, back):
    dp = lax.axis_size("dp")
    part = v.shape[0] // dp
    place = lax.rem(lax.axis_index("dp") + (dp - back), dp)
    return lax.dynamic_slice_in_dim(v, place * part, part, 0)


class RingSum:
    def __init__(self, pair, mine, other=None):
        self.mine, self.other, self.pair = mine, other, pair
        self.terms, self.at, self.done = [], 0, 0

    def total(self, gate=()):
        first = tie(self.terms[0], *gate)
        return sum(t.astype(F32) for t in [first, *self.terms[1:]])

    def one(self, gate):
        dp = lax.axis_size("dp")
        self.done += 1
        new = []
        if self.terms:
            pairs = [(i, (i + 1) % dp) for i in range(dp)]
            new.append(lax.ppermute(self.total(gate).astype(BF), "dp", pairs))
        if self.other is not None:
            new.append(swap_section(tie(dp_rows(self.other, self.done), *gate)))
        self.terms = [*new, dp_rows(self.mine, self.done)]
        return new

    def step(self, *gate):
        self.at += 1
        if self.at == 5:
            self.own = self.total(gate)
            self.came = lax.ppermute(self.own.astype(BF), "section", [self.pair])
            return [self.came]
        count = 1 if self.at == 1 else len(third(range(lax.axis_size("dp") - 1), self.at - 2))
        return [v for i in range(count) for v in self.one(gate if i == 0 else ())]


def standardize(v):
    centred = v - jnp.mean(v, axis=-1, keepdims=True)
    var = jnp.mean(centred * centred, axis=-1, keepdims=True)
    scale = lax.rsqrt(var + EPSILON)
    return centred * scale, scale


def norm_of(v, vec, gain, shift):
    return (standardize(v)[0] * vec[gain : gain + 1, :] + vec[shift : shift + 1, :]).astype(BF)


def norm_back(v, grad, gain):
    xh, scale = standardize(v)
    dxh = grad * gain
    inner = jnp.mean(dxh * xh, axis=-1, keepdims=True)
    out = scale * (dxh - jnp.mean(dxh, axis=-1, keepdims=True) - xh * inner)
    return out, grad * xh


def total(refs):
    out = refs[0][...].astype(F32)
    for ref in refs[1:]:
        out = out + ref[...].astype(F32)
    return out


def fold(v, op):
    return op(v.reshape(-1, 8, v.shape[1]), axis=0)


def add_rows(ref, rows):
    for k, row in enumerate(rows):
        ref[8 * k : 8 * k + 8, :] += fold(row, jnp.sum)


def rowwise(body, row_ins, fulls, row_outs, sums, name):
    rows, width = row_ins[0].shape
    step = min(128, rows)
    some, outs = len(row_ins) + len(fulls), len(row_outs)

    def kernel(*refs):
        if not sums:
            body(*refs)
            return
        sum_ref, acc_ref = refs[some + outs :]

        @pl.when(pl.program_id(0) == 0)
        def _():
            acc_ref[...] = jnp.zeros_like(acc_ref)

        body(*refs[: some + outs], acc_ref)

        @pl.when(pl.program_id(0) == pl.num_programs(0) - 1)
        def _():
            for k in range(sums):
                sum_ref[k : k + 1, :] = jnp.sum(
                    acc_ref[8 * k : 8 * k + 8, :], axis=0, keepdims=True
                )

    out_shape = [sds((rows, width), d) for d in row_outs]
    out_shape += [sds((sums, width), F32)] if sums else []
    block = pl.BlockSpec((step, width), lambda i: (i, 0))
    return pl.pallas_call(
        kernel,
        grid=(rows // step,),
        in_specs=[block] * len(row_ins) + [whole(a.shape) for a in fulls],
        out_specs=[block] * outs + ([whole((sums, width))] if sums else []),
        out_shape=out_shape,
        scratch_shapes=[pltpu.VMEM((8 * sums, width), F32)] if sums else [],
        compiler_params=params(8, 1),
        cost_estimate=cost(2),
        name=name,
    )(*row_ins, *fulls)


def norm_first(x, vec):
    def body(x_ref, vec_ref, out_ref):
        out_ref[...] = norm_of(x_ref[...].astype(F32), vec_ref[...], LN1_G, LN1_B)

    return rowwise(body, [x], [vec], [BF], 0, "norm_first")[0]


def after_attention(x, terms, vec):
    count = len(terms)

    def body(*refs):
        x_ref, term_refs, vec_ref = refs[0], refs[1 : 1 + count], refs[1 + count]
        att_ref, res_ref, norm_ref = refs[2 + count :]
        v = vec_ref[...]
        attended = total(term_refs) + v[OUT_B : OUT_B + 1, :]
        residual = x_ref[...].astype(F32) + v[SC_ATTN : SC_ATTN + 1, :] * attended
        att_ref[...] = attended.astype(BF)
        res_ref[...] = residual
        norm_ref[...] = norm_of(residual, v, LN2_G, LN2_B)

    return rowwise(body, [x, *terms], [vec], [BF, F32, BF], 0, "after_attention")


def after_mlp(residual, terms, vec, vec_next):
    count = len(terms)

    def body(*refs):
        res_ref, term_refs = refs[0], refs[1 : 1 + count]
        vec_ref, next_ref, mlp_ref, y_ref, norm_ref = refs[1 + count :]
        v = vec_ref[...]
        mlp = total(term_refs) + v[FC2_B : FC2_B + 1, :]
        y = (res_ref[...] + v[SC_MLP : SC_MLP + 1, :] * mlp).astype(BF)
        mlp_ref[...] = mlp.astype(BF)
        y_ref[...] = y
        norm_ref[...] = norm_of(y.astype(F32), next_ref[...], LN1_G, LN1_B)

    return rowwise(body, [residual, *terms], [vec, vec_next], [BF, BF, BF], 0, "after_mlp")


def last_output(residual, terms, grad, vec):
    count = len(terms)

    def body(*refs):
        res_ref, term_refs = refs[0], refs[1 : 1 + count]
        grad_ref, vec_ref, y_ref, sum_ref = refs[1 + count :]
        v = vec_ref[...]
        mlp = total(term_refs) + v[FC2_B : FC2_B + 1, :]
        y_ref[...] = (res_ref[...] + v[SC_MLP : SC_MLP + 1, :] * mlp).astype(BF)
        add_rows(sum_ref, [grad_ref[...].astype(F32) * mlp])

    return rowwise(body, [residual, *terms, grad], [vec], [BF], 1, "last_output")


def start_back(grad, vec):
    def body(grad_ref, vec_ref, out_ref, sum_ref):
        low = (vec_ref[...][SC_MLP : SC_MLP + 1, :] * grad_ref[...].astype(F32)).astype(BF)
        out_ref[...] = low
        add_rows(sum_ref, [low.astype(F32)])

    return rowwise(body, [grad], [vec], [BF], 1, "start_back")


def back_second(grad, residual, attended, terms, vec):
    count = len(terms)

    def body(*refs):
        grad_ref, res_ref, att_ref = refs[:3]
        term_refs = refs[3 : 3 + count]
        vec_ref, dres_ref, low_ref, sum_ref = refs[3 + count :]
        v = vec_ref[...]
        dn = total(term_refs)
        back, dgain = norm_back(res_ref[...], dn, v[LN2_G : LN2_G + 1, :])
        dres = grad_ref[...].astype(F32) + back
        low = (v[SC_ATTN : SC_ATTN + 1, :] * dres).astype(BF)
        dres_ref[...] = dres
        low_ref[...] = low
        add_rows(sum_ref, [dgain, dn, dres * att_ref[...].astype(F32), low.astype(F32)])

    return rowwise(
        body, [grad, residual, attended, *terms], [vec], [F32, BF], 4, "back_second"
    )


def back_first(dres, x, terms, vec, mlp_below=None, vec_below=None):
    count = len(terms)
    below = mlp_below is not None

    def body(*refs):
        dres_ref, x_ref = refs[:2]
        term_refs = refs[2 : 2 + count]
        rest = refs[2 + count :]
        if below:
            mlp_ref, vec_ref, under_ref, dx_ref, low_ref, sum_ref = rest
        else:
            vec_ref, dx_ref, sum_ref = rest
        v = vec_ref[...]
        dn = total(term_refs)
        back, dgain = norm_back(x_ref[...].astype(F32), dn, v[LN1_G : LN1_G + 1, :])
        dx = (dres_ref[...] + back).astype(BF)
        dx_ref[...] = dx
        rows = [dgain, dn]
        if below:
            wide = dx.astype(F32)
            low = (under_ref[...][SC_MLP : SC_MLP + 1, :] * wide).astype(BF)
            low_ref[...] = low
            rows += [wide * mlp_ref[...].astype(F32), low.astype(F32)]
        add_rows(sum_ref, rows)

    row_ins = [dres, x, *terms] + ([mlp_below] if below else [])
    fulls = [vec] + ([vec_below] if below else [])
    return rowwise(body, row_ins, fulls, [BF, BF] if below else [BF], 4 if below else 2, "back_first")


def project_qkv(pair, weight, bias):
    rows, width = pair[0].shape
    cols = bias.shape[1]

    def body(a_ref, b_ref, w_ref, bias_ref, out_ref):
        w = w_ref[...]
        shift = bias_ref[...]
        out_ref[:rows, :] = (dot(a_ref[...], w) + shift).astype(BF)
        out_ref[rows:, :] = (dot(b_ref[...], w) + shift).astype(BF)

    return pl.pallas_call(
        body,
        grid=(1,),
        in_specs=[
            whole((rows, width)), whole((rows, width)), whole((width, cols)), whole((1, cols))
        ],
        out_specs=whole((2 * rows, cols)),
        out_shape=sds((2 * rows, cols), BF),
        compiler_params=params(6, 1),
        cost_estimate=cost(2),
        name="project_qkv",
    )(*pair, weight, bias)


def head_rows(v, head, size):
    rows = lax.broadcasted_iota(jnp.int32, v.shape, 0)
    return jnp.where(rows // size == head, v, jnp.zeros_like(v))


def head_cols(v, head, size):
    cols = lax.broadcasted_iota(jnp.int32, v.shape, 1)
    return jnp.where(cols // size == head, v, jnp.zeros_like(v))


def attention(packed, weight, size):
    chips = len(packed)
    span = packed[0].shape[0]
    half = span // 2
    width = packed[0].shape[1] // 3
    seq = chips * span
    heads = width // size
    model = weight.shape[0]
    step = min(256, seq)
    chunk = min(128, seq)
    score = size**-0.5

    def body(*refs):
        in_refs, w_ref = refs[:chips], refs[chips]
        head_refs = refs[chips + 1 : 2 * chips + 1]
        lse_ref = refs[2 * chips + 1]
        same_refs, other_ref = refs[2 * chips + 2 : 3 * chips + 2], refs[3 * chips + 2]
        k_ref, qt_ref, vt_ref, ot_ref, s_ref, p_ref = refs[3 * chips + 3 :]
        for c in range(chips):
            at = slice(c * span, (c + 1) * span)
            k_ref[at, :] = in_refs[c][:, width : 2 * width]
            qt_ref[:, at] = (turn(in_refs[c][:, :width]) * score).astype(BF)
            vt_ref[:, at] = turn(in_refs[c][:, 2 * width :]).astype(BF)

        def one(i, carry):
            at = pl.ds(pl.multiple_of(i * step, step), step)
            q = qt_ref[:, at]
            s_ref[0] = dot(k_ref[...], head_rows(q, 0, size))
            for h in range(heads):
                if h + 1 < heads:
                    s_ref[(h + 1) % 2] = dot(k_ref[...], head_rows(q, h + 1, size))
                now = h % 2
                top = fold(s_ref[now, :chunk, :], jnp.max)
                for r in range(chunk, seq, chunk):
                    top = jnp.maximum(top, fold(s_ref[now, r : r + chunk, :], jnp.max))
                top = jnp.max(top, axis=0, keepdims=True)
                norm = jnp.zeros((8, step), F32)
                for r in range(0, seq, chunk):
                    p = jnp.exp(s_ref[now, r : r + chunk, :] - top)
                    norm = norm + fold(p, jnp.sum)
                    p_ref[now, r : r + chunk, :] = p.astype(BF)
                norm = jnp.sum(norm, axis=0, keepdims=True)
                rows = slice(h * size, (h + 1) * size)
                ot_ref[rows, at] = dot(vt_ref[rows, :], p_ref[now]) / norm
                lse_ref[h : h + 1, at] = top + jnp.log(norm)
            return carry

        lax.fori_loop(0, seq // step, one, 0)
        for c in range(chips):
            at = slice(c * span, (c + 1) * span)
            o = ot_ref[:, at].T.astype(BF)
            head_refs[c][...] = o
            same_refs[c][...] = dot_bt(o[:half], w_ref[...]).astype(BF)
            other_ref[c * half : (c + 1) * half, :] = dot_bt(o[half:], w_ref[...]).astype(BF)

    out = pl.pallas_call(
        body,
        grid=(1,),
        in_specs=[whole((span, 3 * width))] * chips
        + [pl.BlockSpec((model, width), lambda i: (0, 3), pipeline_mode=pl.Buffered(1))],
        out_specs=[whole((span, width))] * chips
        + [whole((heads, seq))]
        + [whole((half, model))] * chips
        + [whole((seq // 2, model))],
        out_shape=[pltpu.HBM((span, width), BF)] * chips
        + [sds((heads, seq), F32), pltpu.HBM((half, model), BF)]
        + [sds((half, model), BF)] * (chips - 1)
        + [sds((seq // 2, model), BF)],
        scratch_shapes=[
            pltpu.VMEM((seq, width), BF),
            pltpu.VMEM((width, seq), BF),
            pltpu.VMEM((width, seq), BF),
            pltpu.VMEM((width, seq), F32),
            pltpu.VMEM((2, seq, step), F32),
            pltpu.VMEM((2, seq, step), BF),
        ],
        compiler_params=params(14, 1),
        cost_estimate=cost(9),
        name="attention",
    )(*packed, weight)
    return out[:chips], out[chips], out[chips + 1 : -1], out[-1]


def attention_back(packed, heads_kept, lse, datt, weight, size):
    chips = len(packed)
    span = packed[0].shape[0]
    half = span // 2
    width = packed[0].shape[1] // 3
    seq = chips * span
    heads = width // size
    model = weight.shape[0]
    step = min(256, seq)
    chunk = min(128, seq)
    score = size**-0.5

    def body(*refs):
        at = 0

        def take(count):
            nonlocal at
            at += count
            return refs[at - count : at]

        in_refs, kept_refs = take(chips), take(chips)
        (lse_ref,) = take(1)
        datt_refs = take(2 * chips)
        (w_ref,) = take(1)
        dqkv_refs = take(chips)
        same_refs = take(chips)
        other_ref, sum_ref = take(2)
        k_ref, v_ref, kt_ref, qt_ref, q_ref, do_ref, dot_ref = take(7)
        inner_ref, s_ref, g_ref, p_ref, ds_ref, dk_ref, dv_ref, dqt_ref = take(8)
        for c in range(chips):
            rows = slice(c * span, (c + 1) * span)
            q = in_refs[c][:, :width].astype(F32) * score
            k = in_refs[c][:, width : 2 * width]
            q_ref[rows, :] = q.astype(BF)
            qt_ref[:, rows] = q.T.astype(BF)
            k_ref[rows, :] = k
            kt_ref[:, rows] = turn(k).astype(BF)
            v_ref[rows, :] = in_refs[c][:, 2 * width :]
            for b in range(2):
                d = dot(datt_refs[2 * c + b][...], w_ref[:, 3 * width :]).astype(BF)
                here = slice(c * span + b * half, c * span + (b + 1) * half)
                do_ref[here, :] = d
                dt = turn(d)
                dot_ref[:, here] = dt.astype(BF)
                prod = dt * turn(kept_refs[c][b * half : (b + 1) * half, :])
                for h in range(heads):
                    inner_ref[h : h + 1, here] = jnp.sum(
                        prod[h * size : (h + 1) * size, :], axis=0, keepdims=True
                    )

        def one(i, carry):
            at = pl.ds(pl.multiple_of(i * step, step), step)
            qt = qt_ref[:, at]
            dot_t = dot_ref[:, at]
            q = q_ref[at, :]
            do = do_ref[at, :]

            def scores(h):
                s_ref[h % 2] = dot(k_ref[...], head_rows(qt, h, size))
                g_ref[h % 2] = dot(v_ref[...], head_rows(dot_t, h, size))

            scores(0)
            for h in range(heads):
                if h + 1 < heads:
                    scores(h + 1)
                now = h % 2
                cols = slice(h * step, (h + 1) * step)
                lse = lse_ref[h : h + 1, at]
                inner = inner_ref[h : h + 1, at]
                for r in range(0, seq, chunk):
                    p = jnp.exp(s_ref[now, r : r + chunk, :] - lse)
                    ds = p * (g_ref[now, r : r + chunk, :] - inner)
                    p_ref[r : r + chunk, cols] = p.astype(BF)
                    ds_ref[r : r + chunk, cols] = ds.astype(BF)
                rows = slice(h * size, (h + 1) * size)
                dqt_ref[rows, at] = dot(kt_ref[rows, :], ds_ref[:, cols]) * score
            dv = dot(p_ref[...], jnp.concatenate([head_cols(do, h, size) for h in range(heads)], 0))
            dk = dot(ds_ref[...], jnp.concatenate([head_cols(q, h, size) for h in range(heads)], 0))

            @pl.when(i == 0)
            def _():
                dv_ref[...] = dv
                dk_ref[...] = dk

            @pl.when(i > 0)
            def _():
                dv_ref[...] += dv
                dk_ref[...] += dk

            return carry

        lax.fori_loop(0, seq // step, one, 0)
        for c in range(chips):
            rows = slice(c * span, (c + 1) * span)
            out = dqkv_refs[c]
            out[:, :width] = dqt_ref[:, rows].T.astype(BF)
            out[:, width : 2 * width] = dk_ref[rows, :].astype(BF)
            out[:, 2 * width :] = dv_ref[rows, :].astype(BF)
            sums = jnp.sum(out[...].astype(F32), axis=0, keepdims=True)
            if c == 0:
                sum_ref[...] = sums
            else:
                sum_ref[...] += sums
            w = w_ref[:, : 3 * width]
            same_refs[c][...] = dot_bt(out[:half, :], w).astype(BF)
            other_ref[c * half : (c + 1) * half, :] = dot_bt(out[half:, :], w).astype(BF)

    flat = [g for pair in datt for g in pair]
    out_shape = (
        [pltpu.HBM((span, 3 * width), BF)] * chips
        + [pltpu.HBM((half, model), BF)]
        + [sds((half, model), BF)] * (chips - 1)
        + [sds((seq // 2, model), BF), sds((1, 3 * width), F32)]
    )
    operands = (*map(late, (*packed, *heads_kept)), lse, *flat, late(weight))
    out = pl.pallas_call(
        body,
        grid=(1,),
        in_specs=[whole(a.shape) for a in operands],
        out_specs=[whole(a.shape) for a in out_shape],
        out_shape=out_shape,
        scratch_shapes=[
            pltpu.VMEM((seq, width), BF),
            pltpu.VMEM((seq, width), BF),
            pltpu.VMEM((width, seq), BF),
            pltpu.VMEM((width, seq), BF),
            pltpu.VMEM((seq, width), BF),
            pltpu.VMEM((seq, width), BF),
            pltpu.VMEM((width, seq), BF),
            pltpu.VMEM((heads, seq), F32),
            pltpu.VMEM((2, seq, step), F32),
            pltpu.VMEM((2, seq, step), F32),
            pltpu.VMEM((seq, heads * step), BF),
            pltpu.VMEM((seq, heads * step), BF),
            pltpu.VMEM((seq, width), F32),
            pltpu.VMEM((seq, width), F32),
            pltpu.VMEM((width, seq), F32),
        ],
        compiler_params=params(26, 1),
        cost_estimate=cost(15),
        name="attention_back",
    )(*operands)
    return out[:chips], out[chips : 2 * chips], out[2 * chips], out[2 * chips + 1]


def gelu_both(x):
    away = jnp.abs(x)
    t = 1.0 / (1.0 + (0.3275911 * 0.5**0.5) * away)
    bell = jnp.exp(-0.5 * (x * x))
    poly = t * (
        0.127414796
        + t * (-0.142248368 + t * (0.7107068705 + t * (-0.7265760135 + t * 0.5307027145)))
    )
    tail = poly * bell
    phi = jnp.where(x >= 0, 1.0 - tail, tail)
    return x * phi, phi + x * (bell * 0.3989422804014327)


def mlp_call(body, pairs, extra, weight, bias, outs, parts, scratch, name):
    rows, model = pairs[0].shape
    units = weight.shape[1] // 2
    step = min(256, units)
    blocks = units // step
    cols = lambda j: (0, j)
    in_specs = [whole((rows, model)) for _ in pairs]
    in_specs += [pl.BlockSpec((2 * rows, step), cols) for _ in extra]
    in_specs += [
        pl.BlockSpec((model, step), cols),
        pl.BlockSpec((model, step), lambda j: (0, blocks + j)),
        pl.BlockSpec((1, step), cols),
    ]
    out_specs = [pl.BlockSpec((2 * rows, step), cols) for _ in outs]
    out_specs += [pl.BlockSpec((1, step), cols)]
    out_specs += [whole((rows, model))] * (2 * parts)
    out_shape = [pltpu.HBM((2 * rows, units), d) for d in outs] + [sds((1, units), F32)]
    out_shape += [pltpu.HBM((rows, model), BF)] * (2 * parts)
    count = len(pairs) // 2
    return pl.pallas_call(
        body,
        grid=(blocks,),
        in_specs=in_specs,
        out_specs=out_specs,
        out_shape=out_shape,
        scratch_shapes=[pltpu.VMEM((2 * rows, model), F32)] * parts
        + [pltpu.VMEM((2 * rows, step), F32)] * scratch,
        compiler_params=params(8 + 5 * parts, 1),
        cost_estimate=cost(3 + 3 * parts),
        name=name,
    )(*pairs, *map(late, extra), weight, weight, bias)


def clear(*refs):
    @pl.when(pl.program_id(0) == 0)
    def _():
        for ref in refs:
            ref[...] = jnp.zeros_like(ref)


def finish(acc, low, high):
    rows = low.shape[0]

    @pl.when(pl.program_id(0) == pl.num_programs(0) - 1)
    def _():
        low[...] = acc[:rows, :].astype(BF)
        high[...] = acc[rows:, :].astype(BF)


CHUNK = 32


def mlp_forward(pair, weight, bias):
    rows = pair[0].shape[0]

    def body(a, b, w1_ref, w2_ref, bias_ref, act_ref, slope_ref, sum_ref, lo, hi, acc, pre):
        clear(acc, sum_ref)
        shift = bias_ref[...]
        for i, x in enumerate((a, b)):
            pre[i * rows : (i + 1) * rows, :] = dot(x[...], w1_ref[...])
        for i in range(2):
            at = slice(i * rows, (i + 1) * rows)
            for r in range(i * rows, (i + 1) * rows, CHUNK):
                act, slope = gelu_both(pre[r : r + CHUNK, :] + shift)
                act_ref[r : r + CHUNK, :] = act.astype(BF)
                slope_ref[r : r + CHUNK, :] = slope.astype(BF)
            acc[at, :] += dot_bt(act_ref[at, :], w2_ref[...])
        finish(acc, lo, hi)

    act, slope, _, lo, hi = mlp_call(body, pair, [], weight, bias, [BF, BF], 1, 1, "mlp_forward")
    return act, slope, lo, hi


def mlp_backward(pair, slope, weight, bias):
    rows = pair[0].shape[0]

    def body(a, b, slope_ref, w1_ref, w2_ref, bias_ref, dpre_ref, sum_ref, lo, hi, acc, pre):
        clear(acc)
        for i, g in enumerate((a, b)):
            pre[i * rows : (i + 1) * rows, :] = dot(g[...], w2_ref[...])
        sums = jnp.zeros((8, bias_ref.shape[1]), F32)
        for i in range(2):
            at = slice(i * rows, (i + 1) * rows)
            for r in range(i * rows, (i + 1) * rows, CHUNK):
                d = pre[r : r + CHUNK, :] * slope_ref[r : r + CHUNK, :].astype(F32)
                d = d.astype(BF)
                dpre_ref[r : r + CHUNK, :] = d
                sums = sums + fold(d.astype(F32), jnp.sum)
            acc[at, :] += dot_bt(dpre_ref[at, :], w1_ref[...])
        sum_ref[...] = jnp.sum(sums, axis=0, keepdims=True)
        finish(acc, lo, hi)

    dpre, sums, lo, hi = mlp_call(
        body, pair, [slope], weight, bias, [BF], 1, 1, "mlp_backward"
    )
    return dpre, sums, lo, hi


def mlp_both(pair, grads, weight, bias):
    rows = pair[0].shape[0]

    def body(
        a, b, c, d, w1_ref, w2_ref, bias_ref, act_ref, dpre_ref, sum_ref,
        lo, hi, blo, bhi, acc, back, pre, grad,
    ):
        clear(acc, back)
        shift = bias_ref[...]
        for i, (x, g) in enumerate(((a, c), (b, d))):
            at = slice(i * rows, (i + 1) * rows)
            pre[at, :] = dot(x[...], w1_ref[...])
            grad[at, :] = dot(g[...], w2_ref[...])
        sums = jnp.zeros((8, bias_ref.shape[1]), F32)
        for i in range(2):
            at = slice(i * rows, (i + 1) * rows)
            for r in range(i * rows, (i + 1) * rows, CHUNK):
                act, slope = gelu_both(pre[r : r + CHUNK, :] + shift)
                act_ref[r : r + CHUNK, :] = act.astype(BF)
                dpre = (grad[r : r + CHUNK, :] * slope).astype(BF)
                dpre_ref[r : r + CHUNK, :] = dpre
                sums = sums + fold(dpre.astype(F32), jnp.sum)
            back[at, :] += dot_bt(dpre_ref[at, :], w1_ref[...])
            acc[at, :] += dot_bt(act_ref[at, :], w2_ref[...])
        sum_ref[...] = jnp.sum(sums, axis=0, keepdims=True)
        finish(acc, lo, hi)
        finish(back, blo, bhi)

    act, dpre, sums, lo, hi, blo, bhi = mlp_call(
        body, [*pair, *grads], [], weight, bias, [BF, BF], 2, 2, "mlp_both"
    )
    return act, dpre, sums, lo, hi, blo, bhi


def weight_grads(products, dp, side, name, halves=True):
    model = products[0][0][0].shape[1]
    step = model // dp
    half = step // 2
    cut = 2 if halves else 1
    sizes = [(len(left), len(right), right[0].shape[1]) for left, right in products]
    cols = sum(n for _, _, n in sizes)

    def body(side_ref, *refs):
        acc_ref = refs[-1]
        mine, other = refs[-3:-1] if halves else (refs[-2], None)
        at = base = 0
        for many, few, n in sizes:
            lefts, rights = refs[at : at + many], refs[at + many : at + many + few]
            at += many + few
            ratio = many // few
            acc = None
            for i in range(many):
                size = lefts[i].shape[0]
                here = slice((i % ratio) * size, (i % ratio + 1) * size)
                term = dot_at(lefts[i][...], rights[i // ratio][here, :])
                acc = term if acc is None else acc + term
            if halves:
                acc_ref[:, base : base + n] = acc
            else:
                mine[:, base : base + n] = acc.astype(BF)
            base += n
        if not halves:
            return
        low = pl.multiple_of(side_ref[0] * half, half)
        high = pl.multiple_of((1 - side_ref[0]) * half, half)
        mine[...] = acc_ref[pl.ds(low, half), :].astype(BF)
        other[...] = acc_ref[pl.ds(high, half), :].astype(BF)

    specs, operands = [pl.BlockSpec(memory_space=pltpu.SMEM)], [side.reshape(1)]
    for left, right in products:
        specs += [pl.BlockSpec((a.shape[0], step), lambda i: (0, i)) for a in left]
        specs += [whole(b.shape) for b in right]
        operands += [*left, *right]
    return pl.pallas_call(
        body,
        grid=(dp,),
        in_specs=specs,
        out_specs=[pl.BlockSpec((step // cut, cols), lambda i: (i, 0))] * cut,
        out_shape=[sds((model // cut, cols), BF)] * cut,
        scratch_shapes=[pltpu.VMEM((step, cols), F32)],
        compiler_params=params(14, 1),
        cost_estimate=cost(5),
        name=name,
    )(*operands)


def pieces(chunks):
    return [p for pair in chunks for p in pair]


def shards(
    tokens, cotangent, ln1_gain, ln1_bias, w_qkv, qv_bias, w_out, out_bias, scale_attn,
    ln2_gain, ln2_bias, w_fc1, fc1_bias, w_fc2, fc2_bias, scale_mlp,
):
    side = lax.axis_index("section")
    first = side == 0
    dp = lax.axis_size("dp")
    here = lax.axis_index("dp")
    chips = lax.axis_size("tensor") // 2
    rows, model = tokens.shape[2:]
    heads = qv_bias.shape[1]
    size = qv_bias.shape[2] * dp // 2
    width = heads * size
    units = w_fc1.shape[2]
    part = model // dp

    x0 = lax.dynamic_index_in_dim(tokens, side, 0, keepdims=False).reshape(rows, model)
    grad_top = lax.dynamic_index_in_dim(cotangent, side, 0, keepdims=False).reshape(rows, model)

    vectors = (ln1_gain, ln1_bias, out_bias, scale_attn, ln2_gain, ln2_bias, fc2_bias, scale_mlp)
    packed = jnp.concatenate(
        [v.reshape(-1) for v in vectors] + [fc1_bias.reshape(-1), qv_bias.reshape(-1)]
    )
    own_qkv = w_qkv.reshape(part, heads, 3, size).swapaxes(1, 2).reshape(part, 3 * width)
    own_att = jnp.concatenate([own_qkv, w_out[0].T], axis=1)
    own_ff = jnp.concatenate([w_fc1[0], w_fc2[0].T], axis=1)

    def halves(own, came, rest):
        mine, left = half_of(own, side), half_of(own, 1 - side)
        return (
            (jnp.where(first, mine, came), jnp.where(first, left, rest)),
            (jnp.where(first, came, mine), jnp.where(first, rest, left)),
        )

    came_att = swap_section(half_of(own_att, 1 - side))
    ring_att0 = jnp.where(first, half_of(own_att, side), came_att)
    small = gather_small(packed, first, ring_att0).astype(F32)
    cut = 8 * part
    vecs = small[:, :, :cut].reshape(2, dp, 8, part).swapaxes(1, 2).reshape(2, 8, model)
    bias_fc1 = small[:, :, cut : cut + units // dp].reshape(2, 1, units)
    qv = small[:, :, cut + units // dp :].reshape(2, dp, heads, -1).swapaxes(1, 2)
    qv = qv.reshape(2, heads, 2, size)
    bias_qkv = jnp.stack([qv[:, :, 0], jnp.zeros_like(qv[:, :, 0]), qv[:, :, 1]], axis=1)
    bias_qkv = bias_qkv.reshape(2, 1, 3 * width)
    vecs = (vecs[0], vecs[1])

    norm1 = norm_first(tie(x0, came_att), vecs[0])
    came_ff = swap_section(tie(half_of(own_ff, 1 - side), came_att))
    rest_att = swap_section(tie(half_of(own_att, side), came_att))
    half_att0, half_att1 = halves(own_att, came_att, rest_att)
    ring_ff0 = jnp.where(first, half_of(own_ff, side), came_ff)

    def put_together(half, hops, backs):
        return assemble([half, *zip(hops, backs)], model)

    hops_att0 = direct(ring_att0)
    att0 = put_together(half_att0, hops_att0, [swap_section(tie(v, norm1)) for v in hops_att0])
    ff0, att1 = Ring(tie(ring_ff0, hops_att0[-1])), Ring(half_att1[0])
    hop_ff0 = ff0.hop()
    rest_ff = swap_section(tie(half_of(own_ff, side), hop_ff0[-1]))
    half_ff0, half_ff1 = halves(own_ff, came_ff, rest_ff)
    ff1 = Ring(half_ff1[0])

    def projection(weight, s):
        return lambda pair: project_qkv(pair, weight, bias_qkv[s])

    chunks0, qkv0 = gather_tokens(norm1, projection(att0, 0), hop_ff0)
    gate = qkv0[-1]
    kept0, lse0, sames, others = attention(qkv0, att0, size)
    beside = [rest_ff, *ff0.hop(gate)]
    terms, _ = scatter_tokens(
        sames,
        tie(others, *beside),
        beside=lambda gate: [*ff0.hop(gate), *ff0.back(gate), *ff0.back(gate)],
    )
    attended0, residual0, norm2 = after_attention(x0, terms, vecs[0])
    ff0.back(norm2)
    beside = att1.hop(norm2)
    w_ff0 = put_together(half_ff0, ff0.hops, ff0.backs)
    second0, mlp0 = gather_tokens(
        norm2, lambda pair: mlp_forward(pair, w_ff0, bias_fc1[0]), beside
    )
    act0, slope0, sames, others = zip(*mlp0)
    beside = [*att1.hop(second0[-1][0]), *att1.back(second0[-1][0])]
    terms, _ = scatter_tokens(
        sames,
        [others[0], *[tie(v, *beside) for v in others[1:]]],
        beside=lambda gate: [*att1.hop(gate), *ff1.hop(gate), *att1.back(gate)],
    )
    mlp_out0, y0, norm1 = after_mlp(residual0, terms, vecs[0], vecs[1])

    att1.back(norm1)
    w_att1 = put_together(half_att1, att1.hops, att1.backs)
    low1, sums_fc2_1 = start_back(grad_top, vecs[1])
    beside = [*ff1.hop(norm1), *ff1.back(norm1)]
    chunks1, qkv1 = gather_tokens(norm1, projection(w_att1, 1), beside)
    gate = chunks1[-1][0]
    came = [from_chip(tie(low1, gate), step) for step in range(1, chips)]
    beside = [*came, *ff1.hop(gate), *ff1.back(gate)]
    kept1, lse1, sames, others = attention(qkv1, w_att1, size)
    others = tie(others, *beside)
    grads1 = [(low1, core_swap(low1))] + [(v, core_swap(tie(v, lse1))) for v in came]
    terms, _ = scatter_tokens(
        sames, others, beside=lambda gate: [*ff1.back(gate), *pieces(grads1)]
    )
    attended1, residual1, norm2 = after_attention(y0, terms, vecs[1])
    w_ff1 = put_together(half_ff1, ff1.hops, ff1.backs)
    spare = list(grads1)
    second1, mlp1 = gather_tokens(
        norm2, lambda pair: mlp_both(pair, spare.pop(0), w_ff1, bias_fc1[1])
    )
    act1, dpre1, sums_fc1_1, sames_y1, others_y1, sames, others = zip(*mlp1)

    def grad_ff(second, dpre, grads, act):
        return lambda after: weight_grads(
            [
                (pieces(second), [late(tie(dpre[0], after)), *map(late, dpre[1:])]),
                (pieces(grads), [late(a) for a in act]),
            ],
            dp,
            side,
            "grad_ff",
        )

    def grad_att(chunks, dqkv, datt, kept):
        return lambda after: weight_grads(
            [
                (pieces(chunks), [late(tie(dqkv[0], after)), *map(late, dqkv[1:])]),
                (pieces(datt), [late(a) for a in kept]),
            ],
            dp,
            side,
            "grad_att",
            False,
        )[0]

    old = [tuple(map(late, pair)) for pair in grads1]
    terms, g = scatter_tokens(sames, others, grad_ff(second1, dpre1, old, act1))
    sum_ff1 = RingSum((0, 1), *g)
    dres1, low, sums1 = back_second(grad_top, residual1, attended1, terms, vecs[1])
    came_y0 = lax.ppermute(tie(y0, low), "section", [(1, 0)])
    datt, _ = gather_tokens(low, lambda pair: pair[0], sum_ff1.step())
    sums_y1, local_y1 = core_sums(sames_y1, [tie(v, low) for v in others_y1])
    terms_y1 = send_sums([tie(v, datt[-1][0]) for v in sums_y1])
    beside = [came_y0, *terms_y1, *sum_ff1.step(low)]
    dqkv, sames, others, qkv_sums1 = attention_back(qkv1, kept1, lse1, datt, w_att1, size)
    old = [tuple(map(late, pair)) for pair in chunks1]
    terms, g = scatter_tokens(
        sames, tie(others, *beside), grad_att(old, dqkv, datt, kept1), sum_ff1.step
    )
    sum_att1 = RingSum((0, 1), g)
    dx1, low0, edge1 = back_first(dres1, late(y0), terms, vecs[1], late(mlp_out0), vecs[0])
    y1, sums_sc_1 = last_output(
        residual1, [tie(sames_y1[0], low0), *terms_y1, local_y1], grad_top, vecs[1]
    )

    slopes = list(slope0)
    grads0, mlp_back0 = gather_tokens(
        low0,
        lambda pair: mlp_backward(pair, slopes.pop(0), w_ff0, bias_fc1[0]),
        [y1, *sum_ff1.step(low0)],
    )
    dpre0, sums_fc1_0, sames, others = zip(*mlp_back0)
    old = [tuple(map(late, pair)) for pair in second0]
    sum_att1.step()
    terms, g = scatter_tokens(
        sames,
        others,
        grad_ff(old, dpre0, grads0, act0),
        lambda gate: [*sum_ff1.step(gate), *sum_att1.step(gate)],
    )
    sum_ff0 = RingSum((1, 0), *g)
    dres0, low, sums0 = back_second(
        dx1, late(residual0), late(attended0), terms, vecs[0]
    )
    beside = [*sum_att1.step(low), *sum_ff0.step(low)]
    datt, _ = gather_tokens(low, lambda pair: pair[0], beside)
    beside = [*sum_att1.step(low), *sum_ff0.step(low)]
    dqkv, sames, others, qkv_sums0 = attention_back(qkv0, kept0, lse0, datt, att0, size)
    old = [tuple(map(late, pair)) for pair in chunks0]
    terms, g = scatter_tokens(
        sames, tie(others, *beside), grad_att(old, dqkv, datt, kept0), sum_ff0.step
    )
    sum_att0 = RingSum((1, 0), g)
    sum_att0.step()
    going = sum_att0.step()
    dx0, edge0 = back_first(dres0, x0, terms, vecs[0])
    came_dx0 = lax.ppermute(dx0, "section", [(1, 0)])
    step_ff0 = sum_ff0.step(dx0)
    second_hop = sum_att0.step(dx0)
    ready = sum_att0.step(*step_ff0)[-1]
    came_y1 = lax.ppermute(tie(y1, second_hop[-1]), "section", [(0, 1)])
    came_dx1 = lax.ppermute(tie(dx1, ready), "section", [(0, 1)])
    last_swaps = [came_y1, *sum_att1.step(second_hop[-1]), *sum_ff0.step()]
    sum_att0.step()

    def both(low, high, came_low, came_high):
        mine = jnp.where(first, low, high)
        came = jnp.where(first, came_low, came_high)
        return jnp.stack([jnp.where(first, mine, came), jnp.where(first, came, mine)])[None, :, None]

    block_out = both(tie(y0, ready), y1, came_y0, came_y1)
    input_grads = both(dx0, dx1, came_dx0, came_dx1)

    def by_unit(qkv_sums, unit_sums):
        q = qkv_sums[:, :width].reshape(heads, 1, size)
        v = qkv_sums[:, 2 * width :].reshape(heads, 1, size)
        bias = jnp.concatenate([q, v], 1).reshape(heads, dp, -1).swapaxes(0, 1).reshape(dp, -1)
        return jnp.concatenate([bias, unit_sums.reshape(dp, -1)], axis=1)

    unit0 = by_unit(tie(qkv_sums0, dx0), sum(sums_fc1_0))
    unit1 = by_unit(tie(qkv_sums1, dx0), sum(sums_fc1_1))
    vec = jnp.concatenate(
        [edge0[:2], sums0[:4], edge1[2:4], edge1[:2], sums1[:4], sums_sc_1[:1], sums_fc2_1[:1]]
    )
    vec = tie(vec, *going)
    vec = vec + core_swap(vec)
    vec = tie(sum([from_chip(vec, step) for step in range(1, chips)], vec), *step_ff0, *second_hop)
    vec = vec.reshape(2, 8, dp, part).swapaxes(1, 2).reshape(2, dp, 8 * part)
    vec0 = jnp.concatenate([vec[0], unit0], axis=1)
    vec1 = jnp.concatenate([vec[1], unit1], axis=1)
    own = jnp.where(first, vec0, vec1) + swap_section(jnp.where(first, vec1, vec0))
    own = tie(own, *last_swaps)
    vec = lax.dynamic_slice_in_dim(own, here, 1, 0)
    for step in range(1, dp):
        pairs = [(i, (i + step) % dp) for i in range(dp)]
        other = lax.dynamic_slice_in_dim(own, lax.rem(here + step, dp), 1, 0)
        vec = vec + lax.ppermute(other, "dp", pairs)
    cut = 8 * part + heads * (2 * size // dp)
    bias_grad = vec[:, 8 * part : cut].reshape(1, heads, -1)
    fc1_grad = vec[:, cut:].reshape(1, 1, -1)
    g_ln1, b_ln1, g_ln2, b_ln2, g_sc_attn, g_out_bias, g_sc_mlp, g_fc2_bias = (
        vec[:, i * part : (i + 1) * part] for i in range(8)
    )

    def owned(low, high):
        top = jnp.where(first, low.own, high.came.astype(F32))
        bottom = jnp.where(first, low.came.astype(F32), high.own)
        return jnp.concatenate([top, bottom], 0)

    g_ff = owned(sum_ff0, sum_ff1)
    g_att = jnp.where(
        first,
        sum_att0.own + sum_att0.came.astype(F32),
        sum_att1.own + sum_att1.came.astype(F32),
    )
    g_qkv = g_att[:, : 3 * width].reshape(part, 3, heads, size).swapaxes(1, 2)
    g_qkv = g_qkv.reshape(1, part, 3 * width)
    g_out = g_att[:, 3 * width :].T[None]
    g_fc1 = g_ff[:, :units][None]
    g_fc2 = g_ff[:, units:].T[None]
    return (
        block_out, input_grads, g_ln1, b_ln1, g_qkv, bias_grad, g_out, g_out_bias, g_sc_attn,
        g_ln2, b_ln2, g_fc1, fc1_grad, g_fc2, g_fc2_bias, g_sc_mlp,
    )


def solution(mesh):
    vec = P("section", "dp")
    by_row = P("section", "dp", "tensor")
    by_unit = P("section", "tensor", "dp")
    data = P(None, "dp", "tensor", None)
    split = P("section", None, "dp", "tensor", None)
    given = (
        vec, vec, by_row, by_unit, by_unit, vec, vec, vec, vec, by_row, by_unit, by_unit, vec, vec,
    )
    return jax.shard_map(
        shards,
        mesh=mesh,
        in_specs=(data, data) + given,
        out_specs=(split, split) + given,
        check_vma=False,
    )
```

```python
from functools import partial

import jax
import jax.numpy as jnp
from jax import lax
from jax.experimental import pallas as pl
from jax.experimental.pallas import tpu as pltpu
from jax.sharding import PartitionSpec as P

EPSILON = 1e-06
BF = jnp.bfloat16
F32 = jnp.float32
MIB = 1 << 20

LN1_G, LN1_B, OUT_B, SC_ATTN, LN2_G, LN2_B, FC2_B, SC_MLP = range(8)


def dot(a, b):
    return lax.dot_general(a, b, (((1,), (0,)), ((), ())), preferred_element_type=F32)


def dot_bt(a, b):
    return lax.dot_general(a, b, (((1,), (1,)), ((), ())), preferred_element_type=F32)


def dot_at(a, b):
    return lax.dot_general(a, b, (((0,), (0,)), ((), ())), preferred_element_type=F32)


def turn(v):
    return v.astype(F32).T


def params(limit, grid=0):
    return pltpu.CompilerParams(
        vmem_limit_bytes=limit * MIB,
        dimension_semantics=("arbitrary",) * grid if grid else None,
    )


def late(v):
    return pltpu.with_memory_space_constraint(v, pltpu.HBM)


def whole(shape):
    return pl.BlockSpec(shape, lambda i: (0, 0), pipeline_mode=pl.Buffered(1))


def cost(micros):
    return pl.CostEstimate(flops=int(micros * 1.15e9), bytes_accessed=0, transcendentals=0)


def sds(shape, dtype):
    return jax.ShapeDtypeStruct(shape, dtype)


def core_swap(v):
    count = lax.axis_size("tensor")
    return lax.ppermute(v, "tensor", [(i, i ^ 1) for i in range(count)])


def from_chip(v, step):
    count = lax.axis_size("tensor")
    chips = count // 2
    pairs = [(((i // 2 + step) % chips) * 2 + i % 2, i) for i in range(count)]
    return lax.ppermute(v, "tensor", pairs)


def tie(v, *after):
    if not after:
        return v
    return lax.optimization_barrier((v, *after))[0]


def tie_all(vs, *after):
    return lax.optimization_barrier((*vs, *after))[: len(vs)]


def gather_tokens(own, work, beside=()):
    chips = lax.axis_size("tensor") // 2
    came = [from_chip(own, step) for step in range(1, chips)]
    chunks = [(own, core_swap(own))]
    results = [work(chunks[0])]
    for same in came:
        same = tie(same, results[-1], *beside)
        chunks.append((same, core_swap(same)))
        results.append(work(chunks[-1]))
    return chunks, results


def core_sums(sames, others):
    chips, rows = len(sames), sames[0].shape[0]
    if isinstance(others, (list, tuple)):
        came = [core_swap(v) for v in others[1:]]
        local = core_swap(tie(others[0], came[-1]))
    else:
        local = core_swap(others)
        came = [local[c * rows : (c + 1) * rows] for c in range(1, chips)]
    sums = [(a.astype(F32) + b.astype(F32)).astype(BF) for a, b in zip(sames[1:], came)]
    return sums, local


def send_sums(sums):
    chips = len(sums) + 1
    return [from_chip(both, chips - step) for step, both in enumerate(sums, 1)]


def scatter_tokens(sames, others, work=None, beside=None):
    sums, local = core_sums(sames, others)
    terms = send_sums(sums)
    made = work(sums[-1]) if work else local
    more = beside(sums[-1]) if beside else ()
    terms = [tie(t, made, local, *more) for t in terms]
    return [late(sames[0]), *terms, local], made


def swap_section(v):
    return lax.ppermute(v, "section", [(0, 1), (1, 0)])


def assemble(shards, rows):
    count = len(shards)
    cut = len(shards[0])
    size, cols = rows // (count * cut), shards[0][0].shape[1]
    place = jnp.stack([lax.axis_index("dp"), lax.axis_index("section")])

    def body(place_ref, *refs):
        out_ref, sems = refs[count * cut :]
        z, x = place_ref[0], place_ref[1]
        started = []
        for k in range(count):
            base = lax.rem(z + (count - k), count) * (cut * size)
            for i, at in enumerate([base] if cut == 1 else [base + x * size, base + (1 - x) * size]):
                copy = pltpu.make_async_copy(
                    refs[k * cut + i].at[pl.ds(0, size), :],
                    out_ref.at[pl.ds(pl.multiple_of(at, size), size), :],
                    sems.at[k * cut + i],
                )
                copy.start()
                started.append(copy)
        for copy in started:
            copy.wait()

    hbm = pl.BlockSpec(memory_space=pl.ANY)
    return pl.pallas_call(
        body,
        in_specs=[pl.BlockSpec(memory_space=pltpu.SMEM)] + [hbm] * (count * cut),
        out_specs=pl.BlockSpec(memory_space=pltpu.VMEM),
        out_shape=sds((rows, cols), shards[0][0].dtype),
        scratch_shapes=[pltpu.SemaphoreType.DMA((count * cut,))],
        compiler_params=params(6),
        cost_estimate=cost(2),
        name="assemble",
    )(place, *[v for shard in shards for v in shard])


def half_of(v, which):
    half = v.shape[0] // 2
    return lax.dynamic_slice_in_dim(v, which * half, half, 0)


def direct(own):
    count = lax.axis_size("dp")
    return [
        lax.ppermute(own, "dp", [(i, (i + step) % count) for i in range(count)])
        for step in range(1, count)
    ]


def third(values, index):
    cuts = [-(-len(values) * i // 3) for i in range(4)]
    return values[cuts[index] : cuts[index + 1]]


class Ring:
    def __init__(self, own):
        self.last, self.hops, self.backs, self.at, self.back_at = own, [], [], 0, 0

    def hop(self, *gate):
        count = lax.axis_size("dp")
        pairs = [(i, (i + 1) % count) for i in range(count)]
        new = []
        for i in range(len(third(range(count - 1), self.at))):
            self.last = lax.ppermute(tie(self.last, *gate) if i == 0 else self.last, "dp", pairs)
            new.append(self.last)
        self.hops += new
        self.at += 1
        return new

    def back(self, *gate):
        count = lax.axis_size("dp")
        which = third(range(count - 1), self.back_at)
        new = [swap_section(tie(self.hops[i], *gate)) for i in which]
        self.backs += new
        self.back_at += 1
        return new


def in_order(back):
    count = len(back)
    ahead = [back[0], *back[:0:-1]]
    twice = jnp.stack(ahead + ahead)
    return lax.dynamic_slice_in_dim(twice, count - lax.axis_index("dp"), count, 0)


def dp_rows(v, back):
    dp = lax.axis_size("dp")
    part = v.shape[0] // dp
    place = lax.rem(lax.axis_index("dp") + (dp - back), dp)
    return lax.dynamic_slice_in_dim(v, place * part, part, 0)


class RingSum:
    def __init__(self, pair, mine, other=None):
        self.mine, self.other, self.pair = mine, other, pair
        self.terms, self.at, self.done = [], 0, 0

    def total(self, gate=()):
        first = tie(self.terms[0], *gate)
        return sum(t.astype(F32) for t in [first, *self.terms[1:]])

    def one(self, gate):
        dp = lax.axis_size("dp")
        self.done += 1
        new = []
        if self.terms:
            pairs = [(i, (i + 1) % dp) for i in range(dp)]
            self.sent = self.total(gate).astype(BF)
            new.append(lax.ppermute(self.sent, "dp", pairs))
        if self.other is not None:
            new.append(swap_section(tie(dp_rows(self.other, self.done), *gate)))
        self.terms = [*new, dp_rows(self.mine, self.done)]
        return new

    def step(self, *gate):
        self.at += 1
        if self.at == 5:
            self.own = self.total(gate)
            self.came = lax.ppermute(self.own.astype(BF), "section", [self.pair])
            return [self.came]
        count = 1 if self.at == 1 else len(third(range(lax.axis_size("dp") - 1), self.at - 2))
        return [v for i in range(count) for v in self.one(gate if i == 0 else ())]


def standardize(v):
    centred = v - jnp.mean(v, axis=-1, keepdims=True)
    var = jnp.mean(centred * centred, axis=-1, keepdims=True)
    scale = lax.rsqrt(var + EPSILON)
    return centred * scale, scale


def norm_of(v, vec, gain, shift):
    return (standardize(v)[0] * vec[gain : gain + 1, :] + vec[shift : shift + 1, :]).astype(BF)


def norm_back(v, grad, gain):
    xh, scale = standardize(v)
    dxh = grad * gain
    inner = jnp.mean(dxh * xh, axis=-1, keepdims=True)
    out = scale * (dxh - jnp.mean(dxh, axis=-1, keepdims=True) - xh * inner)
    return out, grad * xh


def total(refs):
    out = refs[0][...].astype(F32)
    for ref in refs[1:]:
        out = out + ref[...].astype(F32)
    return out


def fold(v, op):
    return op(v.reshape(-1, 8, v.shape[1]), axis=0)


def add_rows(ref, rows):
    for k, row in enumerate(rows):
        ref[8 * k : 8 * k + 8, :] += fold(row, jnp.sum)


def rowwise(body, row_ins, fulls, row_outs, sums, name):
    rows, width = row_ins[0].shape
    step = min(128, rows)
    some, outs = len(row_ins) + len(fulls), len(row_outs)

    def kernel(*refs):
        if not sums:
            body(*refs)
            return
        sum_ref, acc_ref = refs[some + outs :]

        @pl.when(pl.program_id(0) == 0)
        def _():
            acc_ref[...] = jnp.zeros_like(acc_ref)

        body(*refs[: some + outs], acc_ref)

        @pl.when(pl.program_id(0) == pl.num_programs(0) - 1)
        def _():
            for k in range(sums):
                sum_ref[k : k + 1, :] = jnp.sum(
                    acc_ref[8 * k : 8 * k + 8, :], axis=0, keepdims=True
                )

    out_shape = [sds((rows, width), d) for d in row_outs]
    out_shape += [sds((sums, width), F32)] if sums else []
    block = pl.BlockSpec((step, width), lambda i: (i, 0))
    return pl.pallas_call(
        kernel,
        grid=(rows // step,),
        in_specs=[block] * len(row_ins) + [whole(a.shape) for a in fulls],
        out_specs=[block] * outs + ([whole((sums, width))] if sums else []),
        out_shape=out_shape,
        scratch_shapes=[pltpu.VMEM((8 * sums, width), F32)] if sums else [],
        compiler_params=params(8, 1),
        cost_estimate=cost(2),
        name=name,
    )(*row_ins, *fulls)


def norm_first(x, vec):
    def body(x_ref, vec_ref, out_ref):
        out_ref[...] = norm_of(x_ref[...].astype(F32), vec_ref[...], LN1_G, LN1_B)

    return rowwise(body, [x], [vec], [BF], 0, "norm_first")[0]


def after_attention(x, terms, vec):
    count = len(terms)

    def body(*refs):
        x_ref, term_refs, vec_ref = refs[0], refs[1 : 1 + count], refs[1 + count]
        att_ref, res_ref, norm_ref = refs[2 + count :]
        v = vec_ref[...]
        attended = total(term_refs) + v[OUT_B : OUT_B + 1, :]
        residual = x_ref[...].astype(F32) + v[SC_ATTN : SC_ATTN + 1, :] * attended
        att_ref[...] = attended.astype(BF)
        res_ref[...] = residual
        norm_ref[...] = norm_of(residual, v, LN2_G, LN2_B)

    return rowwise(body, [x, *terms], [vec], [BF, F32, BF], 0, "after_attention")


def after_mlp(residual, terms, vec, vec_next):
    count = len(terms)

    def body(*refs):
        res_ref, term_refs = refs[0], refs[1 : 1 + count]
        vec_ref, next_ref, mlp_ref, y_ref, norm_ref = refs[1 + count :]
        v = vec_ref[...]
        mlp = total(term_refs) + v[FC2_B : FC2_B + 1, :]
        y = (res_ref[...] + v[SC_MLP : SC_MLP + 1, :] * mlp).astype(BF)
        mlp_ref[...] = mlp.astype(BF)
        y_ref[...] = y
        norm_ref[...] = norm_of(y.astype(F32), next_ref[...], LN1_G, LN1_B)

    return rowwise(body, [residual, *terms], [vec, vec_next], [BF, BF, BF], 0, "after_mlp")


def last_output(residual, terms, grad, vec):
    count = len(terms)

    def body(*refs):
        res_ref, term_refs = refs[0], refs[1 : 1 + count]
        grad_ref, vec_ref, y_ref, sum_ref = refs[1 + count :]
        v = vec_ref[...]
        mlp = total(term_refs) + v[FC2_B : FC2_B + 1, :]
        y_ref[...] = (res_ref[...] + v[SC_MLP : SC_MLP + 1, :] * mlp).astype(BF)
        add_rows(sum_ref, [grad_ref[...].astype(F32) * mlp])

    return rowwise(body, [residual, *terms, grad], [vec], [BF], 1, "last_output")


def start_back(grad, vec):
    def body(grad_ref, vec_ref, out_ref, sum_ref):
        low = (vec_ref[...][SC_MLP : SC_MLP + 1, :] * grad_ref[...].astype(F32)).astype(BF)
        out_ref[...] = low
        add_rows(sum_ref, [low.astype(F32)])

    return rowwise(body, [grad], [vec], [BF], 1, "start_back")


def back_second(grad, residual, attended, terms, vec):
    count = len(terms)

    def body(*refs):
        grad_ref, res_ref, att_ref = refs[:3]
        term_refs = refs[3 : 3 + count]
        vec_ref, dres_ref, low_ref, sum_ref = refs[3 + count :]
        v = vec_ref[...]
        dn = total(term_refs)
        back, dgain = norm_back(res_ref[...], dn, v[LN2_G : LN2_G + 1, :])
        dres = grad_ref[...].astype(F32) + back
        low = (v[SC_ATTN : SC_ATTN + 1, :] * dres).astype(BF)
        dres_ref[...] = dres
        low_ref[...] = low
        add_rows(sum_ref, [dgain, dn, dres * att_ref[...].astype(F32), low.astype(F32)])

    return rowwise(
        body, [grad, residual, attended, *terms], [vec], [F32, BF], 4, "back_second"
    )


def back_first(dres, x, terms, vec, mlp_below=None, vec_below=None):
    count = len(terms)
    below = mlp_below is not None

    def body(*refs):
        dres_ref, x_ref = refs[:2]
        term_refs = refs[2 : 2 + count]
        rest = refs[2 + count :]
        if below:
            mlp_ref, vec_ref, under_ref, dx_ref, low_ref, sum_ref = rest
        else:
            vec_ref, dx_ref, sum_ref = rest
        v = vec_ref[...]
        dn = total(term_refs)
        back, dgain = norm_back(x_ref[...].astype(F32), dn, v[LN1_G : LN1_G + 1, :])
        dx = (dres_ref[...] + back).astype(BF)
        dx_ref[...] = dx
        rows = [dgain, dn]
        if below:
            wide = dx.astype(F32)
            low = (under_ref[...][SC_MLP : SC_MLP + 1, :] * wide).astype(BF)
            low_ref[...] = low
            rows += [wide * mlp_ref[...].astype(F32), low.astype(F32)]
        add_rows(sum_ref, rows)

    row_ins = [dres, x, *terms] + ([mlp_below] if below else [])
    fulls = [vec] + ([vec_below] if below else [])
    return rowwise(body, row_ins, fulls, [BF, BF] if below else [BF], 4 if below else 2, "back_first")


def project_qkv(pair, weight, bias):
    rows, width = pair[0].shape
    cols = bias.shape[1]

    def body(a_ref, b_ref, w_ref, bias_ref, out_ref):
        w = w_ref[...]
        shift = bias_ref[...]
        out_ref[:rows, :] = (dot(a_ref[...], w) + shift).astype(BF)
        out_ref[rows:, :] = (dot(b_ref[...], w) + shift).astype(BF)

    return pl.pallas_call(
        body,
        grid=(1,),
        in_specs=[
            whole((rows, width)), whole((rows, width)), whole((width, cols)), whole((1, cols))
        ],
        out_specs=whole((2 * rows, cols)),
        out_shape=sds((2 * rows, cols), BF),
        compiler_params=params(6, 1),
        cost_estimate=cost(2),
        name="project_qkv",
    )(*pair, weight, bias)


def head_rows(v, head, size):
    rows = lax.broadcasted_iota(jnp.int32, v.shape, 0)
    return jnp.where(rows // size == head, v, jnp.zeros_like(v))


def head_cols(v, head, size):
    cols = lax.broadcasted_iota(jnp.int32, v.shape, 1)
    return jnp.where(cols // size == head, v, jnp.zeros_like(v))


def attention(packed, weight, size):
    chips = len(packed)
    span = packed[0].shape[0]
    half = span // 2
    width = packed[0].shape[1] // 3
    seq = chips * span
    heads = width // size
    model = weight.shape[0]
    step = min(256, seq)
    chunk = min(128, seq)
    score = size**-0.5

    def body(*refs):
        in_refs, w_ref = refs[:chips], refs[chips]
        head_refs = refs[chips + 1 : 2 * chips + 1]
        lse_ref = refs[2 * chips + 1]
        same_refs, other_ref = refs[2 * chips + 2 : 3 * chips + 2], refs[3 * chips + 2]
        k_ref, qt_ref, vt_ref, ot_ref, s_ref, p_ref = refs[3 * chips + 3 :]
        for c in range(chips):
            at = slice(c * span, (c + 1) * span)
            k_ref[at, :] = in_refs[c][:, width : 2 * width]
            qt_ref[:, at] = (turn(in_refs[c][:, :width]) * score).astype(BF)
            vt_ref[:, at] = turn(in_refs[c][:, 2 * width :]).astype(BF)

        def one(i, carry):
            at = pl.ds(pl.multiple_of(i * step, step), step)
            q = qt_ref[:, at]
            s_ref[0] = dot(k_ref[...], head_rows(q, 0, size))
            for h in range(heads):
                if h + 1 < heads:
                    s_ref[(h + 1) % 2] = dot(k_ref[...], head_rows(q, h + 1, size))
                now = h % 2
                top = fold(s_ref[now, :chunk, :], jnp.max)
                for r in range(chunk, seq, chunk):
                    top = jnp.maximum(top, fold(s_ref[now, r : r + chunk, :], jnp.max))
                top = jnp.max(top, axis=0, keepdims=True)
                norm = jnp.zeros((8, step), F32)
                for r in range(0, seq, chunk):
                    p = jnp.exp(s_ref[now, r : r + chunk, :] - top)
                    norm = norm + fold(p, jnp.sum)
                    p_ref[now, r : r + chunk, :] = p.astype(BF)
                norm = jnp.sum(norm, axis=0, keepdims=True)
                rows = slice(h * size, (h + 1) * size)
                ot_ref[rows, at] = dot(vt_ref[rows, :], p_ref[now]) / norm
                lse_ref[h : h + 1, at] = top + jnp.log(norm)
            return carry

        lax.fori_loop(0, seq // step, one, 0)
        for c in range(chips):
            at = slice(c * span, (c + 1) * span)
            o = ot_ref[:, at].T.astype(BF)
            head_refs[c][...] = o
            same_refs[c][...] = dot_bt(o[:half], w_ref[...]).astype(BF)
            other_ref[c * half : (c + 1) * half, :] = dot_bt(o[half:], w_ref[...]).astype(BF)

    out = pl.pallas_call(
        body,
        grid=(1,),
        in_specs=[whole((span, 3 * width))] * chips
        + [pl.BlockSpec((model, width), lambda i: (0, 3), pipeline_mode=pl.Buffered(1))],
        out_specs=[whole((span, width))] * chips
        + [whole((heads, seq))]
        + [whole((half, model))] * chips
        + [whole((seq // 2, model))],
        out_shape=[pltpu.HBM((span, width), BF)] * chips
        + [sds((heads, seq), F32), pltpu.HBM((half, model), BF)]
        + [sds((half, model), BF)] * (chips - 1)
        + [sds((seq // 2, model), BF)],
        scratch_shapes=[
            pltpu.VMEM((seq, width), BF),
            pltpu.VMEM((width, seq), BF),
            pltpu.VMEM((width, seq), BF),
            pltpu.VMEM((width, seq), F32),
            pltpu.VMEM((2, seq, step), F32),
            pltpu.VMEM((2, seq, step), BF),
        ],
        compiler_params=params(14, 1),
        cost_estimate=cost(9),
        name="attention",
    )(*packed, weight)
    return out[:chips], out[chips], out[chips + 1 : -1], out[-1]


def attention_back(packed, heads_kept, lse, datt, weight, size):
    chips = len(packed)
    span = packed[0].shape[0]
    half = span // 2
    width = packed[0].shape[1] // 3
    seq = chips * span
    heads = width // size
    model = weight.shape[0]
    step = min(256, seq)
    chunk = min(128, seq)
    score = size**-0.5

    def body(*refs):
        at = 0

        def take(count):
            nonlocal at
            at += count
            return refs[at - count : at]

        in_refs, kept_refs = take(chips), take(chips)
        (lse_ref,) = take(1)
        datt_refs = take(2 * chips)
        (w_ref,) = take(1)
        dqkv_refs = take(chips)
        same_refs = take(chips)
        other_ref, sum_ref = take(2)
        k_ref, v_ref, kt_ref, qt_ref, q_ref, do_ref, dot_ref = take(7)
        inner_ref, s_ref, g_ref, p_ref, ds_ref, dk_ref, dv_ref, dqt_ref = take(8)
        for c in range(chips):
            rows = slice(c * span, (c + 1) * span)
            q = in_refs[c][:, :width].astype(F32) * score
            k = in_refs[c][:, width : 2 * width]
            q_ref[rows, :] = q.astype(BF)
            qt_ref[:, rows] = q.T.astype(BF)
            k_ref[rows, :] = k
            kt_ref[:, rows] = turn(k).astype(BF)
            v_ref[rows, :] = in_refs[c][:, 2 * width :]
            for b in range(2):
                d = dot(datt_refs[2 * c + b][...], w_ref[:, 3 * width :]).astype(BF)
                here = slice(c * span + b * half, c * span + (b + 1) * half)
                do_ref[here, :] = d
                dt = turn(d)
                dot_ref[:, here] = dt.astype(BF)
                prod = dt * turn(kept_refs[c][b * half : (b + 1) * half, :])
                for h in range(heads):
                    inner_ref[h : h + 1, here] = jnp.sum(
                        prod[h * size : (h + 1) * size, :], axis=0, keepdims=True
                    )

        def one(i, carry):
            at = pl.ds(pl.multiple_of(i * step, step), step)
            qt = qt_ref[:, at]
            dot_t = dot_ref[:, at]
            q = q_ref[at, :]
            do = do_ref[at, :]

            def scores(h):
                s_ref[h % 2] = dot(k_ref[...], head_rows(qt, h, size))
                g_ref[h % 2] = dot(v_ref[...], head_rows(dot_t, h, size))

            scores(0)
            for h in range(heads):
                if h + 1 < heads:
                    scores(h + 1)
                now = h % 2
                cols = slice(h * step, (h + 1) * step)
                lse = lse_ref[h : h + 1, at]
                inner = inner_ref[h : h + 1, at]
                for r in range(0, seq, chunk):
                    p = jnp.exp(s_ref[now, r : r + chunk, :] - lse)
                    ds = p * (g_ref[now, r : r + chunk, :] - inner)
                    p_ref[r : r + chunk, cols] = p.astype(BF)
                    ds_ref[r : r + chunk, cols] = ds.astype(BF)
                rows = slice(h * size, (h + 1) * size)
                dqt_ref[rows, at] = dot(kt_ref[rows, :], ds_ref[:, cols]) * score
            dv = dot(p_ref[...], jnp.concatenate([head_cols(do, h, size) for h in range(heads)], 0))
            dk = dot(ds_ref[...], jnp.concatenate([head_cols(q, h, size) for h in range(heads)], 0))

            @pl.when(i == 0)
            def _():
                dv_ref[...] = dv
                dk_ref[...] = dk

            @pl.when(i > 0)
            def _():
                dv_ref[...] += dv
                dk_ref[...] += dk

            return carry

        lax.fori_loop(0, seq // step, one, 0)
        for c in range(chips):
            rows = slice(c * span, (c + 1) * span)
            out = dqkv_refs[c]
            out[:, :width] = dqt_ref[:, rows].T.astype(BF)
            out[:, width : 2 * width] = dk_ref[rows, :].astype(BF)
            out[:, 2 * width :] = dv_ref[rows, :].astype(BF)
            sums = jnp.sum(out[...].astype(F32), axis=0, keepdims=True)
            if c == 0:
                sum_ref[...] = sums
            else:
                sum_ref[...] += sums
            w = w_ref[:, : 3 * width]
            same_refs[c][...] = dot_bt(out[:half, :], w).astype(BF)
            other_ref[c * half : (c + 1) * half, :] = dot_bt(out[half:, :], w).astype(BF)

    flat = [g for pair in datt for g in pair]
    out_shape = (
        [pltpu.HBM((span, 3 * width), BF)] * chips
        + [pltpu.HBM((half, model), BF)]
        + [sds((half, model), BF)] * (chips - 1)
        + [sds((seq // 2, model), BF), sds((1, 3 * width), F32)]
    )
    operands = (*map(late, (*packed, *heads_kept)), lse, *flat, late(weight))
    out = pl.pallas_call(
        body,
        grid=(1,),
        in_specs=[whole(a.shape) for a in operands],
        out_specs=[whole(a.shape) for a in out_shape],
        out_shape=out_shape,
        scratch_shapes=[
            pltpu.VMEM((seq, width), BF),
            pltpu.VMEM((seq, width), BF),
            pltpu.VMEM((width, seq), BF),
            pltpu.VMEM((width, seq), BF),
            pltpu.VMEM((seq, width), BF),
            pltpu.VMEM((seq, width), BF),
            pltpu.VMEM((width, seq), BF),
            pltpu.VMEM((heads, seq), F32),
            pltpu.VMEM((2, seq, step), F32),
            pltpu.VMEM((2, seq, step), F32),
            pltpu.VMEM((seq, heads * step), BF),
            pltpu.VMEM((seq, heads * step), BF),
            pltpu.VMEM((seq, width), F32),
            pltpu.VMEM((seq, width), F32),
            pltpu.VMEM((width, seq), F32),
        ],
        compiler_params=params(26, 1),
        cost_estimate=cost(15),
        name="attention_back",
    )(*operands)
    return out[:chips], out[chips : 2 * chips], out[2 * chips], out[2 * chips + 1]


def gelu_both(x):
    away = jnp.abs(x)
    t = 1.0 / (1.0 + (0.3275911 * 0.5**0.5) * away)
    bell = jnp.exp(-0.5 * (x * x))
    poly = t * (
        0.127414796
        + t * (-0.142248368 + t * (0.7107068705 + t * (-0.7265760135 + t * 0.5307027145)))
    )
    tail = poly * bell
    phi = jnp.where(x >= 0, 1.0 - tail, tail)
    return x * phi, phi + x * (bell * 0.3989422804014327)


def mlp_call(body, pairs, extra, weight, bias, outs, parts, scratch, name):
    rows, model = pairs[0].shape
    units = weight.shape[1] // 2
    step = min(256, units)
    blocks = units // step
    cols = lambda j: (0, j)
    in_specs = [whole((rows, model)) for _ in pairs]
    in_specs += [pl.BlockSpec((2 * rows, step), cols) for _ in extra]
    in_specs += [
        pl.BlockSpec((model, step), cols),
        pl.BlockSpec((model, step), lambda j: (0, blocks + j)),
        pl.BlockSpec((1, step), cols),
    ]
    out_specs = [pl.BlockSpec((2 * rows, step), cols) for _ in outs]
    out_specs += [pl.BlockSpec((1, step), cols)]
    out_specs += [whole((rows, model))] * (2 * parts)
    out_shape = [pltpu.HBM((2 * rows, units), d) for d in outs] + [sds((1, units), F32)]
    out_shape += [pltpu.HBM((rows, model), BF)] * (2 * parts)
    count = len(pairs) // 2
    return pl.pallas_call(
        body,
        grid=(blocks,),
        in_specs=in_specs,
        out_specs=out_specs,
        out_shape=out_shape,
        scratch_shapes=[pltpu.VMEM((2 * rows, model), F32)] * parts
        + [pltpu.VMEM((2 * rows, step), F32)] * scratch,
        compiler_params=params(8 + 5 * parts, 1),
        cost_estimate=cost(3 + 3 * parts),
        name=name,
    )(*pairs, *map(late, extra), weight, weight, bias)


def clear(*refs):
    @pl.when(pl.program_id(0) == 0)
    def _():
        for ref in refs:
            ref[...] = jnp.zeros_like(ref)


def finish(acc, low, high):
    rows = low.shape[0]

    @pl.when(pl.program_id(0) == pl.num_programs(0) - 1)
    def _():
        low[...] = acc[:rows, :].astype(BF)
        high[...] = acc[rows:, :].astype(BF)


CHUNK = 32


def mlp_forward(pair, weight, bias):
    rows = pair[0].shape[0]

    def body(a, b, w1_ref, w2_ref, bias_ref, act_ref, slope_ref, sum_ref, lo, hi, acc, pre):
        clear(acc, sum_ref)
        shift = bias_ref[...]
        for i, x in enumerate((a, b)):
            pre[i * rows : (i + 1) * rows, :] = dot(x[...], w1_ref[...])
        for i in range(2):
            at = slice(i * rows, (i + 1) * rows)
            for r in range(i * rows, (i + 1) * rows, CHUNK):
                act, slope = gelu_both(pre[r : r + CHUNK, :] + shift)
                act_ref[r : r + CHUNK, :] = act.astype(BF)
                slope_ref[r : r + CHUNK, :] = slope.astype(BF)
            acc[at, :] += dot_bt(act_ref[at, :], w2_ref[...])
        finish(acc, lo, hi)

    act, slope, _, lo, hi = mlp_call(body, pair, [], weight, bias, [BF, BF], 1, 1, "mlp_forward")
    return act, slope, lo, hi


def mlp_backward(pair, slope, weight, bias):
    rows = pair[0].shape[0]

    def body(a, b, slope_ref, w1_ref, w2_ref, bias_ref, dpre_ref, sum_ref, lo, hi, acc, pre):
        clear(acc)
        for i, g in enumerate((a, b)):
            pre[i * rows : (i + 1) * rows, :] = dot(g[...], w2_ref[...])
        sums = jnp.zeros((8, bias_ref.shape[1]), F32)
        for i in range(2):
            at = slice(i * rows, (i + 1) * rows)
            for r in range(i * rows, (i + 1) * rows, CHUNK):
                d = pre[r : r + CHUNK, :] * slope_ref[r : r + CHUNK, :].astype(F32)
                d = d.astype(BF)
                dpre_ref[r : r + CHUNK, :] = d
                sums = sums + fold(d.astype(F32), jnp.sum)
            acc[at, :] += dot_bt(dpre_ref[at, :], w1_ref[...])
        sum_ref[...] = jnp.sum(sums, axis=0, keepdims=True)
        finish(acc, lo, hi)

    dpre, sums, lo, hi = mlp_call(
        body, pair, [slope], weight, bias, [BF], 1, 1, "mlp_backward"
    )
    return dpre, sums, lo, hi


def mlp_both(pair, grads, weight, bias):
    rows = pair[0].shape[0]

    def body(
        a, b, c, d, w1_ref, w2_ref, bias_ref, act_ref, dpre_ref, sum_ref,
        lo, hi, blo, bhi, acc, back, pre, grad,
    ):
        clear(acc, back)
        shift = bias_ref[...]
        for i, (x, g) in enumerate(((a, c), (b, d))):
            at = slice(i * rows, (i + 1) * rows)
            pre[at, :] = dot(x[...], w1_ref[...])
            grad[at, :] = dot(g[...], w2_ref[...])
        sums = jnp.zeros((8, bias_ref.shape[1]), F32)
        for i in range(2):
            at = slice(i * rows, (i + 1) * rows)
            for r in range(i * rows, (i + 1) * rows, CHUNK):
                act, slope = gelu_both(pre[r : r + CHUNK, :] + shift)
                act_ref[r : r + CHUNK, :] = act.astype(BF)
                dpre = (grad[r : r + CHUNK, :] * slope).astype(BF)
                dpre_ref[r : r + CHUNK, :] = dpre
                sums = sums + fold(dpre.astype(F32), jnp.sum)
            back[at, :] += dot_bt(dpre_ref[at, :], w1_ref[...])
            acc[at, :] += dot_bt(act_ref[at, :], w2_ref[...])
        sum_ref[...] = jnp.sum(sums, axis=0, keepdims=True)
        finish(acc, lo, hi)
        finish(back, blo, bhi)

    act, dpre, sums, lo, hi, blo, bhi = mlp_call(
        body, [*pair, *grads], [], weight, bias, [BF, BF], 2, 2, "mlp_both"
    )
    return act, dpre, sums, lo, hi, blo, bhi


def weight_grads(products, dp, side, name, halves=True, heads=0):
    model = products[0][0][0].shape[1]
    step = model // dp
    half = step // 2
    cut = 2 if halves else 1
    sizes = [(len(left), len(right), right[0].shape[1]) for left, right in products]
    cols = sum(n for _, _, n in sizes)

    def body(side_ref, *refs):
        acc_ref = refs[-1]
        mine, other = refs[-3:-1] if halves else (refs[-2], None)
        at = base = 0
        for many, few, n in sizes:
            lefts, rights = refs[at : at + many], refs[at + many : at + many + few]
            at += many + few
            ratio = many // few
            acc = None
            for i in range(many):
                size = lefts[i].shape[0]
                here = slice((i % ratio) * size, (i % ratio + 1) * size)
                term = dot_at(lefts[i][...], rights[i // ratio][here, :])
                acc = term if acc is None else acc + term
            if halves:
                acc_ref[:, base : base + n] = acc
            elif heads and not base:
                size = n // (3 * heads)
                for k in range(3 * heads):
                    head, kind = k // 3, k % 3
                    at_k = (kind * heads + head) * size
                    mine[:, k * size : (k + 1) * size] = acc[:, at_k : at_k + size].astype(BF)
            else:
                mine[:, base : base + n] = acc.astype(BF)
            base += n
        if not halves:
            return
        low = pl.multiple_of(side_ref[0] * half, half)
        high = pl.multiple_of((1 - side_ref[0]) * half, half)
        mine[...] = acc_ref[pl.ds(low, half), :].astype(BF)
        other[...] = acc_ref[pl.ds(high, half), :].astype(BF)

    specs, operands = [pl.BlockSpec(memory_space=pltpu.SMEM)], [side.reshape(1)]
    for left, right in products:
        specs += [pl.BlockSpec((a.shape[0], step), lambda i: (0, i)) for a in left]
        specs += [whole(b.shape) for b in right]
        operands += [*left, *right]
    return pl.pallas_call(
        body,
        grid=(dp,),
        in_specs=specs,
        out_specs=[pl.BlockSpec((step // cut, cols), lambda i: (i, 0))] * cut,
        out_shape=[sds((model // cut, cols), BF)] * cut,
        scratch_shapes=[pltpu.VMEM((step, cols), F32)],
        compiler_params=params(14, 1),
        cost_estimate=cost(5),
        name=name,
    )(*operands)


def pieces(chunks):
    return [p for pair in chunks for p in pair]


def shards(
    tokens, cotangent, ln1_gain, ln1_bias, w_qkv, qv_bias, w_out, out_bias, scale_attn,
    ln2_gain, ln2_bias, w_fc1, fc1_bias, w_fc2, fc2_bias, scale_mlp,
):
    side = lax.axis_index("section")
    first = side == 0
    dp = lax.axis_size("dp")
    here = lax.axis_index("dp")
    chips = lax.axis_size("tensor") // 2
    rows, model = tokens.shape[2:]
    heads = qv_bias.shape[1]
    size = qv_bias.shape[2] * dp // 2
    width = heads * size
    units = w_fc1.shape[2]
    part = model // dp

    x0 = lax.dynamic_index_in_dim(tokens, side, 0, keepdims=False).reshape(rows, model)
    grad_top = lax.dynamic_index_in_dim(cotangent, side, 0, keepdims=False).reshape(rows, model)

    vectors = (ln1_gain, ln1_bias, out_bias, scale_attn, ln2_gain, ln2_bias, fc2_bias, scale_mlp)
    packed = jnp.concatenate(
        [v.reshape(-1) for v in vectors] + [fc1_bias.reshape(-1), qv_bias.reshape(-1)]
    )
    own_qkv = w_qkv.reshape(part, heads, 3, size).swapaxes(1, 2).reshape(part, 3 * width)
    own_att = jnp.concatenate([own_qkv, w_out[0].T], axis=1)
    give_att = half_of(own_att, 1 - side)
    came_att = swap_section(give_att)
    came_small = swap_section(tie(packed, give_att))
    both_small = jnp.concatenate(
        [jnp.where(first, packed, came_small), jnp.where(first, came_small, packed)]
    )
    cols = 4 * width
    tail = -(-both_small.size // (16 * cols)) * 16
    both_small = jnp.pad(both_small, (0, tail * cols - both_small.size)).reshape(tail, cols)
    mine_att = half_of(own_att, side)
    ring_att0 = jnp.concatenate([jnp.where(first, mine_att, came_att), both_small])
    ring_att1 = jnp.where(first, came_att, mine_att)
    hops_att0 = direct(ring_att0)
    own_ff = jnp.concatenate([w_fc1[0], w_fc2[0].T], axis=1)
    rest_att = swap_section(tie(mine_att, ring_att0))
    came_ff = swap_section(tie(own_ff, ring_att0))
    shard_ff0, shard_ff1 = jnp.where(first, own_ff, came_ff), jnp.where(first, came_ff, own_ff)
    ring_ff0, ring_ff1 = half_of(shard_ff0, side), half_of(shard_ff1, side)

    back = [ring_att0, *hops_att0]
    flat = in_order([v[-tail:] for v in back])
    flat = flat.reshape(dp, -1)[:, : 2 * packed.size].reshape(dp, 2, -1).astype(F32)
    cut = 8 * part
    vecs = flat[:, :, :cut].reshape(dp, 2, 8, part).transpose(1, 2, 0, 3).reshape(2, 8, model)
    vecs = (vecs[0], vecs[1])
    bias_fc1 = flat[:, :, cut : cut + units // dp].swapaxes(0, 1).reshape(2, 1, units)
    qv = flat[:, :, cut + units // dp :].reshape(dp, 2, heads, -1).transpose(1, 2, 0, 3)
    qv = qv.reshape(2, heads, 2, size)
    bias_qkv = jnp.stack([qv[:, :, 0], jnp.zeros_like(qv[:, :, 0]), qv[:, :, 1]], axis=1)
    bias_qkv = bias_qkv.reshape(2, 1, 3 * width)

    norm1 = norm_first(tie(x0, came_ff), vecs[0])
    left = half_of(own_att, 1 - side)
    rest_att0, rest_att1 = jnp.where(first, left, rest_att), jnp.where(first, rest_att, left)
    rest_ff0, rest_ff1 = half_of(shard_ff0, 1 - side), half_of(shard_ff1, 1 - side)
    backs = [swap_section(tie(v, came_ff)) for v in hops_att0]
    att1 = Ring(ring_att1)
    att0 = assemble([(tie(ring_att0, norm1), rest_att0), *zip(hops_att0, backs)], model)
    ff0, ff1 = Ring(ring_ff0), Ring(ring_ff1)
    hop_ff0 = ff0.hop(norm1)

    def projection(weight, s):
        return lambda pair: project_qkv(pair, weight, bias_qkv[s])

    chunks0, qkv0 = gather_tokens(norm1, projection(att0, 0), hop_ff0)
    beside = [*ff0.hop(), *ff0.back()]
    kept0, lse0, sames, others = attention(qkv0, att0, size)
    gate = others
    others = tie(others, *beside)
    beside = [*ff0.hop(gate), *ff0.back(gate)]
    terms, _ = scatter_tokens(
        sames, others, beside=lambda gate: [*beside, *att1.hop(gate)]
    )
    attended0, residual0, norm2 = after_attention(x0, terms, vecs[0])
    ff0.back()
    beside = att1.hop(norm2)
    w_ff0 = assemble([(ring_ff0, rest_ff0), *zip(ff0.hops, ff0.backs)], model)
    second0, mlp0 = gather_tokens(
        norm2, lambda pair: mlp_forward(pair, w_ff0, bias_fc1[0]), beside
    )
    act0, slope0, sames, others = zip(*mlp0)
    beside = att1.hop(second0[-1][0])
    terms, _ = scatter_tokens(
        sames,
        [others[0], *[tie(v, *beside) for v in others[1:]]],
        beside=lambda gate: [
            *ff1.hop(gate), *att1.back(gate), *att1.back(gate), *att1.back(gate)
        ],
    )
    mlp_out0, y0, norm1 = after_mlp(residual0, terms, vecs[0], vecs[1])

    w_att1 = assemble([(ring_att1, rest_att1), *zip(att1.hops, att1.backs)], model)
    low1, sums_fc2_1 = start_back(grad_top, vecs[1])
    beside = [*ff1.hop(norm1), *ff1.back(norm1)]
    chunks1, qkv1 = gather_tokens(norm1, projection(w_att1, 1), beside)
    gate = chunks1[-1][0]
    came = [from_chip(tie(low1, gate), step) for step in range(1, chips)]
    beside = [*came, *ff1.hop(gate), *ff1.back(gate)]
    kept1, lse1, sames, others = attention(qkv1, w_att1, size)
    others = tie(others, *beside)
    grads1 = [(low1, core_swap(low1))] + [(v, core_swap(tie(v, lse1))) for v in came]
    terms, _ = scatter_tokens(
        sames, others, beside=lambda gate: [*ff1.back(gate), *pieces(grads1)]
    )
    attended1, residual1, norm2 = after_attention(y0, terms, vecs[1])
    w_ff1 = assemble([(ring_ff1, rest_ff1), *zip(ff1.hops, ff1.backs)], model)
    spare = list(grads1)
    second1, mlp1 = gather_tokens(
        norm2, lambda pair: mlp_both(pair, spare.pop(0), w_ff1, bias_fc1[1])
    )
    act1, dpre1, sums_fc1_1, sames_y1, others_y1, sames, others = zip(*mlp1)

    def grad_ff(second, dpre, grads, act):
        return lambda after: weight_grads(
            [
                (pieces(second), [late(tie(dpre[0], after)), *map(late, dpre[1:])]),
                (pieces(grads), [late(a) for a in act]),
            ],
            dp,
            side,
            "grad_ff",
        )

    def grad_att(chunks, dqkv, datt, kept):
        return lambda after: weight_grads(
            [
                (pieces(chunks), [late(tie(dqkv[0], after)), *map(late, dqkv[1:])]),
                (pieces(datt), [late(a) for a in kept]),
            ],
            dp,
            side,
            "grad_att",
            False,
            heads,
        )[0]

    old = [tuple(map(late, pair)) for pair in grads1]
    terms, g = scatter_tokens(sames, others, grad_ff(second1, dpre1, old, act1))
    sum_ff1 = RingSum((0, 1), *g)
    dres1, low, sums1 = back_second(grad_top, residual1, attended1, terms, vecs[1])
    came_y0 = lax.ppermute(tie(y0, low), "section", [(1, 0)])
    datt, _ = gather_tokens(low, lambda pair: pair[0], sum_ff1.step())
    sums_y1, local_y1 = core_sums(sames_y1, [tie(v, low) for v in others_y1])
    terms_y1 = send_sums([tie(v, datt[-1][0]) for v in sums_y1])
    beside = [came_y0, *terms_y1, *sum_ff1.step(low)]
    dqkv, sames, others, qkv_sums1 = attention_back(qkv1, kept1, lse1, datt, w_att1, size)
    old = [tuple(map(late, pair)) for pair in chunks1]
    made = []

    def beside_y1(gate):
        y1, sums = last_output(
            residual1, [tie(sames_y1[0], gate), *terms_y1, local_y1], grad_top, vecs[1]
        )
        made.extend([y1, sums, lax.ppermute(y1, "section", [(0, 1)])])
        return sum_ff1.step(gate)

    terms, g = scatter_tokens(
        sames, tie(others, *beside), grad_att(old, dqkv, datt, kept1), beside_y1
    )
    y1, sums_sc_1, came_y1 = made
    sum_att1 = RingSum((0, 1), g)
    sum_att1.step()
    dx1, low0, edge1 = back_first(dres1, late(y0), terms, vecs[1], late(mlp_out0), vecs[0])

    slopes = list(slope0)
    grads0, mlp_back0 = gather_tokens(
        low0,
        lambda pair: mlp_backward(pair, slopes.pop(0), w_ff0, bias_fc1[0]),
        [came_y1, *sum_ff1.step(low0), *sum_att1.step(low0)],
    )
    dpre0, sums_fc1_0, sames, others = zip(*mlp_back0)
    old = [tuple(map(late, pair)) for pair in second0]
    terms, g = scatter_tokens(
        sames,
        others,
        grad_ff(old, dpre0, grads0, act0),
        lambda gate: [*sum_ff1.step(gate), *sum_att1.step(gate)],
    )
    sum_ff0 = RingSum((1, 0), *g)
    dres0, low, sums0 = back_second(
        dx1, late(residual0), late(attended0), terms, vecs[0]
    )
    came_dx1 = lax.ppermute(tie(dx1, terms[1]), "section", [(0, 1)])
    beside = [came_dx1, *sum_att1.step(low), *sum_ff0.step(low)]
    datt, _ = gather_tokens(low, lambda pair: pair[0], beside)
    beside = sum_ff0.step(low)
    dqkv, sames, others, qkv_sums0 = attention_back(qkv0, kept0, lse0, datt, att0, size)
    old = [tuple(map(late, pair)) for pair in chunks0]
    terms, g = scatter_tokens(
        sames, tie(others, *beside), grad_att(old, dqkv, datt, kept0), sum_ff0.step
    )
    sum_att0 = RingSum((1, 0), g)
    sum_att0.step()
    going = sum_att0.step()
    dx0, edge0 = back_first(dres0, x0, terms, vecs[0])
    came_dx0 = lax.ppermute(dx0, "section", [(1, 0)])
    step_ff0 = sum_ff0.step(dx0)
    second_hop = sum_att0.step(dx0)
    step_att1 = sum_att1.step(sames[0])
    third_hop = sum_att0.step(*step_ff0)
    last_ff0 = sum_ff0.step()
    sum_att0.step()

    def both(low, high, came_low, came_high):
        mine = jnp.where(first, low, high)
        came = jnp.where(first, came_low, came_high)
        return jnp.stack([jnp.where(first, mine, came), jnp.where(first, came, mine)])[None, :, None]

    block_out = both(y0, tie(y1, *second_hop), came_y0, came_y1)
    input_grads = both(dx0, dx1, came_dx0, came_dx1)
    sum_att0.came = tie(sum_att0.came, block_out, input_grads)

    def by_unit(qkv_sums, unit_sums):
        q = qkv_sums[:, :width].reshape(heads, 1, size)
        v = qkv_sums[:, 2 * width :].reshape(heads, 1, size)
        bias = jnp.concatenate([q, v], 1).reshape(heads, dp, -1).swapaxes(0, 1).reshape(dp, -1)
        return jnp.concatenate([bias, unit_sums.reshape(dp, -1)], axis=1)

    unit0 = by_unit(tie(qkv_sums0, dx0), sum(sums_fc1_0))
    unit1 = by_unit(tie(qkv_sums1, dx0), sum(sums_fc1_1))
    vec = jnp.concatenate(
        [edge0[:2], sums0[:4], edge1[2:4], edge1[:2], sums1[:4], sums_sc_1[:1], sums_fc2_1[:1]]
    )
    vec = tie(vec, *going, *step_att1)
    vec = vec + core_swap(vec)
    vec = tie(sum([from_chip(vec, step) for step in range(1, chips)], vec), *step_ff0, *second_hop)
    vec = tie(vec, sum_att0.sent)
    vec = vec.reshape(2, 8, dp, part).swapaxes(1, 2).reshape(2, dp, 8 * part)
    vec0 = jnp.concatenate([vec[0], unit0], axis=1)
    vec1 = jnp.concatenate([vec[1], unit1], axis=1)
    own = jnp.where(first, vec0, vec1) + swap_section(jnp.where(first, vec1, vec0))
    own = tie(own, *last_ff0)
    vec = lax.dynamic_slice_in_dim(own, here, 1, 0)
    for step in range(1, dp):
        pairs = [(i, (i + step) % dp) for i in range(dp)]
        other = lax.dynamic_slice_in_dim(own, lax.rem(here + step, dp), 1, 0)
        vec = vec + lax.ppermute(other, "dp", pairs)
    cut = 8 * part + heads * (2 * size // dp)
    bias_grad = vec[:, 8 * part : cut].reshape(1, heads, -1)
    fc1_grad = vec[:, cut:].reshape(1, 1, -1)
    g_ln1, b_ln1, g_ln2, b_ln2, g_sc_attn, g_out_bias, g_sc_mlp, g_fc2_bias = (
        vec[:, i * part : (i + 1) * part] for i in range(8)
    )

    def owned(low, high):
        top = jnp.where(first, low.own, high.came.astype(F32))
        bottom = jnp.where(first, low.came.astype(F32), high.own)
        return jnp.concatenate([top, bottom], 0)

    g_ff = owned(sum_ff0, sum_ff1)
    g_att = jnp.where(
        first,
        sum_att0.own + sum_att0.came.astype(F32),
        sum_att1.own + sum_att1.came.astype(F32),
    )
    g_qkv = g_att[None, :, : 3 * width]
    g_out = g_att[:, 3 * width :].T[None]
    g_fc1 = g_ff[:, :units][None]
    g_fc2 = g_ff[:, units:].T[None]
    return (
        block_out, input_grads, g_ln1, b_ln1, g_qkv, bias_grad, g_out, g_out_bias, g_sc_attn,
        g_ln2, b_ln2, g_fc1, fc1_grad, g_fc2, g_fc2_bias, g_sc_mlp,
    )


def solution(mesh):
    vec = P("section", "dp")
    by_row = P("section", "dp", "tensor")
    by_unit = P("section", "tensor", "dp")
    data = P(None, "dp", "tensor", None)
    split = P("section", None, "dp", "tensor", None)
    given = (
        vec, vec, by_row, by_unit, by_unit, vec, vec, vec, vec, by_row, by_unit, by_unit, vec, vec,
    )
    return jax.shard_map(
        shards,
        mesh=mesh,
        in_specs=(data, data) + given,
        out_specs=(split, split) + given,
        check_vma=False,
    )
```

```python
from functools import partial

import jax
import jax.numpy as jnp
from jax import lax
from jax.experimental import pallas as pl
from jax.experimental.pallas import tpu as pltpu
from jax.sharding import PartitionSpec as P

EPSILON = 1e-06
BF = jnp.bfloat16
F32 = jnp.float32
MIB = 1 << 20

LN1_G, LN1_B, OUT_B, SC_ATTN, LN2_G, LN2_B, FC2_B, SC_MLP = range(8)


def dot(a, b):
    return lax.dot_general(a, b, (((1,), (0,)), ((), ())), preferred_element_type=F32)


def dot_bt(a, b):
    return lax.dot_general(a, b, (((1,), (1,)), ((), ())), preferred_element_type=F32)


def dot_at(a, b):
    return lax.dot_general(a, b, (((0,), (0,)), ((), ())), preferred_element_type=F32)


def turn(v):
    return v.astype(F32).T


def params(limit, grid=0):
    return pltpu.CompilerParams(
        vmem_limit_bytes=limit * MIB,
        dimension_semantics=("arbitrary",) * grid if grid else None,
    )


def late(v):
    return pltpu.with_memory_space_constraint(v, pltpu.HBM)


def whole(shape):
    return pl.BlockSpec(shape, lambda i: (0, 0), pipeline_mode=pl.Buffered(1))


def cost(micros):
    return pl.CostEstimate(flops=int(micros * 1.15e9), bytes_accessed=0, transcendentals=0)


def sds(shape, dtype):
    return jax.ShapeDtypeStruct(shape, dtype)


def core_swap(v):
    count = lax.axis_size("tensor")
    return lax.ppermute(v, "tensor", [(i, i ^ 1) for i in range(count)])


def from_chip(v, step):
    count = lax.axis_size("tensor")
    chips = count // 2
    pairs = [(((i // 2 + step) % chips) * 2 + i % 2, i) for i in range(count)]
    return lax.ppermute(v, "tensor", pairs)


def tie(v, *after):
    if not after:
        return v
    return lax.optimization_barrier((v, *after))[0]


def tie_all(vs, *after):
    return lax.optimization_barrier((*vs, *after))[: len(vs)]


def gather_tokens(own, work, beside=()):
    chips = lax.axis_size("tensor") // 2
    came = [from_chip(own, step) for step in range(1, chips)]
    chunks = [(own, core_swap(own))]
    results = [work(chunks[0])]
    for same in came:
        same = tie(same, results[-1], *beside)
        chunks.append((same, core_swap(same)))
        results.append(work(chunks[-1]))
    return chunks, results


def core_sums(sames, others):
    chips, rows = len(sames), sames[0].shape[0]
    if isinstance(others, (list, tuple)):
        came = [core_swap(v) for v in others[1:]]
        local = core_swap(tie(others[0], came[-1]))
    else:
        local = core_swap(others)
        came = [local[c * rows : (c + 1) * rows] for c in range(1, chips)]
    sums = [(a.astype(F32) + b.astype(F32)).astype(BF) for a, b in zip(sames[1:], came)]
    return sums, local


def send_sums(sums):
    chips = len(sums) + 1
    return [from_chip(both, chips - step) for step, both in enumerate(sums, 1)]


def scatter_tokens(sames, others, work=None, beside=None):
    sums, local = core_sums(sames, others)
    terms = send_sums(sums)
    made = work(sums[-1]) if work else local
    more = beside(sums[-1]) if beside else ()
    terms = [tie(t, made, local, *more) for t in terms]
    return [sames[0], *terms, local], made


def swap_section(v):
    return lax.ppermute(v, "section", [(0, 1), (1, 0)])


def assemble(shards, rows):
    count = len(shards)
    cut = len(shards[0])
    size, cols = rows // (count * cut), shards[0][0].shape[1]
    place = jnp.stack([lax.axis_index("dp"), lax.axis_index("section")])

    def body(place_ref, *refs):
        out_ref, sems = refs[count * cut :]
        z, x = place_ref[0], place_ref[1]
        started = []
        for k in range(count):
            base = lax.rem(z + (count - k), count) * (cut * size)
            for i, at in enumerate([base] if cut == 1 else [base + x * size, base + (1 - x) * size]):
                copy = pltpu.make_async_copy(
                    refs[k * cut + i].at[pl.ds(0, size), :],
                    out_ref.at[pl.ds(pl.multiple_of(at, size), size), :],
                    sems.at[k * cut + i],
                )
                copy.start()
                started.append(copy)
        for copy in started:
            copy.wait()

    hbm = pl.BlockSpec(memory_space=pl.ANY)
    return pl.pallas_call(
        body,
        in_specs=[pl.BlockSpec(memory_space=pltpu.SMEM)] + [hbm] * (count * cut),
        out_specs=pl.BlockSpec(memory_space=pltpu.VMEM),
        out_shape=sds((rows, cols), shards[0][0].dtype),
        scratch_shapes=[pltpu.SemaphoreType.DMA((count * cut,))],
        compiler_params=params(6),
        cost_estimate=cost(2),
        name="assemble",
    )(place, *[v for shard in shards for v in shard])


def half_of(v, which):
    half = v.shape[0] // 2
    return lax.dynamic_slice_in_dim(v, which * half, half, 0)


def direct(own):
    count = lax.axis_size("dp")
    return [
        lax.ppermute(own, "dp", [(i, (i + step) % count) for i in range(count)])
        for step in range(1, count)
    ]


def third(values, index):
    cuts = [-(-len(values) * i // 3) for i in range(4)]
    return values[cuts[index] : cuts[index + 1]]


class Ring:
    def __init__(self, own):
        self.last, self.hops, self.backs, self.at, self.back_at = own, [], [], 0, 0

    def hop(self, *gate):
        count = lax.axis_size("dp")
        pairs = [(i, (i + 1) % count) for i in range(count)]
        new = []
        for i in range(len(third(range(count - 1), self.at))):
            self.last = lax.ppermute(tie(self.last, *gate) if i == 0 else self.last, "dp", pairs)
            new.append(self.last)
        self.hops += new
        self.at += 1
        return new

    def back(self, *gate):
        count = lax.axis_size("dp")
        which = third(range(count - 1), self.back_at)
        new = [swap_section(tie(self.hops[i], *gate)) for i in which]
        self.backs += new
        self.back_at += 1
        return new


def in_order(back):
    count = len(back)
    ahead = [back[0], *back[:0:-1]]
    twice = jnp.stack(ahead + ahead)
    return lax.dynamic_slice_in_dim(twice, count - lax.axis_index("dp"), count, 0)


def dp_rows(v, back):
    dp = lax.axis_size("dp")
    part = v.shape[0] // dp
    place = lax.rem(lax.axis_index("dp") + (dp - back), dp)
    return lax.dynamic_slice_in_dim(v, place * part, part, 0)


class RingSum:
    def __init__(self, pair, mine, other=None):
        self.mine, self.other, self.pair = mine, other, pair
        self.terms, self.at, self.done = [], 0, 0

    def total(self, gate=()):
        first = tie(self.terms[0], *gate)
        return sum(t.astype(F32) for t in [first, *self.terms[1:]])

    def one(self, gate):
        dp = lax.axis_size("dp")
        self.done += 1
        new = []
        if self.terms:
            pairs = [(i, (i + 1) % dp) for i in range(dp)]
            self.sent = self.total(gate).astype(BF)
            new.append(lax.ppermute(self.sent, "dp", pairs))
        if self.other is not None:
            new.append(swap_section(tie(dp_rows(self.other, self.done), *gate)))
        self.terms = [*new, dp_rows(self.mine, self.done)]
        return new

    def step(self, *gate):
        self.at += 1
        if self.at == 5:
            self.own = self.total(gate)
            self.came = lax.ppermute(self.own.astype(BF), "section", [self.pair])
            return [self.came]
        count = 1 if self.at == 1 else len(third(range(lax.axis_size("dp") - 1), self.at - 2))
        return [v for i in range(count) for v in self.one(gate if i == 0 else ())]


def standardize(v):
    centred = v - jnp.mean(v, axis=-1, keepdims=True)
    var = jnp.mean(centred * centred, axis=-1, keepdims=True)
    scale = lax.rsqrt(var + EPSILON)
    return centred * scale, scale


def norm_of(v, vec, gain, shift):
    return (standardize(v)[0] * vec[gain : gain + 1, :] + vec[shift : shift + 1, :]).astype(BF)


def norm_back(v, grad, gain):
    xh, scale = standardize(v)
    dxh = grad * gain
    inner = jnp.mean(dxh * xh, axis=-1, keepdims=True)
    out = scale * (dxh - jnp.mean(dxh, axis=-1, keepdims=True) - xh * inner)
    return out, grad * xh


def total(refs):
    out = refs[0][...].astype(F32)
    for ref in refs[1:]:
        out = out + ref[...].astype(F32)
    return out


def fold(v, op):
    return op(v.reshape(-1, 8, v.shape[1]), axis=0)


def add_rows(ref, rows):
    for k, row in enumerate(rows):
        ref[8 * k : 8 * k + 8, :] += fold(row, jnp.sum)


def rowwise(body, row_ins, fulls, row_outs, sums, name):
    rows, width = row_ins[0].shape
    step = min(128, rows)
    some, outs = len(row_ins) + len(fulls), len(row_outs)

    def kernel(*refs):
        if not sums:
            body(*refs)
            return
        sum_ref, acc_ref = refs[some + outs :]

        @pl.when(pl.program_id(0) == 0)
        def _():
            acc_ref[...] = jnp.zeros_like(acc_ref)

        body(*refs[: some + outs], acc_ref)

        @pl.when(pl.program_id(0) == pl.num_programs(0) - 1)
        def _():
            for k in range(sums):
                sum_ref[k : k + 1, :] = jnp.sum(
                    acc_ref[8 * k : 8 * k + 8, :], axis=0, keepdims=True
                )

    out_shape = [sds((rows, width), d) for d in row_outs]
    out_shape += [sds((sums, width), F32)] if sums else []
    block = pl.BlockSpec((step, width), lambda i: (i, 0))
    return pl.pallas_call(
        kernel,
        grid=(rows // step,),
        in_specs=[block] * len(row_ins) + [whole(a.shape) for a in fulls],
        out_specs=[block] * outs + ([whole((sums, width))] if sums else []),
        out_shape=out_shape,
        scratch_shapes=[pltpu.VMEM((8 * sums, width), F32)] if sums else [],
        compiler_params=params(8, 1),
        cost_estimate=cost(2),
        name=name,
    )(*row_ins, *fulls)


def norm_first(x, vec):
    def body(x_ref, vec_ref, out_ref):
        out_ref[...] = norm_of(x_ref[...].astype(F32), vec_ref[...], LN1_G, LN1_B)

    return rowwise(body, [x], [vec], [BF], 0, "norm_first")[0]


def after_attention(x, terms, vec):
    count = len(terms)

    def body(*refs):
        x_ref, term_refs, vec_ref = refs[0], refs[1 : 1 + count], refs[1 + count]
        att_ref, res_ref, norm_ref = refs[2 + count :]
        v = vec_ref[...]
        attended = total(term_refs) + v[OUT_B : OUT_B + 1, :]
        residual = x_ref[...].astype(F32) + v[SC_ATTN : SC_ATTN + 1, :] * attended
        att_ref[...] = attended.astype(BF)
        res_ref[...] = residual
        norm_ref[...] = norm_of(residual, v, LN2_G, LN2_B)

    return rowwise(body, [x, *terms], [vec], [BF, F32, BF], 0, "after_attention")


def after_mlp(residual, terms, vec, vec_next):
    count = len(terms)

    def body(*refs):
        res_ref, term_refs = refs[0], refs[1 : 1 + count]
        vec_ref, next_ref, mlp_ref, y_ref, norm_ref = refs[1 + count :]
        v = vec_ref[...]
        mlp = total(term_refs) + v[FC2_B : FC2_B + 1, :]
        y = (res_ref[...] + v[SC_MLP : SC_MLP + 1, :] * mlp).astype(BF)
        mlp_ref[...] = mlp.astype(BF)
        y_ref[...] = y
        norm_ref[...] = norm_of(y.astype(F32), next_ref[...], LN1_G, LN1_B)

    return rowwise(body, [residual, *terms], [vec, vec_next], [BF, BF, BF], 0, "after_mlp")


def last_output(residual, terms, grad, vec):
    count = len(terms)

    def body(*refs):
        res_ref, term_refs = refs[0], refs[1 : 1 + count]
        grad_ref, vec_ref, y_ref, sum_ref = refs[1 + count :]
        v = vec_ref[...]
        mlp = total(term_refs) + v[FC2_B : FC2_B + 1, :]
        y_ref[...] = (res_ref[...] + v[SC_MLP : SC_MLP + 1, :] * mlp).astype(BF)
        add_rows(sum_ref, [grad_ref[...].astype(F32) * mlp])

    return rowwise(body, [residual, *terms, grad], [vec], [BF], 1, "last_output")


def start_back(grad, vec):
    def body(grad_ref, vec_ref, out_ref, sum_ref):
        low = (vec_ref[...][SC_MLP : SC_MLP + 1, :] * grad_ref[...].astype(F32)).astype(BF)
        out_ref[...] = low
        add_rows(sum_ref, [low.astype(F32)])

    return rowwise(body, [grad], [vec], [BF], 1, "start_back")


def back_second(grad, residual, attended, terms, vec):
    count = len(terms)

    def body(*refs):
        grad_ref, res_ref, att_ref = refs[:3]
        term_refs = refs[3 : 3 + count]
        vec_ref, dres_ref, low_ref, sum_ref = refs[3 + count :]
        v = vec_ref[...]
        dn = total(term_refs)
        back, dgain = norm_back(res_ref[...], dn, v[LN2_G : LN2_G + 1, :])
        dres = grad_ref[...].astype(F32) + back
        low = (v[SC_ATTN : SC_ATTN + 1, :] * dres).astype(BF)
        dres_ref[...] = dres
        low_ref[...] = low
        add_rows(sum_ref, [dgain, dn, dres * att_ref[...].astype(F32), low.astype(F32)])

    return rowwise(
        body, [grad, residual, attended, *terms], [vec], [F32, BF], 4, "back_second"
    )


def back_first(dres, x, terms, vec, mlp_below=None, vec_below=None):
    count = len(terms)
    below = mlp_below is not None

    def body(*refs):
        dres_ref, x_ref = refs[:2]
        term_refs = refs[2 : 2 + count]
        rest = refs[2 + count :]
        if below:
            mlp_ref, vec_ref, under_ref, dx_ref, low_ref, sum_ref = rest
        else:
            vec_ref, dx_ref, sum_ref = rest
        v = vec_ref[...]
        dn = total(term_refs)
        back, dgain = norm_back(x_ref[...].astype(F32), dn, v[LN1_G : LN1_G + 1, :])
        dx = (dres_ref[...] + back).astype(BF)
        dx_ref[...] = dx
        rows = [dgain, dn]
        if below:
            wide = dx.astype(F32)
            low = (under_ref[...][SC_MLP : SC_MLP + 1, :] * wide).astype(BF)
            low_ref[...] = low
            rows += [wide * mlp_ref[...].astype(F32), low.astype(F32)]
        add_rows(sum_ref, rows)

    row_ins = [dres, x, *terms] + ([mlp_below] if below else [])
    fulls = [vec] + ([vec_below] if below else [])
    return rowwise(body, row_ins, fulls, [BF, BF] if below else [BF], 4 if below else 2, "back_first")


def project_qkv(pair, weight, bias):
    rows, width = pair[0].shape
    cols = bias.shape[1]

    def body(a_ref, b_ref, w_ref, bias_ref, out_ref):
        w = w_ref[...]
        shift = bias_ref[...]
        out_ref[:rows, :] = (dot(a_ref[...], w) + shift).astype(BF)
        out_ref[rows:, :] = (dot(b_ref[...], w) + shift).astype(BF)

    return pl.pallas_call(
        body,
        grid=(1,),
        in_specs=[
            whole((rows, width)), whole((rows, width)), whole((width, cols)), whole((1, cols))
        ],
        out_specs=whole((2 * rows, cols)),
        out_shape=sds((2 * rows, cols), BF),
        compiler_params=params(6, 1),
        cost_estimate=cost(0.5),
        name="project_qkv",
    )(*pair, weight, bias)


def head_rows(v, head, size):
    rows = lax.broadcasted_iota(jnp.int32, v.shape, 0)
    return jnp.where(rows // size == head, v, jnp.zeros_like(v))


def head_cols(v, head, size):
    cols = lax.broadcasted_iota(jnp.int32, v.shape, 1)
    return jnp.where(cols // size == head, v, jnp.zeros_like(v))


def attention(packed, weight, size):
    chips = len(packed)
    span = packed[0].shape[0]
    half = span // 2
    width = packed[0].shape[1] // 3
    seq = chips * span
    heads = width // size
    model = weight.shape[0]
    step = min(256, seq)
    chunk = min(128, seq)
    score = size**-0.5

    def body(*refs):
        in_refs, w_ref = refs[:chips], refs[chips]
        head_refs = refs[chips + 1 : 2 * chips + 1]
        lse_ref = refs[2 * chips + 1]
        same_refs, other_ref = refs[2 * chips + 2 : 3 * chips + 2], refs[3 * chips + 2]
        k_ref, qt_ref, vt_ref, ot_ref, s_ref, p_ref = refs[3 * chips + 3 :]
        for c in range(chips):
            at = slice(c * span, (c + 1) * span)
            k_ref[at, :] = in_refs[c][:, width : 2 * width]
            qt_ref[:, at] = (turn(in_refs[c][:, :width]) * score).astype(BF)
            vt_ref[:, at] = turn(in_refs[c][:, 2 * width :]).astype(BF)

        def one(i, carry):
            at = pl.ds(pl.multiple_of(i * step, step), step)
            q = qt_ref[:, at]
            s_ref[0] = dot(k_ref[...], head_rows(q, 0, size))
            for h in range(heads):
                if h + 1 < heads:
                    s_ref[(h + 1) % 2] = dot(k_ref[...], head_rows(q, h + 1, size))
                now = h % 2
                top = fold(s_ref[now, :chunk, :], jnp.max)
                for r in range(chunk, seq, chunk):
                    top = jnp.maximum(top, fold(s_ref[now, r : r + chunk, :], jnp.max))
                top = jnp.max(top, axis=0, keepdims=True)
                norm = jnp.zeros((8, step), F32)
                for r in range(0, seq, chunk):
                    p = jnp.exp(s_ref[now, r : r + chunk, :] - top)
                    norm = norm + fold(p, jnp.sum)
                    p_ref[now, r : r + chunk, :] = p.astype(BF)
                norm = jnp.sum(norm, axis=0, keepdims=True)
                rows = slice(h * size, (h + 1) * size)
                ot_ref[rows, at] = dot(vt_ref[rows, :], p_ref[now]) / norm
                lse_ref[h : h + 1, at] = top + jnp.log(norm)
            return carry

        lax.fori_loop(0, seq // step, one, 0)
        for c in range(chips):
            at = slice(c * span, (c + 1) * span)
            o = ot_ref[:, at].T.astype(BF)
            head_refs[c][...] = o
            same_refs[c][...] = dot_bt(o[:half], w_ref[...]).astype(BF)
            other_ref[c * half : (c + 1) * half, :] = dot_bt(o[half:], w_ref[...]).astype(BF)

    out = pl.pallas_call(
        body,
        grid=(1,),
        in_specs=[whole((span, 3 * width))] * chips
        + [pl.BlockSpec((model, width), lambda i: (0, 3), pipeline_mode=pl.Buffered(1))],
        out_specs=[whole((span, width))] * chips
        + [whole((heads, seq))]
        + [whole((half, model))] * chips
        + [whole((seq // 2, model))],
        out_shape=[pltpu.HBM((span, width), BF)] * chips
        + [sds((heads, seq), F32)]
        + [sds((half, model), BF)] * chips
        + [sds((seq // 2, model), BF)],
        scratch_shapes=[
            pltpu.VMEM((seq, width), BF),
            pltpu.VMEM((width, seq), BF),
            pltpu.VMEM((width, seq), BF),
            pltpu.VMEM((width, seq), F32),
            pltpu.VMEM((2, seq, step), F32),
            pltpu.VMEM((2, seq, step), BF),
        ],
        compiler_params=params(14, 1),
        cost_estimate=cost(9),
        name="attention",
    )(*packed, weight)
    return out[:chips], out[chips], out[chips + 1 : -1], out[-1]


def attention_back(packed, heads_kept, lse, datt, weight, size):
    chips = len(packed)
    span = packed[0].shape[0]
    half = span // 2
    width = packed[0].shape[1] // 3
    seq = chips * span
    heads = width // size
    model = weight.shape[0]
    step = min(256, seq)
    chunk = min(128, seq)
    score = size**-0.5

    def body(*refs):
        at = 0

        def take(count):
            nonlocal at
            at += count
            return refs[at - count : at]

        in_refs, kept_refs = take(chips), take(chips)
        (lse_ref,) = take(1)
        datt_refs = take(2 * chips)
        (w_ref,) = take(1)
        dqkv_refs = take(chips)
        same_refs = take(chips)
        other_ref, sum_ref = take(2)
        k_ref, v_ref, kt_ref, qt_ref, q_ref, do_ref, dot_ref = take(7)
        inner_ref, s_ref, g_ref, p_ref, ds_ref, dk_ref, dv_ref, dqt_ref = take(8)
        for c in range(chips):
            rows = slice(c * span, (c + 1) * span)
            q = in_refs[c][:, :width].astype(F32) * score
            k = in_refs[c][:, width : 2 * width]
            q_ref[rows, :] = q.astype(BF)
            qt_ref[:, rows] = q.T.astype(BF)
            k_ref[rows, :] = k
            kt_ref[:, rows] = turn(k).astype(BF)
            v_ref[rows, :] = in_refs[c][:, 2 * width :]
            for b in range(2):
                d = dot(datt_refs[2 * c + b][...], w_ref[:, 3 * width :]).astype(BF)
                here = slice(c * span + b * half, c * span + (b + 1) * half)
                do_ref[here, :] = d
                dt = turn(d)
                dot_ref[:, here] = dt.astype(BF)
                prod = dt * turn(kept_refs[c][b * half : (b + 1) * half, :])
                for h in range(heads):
                    inner_ref[h : h + 1, here] = jnp.sum(
                        prod[h * size : (h + 1) * size, :], axis=0, keepdims=True
                    )

        def one(i, carry):
            at = pl.ds(pl.multiple_of(i * step, step), step)
            qt = qt_ref[:, at]
            dot_t = dot_ref[:, at]
            q = q_ref[at, :]
            do = do_ref[at, :]

            def scores(h):
                s_ref[h % 2] = dot(k_ref[...], head_rows(qt, h, size))
                g_ref[h % 2] = dot(v_ref[...], head_rows(dot_t, h, size))

            scores(0)
            for h in range(heads):
                if h + 1 < heads:
                    scores(h + 1)
                now = h % 2
                cols = slice(h * step, (h + 1) * step)
                lse = lse_ref[h : h + 1, at]
                inner = inner_ref[h : h + 1, at]
                for r in range(0, seq, chunk):
                    p = jnp.exp(s_ref[now, r : r + chunk, :] - lse)
                    ds = p * (g_ref[now, r : r + chunk, :] - inner)
                    p_ref[r : r + chunk, cols] = p.astype(BF)
                    ds_ref[r : r + chunk, cols] = ds.astype(BF)
                rows = slice(h * size, (h + 1) * size)
                dqt_ref[rows, at] = dot(kt_ref[rows, :], ds_ref[:, cols]) * score
            dv = dot(p_ref[...], jnp.concatenate([head_cols(do, h, size) for h in range(heads)], 0))
            dk = dot(ds_ref[...], jnp.concatenate([head_cols(q, h, size) for h in range(heads)], 0))

            @pl.when(i == 0)
            def _():
                dv_ref[...] = dv
                dk_ref[...] = dk

            @pl.when(i > 0)
            def _():
                dv_ref[...] += dv
                dk_ref[...] += dk

            return carry

        lax.fori_loop(0, seq // step, one, 0)
        for c in range(chips):
            rows = slice(c * span, (c + 1) * span)
            out = dqkv_refs[c]
            out[:, :width] = dqt_ref[:, rows].T.astype(BF)
            out[:, width : 2 * width] = dk_ref[rows, :].astype(BF)
            out[:, 2 * width :] = dv_ref[rows, :].astype(BF)
            sums = jnp.sum(out[...].astype(F32), axis=0, keepdims=True)
            if c == 0:
                sum_ref[...] = sums
            else:
                sum_ref[...] += sums
            w = w_ref[:, : 3 * width]
            same_refs[c][...] = dot_bt(out[:half, :], w).astype(BF)
            other_ref[c * half : (c + 1) * half, :] = dot_bt(out[half:, :], w).astype(BF)

    flat = [g for pair in datt for g in pair]
    out_shape = (
        [pltpu.HBM((span, 3 * width), BF)] * chips
        + [sds((half, model), BF)] * chips
        + [sds((seq // 2, model), BF), sds((1, 3 * width), F32)]
    )
    operands = (*map(late, (*packed, *heads_kept)), lse, *flat, late(weight))
    out = pl.pallas_call(
        body,
        grid=(1,),
        in_specs=[whole(a.shape) for a in operands],
        out_specs=[whole(a.shape) for a in out_shape],
        out_shape=out_shape,
        scratch_shapes=[
            pltpu.VMEM((seq, width), BF),
            pltpu.VMEM((seq, width), BF),
            pltpu.VMEM((width, seq), BF),
            pltpu.VMEM((width, seq), BF),
            pltpu.VMEM((seq, width), BF),
            pltpu.VMEM((seq, width), BF),
            pltpu.VMEM((width, seq), BF),
            pltpu.VMEM((heads, seq), F32),
            pltpu.VMEM((2, seq, step), F32),
            pltpu.VMEM((2, seq, step), F32),
            pltpu.VMEM((seq, heads * step), BF),
            pltpu.VMEM((seq, heads * step), BF),
            pltpu.VMEM((seq, width), F32),
            pltpu.VMEM((seq, width), F32),
            pltpu.VMEM((width, seq), F32),
        ],
        compiler_params=params(26, 1),
        cost_estimate=cost(15),
        name="attention_back",
    )(*operands)
    return out[:chips], out[chips : 2 * chips], out[2 * chips], out[2 * chips + 1]


def gelu_both(x):
    away = jnp.abs(x)
    t = 1.0 / (1.0 + (0.3275911 * 0.5**0.5) * away)
    bell = jnp.exp(-0.5 * (x * x))
    poly = t * (
        0.127414796
        + t * (-0.142248368 + t * (0.7107068705 + t * (-0.7265760135 + t * 0.5307027145)))
    )
    tail = poly * bell
    phi = jnp.where(x >= 0, 1.0 - tail, tail)
    return x * phi, phi + x * (bell * 0.3989422804014327)


def mlp_call(body, pairs, extra, weight, bias, outs, parts, scratch, name):
    rows, model = pairs[0].shape
    units = weight.shape[1] // 2
    step = min(256, units)
    blocks = units // step
    cols = lambda j: (0, j)
    in_specs = [whole((rows, model)) for _ in pairs]
    in_specs += [pl.BlockSpec((2 * rows, step), cols) for _ in extra]
    in_specs += [
        pl.BlockSpec((model, step), cols),
        pl.BlockSpec((model, step), lambda j: (0, blocks + j)),
        pl.BlockSpec((1, step), cols),
    ]
    out_specs = [pl.BlockSpec((2 * rows, step), cols) for _ in outs]
    out_specs += [pl.BlockSpec((1, step), cols)]
    out_specs += [whole((rows, model))] * (2 * parts)
    out_shape = [pltpu.HBM((2 * rows, units), d) for d in outs] + [sds((1, units), F32)]
    out_shape += [sds((rows, model), BF)] * (2 * parts)
    count = len(pairs) // 2
    return pl.pallas_call(
        body,
        grid=(blocks,),
        in_specs=in_specs,
        out_specs=out_specs,
        out_shape=out_shape,
        scratch_shapes=[pltpu.VMEM((2 * rows, model), F32)] * parts
        + [pltpu.VMEM((2 * rows, step), F32)] * scratch,
        compiler_params=params(8 + 5 * parts, 1),
        cost_estimate=cost(0.5),
        name=name,
    )(*pairs, *map(late, extra), weight, weight, bias)


def clear(*refs):
    @pl.when(pl.program_id(0) == 0)
    def _():
        for ref in refs:
            ref[...] = jnp.zeros_like(ref)


def finish(acc, low, high):
    rows = low.shape[0]

    @pl.when(pl.program_id(0) == pl.num_programs(0) - 1)
    def _():
        low[...] = acc[:rows, :].astype(BF)
        high[...] = acc[rows:, :].astype(BF)


CHUNK = 32


def mlp_forward(pair, weight, bias):
    rows = pair[0].shape[0]

    def body(a, b, w1_ref, w2_ref, bias_ref, act_ref, slope_ref, sum_ref, lo, hi, acc, pre):
        clear(acc, sum_ref)
        shift = bias_ref[...]
        for i, x in enumerate((a, b)):
            pre[i * rows : (i + 1) * rows, :] = dot(x[...], w1_ref[...])
        for i in range(2):
            at = slice(i * rows, (i + 1) * rows)
            for r in range(i * rows, (i + 1) * rows, CHUNK):
                act, slope = gelu_both(pre[r : r + CHUNK, :] + shift)
                act_ref[r : r + CHUNK, :] = act.astype(BF)
                slope_ref[r : r + CHUNK, :] = slope.astype(BF)
            acc[at, :] += dot_bt(act_ref[at, :], w2_ref[...])
        finish(acc, lo, hi)

    act, slope, _, lo, hi = mlp_call(body, pair, [], weight, bias, [BF, BF], 1, 1, "mlp_forward")
    return act, slope, lo, hi


def mlp_backward(pair, slope, weight, bias):
    rows = pair[0].shape[0]

    def body(a, b, slope_ref, w1_ref, w2_ref, bias_ref, dpre_ref, sum_ref, lo, hi, acc, pre):
        clear(acc)
        for i, g in enumerate((a, b)):
            pre[i * rows : (i + 1) * rows, :] = dot(g[...], w2_ref[...])
        sums = jnp.zeros((8, bias_ref.shape[1]), F32)
        for i in range(2):
            at = slice(i * rows, (i + 1) * rows)
            for r in range(i * rows, (i + 1) * rows, CHUNK):
                d = pre[r : r + CHUNK, :] * slope_ref[r : r + CHUNK, :].astype(F32)
                d = d.astype(BF)
                dpre_ref[r : r + CHUNK, :] = d
                sums = sums + fold(d.astype(F32), jnp.sum)
            acc[at, :] += dot_bt(dpre_ref[at, :], w1_ref[...])
        sum_ref[...] = jnp.sum(sums, axis=0, keepdims=True)
        finish(acc, lo, hi)

    dpre, sums, lo, hi = mlp_call(
        body, pair, [slope], weight, bias, [BF], 1, 1, "mlp_backward"
    )
    return dpre, sums, lo, hi


def mlp_both(pair, grads, weight, bias):
    rows = pair[0].shape[0]

    def body(
        a, b, c, d, w1_ref, w2_ref, bias_ref, act_ref, dpre_ref, sum_ref,
        lo, hi, blo, bhi, acc, back, pre, grad,
    ):
        clear(acc, back)
        shift = bias_ref[...]
        for i, (x, g) in enumerate(((a, c), (b, d))):
            at = slice(i * rows, (i + 1) * rows)
            pre[at, :] = dot(x[...], w1_ref[...])
            grad[at, :] = dot(g[...], w2_ref[...])
        sums = jnp.zeros((8, bias_ref.shape[1]), F32)
        for i in range(2):
            at = slice(i * rows, (i + 1) * rows)
            for r in range(i * rows, (i + 1) * rows, CHUNK):
                act, slope = gelu_both(pre[r : r + CHUNK, :] + shift)
                act_ref[r : r + CHUNK, :] = act.astype(BF)
                dpre = (grad[r : r + CHUNK, :] * slope).astype(BF)
                dpre_ref[r : r + CHUNK, :] = dpre
                sums = sums + fold(dpre.astype(F32), jnp.sum)
            back[at, :] += dot_bt(dpre_ref[at, :], w1_ref[...])
            acc[at, :] += dot_bt(act_ref[at, :], w2_ref[...])
        sum_ref[...] = jnp.sum(sums, axis=0, keepdims=True)
        finish(acc, lo, hi)
        finish(back, blo, bhi)

    act, dpre, sums, lo, hi, blo, bhi = mlp_call(
        body, [*pair, *grads], [], weight, bias, [BF, BF], 2, 2, "mlp_both"
    )
    return act, dpre, sums, lo, hi, blo, bhi


def weight_grads(products, dp, side, name, halves=True, heads=0):
    model = products[0][0][0].shape[1]
    step = model // dp
    half = step // 2
    cut = 2 if halves else 1
    sizes = [(len(left), len(right), right[0].shape[1]) for left, right in products]
    cols = sum(n for _, _, n in sizes)

    def body(side_ref, *refs):
        acc_ref = refs[-1]
        mine, other = refs[-3:-1] if halves else (refs[-2], None)
        at = base = 0
        for many, few, n in sizes:
            lefts, rights = refs[at : at + many], refs[at + many : at + many + few]
            at += many + few
            ratio = many // few
            acc = None
            for i in range(many):
                size = lefts[i].shape[0]
                here = slice((i % ratio) * size, (i % ratio + 1) * size)
                term = dot_at(lefts[i][...], rights[i // ratio][here, :])
                acc = term if acc is None else acc + term
            if halves:
                acc_ref[:, base : base + n] = acc
            elif heads and not base:
                size = n // (3 * heads)
                for k in range(3 * heads):
                    head, kind = k // 3, k % 3
                    at_k = (kind * heads + head) * size
                    mine[:, k * size : (k + 1) * size] = acc[:, at_k : at_k + size].astype(BF)
            else:
                mine[:, base : base + n] = acc.astype(BF)
            base += n
        if not halves:
            return
        low = pl.multiple_of(side_ref[0] * half, half)
        high = pl.multiple_of((1 - side_ref[0]) * half, half)
        mine[...] = acc_ref[pl.ds(low, half), :].astype(BF)
        other[...] = acc_ref[pl.ds(high, half), :].astype(BF)

    specs, operands = [pl.BlockSpec(memory_space=pltpu.SMEM)], [side.reshape(1)]
    for left, right in products:
        specs += [pl.BlockSpec((a.shape[0], step), lambda i: (0, i)) for a in left]
        specs += [whole(b.shape) for b in right]
        operands += [*left, *right]
    return pl.pallas_call(
        body,
        grid=(dp,),
        in_specs=specs,
        out_specs=[pl.BlockSpec((step // cut, cols), lambda i: (i, 0))] * cut,
        out_shape=[sds((model // cut, cols), BF)] * cut,
        scratch_shapes=[pltpu.VMEM((step, cols), F32)],
        compiler_params=params(14, 1),
        cost_estimate=cost(5),
        name=name,
    )(*operands)


def pieces(chunks):
    return [p for pair in chunks for p in pair]


def shards(
    tokens, cotangent, ln1_gain, ln1_bias, w_qkv, qv_bias, w_out, out_bias, scale_attn,
    ln2_gain, ln2_bias, w_fc1, fc1_bias, w_fc2, fc2_bias, scale_mlp,
):
    side = lax.axis_index("section")
    first = side == 0
    dp = lax.axis_size("dp")
    here = lax.axis_index("dp")
    chips = lax.axis_size("tensor") // 2
    rows, model = tokens.shape[2:]
    heads = qv_bias.shape[1]
    size = qv_bias.shape[2] * dp // 2
    width = heads * size
    units = w_fc1.shape[2]
    part = model // dp

    x0 = lax.dynamic_index_in_dim(tokens, side, 0, keepdims=False).reshape(rows, model)
    grad_top = lax.dynamic_index_in_dim(cotangent, side, 0, keepdims=False).reshape(rows, model)

    vectors = (ln1_gain, ln1_bias, out_bias, scale_attn, ln2_gain, ln2_bias, fc2_bias, scale_mlp)
    packed = jnp.concatenate(
        [v.reshape(-1) for v in vectors] + [fc1_bias.reshape(-1), qv_bias.reshape(-1)]
    )
    own_qkv = w_qkv.reshape(part, heads, 3, size).swapaxes(1, 2).reshape(part, 3 * width)
    own_att = jnp.concatenate([own_qkv, w_out[0].T], axis=1)
    give_att = half_of(own_att, 1 - side)
    came_att = swap_section(give_att)
    came_small = swap_section(tie(packed, give_att))
    both_small = jnp.concatenate(
        [jnp.where(first, packed, came_small), jnp.where(first, came_small, packed)]
    )
    cols = 4 * width
    tail = -(-both_small.size // (16 * cols)) * 16
    both_small = jnp.pad(both_small, (0, tail * cols - both_small.size)).reshape(tail, cols)
    mine_att = half_of(own_att, side)
    ring_att0 = jnp.concatenate([jnp.where(first, mine_att, came_att), both_small])
    ring_att1 = jnp.where(first, came_att, mine_att)
    hops_att0 = direct(ring_att0)
    own_ff = jnp.concatenate([w_fc1[0], w_fc2[0].T], axis=1)
    rest_att = swap_section(tie(mine_att, ring_att0))
    came_ff = swap_section(tie(half_of(own_ff, 1 - side), ring_att0))
    mine_ff = half_of(own_ff, side)
    ring_ff0 = jnp.where(first, mine_ff, came_ff)
    ring_ff1 = jnp.where(first, came_ff, mine_ff)

    def other_half(own, rest):
        left = half_of(own, 1 - side)
        return jnp.where(first, left, rest), jnp.where(first, rest, left)


    backs = [swap_section(v) for v in hops_att0]
    back = [ring_att0, *hops_att0]
    back[2] = tie(back[2], backs[0], *backs[2:])
    flat = in_order([v[-tail:] for v in back])
    flat = flat.reshape(dp, -1)[:, : 2 * packed.size].reshape(dp, 2, -1).astype(F32)
    cut = 8 * part
    vecs = flat[:, :, :cut].reshape(dp, 2, 8, part).transpose(1, 2, 0, 3).reshape(2, 8, model)
    vecs = (vecs[0], vecs[1])
    bias_fc1 = flat[:, :, cut : cut + units // dp].swapaxes(0, 1).reshape(2, 1, units)
    qv = flat[:, :, cut + units // dp :].reshape(dp, 2, heads, -1).transpose(1, 2, 0, 3)
    qv = qv.reshape(2, heads, 2, size)
    bias_qkv = jnp.stack([qv[:, :, 0], jnp.zeros_like(qv[:, :, 0]), qv[:, :, 1]], axis=1)
    bias_qkv = bias_qkv.reshape(2, 1, 3 * width)

    norm1 = norm_first(tie(x0, came_ff), vecs[0])
    rest_ff = swap_section(tie(mine_ff, norm1))
    rest_att0, rest_att1 = other_half(own_att, rest_att)
    rest_ff0, rest_ff1 = other_half(own_ff, rest_ff)
    att1 = Ring(ring_att1)
    att0 = assemble([(tie(ring_att0, norm1), rest_att0), *zip(hops_att0, backs)], model)
    ff0, ff1 = Ring(ring_ff0), Ring(ring_ff1)
    hop_ff0 = ff0.hop(norm1)

    def projection(weight, s):
        return lambda pair: project_qkv(pair, weight, bias_qkv[s])

    chunks0, qkv0 = gather_tokens(norm1, projection(att0, 0), [rest_ff, *hop_ff0])
    beside = [*ff0.hop(), *ff0.back()]
    kept0, lse0, sames, others = attention(qkv0, att0, size)
    terms, _ = scatter_tokens(
        sames,
        tie(others, *beside),
        beside=lambda gate: [*ff0.hop(gate), *ff0.back(gate), *att1.hop(gate)],
    )
    attended0, residual0, norm2 = after_attention(x0, terms, vecs[0])
    ff0.back()
    beside = [*att1.hop(norm2), *att1.back(norm2)]
    w_ff0 = assemble([(ring_ff0, rest_ff0), *zip(ff0.hops, ff0.backs)], model)
    second0, mlp0 = gather_tokens(
        norm2, lambda pair: mlp_forward(pair, w_ff0, bias_fc1[0]), beside
    )
    act0, slope0, sames, others = zip(*mlp0)
    beside = [*att1.hop(second0[-1][0]), *att1.back(second0[-1][0])]
    terms, _ = scatter_tokens(
        sames,
        [others[0], *[tie(v, *beside) for v in others[1:]]],
        beside=lambda gate: [*ff1.hop(gate), *att1.back(gate)],
    )
    mlp_out0, y0, norm1 = after_mlp(residual0, terms, vecs[0], vecs[1])

    w_att1 = assemble([(ring_att1, rest_att1), *zip(att1.hops, att1.backs)], model)
    low1, sums_fc2_1 = start_back(grad_top, vecs[1])
    beside = [*ff1.hop(norm1), *ff1.back(norm1)]
    chunks1, qkv1 = gather_tokens(norm1, projection(w_att1, 1), beside)
    gate = chunks1[-1][0]
    came = [from_chip(tie(low1, gate), step) for step in range(1, chips)]
    beside = [*came, *ff1.hop(gate), *ff1.back(gate)]
    kept1, lse1, sames, others = attention(qkv1, w_att1, size)
    others = tie(others, *beside)
    grads1 = [(low1, core_swap(low1))] + [(v, core_swap(tie(v, lse1))) for v in came]
    terms, _ = scatter_tokens(
        sames, others, beside=lambda gate: [*ff1.back(gate), *pieces(grads1)]
    )
    attended1, residual1, norm2 = after_attention(y0, terms, vecs[1])
    w_ff1 = assemble([(ring_ff1, rest_ff1), *zip(ff1.hops, ff1.backs)], model)
    spare = list(grads1)
    second1, mlp1 = gather_tokens(
        norm2, lambda pair: mlp_both(pair, spare.pop(0), w_ff1, bias_fc1[1])
    )
    act1, dpre1, sums_fc1_1, sames_y1, others_y1, sames, others = zip(*mlp1)

    def grad_ff(second, dpre, grads, act):
        return lambda after: weight_grads(
            [
                (pieces(second), [late(tie(dpre[0], after)), *map(late, dpre[1:])]),
                (pieces(grads), [late(a) for a in act]),
            ],
            dp,
            side,
            "grad_ff",
        )

    def grad_att(chunks, dqkv, datt, kept):
        return lambda after: weight_grads(
            [
                (pieces(chunks), [late(tie(dqkv[0], after)), *map(late, dqkv[1:])]),
                (pieces(datt), [late(a) for a in kept]),
            ],
            dp,
            side,
            "grad_att",
            False,
            heads,
        )[0]

    old = [tuple(map(late, pair)) for pair in grads1]
    terms, g = scatter_tokens(sames, others, grad_ff(second1, dpre1, old, act1))
    sum_ff1 = RingSum((0, 1), *g)
    dres1, low, sums1 = back_second(grad_top, residual1, attended1, terms, vecs[1])
    came_y0 = lax.ppermute(tie(y0, low), "section", [(1, 0)])
    datt, _ = gather_tokens(low, lambda pair: pair[0], sum_ff1.step())
    sums_y1, local_y1 = core_sums(sames_y1, [tie(v, low) for v in others_y1])
    terms_y1 = send_sums([tie(v, datt[-1][0]) for v in sums_y1])
    beside = [came_y0, *terms_y1, *sum_ff1.step(low)]
    dqkv, sames, others, qkv_sums1 = attention_back(qkv1, kept1, lse1, datt, w_att1, size)
    old = [tuple(map(late, pair)) for pair in chunks1]
    terms, g = scatter_tokens(
        sames, tie(others, *beside), grad_att(old, dqkv, datt, kept1), sum_ff1.step
    )
    sum_att1 = RingSum((0, 1), g)
    sum_att1.step()
    dx1, low0, edge1 = back_first(dres1, late(y0), terms, vecs[1], late(mlp_out0), vecs[0])

    y1, sums_sc_1 = last_output(
        residual1, [tie(sames_y1[0], low0), *terms_y1, local_y1], grad_top, vecs[1]
    )

    slopes = list(slope0)
    grads0, mlp_back0 = gather_tokens(
        low0,
        lambda pair: mlp_backward(pair, slopes.pop(0), w_ff0, bias_fc1[0]),
        [y1, *sum_ff1.step(low0)],
    )
    dpre0, sums_fc1_0, sames, others = zip(*mlp_back0)
    old = [tuple(map(late, pair)) for pair in second0]
    terms, g = scatter_tokens(
        sames,
        others,
        grad_ff(old, dpre0, grads0, act0),
        lambda gate: [*sum_ff1.step(gate), *sum_att1.step(gate)],
    )
    sum_ff0 = RingSum((1, 0), *g)
    dres0, low, sums0 = back_second(
        dx1, late(residual0), late(attended0), terms, vecs[0]
    )
    beside = [*sum_att1.step(low), *sum_ff0.step(low)]
    datt, _ = gather_tokens(low, lambda pair: pair[0], beside)
    came_y1 = lax.ppermute(tie(y1, low), "section", [(0, 1)])
    beside = [came_y1, *sum_att1.step(low), *sum_ff0.step(low)]
    dqkv, sames, others, qkv_sums0 = attention_back(qkv0, kept0, lse0, datt, att0, size)
    old = [tuple(map(late, pair)) for pair in chunks0]
    terms, g = scatter_tokens(
        sames, tie(others, *beside), grad_att(old, dqkv, datt, kept0), sum_ff0.step
    )
    sum_att0 = RingSum((1, 0), g)
    sum_att0.step()
    going = sum_att0.step()
    dx0, edge0 = back_first(dres0, x0, terms, vecs[0])
    came_dx0 = lax.ppermute(dx0, "section", [(1, 0)])
    step_ff0 = sum_ff0.step(dx0)
    second_hop = sum_att0.step(dx0)
    step_att1 = sum_att1.step(sames[0])
    third_hop = sum_att0.step()
    last_ff0 = sum_ff0.step()
    sum_att0.step()
    came_dx1 = lax.ppermute(tie(dx1, sum_att0.own), "section", [(0, 1)])

    def both(low, high, came_low, came_high):
        mine = jnp.where(first, low, high)
        came = jnp.where(first, came_low, came_high)
        return jnp.stack([jnp.where(first, mine, came), jnp.where(first, came, mine)])[None, :, None]

    block_out = both(y0, tie(y1, *second_hop), came_y0, came_y1)
    input_grads = both(dx0, dx1, came_dx0, came_dx1)
    sum_att0.came = tie(sum_att0.came, block_out, input_grads)

    def by_unit(qkv_sums, unit_sums):
        q = qkv_sums[:, :width].reshape(heads, 1, size)
        v = qkv_sums[:, 2 * width :].reshape(heads, 1, size)
        bias = jnp.concatenate([q, v], 1).reshape(heads, dp, -1).swapaxes(0, 1).reshape(dp, -1)
        return jnp.concatenate([bias, unit_sums.reshape(dp, -1)], axis=1)

    unit0 = by_unit(tie(qkv_sums0, dx0), sum(sums_fc1_0))
    unit1 = by_unit(tie(qkv_sums1, dx0), sum(sums_fc1_1))
    vec = jnp.concatenate(
        [edge0[:2], sums0[:4], edge1[2:4], edge1[:2], sums1[:4], sums_sc_1[:1], sums_fc2_1[:1]]
    )
    vec = tie(vec, *going, *step_att1)
    vec = vec + core_swap(vec)
    vec = tie(sum([from_chip(vec, step) for step in range(1, chips)], vec), *step_ff0, *second_hop)
    vec = tie(vec, sum_att0.sent)
    vec = vec.reshape(2, 8, dp, part).swapaxes(1, 2).reshape(2, dp, 8 * part)
    vec0 = jnp.concatenate([vec[0], unit0], axis=1)
    vec1 = jnp.concatenate([vec[1], unit1], axis=1)
    own = jnp.where(first, vec0, vec1) + swap_section(jnp.where(first, vec1, vec0))
    own = tie(own, *last_ff0)
    vec = lax.dynamic_slice_in_dim(own, here, 1, 0)
    for step in range(1, dp):
        pairs = [(i, (i + step) % dp) for i in range(dp)]
        other = lax.dynamic_slice_in_dim(own, lax.rem(here + step, dp), 1, 0)
        vec = vec + lax.ppermute(other, "dp", pairs)
    cut = 8 * part + heads * (2 * size // dp)
    bias_grad = vec[:, 8 * part : cut].reshape(1, heads, -1)
    fc1_grad = vec[:, cut:].reshape(1, 1, -1)
    g_ln1, b_ln1, g_ln2, b_ln2, g_sc_attn, g_out_bias, g_sc_mlp, g_fc2_bias = (
        vec[:, i * part : (i + 1) * part] for i in range(8)
    )

    def owned(low, high):
        top = jnp.where(first, low.own, high.came.astype(F32))
        bottom = jnp.where(first, low.came.astype(F32), high.own)
        return jnp.concatenate([top, bottom], 0)

    g_ff = owned(sum_ff0, sum_ff1)
    g_att = jnp.where(
        first,
        sum_att0.own + sum_att0.came.astype(F32),
        sum_att1.own + sum_att1.came.astype(F32),
    )
    g_qkv = g_att[None, :, : 3 * width]
    g_out = g_att[:, 3 * width :].T[None]
    g_fc1 = g_ff[:, :units][None]
    g_fc2 = g_ff[:, units:].T[None]
    return (
        block_out, input_grads, g_ln1, b_ln1, g_qkv, bias_grad, g_out, g_out_bias, g_sc_attn,
        g_ln2, b_ln2, g_fc1, fc1_grad, g_fc2, g_fc2_bias, g_sc_mlp,
    )


def solution(mesh):
    vec = P("section", "dp")
    by_row = P("section", "dp", "tensor")
    by_unit = P("section", "tensor", "dp")
    data = P(None, "dp", "tensor", None)
    split = P("section", None, "dp", "tensor", None)
    given = (
        vec, vec, by_row, by_unit, by_unit, vec, vec, vec, vec, by_row, by_unit, by_unit, vec, vec,
    )
    return jax.shard_map(
        shards,
        mesh=mesh,
        in_specs=(data, data) + given,
        out_specs=(split, split) + given,
        check_vma=False,
    )
```

```python
from functools import partial

import jax
import jax.numpy as jnp
from jax import lax
from jax.experimental import pallas as pl
from jax.experimental.pallas import tpu as pltpu
from jax.sharding import PartitionSpec as P

EPSILON = 1e-06
BF = jnp.bfloat16
F32 = jnp.float32
MIB = 1 << 20

LN1_G, LN1_B, OUT_B, SC_ATTN, LN2_G, LN2_B, FC2_B, SC_MLP = range(8)


def dot(a, b):
    return lax.dot_general(a, b, (((1,), (0,)), ((), ())), preferred_element_type=F32)


def dot_bt(a, b):
    return lax.dot_general(a, b, (((1,), (1,)), ((), ())), preferred_element_type=F32)


def dot_at(a, b):
    return lax.dot_general(a, b, (((0,), (0,)), ((), ())), preferred_element_type=F32)


def turn(v):
    return v.astype(F32).T


def params(limit, grid=0):
    return pltpu.CompilerParams(
        vmem_limit_bytes=limit * MIB,
        dimension_semantics=("arbitrary",) * grid if grid else None,
    )


def late(v):
    return pltpu.with_memory_space_constraint(v, pltpu.HBM)


def whole(shape):
    return pl.BlockSpec(shape, lambda i: (0, 0), pipeline_mode=pl.Buffered(1))


def cost(micros):
    return pl.CostEstimate(flops=int(micros * 1.15e9), bytes_accessed=0, transcendentals=0)


def sds(shape, dtype):
    return jax.ShapeDtypeStruct(shape, dtype)


def core_swap(v):
    count = lax.axis_size("tensor")
    return lax.ppermute(v, "tensor", [(i, i ^ 1) for i in range(count)])


def from_chip(v, step):
    count = lax.axis_size("tensor")
    chips = count // 2
    pairs = [(((i // 2 + step) % chips) * 2 + i % 2, i) for i in range(count)]
    return lax.ppermute(v, "tensor", pairs)


def tie(v, *after):
    if not after:
        return v
    return lax.optimization_barrier((v, *after))[0]


def tie_all(vs, *after):
    return lax.optimization_barrier((*vs, *after))[: len(vs)]


def gather_tokens(own, work, beside=()):
    chips = lax.axis_size("tensor") // 2
    came = [from_chip(own, step) for step in range(1, chips)]
    chunks = [(own, core_swap(own))]
    results = [work(chunks[0])]
    for same in came:
        same = tie(same, results[-1], *beside)
        chunks.append((same, core_swap(same)))
        results.append(work(chunks[-1]))
    return chunks, results


def core_sums(sames, others):
    chips, rows = len(sames), sames[0].shape[0]
    if isinstance(others, (list, tuple)):
        came = [core_swap(v) for v in others[1:]]
        local = core_swap(tie(others[0], came[-1]))
    else:
        local = core_swap(others)
        came = [local[c * rows : (c + 1) * rows] for c in range(1, chips)]
    sums = [(a.astype(F32) + b.astype(F32)).astype(BF) for a, b in zip(sames[1:], came)]
    return sums, local


def send_sums(sums):
    chips = len(sums) + 1
    return [from_chip(both, chips - step) for step, both in enumerate(sums, 1)]


def scatter_tokens(sames, others, work=None, beside=None):
    sums, local = core_sums(sames, others)
    terms = send_sums(sums)
    made = work(sums[-1]) if work else local
    more = beside(sums[-1]) if beside else ()
    terms = [tie(t, made, local, *more) for t in terms]
    return [sames[0], *terms, local], made


def swap_section(v):
    return lax.ppermute(v, "section", [(0, 1), (1, 0)])


def assemble(shards, rows):
    count = len(shards)
    cut = len(shards[0])
    size, cols = rows // (count * cut), shards[0][0].shape[1]
    place = jnp.stack([lax.axis_index("dp"), lax.axis_index("section")])

    def body(place_ref, *refs):
        out_ref, sems = refs[count * cut :]
        z, x = place_ref[0], place_ref[1]
        started = []
        for k in range(count):
            base = lax.rem(z + (count - k), count) * (cut * size)
            for i, at in enumerate([base] if cut == 1 else [base + x * size, base + (1 - x) * size]):
                copy = pltpu.make_async_copy(
                    refs[k * cut + i].at[pl.ds(0, size), :],
                    out_ref.at[pl.ds(pl.multiple_of(at, size), size), :],
                    sems.at[k * cut + i],
                )
                copy.start()
                started.append(copy)
        for copy in started:
            copy.wait()

    hbm = pl.BlockSpec(memory_space=pl.ANY)
    return pl.pallas_call(
        body,
        in_specs=[pl.BlockSpec(memory_space=pltpu.SMEM)] + [hbm] * (count * cut),
        out_specs=pl.BlockSpec(memory_space=pltpu.VMEM),
        out_shape=sds((rows, cols), shards[0][0].dtype),
        scratch_shapes=[pltpu.SemaphoreType.DMA((count * cut,))],
        compiler_params=params(6),
        cost_estimate=cost(2),
        name="assemble",
    )(place, *[late(v) for shard in shards for v in shard])


def half_of(v, which):
    half = v.shape[0] // 2
    return lax.dynamic_slice_in_dim(v, which * half, half, 0)


def direct(own):
    count = lax.axis_size("dp")
    return [
        lax.ppermute(own, "dp", [(i, (i + step) % count) for i in range(count)])
        for step in range(1, count)
    ]


def third(values, index):
    cuts = [-(-len(values) * i // 3) for i in range(4)]
    return values[cuts[index] : cuts[index + 1]]


class Ring:
    def __init__(self, own):
        self.last, self.hops, self.backs, self.at, self.back_at = own, [], [], 0, 0

    def hop(self, *gate):
        count = lax.axis_size("dp")
        pairs = [(i, (i + 1) % count) for i in range(count)]
        new = []
        for i in range(len(third(range(count - 1), self.at))):
            self.last = lax.ppermute(tie(self.last, *gate) if i == 0 else self.last, "dp", pairs)
            new.append(self.last)
        self.hops += new
        self.at += 1
        return new

    def back(self, *gate):
        count = lax.axis_size("dp")
        which = third(range(count - 1), self.back_at)
        new = [swap_section(tie(self.hops[i], *gate)) for i in which]
        self.backs += new
        self.back_at += 1
        return new


def in_order(back):
    count = len(back)
    ahead = [back[0], *back[:0:-1]]
    twice = jnp.stack(ahead + ahead)
    return lax.dynamic_slice_in_dim(twice, count - lax.axis_index("dp"), count, 0)


def dp_rows(v, back):
    dp = lax.axis_size("dp")
    part = v.shape[0] // dp
    place = lax.rem(lax.axis_index("dp") + (dp - back), dp)
    return lax.dynamic_slice_in_dim(v, place * part, part, 0)


class RingSum:
    def __init__(self, pair, mine, other=None):
        self.mine, self.other, self.pair = mine, other, pair
        self.terms, self.at, self.done = [], 0, 0

    def total(self, gate=()):
        first = tie(self.terms[0], *gate)
        return sum(t.astype(F32) for t in [first, *self.terms[1:]])

    def one(self, gate):
        dp = lax.axis_size("dp")
        self.done += 1
        new = []
        if self.terms:
            pairs = [(i, (i + 1) % dp) for i in range(dp)]
            self.sent = self.total(gate).astype(BF)
            new.append(lax.ppermute(self.sent, "dp", pairs))
        if self.other is not None:
            new.append(swap_section(tie(dp_rows(self.other, self.done), *gate)))
        self.terms = [*new, dp_rows(self.mine, self.done)]
        return new

    def step(self, *gate):
        self.at += 1
        if self.at == 5:
            self.own = self.total(gate)
            self.came = lax.ppermute(self.own.astype(BF), "section", [self.pair])
            return [self.came]
        count = 1 if self.at == 1 else len(third(range(lax.axis_size("dp") - 1), self.at - 2))
        return [v for i in range(count) for v in self.one(gate if i == 0 else ())]


def standardize(v):
    centred = v - jnp.mean(v, axis=-1, keepdims=True)
    var = jnp.mean(centred * centred, axis=-1, keepdims=True)
    scale = lax.rsqrt(var + EPSILON)
    return centred * scale, scale


def norm_of(v, vec, gain, shift):
    return (standardize(v)[0] * vec[gain : gain + 1, :] + vec[shift : shift + 1, :]).astype(BF)


def norm_back(v, grad, gain):
    xh, scale = standardize(v)
    dxh = grad * gain
    inner = jnp.mean(dxh * xh, axis=-1, keepdims=True)
    out = scale * (dxh - jnp.mean(dxh, axis=-1, keepdims=True) - xh * inner)
    return out, grad * xh


def total(refs):
    out = refs[0][...].astype(F32)
    for ref in refs[1:]:
        out = out + ref[...].astype(F32)
    return out


def fold(v, op):
    return op(v.reshape(-1, 8, v.shape[1]), axis=0)


def add_rows(ref, rows):
    for k, row in enumerate(rows):
        ref[8 * k : 8 * k + 8, :] += fold(row, jnp.sum)


def rowwise(body, row_ins, fulls, row_outs, sums, name):
    rows, width = row_ins[0].shape
    step = min(128, rows)
    some, outs = len(row_ins) + len(fulls), len(row_outs)

    def kernel(*refs):
        if not sums:
            body(*refs)
            return
        sum_ref, acc_ref = refs[some + outs :]

        @pl.when(pl.program_id(0) == 0)
        def _():
            acc_ref[...] = jnp.zeros_like(acc_ref)

        body(*refs[: some + outs], acc_ref)

        @pl.when(pl.program_id(0) == pl.num_programs(0) - 1)
        def _():
            for k in range(sums):
                sum_ref[k : k + 1, :] = jnp.sum(
                    acc_ref[8 * k : 8 * k + 8, :], axis=0, keepdims=True
                )

    out_shape = [sds((rows, width), d) for d in row_outs]
    out_shape += [sds((sums, width), F32)] if sums else []
    block = pl.BlockSpec((step, width), lambda i: (i, 0))
    return pl.pallas_call(
        kernel,
        grid=(rows // step,),
        in_specs=[block] * len(row_ins) + [whole(a.shape) for a in fulls],
        out_specs=[block] * outs + ([whole((sums, width))] if sums else []),
        out_shape=out_shape,
        scratch_shapes=[pltpu.VMEM((8 * sums, width), F32)] if sums else [],
        compiler_params=params(8, 1),
        cost_estimate=cost(2),
        name=name,
    )(*row_ins, *fulls)


def norm_first(x, vec):
    def body(x_ref, vec_ref, out_ref):
        out_ref[...] = norm_of(x_ref[...].astype(F32), vec_ref[...], LN1_G, LN1_B)

    return rowwise(body, [x], [vec], [BF], 0, "norm_first")[0]


def after_attention(x, terms, vec):
    count = len(terms)

    def body(*refs):
        x_ref, term_refs, vec_ref = refs[0], refs[1 : 1 + count], refs[1 + count]
        att_ref, res_ref, norm_ref = refs[2 + count :]
        v = vec_ref[...]
        attended = total(term_refs) + v[OUT_B : OUT_B + 1, :]
        residual = x_ref[...].astype(F32) + v[SC_ATTN : SC_ATTN + 1, :] * attended
        att_ref[...] = attended.astype(BF)
        res_ref[...] = residual
        norm_ref[...] = norm_of(residual, v, LN2_G, LN2_B)

    return rowwise(body, [x, *terms], [vec], [BF, F32, BF], 0, "after_attention")


def after_mlp(residual, terms, vec, vec_next):
    count = len(terms)

    def body(*refs):
        res_ref, term_refs = refs[0], refs[1 : 1 + count]
        vec_ref, next_ref, mlp_ref, y_ref, norm_ref = refs[1 + count :]
        v = vec_ref[...]
        mlp = total(term_refs) + v[FC2_B : FC2_B + 1, :]
        y = (res_ref[...] + v[SC_MLP : SC_MLP + 1, :] * mlp).astype(BF)
        mlp_ref[...] = mlp.astype(BF)
        y_ref[...] = y
        norm_ref[...] = norm_of(y.astype(F32), next_ref[...], LN1_G, LN1_B)

    return rowwise(body, [residual, *terms], [vec, vec_next], [BF, BF, BF], 0, "after_mlp")


def last_output(residual, terms, grad, vec):
    count = len(terms)

    def body(*refs):
        res_ref, term_refs = refs[0], refs[1 : 1 + count]
        grad_ref, vec_ref, y_ref, sum_ref = refs[1 + count :]
        v = vec_ref[...]
        mlp = total(term_refs) + v[FC2_B : FC2_B + 1, :]
        y_ref[...] = (res_ref[...] + v[SC_MLP : SC_MLP + 1, :] * mlp).astype(BF)
        add_rows(sum_ref, [grad_ref[...].astype(F32) * mlp])

    return rowwise(body, [residual, *terms, grad], [vec], [BF], 1, "last_output")


def start_back(grad, vec):
    def body(grad_ref, vec_ref, out_ref, sum_ref):
        low = (vec_ref[...][SC_MLP : SC_MLP + 1, :] * grad_ref[...].astype(F32)).astype(BF)
        out_ref[...] = low
        add_rows(sum_ref, [low.astype(F32)])

    return rowwise(body, [grad], [vec], [BF], 1, "start_back")


def back_second(grad, residual, attended, terms, vec):
    count = len(terms)

    def body(*refs):
        grad_ref, res_ref, att_ref = refs[:3]
        term_refs = refs[3 : 3 + count]
        vec_ref, dres_ref, low_ref, sum_ref = refs[3 + count :]
        v = vec_ref[...]
        dn = total(term_refs)
        back, dgain = norm_back(res_ref[...], dn, v[LN2_G : LN2_G + 1, :])
        dres = grad_ref[...].astype(F32) + back
        low = (v[SC_ATTN : SC_ATTN + 1, :] * dres).astype(BF)
        dres_ref[...] = dres
        low_ref[...] = low
        add_rows(sum_ref, [dgain, dn, dres * att_ref[...].astype(F32), low.astype(F32)])

    return rowwise(
        body, [grad, residual, attended, *terms], [vec], [F32, BF], 4, "back_second"
    )


def back_first(dres, x, terms, vec, mlp_below=None, vec_below=None):
    count = len(terms)
    below = mlp_below is not None

    def body(*refs):
        dres_ref, x_ref = refs[:2]
        term_refs = refs[2 : 2 + count]
        rest = refs[2 + count :]
        if below:
            mlp_ref, vec_ref, under_ref, dx_ref, low_ref, sum_ref = rest
        else:
            vec_ref, dx_ref, sum_ref = rest
        v = vec_ref[...]
        dn = total(term_refs)
        back, dgain = norm_back(x_ref[...].astype(F32), dn, v[LN1_G : LN1_G + 1, :])
        dx = (dres_ref[...] + back).astype(BF)
        dx_ref[...] = dx
        rows = [dgain, dn]
        if below:
            wide = dx.astype(F32)
            low = (under_ref[...][SC_MLP : SC_MLP + 1, :] * wide).astype(BF)
            low_ref[...] = low
            rows += [wide * mlp_ref[...].astype(F32), low.astype(F32)]
        add_rows(sum_ref, rows)

    row_ins = [dres, x, *terms] + ([mlp_below] if below else [])
    fulls = [vec] + ([vec_below] if below else [])
    return rowwise(body, row_ins, fulls, [BF, BF] if below else [BF], 4 if below else 2, "back_first")


def project_qkv(pair, weight, bias):
    rows, width = pair[0].shape
    cols = bias.shape[1]

    def body(a_ref, b_ref, w_ref, bias_ref, out_ref):
        w = w_ref[...]
        shift = bias_ref[...]
        out_ref[:rows, :] = (dot(a_ref[...], w) + shift).astype(BF)
        out_ref[rows:, :] = (dot(b_ref[...], w) + shift).astype(BF)

    return pl.pallas_call(
        body,
        grid=(1,),
        in_specs=[
            whole((rows, width)), whole((rows, width)), whole((width, cols)), whole((1, cols))
        ],
        out_specs=whole((2 * rows, cols)),
        out_shape=sds((2 * rows, cols), BF),
        compiler_params=params(6, 1),
        cost_estimate=cost(0.5),
        name="project_qkv",
    )(*pair, weight, bias)


def head_rows(v, head, size):
    rows = lax.broadcasted_iota(jnp.int32, v.shape, 0)
    return jnp.where(rows // size == head, v, jnp.zeros_like(v))


def head_cols(v, head, size):
    cols = lax.broadcasted_iota(jnp.int32, v.shape, 1)
    return jnp.where(cols // size == head, v, jnp.zeros_like(v))


def attention(packed, weight, size):
    chips = len(packed)
    span = packed[0].shape[0]
    half = span // 2
    width = packed[0].shape[1] // 3
    seq = chips * span
    heads = width // size
    model = weight.shape[0]
    step = min(256, seq)
    chunk = min(128, seq)
    score = size**-0.5

    def body(*refs):
        in_refs, w_ref = refs[:chips], refs[chips]
        head_refs = refs[chips + 1 : 2 * chips + 1]
        lse_ref = refs[2 * chips + 1]
        same_refs, other_ref = refs[2 * chips + 2 : 3 * chips + 2], refs[3 * chips + 2]
        k_ref, qt_ref, vt_ref, ot_ref, s_ref, p_ref = refs[3 * chips + 3 :]
        for c in range(chips):
            at = slice(c * span, (c + 1) * span)
            k_ref[at, :] = in_refs[c][:, width : 2 * width]
            qt_ref[:, at] = (turn(in_refs[c][:, :width]) * score).astype(BF)
            vt_ref[:, at] = turn(in_refs[c][:, 2 * width :]).astype(BF)

        def one(i, carry):
            at = pl.ds(pl.multiple_of(i * step, step), step)
            q = qt_ref[:, at]
            s_ref[0] = dot(k_ref[...], head_rows(q, 0, size))
            for h in range(heads):
                if h + 1 < heads:
                    s_ref[(h + 1) % 2] = dot(k_ref[...], head_rows(q, h + 1, size))
                now = h % 2
                top = fold(s_ref[now, :chunk, :], jnp.max)
                for r in range(chunk, seq, chunk):
                    top = jnp.maximum(top, fold(s_ref[now, r : r + chunk, :], jnp.max))
                top = jnp.max(top, axis=0, keepdims=True)
                norm = jnp.zeros((8, step), F32)
                for r in range(0, seq, chunk):
                    p = jnp.exp(s_ref[now, r : r + chunk, :] - top)
                    norm = norm + fold(p, jnp.sum)
                    p_ref[now, r : r + chunk, :] = p.astype(BF)
                norm = jnp.sum(norm, axis=0, keepdims=True)
                rows = slice(h * size, (h + 1) * size)
                ot_ref[rows, at] = dot(vt_ref[rows, :], p_ref[now]) / norm
                lse_ref[h : h + 1, at] = top + jnp.log(norm)
            return carry

        lax.fori_loop(0, seq // step, one, 0)
        for c in range(chips):
            at = slice(c * span, (c + 1) * span)
            o = ot_ref[:, at].T.astype(BF)
            head_refs[c][...] = o
            same_refs[c][...] = dot_bt(o[:half], w_ref[...]).astype(BF)
            other_ref[c * half : (c + 1) * half, :] = dot_bt(o[half:], w_ref[...]).astype(BF)

    out = pl.pallas_call(
        body,
        grid=(1,),
        in_specs=[whole((span, 3 * width))] * chips
        + [pl.BlockSpec((model, width), lambda i: (0, 3), pipeline_mode=pl.Buffered(1))],
        out_specs=[whole((span, width))] * chips
        + [whole((heads, seq))]
        + [whole((half, model))] * chips
        + [whole((seq // 2, model))],
        out_shape=[pltpu.HBM((span, width), BF)] * chips
        + [sds((heads, seq), F32)]
        + [sds((half, model), BF)] * chips
        + [sds((seq // 2, model), BF)],
        scratch_shapes=[
            pltpu.VMEM((seq, width), BF),
            pltpu.VMEM((width, seq), BF),
            pltpu.VMEM((width, seq), BF),
            pltpu.VMEM((width, seq), F32),
            pltpu.VMEM((2, seq, step), F32),
            pltpu.VMEM((2, seq, step), BF),
        ],
        compiler_params=params(14, 1),
        cost_estimate=cost(9),
        name="attention",
    )(*packed, weight)
    return out[:chips], out[chips], out[chips + 1 : -1], out[-1]


def attention_back(packed, heads_kept, lse, datt, weight, size):
    chips = len(packed)
    span = packed[0].shape[0]
    half = span // 2
    width = packed[0].shape[1] // 3
    seq = chips * span
    heads = width // size
    model = weight.shape[0]
    step = min(256, seq)
    chunk = min(128, seq)
    score = size**-0.5

    def body(*refs):
        at = 0

        def take(count):
            nonlocal at
            at += count
            return refs[at - count : at]

        in_refs, kept_refs = take(chips), take(chips)
        (lse_ref,) = take(1)
        datt_refs = take(2 * chips)
        (w_ref,) = take(1)
        dqkv_refs = take(chips)
        same_refs = take(chips)
        other_ref, sum_ref = take(2)
        k_ref, v_ref, kt_ref, qt_ref, q_ref, do_ref, dot_ref = take(7)
        inner_ref, s_ref, g_ref, p_ref, ds_ref, dk_ref, dv_ref, dqt_ref = take(8)
        for c in range(chips):
            rows = slice(c * span, (c + 1) * span)
            q = in_refs[c][:, :width].astype(F32) * score
            k = in_refs[c][:, width : 2 * width]
            q_ref[rows, :] = q.astype(BF)
            qt_ref[:, rows] = q.T.astype(BF)
            k_ref[rows, :] = k
            kt_ref[:, rows] = turn(k).astype(BF)
            v_ref[rows, :] = in_refs[c][:, 2 * width :]
            for b in range(2):
                d = dot(datt_refs[2 * c + b][...], w_ref[:, 3 * width :]).astype(BF)
                here = slice(c * span + b * half, c * span + (b + 1) * half)
                do_ref[here, :] = d
                dt = turn(d)
                dot_ref[:, here] = dt.astype(BF)
                prod = dt * turn(kept_refs[c][b * half : (b + 1) * half, :])
                for h in range(heads):
                    inner_ref[h : h + 1, here] = jnp.sum(
                        prod[h * size : (h + 1) * size, :], axis=0, keepdims=True
                    )

        def one(i, carry):
            at = pl.ds(pl.multiple_of(i * step, step), step)
            qt = qt_ref[:, at]
            dot_t = dot_ref[:, at]
            q = q_ref[at, :]
            do = do_ref[at, :]

            def scores(h):
                s_ref[h % 2] = dot(k_ref[...], head_rows(qt, h, size))
                g_ref[h % 2] = dot(v_ref[...], head_rows(dot_t, h, size))

            scores(0)
            for h in range(heads):
                if h + 1 < heads:
                    scores(h + 1)
                now = h % 2
                cols = slice(h * step, (h + 1) * step)
                lse = lse_ref[h : h + 1, at]
                inner = inner_ref[h : h + 1, at]
                for r in range(0, seq, chunk):
                    p = jnp.exp(s_ref[now, r : r + chunk, :] - lse)
                    ds = p * (g_ref[now, r : r + chunk, :] - inner)
                    p_ref[r : r + chunk, cols] = p.astype(BF)
                    ds_ref[r : r + chunk, cols] = ds.astype(BF)
                rows = slice(h * size, (h + 1) * size)
                dqt_ref[rows, at] = dot(kt_ref[rows, :], ds_ref[:, cols]) * score
            dv = dot(p_ref[...], jnp.concatenate([head_cols(do, h, size) for h in range(heads)], 0))
            dk = dot(ds_ref[...], jnp.concatenate([head_cols(q, h, size) for h in range(heads)], 0))

            @pl.when(i == 0)
            def _():
                dv_ref[...] = dv
                dk_ref[...] = dk

            @pl.when(i > 0)
            def _():
                dv_ref[...] += dv
                dk_ref[...] += dk

            return carry

        lax.fori_loop(0, seq // step, one, 0)
        for c in range(chips):
            rows = slice(c * span, (c + 1) * span)
            out = dqkv_refs[c]
            out[:, :width] = dqt_ref[:, rows].T.astype(BF)
            out[:, width : 2 * width] = dk_ref[rows, :].astype(BF)
            out[:, 2 * width :] = dv_ref[rows, :].astype(BF)
            sums = jnp.sum(out[...].astype(F32), axis=0, keepdims=True)
            if c == 0:
                sum_ref[...] = sums
            else:
                sum_ref[...] += sums
            w = w_ref[:, : 3 * width]
            same_refs[c][...] = dot_bt(out[:half, :], w).astype(BF)
            other_ref[c * half : (c + 1) * half, :] = dot_bt(out[half:, :], w).astype(BF)

    flat = [g for pair in datt for g in pair]
    out_shape = (
        [pltpu.HBM((span, 3 * width), BF)] * chips
        + [sds((half, model), BF)] * chips
        + [sds((seq // 2, model), BF), sds((1, 3 * width), F32)]
    )
    operands = (*map(late, (*packed, *heads_kept)), lse, *flat, late(weight))
    out = pl.pallas_call(
        body,
        grid=(1,),
        in_specs=[whole(a.shape) for a in operands],
        out_specs=[whole(a.shape) for a in out_shape],
        out_shape=out_shape,
        scratch_shapes=[
            pltpu.VMEM((seq, width), BF),
            pltpu.VMEM((seq, width), BF),
            pltpu.VMEM((width, seq), BF),
            pltpu.VMEM((width, seq), BF),
            pltpu.VMEM((seq, width), BF),
            pltpu.VMEM((seq, width), BF),
            pltpu.VMEM((width, seq), BF),
            pltpu.VMEM((heads, seq), F32),
            pltpu.VMEM((2, seq, step), F32),
            pltpu.VMEM((2, seq, step), F32),
            pltpu.VMEM((seq, heads * step), BF),
            pltpu.VMEM((seq, heads * step), BF),
            pltpu.VMEM((seq, width), F32),
            pltpu.VMEM((seq, width), F32),
            pltpu.VMEM((width, seq), F32),
        ],
        compiler_params=params(26, 1),
        cost_estimate=cost(15),
        name="attention_back",
    )(*operands)
    return out[:chips], out[chips : 2 * chips], out[2 * chips], out[2 * chips + 1]


def gelu_both(x):
    away = jnp.abs(x)
    t = 1.0 / (1.0 + (0.3275911 * 0.5**0.5) * away)
    bell = jnp.exp(-0.5 * (x * x))
    poly = t * (
        0.127414796
        + t * (-0.142248368 + t * (0.7107068705 + t * (-0.7265760135 + t * 0.5307027145)))
    )
    tail = poly * bell
    phi = jnp.where(x >= 0, 1.0 - tail, tail)
    return x * phi, phi + x * (bell * 0.3989422804014327)


def mlp_call(body, pairs, extra, weight, bias, outs, parts, scratch, name):
    rows, model = pairs[0].shape
    units = weight.shape[1] // 2
    step = min(256, units)
    blocks = units // step
    cols = lambda j: (0, j)
    in_specs = [whole((rows, model)) for _ in pairs]
    in_specs += [pl.BlockSpec((2 * rows, step), cols) for _ in extra]
    in_specs += [
        pl.BlockSpec((model, step), cols),
        pl.BlockSpec((model, step), lambda j: (0, blocks + j)),
        pl.BlockSpec((1, step), cols),
    ]
    out_specs = [pl.BlockSpec((2 * rows, step), cols) for _ in outs]
    out_specs += [pl.BlockSpec((1, step), cols)]
    out_specs += [whole((rows, model))] * (2 * parts)
    out_shape = [pltpu.HBM((2 * rows, units), d) for d in outs] + [sds((1, units), F32)]
    out_shape += [sds((rows, model), BF)] * (2 * parts)
    count = len(pairs) // 2
    return pl.pallas_call(
        body,
        grid=(blocks,),
        in_specs=in_specs,
        out_specs=out_specs,
        out_shape=out_shape,
        scratch_shapes=[pltpu.VMEM((2 * rows, model), F32)] * parts
        + [pltpu.VMEM((2 * rows, step), F32)] * scratch,
        compiler_params=params(8 + 5 * parts, 1),
        cost_estimate=cost(0.5),
        name=name,
    )(*pairs, *map(late, extra), weight, weight, bias)


def clear(*refs):
    @pl.when(pl.program_id(0) == 0)
    def _():
        for ref in refs:
            ref[...] = jnp.zeros_like(ref)


def finish(acc, low, high):
    rows = low.shape[0]

    @pl.when(pl.program_id(0) == pl.num_programs(0) - 1)
    def _():
        low[...] = acc[:rows, :].astype(BF)
        high[...] = acc[rows:, :].astype(BF)


CHUNK = 32


def mlp_forward(pair, weight, bias):
    rows = pair[0].shape[0]

    def body(a, b, w1_ref, w2_ref, bias_ref, act_ref, slope_ref, sum_ref, lo, hi, acc, pre):
        clear(acc, sum_ref)
        shift = bias_ref[...]
        for i, x in enumerate((a, b)):
            pre[i * rows : (i + 1) * rows, :] = dot(x[...], w1_ref[...])
        for i in range(2):
            at = slice(i * rows, (i + 1) * rows)
            for r in range(i * rows, (i + 1) * rows, CHUNK):
                act, slope = gelu_both(pre[r : r + CHUNK, :] + shift)
                act_ref[r : r + CHUNK, :] = act.astype(BF)
                slope_ref[r : r + CHUNK, :] = slope.astype(BF)
            acc[at, :] += dot_bt(act_ref[at, :], w2_ref[...])
        finish(acc, lo, hi)

    act, slope, _, lo, hi = mlp_call(body, pair, [], weight, bias, [BF, BF], 1, 1, "mlp_forward")
    return act, slope, lo, hi


def mlp_backward(pair, slope, weight, bias):
    rows = pair[0].shape[0]

    def body(a, b, slope_ref, w1_ref, w2_ref, bias_ref, dpre_ref, sum_ref, lo, hi, acc, pre):
        clear(acc)
        for i, g in enumerate((a, b)):
            pre[i * rows : (i + 1) * rows, :] = dot(g[...], w2_ref[...])
        sums = jnp.zeros((8, bias_ref.shape[1]), F32)
        for i in range(2):
            at = slice(i * rows, (i + 1) * rows)
            for r in range(i * rows, (i + 1) * rows, CHUNK):
                d = pre[r : r + CHUNK, :] * slope_ref[r : r + CHUNK, :].astype(F32)
                d = d.astype(BF)
                dpre_ref[r : r + CHUNK, :] = d
                sums = sums + fold(d.astype(F32), jnp.sum)
            acc[at, :] += dot_bt(dpre_ref[at, :], w1_ref[...])
        sum_ref[...] = jnp.sum(sums, axis=0, keepdims=True)
        finish(acc, lo, hi)

    dpre, sums, lo, hi = mlp_call(
        body, pair, [slope], weight, bias, [BF], 1, 1, "mlp_backward"
    )
    return dpre, sums, lo, hi


def mlp_both(pair, grads, weight, bias):
    rows = pair[0].shape[0]

    def body(
        a, b, c, d, w1_ref, w2_ref, bias_ref, act_ref, dpre_ref, sum_ref,
        lo, hi, blo, bhi, acc, back, pre, grad,
    ):
        clear(acc, back)
        shift = bias_ref[...]
        for i, (x, g) in enumerate(((a, c), (b, d))):
            at = slice(i * rows, (i + 1) * rows)
            pre[at, :] = dot(x[...], w1_ref[...])
            grad[at, :] = dot(g[...], w2_ref[...])
        sums = jnp.zeros((8, bias_ref.shape[1]), F32)
        for i in range(2):
            at = slice(i * rows, (i + 1) * rows)
            for r in range(i * rows, (i + 1) * rows, CHUNK):
                act, slope = gelu_both(pre[r : r + CHUNK, :] + shift)
                act_ref[r : r + CHUNK, :] = act.astype(BF)
                dpre = (grad[r : r + CHUNK, :] * slope).astype(BF)
                dpre_ref[r : r + CHUNK, :] = dpre
                sums = sums + fold(dpre.astype(F32), jnp.sum)
            back[at, :] += dot_bt(dpre_ref[at, :], w1_ref[...])
            acc[at, :] += dot_bt(act_ref[at, :], w2_ref[...])
        sum_ref[...] = jnp.sum(sums, axis=0, keepdims=True)
        finish(acc, lo, hi)
        finish(back, blo, bhi)

    act, dpre, sums, lo, hi, blo, bhi = mlp_call(
        body, [*pair, *grads], [], weight, bias, [BF, BF], 2, 2, "mlp_both"
    )
    return act, dpre, sums, lo, hi, blo, bhi


def weight_grads(products, dp, side, name, halves=True, heads=0):
    model = products[0][0][0].shape[1]
    step = model // dp
    half = step // 2
    cut = 2 if halves else 1
    sizes = [(len(left), len(right), right[0].shape[1]) for left, right in products]
    cols = sum(n for _, _, n in sizes)

    def body(side_ref, *refs):
        acc_ref = refs[-1]
        mine, other = refs[-3:-1] if halves else (refs[-2], None)
        at = base = 0
        for many, few, n in sizes:
            lefts, rights = refs[at : at + many], refs[at + many : at + many + few]
            at += many + few
            ratio = many // few
            acc = None
            for i in range(many):
                size = lefts[i].shape[0]
                here = slice((i % ratio) * size, (i % ratio + 1) * size)
                term = dot_at(lefts[i][...], rights[i // ratio][here, :])
                acc = term if acc is None else acc + term
            if halves:
                acc_ref[:, base : base + n] = acc
            elif heads and not base:
                size = n // (3 * heads)
                for k in range(3 * heads):
                    head, kind = k // 3, k % 3
                    at_k = (kind * heads + head) * size
                    mine[:, k * size : (k + 1) * size] = acc[:, at_k : at_k + size].astype(BF)
            else:
                mine[:, base : base + n] = acc.astype(BF)
            base += n
        if not halves:
            return
        low = pl.multiple_of(side_ref[0] * half, half)
        high = pl.multiple_of((1 - side_ref[0]) * half, half)
        mine[...] = acc_ref[pl.ds(low, half), :].astype(BF)
        other[...] = acc_ref[pl.ds(high, half), :].astype(BF)

    specs, operands = [pl.BlockSpec(memory_space=pltpu.SMEM)], [side.reshape(1)]
    for left, right in products:
        specs += [pl.BlockSpec((a.shape[0], step), lambda i: (0, i)) for a in left]
        specs += [whole(b.shape) for b in right]
        operands += [*left, *right]
    return pl.pallas_call(
        body,
        grid=(dp,),
        in_specs=specs,
        out_specs=[pl.BlockSpec((step // cut, cols), lambda i: (i, 0))] * cut,
        out_shape=[sds((model // cut, cols), BF)] * cut,
        scratch_shapes=[pltpu.VMEM((step, cols), F32)],
        compiler_params=params(14, 1),
        cost_estimate=cost(5),
        name=name,
    )(*operands)


def pieces(chunks):
    return [p for pair in chunks for p in pair]


def shards(
    tokens, cotangent, ln1_gain, ln1_bias, w_qkv, qv_bias, w_out, out_bias, scale_attn,
    ln2_gain, ln2_bias, w_fc1, fc1_bias, w_fc2, fc2_bias, scale_mlp,
):
    side = lax.axis_index("section")
    first = side == 0
    dp = lax.axis_size("dp")
    here = lax.axis_index("dp")
    chips = lax.axis_size("tensor") // 2
    rows, model = tokens.shape[2:]
    heads = qv_bias.shape[1]
    size = qv_bias.shape[2] * dp // 2
    width = heads * size
    units = w_fc1.shape[2]
    part = model // dp

    x0 = lax.dynamic_index_in_dim(tokens, side, 0, keepdims=False).reshape(rows, model)
    grad_top = lax.dynamic_index_in_dim(cotangent, side, 0, keepdims=False).reshape(rows, model)

    vectors = (ln1_gain, ln1_bias, out_bias, scale_attn, ln2_gain, ln2_bias, fc2_bias, scale_mlp)
    packed = jnp.concatenate(
        [v.reshape(-1) for v in vectors] + [fc1_bias.reshape(-1), qv_bias.reshape(-1)]
    )
    own_qkv = w_qkv.reshape(part, heads, 3, size).swapaxes(1, 2).reshape(part, 3 * width)
    own_att = jnp.concatenate([own_qkv, w_out[0].T], axis=1)
    give_att = half_of(own_att, 1 - side)
    came_att = swap_section(give_att)
    came_small = swap_section(tie(packed, give_att))
    both_small = jnp.concatenate(
        [jnp.where(first, packed, came_small), jnp.where(first, came_small, packed)]
    )
    cols = 4 * width
    tail = -(-both_small.size // (16 * cols)) * 16
    both_small = jnp.pad(both_small, (0, tail * cols - both_small.size)).reshape(tail, cols)
    mine_att = half_of(own_att, side)
    ring_att0 = jnp.concatenate([jnp.where(first, mine_att, came_att), both_small])
    ring_att1 = jnp.where(first, came_att, mine_att)
    hops_att0 = direct(ring_att0)
    own_ff = jnp.concatenate([w_fc1[0], w_fc2[0].T], axis=1)
    rest_att = swap_section(tie(mine_att, ring_att0))
    came_ff = swap_section(tie(half_of(own_ff, 1 - side), ring_att0))
    mine_ff = half_of(own_ff, side)
    ring_ff0 = jnp.where(first, mine_ff, came_ff)
    ring_ff1 = jnp.where(first, came_ff, mine_ff)

    def other_half(own, rest):
        left = half_of(own, 1 - side)
        return jnp.where(first, left, rest), jnp.where(first, rest, left)


    backs = [swap_section(v) for v in hops_att0]
    back = [ring_att0, *hops_att0]
    back[2] = tie(back[2], backs[-1])
    flat = in_order([v[-tail:] for v in back])
    flat = flat.reshape(dp, -1)[:, : 2 * packed.size].reshape(dp, 2, -1).astype(F32)
    cut = 8 * part
    vecs = flat[:, :, :cut].reshape(dp, 2, 8, part).transpose(1, 2, 0, 3).reshape(2, 8, model)
    vecs = (vecs[0], vecs[1])
    bias_fc1 = flat[:, :, cut : cut + units // dp].swapaxes(0, 1).reshape(2, 1, units)
    qv = flat[:, :, cut + units // dp :].reshape(dp, 2, heads, -1).transpose(1, 2, 0, 3)
    qv = qv.reshape(2, heads, 2, size)
    bias_qkv = jnp.stack([qv[:, :, 0], jnp.zeros_like(qv[:, :, 0]), qv[:, :, 1]], axis=1)
    bias_qkv = bias_qkv.reshape(2, 1, 3 * width)

    norm1 = norm_first(tie(x0, came_ff), vecs[0])
    rest_ff = swap_section(tie(mine_ff, norm1))
    rest_att0, rest_att1 = other_half(own_att, rest_att)
    rest_ff0, rest_ff1 = other_half(own_ff, rest_ff)
    att1 = Ring(ring_att1)
    att0 = assemble([(tie(ring_att0, norm1), rest_att0), *zip(hops_att0, backs)], model)
    ff0, ff1 = Ring(ring_ff0), Ring(ring_ff1)
    hop_ff0 = ff0.hop(norm1)

    def projection(weight, s):
        return lambda pair: project_qkv(pair, weight, bias_qkv[s])

    chunks0, qkv0 = gather_tokens(norm1, projection(att0, 0), [rest_ff, *hop_ff0])
    beside = [*ff0.hop(), *ff0.back()]
    kept0, lse0, sames, others = attention(qkv0, att0, size)
    terms, _ = scatter_tokens(
        sames,
        tie(others, *beside),
        beside=lambda gate: [*ff0.hop(gate), *ff0.back(gate)],
    )
    attended0, residual0, norm2 = after_attention(x0, terms, vecs[0])
    ff0.back()
    beside = [*att1.hop(norm2), *att1.hop()]
    w_ff0 = assemble([(ring_ff0, rest_ff0), *zip(ff0.hops, ff0.backs)], model)
    second0, mlp0 = gather_tokens(
        norm2, lambda pair: mlp_forward(pair, w_ff0, bias_fc1[0]), beside
    )
    act0, slope0, sames, others = zip(*mlp0)
    beside = [*att1.hop(second0[-1][0]), *att1.back(second0[-1][0])]
    terms, _ = scatter_tokens(
        sames,
        [others[0], *[tie(v, *beside) for v in others[1:]]],
        beside=lambda gate: [*ff1.hop(gate), *att1.back(gate), *att1.back(gate)],
    )
    mlp_out0, y0, norm1 = after_mlp(residual0, terms, vecs[0], vecs[1])

    w_att1 = assemble([(ring_att1, rest_att1), *zip(att1.hops, att1.backs)], model)
    low1, sums_fc2_1 = start_back(grad_top, vecs[1])
    beside = [*ff1.hop(norm1), *ff1.back(norm1)]
    chunks1, qkv1 = gather_tokens(norm1, projection(w_att1, 1), beside)
    gate = chunks1[-1][0]
    came = [from_chip(tie(low1, gate), step) for step in range(1, chips)]
    beside = [*came, *ff1.hop(gate), *ff1.back(gate)]
    kept1, lse1, sames, others = attention(qkv1, w_att1, size)
    others = tie(others, *beside)
    grads1 = [(low1, core_swap(low1))] + [(v, core_swap(tie(v, lse1))) for v in came]
    terms, _ = scatter_tokens(
        sames, others, beside=lambda gate: [*ff1.back(gate), *pieces(grads1)]
    )
    attended1, residual1, norm2 = after_attention(y0, terms, vecs[1])
    w_ff1 = assemble([(ring_ff1, rest_ff1), *zip(ff1.hops, ff1.backs)], model)
    spare = list(grads1)
    second1, mlp1 = gather_tokens(
        norm2, lambda pair: mlp_both(pair, spare.pop(0), w_ff1, bias_fc1[1])
    )
    act1, dpre1, sums_fc1_1, sames_y1, others_y1, sames, others = zip(*mlp1)

    def grad_ff(second, dpre, grads, act):
        return lambda after: weight_grads(
            [
                (pieces(second), [late(tie(dpre[0], after)), *map(late, dpre[1:])]),
                (pieces(grads), [late(a) for a in act]),
            ],
            dp,
            side,
            "grad_ff",
        )

    def grad_att(chunks, dqkv, datt, kept):
        return lambda after: weight_grads(
            [
                (pieces(chunks), [late(tie(dqkv[0], after)), *map(late, dqkv[1:])]),
                (pieces(datt), [late(a) for a in kept]),
            ],
            dp,
            side,
            "grad_att",
            False,
            heads,
        )[0]

    old = [tuple(map(late, pair)) for pair in grads1]
    terms, g = scatter_tokens(sames, others, grad_ff(second1, dpre1, old, act1))
    sum_ff1 = RingSum((0, 1), *g)
    dres1, low, sums1 = back_second(grad_top, residual1, attended1, terms, vecs[1])
    came_y0 = lax.ppermute(tie(y0, low), "section", [(1, 0)])
    datt, _ = gather_tokens(low, lambda pair: pair[0], sum_ff1.step())
    sums_y1, local_y1 = core_sums(sames_y1, [tie(v, low) for v in others_y1])
    terms_y1 = send_sums([tie(v, datt[-1][0]) for v in sums_y1])
    beside = [came_y0, *terms_y1, *sum_ff1.step(low)]
    dqkv, sames, others, qkv_sums1 = attention_back(qkv1, kept1, lse1, datt, w_att1, size)
    old = [tuple(map(late, pair)) for pair in chunks1]
    terms, g = scatter_tokens(
        sames, tie(others, *beside), grad_att(old, dqkv, datt, kept1), sum_ff1.step
    )
    sum_att1 = RingSum((0, 1), g)
    sum_att1.step()
    dx1, low0, edge1 = back_first(dres1, late(y0), terms, vecs[1], late(mlp_out0), vecs[0])

    y1, sums_sc_1 = last_output(
        residual1, [tie(sames_y1[0], low0), *terms_y1, local_y1], grad_top, vecs[1]
    )

    slopes = list(slope0)
    grads0, mlp_back0 = gather_tokens(
        low0,
        lambda pair: mlp_backward(pair, slopes.pop(0), w_ff0, bias_fc1[0]),
        [y1, *sum_ff1.step(low0)],
    )
    dpre0, sums_fc1_0, sames, others = zip(*mlp_back0)
    old = [tuple(map(late, pair)) for pair in second0]
    terms, g = scatter_tokens(
        sames,
        others,
        grad_ff(old, dpre0, grads0, act0),
        lambda gate: [*sum_ff1.step(gate), *sum_att1.step(gate)],
    )
    sum_ff0 = RingSum((1, 0), *g)
    dres0, low, sums0 = back_second(
        dx1, late(residual0), late(attended0), terms, vecs[0]
    )
    beside = [*sum_att1.step(low), *sum_ff0.step(low)]
    datt, _ = gather_tokens(low, lambda pair: pair[0], beside)
    beside = [*sum_att1.step(low), *sum_ff0.step(low)]
    dqkv, sames, others, qkv_sums0 = attention_back(qkv0, kept0, lse0, datt, att0, size)
    old = [tuple(map(late, pair)) for pair in chunks0]
    terms, g = scatter_tokens(
        sames, tie(others, *beside), grad_att(old, dqkv, datt, kept0), sum_ff0.step
    )
    sum_att0 = RingSum((1, 0), g)
    sum_att0.step()
    going = sum_att0.step()
    dx0, edge0 = back_first(dres0, x0, terms, vecs[0])
    came_dx0 = lax.ppermute(dx0, "section", [(1, 0)])
    step_ff0 = sum_ff0.step(dx0)
    second_hop = sum_att0.step(dx0)
    step_att1 = sum_att1.step(sames[0])
    third_hop = sum_att0.step()
    sent = sum_att0.sent
    last_ff0 = sum_ff0.step(sent)
    sum_att0.step()
    came_y1 = lax.ppermute(tie(y1, dx0), "section", [(0, 1)])
    came_dx1 = lax.ppermute(tie(dx1, sent), "section", [(0, 1)])

    def both(low, high, came_low, came_high):
        mine = jnp.where(first, low, high)
        came = jnp.where(first, came_low, came_high)
        return jnp.stack([jnp.where(first, mine, came), jnp.where(first, came, mine)])[None, :, None]

    block_out = both(y0, y1, came_y0, came_y1)
    input_grads = both(dx0, dx1, came_dx0, came_dx1)
    sum_att0.came = tie(sum_att0.came, block_out, input_grads)

    def by_unit(qkv_sums, unit_sums):
        q = qkv_sums[:, :width].reshape(heads, 1, size)
        v = qkv_sums[:, 2 * width :].reshape(heads, 1, size)
        bias = jnp.concatenate([q, v], 1).reshape(heads, dp, -1).swapaxes(0, 1).reshape(dp, -1)
        return jnp.concatenate([bias, unit_sums.reshape(dp, -1)], axis=1)

    unit0 = by_unit(tie(qkv_sums0, dx0), sum(sums_fc1_0))
    unit1 = by_unit(tie(qkv_sums1, dx0), sum(sums_fc1_1))
    vec = jnp.concatenate(
        [edge0[:2], sums0[:4], edge1[2:4], edge1[:2], sums1[:4], sums_sc_1[:1], sums_fc2_1[:1]]
    )
    vec = tie(vec, *going, *step_att1)
    vec = vec + core_swap(vec)
    vec = tie(sum([from_chip(vec, step) for step in range(1, chips)], vec), *second_hop, came_y1)
    vec = tie(vec, sent)
    vec = vec.reshape(2, 8, dp, part).swapaxes(1, 2).reshape(2, dp, 8 * part)
    vec0 = jnp.concatenate([vec[0], unit0], axis=1)
    vec1 = jnp.concatenate([vec[1], unit1], axis=1)
    own = jnp.where(first, vec0, vec1) + swap_section(jnp.where(first, vec1, vec0))
    own = tie(own, *last_ff0, came_dx1)
    vec = lax.dynamic_slice_in_dim(own, here, 1, 0)
    for step in range(1, dp):
        pairs = [(i, (i + step) % dp) for i in range(dp)]
        other = lax.dynamic_slice_in_dim(own, lax.rem(here + step, dp), 1, 0)
        vec = vec + lax.ppermute(other, "dp", pairs)
    cut = 8 * part + heads * (2 * size // dp)
    bias_grad = vec[:, 8 * part : cut].reshape(1, heads, -1)
    fc1_grad = vec[:, cut:].reshape(1, 1, -1)
    g_ln1, b_ln1, g_ln2, b_ln2, g_sc_attn, g_out_bias, g_sc_mlp, g_fc2_bias = (
        vec[:, i * part : (i + 1) * part] for i in range(8)
    )

    def owned(low, high):
        top = jnp.where(first, low.own, high.came.astype(F32))
        bottom = jnp.where(first, low.came.astype(F32), high.own)
        return jnp.concatenate([top, bottom], 0)

    g_ff = owned(sum_ff0, sum_ff1)
    g_att = jnp.where(
        first,
        sum_att0.own + sum_att0.came.astype(F32),
        sum_att1.own + sum_att1.came.astype(F32),
    )
    g_qkv = g_att[None, :, : 3 * width]
    g_out = g_att[:, 3 * width :].T[None]
    g_fc1 = g_ff[:, :units][None]
    g_fc2 = g_ff[:, units:].T[None]
    return (
        block_out, input_grads, g_ln1, b_ln1, g_qkv, bias_grad, g_out, g_out_bias, g_sc_attn,
        g_ln2, b_ln2, g_fc1, fc1_grad, g_fc2, g_fc2_bias, g_sc_mlp,
    )


def solution(mesh):
    vec = P("section", "dp")
    by_row = P("section", "dp", "tensor")
    by_unit = P("section", "tensor", "dp")
    data = P(None, "dp", "tensor", None)
    split = P("section", None, "dp", "tensor", None)
    given = (
        vec, vec, by_row, by_unit, by_unit, vec, vec, vec, vec, by_row, by_unit, by_unit, vec, vec,
    )
    return jax.shard_map(
        shards,
        mesh=mesh,
        in_specs=(data, data) + given,
        out_specs=(split, split) + given,
        check_vma=False,
    )
```

```python
from functools import partial

import jax
import jax.numpy as jnp
from jax import lax
from jax.experimental import pallas as pl
from jax.experimental.pallas import tpu as pltpu
from jax.sharding import PartitionSpec as P

EPSILON = 1e-06
BF = jnp.bfloat16
F32 = jnp.float32
MIB = 1 << 20

LN1_G, LN1_B, OUT_B, SC_ATTN, LN2_G, LN2_B, FC2_B, SC_MLP = range(8)


def dot(a, b):
    return lax.dot_general(a, b, (((1,), (0,)), ((), ())), preferred_element_type=F32)


def dot_bt(a, b):
    return lax.dot_general(a, b, (((1,), (1,)), ((), ())), preferred_element_type=F32)


def dot_at(a, b):
    return lax.dot_general(a, b, (((0,), (0,)), ((), ())), preferred_element_type=F32)


def turn(v):
    return v.astype(F32).T


def params(limit, grid=0):
    return pltpu.CompilerParams(
        vmem_limit_bytes=limit * MIB,
        dimension_semantics=("arbitrary",) * grid if grid else None,
    )


def late(v):
    return pltpu.with_memory_space_constraint(v, pltpu.HBM)


def whole(shape):
    return pl.BlockSpec(shape, lambda i: (0, 0), pipeline_mode=pl.Buffered(1))


def cost(micros):
    return pl.CostEstimate(flops=int(micros * 1.15e9), bytes_accessed=0, transcendentals=0)


def sds(shape, dtype):
    return jax.ShapeDtypeStruct(shape, dtype)


def core_swap(v):
    count = lax.axis_size("tensor")
    return lax.ppermute(v, "tensor", [(i, i ^ 1) for i in range(count)])


def from_chip(v, step):
    count = lax.axis_size("tensor")
    chips = count // 2
    pairs = [(((i // 2 + step) % chips) * 2 + i % 2, i) for i in range(count)]
    return lax.ppermute(v, "tensor", pairs)


def tie(v, *after):
    if not after:
        return v
    return lax.optimization_barrier((v, *after))[0]


def tie_all(vs, *after):
    return lax.optimization_barrier((*vs, *after))[: len(vs)]


def gather_tokens(own, work, beside=()):
    chips = lax.axis_size("tensor") // 2
    came = [from_chip(own, step) for step in range(1, chips)]
    chunks = [(own, core_swap(own))]
    results = [work(chunks[0])]
    for same in came:
        same = tie(same, results[-1], *beside)
        chunks.append((same, core_swap(same)))
        results.append(work(chunks[-1]))
    return chunks, results


def core_sums(sames, others):
    chips, rows = len(sames), sames[0].shape[0]
    if isinstance(others, (list, tuple)):
        came = [core_swap(v) for v in others[1:]]
        local = core_swap(tie(others[0], came[-1]))
    else:
        local = core_swap(others)
        came = [local[c * rows : (c + 1) * rows] for c in range(1, chips)]
    sums = [(a.astype(F32) + b.astype(F32)).astype(BF) for a, b in zip(sames[1:], came)]
    return sums, local


def send_sums(sums):
    chips = len(sums) + 1
    return [from_chip(both, chips - step) for step, both in enumerate(sums, 1)]


def scatter_tokens(sames, others, work=None, beside=None):
    sums, local = core_sums(sames, others)
    terms = send_sums(sums)
    made = work(sums[-1]) if work else local
    more = beside(sums[-1]) if beside else ()
    terms = [tie(t, made, local, *more) for t in terms]
    return [sames[0], *terms, local], made


def swap_section(v):
    return lax.ppermute(v, "section", [(0, 1), (1, 0)])


def assemble(shards, rows):
    count = len(shards)
    cut = len(shards[0])
    size, cols = rows // (count * cut), shards[0][0].shape[1]
    place = jnp.stack([lax.axis_index("dp"), lax.axis_index("section")])

    def body(place_ref, *refs):
        out_ref, sems = refs[count * cut :]
        z, x = place_ref[0], place_ref[1]
        started = []
        for k in range(count):
            base = lax.rem(z + (count - k), count) * (cut * size)
            for i, at in enumerate([base] if cut == 1 else [base + x * size, base + (1 - x) * size]):
                copy = pltpu.make_async_copy(
                    refs[k * cut + i].at[pl.ds(0, size), :],
                    out_ref.at[pl.ds(pl.multiple_of(at, size), size), :],
                    sems.at[k * cut + i],
                )
                copy.start()
                started.append(copy)
        for copy in started:
            copy.wait()

    hbm = pl.BlockSpec(memory_space=pl.ANY)
    return pl.pallas_call(
        body,
        in_specs=[pl.BlockSpec(memory_space=pltpu.SMEM)] + [hbm] * (count * cut),
        out_specs=pl.BlockSpec(memory_space=pltpu.VMEM),
        out_shape=sds((rows, cols), shards[0][0].dtype),
        scratch_shapes=[pltpu.SemaphoreType.DMA((count * cut,))],
        compiler_params=params(6),
        cost_estimate=cost(2),
        name="assemble",
    )(place, *[late(v) for shard in shards for v in shard])


def half_of(v, which):
    half = v.shape[0] // 2
    return lax.dynamic_slice_in_dim(v, which * half, half, 0)


def direct(own):
    count = lax.axis_size("dp")
    return [
        lax.ppermute(own, "dp", [(i, (i + step) % count) for i in range(count)])
        for step in range(1, count)
    ]


def third(values, index):
    cuts = [-(-len(values) * i // 3) for i in range(4)]
    return values[cuts[index] : cuts[index + 1]]


class Ring:
    def __init__(self, own):
        self.last, self.hops, self.backs, self.at, self.back_at = own, [], [], 0, 0

    def hop(self, *gate):
        count = lax.axis_size("dp")
        pairs = [(i, (i + 1) % count) for i in range(count)]
        new = []
        for i in range(len(third(range(count - 1), self.at))):
            self.last = lax.ppermute(tie(self.last, *gate) if i == 0 else self.last, "dp", pairs)
            new.append(self.last)
        self.hops += new
        self.at += 1
        return new

    def back(self, *gate):
        count = lax.axis_size("dp")
        which = third(range(count - 1), self.back_at)
        new = [swap_section(tie(self.hops[i], *gate)) for i in which]
        self.backs += new
        self.back_at += 1
        return new


def in_order(back):
    count = len(back)
    ahead = [back[0], *back[:0:-1]]
    twice = jnp.stack(ahead + ahead)
    return lax.dynamic_slice_in_dim(twice, count - lax.axis_index("dp"), count, 0)


def dp_rows(v, back):
    dp = lax.axis_size("dp")
    part = v.shape[0] // dp
    place = lax.rem(lax.axis_index("dp") + (dp - back), dp)
    return lax.dynamic_slice_in_dim(v, place * part, part, 0)


class RingSum:
    def __init__(self, pair, mine, other=None):
        self.mine, self.other, self.pair = mine, other, pair
        self.terms, self.at, self.done = [], 0, 0

    def total(self, gate=()):
        first = tie(self.terms[0], *gate)
        return sum(t.astype(F32) for t in [first, *self.terms[1:]])

    def one(self, gate):
        dp = lax.axis_size("dp")
        self.done += 1
        new = []
        if self.terms:
            pairs = [(i, (i + 1) % dp) for i in range(dp)]
            self.sent = self.total(gate).astype(BF)
            new.append(lax.ppermute(self.sent, "dp", pairs))
        if self.other is not None:
            new.append(swap_section(tie(dp_rows(self.other, self.done), *gate)))
        self.terms = [*new, dp_rows(self.mine, self.done)]
        return new

    def step(self, *gate):
        self.at += 1
        if self.at == 5:
            self.own = self.total(gate)
            self.came = lax.ppermute(self.own.astype(BF), "section", [self.pair])
            return [self.came]
        count = 1 if self.at == 1 else len(third(range(lax.axis_size("dp") - 1), self.at - 2))
        return [v for i in range(count) for v in self.one(gate if i == 0 else ())]


def standardize(v):
    centred = v - jnp.mean(v, axis=-1, keepdims=True)
    var = jnp.mean(centred * centred, axis=-1, keepdims=True)
    scale = lax.rsqrt(var + EPSILON)
    return centred * scale, scale


def norm_of(v, vec, gain, shift):
    return (standardize(v)[0] * vec[gain : gain + 1, :] + vec[shift : shift + 1, :]).astype(BF)


def norm_back(v, grad, gain):
    xh, scale = standardize(v)
    dxh = grad * gain
    inner = jnp.mean(dxh * xh, axis=-1, keepdims=True)
    out = scale * (dxh - jnp.mean(dxh, axis=-1, keepdims=True) - xh * inner)
    return out, grad * xh


def total(refs):
    out = refs[0][...].astype(F32)
    for ref in refs[1:]:
        out = out + ref[...].astype(F32)
    return out


def fold(v, op):
    return op(v.reshape(-1, 8, v.shape[1]), axis=0)


def add_rows(ref, rows):
    for k, row in enumerate(rows):
        ref[8 * k : 8 * k + 8, :] += fold(row, jnp.sum)


def rowwise(body, row_ins, fulls, row_outs, sums, name):
    rows, width = row_ins[0].shape
    step = min(128, rows)
    some, outs = len(row_ins) + len(fulls), len(row_outs)

    def kernel(*refs):
        if not sums:
            body(*refs)
            return
        sum_ref, acc_ref = refs[some + outs :]

        @pl.when(pl.program_id(0) == 0)
        def _():
            acc_ref[...] = jnp.zeros_like(acc_ref)

        body(*refs[: some + outs], acc_ref)

        @pl.when(pl.program_id(0) == pl.num_programs(0) - 1)
        def _():
            for k in range(sums):
                sum_ref[k : k + 1, :] = jnp.sum(
                    acc_ref[8 * k : 8 * k + 8, :], axis=0, keepdims=True
                )

    out_shape = [sds((rows, width), d) for d in row_outs]
    out_shape += [sds((sums, width), F32)] if sums else []
    block = pl.BlockSpec((step, width), lambda i: (i, 0))
    return pl.pallas_call(
        kernel,
        grid=(rows // step,),
        in_specs=[block] * len(row_ins) + [whole(a.shape) for a in fulls],
        out_specs=[block] * outs + ([whole((sums, width))] if sums else []),
        out_shape=out_shape,
        scratch_shapes=[pltpu.VMEM((8 * sums, width), F32)] if sums else [],
        compiler_params=params(8, 1),
        cost_estimate=cost(2),
        name=name,
    )(*row_ins, *fulls)


def norm_first(x, vec):
    def body(x_ref, vec_ref, out_ref):
        out_ref[...] = norm_of(x_ref[...].astype(F32), vec_ref[...], LN1_G, LN1_B)

    return rowwise(body, [x], [vec], [BF], 0, "norm_first")[0]


def after_attention(x, terms, vec):
    count = len(terms)

    def body(*refs):
        x_ref, term_refs, vec_ref = refs[0], refs[1 : 1 + count], refs[1 + count]
        att_ref, res_ref, norm_ref = refs[2 + count :]
        v = vec_ref[...]
        attended = total(term_refs) + v[OUT_B : OUT_B + 1, :]
        residual = x_ref[...].astype(F32) + v[SC_ATTN : SC_ATTN + 1, :] * attended
        att_ref[...] = attended.astype(BF)
        res_ref[...] = residual
        norm_ref[...] = norm_of(residual, v, LN2_G, LN2_B)

    return rowwise(body, [x, *terms], [vec], [BF, F32, BF], 0, "after_attention")


def after_mlp(residual, terms, vec, vec_next):
    count = len(terms)

    def body(*refs):
        res_ref, term_refs = refs[0], refs[1 : 1 + count]
        vec_ref, next_ref, mlp_ref, y_ref, norm_ref = refs[1 + count :]
        v = vec_ref[...]
        mlp = total(term_refs) + v[FC2_B : FC2_B + 1, :]
        y = (res_ref[...] + v[SC_MLP : SC_MLP + 1, :] * mlp).astype(BF)
        mlp_ref[...] = mlp.astype(BF)
        y_ref[...] = y
        norm_ref[...] = norm_of(y.astype(F32), next_ref[...], LN1_G, LN1_B)

    return rowwise(body, [residual, *terms], [vec, vec_next], [BF, BF, BF], 0, "after_mlp")


def last_output(residual, terms, grad, vec):
    count = len(terms)

    def body(*refs):
        res_ref, term_refs = refs[0], refs[1 : 1 + count]
        grad_ref, vec_ref, y_ref, sum_ref = refs[1 + count :]
        v = vec_ref[...]
        mlp = total(term_refs) + v[FC2_B : FC2_B + 1, :]
        y_ref[...] = (res_ref[...] + v[SC_MLP : SC_MLP + 1, :] * mlp).astype(BF)
        add_rows(sum_ref, [grad_ref[...].astype(F32) * mlp])

    return rowwise(body, [residual, *terms, grad], [vec], [BF], 1, "last_output")


def start_back(grad, vec):
    def body(grad_ref, vec_ref, out_ref, sum_ref):
        low = (vec_ref[...][SC_MLP : SC_MLP + 1, :] * grad_ref[...].astype(F32)).astype(BF)
        out_ref[...] = low
        add_rows(sum_ref, [low.astype(F32)])

    return rowwise(body, [grad], [vec], [BF], 1, "start_back")


def back_second(grad, residual, attended, terms, vec):
    count = len(terms)

    def body(*refs):
        grad_ref, res_ref, att_ref = refs[:3]
        term_refs = refs[3 : 3 + count]
        vec_ref, dres_ref, low_ref, sum_ref = refs[3 + count :]
        v = vec_ref[...]
        dn = total(term_refs)
        back, dgain = norm_back(res_ref[...], dn, v[LN2_G : LN2_G + 1, :])
        dres = grad_ref[...].astype(F32) + back
        low = (v[SC_ATTN : SC_ATTN + 1, :] * dres).astype(BF)
        dres_ref[...] = dres
        low_ref[...] = low
        add_rows(sum_ref, [dgain, dn, dres * att_ref[...].astype(F32), low.astype(F32)])

    return rowwise(
        body, [grad, residual, attended, *terms], [vec], [F32, BF], 4, "back_second"
    )


def back_first(dres, x, terms, vec, mlp_below=None, vec_below=None):
    count = len(terms)
    below = mlp_below is not None

    def body(*refs):
        dres_ref, x_ref = refs[:2]
        term_refs = refs[2 : 2 + count]
        rest = refs[2 + count :]
        if below:
            mlp_ref, vec_ref, under_ref, dx_ref, low_ref, sum_ref = rest
        else:
            vec_ref, dx_ref, sum_ref = rest
        v = vec_ref[...]
        dn = total(term_refs)
        back, dgain = norm_back(x_ref[...].astype(F32), dn, v[LN1_G : LN1_G + 1, :])
        dx = (dres_ref[...] + back).astype(BF)
        dx_ref[...] = dx
        rows = [dgain, dn]
        if below:
            wide = dx.astype(F32)
            low = (under_ref[...][SC_MLP : SC_MLP + 1, :] * wide).astype(BF)
            low_ref[...] = low
            rows += [wide * mlp_ref[...].astype(F32), low.astype(F32)]
        add_rows(sum_ref, rows)

    row_ins = [dres, x, *terms] + ([mlp_below] if below else [])
    fulls = [vec] + ([vec_below] if below else [])
    return rowwise(body, row_ins, fulls, [BF, BF] if below else [BF], 4 if below else 2, "back_first")


def project_qkv(pair, weight, bias):
    rows, width = pair[0].shape
    cols = bias.shape[1]

    def body(a_ref, b_ref, w_ref, bias_ref, out_ref):
        w = w_ref[...]
        shift = bias_ref[...]
        out_ref[:rows, :] = (dot(a_ref[...], w) + shift).astype(BF)
        out_ref[rows:, :] = (dot(b_ref[...], w) + shift).astype(BF)

    return pl.pallas_call(
        body,
        grid=(1,),
        in_specs=[
            whole((rows, width)), whole((rows, width)), whole((width, cols)), whole((1, cols))
        ],
        out_specs=whole((2 * rows, cols)),
        out_shape=sds((2 * rows, cols), BF),
        compiler_params=params(6, 1),
        cost_estimate=cost(0.5),
        name="project_qkv",
    )(*pair, weight, bias)


def head_rows(v, head, size):
    rows = lax.broadcasted_iota(jnp.int32, v.shape, 0)
    return jnp.where(rows // size == head, v, jnp.zeros_like(v))


def head_cols(v, head, size):
    cols = lax.broadcasted_iota(jnp.int32, v.shape, 1)
    return jnp.where(cols // size == head, v, jnp.zeros_like(v))


def attention(packed, weight, size):
    chips = len(packed)
    span = packed[0].shape[0]
    half = span // 2
    width = packed[0].shape[1] // 3
    seq = chips * span
    heads = width // size
    model = weight.shape[0]
    step = min(256, seq)
    chunk = min(128, seq)
    score = size**-0.5

    def body(*refs):
        in_refs, w_ref = refs[:chips], refs[chips]
        head_refs = refs[chips + 1 : 2 * chips + 1]
        lse_ref = refs[2 * chips + 1]
        same_refs, other_ref = refs[2 * chips + 2 : 3 * chips + 2], refs[3 * chips + 2]
        k_ref, qt_ref, vt_ref, ot_ref, s_ref, p_ref = refs[3 * chips + 3 :]
        for c in range(chips):
            at = slice(c * span, (c + 1) * span)
            k_ref[at, :] = in_refs[c][:, width : 2 * width]
            qt_ref[:, at] = (turn(in_refs[c][:, :width]) * score).astype(BF)
            vt_ref[:, at] = turn(in_refs[c][:, 2 * width :]).astype(BF)

        def one(i, carry):
            at = pl.ds(pl.multiple_of(i * step, step), step)
            q = qt_ref[:, at]
            s_ref[0] = dot(k_ref[...], head_rows(q, 0, size))
            for h in range(heads):
                if h + 1 < heads:
                    s_ref[(h + 1) % 2] = dot(k_ref[...], head_rows(q, h + 1, size))
                now = h % 2
                top = fold(s_ref[now, :chunk, :], jnp.max)
                for r in range(chunk, seq, chunk):
                    top = jnp.maximum(top, fold(s_ref[now, r : r + chunk, :], jnp.max))
                top = jnp.max(top, axis=0, keepdims=True)
                norm = jnp.zeros((8, step), F32)
                for r in range(0, seq, chunk):
                    p = jnp.exp(s_ref[now, r : r + chunk, :] - top)
                    norm = norm + fold(p, jnp.sum)
                    p_ref[now, r : r + chunk, :] = p.astype(BF)
                norm = jnp.sum(norm, axis=0, keepdims=True)
                rows = slice(h * size, (h + 1) * size)
                ot_ref[rows, at] = dot(vt_ref[rows, :], p_ref[now]) / norm
                lse_ref[h : h + 1, at] = top + jnp.log(norm)
            return carry

        lax.fori_loop(0, seq // step, one, 0)
        for c in range(chips):
            at = slice(c * span, (c + 1) * span)
            o = ot_ref[:, at].T.astype(BF)
            head_refs[c][...] = o
            same_refs[c][...] = dot_bt(o[:half], w_ref[...]).astype(BF)
            other_ref[c * half : (c + 1) * half, :] = dot_bt(o[half:], w_ref[...]).astype(BF)

    out = pl.pallas_call(
        body,
        grid=(1,),
        in_specs=[whole((span, 3 * width))] * chips
        + [pl.BlockSpec((model, width), lambda i: (0, 3), pipeline_mode=pl.Buffered(1))],
        out_specs=[whole((span, width))] * chips
        + [whole((heads, seq))]
        + [whole((half, model))] * chips
        + [whole((seq // 2, model))],
        out_shape=[pltpu.HBM((span, width), BF)] * chips
        + [sds((heads, seq), F32)]
        + [sds((half, model), BF)] * chips
        + [sds((seq // 2, model), BF)],
        scratch_shapes=[
            pltpu.VMEM((seq, width), BF),
            pltpu.VMEM((width, seq), BF),
            pltpu.VMEM((width, seq), BF),
            pltpu.VMEM((width, seq), F32),
            pltpu.VMEM((2, seq, step), F32),
            pltpu.VMEM((2, seq, step), BF),
        ],
        compiler_params=params(14, 1),
        cost_estimate=cost(9),
        name="attention",
    )(*packed, weight)
    return out[:chips], out[chips], out[chips + 1 : -1], out[-1]


def attention_back(packed, heads_kept, lse, datt, weight, size):
    chips = len(packed)
    span = packed[0].shape[0]
    half = span // 2
    width = packed[0].shape[1] // 3
    seq = chips * span
    heads = width // size
    model = weight.shape[0]
    step = min(256, seq)
    chunk = min(128, seq)
    score = size**-0.5

    def body(*refs):
        at = 0

        def take(count):
            nonlocal at
            at += count
            return refs[at - count : at]

        in_refs, kept_refs = take(chips), take(chips)
        (lse_ref,) = take(1)
        datt_refs = take(2 * chips)
        (w_ref,) = take(1)
        dqkv_refs = take(chips)
        same_refs = take(chips)
        other_ref, sum_ref = take(2)
        k_ref, v_ref, kt_ref, qt_ref, q_ref, do_ref, dot_ref = take(7)
        inner_ref, s_ref, g_ref, p_ref, ds_ref, dk_ref, dv_ref, dqt_ref = take(8)
        for c in range(chips):
            rows = slice(c * span, (c + 1) * span)
            q = in_refs[c][:, :width].astype(F32) * score
            k = in_refs[c][:, width : 2 * width]
            q_ref[rows, :] = q.astype(BF)
            qt_ref[:, rows] = q.T.astype(BF)
            k_ref[rows, :] = k
            kt_ref[:, rows] = turn(k).astype(BF)
            v_ref[rows, :] = in_refs[c][:, 2 * width :]
            for b in range(2):
                d = dot(datt_refs[2 * c + b][...], w_ref[:, 3 * width :]).astype(BF)
                here = slice(c * span + b * half, c * span + (b + 1) * half)
                do_ref[here, :] = d
                dt = turn(d)
                dot_ref[:, here] = dt.astype(BF)
                prod = dt * turn(kept_refs[c][b * half : (b + 1) * half, :])
                for h in range(heads):
                    inner_ref[h : h + 1, here] = jnp.sum(
                        prod[h * size : (h + 1) * size, :], axis=0, keepdims=True
                    )

        def one(i, carry):
            at = pl.ds(pl.multiple_of(i * step, step), step)
            qt = qt_ref[:, at]
            dot_t = dot_ref[:, at]
            q = q_ref[at, :]
            do = do_ref[at, :]

            def scores(h):
                s_ref[h % 2] = dot(k_ref[...], head_rows(qt, h, size))
                g_ref[h % 2] = dot(v_ref[...], head_rows(dot_t, h, size))

            scores(0)
            for h in range(heads):
                if h + 1 < heads:
                    scores(h + 1)
                now = h % 2
                cols = slice(h * step, (h + 1) * step)
                lse = lse_ref[h : h + 1, at]
                inner = inner_ref[h : h + 1, at]
                for r in range(0, seq, chunk):
                    p = jnp.exp(s_ref[now, r : r + chunk, :] - lse)
                    ds = p * (g_ref[now, r : r + chunk, :] - inner)
                    p_ref[r : r + chunk, cols] = p.astype(BF)
                    ds_ref[r : r + chunk, cols] = ds.astype(BF)
                rows = slice(h * size, (h + 1) * size)
                dqt_ref[rows, at] = dot(kt_ref[rows, :], ds_ref[:, cols]) * score
            dv = dot(p_ref[...], jnp.concatenate([head_cols(do, h, size) for h in range(heads)], 0))
            dk = dot(ds_ref[...], jnp.concatenate([head_cols(q, h, size) for h in range(heads)], 0))

            @pl.when(i == 0)
            def _():
                dv_ref[...] = dv
                dk_ref[...] = dk

            @pl.when(i > 0)
            def _():
                dv_ref[...] += dv
                dk_ref[...] += dk

            return carry

        lax.fori_loop(0, seq // step, one, 0)
        for c in range(chips):
            rows = slice(c * span, (c + 1) * span)
            out = dqkv_refs[c]
            out[:, :width] = dqt_ref[:, rows].T.astype(BF)
            out[:, width : 2 * width] = dk_ref[rows, :].astype(BF)
            out[:, 2 * width :] = dv_ref[rows, :].astype(BF)
            sums = jnp.sum(out[...].astype(F32), axis=0, keepdims=True)
            if c == 0:
                sum_ref[...] = sums
            else:
                sum_ref[...] += sums
            w = w_ref[:, : 3 * width]
            same_refs[c][...] = dot_bt(out[:half, :], w).astype(BF)
            other_ref[c * half : (c + 1) * half, :] = dot_bt(out[half:, :], w).astype(BF)

    flat = [g for pair in datt for g in pair]
    out_shape = (
        [pltpu.HBM((span, 3 * width), BF)] * chips
        + [sds((half, model), BF)] * chips
        + [sds((seq // 2, model), BF), sds((1, 3 * width), F32)]
    )
    operands = (*map(late, (*packed, *heads_kept)), lse, *flat, late(weight))
    out = pl.pallas_call(
        body,
        grid=(1,),
        in_specs=[whole(a.shape) for a in operands],
        out_specs=[whole(a.shape) for a in out_shape],
        out_shape=out_shape,
        scratch_shapes=[
            pltpu.VMEM((seq, width), BF),
            pltpu.VMEM((seq, width), BF),
            pltpu.VMEM((width, seq), BF),
            pltpu.VMEM((width, seq), BF),
            pltpu.VMEM((seq, width), BF),
            pltpu.VMEM((seq, width), BF),
            pltpu.VMEM((width, seq), BF),
            pltpu.VMEM((heads, seq), F32),
            pltpu.VMEM((2, seq, step), F32),
            pltpu.VMEM((2, seq, step), F32),
            pltpu.VMEM((seq, heads * step), BF),
            pltpu.VMEM((seq, heads * step), BF),
            pltpu.VMEM((seq, width), F32),
            pltpu.VMEM((seq, width), F32),
            pltpu.VMEM((width, seq), F32),
        ],
        compiler_params=params(26, 1),
        cost_estimate=cost(15),
        name="attention_back",
    )(*operands)
    return out[:chips], out[chips : 2 * chips], out[2 * chips], out[2 * chips + 1]


def gelu_both(x):
    away = jnp.abs(x)
    t = 1.0 / (1.0 + (0.3275911 * 0.5**0.5) * away)
    bell = jnp.exp(-0.5 * (x * x))
    poly = t * (
        0.127414796
        + t * (-0.142248368 + t * (0.7107068705 + t * (-0.7265760135 + t * 0.5307027145)))
    )
    tail = poly * bell
    phi = jnp.where(x >= 0, 1.0 - tail, tail)
    return x * phi, phi + x * (bell * 0.3989422804014327)


def mlp_call(body, pairs, extra, weight, bias, outs, parts, scratch, name):
    rows, model = pairs[0].shape
    units = weight.shape[1] // 2
    step = min(256, units)
    blocks = units // step
    cols = lambda j: (0, j)
    in_specs = [whole((rows, model)) for _ in pairs]
    in_specs += [pl.BlockSpec((2 * rows, step), cols) for _ in extra]
    in_specs += [
        pl.BlockSpec((model, step), cols),
        pl.BlockSpec((model, step), lambda j: (0, blocks + j)),
        pl.BlockSpec((1, step), cols),
    ]
    out_specs = [pl.BlockSpec((2 * rows, step), cols) for _ in outs]
    out_specs += [pl.BlockSpec((1, step), cols)]
    out_specs += [whole((rows, model))] * (2 * parts)
    out_shape = [pltpu.HBM((2 * rows, units), d) for d in outs] + [sds((1, units), F32)]
    out_shape += [sds((rows, model), BF)] * (2 * parts)
    count = len(pairs) // 2
    return pl.pallas_call(
        body,
        grid=(blocks,),
        in_specs=in_specs,
        out_specs=out_specs,
        out_shape=out_shape,
        scratch_shapes=[pltpu.VMEM((2 * rows, model), F32)] * parts
        + [pltpu.VMEM((2 * rows, step), F32)] * scratch,
        compiler_params=params(8 + 5 * parts, 1),
        cost_estimate=cost(0.5),
        name=name,
    )(*pairs, *map(late, extra), weight, weight, bias)


def clear(*refs):
    @pl.when(pl.program_id(0) == 0)
    def _():
        for ref in refs:
            ref[...] = jnp.zeros_like(ref)


def finish(acc, low, high):
    rows = low.shape[0]

    @pl.when(pl.program_id(0) == pl.num_programs(0) - 1)
    def _():
        low[...] = acc[:rows, :].astype(BF)
        high[...] = acc[rows:, :].astype(BF)


CHUNK = 32


def mlp_forward(pair, weight, bias):
    rows = pair[0].shape[0]

    def body(a, b, w1_ref, w2_ref, bias_ref, act_ref, slope_ref, sum_ref, lo, hi, acc, pre):
        clear(acc, sum_ref)
        shift = bias_ref[...]
        for i, x in enumerate((a, b)):
            pre[i * rows : (i + 1) * rows, :] = dot(x[...], w1_ref[...])
        for i in range(2):
            at = slice(i * rows, (i + 1) * rows)
            for r in range(i * rows, (i + 1) * rows, CHUNK):
                act, slope = gelu_both(pre[r : r + CHUNK, :] + shift)
                act_ref[r : r + CHUNK, :] = act.astype(BF)
                slope_ref[r : r + CHUNK, :] = slope.astype(BF)
            acc[at, :] += dot_bt(act_ref[at, :], w2_ref[...])
        finish(acc, lo, hi)

    act, slope, _, lo, hi = mlp_call(body, pair, [], weight, bias, [BF, BF], 1, 1, "mlp_forward")
    return act, slope, lo, hi


def mlp_backward(pair, slope, weight, bias):
    rows = pair[0].shape[0]

    def body(a, b, slope_ref, w1_ref, w2_ref, bias_ref, dpre_ref, sum_ref, lo, hi, acc, pre):
        clear(acc)
        for i, g in enumerate((a, b)):
            pre[i * rows : (i + 1) * rows, :] = dot(g[...], w2_ref[...])
        sums = jnp.zeros((8, bias_ref.shape[1]), F32)
        for i in range(2):
            at = slice(i * rows, (i + 1) * rows)
            for r in range(i * rows, (i + 1) * rows, CHUNK):
                d = pre[r : r + CHUNK, :] * slope_ref[r : r + CHUNK, :].astype(F32)
                d = d.astype(BF)
                dpre_ref[r : r + CHUNK, :] = d
                sums = sums + fold(d.astype(F32), jnp.sum)
            acc[at, :] += dot_bt(dpre_ref[at, :], w1_ref[...])
        sum_ref[...] = jnp.sum(sums, axis=0, keepdims=True)
        finish(acc, lo, hi)

    dpre, sums, lo, hi = mlp_call(
        body, pair, [slope], weight, bias, [BF], 1, 1, "mlp_backward"
    )
    return dpre, sums, lo, hi


def mlp_both(pair, grads, weight, bias):
    rows = pair[0].shape[0]

    def body(
        a, b, c, d, w1_ref, w2_ref, bias_ref, act_ref, dpre_ref, sum_ref,
        lo, hi, blo, bhi, acc, back, pre, grad,
    ):
        clear(acc, back)
        shift = bias_ref[...]
        for i, (x, g) in enumerate(((a, c), (b, d))):
            at = slice(i * rows, (i + 1) * rows)
            pre[at, :] = dot(x[...], w1_ref[...])
            grad[at, :] = dot(g[...], w2_ref[...])
        sums = jnp.zeros((8, bias_ref.shape[1]), F32)
        for i in range(2):
            at = slice(i * rows, (i + 1) * rows)
            for r in range(i * rows, (i + 1) * rows, CHUNK):
                act, slope = gelu_both(pre[r : r + CHUNK, :] + shift)
                act_ref[r : r + CHUNK, :] = act.astype(BF)
                dpre = (grad[r : r + CHUNK, :] * slope).astype(BF)
                dpre_ref[r : r + CHUNK, :] = dpre
                sums = sums + fold(dpre.astype(F32), jnp.sum)
            back[at, :] += dot_bt(dpre_ref[at, :], w1_ref[...])
            acc[at, :] += dot_bt(act_ref[at, :], w2_ref[...])
        sum_ref[...] = jnp.sum(sums, axis=0, keepdims=True)
        finish(acc, lo, hi)
        finish(back, blo, bhi)

    act, dpre, sums, lo, hi, blo, bhi = mlp_call(
        body, [*pair, *grads], [], weight, bias, [BF, BF], 2, 2, "mlp_both"
    )
    return act, dpre, sums, lo, hi, blo, bhi


def weight_grads(products, dp, side, name, halves=True, heads=0):
    model = products[0][0][0].shape[1]
    step = model // dp
    half = step // 2
    cut = 2 if halves else 1
    sizes = [(len(left), len(right), right[0].shape[1]) for left, right in products]
    cols = sum(n for _, _, n in sizes)

    def body(side_ref, *refs):
        acc_ref = refs[-1]
        mine, other = refs[-3:-1] if halves else (refs[-2], None)
        at = base = 0
        for many, few, n in sizes:
            lefts, rights = refs[at : at + many], refs[at + many : at + many + few]
            at += many + few
            ratio = many // few
            acc = None
            for i in range(many):
                size = lefts[i].shape[0]
                here = slice((i % ratio) * size, (i % ratio + 1) * size)
                term = dot_at(lefts[i][...], rights[i // ratio][here, :])
                acc = term if acc is None else acc + term
            if halves:
                acc_ref[:, base : base + n] = acc
            elif heads and not base:
                size = n // (3 * heads)
                for k in range(3 * heads):
                    head, kind = k // 3, k % 3
                    at_k = (kind * heads + head) * size
                    mine[:, k * size : (k + 1) * size] = acc[:, at_k : at_k + size].astype(BF)
            else:
                mine[:, base : base + n] = acc.astype(BF)
            base += n
        if not halves:
            return
        low = pl.multiple_of(side_ref[0] * half, half)
        high = pl.multiple_of((1 - side_ref[0]) * half, half)
        mine[...] = acc_ref[pl.ds(low, half), :].astype(BF)
        other[...] = acc_ref[pl.ds(high, half), :].astype(BF)

    specs, operands = [pl.BlockSpec(memory_space=pltpu.SMEM)], [side.reshape(1)]
    for left, right in products:
        specs += [pl.BlockSpec((a.shape[0], step), lambda i: (0, i)) for a in left]
        specs += [whole(b.shape) for b in right]
        operands += [*left, *right]
    return pl.pallas_call(
        body,
        grid=(dp,),
        in_specs=specs,
        out_specs=[pl.BlockSpec((step // cut, cols), lambda i: (i, 0))] * cut,
        out_shape=[sds((model // cut, cols), BF)] * cut,
        scratch_shapes=[pltpu.VMEM((step, cols), F32)],
        compiler_params=params(14, 1),
        cost_estimate=cost(5),
        name=name,
    )(*operands)


def pieces(chunks):
    return [p for pair in chunks for p in pair]


def shards(
    tokens, cotangent, ln1_gain, ln1_bias, w_qkv, qv_bias, w_out, out_bias, scale_attn,
    ln2_gain, ln2_bias, w_fc1, fc1_bias, w_fc2, fc2_bias, scale_mlp,
):
    side = lax.axis_index("section")
    first = side == 0
    dp = lax.axis_size("dp")
    here = lax.axis_index("dp")
    chips = lax.axis_size("tensor") // 2
    rows, model = tokens.shape[2:]
    heads = qv_bias.shape[1]
    size = qv_bias.shape[2] * dp // 2
    width = heads * size
    units = w_fc1.shape[2]
    part = model // dp

    x0 = lax.dynamic_index_in_dim(tokens, side, 0, keepdims=False).reshape(rows, model)
    grad_top = lax.dynamic_index_in_dim(cotangent, side, 0, keepdims=False).reshape(rows, model)

    vectors = (ln1_gain, ln1_bias, out_bias, scale_attn, ln2_gain, ln2_bias, fc2_bias, scale_mlp)
    packed = jnp.concatenate(
        [v.reshape(-1) for v in vectors] + [fc1_bias.reshape(-1), qv_bias.reshape(-1)]
    )
    own_qkv = w_qkv.reshape(part, heads, 3, size).swapaxes(1, 2).reshape(part, 3 * width)
    own_att = jnp.concatenate([own_qkv, w_out[0].T], axis=1)
    give_att = half_of(own_att, 1 - side)
    came_att = swap_section(give_att)
    came_small = swap_section(tie(packed, give_att))
    both_small = jnp.concatenate(
        [jnp.where(first, packed, came_small), jnp.where(first, came_small, packed)]
    )
    cols = 4 * width
    tail = -(-both_small.size // (16 * cols)) * 16
    both_small = jnp.pad(both_small, (0, tail * cols - both_small.size)).reshape(tail, cols)
    mine_att = half_of(own_att, side)
    ring_att0 = jnp.concatenate([jnp.where(first, mine_att, came_att), both_small])
    ring_att1 = jnp.where(first, came_att, mine_att)
    hops_att0 = direct(ring_att0)
    own_ff = jnp.concatenate([w_fc1[0], w_fc2[0].T], axis=1)
    rest_att = swap_section(tie(mine_att, ring_att0))
    came_ff = swap_section(tie(half_of(own_ff, 1 - side), ring_att0))
    mine_ff = half_of(own_ff, side)
    ring_ff0 = jnp.where(first, mine_ff, came_ff)
    ring_ff1 = jnp.where(first, came_ff, mine_ff)

    def other_half(own, rest):
        left = half_of(own, 1 - side)
        return jnp.where(first, left, rest), jnp.where(first, rest, left)


    backs = [swap_section(v) for v in hops_att0]
    back = [ring_att0, *hops_att0]
    back[2] = tie(back[2], backs[-1])
    flat = in_order([v[-tail:] for v in back])
    flat = flat.reshape(dp, -1)[:, : 2 * packed.size].reshape(dp, 2, -1).astype(F32)
    cut = 8 * part
    vecs = flat[:, :, :cut].reshape(dp, 2, 8, part).transpose(1, 2, 0, 3).reshape(2, 8, model)
    vecs = (vecs[0], vecs[1])
    bias_fc1 = flat[:, :, cut : cut + units // dp].swapaxes(0, 1).reshape(2, 1, units)
    qv = flat[:, :, cut + units // dp :].reshape(dp, 2, heads, -1).transpose(1, 2, 0, 3)
    qv = qv.reshape(2, heads, 2, size)
    bias_qkv = jnp.stack([qv[:, :, 0], jnp.zeros_like(qv[:, :, 0]), qv[:, :, 1]], axis=1)
    bias_qkv = bias_qkv.reshape(2, 1, 3 * width)

    norm1 = norm_first(tie(x0, came_ff), vecs[0])
    rest_ff = swap_section(tie(mine_ff, norm1))
    rest_att0, rest_att1 = other_half(own_att, rest_att)
    rest_ff0, rest_ff1 = other_half(own_ff, rest_ff)
    att1 = Ring(ring_att1)
    att0 = assemble([(tie(ring_att0, norm1), rest_att0), *zip(hops_att0, backs)], model)
    ff0, ff1 = Ring(ring_ff0), Ring(ring_ff1)
    hop_ff0 = ff0.hop(norm1)

    def projection(weight, s):
        return lambda pair: project_qkv(pair, weight, bias_qkv[s])

    chunks0, qkv0 = gather_tokens(norm1, projection(att0, 0), [rest_ff, *hop_ff0])
    beside = [*ff0.hop(), *ff0.back()]
    kept0, lse0, sames, others = attention(qkv0, att0, size)
    terms, _ = scatter_tokens(
        sames,
        tie(others, *beside),
        beside=lambda gate: [*ff0.hop(gate), *ff0.back(gate)],
    )
    attended0, residual0, norm2 = after_attention(x0, terms, vecs[0])
    ff0.back()
    beside = [*att1.hop(norm2), *att1.hop()]
    w_ff0 = assemble([(ring_ff0, rest_ff0), *zip(ff0.hops, ff0.backs)], model)
    second0, mlp0 = gather_tokens(
        norm2, lambda pair: mlp_forward(pair, w_ff0, bias_fc1[0]), beside
    )
    act0, slope0, sames, others = zip(*mlp0)
    beside = [*att1.hop(second0[-1][0]), *att1.back(second0[-1][0])]
    terms, _ = scatter_tokens(
        sames,
        [others[0], *[tie(v, *beside) for v in others[1:]]],
        beside=lambda gate: [*ff1.hop(gate), *att1.back(gate), *att1.back(gate)],
    )
    mlp_out0, y0, norm1 = after_mlp(residual0, terms, vecs[0], vecs[1])

    w_att1 = assemble([(ring_att1, rest_att1), *zip(att1.hops, att1.backs)], model)
    low1, sums_fc2_1 = start_back(grad_top, vecs[1])
    beside = [*ff1.hop(norm1), *ff1.back(norm1)]
    chunks1, qkv1 = gather_tokens(norm1, projection(w_att1, 1), beside)
    gate = chunks1[-1][0]
    came = [from_chip(tie(low1, gate), step) for step in range(1, chips)]
    beside = [*came, *ff1.hop(gate), *ff1.back(gate)]
    kept1, lse1, sames, others = attention(qkv1, w_att1, size)
    others = tie(others, *beside)
    grads1 = [(low1, core_swap(low1))] + [(v, core_swap(tie(v, lse1))) for v in came]
    terms, _ = scatter_tokens(
        sames, others, beside=lambda gate: [*ff1.back(gate), *pieces(grads1)]
    )
    attended1, residual1, norm2 = after_attention(y0, terms, vecs[1])
    w_ff1 = assemble([(ring_ff1, rest_ff1), *zip(ff1.hops, ff1.backs)], model)
    spare = list(grads1)
    second1, mlp1 = gather_tokens(
        norm2, lambda pair: mlp_both(pair, spare.pop(0), w_ff1, bias_fc1[1])
    )
    act1, dpre1, sums_fc1_1, sames_y1, others_y1, sames, others = zip(*mlp1)

    def grad_ff(second, dpre, grads, act):
        return lambda after: weight_grads(
            [
                (pieces(second), [late(tie(dpre[0], after)), *map(late, dpre[1:])]),
                (pieces(grads), [late(a) for a in act]),
            ],
            dp,
            side,
            "grad_ff",
        )

    def grad_att(chunks, dqkv, datt, kept):
        return lambda after: weight_grads(
            [
                (pieces(chunks), [late(tie(dqkv[0], after)), *map(late, dqkv[1:])]),
                (pieces(datt), [late(a) for a in kept]),
            ],
            dp,
            side,
            "grad_att",
            False,
            heads,
        )[0]

    old = [tuple(map(late, pair)) for pair in grads1]
    terms, g = scatter_tokens(sames, others, grad_ff(second1, dpre1, old, act1))
    sum_ff1 = RingSum((0, 1), *g)
    dres1, low, sums1 = back_second(grad_top, residual1, attended1, terms, vecs[1])
    came_y0 = lax.ppermute(tie(y0, low), "section", [(1, 0)])
    datt, _ = gather_tokens(low, lambda pair: pair[0], sum_ff1.step())
    sums_y1, local_y1 = core_sums(sames_y1, [tie(v, low) for v in others_y1])
    terms_y1 = send_sums([tie(v, datt[-1][0]) for v in sums_y1])
    beside = [came_y0, *terms_y1, *sum_ff1.step(low)]
    dqkv, sames, others, qkv_sums1 = attention_back(qkv1, kept1, lse1, datt, w_att1, size)
    old = [tuple(map(late, pair)) for pair in chunks1]
    terms, g = scatter_tokens(
        sames, tie(others, *beside), grad_att(old, dqkv, datt, kept1), sum_ff1.step
    )
    sum_att1 = RingSum((0, 1), g)
    sum_att1.step()
    dx1, low0, edge1 = back_first(dres1, late(y0), terms, vecs[1], late(mlp_out0), vecs[0])

    y1, sums_sc_1 = last_output(
        residual1, [tie(sames_y1[0], low0), *terms_y1, local_y1], grad_top, vecs[1]
    )

    slopes = list(slope0)
    grads0, mlp_back0 = gather_tokens(
        low0,
        lambda pair: mlp_backward(pair, slopes.pop(0), w_ff0, bias_fc1[0]),
        [y1, *sum_ff1.step(low0)],
    )
    dpre0, sums_fc1_0, sames, others = zip(*mlp_back0)
    hop_att1 = sum_att1.step(grads0[-1][0])
    old = [tuple(map(late, pair)) for pair in second0]
    terms, g = scatter_tokens(
        sames,
        others,
        grad_ff(old, dpre0, grads0, act0),
        lambda gate: [*sum_ff1.step(gate), *hop_att1],
    )
    sum_ff0 = RingSum((1, 0), *g)
    dres0, low, sums0 = back_second(
        dx1, late(residual0), late(attended0), terms, vecs[0]
    )
    beside = [*sum_att1.step(low), *sum_ff0.step(low)]
    datt, _ = gather_tokens(low, lambda pair: pair[0], beside)
    beside = [*sum_att1.step(low), *sum_ff0.step(low)]
    dqkv, sames, others, qkv_sums0 = attention_back(qkv0, kept0, lse0, datt, att0, size)
    old = [tuple(map(late, pair)) for pair in chunks0]
    terms, g = scatter_tokens(
        sames,
        tie(others, *beside),
        grad_att(old, dqkv, datt, kept0),
        sum_ff0.step,
    )
    sum_att0 = RingSum((1, 0), g)
    sum_att0.step()
    going = sum_att0.step()
    dx0, edge0 = back_first(dres0, x0, terms, vecs[0])
    came_dx0 = lax.ppermute(dx0, "section", [(1, 0)])
    step_ff0 = sum_ff0.step(dx0)
    second_hop = sum_att0.step(dx0)
    came_y1 = lax.ppermute(tie(y1, sum_att0.sent), "section", [(0, 1)])
    step_att1 = sum_att1.step(dx0)
    third_hop = sum_att0.step()
    sent = sum_att0.sent
    last_ff0 = sum_ff0.step()
    sum_att0.step()
    came_dx1 = lax.ppermute(tie(dx1, sent), "section", [(0, 1)])

    def both(low, high, came_low, came_high):
        mine = jnp.where(first, low, high)
        came = jnp.where(first, came_low, came_high)
        return jnp.stack([jnp.where(first, mine, came), jnp.where(first, came, mine)])[None, :, None]

    block_out = both(y0, y1, came_y0, came_y1)
    input_grads = both(dx0, dx1, came_dx0, came_dx1)
    sum_att0.came = tie(sum_att0.came, block_out, input_grads)

    def by_unit(qkv_sums, unit_sums):
        q = qkv_sums[:, :width].reshape(heads, 1, size)
        v = qkv_sums[:, 2 * width :].reshape(heads, 1, size)
        bias = jnp.concatenate([q, v], 1).reshape(heads, dp, -1).swapaxes(0, 1).reshape(dp, -1)
        return jnp.concatenate([bias, unit_sums.reshape(dp, -1)], axis=1)

    unit0 = by_unit(tie(qkv_sums0, dx0), sum(sums_fc1_0))
    unit1 = by_unit(tie(qkv_sums1, dx0), sum(sums_fc1_1))
    vec = jnp.concatenate(
        [edge0[:2], sums0[:4], edge1[2:4], edge1[:2], sums1[:4], sums_sc_1[:1], sums_fc2_1[:1]]
    )
    vec = tie(vec, *going)
    vec = vec + core_swap(vec)
    vec = tie(sum([from_chip(vec, step) for step in range(1, chips)], vec), *second_hop, *step_ff0, came_y1)
    vec = tie(vec, sent, *last_ff0)
    vec = vec.reshape(2, 8, dp, part).swapaxes(1, 2).reshape(2, dp, 8 * part)
    vec0 = jnp.concatenate([vec[0], unit0], axis=1)
    vec1 = jnp.concatenate([vec[1], unit1], axis=1)
    own = jnp.where(first, vec0, vec1) + swap_section(jnp.where(first, vec1, vec0))
    own = tie(own, *step_att1, came_dx1, sum_att0.own)
    vec = lax.dynamic_slice_in_dim(own, here, 1, 0)
    for step in range(1, dp):
        pairs = [(i, (i + step) % dp) for i in range(dp)]
        other = lax.dynamic_slice_in_dim(own, lax.rem(here + step, dp), 1, 0)
        vec = vec + lax.ppermute(other, "dp", pairs)
    cut = 8 * part + heads * (2 * size // dp)
    bias_grad = vec[:, 8 * part : cut].reshape(1, heads, -1)
    fc1_grad = vec[:, cut:].reshape(1, 1, -1)
    g_ln1, b_ln1, g_ln2, b_ln2, g_sc_attn, g_out_bias, g_sc_mlp, g_fc2_bias = (
        vec[:, i * part : (i + 1) * part] for i in range(8)
    )

    def owned(low, high):
        top = jnp.where(first, low.own, high.came.astype(F32))
        bottom = jnp.where(first, low.came.astype(F32), high.own)
        return jnp.concatenate([top, bottom], 0)

    g_ff = owned(sum_ff0, sum_ff1)
    g_att = jnp.where(
        first,
        sum_att0.own + sum_att0.came.astype(F32),
        sum_att1.own + sum_att1.came.astype(F32),
    )
    g_qkv = g_att[None, :, : 3 * width]
    g_out = g_att[:, 3 * width :].T[None]
    g_fc1 = g_ff[:, :units][None]
    g_fc2 = g_ff[:, units:].T[None]
    return (
        block_out, input_grads, g_ln1, b_ln1, g_qkv, bias_grad, g_out, g_out_bias, g_sc_attn,
        g_ln2, b_ln2, g_fc1, fc1_grad, g_fc2, g_fc2_bias, g_sc_mlp,
    )


def solution(mesh):
    vec = P("section", "dp")
    by_row = P("section", "dp", "tensor")
    by_unit = P("section", "tensor", "dp")
    data = P(None, "dp", "tensor", None)
    split = P("section", None, "dp", "tensor", None)
    given = (
        vec, vec, by_row, by_unit, by_unit, vec, vec, vec, vec, by_row, by_unit, by_unit, vec, vec,
    )
    return jax.shard_map(
        shards,
        mesh=mesh,
        in_specs=(data, data) + given,
        out_specs=(split, split) + given,
        check_vma=False,
    )
```

```python
from functools import partial

import jax
import jax.numpy as jnp
from jax import lax
from jax.experimental import pallas as pl
from jax.experimental.pallas import tpu as pltpu
from jax.sharding import PartitionSpec as P

EPSILON = 1e-06
BF = jnp.bfloat16
F32 = jnp.float32
MIB = 1 << 20

LN1_G, LN1_B, OUT_B, SC_ATTN, LN2_G, LN2_B, FC2_B, SC_MLP = range(8)


def dot(a, b):
    return lax.dot_general(a, b, (((1,), (0,)), ((), ())), preferred_element_type=F32)


def dot_bt(a, b):
    return lax.dot_general(a, b, (((1,), (1,)), ((), ())), preferred_element_type=F32)


def dot_at(a, b):
    return lax.dot_general(a, b, (((0,), (0,)), ((), ())), preferred_element_type=F32)


def turn(v):
    return v.astype(F32).T


def params(limit, grid=0):
    return pltpu.CompilerParams(
        vmem_limit_bytes=limit * MIB,
        dimension_semantics=("arbitrary",) * grid if grid else None,
    )


def late(v):
    return pltpu.with_memory_space_constraint(v, pltpu.HBM)


def whole(shape):
    return pl.BlockSpec(shape, lambda i: (0, 0), pipeline_mode=pl.Buffered(1))


def cost(micros):
    return pl.CostEstimate(flops=int(micros * 1.15e9), bytes_accessed=0, transcendentals=0)


def sds(shape, dtype):
    return jax.ShapeDtypeStruct(shape, dtype)


def core_swap(v):
    count = lax.axis_size("tensor")
    return lax.ppermute(v, "tensor", [(i, i ^ 1) for i in range(count)])


def from_chip(v, step):
    count = lax.axis_size("tensor")
    chips = count // 2
    pairs = [(((i // 2 + step) % chips) * 2 + i % 2, i) for i in range(count)]
    return lax.ppermute(v, "tensor", pairs)


def tie(v, *after):
    if not after:
        return v
    return lax.optimization_barrier((v, *after))[0]


def tie_all(vs, *after):
    return lax.optimization_barrier((*vs, *after))[: len(vs)]


def gather_tokens(own, work, beside=()):
    chips = lax.axis_size("tensor") // 2
    came = [from_chip(own, step) for step in range(1, chips)]
    chunks = [(own, core_swap(own))]
    results = [work(chunks[0])]
    for same in came:
        same = tie(same, results[-1], *beside)
        chunks.append((same, core_swap(same)))
        results.append(work(chunks[-1]))
    return chunks, results


def core_sums(sames, others):
    chips, rows = len(sames), sames[0].shape[0]
    if isinstance(others, (list, tuple)):
        came = [core_swap(v) for v in others[1:]]
        local = core_swap(tie(others[0], came[-1]))
    else:
        local = core_swap(others)
        came = [local[c * rows : (c + 1) * rows] for c in range(1, chips)]
    sums = [(a.astype(F32) + b.astype(F32)).astype(BF) for a, b in zip(sames[1:], came)]
    return sums, local


def send_sums(sums):
    chips = len(sums) + 1
    return [from_chip(both, chips - step) for step, both in enumerate(sums, 1)]


def scatter_tokens(sames, others, work=None, beside=None):
    sums, local = core_sums(sames, others)
    terms = send_sums(sums)
    made = work(sums[-1]) if work else local
    more = beside(sums[-1]) if beside else ()
    terms = [tie(t, made, local, *more) for t in terms]
    return [sames[0], *terms, local], made


def swap_section(v):
    return lax.ppermute(v, "section", [(0, 1), (1, 0)])


def assemble(shards, rows):
    count = len(shards)
    cut = len(shards[0])
    size, cols = rows // (count * cut), shards[0][0].shape[1]
    place = jnp.stack([lax.axis_index("dp"), lax.axis_index("section")])

    def body(place_ref, *refs):
        out_ref, sems = refs[count * cut :]
        z, x = place_ref[0], place_ref[1]
        started = []
        for k in range(count):
            base = lax.rem(z + (count - k), count) * (cut * size)
            for i, at in enumerate([base] if cut == 1 else [base + x * size, base + (1 - x) * size]):
                copy = pltpu.make_async_copy(
                    refs[k * cut + i].at[pl.ds(0, size), :],
                    out_ref.at[pl.ds(pl.multiple_of(at, size), size), :],
                    sems.at[k * cut + i],
                )
                copy.start()
                started.append(copy)
        for copy in started:
            copy.wait()

    hbm = pl.BlockSpec(memory_space=pl.ANY)
    return pl.pallas_call(
        body,
        in_specs=[pl.BlockSpec(memory_space=pltpu.SMEM)] + [hbm] * (count * cut),
        out_specs=pl.BlockSpec(memory_space=pltpu.VMEM),
        out_shape=sds((rows, cols), shards[0][0].dtype),
        scratch_shapes=[pltpu.SemaphoreType.DMA((count * cut,))],
        compiler_params=params(6),
        cost_estimate=cost(2),
        name="assemble",
    )(place, *[late(v) for shard in shards for v in shard])


def half_of(v, which):
    half = v.shape[0] // 2
    return lax.dynamic_slice_in_dim(v, which * half, half, 0)


def direct(own):
    count = lax.axis_size("dp")
    return [
        lax.ppermute(own, "dp", [(i, (i + step) % count) for i in range(count)])
        for step in range(1, count)
    ]


def third(values, index):
    cuts = [-(-len(values) * i // 3) for i in range(4)]
    return values[cuts[index] : cuts[index + 1]]


class Ring:
    def __init__(self, own):
        self.last, self.hops, self.backs, self.at, self.back_at = own, [], [], 0, 0

    def hop(self, *gate):
        count = lax.axis_size("dp")
        pairs = [(i, (i + 1) % count) for i in range(count)]
        new = []
        for i in range(len(third(range(count - 1), self.at))):
            self.last = lax.ppermute(tie(self.last, *gate) if i == 0 else self.last, "dp", pairs)
            new.append(self.last)
        self.hops += new
        self.at += 1
        return new

    def back(self, *gate):
        count = lax.axis_size("dp")
        which = third(range(count - 1), self.back_at)
        new = [swap_section(tie(self.hops[i], *gate)) for i in which]
        self.backs += new
        self.back_at += 1
        return new


def in_order(back):
    count = len(back)
    ahead = [back[0], *back[:0:-1]]
    twice = jnp.stack(ahead + ahead)
    return lax.dynamic_slice_in_dim(twice, count - lax.axis_index("dp"), count, 0)


def dp_rows(v, back):
    dp = lax.axis_size("dp")
    part = v.shape[0] // dp
    place = lax.rem(lax.axis_index("dp") + (dp - back), dp)
    return lax.dynamic_slice_in_dim(v, place * part, part, 0)


class RingSum:
    def __init__(self, pair, mine, other=None):
        self.mine, self.other, self.pair = mine, other, pair
        self.terms, self.at, self.done = [], 0, 0

    def total(self, gate=()):
        first = tie(self.terms[0], *gate)
        return sum(t.astype(F32) for t in [first, *self.terms[1:]])

    def one(self, gate):
        dp = lax.axis_size("dp")
        self.done += 1
        new = []
        if self.terms:
            pairs = [(i, (i + 1) % dp) for i in range(dp)]
            self.sent = self.total(gate).astype(BF)
            new.append(lax.ppermute(self.sent, "dp", pairs))
        if self.other is not None:
            new.append(swap_section(tie(dp_rows(self.other, self.done), *gate)))
        self.terms = [*new, dp_rows(self.mine, self.done)]
        return new

    def step(self, *gate):
        self.at += 1
        if self.at == 5:
            self.own = self.total(gate)
            self.came = lax.ppermute(self.own.astype(BF), "section", [self.pair])
            return [self.came]
        count = 1 if self.at == 1 else len(third(range(lax.axis_size("dp") - 1), self.at - 2))
        return [v for i in range(count) for v in self.one(gate if i == 0 else ())]


def standardize(v):
    centred = v - jnp.mean(v, axis=-1, keepdims=True)
    var = jnp.mean(centred * centred, axis=-1, keepdims=True)
    scale = lax.rsqrt(var + EPSILON)
    return centred * scale, scale


def norm_of(v, vec, gain, shift):
    return (standardize(v)[0] * vec[gain : gain + 1, :] + vec[shift : shift + 1, :]).astype(BF)


def norm_back(v, grad, gain):
    xh, scale = standardize(v)
    dxh = grad * gain
    inner = jnp.mean(dxh * xh, axis=-1, keepdims=True)
    out = scale * (dxh - jnp.mean(dxh, axis=-1, keepdims=True) - xh * inner)
    return out, grad * xh


def total(refs):
    out = refs[0][...].astype(F32)
    for ref in refs[1:]:
        out = out + ref[...].astype(F32)
    return out


def fold(v, op):
    return op(v.reshape(-1, 8, v.shape[1]), axis=0)


def add_rows(ref, rows):
    for k, row in enumerate(rows):
        ref[8 * k : 8 * k + 8, :] += fold(row, jnp.sum)


def rowwise(body, row_ins, fulls, row_outs, sums, name):
    rows, width = row_ins[0].shape
    step = min(128, rows)
    some, outs = len(row_ins) + len(fulls), len(row_outs)

    def kernel(*refs):
        if not sums:
            body(*refs)
            return
        sum_ref, acc_ref = refs[some + outs :]

        @pl.when(pl.program_id(0) == 0)
        def _():
            acc_ref[...] = jnp.zeros_like(acc_ref)

        body(*refs[: some + outs], acc_ref)

        @pl.when(pl.program_id(0) == pl.num_programs(0) - 1)
        def _():
            for k in range(sums):
                sum_ref[k : k + 1, :] = jnp.sum(
                    acc_ref[8 * k : 8 * k + 8, :], axis=0, keepdims=True
                )

    out_shape = [sds((rows, width), d) for d in row_outs]
    out_shape += [sds((sums, width), F32)] if sums else []
    block = pl.BlockSpec((step, width), lambda i: (i, 0))
    return pl.pallas_call(
        kernel,
        grid=(rows // step,),
        in_specs=[block] * len(row_ins) + [whole(a.shape) for a in fulls],
        out_specs=[block] * outs + ([whole((sums, width))] if sums else []),
        out_shape=out_shape,
        scratch_shapes=[pltpu.VMEM((8 * sums, width), F32)] if sums else [],
        compiler_params=params(8, 1),
        cost_estimate=cost(2),
        name=name,
    )(*row_ins, *fulls)


def norm_first(x, vec):
    def body(x_ref, vec_ref, out_ref):
        out_ref[...] = norm_of(x_ref[...].astype(F32), vec_ref[...], LN1_G, LN1_B)

    return rowwise(body, [x], [vec], [BF], 0, "norm_first")[0]


def after_attention(x, terms, vec):
    count = len(terms)

    def body(*refs):
        x_ref, term_refs, vec_ref = refs[0], refs[1 : 1 + count], refs[1 + count]
        att_ref, res_ref, norm_ref = refs[2 + count :]
        v = vec_ref[...]
        attended = total(term_refs) + v[OUT_B : OUT_B + 1, :]
        residual = x_ref[...].astype(F32) + v[SC_ATTN : SC_ATTN + 1, :] * attended
        att_ref[...] = attended.astype(BF)
        res_ref[...] = residual
        norm_ref[...] = norm_of(residual, v, LN2_G, LN2_B)

    return rowwise(body, [x, *terms], [vec], [BF, F32, BF], 0, "after_attention")


def after_mlp(residual, terms, vec, vec_next):
    count = len(terms)

    def body(*refs):
        res_ref, term_refs = refs[0], refs[1 : 1 + count]
        vec_ref, next_ref, mlp_ref, y_ref, norm_ref = refs[1 + count :]
        v = vec_ref[...]
        mlp = total(term_refs) + v[FC2_B : FC2_B + 1, :]
        y = (res_ref[...] + v[SC_MLP : SC_MLP + 1, :] * mlp).astype(BF)
        mlp_ref[...] = mlp.astype(BF)
        y_ref[...] = y
        norm_ref[...] = norm_of(y.astype(F32), next_ref[...], LN1_G, LN1_B)

    return rowwise(body, [residual, *terms], [vec, vec_next], [BF, BF, BF], 0, "after_mlp")


def last_output(residual, terms, grad, vec):
    count = len(terms)

    def body(*refs):
        res_ref, term_refs = refs[0], refs[1 : 1 + count]
        grad_ref, vec_ref, y_ref, sum_ref = refs[1 + count :]
        v = vec_ref[...]
        mlp = total(term_refs) + v[FC2_B : FC2_B + 1, :]
        y_ref[...] = (res_ref[...] + v[SC_MLP : SC_MLP + 1, :] * mlp).astype(BF)
        add_rows(sum_ref, [grad_ref[...].astype(F32) * mlp])

    return rowwise(body, [residual, *terms, grad], [vec], [BF], 1, "last_output")


def start_back(grad, vec):
    def body(grad_ref, vec_ref, out_ref, sum_ref):
        low = (vec_ref[...][SC_MLP : SC_MLP + 1, :] * grad_ref[...].astype(F32)).astype(BF)
        out_ref[...] = low
        add_rows(sum_ref, [low.astype(F32)])

    return rowwise(body, [grad], [vec], [BF], 1, "start_back")


def back_second(grad, residual, attended, terms, vec):
    count = len(terms)

    def body(*refs):
        grad_ref, res_ref, att_ref = refs[:3]
        term_refs = refs[3 : 3 + count]
        vec_ref, dres_ref, low_ref, sum_ref = refs[3 + count :]
        v = vec_ref[...]
        dn = total(term_refs)
        back, dgain = norm_back(res_ref[...], dn, v[LN2_G : LN2_G + 1, :])
        dres = grad_ref[...].astype(F32) + back
        low = (v[SC_ATTN : SC_ATTN + 1, :] * dres).astype(BF)
        dres_ref[...] = dres
        low_ref[...] = low
        add_rows(sum_ref, [dgain, dn, dres * att_ref[...].astype(F32), low.astype(F32)])

    return rowwise(
        body, [grad, residual, attended, *terms], [vec], [F32, BF], 4, "back_second"
    )


def back_first(dres, x, terms, vec, mlp_below=None, vec_below=None):
    count = len(terms)
    below = mlp_below is not None

    def body(*refs):
        dres_ref, x_ref = refs[:2]
        term_refs = refs[2 : 2 + count]
        rest = refs[2 + count :]
        if below:
            mlp_ref, vec_ref, under_ref, dx_ref, low_ref, sum_ref = rest
        else:
            vec_ref, dx_ref, sum_ref = rest
        v = vec_ref[...]
        dn = total(term_refs)
        back, dgain = norm_back(x_ref[...].astype(F32), dn, v[LN1_G : LN1_G + 1, :])
        dx = (dres_ref[...] + back).astype(BF)
        dx_ref[...] = dx
        rows = [dgain, dn]
        if below:
            wide = dx.astype(F32)
            low = (under_ref[...][SC_MLP : SC_MLP + 1, :] * wide).astype(BF)
            low_ref[...] = low
            rows += [wide * mlp_ref[...].astype(F32), low.astype(F32)]
        add_rows(sum_ref, rows)

    row_ins = [dres, x, *terms] + ([mlp_below] if below else [])
    fulls = [vec] + ([vec_below] if below else [])
    return rowwise(body, row_ins, fulls, [BF, BF] if below else [BF], 4 if below else 2, "back_first")


def project_qkv(pair, weight, bias):
    rows, width = pair[0].shape
    cols = bias.shape[1]

    def body(a_ref, b_ref, w_ref, bias_ref, out_ref):
        w = w_ref[...]
        shift = bias_ref[...]
        out_ref[:rows, :] = (dot(a_ref[...], w) + shift).astype(BF)
        out_ref[rows:, :] = (dot(b_ref[...], w) + shift).astype(BF)

    return pl.pallas_call(
        body,
        grid=(1,),
        in_specs=[
            whole((rows, width)), whole((rows, width)), whole((width, cols)), whole((1, cols))
        ],
        out_specs=whole((2 * rows, cols)),
        out_shape=sds((2 * rows, cols), BF),
        compiler_params=params(6, 1),
        cost_estimate=cost(0.5),
        name="project_qkv",
    )(*pair, weight, bias)


def head_rows(v, head, size):
    rows = lax.broadcasted_iota(jnp.int32, v.shape, 0)
    return jnp.where(rows // size == head, v, jnp.zeros_like(v))


def head_cols(v, head, size):
    cols = lax.broadcasted_iota(jnp.int32, v.shape, 1)
    return jnp.where(cols // size == head, v, jnp.zeros_like(v))


def attention(packed, weight, size):
    chips = len(packed)
    span = packed[0].shape[0]
    half = span // 2
    width = packed[0].shape[1] // 3
    seq = chips * span
    heads = width // size
    model = weight.shape[0]
    step = min(256, seq)
    chunk = min(128, seq)
    score = size**-0.5

    def body(*refs):
        in_refs, w_ref = refs[:chips], refs[chips]
        head_refs = refs[chips + 1 : 2 * chips + 1]
        lse_ref = refs[2 * chips + 1]
        same_refs, other_ref = refs[2 * chips + 2 : 3 * chips + 2], refs[3 * chips + 2]
        k_ref, qt_ref, vt_ref, ot_ref, s_ref, p_ref = refs[3 * chips + 3 :]
        for c in range(chips):
            at = slice(c * span, (c + 1) * span)
            k_ref[at, :] = in_refs[c][:, width : 2 * width]
            qt_ref[:, at] = (turn(in_refs[c][:, :width]) * score).astype(BF)
            vt_ref[:, at] = turn(in_refs[c][:, 2 * width :]).astype(BF)

        def one(i, carry):
            at = pl.ds(pl.multiple_of(i * step, step), step)
            q = qt_ref[:, at]
            s_ref[0] = dot(k_ref[...], head_rows(q, 0, size))
            for h in range(heads):
                if h + 1 < heads:
                    s_ref[(h + 1) % 2] = dot(k_ref[...], head_rows(q, h + 1, size))
                now = h % 2
                top = fold(s_ref[now, :chunk, :], jnp.max)
                for r in range(chunk, seq, chunk):
                    top = jnp.maximum(top, fold(s_ref[now, r : r + chunk, :], jnp.max))
                top = jnp.max(top, axis=0, keepdims=True)
                norm = jnp.zeros((8, step), F32)
                for r in range(0, seq, chunk):
                    p = jnp.exp(s_ref[now, r : r + chunk, :] - top)
                    norm = norm + fold(p, jnp.sum)
                    p_ref[now, r : r + chunk, :] = p.astype(BF)
                norm = jnp.sum(norm, axis=0, keepdims=True)
                rows = slice(h * size, (h + 1) * size)
                ot_ref[rows, at] = dot(vt_ref[rows, :], p_ref[now]) / norm
                lse_ref[h : h + 1, at] = top + jnp.log(norm)
            return carry

        lax.fori_loop(0, seq // step, one, 0)
        for c in range(chips):
            at = slice(c * span, (c + 1) * span)
            o = ot_ref[:, at].T.astype(BF)
            head_refs[c][...] = o
            same_refs[c][...] = dot_bt(o[:half], w_ref[...]).astype(BF)
            other_ref[c * half : (c + 1) * half, :] = dot_bt(o[half:], w_ref[...]).astype(BF)

    out = pl.pallas_call(
        body,
        grid=(1,),
        in_specs=[whole((span, 3 * width))] * chips
        + [pl.BlockSpec((model, width), lambda i: (0, 3), pipeline_mode=pl.Buffered(1))],
        out_specs=[whole((span, width))] * chips
        + [whole((heads, seq))]
        + [whole((half, model))] * chips
        + [whole((seq // 2, model))],
        out_shape=[pltpu.HBM((span, width), BF)] * chips
        + [sds((heads, seq), F32)]
        + [sds((half, model), BF)] * chips
        + [sds((seq // 2, model), BF)],
        scratch_shapes=[
            pltpu.VMEM((seq, width), BF),
            pltpu.VMEM((width, seq), BF),
            pltpu.VMEM((width, seq), BF),
            pltpu.VMEM((width, seq), F32),
            pltpu.VMEM((2, seq, step), F32),
            pltpu.VMEM((2, seq, step), BF),
        ],
        compiler_params=params(14, 1),
        cost_estimate=cost(9),
        name="attention",
    )(*packed, weight)
    return out[:chips], out[chips], out[chips + 1 : -1], out[-1]


def attention_back(packed, heads_kept, lse, datt, weight, size):
    chips = len(packed)
    span = packed[0].shape[0]
    half = span // 2
    width = packed[0].shape[1] // 3
    seq = chips * span
    heads = width // size
    model = weight.shape[0]
    step = min(256, seq)
    chunk = min(128, seq)
    score = size**-0.5

    def body(*refs):
        at = 0

        def take(count):
            nonlocal at
            at += count
            return refs[at - count : at]

        in_refs, kept_refs = take(chips), take(chips)
        (lse_ref,) = take(1)
        datt_refs = take(2 * chips)
        (w_ref,) = take(1)
        dqkv_refs = take(chips)
        same_refs = take(chips)
        other_ref, sum_ref = take(2)
        k_ref, v_ref, kt_ref, qt_ref, q_ref, do_ref, dot_ref = take(7)
        inner_ref, s_ref, g_ref, p_ref, ds_ref, dk_ref, dv_ref, dqt_ref = take(8)
        for c in range(chips):
            rows = slice(c * span, (c + 1) * span)
            q = in_refs[c][:, :width].astype(F32) * score
            k = in_refs[c][:, width : 2 * width]
            q_ref[rows, :] = q.astype(BF)
            qt_ref[:, rows] = q.T.astype(BF)
            k_ref[rows, :] = k
            kt_ref[:, rows] = turn(k).astype(BF)
            v_ref[rows, :] = in_refs[c][:, 2 * width :]
            for b in range(2):
                d = dot(datt_refs[2 * c + b][...], w_ref[:, 3 * width :]).astype(BF)
                here = slice(c * span + b * half, c * span + (b + 1) * half)
                do_ref[here, :] = d
                dt = turn(d)
                dot_ref[:, here] = dt.astype(BF)
                prod = dt * turn(kept_refs[c][b * half : (b + 1) * half, :])
                for h in range(heads):
                    inner_ref[h : h + 1, here] = jnp.sum(
                        prod[h * size : (h + 1) * size, :], axis=0, keepdims=True
                    )

        def one(i, carry):
            at = pl.ds(pl.multiple_of(i * step, step), step)
            qt = qt_ref[:, at]
            dot_t = dot_ref[:, at]
            q = q_ref[at, :]
            do = do_ref[at, :]

            def scores(h):
                s_ref[h % 2] = dot(k_ref[...], head_rows(qt, h, size))
                g_ref[h % 2] = dot(v_ref[...], head_rows(dot_t, h, size))

            scores(0)
            for h in range(heads):
                if h + 1 < heads:
                    scores(h + 1)
                now = h % 2
                cols = slice(h * step, (h + 1) * step)
                lse = lse_ref[h : h + 1, at]
                inner = inner_ref[h : h + 1, at]
                for r in range(0, seq, chunk):
                    p = jnp.exp(s_ref[now, r : r + chunk, :] - lse)
                    ds = p * (g_ref[now, r : r + chunk, :] - inner)
                    p_ref[r : r + chunk, cols] = p.astype(BF)
                    ds_ref[r : r + chunk, cols] = ds.astype(BF)
                rows = slice(h * size, (h + 1) * size)
                dqt_ref[rows, at] = dot(kt_ref[rows, :], ds_ref[:, cols]) * score
            dv = dot(p_ref[...], jnp.concatenate([head_cols(do, h, size) for h in range(heads)], 0))
            dk = dot(ds_ref[...], jnp.concatenate([head_cols(q, h, size) for h in range(heads)], 0))

            @pl.when(i == 0)
            def _():
                dv_ref[...] = dv
                dk_ref[...] = dk

            @pl.when(i > 0)
            def _():
                dv_ref[...] += dv
                dk_ref[...] += dk

            return carry

        lax.fori_loop(0, seq // step, one, 0)
        for c in range(chips):
            rows = slice(c * span, (c + 1) * span)
            out = dqkv_refs[c]
            out[:, :width] = dqt_ref[:, rows].T.astype(BF)
            out[:, width : 2 * width] = dk_ref[rows, :].astype(BF)
            out[:, 2 * width :] = dv_ref[rows, :].astype(BF)
            sums = jnp.sum(out[...].astype(F32), axis=0, keepdims=True)
            if c == 0:
                sum_ref[...] = sums
            else:
                sum_ref[...] += sums
            w = w_ref[:, : 3 * width]
            same_refs[c][...] = dot_bt(out[:half, :], w).astype(BF)
            other_ref[c * half : (c + 1) * half, :] = dot_bt(out[half:, :], w).astype(BF)

    flat = [g for pair in datt for g in pair]
    out_shape = (
        [pltpu.HBM((span, 3 * width), BF)] * chips
        + [pltpu.HBM((half, model), BF)] * chips
        + [sds((seq // 2, model), BF), sds((1, 3 * width), F32)]
    )
    operands = (*map(late, (*packed, *heads_kept)), lse, *flat, late(weight))
    out = pl.pallas_call(
        body,
        grid=(1,),
        in_specs=[whole(a.shape) for a in operands],
        out_specs=[whole(a.shape) for a in out_shape],
        out_shape=out_shape,
        scratch_shapes=[
            pltpu.VMEM((seq, width), BF),
            pltpu.VMEM((seq, width), BF),
            pltpu.VMEM((width, seq), BF),
            pltpu.VMEM((width, seq), BF),
            pltpu.VMEM((seq, width), BF),
            pltpu.VMEM((seq, width), BF),
            pltpu.VMEM((width, seq), BF),
            pltpu.VMEM((heads, seq), F32),
            pltpu.VMEM((2, seq, step), F32),
            pltpu.VMEM((2, seq, step), F32),
            pltpu.VMEM((seq, heads * step), BF),
            pltpu.VMEM((seq, heads * step), BF),
            pltpu.VMEM((seq, width), F32),
            pltpu.VMEM((seq, width), F32),
            pltpu.VMEM((width, seq), F32),
        ],
        compiler_params=params(26, 1),
        cost_estimate=cost(15),
        name="attention_back",
    )(*operands)
    return out[:chips], out[chips : 2 * chips], out[2 * chips], out[2 * chips + 1]


def gelu_both(x):
    away = jnp.abs(x)
    t = 1.0 / (1.0 + (0.3275911 * 0.5**0.5) * away)
    bell = jnp.exp(-0.5 * (x * x))
    poly = t * (
        0.127414796
        + t * (-0.142248368 + t * (0.7107068705 + t * (-0.7265760135 + t * 0.5307027145)))
    )
    tail = poly * bell
    phi = jnp.where(x >= 0, 1.0 - tail, tail)
    return x * phi, phi + x * (bell * 0.3989422804014327)


def mlp_call(body, pairs, extra, weight, bias, outs, parts, scratch, name):
    rows, model = pairs[0].shape
    units = weight.shape[1] // 2
    step = min(256, units)
    blocks = units // step
    cols = lambda j: (0, j)
    in_specs = [whole((rows, model)) for _ in pairs]
    in_specs += [pl.BlockSpec((2 * rows, step), cols) for _ in extra]
    in_specs += [
        pl.BlockSpec((model, step), cols),
        pl.BlockSpec((model, step), lambda j: (0, blocks + j)),
        pl.BlockSpec((1, step), cols),
    ]
    out_specs = [pl.BlockSpec((2 * rows, step), cols) for _ in outs]
    out_specs += [pl.BlockSpec((1, step), cols)]
    out_specs += [whole((rows, model))] * (2 * parts)
    out_shape = [pltpu.HBM((2 * rows, units), d) for d in outs] + [sds((1, units), F32)]
    out_shape += [sds((rows, model), BF)] * (2 * parts)
    count = len(pairs) // 2
    return pl.pallas_call(
        body,
        grid=(blocks,),
        in_specs=in_specs,
        out_specs=out_specs,
        out_shape=out_shape,
        scratch_shapes=[pltpu.VMEM((2 * rows, model), F32)] * parts
        + [pltpu.VMEM((2 * rows, step), F32)] * scratch,
        compiler_params=params(8 + 5 * parts, 1),
        cost_estimate=cost(0.5),
        name=name,
    )(*pairs, *map(late, extra), weight, weight, bias)


def clear(*refs):
    @pl.when(pl.program_id(0) == 0)
    def _():
        for ref in refs:
            ref[...] = jnp.zeros_like(ref)


def finish(acc, low, high):
    rows = low.shape[0]

    @pl.when(pl.program_id(0) == pl.num_programs(0) - 1)
    def _():
        low[...] = acc[:rows, :].astype(BF)
        high[...] = acc[rows:, :].astype(BF)


CHUNK = 32


def mlp_forward(pair, weight, bias):
    rows = pair[0].shape[0]

    def body(a, b, w1_ref, w2_ref, bias_ref, act_ref, slope_ref, sum_ref, lo, hi, acc, pre):
        clear(acc, sum_ref)
        shift = bias_ref[...]
        for i, x in enumerate((a, b)):
            pre[i * rows : (i + 1) * rows, :] = dot(x[...], w1_ref[...])
        for i in range(2):
            at = slice(i * rows, (i + 1) * rows)
            for r in range(i * rows, (i + 1) * rows, CHUNK):
                act, slope = gelu_both(pre[r : r + CHUNK, :] + shift)
                act_ref[r : r + CHUNK, :] = act.astype(BF)
                slope_ref[r : r + CHUNK, :] = slope.astype(BF)
            acc[at, :] += dot_bt(act_ref[at, :], w2_ref[...])
        finish(acc, lo, hi)

    act, slope, _, lo, hi = mlp_call(body, pair, [], weight, bias, [BF, BF], 1, 1, "mlp_forward")
    return act, slope, lo, hi


def mlp_backward(pair, slope, weight, bias):
    rows = pair[0].shape[0]

    def body(a, b, slope_ref, w1_ref, w2_ref, bias_ref, dpre_ref, sum_ref, lo, hi, acc, pre):
        clear(acc)
        for i, g in enumerate((a, b)):
            pre[i * rows : (i + 1) * rows, :] = dot(g[...], w2_ref[...])
        sums = jnp.zeros((8, bias_ref.shape[1]), F32)
        for i in range(2):
            at = slice(i * rows, (i + 1) * rows)
            for r in range(i * rows, (i + 1) * rows, CHUNK):
                d = pre[r : r + CHUNK, :] * slope_ref[r : r + CHUNK, :].astype(F32)
                d = d.astype(BF)
                dpre_ref[r : r + CHUNK, :] = d
                sums = sums + fold(d.astype(F32), jnp.sum)
            acc[at, :] += dot_bt(dpre_ref[at, :], w1_ref[...])
        sum_ref[...] = jnp.sum(sums, axis=0, keepdims=True)
        finish(acc, lo, hi)

    dpre, sums, lo, hi = mlp_call(
        body, pair, [slope], weight, bias, [BF], 1, 1, "mlp_backward"
    )
    return dpre, sums, lo, hi


def mlp_both(pair, grads, weight, bias):
    rows = pair[0].shape[0]

    def body(
        a, b, c, d, w1_ref, w2_ref, bias_ref, act_ref, dpre_ref, sum_ref,
        lo, hi, blo, bhi, acc, back, pre, grad,
    ):
        clear(acc, back)
        shift = bias_ref[...]
        for i, (x, g) in enumerate(((a, c), (b, d))):
            at = slice(i * rows, (i + 1) * rows)
            pre[at, :] = dot(x[...], w1_ref[...])
            grad[at, :] = dot(g[...], w2_ref[...])
        sums = jnp.zeros((8, bias_ref.shape[1]), F32)
        for i in range(2):
            at = slice(i * rows, (i + 1) * rows)
            for r in range(i * rows, (i + 1) * rows, CHUNK):
                act, slope = gelu_both(pre[r : r + CHUNK, :] + shift)
                act_ref[r : r + CHUNK, :] = act.astype(BF)
                dpre = (grad[r : r + CHUNK, :] * slope).astype(BF)
                dpre_ref[r : r + CHUNK, :] = dpre
                sums = sums + fold(dpre.astype(F32), jnp.sum)
            back[at, :] += dot_bt(dpre_ref[at, :], w1_ref[...])
            acc[at, :] += dot_bt(act_ref[at, :], w2_ref[...])
        sum_ref[...] = jnp.sum(sums, axis=0, keepdims=True)
        finish(acc, lo, hi)
        finish(back, blo, bhi)

    act, dpre, sums, lo, hi, blo, bhi = mlp_call(
        body, [*pair, *grads], [], weight, bias, [BF, BF], 2, 2, "mlp_both"
    )
    return act, dpre, sums, lo, hi, blo, bhi


def weight_grads(products, dp, side, name, halves=True, heads=0):
    model = products[0][0][0].shape[1]
    step = model // dp
    half = step // 2
    cut = 2 if halves else 1
    sizes = [(len(left), len(right), right[0].shape[1]) for left, right in products]
    cols = sum(n for _, _, n in sizes)

    def body(side_ref, *refs):
        acc_ref = refs[-1]
        mine, other = refs[-3:-1] if halves else (refs[-2], None)
        at = base = 0
        for many, few, n in sizes:
            lefts, rights = refs[at : at + many], refs[at + many : at + many + few]
            at += many + few
            ratio = many // few
            acc = None
            for i in range(many):
                size = lefts[i].shape[0]
                here = slice((i % ratio) * size, (i % ratio + 1) * size)
                term = dot_at(lefts[i][...], rights[i // ratio][here, :])
                acc = term if acc is None else acc + term
            if halves:
                acc_ref[:, base : base + n] = acc
            elif heads and not base:
                size = n // (3 * heads)
                for k in range(3 * heads):
                    head, kind = k // 3, k % 3
                    at_k = (kind * heads + head) * size
                    mine[:, k * size : (k + 1) * size] = acc[:, at_k : at_k + size].astype(BF)
            else:
                mine[:, base : base + n] = acc.astype(BF)
            base += n
        if not halves:
            return
        low = pl.multiple_of(side_ref[0] * half, half)
        high = pl.multiple_of((1 - side_ref[0]) * half, half)
        mine[...] = acc_ref[pl.ds(low, half), :].astype(BF)
        other[...] = acc_ref[pl.ds(high, half), :].astype(BF)

    specs, operands = [pl.BlockSpec(memory_space=pltpu.SMEM)], [side.reshape(1)]
    for left, right in products:
        specs += [pl.BlockSpec((a.shape[0], step), lambda i: (0, i)) for a in left]
        specs += [whole(b.shape) for b in right]
        operands += [*left, *right]
    return pl.pallas_call(
        body,
        grid=(dp,),
        in_specs=specs,
        out_specs=[pl.BlockSpec((step // cut, cols), lambda i: (i, 0))] * cut,
        out_shape=[sds((model // cut, cols), BF)] * cut,
        scratch_shapes=[pltpu.VMEM((step, cols), F32)],
        compiler_params=params(14, 1),
        cost_estimate=cost(5),
        name=name,
    )(*operands)


def pieces(chunks):
    return [p for pair in chunks for p in pair]


def shards(
    tokens, cotangent, ln1_gain, ln1_bias, w_qkv, qv_bias, w_out, out_bias, scale_attn,
    ln2_gain, ln2_bias, w_fc1, fc1_bias, w_fc2, fc2_bias, scale_mlp,
):
    side = lax.axis_index("section")
    first = side == 0
    dp = lax.axis_size("dp")
    here = lax.axis_index("dp")
    chips = lax.axis_size("tensor") // 2
    rows, model = tokens.shape[2:]
    heads = qv_bias.shape[1]
    size = qv_bias.shape[2] * dp // 2
    width = heads * size
    units = w_fc1.shape[2]
    part = model // dp

    x0 = lax.dynamic_index_in_dim(tokens, side, 0, keepdims=False).reshape(rows, model)
    grad_top = lax.dynamic_index_in_dim(cotangent, side, 0, keepdims=False).reshape(rows, model)

    vectors = (ln1_gain, ln1_bias, out_bias, scale_attn, ln2_gain, ln2_bias, fc2_bias, scale_mlp)
    packed = jnp.concatenate(
        [v.reshape(-1) for v in vectors] + [fc1_bias.reshape(-1), qv_bias.reshape(-1)]
    )
    own_qkv = w_qkv.reshape(part, heads, 3, size).swapaxes(1, 2).reshape(part, 3 * width)
    own_att = jnp.concatenate([own_qkv, w_out[0].T], axis=1)
    give_att = half_of(own_att, 1 - side)
    came_att = swap_section(give_att)
    came_small = swap_section(tie(packed, give_att))
    both_small = jnp.concatenate(
        [jnp.where(first, packed, came_small), jnp.where(first, came_small, packed)]
    )
    cols = 4 * width
    tail = -(-both_small.size // (16 * cols)) * 16
    both_small = jnp.pad(both_small, (0, tail * cols - both_small.size)).reshape(tail, cols)
    mine_att = half_of(own_att, side)
    ring_att0 = jnp.concatenate([jnp.where(first, mine_att, came_att), both_small])
    ring_att1 = jnp.where(first, came_att, mine_att)
    hops_att0 = direct(ring_att0)
    own_ff = jnp.concatenate([w_fc1[0], w_fc2[0].T], axis=1)
    rest_att = swap_section(tie(mine_att, ring_att0))
    came_ff = swap_section(tie(half_of(own_ff, 1 - side), ring_att0))
    mine_ff = half_of(own_ff, side)
    ring_ff0 = jnp.where(first, mine_ff, came_ff)
    ring_ff1 = jnp.where(first, came_ff, mine_ff)

    def other_half(own, rest):
        left = half_of(own, 1 - side)
        return jnp.where(first, left, rest), jnp.where(first, rest, left)


    backs = [swap_section(v) for v in hops_att0]
    back = [ring_att0, *hops_att0]
    back[2] = tie(back[2], backs[-1])
    flat = in_order([v[-tail:] for v in back])
    flat = flat.reshape(dp, -1)[:, : 2 * packed.size].reshape(dp, 2, -1).astype(F32)
    cut = 8 * part
    vecs = flat[:, :, :cut].reshape(dp, 2, 8, part).transpose(1, 2, 0, 3).reshape(2, 8, model)
    vecs = (vecs[0], vecs[1])
    bias_fc1 = flat[:, :, cut : cut + units // dp].swapaxes(0, 1).reshape(2, 1, units)
    qv = flat[:, :, cut + units // dp :].reshape(dp, 2, heads, -1).transpose(1, 2, 0, 3)
    qv = qv.reshape(2, heads, 2, size)
    bias_qkv = jnp.stack([qv[:, :, 0], jnp.zeros_like(qv[:, :, 0]), qv[:, :, 1]], axis=1)
    bias_qkv = bias_qkv.reshape(2, 1, 3 * width)

    norm1 = norm_first(tie(x0, came_ff), vecs[0])
    rest_ff = swap_section(tie(mine_ff, norm1))
    rest_att0, rest_att1 = other_half(own_att, rest_att)
    rest_ff0, rest_ff1 = other_half(own_ff, rest_ff)
    att1 = Ring(ring_att1)
    att0 = assemble([(tie(ring_att0, norm1), rest_att0), *zip(hops_att0, backs)], model)
    ff0, ff1 = Ring(ring_ff0), Ring(ring_ff1)
    hop_ff0 = ff0.hop(norm1)

    def projection(weight, s):
        return lambda pair: project_qkv(pair, weight, bias_qkv[s])

    chunks0, qkv0 = gather_tokens(norm1, projection(att0, 0), [rest_ff, *hop_ff0])
    beside = [*ff0.hop(), *ff0.back()]
    kept0, lse0, sames, others = attention(qkv0, att0, size)
    terms, _ = scatter_tokens(
        sames,
        tie(others, *beside),
        beside=lambda gate: [*ff0.hop(gate), *ff0.back(gate)],
    )
    attended0, residual0, norm2 = after_attention(x0, terms, vecs[0])
    ff0.back()
    beside = [*att1.hop(norm2), *att1.hop()]
    w_ff0 = assemble([(ring_ff0, rest_ff0), *zip(ff0.hops, ff0.backs)], model)
    second0, mlp0 = gather_tokens(
        norm2, lambda pair: mlp_forward(pair, w_ff0, bias_fc1[0]), beside
    )
    act0, slope0, sames, others = zip(*mlp0)
    beside = [*att1.hop(second0[-1][0]), *att1.back(second0[-1][0])]
    terms, _ = scatter_tokens(
        sames,
        [others[0], *[tie(v, *beside) for v in others[1:]]],
        beside=lambda gate: [*ff1.hop(gate), *att1.back(gate), *att1.back(gate)],
    )
    mlp_out0, y0, norm1 = after_mlp(residual0, terms, vecs[0], vecs[1])

    w_att1 = assemble([(ring_att1, rest_att1), *zip(att1.hops, att1.backs)], model)
    low1, sums_fc2_1 = start_back(grad_top, vecs[1])
    beside = [*ff1.hop(norm1), *ff1.back(norm1)]
    chunks1, qkv1 = gather_tokens(norm1, projection(w_att1, 1), beside)
    gate = chunks1[-1][0]
    came = [from_chip(tie(low1, gate), step) for step in range(1, chips)]
    beside = [*came, *ff1.hop(gate), *ff1.back(gate)]
    kept1, lse1, sames, others = attention(qkv1, w_att1, size)
    others = tie(others, *beside)
    grads1 = [(low1, core_swap(low1))] + [(v, core_swap(tie(v, lse1))) for v in came]
    terms, _ = scatter_tokens(
        sames, others, beside=lambda gate: [*ff1.back(gate), *pieces(grads1)]
    )
    attended1, residual1, norm2 = after_attention(y0, terms, vecs[1])
    w_ff1 = assemble([(ring_ff1, rest_ff1), *zip(ff1.hops, ff1.backs)], model)
    spare = list(grads1)
    second1, mlp1 = gather_tokens(
        norm2, lambda pair: mlp_both(pair, spare.pop(0), w_ff1, bias_fc1[1])
    )
    act1, dpre1, sums_fc1_1, sames_y1, others_y1, sames, others = zip(*mlp1)

    def grad_ff(second, dpre, grads, act):
        return lambda after: weight_grads(
            [
                (pieces(second), [late(tie(dpre[0], after)), *map(late, dpre[1:])]),
                (pieces(grads), [late(a) for a in act]),
            ],
            dp,
            side,
            "grad_ff",
        )

    def grad_att(chunks, dqkv, datt, kept):
        return lambda after: weight_grads(
            [
                (pieces(chunks), [late(tie(dqkv[0], after)), *map(late, dqkv[1:])]),
                (pieces(datt), [late(a) for a in kept]),
            ],
            dp,
            side,
            "grad_att",
            False,
            heads,
        )[0]

    old = [tuple(map(late, pair)) for pair in grads1]
    terms, g = scatter_tokens(sames, others, grad_ff(second1, dpre1, old, act1))
    sum_ff1 = RingSum((0, 1), *g)
    dres1, low, sums1 = back_second(grad_top, residual1, attended1, terms, vecs[1])
    came_y0 = lax.ppermute(tie(y0, low), "section", [(1, 0)])
    datt, _ = gather_tokens(low, lambda pair: pair[0], sum_ff1.step())
    sums_y1, local_y1 = core_sums(sames_y1, [tie(v, low) for v in others_y1])
    terms_y1 = send_sums([tie(v, datt[-1][0]) for v in sums_y1])
    beside = [came_y0, *terms_y1, *sum_ff1.step(low)]
    dqkv, sames, others, qkv_sums1 = attention_back(qkv1, kept1, lse1, datt, w_att1, size)
    old = [tuple(map(late, pair)) for pair in chunks1]
    terms, g = scatter_tokens(
        sames, tie(others, *beside), grad_att(old, dqkv, datt, kept1), sum_ff1.step
    )
    sum_att1 = RingSum((0, 1), g)
    sum_att1.step()
    dx1, low0, edge1 = back_first(dres1, late(y0), terms, vecs[1], late(mlp_out0), vecs[0])

    y1, sums_sc_1 = last_output(
        residual1, [tie(sames_y1[0], low0), *terms_y1, local_y1], grad_top, vecs[1]
    )

    slopes = list(slope0)
    grads0, mlp_back0 = gather_tokens(
        low0,
        lambda pair: mlp_backward(pair, slopes.pop(0), w_ff0, bias_fc1[0]),
        [y1, *sum_ff1.step(low0)],
    )
    dpre0, sums_fc1_0, sames, others = zip(*mlp_back0)
    hop_att1 = sum_att1.step(grads0[-1][0])
    old = [tuple(map(late, pair)) for pair in second0]
    terms, g = scatter_tokens(
        sames,
        others,
        grad_ff(old, dpre0, grads0, act0),
        lambda gate: [*sum_ff1.step(gate), *hop_att1],
    )
    sum_ff0 = RingSum((1, 0), *g)
    dres0, low, sums0 = back_second(
        dx1, late(residual0), late(attended0), terms, vecs[0]
    )
    beside = [*sum_att1.step(low), *sum_ff0.step(low)]
    datt, _ = gather_tokens(low, lambda pair: pair[0], beside)
    beside = [*sum_att1.step(low), *sum_ff0.step(low)]
    dqkv, sames, others, qkv_sums0 = attention_back(qkv0, kept0, lse0, datt, att0, size)
    old = [tuple(map(late, pair)) for pair in chunks0]
    others = tie(others, *beside)
    beside = sum_ff0.step(others)
    terms, g = scatter_tokens(
        sames, others, grad_att(old, dqkv, datt, kept0), lambda gate: beside
    )
    step_ff0 = sum_ff0.step(terms[1])
    sum_att0 = RingSum((1, 0), g)
    sum_att0.step()
    going = sum_att0.step()
    terms = [late(terms[0]), *terms[1:-1], late(terms[-1])]
    dx0, edge0 = back_first(late(dres0), late(x0), terms, vecs[0])
    came_dx0 = lax.ppermute(dx0, "section", [(1, 0)])
    second_hop = sum_att0.step(dx0)
    came_y1 = lax.ppermute(tie(y1, sum_att0.sent), "section", [(0, 1)])
    step_att1 = sum_att1.step(dx0)
    third_hop = sum_att0.step()
    sent = sum_att0.sent
    last_ff0 = sum_ff0.step()
    sum_att0.step()
    came_dx1 = lax.ppermute(tie(dx1, sent), "section", [(0, 1)])

    def both(low, high, came_low, came_high):
        mine = jnp.where(first, low, high)
        came = jnp.where(first, came_low, came_high)
        return jnp.stack([jnp.where(first, mine, came), jnp.where(first, came, mine)])[None, :, None]

    block_out = both(y0, y1, came_y0, came_y1)
    input_grads = both(dx0, dx1, came_dx0, came_dx1)
    sum_att0.came = tie(sum_att0.came, block_out, input_grads)

    def by_unit(qkv_sums, unit_sums):
        q = qkv_sums[:, :width].reshape(heads, 1, size)
        v = qkv_sums[:, 2 * width :].reshape(heads, 1, size)
        bias = jnp.concatenate([q, v], 1).reshape(heads, dp, -1).swapaxes(0, 1).reshape(dp, -1)
        return jnp.concatenate([bias, unit_sums.reshape(dp, -1)], axis=1)

    unit0 = by_unit(tie(qkv_sums0, dx0), sum(sums_fc1_0))
    unit1 = by_unit(tie(qkv_sums1, dx0), sum(sums_fc1_1))
    vec = jnp.concatenate(
        [edge0[:2], sums0[:4], edge1[2:4], edge1[:2], sums1[:4], sums_sc_1[:1], sums_fc2_1[:1]]
    )
    vec = tie(vec, *going, *step_ff0)
    vec = vec + core_swap(vec)
    vec = tie(sum([from_chip(vec, step) for step in range(1, chips)], vec), *second_hop, came_y1)
    vec = tie(vec, sent, *last_ff0)
    vec = vec.reshape(2, 8, dp, part).swapaxes(1, 2).reshape(2, dp, 8 * part)
    vec0 = jnp.concatenate([vec[0], unit0], axis=1)
    vec1 = jnp.concatenate([vec[1], unit1], axis=1)
    own = jnp.where(first, vec0, vec1) + swap_section(jnp.where(first, vec1, vec0))
    own = tie(own, *step_att1, came_dx1, sum_att0.own)
    vec = lax.dynamic_slice_in_dim(own, here, 1, 0)
    for step in range(1, dp):
        pairs = [(i, (i + step) % dp) for i in range(dp)]
        other = lax.dynamic_slice_in_dim(own, lax.rem(here + step, dp), 1, 0)
        vec = vec + lax.ppermute(other, "dp", pairs)
    cut = 8 * part + heads * (2 * size // dp)
    bias_grad = vec[:, 8 * part : cut].reshape(1, heads, -1)
    fc1_grad = vec[:, cut:].reshape(1, 1, -1)
    g_ln1, b_ln1, g_ln2, b_ln2, g_sc_attn, g_out_bias, g_sc_mlp, g_fc2_bias = (
        vec[:, i * part : (i + 1) * part] for i in range(8)
    )

    def owned(low, high):
        top = jnp.where(first, low.own, high.came.astype(F32))
        bottom = jnp.where(first, low.came.astype(F32), high.own)
        return jnp.concatenate([top, bottom], 0)

    g_ff = owned(sum_ff0, sum_ff1)
    g_att = jnp.where(
        first,
        sum_att0.own + sum_att0.came.astype(F32),
        sum_att1.own + sum_att1.came.astype(F32),
    )
    g_qkv = g_att[None, :, : 3 * width]
    g_out = g_att[:, 3 * width :].T[None]
    g_fc1 = g_ff[:, :units][None]
    g_fc2 = g_ff[:, units:].T[None]
    return (
        block_out, input_grads, g_ln1, b_ln1, g_qkv, bias_grad, g_out, g_out_bias, g_sc_attn,
        g_ln2, b_ln2, g_fc1, fc1_grad, g_fc2, g_fc2_bias, g_sc_mlp,
    )


def solution(mesh):
    vec = P("section", "dp")
    by_row = P("section", "dp", "tensor")
    by_unit = P("section", "tensor", "dp")
    data = P(None, "dp", "tensor", None)
    split = P("section", None, "dp", "tensor", None)
    given = (
        vec, vec, by_row, by_unit, by_unit, vec, vec, vec, vec, by_row, by_unit, by_unit, vec, vec,
    )
    return jax.shard_map(
        shards,
        mesh=mesh,
        in_specs=(data, data) + given,
        out_specs=(split, split) + given,
        check_vma=False,
    )
```

```python
from functools import partial

import jax
import jax.numpy as jnp
from jax import lax
from jax.experimental import pallas as pl
from jax.experimental.pallas import tpu as pltpu
from jax.sharding import PartitionSpec as P

EPSILON = 1e-06
BF = jnp.bfloat16
F32 = jnp.float32
MIB = 1 << 20

LN1_G, LN1_B, OUT_B, SC_ATTN, LN2_G, LN2_B, FC2_B, SC_MLP = range(8)


def dot(a, b):
    return lax.dot_general(a, b, (((1,), (0,)), ((), ())), preferred_element_type=F32)


def dot_bt(a, b):
    return lax.dot_general(a, b, (((1,), (1,)), ((), ())), preferred_element_type=F32)


def dot_at(a, b):
    return lax.dot_general(a, b, (((0,), (0,)), ((), ())), preferred_element_type=F32)


def turn(v):
    return v.astype(F32).T


def params(limit, grid=0):
    return pltpu.CompilerParams(
        vmem_limit_bytes=limit * MIB,
        dimension_semantics=("arbitrary",) * grid if grid else None,
    )


def late(v):
    return pltpu.with_memory_space_constraint(v, pltpu.HBM)


def whole(shape):
    return pl.BlockSpec(shape, lambda i: (0, 0), pipeline_mode=pl.Buffered(1))


def cost(micros):
    return pl.CostEstimate(flops=int(micros * 1.15e9), bytes_accessed=0, transcendentals=0)


def sds(shape, dtype):
    return jax.ShapeDtypeStruct(shape, dtype)


def core_swap(v):
    count = lax.axis_size("tensor")
    return lax.ppermute(v, "tensor", [(i, i ^ 1) for i in range(count)])


def from_chip(v, step):
    count = lax.axis_size("tensor")
    chips = count // 2
    pairs = [(((i // 2 + step) % chips) * 2 + i % 2, i) for i in range(count)]
    return lax.ppermute(v, "tensor", pairs)


def tie(v, *after):
    if not after:
        return v
    return lax.optimization_barrier((v, *after))[0]


def tie_all(vs, *after):
    return lax.optimization_barrier((*vs, *after))[: len(vs)]


def gather_tokens(own, work, beside=()):
    chips = lax.axis_size("tensor") // 2
    came = [from_chip(own, step) for step in range(1, chips)]
    chunks = [(own, core_swap(own))]
    results = [work(chunks[0])]
    for same in came:
        same = tie(same, results[-1], *beside)
        chunks.append((same, core_swap(same)))
        results.append(work(chunks[-1]))
    return chunks, results


def core_sums(sames, others):
    chips, rows = len(sames), sames[0].shape[0]
    if isinstance(others, (list, tuple)):
        came = [core_swap(v) for v in others[1:]]
        local = core_swap(tie(others[0], came[-1]))
    else:
        local = core_swap(others)
        came = [local[c * rows : (c + 1) * rows] for c in range(1, chips)]
    sums = [(a.astype(F32) + b.astype(F32)).astype(BF) for a, b in zip(sames[1:], came)]
    return sums, local


def send_sums(sums):
    chips = len(sums) + 1
    return [from_chip(both, chips - step) for step, both in enumerate(sums, 1)]


def scatter_tokens(sames, others, work=None, beside=None):
    sums, local = core_sums(sames, others)
    terms = send_sums(sums)
    made = work(sums[-1]) if work else local
    more = beside(sums[-1]) if beside else ()
    terms = [tie(t, made, local, *more) for t in terms]
    return [sames[0], *terms, local], made


def swap_section(v):
    return lax.ppermute(v, "section", [(0, 1), (1, 0)])


def assemble(shards, rows):
    count = len(shards)
    cut = len(shards[0])
    size, cols = rows // (count * cut), shards[0][0].shape[1]
    place = jnp.stack([lax.axis_index("dp"), lax.axis_index("section")])

    def body(place_ref, *refs):
        out_ref, sems = refs[count * cut :]
        z, x = place_ref[0], place_ref[1]
        started = []
        for k in range(count):
            base = lax.rem(z + (count - k), count) * (cut * size)
            for i, at in enumerate([base] if cut == 1 else [base + x * size, base + (1 - x) * size]):
                copy = pltpu.make_async_copy(
                    refs[k * cut + i].at[pl.ds(0, size), :],
                    out_ref.at[pl.ds(pl.multiple_of(at, size), size), :],
                    sems.at[k * cut + i],
                )
                copy.start()
                started.append(copy)
        for copy in started:
            copy.wait()

    hbm = pl.BlockSpec(memory_space=pl.ANY)
    return pl.pallas_call(
        body,
        in_specs=[pl.BlockSpec(memory_space=pltpu.SMEM)] + [hbm] * (count * cut),
        out_specs=pl.BlockSpec(memory_space=pltpu.VMEM),
        out_shape=sds((rows, cols), shards[0][0].dtype),
        scratch_shapes=[pltpu.SemaphoreType.DMA((count * cut,))],
        compiler_params=params(6),
        cost_estimate=cost(2),
        name="assemble",
    )(place, *[late(v) for shard in shards for v in shard])


def half_of(v, which):
    half = v.shape[0] // 2
    return lax.dynamic_slice_in_dim(v, which * half, half, 0)


def direct(own):
    count = lax.axis_size("dp")
    return [
        lax.ppermute(own, "dp", [(i, (i + step) % count) for i in range(count)])
        for step in range(1, count)
    ]


def third(values, index):
    cuts = [-(-len(values) * i // 3) for i in range(4)]
    return values[cuts[index] : cuts[index + 1]]


class Ring:
    def __init__(self, own):
        self.last, self.hops, self.backs, self.at, self.back_at = own, [], [], 0, 0

    def hop(self, *gate):
        count = lax.axis_size("dp")
        pairs = [(i, (i + 1) % count) for i in range(count)]
        new = []
        for i in range(len(third(range(count - 1), self.at))):
            self.last = lax.ppermute(tie(self.last, *gate) if i == 0 else self.last, "dp", pairs)
            new.append(self.last)
        self.hops += new
        self.at += 1
        return new

    def back(self, *gate):
        count = lax.axis_size("dp")
        which = third(range(count - 1), self.back_at)
        new = [swap_section(tie(self.hops[i], *gate)) for i in which]
        self.backs += new
        self.back_at += 1
        return new


def in_order(back):
    count = len(back)
    ahead = [back[0], *back[:0:-1]]
    twice = jnp.stack(ahead + ahead)
    return lax.dynamic_slice_in_dim(twice, count - lax.axis_index("dp"), count, 0)


def dp_rows(v, back):
    dp = lax.axis_size("dp")
    part = v.shape[0] // dp
    place = lax.rem(lax.axis_index("dp") + (dp - back), dp)
    return lax.dynamic_slice_in_dim(v, place * part, part, 0)


class RingSum:
    def __init__(self, pair, mine, other=None):
        self.mine, self.other, self.pair = mine, other, pair
        self.terms, self.at, self.done = [], 0, 0

    def total(self, gate=()):
        first = tie(self.terms[0], *gate)
        return sum(t.astype(F32) for t in [first, *self.terms[1:]])

    def one(self, gate):
        dp = lax.axis_size("dp")
        self.done += 1
        new = []
        if self.terms:
            pairs = [(i, (i + 1) % dp) for i in range(dp)]
            self.sent = self.total(gate).astype(BF)
            new.append(lax.ppermute(self.sent, "dp", pairs))
        if self.other is not None:
            new.append(swap_section(tie(dp_rows(self.other, self.done), *gate)))
        self.terms = [*new, dp_rows(self.mine, self.done)]
        return new

    def step(self, *gate):
        self.at += 1
        if self.at == 5:
            self.own = self.total(gate)
            self.came = lax.ppermute(self.own.astype(BF), "section", [self.pair])
            return [self.came]
        count = 1 if self.at == 1 else len(third(range(lax.axis_size("dp") - 1), self.at - 2))
        return [v for i in range(count) for v in self.one(gate if i == 0 else ())]


def standardize(v):
    centred = v - jnp.mean(v, axis=-1, keepdims=True)
    var = jnp.mean(centred * centred, axis=-1, keepdims=True)
    scale = lax.rsqrt(var + EPSILON)
    return centred * scale, scale


def norm_of(v, vec, gain, shift):
    return (standardize(v)[0] * vec[gain : gain + 1, :] + vec[shift : shift + 1, :]).astype(BF)


def norm_back(v, grad, gain):
    xh, scale = standardize(v)
    dxh = grad * gain
    inner = jnp.mean(dxh * xh, axis=-1, keepdims=True)
    out = scale * (dxh - jnp.mean(dxh, axis=-1, keepdims=True) - xh * inner)
    return out, grad * xh


def total(refs):
    out = refs[0][...].astype(F32)
    for ref in refs[1:]:
        out = out + ref[...].astype(F32)
    return out


def fold(v, op):
    return op(v.reshape(-1, 8, v.shape[1]), axis=0)


def add_rows(ref, rows):
    for k, row in enumerate(rows):
        ref[8 * k : 8 * k + 8, :] += fold(row, jnp.sum)


def rowwise(body, row_ins, fulls, row_outs, sums, name):
    rows, width = row_ins[0].shape
    step = min(128, rows)
    some, outs = len(row_ins) + len(fulls), len(row_outs)

    def kernel(*refs):
        if not sums:
            body(*refs)
            return
        sum_ref, acc_ref = refs[some + outs :]

        @pl.when(pl.program_id(0) == 0)
        def _():
            acc_ref[...] = jnp.zeros_like(acc_ref)

        body(*refs[: some + outs], acc_ref)

        @pl.when(pl.program_id(0) == pl.num_programs(0) - 1)
        def _():
            for k in range(sums):
                sum_ref[k : k + 1, :] = jnp.sum(
                    acc_ref[8 * k : 8 * k + 8, :], axis=0, keepdims=True
                )

    out_shape = [sds((rows, width), d) for d in row_outs]
    out_shape += [sds((sums, width), F32)] if sums else []
    block = pl.BlockSpec((step, width), lambda i: (i, 0))
    return pl.pallas_call(
        kernel,
        grid=(rows // step,),
        in_specs=[block] * len(row_ins) + [whole(a.shape) for a in fulls],
        out_specs=[block] * outs + ([whole((sums, width))] if sums else []),
        out_shape=out_shape,
        scratch_shapes=[pltpu.VMEM((8 * sums, width), F32)] if sums else [],
        compiler_params=params(8, 1),
        cost_estimate=cost(2),
        name=name,
    )(*row_ins, *fulls)


def norm_first(x, vec):
    def body(x_ref, vec_ref, out_ref):
        out_ref[...] = norm_of(x_ref[...].astype(F32), vec_ref[...], LN1_G, LN1_B)

    return rowwise(body, [x], [vec], [BF], 0, "norm_first")[0]


def after_attention(x, terms, vec):
    count = len(terms)

    def body(*refs):
        x_ref, term_refs, vec_ref = refs[0], refs[1 : 1 + count], refs[1 + count]
        att_ref, res_ref, norm_ref = refs[2 + count :]
        v = vec_ref[...]
        attended = total(term_refs) + v[OUT_B : OUT_B + 1, :]
        residual = x_ref[...].astype(F32) + v[SC_ATTN : SC_ATTN + 1, :] * attended
        att_ref[...] = attended.astype(BF)
        res_ref[...] = residual
        norm_ref[...] = norm_of(residual, v, LN2_G, LN2_B)

    return rowwise(body, [x, *terms], [vec], [BF, F32, BF], 0, "after_attention")


def after_mlp(residual, terms, vec, vec_next):
    count = len(terms)

    def body(*refs):
        res_ref, term_refs = refs[0], refs[1 : 1 + count]
        vec_ref, next_ref, mlp_ref, y_ref, norm_ref = refs[1 + count :]
        v = vec_ref[...]
        mlp = total(term_refs) + v[FC2_B : FC2_B + 1, :]
        y = (res_ref[...] + v[SC_MLP : SC_MLP + 1, :] * mlp).astype(BF)
        mlp_ref[...] = mlp.astype(BF)
        y_ref[...] = y
        norm_ref[...] = norm_of(y.astype(F32), next_ref[...], LN1_G, LN1_B)

    return rowwise(body, [residual, *terms], [vec, vec_next], [BF, BF, BF], 0, "after_mlp")


def last_output(residual, terms, grad, vec):
    count = len(terms)

    def body(*refs):
        res_ref, term_refs = refs[0], refs[1 : 1 + count]
        grad_ref, vec_ref, y_ref, sum_ref = refs[1 + count :]
        v = vec_ref[...]
        mlp = total(term_refs) + v[FC2_B : FC2_B + 1, :]
        y_ref[...] = (res_ref[...] + v[SC_MLP : SC_MLP + 1, :] * mlp).astype(BF)
        add_rows(sum_ref, [grad_ref[...].astype(F32) * mlp])

    return rowwise(body, [residual, *terms, grad], [vec], [BF], 1, "last_output")


def start_back(grad, vec):
    def body(grad_ref, vec_ref, out_ref, sum_ref):
        low = (vec_ref[...][SC_MLP : SC_MLP + 1, :] * grad_ref[...].astype(F32)).astype(BF)
        out_ref[...] = low
        add_rows(sum_ref, [low.astype(F32)])

    return rowwise(body, [grad], [vec], [BF], 1, "start_back")


def back_second(grad, residual, attended, terms, vec):
    count = len(terms)

    def body(*refs):
        grad_ref, res_ref, att_ref = refs[:3]
        term_refs = refs[3 : 3 + count]
        vec_ref, dres_ref, low_ref, sum_ref = refs[3 + count :]
        v = vec_ref[...]
        dn = total(term_refs)
        back, dgain = norm_back(res_ref[...], dn, v[LN2_G : LN2_G + 1, :])
        dres = grad_ref[...].astype(F32) + back
        low = (v[SC_ATTN : SC_ATTN + 1, :] * dres).astype(BF)
        dres_ref[...] = dres
        low_ref[...] = low
        add_rows(sum_ref, [dgain, dn, dres * att_ref[...].astype(F32), low.astype(F32)])

    return rowwise(
        body, [grad, residual, attended, *terms], [vec], [F32, BF], 4, "back_second"
    )


def back_first(dres, x, terms, vec, mlp_below=None, vec_below=None):
    count = len(terms)
    below = mlp_below is not None

    def body(*refs):
        dres_ref, x_ref = refs[:2]
        term_refs = refs[2 : 2 + count]
        rest = refs[2 + count :]
        if below:
            mlp_ref, vec_ref, under_ref, dx_ref, low_ref, sum_ref = rest
        else:
            vec_ref, dx_ref, sum_ref = rest
        v = vec_ref[...]
        dn = total(term_refs)
        back, dgain = norm_back(x_ref[...].astype(F32), dn, v[LN1_G : LN1_G + 1, :])
        dx = (dres_ref[...] + back).astype(BF)
        dx_ref[...] = dx
        rows = [dgain, dn]
        if below:
            wide = dx.astype(F32)
            low = (under_ref[...][SC_MLP : SC_MLP + 1, :] * wide).astype(BF)
            low_ref[...] = low
            rows += [wide * mlp_ref[...].astype(F32), low.astype(F32)]
        add_rows(sum_ref, rows)

    row_ins = [dres, x, *terms] + ([mlp_below] if below else [])
    fulls = [vec] + ([vec_below] if below else [])
    return rowwise(body, row_ins, fulls, [BF, BF] if below else [BF], 4 if below else 2, "back_first")


def project_qkv(pair, weight, bias):
    rows, width = pair[0].shape
    cols = bias.shape[1]

    def body(a_ref, b_ref, w_ref, bias_ref, out_ref):
        w = w_ref[...]
        shift = bias_ref[...]
        out_ref[:rows, :] = (dot(a_ref[...], w) + shift).astype(BF)
        out_ref[rows:, :] = (dot(b_ref[...], w) + shift).astype(BF)

    return pl.pallas_call(
        body,
        grid=(1,),
        in_specs=[
            whole((rows, width)), whole((rows, width)), whole((width, cols)), whole((1, cols))
        ],
        out_specs=whole((2 * rows, cols)),
        out_shape=sds((2 * rows, cols), BF),
        compiler_params=params(6, 1),
        cost_estimate=cost(0.5),
        name="project_qkv",
    )(*pair, weight, bias)


def head_rows(v, head, size):
    rows = lax.broadcasted_iota(jnp.int32, v.shape, 0)
    return jnp.where(rows // size == head, v, jnp.zeros_like(v))


def head_cols(v, head, size):
    cols = lax.broadcasted_iota(jnp.int32, v.shape, 1)
    return jnp.where(cols // size == head, v, jnp.zeros_like(v))


def attention(packed, weight, size):
    chips = len(packed)
    span = packed[0].shape[0]
    half = span // 2
    width = packed[0].shape[1] // 3
    seq = chips * span
    heads = width // size
    model = weight.shape[0]
    step = min(256, seq)
    chunk = min(128, seq)
    score = size**-0.5

    def body(*refs):
        in_refs, w_ref = refs[:chips], refs[chips]
        head_refs = refs[chips + 1 : 2 * chips + 1]
        lse_ref = refs[2 * chips + 1]
        same_refs, other_ref = refs[2 * chips + 2 : 3 * chips + 2], refs[3 * chips + 2]
        k_ref, qt_ref, vt_ref, ot_ref, s_ref, p_ref = refs[3 * chips + 3 :]
        for c in range(chips):
            at = slice(c * span, (c + 1) * span)
            k_ref[at, :] = in_refs[c][:, width : 2 * width]
            qt_ref[:, at] = (turn(in_refs[c][:, :width]) * score).astype(BF)
            vt_ref[:, at] = turn(in_refs[c][:, 2 * width :]).astype(BF)

        def one(i, carry):
            at = pl.ds(pl.multiple_of(i * step, step), step)
            q = qt_ref[:, at]
            s_ref[0] = dot(k_ref[...], head_rows(q, 0, size))
            for h in range(heads):
                if h + 1 < heads:
                    s_ref[(h + 1) % 2] = dot(k_ref[...], head_rows(q, h + 1, size))
                now = h % 2
                top = fold(s_ref[now, :chunk, :], jnp.max)
                for r in range(chunk, seq, chunk):
                    top = jnp.maximum(top, fold(s_ref[now, r : r + chunk, :], jnp.max))
                top = jnp.max(top, axis=0, keepdims=True)
                norm = jnp.zeros((8, step), F32)
                for r in range(0, seq, chunk):
                    p = jnp.exp(s_ref[now, r : r + chunk, :] - top)
                    norm = norm + fold(p, jnp.sum)
                    p_ref[now, r : r + chunk, :] = p.astype(BF)
                norm = jnp.sum(norm, axis=0, keepdims=True)
                rows = slice(h * size, (h + 1) * size)
                ot_ref[rows, at] = dot(vt_ref[rows, :], p_ref[now]) / norm
                lse_ref[h : h + 1, at] = top + jnp.log(norm)
            return carry

        lax.fori_loop(0, seq // step, one, 0)
        for c in range(chips):
            at = slice(c * span, (c + 1) * span)
            o = ot_ref[:, at].T.astype(BF)
            head_refs[c][...] = o
            same_refs[c][...] = dot_bt(o[:half], w_ref[...]).astype(BF)
            other_ref[c * half : (c + 1) * half, :] = dot_bt(o[half:], w_ref[...]).astype(BF)

    out = pl.pallas_call(
        body,
        grid=(1,),
        in_specs=[whole((span, 3 * width))] * chips
        + [pl.BlockSpec((model, width), lambda i: (0, 3), pipeline_mode=pl.Buffered(1))],
        out_specs=[whole((span, width))] * chips
        + [whole((heads, seq))]
        + [whole((half, model))] * chips
        + [whole((seq // 2, model))],
        out_shape=[pltpu.HBM((span, width), BF)] * chips
        + [sds((heads, seq), F32)]
        + [sds((half, model), BF)] * chips
        + [sds((seq // 2, model), BF)],
        scratch_shapes=[
            pltpu.VMEM((seq, width), BF),
            pltpu.VMEM((width, seq), BF),
            pltpu.VMEM((width, seq), BF),
            pltpu.VMEM((width, seq), F32),
            pltpu.VMEM((2, seq, step), F32),
            pltpu.VMEM((2, seq, step), BF),
        ],
        compiler_params=params(14, 1),
        cost_estimate=cost(9),
        name="attention",
    )(*packed, weight)
    return out[:chips], out[chips], out[chips + 1 : -1], out[-1]


def attention_back(packed, heads_kept, lse, datt, weight, size):
    chips = len(packed)
    span = packed[0].shape[0]
    half = span // 2
    width = packed[0].shape[1] // 3
    seq = chips * span
    heads = width // size
    model = weight.shape[0]
    step = min(256, seq)
    chunk = min(128, seq)
    score = size**-0.5

    def body(*refs):
        at = 0

        def take(count):
            nonlocal at
            at += count
            return refs[at - count : at]

        in_refs, kept_refs = take(chips), take(chips)
        (lse_ref,) = take(1)
        datt_refs = take(2 * chips)
        (w_ref,) = take(1)
        dqkv_refs = take(chips)
        same_refs = take(chips)
        other_ref, sum_ref = take(2)
        k_ref, v_ref, kt_ref, qt_ref, q_ref, do_ref, dot_ref = take(7)
        inner_ref, s_ref, g_ref, p_ref, ds_ref, dk_ref, dv_ref, dqt_ref = take(8)
        for c in range(chips):
            rows = slice(c * span, (c + 1) * span)
            q = in_refs[c][:, :width].astype(F32) * score
            k = in_refs[c][:, width : 2 * width]
            q_ref[rows, :] = q.astype(BF)
            qt_ref[:, rows] = q.T.astype(BF)
            k_ref[rows, :] = k
            kt_ref[:, rows] = turn(k).astype(BF)
            v_ref[rows, :] = in_refs[c][:, 2 * width :]
            for b in range(2):
                d = dot(datt_refs[2 * c + b][...], w_ref[:, 3 * width :]).astype(BF)
                here = slice(c * span + b * half, c * span + (b + 1) * half)
                do_ref[here, :] = d
                dt = turn(d)
                dot_ref[:, here] = dt.astype(BF)
                prod = dt * turn(kept_refs[c][b * half : (b + 1) * half, :])
                for h in range(heads):
                    inner_ref[h : h + 1, here] = jnp.sum(
                        prod[h * size : (h + 1) * size, :], axis=0, keepdims=True
                    )

        def one(i, carry):
            at = pl.ds(pl.multiple_of(i * step, step), step)
            qt = qt_ref[:, at]
            dot_t = dot_ref[:, at]
            q = q_ref[at, :]
            do = do_ref[at, :]

            def scores(h):
                s_ref[h % 2] = dot(k_ref[...], head_rows(qt, h, size))
                g_ref[h % 2] = dot(v_ref[...], head_rows(dot_t, h, size))

            scores(0)
            for h in range(heads):
                if h + 1 < heads:
                    scores(h + 1)
                now = h % 2
                cols = slice(h * step, (h + 1) * step)
                lse = lse_ref[h : h + 1, at]
                inner = inner_ref[h : h + 1, at]
                for r in range(0, seq, chunk):
                    p = jnp.exp(s_ref[now, r : r + chunk, :] - lse)
                    ds = p * (g_ref[now, r : r + chunk, :] - inner)
                    p_ref[r : r + chunk, cols] = p.astype(BF)
                    ds_ref[r : r + chunk, cols] = ds.astype(BF)
                rows = slice(h * size, (h + 1) * size)
                dqt_ref[rows, at] = dot(kt_ref[rows, :], ds_ref[:, cols]) * score
            dv = dot(p_ref[...], jnp.concatenate([head_cols(do, h, size) for h in range(heads)], 0))
            dk = dot(ds_ref[...], jnp.concatenate([head_cols(q, h, size) for h in range(heads)], 0))

            @pl.when(i == 0)
            def _():
                dv_ref[...] = dv
                dk_ref[...] = dk

            @pl.when(i > 0)
            def _():
                dv_ref[...] += dv
                dk_ref[...] += dk

            return carry

        lax.fori_loop(0, seq // step, one, 0)
        for c in range(chips):
            rows = slice(c * span, (c + 1) * span)
            out = dqkv_refs[c]
            out[:, :width] = dqt_ref[:, rows].T.astype(BF)
            out[:, width : 2 * width] = dk_ref[rows, :].astype(BF)
            out[:, 2 * width :] = dv_ref[rows, :].astype(BF)
            sums = jnp.sum(out[...].astype(F32), axis=0, keepdims=True)
            if c == 0:
                sum_ref[...] = sums
            else:
                sum_ref[...] += sums
            w = w_ref[:, : 3 * width]
            same_refs[c][...] = dot_bt(out[:half, :], w).astype(BF)
            other_ref[c * half : (c + 1) * half, :] = dot_bt(out[half:, :], w).astype(BF)

    flat = [g for pair in datt for g in pair]
    out_shape = (
        [pltpu.HBM((span, 3 * width), BF)] * chips
        + [pltpu.HBM((half, model), BF)] * chips
        + [sds((seq // 2, model), BF), sds((1, 3 * width), F32)]
    )
    operands = (*map(late, (*packed, *heads_kept)), lse, *flat, late(weight))
    out = pl.pallas_call(
        body,
        grid=(1,),
        in_specs=[whole(a.shape) for a in operands],
        out_specs=[whole(a.shape) for a in out_shape],
        out_shape=out_shape,
        scratch_shapes=[
            pltpu.VMEM((seq, width), BF),
            pltpu.VMEM((seq, width), BF),
            pltpu.VMEM((width, seq), BF),
            pltpu.VMEM((width, seq), BF),
            pltpu.VMEM((seq, width), BF),
            pltpu.VMEM((seq, width), BF),
            pltpu.VMEM((width, seq), BF),
            pltpu.VMEM((heads, seq), F32),
            pltpu.VMEM((2, seq, step), F32),
            pltpu.VMEM((2, seq, step), F32),
            pltpu.VMEM((seq, heads * step), BF),
            pltpu.VMEM((seq, heads * step), BF),
            pltpu.VMEM((seq, width), F32),
            pltpu.VMEM((seq, width), F32),
            pltpu.VMEM((width, seq), F32),
        ],
        compiler_params=params(26, 1),
        cost_estimate=cost(15),
        name="attention_back",
    )(*operands)
    return out[:chips], out[chips : 2 * chips], out[2 * chips], out[2 * chips + 1]


def gelu_both(x):
    away = jnp.abs(x)
    t = 1.0 / (1.0 + (0.3275911 * 0.5**0.5) * away)
    bell = jnp.exp(-0.5 * (x * x))
    poly = t * (
        0.127414796
        + t * (-0.142248368 + t * (0.7107068705 + t * (-0.7265760135 + t * 0.5307027145)))
    )
    tail = poly * bell
    phi = jnp.where(x >= 0, 1.0 - tail, tail)
    return x * phi, phi + x * (bell * 0.3989422804014327)


def mlp_call(body, pairs, extra, weight, bias, outs, parts, scratch, name):
    rows, model = pairs[0].shape
    units = weight.shape[1] // 2
    step = min(256, units)
    blocks = units // step
    cols = lambda j: (0, j)
    in_specs = [whole((rows, model)) for _ in pairs]
    in_specs += [pl.BlockSpec((2 * rows, step), cols) for _ in extra]
    in_specs += [
        pl.BlockSpec((model, step), cols),
        pl.BlockSpec((model, step), lambda j: (0, blocks + j)),
        pl.BlockSpec((1, step), cols),
    ]
    out_specs = [pl.BlockSpec((2 * rows, step), cols) for _ in outs]
    out_specs += [pl.BlockSpec((1, step), cols)]
    out_specs += [whole((rows, model))] * (2 * parts)
    out_shape = [pltpu.HBM((2 * rows, units), d) for d in outs] + [sds((1, units), F32)]
    out_shape += [sds((rows, model), BF)] * (2 * parts)
    count = len(pairs) // 2
    return pl.pallas_call(
        body,
        grid=(blocks,),
        in_specs=in_specs,
        out_specs=out_specs,
        out_shape=out_shape,
        scratch_shapes=[pltpu.VMEM((2 * rows, model), F32)] * parts
        + [pltpu.VMEM((2 * rows, step), F32)] * scratch,
        compiler_params=params(8 + 5 * parts, 1),
        cost_estimate=cost(0.5),
        name=name,
    )(*pairs, *map(late, extra), weight, weight, bias)


def clear(*refs):
    @pl.when(pl.program_id(0) == 0)
    def _():
        for ref in refs:
            ref[...] = jnp.zeros_like(ref)


def finish(acc, low, high):
    rows = low.shape[0]

    @pl.when(pl.program_id(0) == pl.num_programs(0) - 1)
    def _():
        low[...] = acc[:rows, :].astype(BF)
        high[...] = acc[rows:, :].astype(BF)


CHUNK = 32


def mlp_forward(pair, weight, bias):
    rows = pair[0].shape[0]

    def body(a, b, w1_ref, w2_ref, bias_ref, act_ref, slope_ref, sum_ref, lo, hi, acc, pre):
        clear(acc, sum_ref)
        shift = bias_ref[...]
        for i, x in enumerate((a, b)):
            pre[i * rows : (i + 1) * rows, :] = dot(x[...], w1_ref[...])
        for i in range(2):
            at = slice(i * rows, (i + 1) * rows)
            for r in range(i * rows, (i + 1) * rows, CHUNK):
                act, slope = gelu_both(pre[r : r + CHUNK, :] + shift)
                act_ref[r : r + CHUNK, :] = act.astype(BF)
                slope_ref[r : r + CHUNK, :] = slope.astype(BF)
            acc[at, :] += dot_bt(act_ref[at, :], w2_ref[...])
        finish(acc, lo, hi)

    act, slope, _, lo, hi = mlp_call(body, pair, [], weight, bias, [BF, BF], 1, 1, "mlp_forward")
    return act, slope, lo, hi


def mlp_backward(pair, slope, weight, bias):
    rows = pair[0].shape[0]

    def body(a, b, slope_ref, w1_ref, w2_ref, bias_ref, dpre_ref, sum_ref, lo, hi, acc, pre):
        clear(acc)
        for i, g in enumerate((a, b)):
            pre[i * rows : (i + 1) * rows, :] = dot(g[...], w2_ref[...])
        sums = jnp.zeros((8, bias_ref.shape[1]), F32)
        for i in range(2):
            at = slice(i * rows, (i + 1) * rows)
            for r in range(i * rows, (i + 1) * rows, CHUNK):
                d = pre[r : r + CHUNK, :] * slope_ref[r : r + CHUNK, :].astype(F32)
                d = d.astype(BF)
                dpre_ref[r : r + CHUNK, :] = d
                sums = sums + fold(d.astype(F32), jnp.sum)
            acc[at, :] += dot_bt(dpre_ref[at, :], w1_ref[...])
        sum_ref[...] = jnp.sum(sums, axis=0, keepdims=True)
        finish(acc, lo, hi)

    dpre, sums, lo, hi = mlp_call(
        body, pair, [slope], weight, bias, [BF], 1, 1, "mlp_backward"
    )
    return dpre, sums, lo, hi


def mlp_both(pair, grads, weight, bias):
    rows = pair[0].shape[0]

    def body(
        a, b, c, d, w1_ref, w2_ref, bias_ref, act_ref, dpre_ref, sum_ref,
        lo, hi, blo, bhi, acc, back, pre, grad,
    ):
        clear(acc, back)
        shift = bias_ref[...]
        for i, (x, g) in enumerate(((a, c), (b, d))):
            at = slice(i * rows, (i + 1) * rows)
            pre[at, :] = dot(x[...], w1_ref[...])
            grad[at, :] = dot(g[...], w2_ref[...])
        sums = jnp.zeros((8, bias_ref.shape[1]), F32)
        for i in range(2):
            at = slice(i * rows, (i + 1) * rows)
            for r in range(i * rows, (i + 1) * rows, CHUNK):
                act, slope = gelu_both(pre[r : r + CHUNK, :] + shift)
                act_ref[r : r + CHUNK, :] = act.astype(BF)
                dpre = (grad[r : r + CHUNK, :] * slope).astype(BF)
                dpre_ref[r : r + CHUNK, :] = dpre
                sums = sums + fold(dpre.astype(F32), jnp.sum)
            back[at, :] += dot_bt(dpre_ref[at, :], w1_ref[...])
            acc[at, :] += dot_bt(act_ref[at, :], w2_ref[...])
        sum_ref[...] = jnp.sum(sums, axis=0, keepdims=True)
        finish(acc, lo, hi)
        finish(back, blo, bhi)

    act, dpre, sums, lo, hi, blo, bhi = mlp_call(
        body, [*pair, *grads], [], weight, bias, [BF, BF], 2, 2, "mlp_both"
    )
    return act, dpre, sums, lo, hi, blo, bhi


def weight_grads(products, dp, side, name, halves=True, heads=0):
    model = products[0][0][0].shape[1]
    step = model // dp
    half = step // 2
    cut = 2 if halves else 1
    sizes = [(len(left), len(right), right[0].shape[1]) for left, right in products]
    cols = sum(n for _, _, n in sizes)

    def body(side_ref, *refs):
        acc_ref = refs[-1]
        mine, other = refs[-3:-1] if halves else (refs[-2], None)
        at = base = 0
        for many, few, n in sizes:
            lefts, rights = refs[at : at + many], refs[at + many : at + many + few]
            at += many + few
            ratio = many // few
            acc = None
            for i in range(many):
                size = lefts[i].shape[0]
                here = slice((i % ratio) * size, (i % ratio + 1) * size)
                term = dot_at(lefts[i][...], rights[i // ratio][here, :])
                acc = term if acc is None else acc + term
            if halves:
                acc_ref[:, base : base + n] = acc
            elif heads and not base:
                size = n // (3 * heads)
                for k in range(3 * heads):
                    head, kind = k // 3, k % 3
                    at_k = (kind * heads + head) * size
                    mine[:, k * size : (k + 1) * size] = acc[:, at_k : at_k + size].astype(BF)
            else:
                mine[:, base : base + n] = acc.astype(BF)
            base += n
        if not halves:
            return
        low = pl.multiple_of(side_ref[0] * half, half)
        high = pl.multiple_of((1 - side_ref[0]) * half, half)
        mine[...] = acc_ref[pl.ds(low, half), :].astype(BF)
        other[...] = acc_ref[pl.ds(high, half), :].astype(BF)

    specs, operands = [pl.BlockSpec(memory_space=pltpu.SMEM)], [side.reshape(1)]
    for left, right in products:
        specs += [pl.BlockSpec((a.shape[0], step), lambda i: (0, i)) for a in left]
        specs += [whole(b.shape) for b in right]
        operands += [*left, *right]
    return pl.pallas_call(
        body,
        grid=(dp,),
        in_specs=specs,
        out_specs=[pl.BlockSpec((step // cut, cols), lambda i: (i, 0))] * cut,
        out_shape=[pltpu.HBM((model // cut, cols), BF)] * cut,
        scratch_shapes=[pltpu.VMEM((step, cols), F32)],
        compiler_params=params(14, 1),
        cost_estimate=cost(5),
        name=name,
    )(*operands)


def pieces(chunks):
    return [p for pair in chunks for p in pair]


def shards(
    tokens, cotangent, ln1_gain, ln1_bias, w_qkv, qv_bias, w_out, out_bias, scale_attn,
    ln2_gain, ln2_bias, w_fc1, fc1_bias, w_fc2, fc2_bias, scale_mlp,
):
    side = lax.axis_index("section")
    first = side == 0
    dp = lax.axis_size("dp")
    here = lax.axis_index("dp")
    chips = lax.axis_size("tensor") // 2
    rows, model = tokens.shape[2:]
    heads = qv_bias.shape[1]
    size = qv_bias.shape[2] * dp // 2
    width = heads * size
    units = w_fc1.shape[2]
    part = model // dp

    x0 = lax.dynamic_index_in_dim(tokens, side, 0, keepdims=False).reshape(rows, model)
    grad_top = lax.dynamic_index_in_dim(cotangent, side, 0, keepdims=False).reshape(rows, model)

    vectors = (ln1_gain, ln1_bias, out_bias, scale_attn, ln2_gain, ln2_bias, fc2_bias, scale_mlp)
    packed = jnp.concatenate(
        [v.reshape(-1) for v in vectors] + [fc1_bias.reshape(-1), qv_bias.reshape(-1)]
    )
    own_qkv = w_qkv.reshape(part, heads, 3, size).swapaxes(1, 2).reshape(part, 3 * width)
    own_att = jnp.concatenate([own_qkv, w_out[0].T], axis=1)
    give_att = half_of(own_att, 1 - side)
    came_att = swap_section(give_att)
    came_small = swap_section(tie(packed, give_att))
    both_small = jnp.concatenate(
        [jnp.where(first, packed, came_small), jnp.where(first, came_small, packed)]
    )
    cols = 4 * width
    tail = -(-both_small.size // (16 * cols)) * 16
    both_small = jnp.pad(both_small, (0, tail * cols - both_small.size)).reshape(tail, cols)
    mine_att = half_of(own_att, side)
    ring_att0 = jnp.concatenate([jnp.where(first, mine_att, came_att), both_small])
    ring_att1 = jnp.where(first, came_att, mine_att)
    hops_att0 = direct(ring_att0)
    own_ff = jnp.concatenate([w_fc1[0], w_fc2[0].T], axis=1)
    rest_att = swap_section(tie(mine_att, ring_att0))
    came_ff = swap_section(tie(half_of(own_ff, 1 - side), ring_att0))
    mine_ff = half_of(own_ff, side)
    ring_ff0 = jnp.where(first, mine_ff, came_ff)
    ring_ff1 = jnp.where(first, came_ff, mine_ff)

    def other_half(own, rest):
        left = half_of(own, 1 - side)
        return jnp.where(first, left, rest), jnp.where(first, rest, left)


    backs = [swap_section(v) for v in hops_att0]
    back = [ring_att0, *hops_att0]
    back[2] = tie(back[2], backs[-1])
    flat = in_order([v[-tail:] for v in back])
    flat = flat.reshape(dp, -1)[:, : 2 * packed.size].reshape(dp, 2, -1).astype(F32)
    cut = 8 * part
    vecs = flat[:, :, :cut].reshape(dp, 2, 8, part).transpose(1, 2, 0, 3).reshape(2, 8, model)
    vecs = (vecs[0], vecs[1])
    bias_fc1 = flat[:, :, cut : cut + units // dp].swapaxes(0, 1).reshape(2, 1, units)
    qv = flat[:, :, cut + units // dp :].reshape(dp, 2, heads, -1).transpose(1, 2, 0, 3)
    qv = qv.reshape(2, heads, 2, size)
    bias_qkv = jnp.stack([qv[:, :, 0], jnp.zeros_like(qv[:, :, 0]), qv[:, :, 1]], axis=1)
    bias_qkv = bias_qkv.reshape(2, 1, 3 * width)

    norm1 = norm_first(tie(x0, came_ff), vecs[0])
    rest_ff = swap_section(tie(mine_ff, norm1))
    rest_att0, rest_att1 = other_half(own_att, rest_att)
    rest_ff0, rest_ff1 = other_half(own_ff, rest_ff)
    att1 = Ring(ring_att1)
    att0 = assemble([(tie(ring_att0, norm1), rest_att0), *zip(hops_att0, backs)], model)
    ff0, ff1 = Ring(ring_ff0), Ring(ring_ff1)
    hop_ff0 = ff0.hop(norm1)

    def projection(weight, s):
        return lambda pair: project_qkv(pair, weight, bias_qkv[s])

    chunks0, qkv0 = gather_tokens(norm1, projection(att0, 0), [rest_ff, *hop_ff0])
    beside = [*ff0.hop(), *ff0.back()]
    kept0, lse0, sames, others = attention(qkv0, att0, size)
    terms, _ = scatter_tokens(
        sames,
        tie(others, *beside),
        beside=lambda gate: [*ff0.hop(gate), *ff0.back(gate)],
    )
    attended0, residual0, norm2 = after_attention(x0, terms, vecs[0])
    ff0.back()
    beside = [*att1.hop(norm2), *att1.hop()]
    w_ff0 = assemble([(ring_ff0, rest_ff0), *zip(ff0.hops, ff0.backs)], model)
    second0, mlp0 = gather_tokens(
        norm2, lambda pair: mlp_forward(pair, w_ff0, bias_fc1[0]), beside
    )
    act0, slope0, sames, others = zip(*mlp0)
    beside = [*att1.hop(second0[-1][0]), *att1.back(second0[-1][0])]
    terms, _ = scatter_tokens(
        sames,
        [others[0], *[tie(v, *beside) for v in others[1:]]],
        beside=lambda gate: [*ff1.hop(gate), *att1.back(gate), *att1.back(gate)],
    )
    mlp_out0, y0, norm1 = after_mlp(residual0, terms, vecs[0], vecs[1])

    w_att1 = assemble([(ring_att1, rest_att1), *zip(att1.hops, att1.backs)], model)
    low1, sums_fc2_1 = start_back(grad_top, vecs[1])
    beside = [*ff1.hop(norm1), *ff1.back(norm1)]
    chunks1, qkv1 = gather_tokens(norm1, projection(w_att1, 1), beside)
    gate = chunks1[-1][0]
    came = [from_chip(tie(low1, gate), step) for step in range(1, chips)]
    beside = [*came, *ff1.hop(gate), *ff1.back(gate)]
    kept1, lse1, sames, others = attention(qkv1, w_att1, size)
    others = tie(others, *beside)
    grads1 = [(low1, core_swap(low1))] + [(v, core_swap(tie(v, lse1))) for v in came]
    terms, _ = scatter_tokens(
        sames, others, beside=lambda gate: [*ff1.back(gate), *pieces(grads1)]
    )
    attended1, residual1, norm2 = after_attention(y0, terms, vecs[1])
    w_ff1 = assemble([(ring_ff1, rest_ff1), *zip(ff1.hops, ff1.backs)], model)
    spare = list(grads1)
    second1, mlp1 = gather_tokens(
        norm2, lambda pair: mlp_both(pair, spare.pop(0), w_ff1, bias_fc1[1])
    )
    act1, dpre1, sums_fc1_1, sames_y1, others_y1, sames, others = zip(*mlp1)

    def grad_ff(second, dpre, grads, act):
        return lambda after: weight_grads(
            [
                (pieces(second), [late(tie(dpre[0], after)), *map(late, dpre[1:])]),
                (pieces(grads), [late(a) for a in act]),
            ],
            dp,
            side,
            "grad_ff",
        )

    def grad_att(chunks, dqkv, datt, kept):
        return lambda after: weight_grads(
            [
                (pieces(chunks), [late(tie(dqkv[0], after)), *map(late, dqkv[1:])]),
                (pieces(datt), [late(a) for a in kept]),
            ],
            dp,
            side,
            "grad_att",
            False,
            heads,
        )[0]

    old = [tuple(map(late, pair)) for pair in grads1]
    terms, g = scatter_tokens(sames, others, grad_ff(second1, dpre1, old, act1))
    sum_ff1 = RingSum((0, 1), *g)
    dres1, low, sums1 = back_second(grad_top, residual1, attended1, terms, vecs[1])
    came_y0 = lax.ppermute(tie(y0, low), "section", [(1, 0)])
    datt, _ = gather_tokens(low, lambda pair: pair[0], sum_ff1.step())
    sums_y1, local_y1 = core_sums(sames_y1, [tie(v, low) for v in others_y1])
    terms_y1 = send_sums([tie(v, datt[-1][0]) for v in sums_y1])
    beside = [came_y0, *terms_y1, *sum_ff1.step(low)]
    dqkv, sames, others, qkv_sums1 = attention_back(qkv1, kept1, lse1, datt, w_att1, size)
    old = [tuple(map(late, pair)) for pair in chunks1]
    terms, g = scatter_tokens(
        sames, tie(others, *beside), grad_att(old, dqkv, datt, kept1), sum_ff1.step
    )
    sum_att1 = RingSum((0, 1), g)
    sum_att1.step()
    dx1, low0, edge1 = back_first(dres1, late(y0), terms, vecs[1], late(mlp_out0), vecs[0])

    y1, sums_sc_1 = last_output(
        residual1, [tie(sames_y1[0], low0), *terms_y1, local_y1], grad_top, vecs[1]
    )

    slopes = list(slope0)
    grads0, mlp_back0 = gather_tokens(
        low0,
        lambda pair: mlp_backward(pair, slopes.pop(0), w_ff0, bias_fc1[0]),
        [y1, *sum_ff1.step(low0)],
    )
    dpre0, sums_fc1_0, sames, others = zip(*mlp_back0)
    hop_att1 = sum_att1.step(grads0[-1][0])
    old = [tuple(map(late, pair)) for pair in second0]
    terms, g = scatter_tokens(
        sames,
        others,
        grad_ff(old, dpre0, grads0, act0),
        lambda gate: [*sum_ff1.step(gate), *hop_att1],
    )
    sum_ff0 = RingSum((1, 0), *g)
    dres0, low, sums0 = back_second(
        dx1, late(residual0), late(attended0), terms, vecs[0]
    )
    beside = [*sum_att1.step(low), *sum_ff0.step(low)]
    datt, _ = gather_tokens(low, lambda pair: pair[0], beside)
    beside = [*sum_att1.step(low), *sum_ff0.step(low)]
    dqkv, sames, others, qkv_sums0 = attention_back(qkv0, kept0, lse0, datt, att0, size)
    old = [tuple(map(late, pair)) for pair in chunks0]
    others = tie(others, *beside)
    beside = sum_ff0.step(others)
    terms, g = scatter_tokens(
        sames, others, grad_att(old, dqkv, datt, kept0), lambda gate: beside
    )
    sum_att0 = RingSum((1, 0), g)
    sum_att0.step()
    going = sum_att0.step()
    terms = [late(terms[0]), *terms[1:-1], late(terms[-1])]
    dx0, edge0 = back_first(late(dres0), late(x0), terms, vecs[0])
    came_dx0 = came_y1 = swap_section(jnp.where(first, y1, dx0))
    second_hop = sum_att0.step(dx0)
    step_att1 = sum_att1.step(dx0)
    third_hop = sum_att0.step()
    sent = sum_att0.sent
    third_hop += sum_ff0.step(sent)
    sum_ff0.step()
    sum_att0.own = sum_att0.total()
    low = sum_att0.own.astype(BF)
    if low.shape == dx1.shape:
        sum_att0.came = came_dx1 = swap_section(jnp.where(first, dx1, low))
    else:
        sum_att0.came = lax.ppermute(low, "section", [(1, 0)])
        came_dx1 = lax.ppermute(dx1, "section", [(0, 1)])

    def both(low, high, came_low, came_high):
        mine = jnp.where(first, low, high)
        came = jnp.where(first, came_low, came_high)
        return jnp.stack([jnp.where(first, mine, came), jnp.where(first, came, mine)])[None, :, None]

    block_out = both(y0, y1, came_y0, came_y1)
    input_grads = both(dx0, dx1, came_dx0, came_dx1)
    sum_att0.came = tie(sum_att0.came, block_out)

    def by_unit(qkv_sums, unit_sums):
        q = qkv_sums[:, :width].reshape(heads, 1, size)
        v = qkv_sums[:, 2 * width :].reshape(heads, 1, size)
        bias = jnp.concatenate([q, v], 1).reshape(heads, dp, -1).swapaxes(0, 1).reshape(dp, -1)
        return jnp.concatenate([bias, unit_sums.reshape(dp, -1)], axis=1)

    unit0 = by_unit(tie(qkv_sums0, dx0), sum(sums_fc1_0))
    unit1 = by_unit(tie(qkv_sums1, dx0), sum(sums_fc1_1))
    vec = jnp.concatenate(
        [edge0[:2], sums0[:4], edge1[2:4], edge1[:2], sums1[:4], sums_sc_1[:1], sums_fc2_1[:1]]
    )
    vec = tie(vec, *going)
    vec = vec + core_swap(vec)
    vec = tie(sum([from_chip(vec, step) for step in range(1, chips)], vec), *second_hop)
    vec = tie(vec, sent)
    vec = vec.reshape(2, 8, dp, part).swapaxes(1, 2).reshape(2, dp, 8 * part)
    vec0 = jnp.concatenate([vec[0], unit0], axis=1)
    vec1 = jnp.concatenate([vec[1], unit1], axis=1)
    own = jnp.where(first, vec0, vec1) + swap_section(jnp.where(first, vec1, vec0))
    own = tie(own, *step_att1, came_y1, *third_hop)
    vec = lax.dynamic_slice_in_dim(own, here, 1, 0)
    for step in range(1, dp):
        pairs = [(i, (i + step) % dp) for i in range(dp)]
        other = lax.dynamic_slice_in_dim(own, lax.rem(here + step, dp), 1, 0)
        vec = vec + lax.ppermute(other, "dp", pairs)
    cut = 8 * part + heads * (2 * size // dp)
    bias_grad = vec[:, 8 * part : cut].reshape(1, heads, -1)
    fc1_grad = vec[:, cut:].reshape(1, 1, -1)
    g_ln1, b_ln1, g_ln2, b_ln2, g_sc_attn, g_out_bias, g_sc_mlp, g_fc2_bias = (
        vec[:, i * part : (i + 1) * part] for i in range(8)
    )

    def owned(low, high):
        top = jnp.where(first, low.own, high.came.astype(F32))
        bottom = jnp.where(first, low.came.astype(F32), high.own)
        return jnp.concatenate([top, bottom], 0)

    g_ff = owned(sum_ff0, sum_ff1)
    g_att = jnp.where(
        first,
        sum_att0.own + sum_att0.came.astype(F32),
        sum_att1.own + sum_att1.came.astype(F32),
    )
    g_qkv = g_att[None, :, : 3 * width]
    g_out = g_att[:, 3 * width :].T[None]
    g_fc1 = g_ff[:, :units][None]
    g_fc2 = g_ff[:, units:].T[None]
    return (
        block_out, input_grads, g_ln1, b_ln1, g_qkv, bias_grad, g_out, g_out_bias, g_sc_attn,
        g_ln2, b_ln2, g_fc1, fc1_grad, g_fc2, g_fc2_bias, g_sc_mlp,
    )


def solution(mesh):
    vec = P("section", "dp")
    by_row = P("section", "dp", "tensor")
    by_unit = P("section", "tensor", "dp")
    data = P(None, "dp", "tensor", None)
    split = P("section", None, "dp", "tensor", None)
    given = (
        vec, vec, by_row, by_unit, by_unit, vec, vec, vec, vec, by_row, by_unit, by_unit, vec, vec,
    )
    return jax.shard_map(
        shards,
        mesh=mesh,
        in_specs=(data, data) + given,
        out_specs=(split, split) + given,
        check_vma=False,
    )
```

```python
from functools import partial

import jax
import jax.numpy as jnp
from jax import lax
from jax.experimental import pallas as pl
from jax.experimental.pallas import tpu as pltpu
from jax.sharding import PartitionSpec as P

EPSILON = 1e-06
BF = jnp.bfloat16
F32 = jnp.float32
MIB = 1 << 20

LN1_G, LN1_B, OUT_B, SC_ATTN, LN2_G, LN2_B, FC2_B, SC_MLP = range(8)


def dot(a, b):
    return lax.dot_general(a, b, (((1,), (0,)), ((), ())), preferred_element_type=F32)


def dot_bt(a, b):
    return lax.dot_general(a, b, (((1,), (1,)), ((), ())), preferred_element_type=F32)


def dot_at(a, b):
    return lax.dot_general(a, b, (((0,), (0,)), ((), ())), preferred_element_type=F32)


def turn(v):
    return v.astype(F32).T


def params(limit, grid=0):
    return pltpu.CompilerParams(
        vmem_limit_bytes=limit * MIB,
        dimension_semantics=("arbitrary",) * grid if grid else None,
    )


def late(v):
    return pltpu.with_memory_space_constraint(v, pltpu.HBM)


def whole(shape):
    return pl.BlockSpec(shape, lambda i: (0, 0), pipeline_mode=pl.Buffered(1))


def cost(micros):
    return pl.CostEstimate(flops=int(micros * 1.15e9), bytes_accessed=0, transcendentals=0)


def sds(shape, dtype):
    return jax.ShapeDtypeStruct(shape, dtype)


def core_swap(v):
    count = lax.axis_size("tensor")
    return lax.ppermute(v, "tensor", [(i, i ^ 1) for i in range(count)])


def from_chip(v, step):
    count = lax.axis_size("tensor")
    chips = count // 2
    pairs = [(((i // 2 + step) % chips) * 2 + i % 2, i) for i in range(count)]
    return lax.ppermute(v, "tensor", pairs)


def tie(v, *after):
    if not after:
        return v
    return lax.optimization_barrier((v, *after))[0]


def tie_all(vs, *after):
    return lax.optimization_barrier((*vs, *after))[: len(vs)]


def gather_tokens(own, work, beside=()):
    chips = lax.axis_size("tensor") // 2
    came = [from_chip(own, step) for step in range(1, chips)]
    chunks = [(own, core_swap(own))]
    results = [work(chunks[0])]
    for same in came:
        same = tie(same, results[-1], *beside)
        chunks.append((same, core_swap(same)))
        results.append(work(chunks[-1]))
    return chunks, results


def core_sums(sames, others):
    chips, rows = len(sames), sames[0].shape[0]
    if isinstance(others, (list, tuple)):
        came = [core_swap(v) for v in others[1:]]
        local = core_swap(tie(others[0], came[-1]))
    else:
        local = core_swap(others)
        came = [local[c * rows : (c + 1) * rows] for c in range(1, chips)]
    sums = [(a.astype(F32) + b.astype(F32)).astype(BF) for a, b in zip(sames[1:], came)]
    return sums, local


def send_sums(sums):
    chips = len(sums) + 1
    return [from_chip(both, chips - step) for step, both in enumerate(sums, 1)]


def scatter_tokens(sames, others, work=None, beside=None):
    sums, local = core_sums(sames, others)
    terms = send_sums(sums)
    made = work(sums[-1]) if work else local
    more = beside(sums[-1]) if beside else ()
    terms = [tie(t, made, local, *more) for t in terms]
    return [sames[0], *terms, local], made


def swap_section(v):
    return lax.ppermute(v, "section", [(0, 1), (1, 0)])


def assemble(shards, rows):
    count = len(shards)
    cut = len(shards[0])
    size, cols = rows // (count * cut), shards[0][0].shape[1]
    place = jnp.stack([lax.axis_index("dp"), lax.axis_index("section")])

    def body(place_ref, *refs):
        out_ref, sems = refs[count * cut :]
        z, x = place_ref[0], place_ref[1]
        started = []
        for k in range(count):
            base = lax.rem(z + (count - k), count) * (cut * size)
            for i, at in enumerate([base] if cut == 1 else [base + x * size, base + (1 - x) * size]):
                copy = pltpu.make_async_copy(
                    refs[k * cut + i].at[pl.ds(0, size), :],
                    out_ref.at[pl.ds(pl.multiple_of(at, size), size), :],
                    sems.at[k * cut + i],
                )
                copy.start()
                started.append(copy)
        for copy in started:
            copy.wait()

    hbm = pl.BlockSpec(memory_space=pl.ANY)
    return pl.pallas_call(
        body,
        in_specs=[pl.BlockSpec(memory_space=pltpu.SMEM)] + [hbm] * (count * cut),
        out_specs=pl.BlockSpec(memory_space=pltpu.VMEM),
        out_shape=sds((rows, cols), shards[0][0].dtype),
        scratch_shapes=[pltpu.SemaphoreType.DMA((count * cut,))],
        compiler_params=params(6),
        cost_estimate=cost(2),
        name="assemble",
    )(place, *[late(v) for shard in shards for v in shard])


def half_of(v, which):
    half = v.shape[0] // 2
    return lax.dynamic_slice_in_dim(v, which * half, half, 0)


def direct(own):
    count = lax.axis_size("dp")
    return [
        lax.ppermute(own, "dp", [(i, (i + step) % count) for i in range(count)])
        for step in range(1, count)
    ]


def third(values, index):
    cuts = [-(-len(values) * i // 3) for i in range(4)]
    return values[cuts[index] : cuts[index + 1]]


class Ring:
    def __init__(self, own):
        self.last, self.hops, self.backs, self.at, self.back_at = own, [], [], 0, 0

    def hop(self, *gate):
        count = lax.axis_size("dp")
        pairs = [(i, (i + 1) % count) for i in range(count)]
        new = []
        for i in range(len(third(range(count - 1), self.at))):
            self.last = lax.ppermute(tie(self.last, *gate) if i == 0 else self.last, "dp", pairs)
            new.append(self.last)
        self.hops += new
        self.at += 1
        return new

    def back(self, *gate):
        count = lax.axis_size("dp")
        which = third(range(count - 1), self.back_at)
        new = [swap_section(tie(self.hops[i], *gate)) for i in which]
        self.backs += new
        self.back_at += 1
        return new


def in_order(back):
    count = len(back)
    ahead = [back[0], *back[:0:-1]]
    twice = jnp.stack(ahead + ahead)
    return lax.dynamic_slice_in_dim(twice, count - lax.axis_index("dp"), count, 0)


def dp_rows(v, back):
    dp = lax.axis_size("dp")
    part = v.shape[0] // dp
    place = lax.rem(lax.axis_index("dp") + (dp - back), dp)
    return lax.dynamic_slice_in_dim(v, place * part, part, 0)


class RingSum:
    def __init__(self, pair, mine, other=None):
        self.mine, self.other, self.pair = mine, other, pair
        self.terms, self.at, self.done = [], 0, 0

    def total(self, gate=()):
        first = tie(self.terms[0], *gate)
        return sum(t.astype(F32) for t in [first, *self.terms[1:]])

    def one(self, gate):
        dp = lax.axis_size("dp")
        self.done += 1
        new = []
        if self.terms:
            pairs = [(i, (i + 1) % dp) for i in range(dp)]
            self.sent = self.total(gate).astype(BF)
            new.append(lax.ppermute(self.sent, "dp", pairs))
        if self.other is not None:
            if self.done == 1:
                new.append(swap_section(dp_rows(tie(self.other, *gate), 1)))
            else:
                new.append(swap_section(tie(dp_rows(self.other, self.done), *gate)))
        self.terms = [*new, dp_rows(self.mine, self.done)]
        return new

    def step(self, *gate):
        self.at += 1
        if self.at == 5:
            self.own = self.total(gate)
            self.came = lax.ppermute(self.own.astype(BF), "section", [self.pair])
            return [self.came]
        count = 1 if self.at == 1 else len(third(range(lax.axis_size("dp") - 1), self.at - 2))
        return [v for i in range(count) for v in self.one(gate if i == 0 else ())]


def standardize(v):
    centred = v - jnp.mean(v, axis=-1, keepdims=True)
    var = jnp.mean(centred * centred, axis=-1, keepdims=True)
    scale = lax.rsqrt(var + EPSILON)
    return centred * scale, scale


def norm_of(v, vec, gain, shift):
    return (standardize(v)[0] * vec[gain : gain + 1, :] + vec[shift : shift + 1, :]).astype(BF)


def norm_back(v, grad, gain):
    xh, scale = standardize(v)
    dxh = grad * gain
    inner = jnp.mean(dxh * xh, axis=-1, keepdims=True)
    out = scale * (dxh - jnp.mean(dxh, axis=-1, keepdims=True) - xh * inner)
    return out, grad * xh


def total(refs):
    out = refs[0][...].astype(F32)
    for ref in refs[1:]:
        out = out + ref[...].astype(F32)
    return out


def fold(v, op):
    return op(v.reshape(-1, 8, v.shape[1]), axis=0)


def add_rows(ref, rows):
    for k, row in enumerate(rows):
        ref[8 * k : 8 * k + 8, :] += fold(row, jnp.sum)


def rowwise(body, row_ins, fulls, row_outs, sums, name):
    rows, width = row_ins[0].shape
    step = min(128, rows)
    some, outs = len(row_ins) + len(fulls), len(row_outs)

    def kernel(*refs):
        if not sums:
            body(*refs)
            return
        sum_ref, acc_ref = refs[some + outs :]

        @pl.when(pl.program_id(0) == 0)
        def _():
            acc_ref[...] = jnp.zeros_like(acc_ref)

        body(*refs[: some + outs], acc_ref)

        @pl.when(pl.program_id(0) == pl.num_programs(0) - 1)
        def _():
            for k in range(sums):
                sum_ref[k : k + 1, :] = jnp.sum(
                    acc_ref[8 * k : 8 * k + 8, :], axis=0, keepdims=True
                )

    out_shape = [sds((rows, width), d) for d in row_outs]
    out_shape += [sds((sums, width), F32)] if sums else []
    block = pl.BlockSpec((step, width), lambda i: (i, 0))
    return pl.pallas_call(
        kernel,
        grid=(rows // step,),
        in_specs=[block] * len(row_ins) + [whole(a.shape) for a in fulls],
        out_specs=[block] * outs + ([whole((sums, width))] if sums else []),
        out_shape=out_shape,
        scratch_shapes=[pltpu.VMEM((8 * sums, width), F32)] if sums else [],
        compiler_params=params(8, 1),
        cost_estimate=cost(2),
        name=name,
    )(*row_ins, *fulls)


def norm_first(x, vec):
    def body(x_ref, vec_ref, out_ref):
        out_ref[...] = norm_of(x_ref[...].astype(F32), vec_ref[...], LN1_G, LN1_B)

    return rowwise(body, [x], [vec], [BF], 0, "norm_first")[0]


def after_attention(x, terms, vec):
    count = len(terms)

    def body(*refs):
        x_ref, term_refs, vec_ref = refs[0], refs[1 : 1 + count], refs[1 + count]
        att_ref, res_ref, norm_ref = refs[2 + count :]
        v = vec_ref[...]
        attended = total(term_refs) + v[OUT_B : OUT_B + 1, :]
        residual = x_ref[...].astype(F32) + v[SC_ATTN : SC_ATTN + 1, :] * attended
        att_ref[...] = attended.astype(BF)
        res_ref[...] = residual
        norm_ref[...] = norm_of(residual, v, LN2_G, LN2_B)

    return rowwise(body, [x, *terms], [vec], [BF, F32, BF], 0, "after_attention")


def after_mlp(residual, terms, vec, vec_next):
    count = len(terms)

    def body(*refs):
        res_ref, term_refs = refs[0], refs[1 : 1 + count]
        vec_ref, next_ref, mlp_ref, y_ref, norm_ref = refs[1 + count :]
        v = vec_ref[...]
        mlp = total(term_refs) + v[FC2_B : FC2_B + 1, :]
        y = (res_ref[...] + v[SC_MLP : SC_MLP + 1, :] * mlp).astype(BF)
        mlp_ref[...] = mlp.astype(BF)
        y_ref[...] = y
        norm_ref[...] = norm_of(y.astype(F32), next_ref[...], LN1_G, LN1_B)

    return rowwise(body, [residual, *terms], [vec, vec_next], [BF, BF, BF], 0, "after_mlp")


def last_output(residual, terms, grad, vec):
    count = len(terms)

    def body(*refs):
        res_ref, term_refs = refs[0], refs[1 : 1 + count]
        grad_ref, vec_ref, y_ref, sum_ref = refs[1 + count :]
        v = vec_ref[...]
        mlp = total(term_refs) + v[FC2_B : FC2_B + 1, :]
        y_ref[...] = (res_ref[...] + v[SC_MLP : SC_MLP + 1, :] * mlp).astype(BF)
        add_rows(sum_ref, [grad_ref[...].astype(F32) * mlp])

    return rowwise(body, [residual, *terms, grad], [vec], [BF], 1, "last_output")


def start_back(grad, vec):
    def body(grad_ref, vec_ref, out_ref, sum_ref):
        low = (vec_ref[...][SC_MLP : SC_MLP + 1, :] * grad_ref[...].astype(F32)).astype(BF)
        out_ref[...] = low
        add_rows(sum_ref, [low.astype(F32)])

    return rowwise(body, [grad], [vec], [BF], 1, "start_back")


def back_second(grad, residual, attended, terms, vec):
    count = len(terms)

    def body(*refs):
        grad_ref, res_ref, att_ref = refs[:3]
        term_refs = refs[3 : 3 + count]
        vec_ref, dres_ref, low_ref, sum_ref = refs[3 + count :]
        v = vec_ref[...]
        dn = total(term_refs)
        back, dgain = norm_back(res_ref[...], dn, v[LN2_G : LN2_G + 1, :])
        dres = grad_ref[...].astype(F32) + back
        low = (v[SC_ATTN : SC_ATTN + 1, :] * dres).astype(BF)
        dres_ref[...] = dres
        low_ref[...] = low
        add_rows(sum_ref, [dgain, dn, dres * att_ref[...].astype(F32), low.astype(F32)])

    return rowwise(
        body, [grad, residual, attended, *terms], [vec], [F32, BF], 4, "back_second"
    )


def back_first(dres, x, terms, vec, mlp_below=None, vec_below=None):
    count = len(terms)
    below = mlp_below is not None

    def body(*refs):
        dres_ref, x_ref = refs[:2]
        term_refs = refs[2 : 2 + count]
        rest = refs[2 + count :]
        if below:
            mlp_ref, vec_ref, under_ref, dx_ref, low_ref, sum_ref = rest
        else:
            vec_ref, dx_ref, sum_ref = rest
        v = vec_ref[...]
        dn = total(term_refs)
        back, dgain = norm_back(x_ref[...].astype(F32), dn, v[LN1_G : LN1_G + 1, :])
        dx = (dres_ref[...] + back).astype(BF)
        dx_ref[...] = dx
        rows = [dgain, dn]
        if below:
            wide = dx.astype(F32)
            low = (under_ref[...][SC_MLP : SC_MLP + 1, :] * wide).astype(BF)
            low_ref[...] = low
            rows += [wide * mlp_ref[...].astype(F32), low.astype(F32)]
        add_rows(sum_ref, rows)

    row_ins = [dres, x, *terms] + ([mlp_below] if below else [])
    fulls = [vec] + ([vec_below] if below else [])
    return rowwise(body, row_ins, fulls, [BF, BF] if below else [BF], 4 if below else 2, "back_first")


def project_qkv(pair, weight, bias):
    rows, width = pair[0].shape
    cols = bias.shape[1]

    def body(a_ref, b_ref, w_ref, bias_ref, out_ref):
        w = w_ref[...]
        shift = bias_ref[...]
        out_ref[:rows, :] = (dot(a_ref[...], w) + shift).astype(BF)
        out_ref[rows:, :] = (dot(b_ref[...], w) + shift).astype(BF)

    return pl.pallas_call(
        body,
        grid=(1,),
        in_specs=[
            whole((rows, width)), whole((rows, width)), whole((width, cols)), whole((1, cols))
        ],
        out_specs=whole((2 * rows, cols)),
        out_shape=sds((2 * rows, cols), BF),
        compiler_params=params(6, 1),
        cost_estimate=cost(0.5),
        name="project_qkv",
    )(*pair, weight, bias)


def head_rows(v, head, size):
    rows = lax.broadcasted_iota(jnp.int32, v.shape, 0)
    return jnp.where(rows // size == head, v, jnp.zeros_like(v))


def head_cols(v, head, size):
    cols = lax.broadcasted_iota(jnp.int32, v.shape, 1)
    return jnp.where(cols // size == head, v, jnp.zeros_like(v))


def attention(packed, weight, size):
    chips = len(packed)
    span = packed[0].shape[0]
    half = span // 2
    width = packed[0].shape[1] // 3
    seq = chips * span
    heads = width // size
    model = weight.shape[0]
    step = min(256, seq)
    chunk = min(128, seq)
    score = size**-0.5

    def body(*refs):
        in_refs, w_ref = refs[:chips], refs[chips]
        head_refs = refs[chips + 1 : 2 * chips + 1]
        lse_ref = refs[2 * chips + 1]
        same_refs, other_ref = refs[2 * chips + 2 : 3 * chips + 2], refs[3 * chips + 2]
        k_ref, qt_ref, vt_ref, ot_ref, s_ref, p_ref = refs[3 * chips + 3 :]
        for c in range(chips):
            at = slice(c * span, (c + 1) * span)
            k_ref[at, :] = in_refs[c][:, width : 2 * width]
            qt_ref[:, at] = (turn(in_refs[c][:, :width]) * score).astype(BF)
            vt_ref[:, at] = turn(in_refs[c][:, 2 * width :]).astype(BF)

        def one(i, carry):
            at = pl.ds(pl.multiple_of(i * step, step), step)
            q = qt_ref[:, at]
            s_ref[0] = dot(k_ref[...], head_rows(q, 0, size))
            for h in range(heads):
                if h + 1 < heads:
                    s_ref[(h + 1) % 2] = dot(k_ref[...], head_rows(q, h + 1, size))
                now = h % 2
                top = fold(s_ref[now, :chunk, :], jnp.max)
                for r in range(chunk, seq, chunk):
                    top = jnp.maximum(top, fold(s_ref[now, r : r + chunk, :], jnp.max))
                top = jnp.max(top, axis=0, keepdims=True)
                norm = jnp.zeros((8, step), F32)
                for r in range(0, seq, chunk):
                    p = jnp.exp(s_ref[now, r : r + chunk, :] - top)
                    norm = norm + fold(p, jnp.sum)
                    p_ref[now, r : r + chunk, :] = p.astype(BF)
                norm = jnp.sum(norm, axis=0, keepdims=True)
                rows = slice(h * size, (h + 1) * size)
                ot_ref[rows, at] = dot(vt_ref[rows, :], p_ref[now]) / norm
                lse_ref[h : h + 1, at] = top + jnp.log(norm)
            return carry

        lax.fori_loop(0, seq // step, one, 0)
        for c in range(chips):
            at = slice(c * span, (c + 1) * span)
            o = ot_ref[:, at].T.astype(BF)
            head_refs[c][...] = o
            same_refs[c][...] = dot_bt(o[:half], w_ref[...]).astype(BF)
            other_ref[c * half : (c + 1) * half, :] = dot_bt(o[half:], w_ref[...]).astype(BF)

    out = pl.pallas_call(
        body,
        grid=(1,),
        in_specs=[whole((span, 3 * width))] * chips
        + [pl.BlockSpec((model, width), lambda i: (0, 3), pipeline_mode=pl.Buffered(1))],
        out_specs=[whole((span, width))] * chips
        + [whole((heads, seq))]
        + [whole((half, model))] * chips
        + [whole((seq // 2, model))],
        out_shape=[pltpu.HBM((span, width), BF)] * chips
        + [sds((heads, seq), F32)]
        + [sds((half, model), BF)] * chips
        + [sds((seq // 2, model), BF)],
        scratch_shapes=[
            pltpu.VMEM((seq, width), BF),
            pltpu.VMEM((width, seq), BF),
            pltpu.VMEM((width, seq), BF),
            pltpu.VMEM((width, seq), F32),
            pltpu.VMEM((2, seq, step), F32),
            pltpu.VMEM((2, seq, step), BF),
        ],
        compiler_params=params(14, 1),
        cost_estimate=cost(9),
        name="attention",
    )(*packed, weight)
    return out[:chips], out[chips], out[chips + 1 : -1], out[-1]


def attention_back(packed, heads_kept, lse, datt, weight, size):
    chips = len(packed)
    span = packed[0].shape[0]
    half = span // 2
    width = packed[0].shape[1] // 3
    seq = chips * span
    heads = width // size
    model = weight.shape[0]
    step = min(256, seq)
    chunk = min(128, seq)
    score = size**-0.5

    def body(*refs):
        at = 0

        def take(count):
            nonlocal at
            at += count
            return refs[at - count : at]

        in_refs, kept_refs = take(chips), take(chips)
        (lse_ref,) = take(1)
        datt_refs = take(2 * chips)
        (w_ref,) = take(1)
        dqkv_refs = take(chips)
        same_refs = take(chips)
        other_ref, sum_ref = take(2)
        k_ref, v_ref, kt_ref, qt_ref, q_ref, do_ref, dot_ref = take(7)
        inner_ref, s_ref, g_ref, p_ref, ds_ref, dk_ref, dv_ref, dqt_ref = take(8)
        for c in range(chips):
            rows = slice(c * span, (c + 1) * span)
            q = in_refs[c][:, :width].astype(F32) * score
            k = in_refs[c][:, width : 2 * width]
            q_ref[rows, :] = q.astype(BF)
            qt_ref[:, rows] = q.T.astype(BF)
            k_ref[rows, :] = k
            kt_ref[:, rows] = turn(k).astype(BF)
            v_ref[rows, :] = in_refs[c][:, 2 * width :]
            for b in range(2):
                d = dot(datt_refs[2 * c + b][...], w_ref[:, 3 * width :]).astype(BF)
                here = slice(c * span + b * half, c * span + (b + 1) * half)
                do_ref[here, :] = d
                dt = turn(d)
                dot_ref[:, here] = dt.astype(BF)
                prod = dt * turn(kept_refs[c][b * half : (b + 1) * half, :])
                for h in range(heads):
                    inner_ref[h : h + 1, here] = jnp.sum(
                        prod[h * size : (h + 1) * size, :], axis=0, keepdims=True
                    )

        def one(i, carry):
            at = pl.ds(pl.multiple_of(i * step, step), step)
            qt = qt_ref[:, at]
            dot_t = dot_ref[:, at]
            q = q_ref[at, :]
            do = do_ref[at, :]

            def scores(h):
                s_ref[h % 2] = dot(k_ref[...], head_rows(qt, h, size))
                g_ref[h % 2] = dot(v_ref[...], head_rows(dot_t, h, size))

            scores(0)
            for h in range(heads):
                if h + 1 < heads:
                    scores(h + 1)
                now = h % 2
                cols = slice(h * step, (h + 1) * step)
                lse = lse_ref[h : h + 1, at]
                inner = inner_ref[h : h + 1, at]
                for r in range(0, seq, chunk):
                    p = jnp.exp(s_ref[now, r : r + chunk, :] - lse)
                    ds = p * (g_ref[now, r : r + chunk, :] - inner)
                    p_ref[r : r + chunk, cols] = p.astype(BF)
                    ds_ref[r : r + chunk, cols] = ds.astype(BF)
                rows = slice(h * size, (h + 1) * size)
                dqt_ref[rows, at] = dot(kt_ref[rows, :], ds_ref[:, cols]) * score
            dv = dot(p_ref[...], jnp.concatenate([head_cols(do, h, size) for h in range(heads)], 0))
            dk = dot(ds_ref[...], jnp.concatenate([head_cols(q, h, size) for h in range(heads)], 0))

            @pl.when(i == 0)
            def _():
                dv_ref[...] = dv
                dk_ref[...] = dk

            @pl.when(i > 0)
            def _():
                dv_ref[...] += dv
                dk_ref[...] += dk

            return carry

        lax.fori_loop(0, seq // step, one, 0)
        for c in range(chips):
            rows = slice(c * span, (c + 1) * span)
            out = dqkv_refs[c]
            out[:, :width] = dqt_ref[:, rows].T.astype(BF)
            out[:, width : 2 * width] = dk_ref[rows, :].astype(BF)
            out[:, 2 * width :] = dv_ref[rows, :].astype(BF)
            sums = jnp.sum(out[...].astype(F32), axis=0, keepdims=True)
            if c == 0:
                sum_ref[...] = sums
            else:
                sum_ref[...] += sums
            w = w_ref[:, : 3 * width]
            same_refs[c][...] = dot_bt(out[:half, :], w).astype(BF)
            other_ref[c * half : (c + 1) * half, :] = dot_bt(out[half:, :], w).astype(BF)

    flat = [g for pair in datt for g in pair]
    out_shape = (
        [pltpu.HBM((span, 3 * width), BF)] * chips
        + [pltpu.HBM((half, model), BF)] * chips
        + [sds((seq // 2, model), BF), sds((1, 3 * width), F32)]
    )
    operands = (*map(late, (*packed, *heads_kept)), lse, *flat, late(weight))
    out = pl.pallas_call(
        body,
        grid=(1,),
        in_specs=[whole(a.shape) for a in operands],
        out_specs=[whole(a.shape) for a in out_shape],
        out_shape=out_shape,
        scratch_shapes=[
            pltpu.VMEM((seq, width), BF),
            pltpu.VMEM((seq, width), BF),
            pltpu.VMEM((width, seq), BF),
            pltpu.VMEM((width, seq), BF),
            pltpu.VMEM((seq, width), BF),
            pltpu.VMEM((seq, width), BF),
            pltpu.VMEM((width, seq), BF),
            pltpu.VMEM((heads, seq), F32),
            pltpu.VMEM((2, seq, step), F32),
            pltpu.VMEM((2, seq, step), F32),
            pltpu.VMEM((seq, heads * step), BF),
            pltpu.VMEM((seq, heads * step), BF),
            pltpu.VMEM((seq, width), F32),
            pltpu.VMEM((seq, width), F32),
            pltpu.VMEM((width, seq), F32),
        ],
        compiler_params=params(26, 1),
        cost_estimate=cost(15),
        name="attention_back",
    )(*operands)
    return out[:chips], out[chips : 2 * chips], out[2 * chips], out[2 * chips + 1]


def gelu_both(x):
    away = jnp.abs(x)
    t = 1.0 / (1.0 + (0.3275911 * 0.5**0.5) * away)
    bell = jnp.exp(-0.5 * (x * x))
    poly = t * (
        0.127414796
        + t * (-0.142248368 + t * (0.7107068705 + t * (-0.7265760135 + t * 0.5307027145)))
    )
    tail = poly * bell
    phi = jnp.where(x >= 0, 1.0 - tail, tail)
    return x * phi, phi + x * (bell * 0.3989422804014327)


def mlp_call(body, pairs, extra, weight, bias, outs, parts, scratch, name):
    rows, model = pairs[0].shape
    units = weight.shape[1] // 2
    step = min(256, units)
    blocks = units // step
    cols = lambda j: (0, j)
    in_specs = [whole((rows, model)) for _ in pairs]
    in_specs += [pl.BlockSpec((2 * rows, step), cols) for _ in extra]
    in_specs += [
        pl.BlockSpec((model, step), cols),
        pl.BlockSpec((model, step), lambda j: (0, blocks + j)),
        pl.BlockSpec((1, step), cols),
    ]
    out_specs = [pl.BlockSpec((2 * rows, step), cols) for _ in outs]
    out_specs += [pl.BlockSpec((1, step), cols)]
    out_specs += [whole((rows, model))] * (2 * parts)
    out_shape = [pltpu.HBM((2 * rows, units), d) for d in outs] + [sds((1, units), F32)]
    out_shape += [sds((rows, model), BF)] * (2 * parts)
    count = len(pairs) // 2
    return pl.pallas_call(
        body,
        grid=(blocks,),
        in_specs=in_specs,
        out_specs=out_specs,
        out_shape=out_shape,
        scratch_shapes=[pltpu.VMEM((2 * rows, model), F32)] * parts
        + [pltpu.VMEM((2 * rows, step), F32)] * scratch,
        compiler_params=params(8 + 5 * parts, 1),
        cost_estimate=cost(0.5),
        name=name,
    )(*pairs, *map(late, extra), weight, weight, bias)


def clear(*refs):
    @pl.when(pl.program_id(0) == 0)
    def _():
        for ref in refs:
            ref[...] = jnp.zeros_like(ref)


def finish(acc, low, high):
    rows = low.shape[0]

    @pl.when(pl.program_id(0) == pl.num_programs(0) - 1)
    def _():
        low[...] = acc[:rows, :].astype(BF)
        high[...] = acc[rows:, :].astype(BF)


CHUNK = 32


def mlp_forward(pair, weight, bias):
    rows = pair[0].shape[0]

    def body(a, b, w1_ref, w2_ref, bias_ref, act_ref, slope_ref, sum_ref, lo, hi, acc, pre):
        clear(acc, sum_ref)
        shift = bias_ref[...]
        for i, x in enumerate((a, b)):
            pre[i * rows : (i + 1) * rows, :] = dot(x[...], w1_ref[...])
        for i in range(2):
            at = slice(i * rows, (i + 1) * rows)
            for r in range(i * rows, (i + 1) * rows, CHUNK):
                act, slope = gelu_both(pre[r : r + CHUNK, :] + shift)
                act_ref[r : r + CHUNK, :] = act.astype(BF)
                slope_ref[r : r + CHUNK, :] = slope.astype(BF)
            acc[at, :] += dot_bt(act_ref[at, :], w2_ref[...])
        finish(acc, lo, hi)

    act, slope, _, lo, hi = mlp_call(body, pair, [], weight, bias, [BF, BF], 1, 1, "mlp_forward")
    return act, slope, lo, hi


def mlp_backward(pair, slope, weight, bias):
    rows = pair[0].shape[0]

    def body(a, b, slope_ref, w1_ref, w2_ref, bias_ref, dpre_ref, sum_ref, lo, hi, acc, pre):
        clear(acc)
        for i, g in enumerate((a, b)):
            pre[i * rows : (i + 1) * rows, :] = dot(g[...], w2_ref[...])
        sums = jnp.zeros((8, bias_ref.shape[1]), F32)
        for i in range(2):
            at = slice(i * rows, (i + 1) * rows)
            for r in range(i * rows, (i + 1) * rows, CHUNK):
                d = pre[r : r + CHUNK, :] * slope_ref[r : r + CHUNK, :].astype(F32)
                d = d.astype(BF)
                dpre_ref[r : r + CHUNK, :] = d
                sums = sums + fold(d.astype(F32), jnp.sum)
            acc[at, :] += dot_bt(dpre_ref[at, :], w1_ref[...])
        sum_ref[...] = jnp.sum(sums, axis=0, keepdims=True)
        finish(acc, lo, hi)

    dpre, sums, lo, hi = mlp_call(
        body, pair, [slope], weight, bias, [BF], 1, 1, "mlp_backward"
    )
    return dpre, sums, lo, hi


def mlp_both(pair, grads, weight, bias):
    rows = pair[0].shape[0]

    def body(
        a, b, c, d, w1_ref, w2_ref, bias_ref, act_ref, dpre_ref, sum_ref,
        lo, hi, blo, bhi, acc, back, pre, grad,
    ):
        clear(acc, back)
        shift = bias_ref[...]
        for i, (x, g) in enumerate(((a, c), (b, d))):
            at = slice(i * rows, (i + 1) * rows)
            pre[at, :] = dot(x[...], w1_ref[...])
            grad[at, :] = dot(g[...], w2_ref[...])
        sums = jnp.zeros((8, bias_ref.shape[1]), F32)
        for i in range(2):
            at = slice(i * rows, (i + 1) * rows)
            for r in range(i * rows, (i + 1) * rows, CHUNK):
                act, slope = gelu_both(pre[r : r + CHUNK, :] + shift)
                act_ref[r : r + CHUNK, :] = act.astype(BF)
                dpre = (grad[r : r + CHUNK, :] * slope).astype(BF)
                dpre_ref[r : r + CHUNK, :] = dpre
                sums = sums + fold(dpre.astype(F32), jnp.sum)
            back[at, :] += dot_bt(dpre_ref[at, :], w1_ref[...])
            acc[at, :] += dot_bt(act_ref[at, :], w2_ref[...])
        sum_ref[...] = jnp.sum(sums, axis=0, keepdims=True)
        finish(acc, lo, hi)
        finish(back, blo, bhi)

    act, dpre, sums, lo, hi, blo, bhi = mlp_call(
        body, [*pair, *grads], [], weight, bias, [BF, BF], 2, 2, "mlp_both"
    )
    return act, dpre, sums, lo, hi, blo, bhi


def weight_grads(products, dp, side, name, halves=True, heads=0):
    model = products[0][0][0].shape[1]
    step = model // dp
    half = step // 2
    cut = 2 if halves else 1
    sizes = [(len(left), len(right), right[0].shape[1]) for left, right in products]
    cols = sum(n for _, _, n in sizes)

    def body(side_ref, *refs):
        acc_ref = refs[-1]
        mine, other = refs[-3:-1] if halves else (refs[-2], None)
        at = base = 0
        for many, few, n in sizes:
            lefts, rights = refs[at : at + many], refs[at + many : at + many + few]
            at += many + few
            ratio = many // few
            acc = None
            for i in range(many):
                size = lefts[i].shape[0]
                here = slice((i % ratio) * size, (i % ratio + 1) * size)
                term = dot_at(lefts[i][...], rights[i // ratio][here, :])
                acc = term if acc is None else acc + term
            if halves:
                acc_ref[:, base : base + n] = acc
            elif heads and not base:
                size = n // (3 * heads)
                for k in range(3 * heads):
                    head, kind = k // 3, k % 3
                    at_k = (kind * heads + head) * size
                    mine[:, k * size : (k + 1) * size] = acc[:, at_k : at_k + size].astype(BF)
            else:
                mine[:, base : base + n] = acc.astype(BF)
            base += n
        if not halves:
            return
        low = pl.multiple_of(side_ref[0] * half, half)
        high = pl.multiple_of((1 - side_ref[0]) * half, half)
        mine[...] = acc_ref[pl.ds(low, half), :].astype(BF)
        other[...] = acc_ref[pl.ds(high, half), :].astype(BF)

    specs, operands = [pl.BlockSpec(memory_space=pltpu.SMEM)], [side.reshape(1)]
    for left, right in products:
        specs += [pl.BlockSpec((a.shape[0], step), lambda i: (0, i)) for a in left]
        specs += [whole(b.shape) for b in right]
        operands += [*left, *right]
    return pl.pallas_call(
        body,
        grid=(dp,),
        in_specs=specs,
        out_specs=[pl.BlockSpec((step // cut, cols), lambda i: (i, 0))] * cut,
        out_shape=[pltpu.HBM((model // cut, cols), BF)] * cut,
        scratch_shapes=[pltpu.VMEM((step, cols), F32)],
        compiler_params=params(14, 1),
        cost_estimate=cost(5),
        name=name,
    )(*operands)


def pieces(chunks):
    return [p for pair in chunks for p in pair]


def shards(
    tokens, cotangent, ln1_gain, ln1_bias, w_qkv, qv_bias, w_out, out_bias, scale_attn,
    ln2_gain, ln2_bias, w_fc1, fc1_bias, w_fc2, fc2_bias, scale_mlp,
):
    side = lax.axis_index("section")
    first = side == 0
    dp = lax.axis_size("dp")
    here = lax.axis_index("dp")
    chips = lax.axis_size("tensor") // 2
    rows, model = tokens.shape[2:]
    heads = qv_bias.shape[1]
    size = qv_bias.shape[2] * dp // 2
    width = heads * size
    units = w_fc1.shape[2]
    part = model // dp

    x0 = lax.dynamic_index_in_dim(tokens, side, 0, keepdims=False).reshape(rows, model)
    grad_top = lax.dynamic_index_in_dim(cotangent, side, 0, keepdims=False).reshape(rows, model)

    vectors = (ln1_gain, ln1_bias, out_bias, scale_attn, ln2_gain, ln2_bias, fc2_bias, scale_mlp)
    packed = jnp.concatenate(
        [v.reshape(-1) for v in vectors] + [fc1_bias.reshape(-1), qv_bias.reshape(-1)]
    )
    own_qkv = w_qkv.reshape(part, heads, 3, size).swapaxes(1, 2).reshape(part, 3 * width)
    own_att = jnp.concatenate([own_qkv, w_out[0].T], axis=1)
    give_att = half_of(own_att, 1 - side)
    came_att = swap_section(give_att)
    came_small = swap_section(tie(packed, give_att))
    both_small = jnp.concatenate(
        [jnp.where(first, packed, came_small), jnp.where(first, came_small, packed)]
    )
    cols = 4 * width
    tail = -(-both_small.size // (16 * cols)) * 16
    both_small = jnp.pad(both_small, (0, tail * cols - both_small.size)).reshape(tail, cols)
    mine_att = half_of(own_att, side)
    ring_att0 = jnp.concatenate([jnp.where(first, mine_att, came_att), both_small])
    ring_att1 = jnp.where(first, came_att, mine_att)
    hops_att0 = direct(ring_att0)
    own_ff = jnp.concatenate([w_fc1[0], w_fc2[0].T], axis=1)
    rest_att = swap_section(tie(mine_att, ring_att0))
    came_ff = swap_section(tie(half_of(own_ff, 1 - side), ring_att0))
    mine_ff = half_of(own_ff, side)
    ring_ff0 = jnp.where(first, mine_ff, came_ff)
    ring_ff1 = jnp.where(first, came_ff, mine_ff)

    def other_half(own, rest):
        left = half_of(own, 1 - side)
        return jnp.where(first, left, rest), jnp.where(first, rest, left)


    backs = [swap_section(v) for v in hops_att0]
    back = [ring_att0, *hops_att0]
    back[2] = tie(back[2], backs[-1])
    flat = in_order([v[-tail:] for v in back])
    flat = flat.reshape(dp, -1)[:, : 2 * packed.size].reshape(dp, 2, -1).astype(F32)
    cut = 8 * part
    vecs = flat[:, :, :cut].reshape(dp, 2, 8, part).transpose(1, 2, 0, 3).reshape(2, 8, model)
    vecs = (vecs[0], vecs[1])
    bias_fc1 = flat[:, :, cut : cut + units // dp].swapaxes(0, 1).reshape(2, 1, units)
    qv = flat[:, :, cut + units // dp :].reshape(dp, 2, heads, -1).transpose(1, 2, 0, 3)
    qv = qv.reshape(2, heads, 2, size)
    bias_qkv = jnp.stack([qv[:, :, 0], jnp.zeros_like(qv[:, :, 0]), qv[:, :, 1]], axis=1)
    bias_qkv = bias_qkv.reshape(2, 1, 3 * width)

    norm1 = norm_first(tie(x0, came_ff), vecs[0])
    rest_ff = swap_section(tie(mine_ff, norm1))
    rest_att0, rest_att1 = other_half(own_att, rest_att)
    rest_ff0, rest_ff1 = other_half(own_ff, rest_ff)
    att1 = Ring(ring_att1)
    att0 = assemble([(tie(ring_att0, norm1), rest_att0), *zip(hops_att0, backs)], model)
    ff0, ff1 = Ring(ring_ff0), Ring(ring_ff1)
    hop_ff0 = ff0.hop(norm1)

    def projection(weight, s):
        return lambda pair: project_qkv(pair, weight, bias_qkv[s])

    chunks0, qkv0 = gather_tokens(norm1, projection(att0, 0), [rest_ff, *hop_ff0])
    beside = [*ff0.hop(), *ff0.back()]
    kept0, lse0, sames, others = attention(qkv0, att0, size)
    terms, _ = scatter_tokens(
        sames,
        tie(others, *beside),
        beside=lambda gate: [*ff0.hop(gate), *ff0.back(gate)],
    )
    attended0, residual0, norm2 = after_attention(x0, terms, vecs[0])
    ff0.back()
    beside = [*att1.hop(norm2), *att1.hop()]
    w_ff0 = assemble([(ring_ff0, rest_ff0), *zip(ff0.hops, ff0.backs)], model)
    second0, mlp0 = gather_tokens(
        norm2, lambda pair: mlp_forward(pair, w_ff0, bias_fc1[0]), beside
    )
    act0, slope0, sames, others = zip(*mlp0)
    beside = [*att1.hop(second0[-1][0]), *att1.back(second0[-1][0])]
    terms, _ = scatter_tokens(
        sames,
        [others[0], *[tie(v, *beside) for v in others[1:]]],
        beside=lambda gate: [*ff1.hop(gate), *att1.back(gate), *att1.back(gate)],
    )
    mlp_out0, y0, norm1 = after_mlp(residual0, terms, vecs[0], vecs[1])

    w_att1 = assemble([(ring_att1, rest_att1), *zip(att1.hops, att1.backs)], model)
    low1, sums_fc2_1 = start_back(grad_top, vecs[1])
    beside = [*ff1.hop(norm1), *ff1.back(norm1)]
    chunks1, qkv1 = gather_tokens(norm1, projection(w_att1, 1), beside)
    gate = chunks1[-1][0]
    came = [from_chip(tie(low1, gate), step) for step in range(1, chips)]
    beside = [*came, *ff1.hop(gate), *ff1.back(gate)]
    kept1, lse1, sames, others = attention(qkv1, w_att1, size)
    others = tie(others, *beside)
    grads1 = [(low1, core_swap(low1))] + [(v, core_swap(tie(v, lse1))) for v in came]
    terms, _ = scatter_tokens(
        sames, others, beside=lambda gate: [*ff1.back(gate), *pieces(grads1)]
    )
    attended1, residual1, norm2 = after_attention(y0, terms, vecs[1])
    w_ff1 = assemble([(ring_ff1, rest_ff1), *zip(ff1.hops, ff1.backs)], model)
    spare = list(grads1)
    second1, mlp1 = gather_tokens(
        norm2, lambda pair: mlp_both(pair, spare.pop(0), w_ff1, bias_fc1[1])
    )
    act1, dpre1, sums_fc1_1, sames_y1, others_y1, sames, others = zip(*mlp1)

    def grad_ff(second, dpre, grads, act):
        return lambda after: weight_grads(
            [
                (pieces(second), [late(tie(dpre[0], after)), *map(late, dpre[1:])]),
                (pieces(grads), [late(a) for a in act]),
            ],
            dp,
            side,
            "grad_ff",
        )

    def grad_att(chunks, dqkv, datt, kept):
        return lambda after: weight_grads(
            [
                (pieces(chunks), [late(tie(dqkv[0], after)), *map(late, dqkv[1:])]),
                (pieces(datt), [late(a) for a in kept]),
            ],
            dp,
            side,
            "grad_att",
            False,
            heads,
        )[0]

    old = [tuple(map(late, pair)) for pair in grads1]
    terms, g = scatter_tokens(sames, others, grad_ff(second1, dpre1, old, act1))
    sum_ff1 = RingSum((0, 1), *g)
    dres1, low, sums1 = back_second(grad_top, residual1, attended1, terms, vecs[1])
    came_y0 = lax.ppermute(tie(y0, low), "section", [(1, 0)])
    datt, _ = gather_tokens(low, lambda pair: pair[0], sum_ff1.step())
    sums_y1, local_y1 = core_sums(sames_y1, [tie(v, low) for v in others_y1])
    terms_y1 = send_sums([tie(v, datt[-1][0]) for v in sums_y1])
    beside = [came_y0, *terms_y1, *sum_ff1.step(low)]
    dqkv, sames, others, qkv_sums1 = attention_back(qkv1, kept1, lse1, datt, w_att1, size)
    old = [tuple(map(late, pair)) for pair in chunks1]
    terms, g = scatter_tokens(
        sames, tie(others, *beside), grad_att(old, dqkv, datt, kept1), sum_ff1.step
    )
    sum_att1 = RingSum((0, 1), g)
    sum_att1.step()
    dx1, low0, edge1 = back_first(dres1, late(y0), terms, vecs[1], late(mlp_out0), vecs[0])

    y1, sums_sc_1 = last_output(
        residual1, [tie(sames_y1[0], low0), *terms_y1, local_y1], grad_top, vecs[1]
    )

    slopes = list(slope0)
    grads0, mlp_back0 = gather_tokens(
        low0,
        lambda pair: mlp_backward(pair, slopes.pop(0), w_ff0, bias_fc1[0]),
        [y1, *sum_ff1.step(low0)],
    )
    dpre0, sums_fc1_0, sames, others = zip(*mlp_back0)
    hop_att1 = sum_att1.step(grads0[-1][0])
    old = [tuple(map(late, pair)) for pair in second0]
    terms, g = scatter_tokens(
        sames,
        others,
        grad_ff(old, dpre0, grads0, act0),
        lambda gate: [*sum_ff1.step(gate), *hop_att1],
    )
    sum_ff0 = RingSum((1, 0), *g)
    dres0, low, sums0 = back_second(
        dx1, late(residual0), late(attended0), terms, vecs[0]
    )
    beside = [*sum_att1.step(low), *sum_ff0.step(low)]
    datt, _ = gather_tokens(low, lambda pair: pair[0], beside)
    beside = [*sum_att1.step(low), *sum_ff0.step(low)]
    dqkv, sames, others, qkv_sums0 = attention_back(qkv0, kept0, lse0, datt, att0, size)
    old = [tuple(map(late, pair)) for pair in chunks0]
    others = tie(others, *beside)
    beside = sum_ff0.step(others)
    terms, g = scatter_tokens(
        sames, others, grad_att(old, dqkv, datt, kept0), lambda gate: beside
    )
    sum_att0 = RingSum((1, 0), g)
    sum_att0.step()
    going = sum_att0.step()
    terms = [late(terms[0]), *terms[1:-1], late(terms[-1])]
    dx0, edge0 = back_first(late(dres0), late(x0), terms, vecs[0])
    came_dx0 = came_y1 = swap_section(jnp.where(first, y1, dx0))
    second_hop = sum_att0.step(dx0)
    step_att1 = sum_att1.step(dx0)
    third_hop = sum_att0.step()
    sent = sum_att0.sent
    third_hop += sum_ff0.step(sent)
    sum_ff0.step()
    sum_att0.own = sum_att0.total()
    low = sum_att0.own.astype(BF)
    if low.shape == dx1.shape:
        sum_att0.came = came_dx1 = swap_section(jnp.where(first, dx1, low))
    else:
        sum_att0.came = lax.ppermute(low, "section", [(1, 0)])
        came_dx1 = lax.ppermute(dx1, "section", [(0, 1)])

    def both(low, high, came_low, came_high):
        mine = jnp.where(first, low, high)
        came = jnp.where(first, came_low, came_high)
        return jnp.stack([jnp.where(first, mine, came), jnp.where(first, came, mine)])[None, :, None]

    block_out = both(y0, y1, came_y0, came_y1)
    input_grads = both(dx0, dx1, came_dx0, came_dx1)
    sum_ff0.came = tie(sum_ff0.came, block_out, input_grads)

    def by_unit(qkv_sums, unit_sums):
        q = qkv_sums[:, :width].reshape(heads, 1, size)
        v = qkv_sums[:, 2 * width :].reshape(heads, 1, size)
        bias = jnp.concatenate([q, v], 1).reshape(heads, dp, -1).swapaxes(0, 1).reshape(dp, -1)
        return jnp.concatenate([bias, unit_sums.reshape(dp, -1)], axis=1)

    unit0 = by_unit(tie(qkv_sums0, dx0), sum(sums_fc1_0))
    unit1 = by_unit(tie(qkv_sums1, dx0), sum(sums_fc1_1))
    vec = jnp.concatenate(
        [edge0[:2], sums0[:4], edge1[2:4], edge1[:2], sums1[:4], sums_sc_1[:1], sums_fc2_1[:1]]
    )
    vec = tie(vec, *going)
    vec = vec + core_swap(vec)
    vec = tie(sum([from_chip(vec, step) for step in range(1, chips)], vec), *second_hop)
    vec = tie(vec, sent)
    vec = vec.reshape(2, 8, dp, part).swapaxes(1, 2).reshape(2, dp, 8 * part)
    vec0 = jnp.concatenate([vec[0], unit0], axis=1)
    vec1 = jnp.concatenate([vec[1], unit1], axis=1)
    own = jnp.where(first, vec0, vec1) + swap_section(jnp.where(first, vec1, vec0))
    own = tie(own, *step_att1, came_y1, *third_hop)
    vec = lax.dynamic_slice_in_dim(own, here, 1, 0)
    for step in range(1, dp):
        pairs = [(i, (i + step) % dp) for i in range(dp)]
        other = lax.dynamic_slice_in_dim(own, lax.rem(here + step, dp), 1, 0)
        vec = vec + lax.ppermute(other, "dp", pairs)
    cut = 8 * part + heads * (2 * size // dp)
    bias_grad = vec[:, 8 * part : cut].reshape(1, heads, -1)
    fc1_grad = vec[:, cut:].reshape(1, 1, -1)
    g_ln1, b_ln1, g_ln2, b_ln2, g_sc_attn, g_out_bias, g_sc_mlp, g_fc2_bias = (
        vec[:, i * part : (i + 1) * part] for i in range(8)
    )

    def owned(low, high):
        top = jnp.where(first, low.own, high.came.astype(F32))
        bottom = jnp.where(first, low.came.astype(F32), high.own)
        return jnp.concatenate([top, bottom], 0)

    g_ff = owned(sum_ff0, sum_ff1)
    g_att = jnp.where(
        first,
        sum_att0.own + sum_att0.came.astype(F32),
        sum_att1.own + sum_att1.came.astype(F32),
    )
    g_qkv = g_att[None, :, : 3 * width]
    g_out = g_att[:, 3 * width :].T[None]
    g_fc1 = g_ff[:, :units][None]
    g_fc2 = g_ff[:, units:].T[None]
    return (
        block_out, input_grads, g_ln1, b_ln1, g_qkv, bias_grad, g_out, g_out_bias, g_sc_attn,
        g_ln2, b_ln2, g_fc1, fc1_grad, g_fc2, g_fc2_bias, g_sc_mlp,
    )


def solution(mesh):
    vec = P("section", "dp")
    by_row = P("section", "dp", "tensor")
    by_unit = P("section", "tensor", "dp")
    data = P(None, "dp", "tensor", None)
    split = P("section", None, "dp", "tensor", None)
    given = (
        vec, vec, by_row, by_unit, by_unit, vec, vec, vec, vec, by_row, by_unit, by_unit, vec, vec,
    )
    return jax.shard_map(
        shards,
        mesh=mesh,
        in_specs=(data, data) + given,
        out_specs=(split, split) + given,
        check_vma=False,
    )
```

```python
from functools import partial

import jax
import jax.numpy as jnp
from jax import lax
from jax.experimental import pallas as pl
from jax.experimental.pallas import tpu as pltpu
from jax.sharding import PartitionSpec as P

EPSILON = 1e-06
BF = jnp.bfloat16
F32 = jnp.float32
MIB = 1 << 20

LN1_G, LN1_B, OUT_B, SC_ATTN, LN2_G, LN2_B, FC2_B, SC_MLP = range(8)


def dot(a, b):
    return lax.dot_general(a, b, (((1,), (0,)), ((), ())), preferred_element_type=F32)


def dot_bt(a, b):
    return lax.dot_general(a, b, (((1,), (1,)), ((), ())), preferred_element_type=F32)


def dot_at(a, b):
    return lax.dot_general(a, b, (((0,), (0,)), ((), ())), preferred_element_type=F32)


def turn(v):
    return v.astype(F32).T


def params(limit, grid=0):
    return pltpu.CompilerParams(
        vmem_limit_bytes=limit * MIB,
        dimension_semantics=("arbitrary",) * grid if grid else None,
    )


def late(v):
    return pltpu.with_memory_space_constraint(v, pltpu.HBM)


def whole(shape):
    return pl.BlockSpec(shape, lambda i: (0, 0), pipeline_mode=pl.Buffered(1))


def cost(micros):
    return pl.CostEstimate(flops=int(micros * 1.15e9), bytes_accessed=0, transcendentals=0)


def sds(shape, dtype):
    return jax.ShapeDtypeStruct(shape, dtype)


def core_swap(v):
    count = lax.axis_size("tensor")
    return lax.ppermute(v, "tensor", [(i, i ^ 1) for i in range(count)])


def from_chip(v, step):
    count = lax.axis_size("tensor")
    chips = count // 2
    pairs = [(((i // 2 + step) % chips) * 2 + i % 2, i) for i in range(count)]
    return lax.ppermute(v, "tensor", pairs)


def tie(v, *after):
    if not after:
        return v
    return lax.optimization_barrier((v, *after))[0]


def tie_all(vs, *after):
    return lax.optimization_barrier((*vs, *after))[: len(vs)]


def gather_tokens(own, work, beside=()):
    chips = lax.axis_size("tensor") // 2
    came = [from_chip(own, step) for step in range(1, chips)]
    chunks = [(own, core_swap(own))]
    results = [work(chunks[0])]
    for same in came:
        same = tie(same, results[-1], *beside)
        chunks.append((same, core_swap(same)))
        results.append(work(chunks[-1]))
    return chunks, results


def core_sums(sames, others):
    chips, rows = len(sames), sames[0].shape[0]
    if isinstance(others, (list, tuple)):
        came = [core_swap(v) for v in others[1:]]
        local = core_swap(tie(others[0], came[-1]))
    else:
        local = core_swap(others)
        came = [local[c * rows : (c + 1) * rows] for c in range(1, chips)]
    sums = [(a.astype(F32) + b.astype(F32)).astype(BF) for a, b in zip(sames[1:], came)]
    return sums, local


def send_sums(sums):
    chips = len(sums) + 1
    return [from_chip(both, chips - step) for step, both in enumerate(sums, 1)]


def scatter_tokens(sames, others, work=None, beside=None):
    sums, local = core_sums(sames, others)
    terms = send_sums(sums)
    made = work(sums[-1]) if work else local
    more = beside(sums[-1]) if beside else ()
    terms = [tie(t, made, local, *more) for t in terms]
    return [sames[0], *terms, local], made


def swap_section(v):
    return lax.ppermute(v, "section", [(0, 1), (1, 0)])


def assemble(shards, rows):
    count = len(shards)
    cut = len(shards[0])
    size, cols = rows // (count * cut), shards[0][0].shape[1]
    place = jnp.stack([lax.axis_index("dp"), lax.axis_index("section")])

    def body(place_ref, *refs):
        out_ref, sems = refs[count * cut :]
        z, x = place_ref[0], place_ref[1]
        started = []
        for k in range(count):
            base = lax.rem(z + (count - k), count) * (cut * size)
            for i, at in enumerate([base] if cut == 1 else [base + x * size, base + (1 - x) * size]):
                copy = pltpu.make_async_copy(
                    refs[k * cut + i].at[pl.ds(0, size), :],
                    out_ref.at[pl.ds(pl.multiple_of(at, size), size), :],
                    sems.at[k * cut + i],
                )
                copy.start()
                started.append(copy)
        for copy in started:
            copy.wait()

    hbm = pl.BlockSpec(memory_space=pl.ANY)
    return pl.pallas_call(
        body,
        in_specs=[pl.BlockSpec(memory_space=pltpu.SMEM)] + [hbm] * (count * cut),
        out_specs=pl.BlockSpec(memory_space=pltpu.VMEM),
        out_shape=sds((rows, cols), shards[0][0].dtype),
        scratch_shapes=[pltpu.SemaphoreType.DMA((count * cut,))],
        compiler_params=params(6),
        cost_estimate=cost(2),
        name="assemble",
    )(place, *[late(v) for shard in shards for v in shard])


def half_of(v, which):
    half = v.shape[0] // 2
    return lax.dynamic_slice_in_dim(v, which * half, half, 0)


def direct(own):
    count = lax.axis_size("dp")
    return [
        lax.ppermute(own, "dp", [(i, (i + step) % count) for i in range(count)])
        for step in range(1, count)
    ]


def third(values, index):
    cuts = [-(-len(values) * i // 3) for i in range(4)]
    return values[cuts[index] : cuts[index + 1]]


class Ring:
    def __init__(self, own):
        self.last, self.hops, self.backs, self.at, self.back_at = own, [], [], 0, 0

    def hop(self, *gate):
        count = lax.axis_size("dp")
        pairs = [(i, (i + 1) % count) for i in range(count)]
        new = []
        for i in range(len(third(range(count - 1), self.at))):
            self.last = lax.ppermute(tie(self.last, *gate) if i == 0 else self.last, "dp", pairs)
            new.append(self.last)
        self.hops += new
        self.at += 1
        return new

    def back(self, *gate):
        count = lax.axis_size("dp")
        which = third(range(count - 1), self.back_at)
        new = [swap_section(tie(self.hops[i], *gate)) for i in which]
        self.backs += new
        self.back_at += 1
        return new


def in_order(back):
    count = len(back)
    ahead = [back[0], *back[:0:-1]]
    twice = jnp.stack(ahead + ahead)
    return lax.dynamic_slice_in_dim(twice, count - lax.axis_index("dp"), count, 0)


def dp_rows(v, back):
    dp = lax.axis_size("dp")
    part = v.shape[0] // dp
    place = lax.rem(lax.axis_index("dp") + (dp - back), dp)
    return lax.dynamic_slice_in_dim(v, place * part, part, 0)


class RingSum:
    def __init__(self, pair, mine, other=None):
        self.mine, self.other, self.pair = mine, other, pair
        self.terms, self.at, self.done = [], 0, 0

    def total(self, gate=()):
        first = tie(self.terms[0], *gate)
        return sum(t.astype(F32) for t in [first, *self.terms[1:]])

    def one(self, gate):
        dp = lax.axis_size("dp")
        self.done += 1
        new = []
        if self.terms:
            pairs = [(i, (i + 1) % dp) for i in range(dp)]
            self.sent = self.total(gate).astype(BF)
            new.append(lax.ppermute(self.sent, "dp", pairs))
        if self.other is not None:
            new.append(swap_section(tie(dp_rows(self.other, self.done), *gate)))
        self.terms = [*new, dp_rows(self.mine, self.done)]
        return new

    def step(self, *gate):
        self.at += 1
        if self.at == 5:
            self.own = self.total(gate)
            self.came = lax.ppermute(self.own.astype(BF), "section", [self.pair])
            return [self.came]
        count = 1 if self.at == 1 else len(third(range(lax.axis_size("dp") - 1), self.at - 2))
        return [v for i in range(count) for v in self.one(gate if i == 0 else ())]


def standardize(v):
    centred = v - jnp.mean(v, axis=-1, keepdims=True)
    var = jnp.mean(centred * centred, axis=-1, keepdims=True)
    scale = lax.rsqrt(var + EPSILON)
    return centred * scale, scale


def norm_of(v, vec, gain, shift):
    return (standardize(v)[0] * vec[gain : gain + 1, :] + vec[shift : shift + 1, :]).astype(BF)


def norm_back(v, grad, gain):
    xh, scale = standardize(v)
    dxh = grad * gain
    inner = jnp.mean(dxh * xh, axis=-1, keepdims=True)
    out = scale * (dxh - jnp.mean(dxh, axis=-1, keepdims=True) - xh * inner)
    return out, grad * xh


def total(refs):
    out = refs[0][...].astype(F32)
    for ref in refs[1:]:
        out = out + ref[...].astype(F32)
    return out


def fold(v, op):
    return op(v.reshape(-1, 8, v.shape[1]), axis=0)


def add_rows(ref, rows):
    for k, row in enumerate(rows):
        ref[8 * k : 8 * k + 8, :] += fold(row, jnp.sum)


def rowwise(body, row_ins, fulls, row_outs, sums, name):
    rows, width = row_ins[0].shape
    step = min(128, rows)
    some, outs = len(row_ins) + len(fulls), len(row_outs)

    def kernel(*refs):
        if not sums:
            body(*refs)
            return
        sum_ref, acc_ref = refs[some + outs :]

        @pl.when(pl.program_id(0) == 0)
        def _():
            acc_ref[...] = jnp.zeros_like(acc_ref)

        body(*refs[: some + outs], acc_ref)

        @pl.when(pl.program_id(0) == pl.num_programs(0) - 1)
        def _():
            for k in range(sums):
                sum_ref[k : k + 1, :] = jnp.sum(
                    acc_ref[8 * k : 8 * k + 8, :], axis=0, keepdims=True
                )

    out_shape = [sds((rows, width), d) for d in row_outs]
    out_shape += [sds((sums, width), F32)] if sums else []
    block = pl.BlockSpec((step, width), lambda i: (i, 0))
    return pl.pallas_call(
        kernel,
        grid=(rows // step,),
        in_specs=[block] * len(row_ins) + [whole(a.shape) for a in fulls],
        out_specs=[block] * outs + ([whole((sums, width))] if sums else []),
        out_shape=out_shape,
        scratch_shapes=[pltpu.VMEM((8 * sums, width), F32)] if sums else [],
        compiler_params=params(8, 1),
        cost_estimate=cost(2),
        name=name,
    )(*row_ins, *fulls)


def norm_first(x, vec):
    def body(x_ref, vec_ref, out_ref):
        out_ref[...] = norm_of(x_ref[...].astype(F32), vec_ref[...], LN1_G, LN1_B)

    return rowwise(body, [x], [vec], [BF], 0, "norm_first")[0]


def after_attention(x, terms, vec):
    count = len(terms)

    def body(*refs):
        x_ref, term_refs, vec_ref = refs[0], refs[1 : 1 + count], refs[1 + count]
        att_ref, res_ref, norm_ref = refs[2 + count :]
        v = vec_ref[...]
        attended = total(term_refs) + v[OUT_B : OUT_B + 1, :]
        residual = x_ref[...].astype(F32) + v[SC_ATTN : SC_ATTN + 1, :] * attended
        att_ref[...] = attended.astype(BF)
        res_ref[...] = residual
        norm_ref[...] = norm_of(residual, v, LN2_G, LN2_B)

    return rowwise(body, [x, *terms], [vec], [BF, F32, BF], 0, "after_attention")


def after_mlp(residual, terms, vec, vec_next):
    count = len(terms)

    def body(*refs):
        res_ref, term_refs = refs[0], refs[1 : 1 + count]
        vec_ref, next_ref, mlp_ref, y_ref, norm_ref = refs[1 + count :]
        v = vec_ref[...]
        mlp = total(term_refs) + v[FC2_B : FC2_B + 1, :]
        y = (res_ref[...] + v[SC_MLP : SC_MLP + 1, :] * mlp).astype(BF)
        mlp_ref[...] = mlp.astype(BF)
        y_ref[...] = y
        norm_ref[...] = norm_of(y.astype(F32), next_ref[...], LN1_G, LN1_B)

    return rowwise(body, [residual, *terms], [vec, vec_next], [BF, BF, BF], 0, "after_mlp")


def last_output(residual, terms, grad, vec):
    count = len(terms)

    def body(*refs):
        res_ref, term_refs = refs[0], refs[1 : 1 + count]
        grad_ref, vec_ref, y_ref, sum_ref = refs[1 + count :]
        v = vec_ref[...]
        mlp = total(term_refs) + v[FC2_B : FC2_B + 1, :]
        y_ref[...] = (res_ref[...] + v[SC_MLP : SC_MLP + 1, :] * mlp).astype(BF)
        add_rows(sum_ref, [grad_ref[...].astype(F32) * mlp])

    return rowwise(body, [residual, *terms, grad], [vec], [BF], 1, "last_output")


def start_back(grad, vec):
    def body(grad_ref, vec_ref, out_ref, sum_ref):
        low = (vec_ref[...][SC_MLP : SC_MLP + 1, :] * grad_ref[...].astype(F32)).astype(BF)
        out_ref[...] = low
        add_rows(sum_ref, [low.astype(F32)])

    return rowwise(body, [grad], [vec], [BF], 1, "start_back")


def back_second(grad, residual, attended, terms, vec):
    count = len(terms)

    def body(*refs):
        grad_ref, res_ref, att_ref = refs[:3]
        term_refs = refs[3 : 3 + count]
        vec_ref, dres_ref, low_ref, sum_ref = refs[3 + count :]
        v = vec_ref[...]
        dn = total(term_refs)
        back, dgain = norm_back(res_ref[...], dn, v[LN2_G : LN2_G + 1, :])
        dres = grad_ref[...].astype(F32) + back
        low = (v[SC_ATTN : SC_ATTN + 1, :] * dres).astype(BF)
        dres_ref[...] = dres
        low_ref[...] = low
        add_rows(sum_ref, [dgain, dn, dres * att_ref[...].astype(F32), low.astype(F32)])

    return rowwise(
        body, [grad, residual, attended, *terms], [vec], [F32, BF], 4, "back_second"
    )


def back_first(dres, x, terms, vec, mlp_below=None, vec_below=None):
    count = len(terms)
    below = mlp_below is not None

    def body(*refs):
        dres_ref, x_ref = refs[:2]
        term_refs = refs[2 : 2 + count]
        rest = refs[2 + count :]
        if below:
            mlp_ref, vec_ref, under_ref, dx_ref, low_ref, sum_ref = rest
        else:
            vec_ref, dx_ref, sum_ref = rest
        v = vec_ref[...]
        dn = total(term_refs)
        back, dgain = norm_back(x_ref[...].astype(F32), dn, v[LN1_G : LN1_G + 1, :])
        dx = (dres_ref[...] + back).astype(BF)
        dx_ref[...] = dx
        rows = [dgain, dn]
        if below:
            wide = dx.astype(F32)
            low = (under_ref[...][SC_MLP : SC_MLP + 1, :] * wide).astype(BF)
            low_ref[...] = low
            rows += [wide * mlp_ref[...].astype(F32), low.astype(F32)]
        add_rows(sum_ref, rows)

    row_ins = [dres, x, *terms] + ([mlp_below] if below else [])
    fulls = [vec] + ([vec_below] if below else [])
    return rowwise(body, row_ins, fulls, [BF, BF] if below else [BF], 4 if below else 2, "back_first")


def project_qkv(pair, weight, bias):
    rows, width = pair[0].shape
    cols = bias.shape[1]

    def body(a_ref, b_ref, w_ref, bias_ref, out_ref):
        w = w_ref[...]
        shift = bias_ref[...]
        out_ref[:rows, :] = (dot(a_ref[...], w) + shift).astype(BF)
        out_ref[rows:, :] = (dot(b_ref[...], w) + shift).astype(BF)

    return pl.pallas_call(
        body,
        grid=(1,),
        in_specs=[
            whole((rows, width)), whole((rows, width)), whole((width, cols)), whole((1, cols))
        ],
        out_specs=whole((2 * rows, cols)),
        out_shape=sds((2 * rows, cols), BF),
        compiler_params=params(6, 1),
        cost_estimate=cost(0.5),
        name="project_qkv",
    )(*pair, weight, bias)


def head_rows(v, head, size):
    rows = lax.broadcasted_iota(jnp.int32, v.shape, 0)
    return jnp.where(rows // size == head, v, jnp.zeros_like(v))


def head_cols(v, head, size):
    cols = lax.broadcasted_iota(jnp.int32, v.shape, 1)
    return jnp.where(cols // size == head, v, jnp.zeros_like(v))


def attention(packed, weight, size):
    chips = len(packed)
    span = packed[0].shape[0]
    half = span // 2
    width = packed[0].shape[1] // 3
    seq = chips * span
    heads = width // size
    model = weight.shape[0]
    step = min(256, seq)
    chunk = min(128, seq)
    score = size**-0.5

    def body(*refs):
        in_refs, w_ref = refs[:chips], refs[chips]
        head_refs = refs[chips + 1 : 2 * chips + 1]
        lse_ref = refs[2 * chips + 1]
        same_refs, other_ref = refs[2 * chips + 2 : 3 * chips + 2], refs[3 * chips + 2]
        k_ref, qt_ref, vt_ref, ot_ref, s_ref, p_ref = refs[3 * chips + 3 :]
        for c in range(chips):
            at = slice(c * span, (c + 1) * span)
            k_ref[at, :] = in_refs[c][:, width : 2 * width]
            qt_ref[:, at] = (turn(in_refs[c][:, :width]) * score).astype(BF)
            vt_ref[:, at] = turn(in_refs[c][:, 2 * width :]).astype(BF)

        def one(i, carry):
            at = pl.ds(pl.multiple_of(i * step, step), step)
            q = qt_ref[:, at]
            s_ref[0] = dot(k_ref[...], head_rows(q, 0, size))
            for h in range(heads):
                if h + 1 < heads:
                    s_ref[(h + 1) % 2] = dot(k_ref[...], head_rows(q, h + 1, size))
                now = h % 2
                top = fold(s_ref[now, :chunk, :], jnp.max)
                for r in range(chunk, seq, chunk):
                    top = jnp.maximum(top, fold(s_ref[now, r : r + chunk, :], jnp.max))
                top = jnp.max(top, axis=0, keepdims=True)
                norm = jnp.zeros((8, step), F32)
                for r in range(0, seq, chunk):
                    p = jnp.exp(s_ref[now, r : r + chunk, :] - top)
                    norm = norm + fold(p, jnp.sum)
                    p_ref[now, r : r + chunk, :] = p.astype(BF)
                norm = jnp.sum(norm, axis=0, keepdims=True)
                rows = slice(h * size, (h + 1) * size)
                ot_ref[rows, at] = dot(vt_ref[rows, :], p_ref[now]) / norm
                lse_ref[h : h + 1, at] = top + jnp.log(norm)
            return carry

        lax.fori_loop(0, seq // step, one, 0, unroll=True)
        for c in range(chips):
            at = slice(c * span, (c + 1) * span)
            o = ot_ref[:, at].T.astype(BF)
            head_refs[c][...] = o
            same_refs[c][...] = dot_bt(o[:half], w_ref[...]).astype(BF)
            other_ref[c * half : (c + 1) * half, :] = dot_bt(o[half:], w_ref[...]).astype(BF)

    out = pl.pallas_call(
        body,
        grid=(1,),
        in_specs=[whole((span, 3 * width))] * chips
        + [pl.BlockSpec((model, width), lambda i: (0, 3), pipeline_mode=pl.Buffered(1))],
        out_specs=[whole((span, width))] * chips
        + [whole((heads, seq))]
        + [whole((half, model))] * chips
        + [whole((seq // 2, model))],
        out_shape=[pltpu.HBM((span, width), BF)] * chips
        + [sds((heads, seq), F32)]
        + [sds((half, model), BF)] * chips
        + [sds((seq // 2, model), BF)],
        scratch_shapes=[
            pltpu.VMEM((seq, width), BF),
            pltpu.VMEM((width, seq), BF),
            pltpu.VMEM((width, seq), BF),
            pltpu.VMEM((width, seq), F32),
            pltpu.VMEM((2, seq, step), F32),
            pltpu.VMEM((2, seq, step), BF),
        ],
        compiler_params=params(14, 1),
        cost_estimate=cost(9),
        name="attention",
    )(*packed, weight)
    return out[:chips], out[chips], out[chips + 1 : -1], out[-1]


def attention_back(packed, heads_kept, lse, datt, weight, size):
    chips = len(packed)
    span = packed[0].shape[0]
    half = span // 2
    width = packed[0].shape[1] // 3
    seq = chips * span
    heads = width // size
    model = weight.shape[0]
    step = min(256, seq)
    chunk = min(128, seq)
    score = size**-0.5

    def body(*refs):
        at = 0

        def take(count):
            nonlocal at
            at += count
            return refs[at - count : at]

        in_refs, kept_refs = take(chips), take(chips)
        (lse_ref,) = take(1)
        datt_refs = take(2 * chips)
        (w_ref,) = take(1)
        dqkv_refs = take(chips)
        same_refs = take(chips)
        other_ref, sum_ref = take(2)
        k_ref, v_ref, kt_ref, qt_ref, q_ref, do_ref, dot_ref = take(7)
        inner_ref, s_ref, g_ref, p_ref, ds_ref, dk_ref, dv_ref, dqt_ref = take(8)
        for c in range(chips):
            rows = slice(c * span, (c + 1) * span)
            q = in_refs[c][:, :width].astype(F32) * score
            k = in_refs[c][:, width : 2 * width]
            q_ref[rows, :] = q.astype(BF)
            qt_ref[:, rows] = q.T.astype(BF)
            k_ref[rows, :] = k
            kt_ref[:, rows] = turn(k).astype(BF)
            v_ref[rows, :] = in_refs[c][:, 2 * width :]
            for b in range(2):
                d = dot(datt_refs[2 * c + b][...], w_ref[:, 3 * width :]).astype(BF)
                here = slice(c * span + b * half, c * span + (b + 1) * half)
                do_ref[here, :] = d
                dt = turn(d)
                dot_ref[:, here] = dt.astype(BF)
                prod = dt * turn(kept_refs[c][b * half : (b + 1) * half, :])
                for h in range(heads):
                    inner_ref[h : h + 1, here] = jnp.sum(
                        prod[h * size : (h + 1) * size, :], axis=0, keepdims=True
                    )

        def one(i, carry):
            at = pl.ds(pl.multiple_of(i * step, step), step)
            qt = qt_ref[:, at]
            dot_t = dot_ref[:, at]
            q = q_ref[at, :]
            do = do_ref[at, :]

            def scores(h):
                s_ref[h % 2] = dot(k_ref[...], head_rows(qt, h, size))
                g_ref[h % 2] = dot(v_ref[...], head_rows(dot_t, h, size))

            scores(0)
            for h in range(heads):
                if h + 1 < heads:
                    scores(h + 1)
                now = h % 2
                cols = slice(h * step, (h + 1) * step)
                lse = lse_ref[h : h + 1, at]
                inner = inner_ref[h : h + 1, at]
                for r in range(0, seq, chunk):
                    p = jnp.exp(s_ref[now, r : r + chunk, :] - lse)
                    ds = p * (g_ref[now, r : r + chunk, :] - inner)
                    p_ref[r : r + chunk, cols] = p.astype(BF)
                    ds_ref[r : r + chunk, cols] = ds.astype(BF)
                rows = slice(h * size, (h + 1) * size)
                dqt_ref[rows, at] = dot(kt_ref[rows, :], ds_ref[:, cols]) * score
            dv = dot(p_ref[...], jnp.concatenate([head_cols(do, h, size) for h in range(heads)], 0))
            dk = dot(ds_ref[...], jnp.concatenate([head_cols(q, h, size) for h in range(heads)], 0))

            @pl.when(i == 0)
            def _():
                dv_ref[...] = dv
                dk_ref[...] = dk

            @pl.when(i > 0)
            def _():
                dv_ref[...] += dv
                dk_ref[...] += dk

            return carry

        lax.fori_loop(0, seq // step, one, 0, unroll=True)
        for c in range(chips):
            rows = slice(c * span, (c + 1) * span)
            out = dqkv_refs[c]
            out[:, :width] = dqt_ref[:, rows].T.astype(BF)
            out[:, width : 2 * width] = dk_ref[rows, :].astype(BF)
            out[:, 2 * width :] = dv_ref[rows, :].astype(BF)
            sums = jnp.sum(out[...].astype(F32), axis=0, keepdims=True)
            if c == 0:
                sum_ref[...] = sums
            else:
                sum_ref[...] += sums
            w = w_ref[:, : 3 * width]
            same_refs[c][...] = dot_bt(out[:half, :], w).astype(BF)
            other_ref[c * half : (c + 1) * half, :] = dot_bt(out[half:, :], w).astype(BF)

    flat = [g for pair in datt for g in pair]
    out_shape = (
        [pltpu.HBM((span, 3 * width), BF)] * chips
        + [pltpu.HBM((half, model), BF)] * chips
        + [sds((seq // 2, model), BF), sds((1, 3 * width), F32)]
    )
    operands = (*map(late, (*packed, *heads_kept)), lse, *flat, late(weight))
    out = pl.pallas_call(
        body,
        grid=(1,),
        in_specs=[whole(a.shape) for a in operands],
        out_specs=[whole(a.shape) for a in out_shape],
        out_shape=out_shape,
        scratch_shapes=[
            pltpu.VMEM((seq, width), BF),
            pltpu.VMEM((seq, width), BF),
            pltpu.VMEM((width, seq), BF),
            pltpu.VMEM((width, seq), BF),
            pltpu.VMEM((seq, width), BF),
            pltpu.VMEM((seq, width), BF),
            pltpu.VMEM((width, seq), BF),
            pltpu.VMEM((heads, seq), F32),
            pltpu.VMEM((2, seq, step), F32),
            pltpu.VMEM((2, seq, step), F32),
            pltpu.VMEM((seq, heads * step), BF),
            pltpu.VMEM((seq, heads * step), BF),
            pltpu.VMEM((seq, width), F32),
            pltpu.VMEM((seq, width), F32),
            pltpu.VMEM((width, seq), F32),
        ],
        compiler_params=params(26, 1),
        cost_estimate=cost(15),
        name="attention_back",
    )(*operands)
    return out[:chips], out[chips : 2 * chips], out[2 * chips], out[2 * chips + 1]


def gelu_both(x):
    away = jnp.abs(x)
    t = 1.0 / (1.0 + (0.3275911 * 0.5**0.5) * away)
    bell = jnp.exp(-0.5 * (x * x))
    poly = t * (
        0.127414796
        + t * (-0.142248368 + t * (0.7107068705 + t * (-0.7265760135 + t * 0.5307027145)))
    )
    tail = poly * bell
    phi = jnp.where(x >= 0, 1.0 - tail, tail)
    return x * phi, phi + x * (bell * 0.3989422804014327)


def mlp_call(body, pairs, extra, weight, bias, outs, parts, scratch, name):
    rows, model = pairs[0].shape
    units = weight.shape[1] // 2
    step = min(256, units)
    blocks = units // step
    cols = lambda j: (0, j)
    in_specs = [whole((rows, model)) for _ in pairs]
    in_specs += [pl.BlockSpec((2 * rows, step), cols) for _ in extra]
    in_specs += [
        pl.BlockSpec((model, step), cols),
        pl.BlockSpec((model, step), lambda j: (0, blocks + j)),
        pl.BlockSpec((1, step), cols),
    ]
    out_specs = [pl.BlockSpec((2 * rows, step), cols) for _ in outs]
    out_specs += [pl.BlockSpec((1, step), cols)]
    out_specs += [whole((rows, model))] * (2 * parts)
    out_shape = [pltpu.HBM((2 * rows, units), d) for d in outs] + [sds((1, units), F32)]
    out_shape += [sds((rows, model), BF)] * (2 * parts)
    count = len(pairs) // 2
    return pl.pallas_call(
        body,
        grid=(blocks,),
        in_specs=in_specs,
        out_specs=out_specs,
        out_shape=out_shape,
        scratch_shapes=[pltpu.VMEM((2 * rows, model), F32)] * parts
        + [pltpu.VMEM((2 * rows, step), F32)] * scratch,
        compiler_params=params(8 + 5 * parts, 1),
        cost_estimate=cost(0.5),
        name=name,
    )(*pairs, *map(late, extra), weight, weight, bias)


def clear(*refs):
    @pl.when(pl.program_id(0) == 0)
    def _():
        for ref in refs:
            ref[...] = jnp.zeros_like(ref)


def finish(acc, low, high):
    rows = low.shape[0]

    @pl.when(pl.program_id(0) == pl.num_programs(0) - 1)
    def _():
        low[...] = acc[:rows, :].astype(BF)
        high[...] = acc[rows:, :].astype(BF)


CHUNK = 32


def mlp_forward(pair, weight, bias):
    rows = pair[0].shape[0]

    def body(a, b, w1_ref, w2_ref, bias_ref, act_ref, slope_ref, sum_ref, lo, hi, acc, pre):
        clear(acc, sum_ref)
        shift = bias_ref[...]
        for i, x in enumerate((a, b)):
            pre[i * rows : (i + 1) * rows, :] = dot(x[...], w1_ref[...])
        for i in range(2):
            at = slice(i * rows, (i + 1) * rows)
            for r in range(i * rows, (i + 1) * rows, CHUNK):
                act, slope = gelu_both(pre[r : r + CHUNK, :] + shift)
                act_ref[r : r + CHUNK, :] = act.astype(BF)
                slope_ref[r : r + CHUNK, :] = slope.astype(BF)
            acc[at, :] += dot_bt(act_ref[at, :], w2_ref[...])
        finish(acc, lo, hi)

    act, slope, _, lo, hi = mlp_call(body, pair, [], weight, bias, [BF, BF], 1, 1, "mlp_forward")
    return act, slope, lo, hi


def mlp_backward(pair, slope, weight, bias):
    rows = pair[0].shape[0]

    def body(a, b, slope_ref, w1_ref, w2_ref, bias_ref, dpre_ref, sum_ref, lo, hi, acc, pre):
        clear(acc)
        for i, g in enumerate((a, b)):
            pre[i * rows : (i + 1) * rows, :] = dot(g[...], w2_ref[...])
        sums = jnp.zeros((8, bias_ref.shape[1]), F32)
        for i in range(2):
            at = slice(i * rows, (i + 1) * rows)
            for r in range(i * rows, (i + 1) * rows, CHUNK):
                d = pre[r : r + CHUNK, :] * slope_ref[r : r + CHUNK, :].astype(F32)
                d = d.astype(BF)
                dpre_ref[r : r + CHUNK, :] = d
                sums = sums + fold(d.astype(F32), jnp.sum)
            acc[at, :] += dot_bt(dpre_ref[at, :], w1_ref[...])
        sum_ref[...] = jnp.sum(sums, axis=0, keepdims=True)
        finish(acc, lo, hi)

    dpre, sums, lo, hi = mlp_call(
        body, pair, [slope], weight, bias, [BF], 1, 1, "mlp_backward"
    )
    return dpre, sums, lo, hi


def mlp_both(pair, grads, weight, bias):
    rows = pair[0].shape[0]

    def body(
        a, b, c, d, w1_ref, w2_ref, bias_ref, act_ref, dpre_ref, sum_ref,
        lo, hi, blo, bhi, acc, back, pre, grad,
    ):
        clear(acc, back)
        shift = bias_ref[...]
        for i, (x, g) in enumerate(((a, c), (b, d))):
            at = slice(i * rows, (i + 1) * rows)
            pre[at, :] = dot(x[...], w1_ref[...])
            grad[at, :] = dot(g[...], w2_ref[...])
        sums = jnp.zeros((8, bias_ref.shape[1]), F32)
        for i in range(2):
            at = slice(i * rows, (i + 1) * rows)
            for r in range(i * rows, (i + 1) * rows, CHUNK):
                act, slope = gelu_both(pre[r : r + CHUNK, :] + shift)
                act_ref[r : r + CHUNK, :] = act.astype(BF)
                dpre = (grad[r : r + CHUNK, :] * slope).astype(BF)
                dpre_ref[r : r + CHUNK, :] = dpre
                sums = sums + fold(dpre.astype(F32), jnp.sum)
            back[at, :] += dot_bt(dpre_ref[at, :], w1_ref[...])
            acc[at, :] += dot_bt(act_ref[at, :], w2_ref[...])
        sum_ref[...] = jnp.sum(sums, axis=0, keepdims=True)
        finish(acc, lo, hi)
        finish(back, blo, bhi)

    act, dpre, sums, lo, hi, blo, bhi = mlp_call(
        body, [*pair, *grads], [], weight, bias, [BF, BF], 2, 2, "mlp_both"
    )
    return act, dpre, sums, lo, hi, blo, bhi


def weight_grads(products, dp, side, name, halves=True, heads=0):
    model = products[0][0][0].shape[1]
    step = model // dp
    half = step // 2
    cut = 2 if halves else 1
    sizes = [(len(left), len(right), right[0].shape[1]) for left, right in products]
    cols = sum(n for _, _, n in sizes)

    def body(side_ref, *refs):
        acc_ref = refs[-1]
        mine, other = refs[-3:-1] if halves else (refs[-2], None)
        at = base = 0
        for many, few, n in sizes:
            lefts, rights = refs[at : at + many], refs[at + many : at + many + few]
            at += many + few
            ratio = many // few
            acc = None
            for i in range(many):
                size = lefts[i].shape[0]
                here = slice((i % ratio) * size, (i % ratio + 1) * size)
                term = dot_at(lefts[i][...], rights[i // ratio][here, :])
                acc = term if acc is None else acc + term
            if halves:
                acc_ref[:, base : base + n] = acc
            elif heads and not base:
                size = n // (3 * heads)
                for k in range(3 * heads):
                    head, kind = k // 3, k % 3
                    at_k = (kind * heads + head) * size
                    mine[:, k * size : (k + 1) * size] = acc[:, at_k : at_k + size].astype(BF)
            else:
                mine[:, base : base + n] = acc.astype(BF)
            base += n
        if not halves:
            return
        low = pl.multiple_of(side_ref[0] * half, half)
        high = pl.multiple_of((1 - side_ref[0]) * half, half)
        mine[...] = acc_ref[pl.ds(low, half), :].astype(BF)
        other[...] = acc_ref[pl.ds(high, half), :].astype(BF)

    specs, operands = [pl.BlockSpec(memory_space=pltpu.SMEM)], [side.reshape(1)]
    for left, right in products:
        specs += [pl.BlockSpec((a.shape[0], step), lambda i: (0, i)) for a in left]
        specs += [whole(b.shape) for b in right]
        operands += [*left, *right]
    return pl.pallas_call(
        body,
        grid=(dp,),
        in_specs=specs,
        out_specs=[pl.BlockSpec((step // cut, cols), lambda i: (i, 0))] * cut,
        out_shape=[pltpu.HBM((model // cut, cols), BF)] * cut,
        scratch_shapes=[pltpu.VMEM((step, cols), F32)],
        compiler_params=params(14, 1),
        cost_estimate=cost(5),
        name=name,
    )(*operands)


def pieces(chunks):
    return [p for pair in chunks for p in pair]


def shards(
    tokens, cotangent, ln1_gain, ln1_bias, w_qkv, qv_bias, w_out, out_bias, scale_attn,
    ln2_gain, ln2_bias, w_fc1, fc1_bias, w_fc2, fc2_bias, scale_mlp,
):
    side = lax.axis_index("section")
    first = side == 0
    dp = lax.axis_size("dp")
    here = lax.axis_index("dp")
    chips = lax.axis_size("tensor") // 2
    rows, model = tokens.shape[2:]
    heads = qv_bias.shape[1]
    size = qv_bias.shape[2] * dp // 2
    width = heads * size
    units = w_fc1.shape[2]
    part = model // dp

    x0 = lax.dynamic_index_in_dim(tokens, side, 0, keepdims=False).reshape(rows, model)
    grad_top = lax.dynamic_index_in_dim(cotangent, side, 0, keepdims=False).reshape(rows, model)

    vectors = (ln1_gain, ln1_bias, out_bias, scale_attn, ln2_gain, ln2_bias, fc2_bias, scale_mlp)
    packed = jnp.concatenate(
        [v.reshape(-1) for v in vectors] + [fc1_bias.reshape(-1), qv_bias.reshape(-1)]
    )
    own_qkv = w_qkv.reshape(part, heads, 3, size).swapaxes(1, 2).reshape(part, 3 * width)
    own_att = jnp.concatenate([own_qkv, w_out[0].T], axis=1)
    give_att = half_of(own_att, 1 - side)
    came_att = swap_section(give_att)
    came_small = swap_section(tie(packed, give_att))
    both_small = jnp.concatenate(
        [jnp.where(first, packed, came_small), jnp.where(first, came_small, packed)]
    )
    cols = 4 * width
    tail = -(-both_small.size // (16 * cols)) * 16
    both_small = jnp.pad(both_small, (0, tail * cols - both_small.size)).reshape(tail, cols)
    mine_att = half_of(own_att, side)
    ring_att0 = jnp.concatenate([jnp.where(first, mine_att, came_att), both_small])
    ring_att1 = jnp.where(first, came_att, mine_att)
    hops_att0 = direct(ring_att0)
    own_ff = jnp.concatenate([w_fc1[0], w_fc2[0].T], axis=1)
    rest_att = swap_section(tie(mine_att, ring_att0))
    came_ff = swap_section(tie(half_of(own_ff, 1 - side), ring_att0))
    mine_ff = half_of(own_ff, side)
    ring_ff0 = jnp.where(first, mine_ff, came_ff)
    ring_ff1 = jnp.where(first, came_ff, mine_ff)

    def other_half(own, rest):
        left = half_of(own, 1 - side)
        return jnp.where(first, left, rest), jnp.where(first, rest, left)


    backs = [swap_section(v) for v in hops_att0]
    back = [ring_att0, *hops_att0]
    back[2] = tie(back[2], backs[-1])
    flat = in_order([v[-tail:] for v in back])
    flat = flat.reshape(dp, -1)[:, : 2 * packed.size].reshape(dp, 2, -1).astype(F32)
    cut = 8 * part
    vecs = flat[:, :, :cut].reshape(dp, 2, 8, part).transpose(1, 2, 0, 3).reshape(2, 8, model)
    vecs = (vecs[0], vecs[1])
    bias_fc1 = flat[:, :, cut : cut + units // dp].swapaxes(0, 1).reshape(2, 1, units)
    qv = flat[:, :, cut + units // dp :].reshape(dp, 2, heads, -1).transpose(1, 2, 0, 3)
    qv = qv.reshape(2, heads, 2, size)
    bias_qkv = jnp.stack([qv[:, :, 0], jnp.zeros_like(qv[:, :, 0]), qv[:, :, 1]], axis=1)
    bias_qkv = bias_qkv.reshape(2, 1, 3 * width)

    norm1 = norm_first(tie(x0, came_ff), vecs[0])
    rest_ff = swap_section(tie(mine_ff, norm1))
    rest_att0, rest_att1 = other_half(own_att, rest_att)
    rest_ff0, rest_ff1 = other_half(own_ff, rest_ff)
    att1 = Ring(ring_att1)
    att0 = assemble([(tie(ring_att0, norm1), rest_att0), *zip(hops_att0, backs)], model)
    ff0, ff1 = Ring(ring_ff0), Ring(ring_ff1)
    hop_ff0 = ff0.hop(norm1)

    def projection(weight, s):
        return lambda pair: project_qkv(pair, weight, bias_qkv[s])

    chunks0, qkv0 = gather_tokens(norm1, projection(att0, 0), [rest_ff, *hop_ff0])
    beside = [*ff0.hop(), *ff0.back()]
    kept0, lse0, sames, others = attention(qkv0, att0, size)
    terms, _ = scatter_tokens(
        sames,
        tie(others, *beside),
        beside=lambda gate: [*ff0.hop(gate), *ff0.back(gate)],
    )
    attended0, residual0, norm2 = after_attention(x0, terms, vecs[0])
    ff0.back()
    beside = [*att1.hop(norm2), *att1.hop()]
    w_ff0 = assemble([(ring_ff0, rest_ff0), *zip(ff0.hops, ff0.backs)], model)
    second0, mlp0 = gather_tokens(
        norm2, lambda pair: mlp_forward(pair, w_ff0, bias_fc1[0]), beside
    )
    act0, slope0, sames, others = zip(*mlp0)
    beside = [*att1.hop(second0[-1][0]), *att1.back(second0[-1][0])]
    terms, _ = scatter_tokens(
        sames,
        [others[0], *[tie(v, *beside) for v in others[1:]]],
        beside=lambda gate: [*ff1.hop(gate), *att1.back(gate), *att1.back(gate)],
    )
    mlp_out0, y0, norm1 = after_mlp(residual0, terms, vecs[0], vecs[1])

    w_att1 = assemble([(ring_att1, rest_att1), *zip(att1.hops, att1.backs)], model)
    low1, sums_fc2_1 = start_back(grad_top, vecs[1])
    beside = [*ff1.hop(norm1), *ff1.back(norm1)]
    chunks1, qkv1 = gather_tokens(norm1, projection(w_att1, 1), beside)
    gate = chunks1[-1][0]
    came = [from_chip(tie(low1, gate), step) for step in range(1, chips)]
    beside = [*came, *ff1.hop(gate), *ff1.back(gate)]
    kept1, lse1, sames, others = attention(qkv1, w_att1, size)
    others = tie(others, *beside)
    grads1 = [(low1, core_swap(low1))] + [(v, core_swap(tie(v, lse1))) for v in came]
    terms, _ = scatter_tokens(
        sames, others, beside=lambda gate: [*ff1.back(gate), *pieces(grads1)]
    )
    attended1, residual1, norm2 = after_attention(y0, terms, vecs[1])
    w_ff1 = assemble([(ring_ff1, rest_ff1), *zip(ff1.hops, ff1.backs)], model)
    spare = list(grads1)
    second1, mlp1 = gather_tokens(
        norm2, lambda pair: mlp_both(pair, spare.pop(0), w_ff1, bias_fc1[1])
    )
    act1, dpre1, sums_fc1_1, sames_y1, others_y1, sames, others = zip(*mlp1)

    def grad_ff(second, dpre, grads, act):
        return lambda after: weight_grads(
            [
                (pieces(second), [late(tie(dpre[0], after)), *map(late, dpre[1:])]),
                (pieces(grads), [late(a) for a in act]),
            ],
            dp,
            side,
            "grad_ff",
        )

    def grad_att(chunks, dqkv, datt, kept):
        return lambda after: weight_grads(
            [
                (pieces(chunks), [late(tie(dqkv[0], after)), *map(late, dqkv[1:])]),
                (pieces(datt), [late(a) for a in kept]),
            ],
            dp,
            side,
            "grad_att",
            False,
            heads,
        )[0]

    old = [tuple(map(late, pair)) for pair in grads1]
    terms, g = scatter_tokens(sames, others, grad_ff(second1, dpre1, old, act1))
    sum_ff1 = RingSum((0, 1), *g)
    dres1, low, sums1 = back_second(grad_top, residual1, attended1, terms, vecs[1])
    came_y0 = lax.ppermute(tie(y0, low), "section", [(1, 0)])
    datt, _ = gather_tokens(low, lambda pair: pair[0], sum_ff1.step())
    sums_y1, local_y1 = core_sums(sames_y1, [tie(v, low) for v in others_y1])
    terms_y1 = send_sums([tie(v, datt[-1][0]) for v in sums_y1])
    beside = [came_y0, *terms_y1, *sum_ff1.step(low)]
    dqkv, sames, others, qkv_sums1 = attention_back(qkv1, kept1, lse1, datt, w_att1, size)
    old = [tuple(map(late, pair)) for pair in chunks1]
    terms, g = scatter_tokens(
        sames, tie(others, *beside), grad_att(old, dqkv, datt, kept1), sum_ff1.step
    )
    sum_att1 = RingSum((0, 1), g)
    sum_att1.step()
    dx1, low0, edge1 = back_first(dres1, late(y0), terms, vecs[1], late(mlp_out0), vecs[0])

    y1, sums_sc_1 = last_output(
        residual1, [tie(sames_y1[0], low0), *terms_y1, local_y1], grad_top, vecs[1]
    )

    slopes = list(slope0)
    grads0, mlp_back0 = gather_tokens(
        low0,
        lambda pair: mlp_backward(pair, slopes.pop(0), w_ff0, bias_fc1[0]),
        [y1, *sum_ff1.step(low0)],
    )
    dpre0, sums_fc1_0, sames, others = zip(*mlp_back0)
    hop_att1 = sum_att1.step(grads0[-1][0])
    old = [tuple(map(late, pair)) for pair in second0]
    terms, g = scatter_tokens(
        sames,
        others,
        grad_ff(old, dpre0, grads0, act0),
        lambda gate: [*sum_ff1.step(gate), *hop_att1],
    )
    sum_ff0 = RingSum((1, 0), *g)
    dres0, low, sums0 = back_second(
        dx1, late(residual0), late(attended0), terms, vecs[0]
    )
    beside = [*sum_att1.step(low), *sum_ff0.step(low)]
    datt, _ = gather_tokens(low, lambda pair: pair[0], beside)
    beside = [*sum_att1.step(low), *sum_ff0.step(low)]
    dqkv, sames, others, qkv_sums0 = attention_back(qkv0, kept0, lse0, datt, att0, size)
    old = [tuple(map(late, pair)) for pair in chunks0]
    others = tie(others, *beside)
    beside = sum_ff0.step(others)
    terms, g = scatter_tokens(
        sames, others, grad_att(old, dqkv, datt, kept0), lambda gate: beside
    )
    sum_att0 = RingSum((1, 0), g)
    sum_att0.step()
    going = sum_att0.step()
    terms = [late(terms[0]), *terms[1:-1], late(terms[-1])]
    dx0, edge0 = back_first(late(dres0), late(x0), terms, vecs[0])
    came_dx0 = came_y1 = swap_section(jnp.where(first, y1, dx0))
    second_hop = sum_att0.step(dx0)
    step_att1 = sum_att1.step(dx0)
    third_hop = sum_att0.step()
    sent = sum_att0.sent
    third_hop += sum_ff0.step(sent)
    sum_ff0.step()
    sum_att0.own = sum_att0.total()
    low = sum_att0.own.astype(BF)
    if low.shape == dx1.shape:
        sum_att0.came = came_dx1 = swap_section(jnp.where(first, dx1, low))
    else:
        sum_att0.came = lax.ppermute(low, "section", [(1, 0)])
        came_dx1 = lax.ppermute(dx1, "section", [(0, 1)])

    def both(low, high, came_low, came_high):
        mine = jnp.where(first, low, high)
        came = jnp.where(first, came_low, came_high)
        return jnp.stack([jnp.where(first, mine, came), jnp.where(first, came, mine)])[None, :, None]

    block_out = both(y0, y1, came_y0, came_y1)
    input_grads = both(dx0, dx1, came_dx0, came_dx1)
    sum_att0.came = tie(sum_att0.came, block_out)

    def by_unit(qkv_sums, unit_sums):
        q = qkv_sums[:, :width].reshape(heads, 1, size)
        v = qkv_sums[:, 2 * width :].reshape(heads, 1, size)
        bias = jnp.concatenate([q, v], 1).reshape(heads, dp, -1).swapaxes(0, 1).reshape(dp, -1)
        return jnp.concatenate([bias, unit_sums.reshape(dp, -1)], axis=1)

    unit0 = by_unit(tie(qkv_sums0, dx0), sum(sums_fc1_0))
    unit1 = by_unit(tie(qkv_sums1, dx0), sum(sums_fc1_1))
    vec = jnp.concatenate(
        [edge0[:2], sums0[:4], edge1[2:4], edge1[:2], sums1[:4], sums_sc_1[:1], sums_fc2_1[:1]]
    )
    vec = tie(vec, *going)
    vec = vec + core_swap(vec)
    vec = tie(sum([from_chip(vec, step) for step in range(1, chips)], vec), *second_hop)
    vec = tie(vec, sent)
    vec = vec.reshape(2, 8, dp, part).swapaxes(1, 2).reshape(2, dp, 8 * part)
    vec0 = jnp.concatenate([vec[0], unit0], axis=1)
    vec1 = jnp.concatenate([vec[1], unit1], axis=1)
    own = jnp.where(first, vec0, vec1) + swap_section(jnp.where(first, vec1, vec0))
    own = tie(own, *step_att1, came_y1, *third_hop)
    vec = lax.dynamic_slice_in_dim(own, here, 1, 0)
    for step in range(1, dp):
        pairs = [(i, (i + step) % dp) for i in range(dp)]
        other = lax.dynamic_slice_in_dim(own, lax.rem(here + step, dp), 1, 0)
        vec = vec + lax.ppermute(other, "dp", pairs)
    cut = 8 * part + heads * (2 * size // dp)
    bias_grad = vec[:, 8 * part : cut].reshape(1, heads, -1)
    fc1_grad = vec[:, cut:].reshape(1, 1, -1)
    g_ln1, b_ln1, g_ln2, b_ln2, g_sc_attn, g_out_bias, g_sc_mlp, g_fc2_bias = (
        vec[:, i * part : (i + 1) * part] for i in range(8)
    )

    def owned(low, high):
        top = jnp.where(first, low.own, high.came.astype(F32))
        bottom = jnp.where(first, low.came.astype(F32), high.own)
        return jnp.concatenate([top, bottom], 0)

    g_ff = owned(sum_ff0, sum_ff1)
    g_att = jnp.where(
        first,
        sum_att0.own + sum_att0.came.astype(F32),
        sum_att1.own + sum_att1.came.astype(F32),
    )
    g_qkv = g_att[None, :, : 3 * width]
    g_out = g_att[:, 3 * width :].T[None]
    g_fc1 = g_ff[:, :units][None]
    g_fc2 = g_ff[:, units:].T[None]
    return (
        block_out, input_grads, g_ln1, b_ln1, g_qkv, bias_grad, g_out, g_out_bias, g_sc_attn,
        g_ln2, b_ln2, g_fc1, fc1_grad, g_fc2, g_fc2_bias, g_sc_mlp,
    )


def solution(mesh):
    vec = P("section", "dp")
    by_row = P("section", "dp", "tensor")
    by_unit = P("section", "tensor", "dp")
    data = P(None, "dp", "tensor", None)
    split = P("section", None, "dp", "tensor", None)
    given = (
        vec, vec, by_row, by_unit, by_unit, vec, vec, vec, vec, by_row, by_unit, by_unit, vec, vec,
    )
    return jax.shard_map(
        shards,
        mesh=mesh,
        in_specs=(data, data) + given,
        out_specs=(split, split) + given,
        check_vma=False,
    )
```
